32 devices in a mesh: dp: 16 (over z, y, x), opt: 2 (over core).
Axes of the slice: x: 2, y: 2, z: 4, core: 2. Of those that a mesh axis runs over, the one named last changes fastest.
Arguments:
- tokens: bfloat16 [16384, 384], P('dp'), may hold values from -6 to 6
- lengths: int32 [16, 16], P('dp'), may hold values from 1 to 128, 1024 in all within a row
- query_index: int32 [128], P('dp'), may hold values from 0 to 15
- doc_index: int32 [128], P('dp'), may hold values from 0 to 15
- targets: int32 [128], P('dp'), may hold values from 0 to 127
- weights: float32 [384, 4608], P('opt')
- first_moment: float32 [384, 4608], P('opt'), may hold values from -1.1920929e-06 to 1.1920929e-06
- second_moment: float32 [384, 4608], P('opt'), may hold values from 5.749459e-15 to 9.1878606e-14
- vectors: float32 [12, 384], P('opt')
- vec_first: float32 [12, 384], P('opt'), may hold values from -4.7683716e-06 to 4.7683716e-06
- vec_second: float32 [12, 384], P('opt'), may hold values from 9.1878606e-14 to 1.4655484e-12
Outputs:
- grad_norm: float32 [], replicated
- input_grad: bfloat16 [16384, 384], P('dp')
- new_weights: float32 [384, 4608], P('opt')
- new_first: float32 [384, 4608], P('opt')
- new_second: float32 [384, 4608], P('opt')
- weight_copy: bfloat16 [384, 4608], P('opt')
- new_vectors: float32 [12, 384], P('opt')
- new_vec_first: float32 [12, 384], P('opt')
- new_vec_second: float32 [12, 384], P('opt')
The draws below stay inside these ranges and needn't reach their ends.
Inputs may be any that keep to these rules, and one draw needn't show every extreme that they name: `query_index`: row r of the device's rows and segment s in it are named r * 16 + s. `doc_index`: numbered as query_index. `targets`: documents are numbered device by device along dp, in pair order. Each row's lengths sum to 1024.
All inputs are finite; a program needn't handle non-finite values.
Results may differ from the reference program's by a relative error of at most 0.012.
Values may be sent and summed in bfloat16 or wider, within the bound.
No kernel may reach another device: no remote copies, remote signals or barrier semaphores. Data moves between devices by JAX's collectives and lax.ppermute only.
A program may use at most 192 MiB of HBM per device.

```python
import math
import jax
import jax.numpy as jnp
import numpy as np
from jax import lax

D = 384
HEADS = 12
HD = 32
FF = 1536
SEQ = 1024
SEGS = 16
MOSTLEN = 128
PAIRS_DEV = 8
ROWS_DEV = 1
STEP = 10
TOK_DEV = 1024
TOKENS = 16384
ROWS = 16
PAIRS = 128
WCOLS = 4608
NPARAM = 1774080
N_DP = 16


def draw_weights(key, part):
    key = jax.random.fold_in(key, 11)
    normal_draw = jax.random.normal(key, (D, WCOLS), jnp.float32)
    columns = jnp.arange(WCOLS)
    column_scale = jnp.where(columns < 3 * D, D ** (-0.5), jnp.where(columns < 4 * D, 4.0 * D ** (-0.5), jnp.where(columns < 4 * D + FF, D ** (-0.5), FF ** (-0.5))))
    return normal_draw * column_scale[None, :]


def draw_vectors(key, part):
    key = jax.random.fold_in(key, 12)
    first_key, second_key = jax.random.split(key)
    shifts = 0.1 * jax.random.normal(first_key, (12, D), jnp.float32)
    rising = (0.6 + 1.2 * jnp.arange(D, dtype=jnp.float32) / D)[None, :] * jax.random.uniform(second_key, (12, D), jnp.float32, 0.8, 1.2)
    row_ids = jnp.arange(12)[:, None]
    gain_rows = (row_ids == 8) | (row_ids == 10)
    return jnp.where(gain_rows, rising, shifts)


def plant(array, rng, low, top_value):
    dims = array.shape
    index_at = [jax.random.randint(jax.random.fold_in(rng, axis), (), 0, dims[axis]) for axis in range(len(dims))]
    array = array.at[tuple(index_at)].set(low)
    longest = dims.index(max(dims))
    index_at[longest] = (index_at[longest] + 1) % dims[longest]
    return array.at[tuple(index_at)].set(top_value)


def block_levels(key, extent, cuts, low, high):
    def one(axis_at, shards_of):
        heights = jax.random.uniform(jax.random.fold_in(jax.random.fold_in(key, 6), axis_at), (shards_of,), jnp.float32, low / len(cuts), high / len(cuts))
        return jnp.repeat(jnp.exp(heights), extent[axis_at] // shards_of).reshape((-1,) + (1,) * (len(extent) - axis_at - 1))

    loudness = one(*cuts[0])
    for cut in cuts[1:]:
        loudness = loudness * one(*cut)
    return loudness


def length_profile(count, total, reach, skew):
    portions = [(1 << 20) // math.isqrt(grade ** skew) + 1 for grade in range(2, count + 1)]
    spare, holding = total - reach - (count - 1), [1] * (count - 1)
    while spare > 0:
        candidates = [i for i in range(count - 1) if holding[i] < reach]
        pool, left = sum([portions[i] for i in candidates]), spare
        for i in candidates:
            addition = min(reach - holding[i], max(1, left * portions[i] // pool), spare)
            holding[i] = holding[i] + addition
            spare = spare - addition
    return np.array([reach] + holding)


def ragged_sizes(own_key, amount, total, reach, lean):
    if amount == 2:
        one = jax.random.randint(own_key, (), max(1, total - reach), min(reach, total - 1) + 1)
        return jnp.stack([one, total - one])
    tallies = jnp.asarray(length_profile(amount, total, reach, lean), jnp.int32)
    twos = (amount - 1) // 2
    source_of, sink = tallies[1:1 + 2 * twos:2], tallies[2:2 + 2 * twos:2]
    slack = jnp.minimum(source_of - 1, reach - sink)
    shifted = jax.random.randint(jax.random.fold_in(own_key, 1), (twos,), 0, 1 << 20) % (slack + 1)
    tallies = tallies.at[1:1 + 2 * twos:2].set(source_of - shifted).at[2:2 + 2 * twos:2].set(sink + shifted)
    return tallies[jax.random.permutation(jax.random.fold_in(own_key, 2), amount)]


def noise(own_key, shape, spread, reach, cuts=(), held_as=jnp.bfloat16):
    level = block_levels(own_key, shape, cuts, -0.22, 0.18) if cuts else 1.0
    drawn = jax.random.normal(own_key, shape, jnp.float32) * spread * level
    return jnp.minimum(jnp.maximum(drawn, -reach), reach).astype(held_as)


def setup_inputs(seed: int = 0) -> dict:
    key_of = jax.random.split(jax.random.key(seed), 12)
    return {
        "tokens": noise(key_of[0], (TOKENS, D), 1.0, 6.0, ((0, 16),)),
        "lengths": jax.vmap(lambda own: ragged_sizes(own, SEGS, SEQ, MOSTLEN, 2))(jax.random.split(key_of[1], ROWS)).reshape((ROWS, SEGS)).astype(jnp.int32),
        "query_index": plant(jax.random.randint(key_of[2], (PAIRS,), 0, ROWS_DEV * SEGS), jax.random.fold_in(key_of[2], 1), 0, (ROWS_DEV * SEGS) - 1).astype(jnp.int32),
        "doc_index": plant(jax.random.randint(key_of[3], (PAIRS,), 0, ROWS_DEV * SEGS), jax.random.fold_in(key_of[3], 1), 0, (ROWS_DEV * SEGS) - 1).astype(jnp.int32),
        "targets": plant(jax.random.randint(key_of[4], (PAIRS,), 0, PAIRS), jax.random.fold_in(key_of[4], 1), 0, PAIRS - 1).astype(jnp.int32),
        "weights": draw_weights(jax.random.fold_in(key_of[11], 71), 0),
        "first_moment": noise(key_of[6], (D, WCOLS), (0.000111 / NPARAM ** 0.5), 1.1920928955078125e-06, ((0, 2),), jnp.float32),
        "second_moment": jnp.clip(jnp.exp(math.log(9.18786056893113e-14) - 2.7713625 * jax.random.uniform(key_of[7], (D, WCOLS), jnp.float32) ** block_levels(key_of[7], (D, WCOLS), ((0, 2),), -0.2, 0.2)), 5.7494588991536914e-15, 9.18786056893113e-14),
        "vectors": draw_vectors(jax.random.fold_in(key_of[11], 71), 0),
        "vec_first": noise(key_of[9], (12, D), (0.000444 / NPARAM ** 0.5), 4.76837158203125e-06, ((0, 2),), jnp.float32),
        "vec_second": jnp.clip(jnp.exp(math.log(1.4655483857733964e-12) - 2.76951657 * jax.random.uniform(key_of[10], (12, D), jnp.float32) ** block_levels(key_of[10], (12, D), ((0, 2),), -0.2, 0.2)), 9.18786056893113e-14, 1.4655483857733964e-12),
    }


LN_EPS = 1e-06
POOL_EPS = 1e-06
SCORE_SCALE = 50.0
CLIP_NORM = 0.001
BETA_ONE = 0.9
BETA_TWO = 0.98
ADAM_EPS = 1e-08
LEARN_RATE = 0.05
VECTOR_RATE = 0.3
DECAY_RATE = 0.01
NEG_BIG = -1000000000.0

@jax.custom_vjp
def low(v):
    return lax.optimization_barrier(v.astype(jnp.bfloat16)).astype(jnp.float32)

@jax.custom_vjp
def low_back(v):
    return v

def low_keep(v):
    return (low(v), None)

def low_pass(kept, grad):
    return (grad,)

def back_keep(v):
    return (v, None)

def back_low(kept, grad):
    return (low(grad),)
low.defvjp(low_keep, low_pass)
low_back.defvjp(back_keep, back_low)

def precise(former, latter):
    return jnp.dot(former, latter, precision=lax.Precision.HIGHEST, preferred_element_type=jnp.float32)

def precise_right(former, latter):
    return lax.dot_general(former, latter, (((1,), (1,)), ((), ())), precision=lax.Precision.HIGHEST, preferred_element_type=jnp.float32)

def segment_ids(row_lengths):
    bounds = jnp.cumsum(row_lengths, axis=1)
    places = jnp.arange(SEQ, dtype=jnp.int32)
    inside = lax.optimization_barrier(jnp.sum((places[None, :, None] >= bounds[:, None, :]).astype(jnp.int32), axis=2))
    offsets = jnp.arange(row_lengths.shape[0], dtype=jnp.int32)[:, None] * row_lengths.shape[1]
    return (inside + offsets).reshape(-1)

def layer_norm(argument, scaling, offset_row):
    average = lax.optimization_barrier(jnp.mean(argument, axis=1, keepdims=True))
    centred = argument - average
    return centred * lax.rsqrt(lax.optimization_barrier(jnp.mean(centred * centred, axis=1, keepdims=True)) + LN_EPS) * scaling + offset_row

def encode_row(row_in, segment, matrices, vectors_low):
    breadth = row_in.shape[1]
    hidden_units = (matrices.shape[1] - 4 * breadth) // 2
    bias_qkv = jnp.concatenate([vectors_low[0], jnp.zeros_like(vectors_low[0]), vectors_low[1]])
    projected = low_back(low(precise(row_in, matrices[:, :3 * breadth]) + bias_qkv))
    query_part = projected[:, :breadth].reshape(SEQ, HEADS, HD)
    key_part = projected[:, breadth:2 * breadth].reshape(SEQ, HEADS, HD)
    value_part = projected[:, 2 * breadth:].reshape(SEQ, HEADS, HD)
    scores = jnp.einsum('qhd,khd->hqk', query_part, key_part, precision=lax.Precision.HIGHEST) * HD ** (-0.5)
    same_doc = segment[:, None] == segment[None, :]
    scores = low_back(jnp.where(same_doc[None], scores, NEG_BIG))
    peak = lax.optimization_barrier(jnp.max(scores, axis=2, keepdims=True))
    powers = jnp.exp(scores - peak)
    attn_prob = low(powers / lax.optimization_barrier(jnp.sum(powers, axis=2, keepdims=True)))
    attended = jnp.einsum('hqk,khd->qhd', attn_prob, value_part, precision=lax.Precision.HIGHEST).reshape(SEQ, breadth)
    attended = low_back(low(attended))
    branch = low_back(precise(attended, matrices[:, 3 * breadth:4 * breadth]))
    hidden = layer_norm(branch + vectors_low[2] + row_in, vectors_low[8], vectors_low[9])
    up_proj = low_back(precise(low(hidden), matrices[:, 4 * breadth:4 * breadth + hidden_units]) + vectors_low[3:7].reshape(-1))
    activated = low(jax.nn.gelu(up_proj, approximate=False))
    down_proj = low_back(precise_right(activated, matrices[:, 4 * breadth + hidden_units:]))
    return layer_norm(down_proj + vectors_low[7] + hidden, vectors_low[10], vectors_low[11])

def pool_units(encoded, segment, chosen):
    onehot = (chosen[:, None] == segment[None, :]).astype(jnp.float32)
    pooled = precise(onehot, encoded) / lax.optimization_barrier(jnp.sum(onehot, axis=1, keepdims=True))
    return pooled * lax.rsqrt(lax.optimization_barrier(jnp.sum(pooled * pooled, axis=1, keepdims=True)) + POOL_EPS)

def adamw(parameter, first_state, second, gradient, factor, step_rate):
    clipped = gradient * factor
    first_new = BETA_ONE * first_state + (1.0 - BETA_ONE) * clipped
    second_new = BETA_TWO * second + (1.0 - BETA_TWO) * clipped * clipped
    direction = first_new / (1.0 - BETA_ONE ** STEP) / (jnp.sqrt(second_new / (1.0 - BETA_TWO ** STEP)) + ADAM_EPS)
    return (parameter - step_rate * (direction + DECAY_RATE * parameter), first_new, second_new)

def reference(tokens, lengths, query_index, doc_index, targets, weights, first_moment, second_moment, vectors, vec_first, vec_second):
    segment = jax.vmap(segment_ids)(lengths.reshape(N_DP, ROWS_DEV, SEGS))
    row_segment = segment.reshape(N_DP * ROWS_DEV, SEQ)
    chosen = jnp.concatenate([query_index.reshape(N_DP, PAIRS_DEV), doc_index.reshape(N_DP, PAIRS_DEV)], axis=1)

    def objective(inputs, matrices, vector_rows):
        matrices_low = low(matrices)
        vectors_low = low(vector_rows)
        row_fn = jax.checkpoint(lambda operands: encode_row(operands[0], operands[1], matrices_low, vectors_low))
        encoded = lax.map(row_fn, (inputs.reshape(N_DP * ROWS_DEV, SEQ, D), row_segment))
        encoded = encoded.reshape(N_DP, TOK_DEV, D)
        unit_rows = jax.vmap(pool_units)(encoded, segment, chosen)
        queries = unit_rows[:, :PAIRS_DEV].reshape(-1, D)
        documents = low(unit_rows[:, PAIRS_DEV:].reshape(-1, D))
        logits = SCORE_SCALE * precise_right(queries, documents)
        peak = lax.optimization_barrier(jnp.max(logits, axis=1, keepdims=True))
        log_total = peak[:, 0] + jnp.log(lax.optimization_barrier(jnp.sum(jnp.exp(logits - peak), axis=1)))
        picked = jnp.take_along_axis(logits, targets[:, None], axis=1)[:, 0]
        return jnp.mean(log_total - picked)
    loss_value, pullback = jax.vjp(objective, tokens.astype(jnp.float32), weights, vectors)
    grad_in, grad_w, grad_v = pullback(jnp.ones_like(loss_value))
    grad_norm = jnp.sqrt(jnp.sum(grad_w * grad_w) + jnp.sum(grad_v * grad_v))
    factor = jnp.minimum(1.0, CLIP_NORM / (grad_norm + 1e-06))
    new_weights, new_first, new_second = adamw(weights, first_moment, second_moment, grad_w, factor, LEARN_RATE)
    new_vectors, new_vec_first, new_vec_second = adamw(vectors, vec_first, vec_second, grad_v, factor, VECTOR_RATE)
    return (grad_norm, grad_in.astype(jnp.bfloat16), new_weights, new_first, new_second, new_weights.astype(jnp.bfloat16), new_vectors, new_vec_first, new_vec_second)
```

```python
import functools

import jax
import jax.numpy as jnp
from jax import lax
from jax.experimental import pallas as pl
from jax.experimental.pallas import tpu as pltpu
from jax.sharding import PartitionSpec as P

D = 384
HEADS = 12
HD = 32
FF = 1536
SEQ = 1024
SEGS = 16
PAIRS = 8
STEP = 10

WIN = 576
OFF = SEQ - WIN
PAD = 640
BLOCK = 128
BANDS = tuple((q, max(0, q - 128), min(WIN, q + 256)) for q in range(0, WIN, BLOCK))
BAND_ROWS = tuple(sum(b[2] - b[1] for b in BANDS[:i]) for i in range(len(BANDS) + 1))
ROWS = 64

LN_EPS = 1e-06
POOL_EPS = 1e-06
SCORE_SCALE = 50.0
CLIP_NORM = 0.001
BETA_ONE = 0.9
BETA_TWO = 0.98
ADAM_EPS = 1e-08
LEARN_RATE = 0.05
VECTOR_RATE = 0.3
DECAY_RATE = 0.01
NEG_BIG = -1e30
HALF = D // 2
EXP2_SCALE = HD ** (-0.5) * 1.4426950408889634

F32 = jnp.float32
BF16 = jnp.bfloat16
VMEM = pl.BlockSpec(memory_space=pltpu.VMEM)
SMEM = pl.BlockSpec(memory_space=pltpu.SMEM)


def nn(a, b):
    return jnp.dot(a, b, preferred_element_type=F32)


def nt(a, b):
    return lax.dot_general(a, b, (((1,), (1,)), ((), ())), preferred_element_type=F32)


def tn(a, b):
    return lax.dot_general(a, b, (((0,), (0,)), ((), ())), preferred_element_type=F32)


def exact(a, b, dims):
    return lax.dot_general(
        a, b, (dims, ((), ())), precision=lax.Precision.HIGHEST, preferred_element_type=F32
    )


def iota(shape, axis):
    return lax.broadcasted_iota(jnp.int32, shape, axis)


def low_pair(value):
    high = value.astype(BF16)
    return high, (value - high.astype(F32)).astype(BF16)


def aligned(start, size, unit):
    return pl.ds(pl.multiple_of(start, unit), size)


def assemble(dst, own, other, opt):
    dst[aligned(HALF * opt, HALF, 64), :] = own[0:HALF, :]
    dst[aligned(HALF * (1 - opt), HALF, 64), :] = other[0:HALF, :]


def call(kernel, ins, outs, scratch=(), flops=0, name=None, vmem=40, transcendentals=0):
    specs = [SMEM if s else VMEM for s, _ in ins]
    shapes = [jax.ShapeDtypeStruct(s, d) for s, d in outs]
    moved = sum(a.size * a.dtype.itemsize for _, a in ins)
    moved += sum(s.size * s.dtype.itemsize for s in shapes)
    return pl.pallas_call(
        kernel,
        out_shape=shapes,
        in_specs=specs,
        out_specs=[VMEM] * len(shapes),
        scratch_shapes=list(scratch),
        compiler_params=pltpu.CompilerParams(vmem_limit_bytes=vmem << 20),
        cost_estimate=pl.CostEstimate(
            flops=flops, bytes_accessed=moved, transcendentals=transcendentals
        ),
        name=name,
    )(*[a for _, a in ins])


def head_stack(rows):
    lane_head = iota(rows.shape, 1) // HD
    zero = jnp.zeros_like(rows)
    return jnp.concatenate([jnp.where(lane_head == j, rows, zero) for j in range(4)], axis=0)


def attend_kernel(
    place, lengths, tokens, w_own, w_other, proj, att, lse, segc, segr, vec, wfull, bias, vt
):
    opt = place[0]
    assemble(wfull, w_own, w_other, opt)
    mine = w_own[HALF : HALF + 16, 0:D].astype(F32)
    others = w_other[HALF : HALF + 16, 0:D].astype(F32)
    first = opt == 0
    vec[0:6, :] = jnp.where(first, mine, others)[0:6]
    vec[6:12, :] = jnp.where(first, others, mine)[0:6]
    vec[12:16, :] = jnp.zeros((4, D), F32)

    pos_col = iota((WIN, 128), 0) + OFF * opt
    pos_row = iota((8, PAD), 1) + OFF * opt
    seg_col = jnp.zeros((WIN, 128), jnp.int32)
    seg_row = jnp.zeros((8, PAD), jnp.int32)
    bound = jnp.int32(0)
    for s in range(SEGS):
        bound = bound + lengths[s]
        seg_col = seg_col + (pos_col >= bound).astype(jnp.int32)
        seg_row = seg_row + (pos_row >= bound).astype(jnp.int32)
    segc[...] = seg_col
    segr[...] = seg_row
    for i, (q0, k0, k1) in enumerate(BANDS):
        bias[BAND_ROWS[i] : BAND_ROWS[i + 1], :] = jnp.where(
            segc[k0:k1, :] == segr[0:1, q0 : q0 + BLOCK], 0.0, NEG_BIG
        )

    x = tokens[aligned(OFF * opt, WIN, 64), :]
    for c in range(3):
        acc = nn(x, wfull[:, c * D : (c + 1) * D])
        if c != 1:
            acc = acc + vec[(0 if c == 0 else 1) : (1 if c == 0 else 2), :]
        proj[0:WIN, c * D : (c + 1) * D] = acc.astype(BF16)
    proj[WIN:PAD, :] = jnp.zeros((PAD - WIN, 3 * D), BF16)

    def group(g, carry):
        def lanes(part):
            return aligned(part * D + 128 * g, 128, 128)

        for t in range(PAD // 128):
            vt[:, 128 * t : 128 * t + 128] = (
                proj[128 * t : 128 * t + 128, lanes(2)].astype(F32).T.astype(BF16)
            )
        for i, (q0, k0, k1) in enumerate(BANDS):
            stack = head_stack(proj[q0 : q0 + BLOCK, lanes(0)])
            st = nt(proj[k0:k1, lanes(1)], stack)
            outs = []
            for j in range(4):
                t = (
                    st[:, j * BLOCK : (j + 1) * BLOCK] * EXP2_SCALE
                    + bias[BAND_ROWS[i] : BAND_ROWS[i + 1], :]
                )
                peak = jnp.max(t, axis=0, keepdims=True)
                powers = jnp.exp2(t - peak)
                total = jnp.sum(powers, axis=0, keepdims=True)
                lse[g, j : j + 1, q0 : q0 + BLOCK] = peak + jnp.log2(total)
                o = nn(vt[j * HD : (j + 1) * HD, k0:k1], powers.astype(BF16))
                outs.append(o * (1.0 / total))
            rows = min(BLOCK, WIN - q0)
            att[q0 : q0 + rows, aligned(128 * g, 128, 128)] = (
                jnp.concatenate(outs, axis=0).T[0:rows].astype(BF16)
            )
        return carry

    lax.fori_loop(0, 3, group, 0)


def attend(place, lengths, tokens, w_own, w_other):
    return call(
        attend_kernel,
        [(1, place), (1, lengths), (0, tokens), (0, w_own), (0, w_other)],
        [
            ((PAD, 3 * D), BF16),
            ((WIN, D), BF16),
            ((3, 4, PAD), F32),
            ((WIN, 128), jnp.int32),
            ((8, PAD), jnp.int32),
            ((16, D), F32),
        ],
        [
            pltpu.VMEM((D, 3 * D), BF16),
            pltpu.VMEM((BAND_ROWS[-1], 128), F32),
            pltpu.VMEM((128, PAD), BF16),
        ],
        flops=2 * WIN * D * 3 * D + 4 * 12 * WIN * 384 * 128,
        name="attend",
    )


def owned(place, lengths, segment):
    bound = jnp.int32(0)
    count = jnp.int32(0)
    for s in range(SEGS):
        bound = bound + lengths[s]
        count = count + (bound <= WIN).astype(jnp.int32)
    low_side = (segment < count).astype(jnp.int32)
    return low_side == (place[0] == 0).astype(jnp.int32)


def mlp_kernel(
    place, lengths, chosen, targets, att, tokens, segr, vec, wo_own, wo_other, wu_own, wu_other,
    wd_own, wd_other, xhat1, inv1, hlow, act, slope, xhat2, inv2, unit, uscale,
    wo, wu, wd, tmp, hid, ench, encl,
):
    opt = place[0]
    assemble(wo, wo_own, wo_other, opt)
    assemble(wu, wu_own, wu_other, opt)
    assemble(wd, wd_own, wd_other, opt)
    tmp[...] = nn(att[...], wo[...])

    def first_norm(i, carry):
        r = aligned(i * ROWS, ROWS, ROWS)
        x = tokens[aligned(OFF * opt + i * ROWS, ROWS, ROWS), :].astype(F32)
        v = tmp[r, :] + vec[2:3, :] + x
        centred = v - jnp.mean(v, axis=1, keepdims=True)
        inverse = lax.rsqrt(jnp.mean(centred * centred, axis=1, keepdims=True) + LN_EPS)
        normed = centred * inverse
        xhat1[r, :] = normed
        inv1[r, :] = jnp.broadcast_to(inverse, (ROWS, 128))
        h = normed * vec[8:9, :] + vec[9:10, :]
        hid[r, :] = h
        hlow[r, :] = h.astype(BF16)
        return carry

    lax.fori_loop(0, WIN // ROWS, first_norm, 0)

    for c in range(4):
        cols = slice(c * D, (c + 1) * D)
        tmp[...] = nn(hlow[...], wu[:, cols])

        def gelu(i, carry, cols=cols, c=c):
            r = aligned(i * ROWS, ROWS, ROWS)
            u = tmp[r, :] + vec[3 + c : 4 + c, :]
            half = lax.erf(u * 0.7071067811865476) * 0.5 + 0.5
            act[r, cols] = (u * half).astype(BF16)
            slope[r, cols] = half + u * jnp.exp(-0.5 * u * u) * 0.3989422804014327
            return carry

        lax.fori_loop(0, WIN // ROWS, gelu, 0)

    tmp[...] = nt(act[...], wd[...])

    def second_norm(i, carry):
        r = aligned(i * ROWS, ROWS, ROWS)
        v = tmp[r, :] + vec[7:8, :] + hid[r, :]
        centred = v - jnp.mean(v, axis=1, keepdims=True)
        inverse = lax.rsqrt(jnp.mean(centred * centred, axis=1, keepdims=True) + LN_EPS)
        normed = centred * inverse
        xhat2[r, :] = normed
        inv2[r, :] = jnp.broadcast_to(inverse, (ROWS, 128))
        high, rest = low_pair(normed * vec[10:11, :] + vec[11:12, :])
        ench[r, :] = high
        encl[r, :] = rest
        return carry

    lax.fori_loop(0, WIN // ROWS, second_norm, 0)

    seg = segr[0:1, 0:WIN]
    row_id = iota((2 * PAIRS, WIN), 0)
    wanted = jnp.zeros((2 * PAIRS, WIN), jnp.int32)
    for j in range(2 * PAIRS):
        wanted = jnp.where(row_id == j, chosen[j], wanted)
    mask = owned(place, lengths, jnp.broadcast_to(seg, (2 * PAIRS, WIN)))
    onehot = jnp.where((wanted == seg) & mask, 1.0, 0.0)
    count = jnp.maximum(jnp.sum(onehot, axis=1, keepdims=True), 1.0)
    hot = onehot.astype(BF16)
    pooled = (nn(hot, ench[...]) + nn(hot, encl[...])) / count
    inverse_len = lax.rsqrt(jnp.sum(pooled * pooled, axis=1, keepdims=True) + POOL_EPS)
    unit[0 : 2 * PAIRS, :] = pooled * inverse_len
    uscale[...] = jnp.broadcast_to(inverse_len / count, (2 * PAIRS, 128))
    lane_row = iota((PAIRS, D), 0)
    marks = jnp.zeros((PAIRS, D), F32)
    for j in range(PAIRS):
        marks = jnp.where(lane_row == j, targets[j].astype(F32), marks)
    unit[2 * PAIRS : 3 * PAIRS, :] = jnp.where(opt == 0, marks, 0.0)


def mlp(place, lengths, chosen, targets, att, tokens, segr, vec, halves):
    return call(
        mlp_kernel,
        [(1, place), (1, lengths), (1, chosen), (1, targets), (0, att), (0, tokens), (0, segr), (0, vec)]
        + [(0, h) for h in halves],
        [
            ((WIN, D), F32),
            ((WIN, 128), F32),
            ((WIN, D), BF16),
            ((WIN, FF), BF16),
            ((WIN, FF), F32),
            ((WIN, D), F32),
            ((WIN, 128), F32),
            ((3 * PAIRS, D), F32),
            ((2 * PAIRS, 128), F32),
        ],
        [
            pltpu.VMEM((D, D), BF16),
            pltpu.VMEM((D, FF), BF16),
            pltpu.VMEM((D, FF), BF16),
            pltpu.VMEM((WIN, D), F32),
            pltpu.VMEM((WIN, D), F32),
            pltpu.VMEM((WIN, D), BF16),
            pltpu.VMEM((WIN, D), BF16),
        ],
        flops=2 * WIN * D * (D + 2 * FF),
        name="mlp",
    )


def split_rows(grad, keep, send, at, opt):
    keep[at, 0:HALF, :] = grad[aligned(HALF * opt, HALF, 64), :].astype(BF16)
    send[at, 0:HALF, :] = grad[aligned(HALF * (1 - opt), HALF, 64), :].astype(BF16)


def down_kernel(
    count, place, lengths, chosen, segc, uscale, xhat2, inv2, act, slope, vec, wd_own, wd_other,
    *rest,
):
    pieces, (dsec, dup, keep, send, sums, queries, docs, marks, wd, dlow, grad) = (
        rest[:-11],
        rest[-11:],
    )
    opt, plane, me = place[0], place[1], place[2]
    assemble(wd, wd_own, wd_other, opt)
    per = pieces[0].shape[0]
    for p, piece in enumerate(pieces):
        for j in range(per):
            r = slice((p * per + j) * PAIRS, (p * per + j + 1) * PAIRS)
            queries[r, :] = piece[j, 0:PAIRS, :]
            docs[r, :] = piece[j, PAIRS : 2 * PAIRS, :].astype(BF16).astype(F32)
            marks[r, :] = piece[j, 2 * PAIRS : 3 * PAIRS, 0:128]
    total = count * PAIRS
    q = queries[...]
    d = docs[...]
    logits = SCORE_SCALE * exact(q, d, ((1,), (1,)))
    peak = jnp.max(logits, axis=1, keepdims=True)
    powers = jnp.exp(logits - peak)
    soft = powers / jnp.sum(powers, axis=1, keepdims=True)
    col = iota((total, total), 1)
    doc_id = ((col // PAIRS) ^ me) * PAIRS + lax.rem(col, PAIRS)
    hit = marks[:, 0:1].astype(jnp.int32) == doc_id
    d_logits = (soft - jnp.where(hit, 1.0, 0.0)) * (1.0 / total)
    d_q = SCORE_SCALE * exact(d_logits[0:PAIRS, :], d, ((1,), (0,)))
    d_d = SCORE_SCALE * exact(d_logits[:, 0:128].T[0:PAIRS, :], q, ((1,), (0,)))
    d_units = jnp.concatenate([d_q, d_d], axis=0)
    units = pieces[0][0, 0 : 2 * PAIRS, :]
    d_pool = uscale[:, 0:1] * (d_units - units * jnp.sum(units * d_units, axis=1, keepdims=True))
    lane = iota((8, 2 * PAIRS), 1)
    wanted = jnp.zeros((8, 2 * PAIRS), jnp.int32)
    for j in range(2 * PAIRS):
        wanted = jnp.where(lane == j, chosen[j], wanted)
    seg = segc[:, 0 : 2 * PAIRS]
    mask = owned(place, lengths, seg)
    hot = jnp.where((seg == wanted[0:1, :]) & mask, 1.0, 0.0).astype(BF16)
    high, rest_low = low_pair(d_pool)
    dsec[...] = nn(hot, high) + nn(hot, rest_low)

    def norm(i, carry):
        scale_sum, shift_sum, bias_sum = carry
        r = aligned(i * ROWS, ROWS, ROWS)
        g = dsec[r, :]
        normed = xhat2[r, :]
        scaled = g * vec[10:11, :]
        inner = (
            scaled
            - jnp.mean(scaled, axis=1, keepdims=True)
            - normed * jnp.mean(scaled * normed, axis=1, keepdims=True)
        ) * inv2[r, 0:1]
        dsec[r, :] = inner
        dlow[r, :] = inner.astype(BF16)
        return (
            scale_sum + jnp.sum((g * normed).reshape(ROWS // 8, 8, D), axis=0),
            shift_sum + jnp.sum(g.reshape(ROWS // 8, 8, D), axis=0),
            bias_sum + jnp.sum(inner.reshape(ROWS // 8, 8, D), axis=0),
        )

    zero = jnp.zeros((8, D), F32)
    scale_sum, shift_sum, bias_sum = lax.fori_loop(0, WIN // ROWS, norm, (zero, zero, zero))
    sums[0:1, :] = jnp.sum(bias_sum, axis=0, keepdims=True)
    sums[1:2, :] = jnp.sum(scale_sum, axis=0, keepdims=True)
    sums[2:3, :] = jnp.sum(shift_sum, axis=0, keepdims=True)
    sums[3:8, :] = jnp.zeros((5, D), F32)
    for c in range(4):
        cols = slice(c * D, (c + 1) * D)
        grad[...] = tn(dlow[...], act[:, cols])
        split_rows(grad, keep, send, c ^ plane, opt)
    for c in range(4):
        cols = slice(c * D, (c + 1) * D)
        dup[:, cols] = (nn(dlow[...], wd[:, cols]) * slope[:, cols]).astype(BF16)


def down_backward(count, place, lengths, chosen, segc, uscale, saved, vec, halves, pieces):
    total = count * PAIRS
    return call(
        functools.partial(down_kernel, count),
        [(1, place), (1, lengths), (1, chosen), (0, segc), (0, uscale)]
        + [(0, s) for s in saved]
        + [(0, vec)]
        + [(0, h) for h in halves]
        + [(0, p) for p in pieces],
        [
            ((WIN, D), F32),
            ((WIN, FF), BF16),
            ((4, HALF, D), BF16),
            ((4, HALF, D), BF16),
            ((8, D), F32),
        ],
        [
            pltpu.VMEM((total, D), F32),
            pltpu.VMEM((total, D), F32),
            pltpu.VMEM((total, 128), F32),
            pltpu.VMEM((D, FF), BF16),
            pltpu.VMEM((WIN, D), BF16),
            pltpu.VMEM((D, D), F32),
        ],
        flops=4 * WIN * D * FF,
        name="down_backward",
    )


def up_kernel(
    place, dup, dsec, hlow, xhat1, inv1, att, vec, wu_own, wu_other, wo_own, wo_other,
    dfirst, datt, delta, keep, send, okeep, osend, sums, wu, wo, grad, dlow,
):
    opt, plane = place[0], place[1]
    assemble(wu, wu_own, wu_other, opt)
    assemble(wo, wo_own, wo_other, opt)
    for c in range(4):
        cols = slice(c * D, (c + 1) * D)
        part = dup[:, cols]
        grad[...] = tn(hlow[...], part)
        split_rows(grad, keep, send, c ^ plane, opt)
        sums[c : c + 1, :] = jnp.sum(part.astype(F32), axis=0, keepdims=True)
    dfirst[...] = nt(dup[...], wu[...])

    def norm(i, carry):
        scale_sum, shift_sum, bias_sum = carry
        r = aligned(i * ROWS, ROWS, ROWS)
        g = dfirst[r, :] + dsec[r, :]
        normed = xhat1[r, :]
        scaled = g * vec[8:9, :]
        inner = (
            scaled
            - jnp.mean(scaled, axis=1, keepdims=True)
            - normed * jnp.mean(scaled * normed, axis=1, keepdims=True)
        ) * inv1[r, 0:1]
        dfirst[r, :] = inner
        dlow[r, :] = inner.astype(BF16)
        return (
            scale_sum + jnp.sum((g * normed).reshape(ROWS // 8, 8, D), axis=0),
            shift_sum + jnp.sum(g.reshape(ROWS // 8, 8, D), axis=0),
            bias_sum + jnp.sum(inner.reshape(ROWS // 8, 8, D), axis=0),
        )

    zero = jnp.zeros((8, D), F32)
    scale_sum, shift_sum, bias_sum = lax.fori_loop(0, WIN // ROWS, norm, (zero, zero, zero))
    sums[4:5, :] = jnp.sum(bias_sum, axis=0, keepdims=True)
    sums[5:6, :] = jnp.sum(scale_sum, axis=0, keepdims=True)
    sums[6:7, :] = jnp.sum(shift_sum, axis=0, keepdims=True)
    sums[7:8, :] = jnp.zeros((1, D), F32)
    grad[...] = tn(att[...], dlow[...])
    okeep[...] = grad[aligned(HALF * opt, HALF, 64), :].astype(BF16)
    osend[...] = grad[aligned(HALF * (1 - opt), HALF, 64), :].astype(BF16)
    da = nt(dlow[...], wo[...]).astype(BF16)
    datt[0:WIN, :] = da
    datt[WIN:PAD, :] = jnp.zeros((PAD - WIN, D), BF16)
    high, rest = low_pair(da.astype(F32) * att[...].astype(F32))
    heads = (iota((16, D), 1) // HD == iota((16, D), 0)).astype(F32).astype(BF16)
    delta[:, 0:WIN] = nt(heads, high) + nt(heads, rest)
    delta[:, WIN:PAD] = jnp.zeros((16, PAD - WIN), F32)


def up_backward(place, dup, dsec, hlow, xhat1, inv1, att, vec, halves):
    return call(
        up_kernel,
        [(1, place)] + [(0, a) for a in (dup, dsec, hlow, xhat1, inv1, att, vec) + tuple(halves)],
        [
            ((WIN, D), F32),
            ((PAD, D), BF16),
            ((16, PAD), F32),
            ((4, HALF, D), BF16),
            ((4, HALF, D), BF16),
            ((HALF, D), BF16),
            ((HALF, D), BF16),
            ((8, D), F32),
        ],
        [
            pltpu.VMEM((D, FF), BF16),
            pltpu.VMEM((D, D), BF16),
            pltpu.VMEM((D, D), F32),
            pltpu.VMEM((WIN, D), BF16),
        ],
        flops=4 * WIN * D * (FF + D),
        name="up_backward",
    )


def heads_kernel(g, proj, datt, lse, delta, segc, segr, dproj, kt, dk, dv):
    def lanes(part):
        return slice(part * D + 128 * g, part * D + 128 * g + 128)

    for t in range(PAD // 128):
        kt[:, 128 * t : 128 * t + 128] = (
            proj[128 * t : 128 * t + 128, lanes(1)].astype(F32).T.astype(BF16)
        )
    dk[...] = jnp.zeros_like(dk)
    dv[...] = jnp.zeros_like(dv)
    for q0, k0, k1 in BANDS:
        qs = head_stack(proj[q0 : q0 + BLOCK, lanes(0)])
        gs = head_stack(datt[q0 : q0 + BLOCK, lanes(0)])
        st = nt(proj[k0:k1, lanes(1)], qs)
        dp = nt(proj[k0:k1, lanes(2)], gs)
        same = segc[k0:k1, :] == segr[0:1, q0 : q0 + BLOCK]
        bias = jnp.where(same, 0.0, NEG_BIG)
        probs, d_scores, dq = [], [], []
        for j in range(4):
            cols = slice(j * BLOCK, (j + 1) * BLOCK)
            prob = jnp.exp2(st[:, cols] * EXP2_SCALE + bias - lse[g, j : j + 1, q0 : q0 + BLOCK])
            ds = prob * (dp[:, cols] - delta[4 * g + j : 4 * g + j + 1, q0 : q0 + BLOCK])
            ds = ds.astype(BF16)
            probs.append(prob.astype(BF16))
            d_scores.append(ds)
            dq.append(nn(kt[j * HD : (j + 1) * HD, k0:k1], ds))
        dv[k0:k1, :] += nn(jnp.concatenate(probs, axis=1), gs)
        dk[k0:k1, :] += nn(jnp.concatenate(d_scores, axis=1), qs)
        rows = min(BLOCK, WIN - q0)
        dqs = jnp.concatenate(dq, axis=0).T[0:rows] * HD ** (-0.5)
        dproj[q0 : q0 + rows, 0:128] = dqs.astype(BF16)
    dproj[:, 128:256] = (dk[...] * HD ** (-0.5)).astype(BF16)
    dproj[:, 256:384] = dv[...].astype(BF16)


def heads_backward(g, proj, datt, lse, delta, segc, segr):
    return call(
        functools.partial(heads_kernel, g),
        [(0, a) for a in (proj, datt, lse, delta, segc, segr)],
        [((WIN, D), BF16)],
        [
            pltpu.VMEM((128, PAD), BF16),
            pltpu.VMEM((WIN, 128), F32),
            pltpu.VMEM((WIN, 128), F32),
        ],
        flops=10 * 4 * WIN * 384 * 128,
        name="heads_backward",
    )[0]


def input_kernel(
    place, tokens, dp0, dp1, dp2, dfirst, okeep, osend, dsums, usums, w_own, w_other,
    keep, send, igrad, wfull, dproj, grad,
):
    opt, plane = place[0], place[1]
    assemble(wfull, w_own, w_other, opt)
    for g, part in enumerate((dp0, dp1, dp2)):
        for c in range(3):
            dproj[:, c * D + 128 * g : c * D + 128 * g + 128] = part[:, 128 * c : 128 * c + 128]
    x = tokens[aligned(OFF * opt, WIN, 64), :]
    for c in range(3):
        grad[...] = tn(x, dproj[:, c * D : (c + 1) * D])
        split_rows(grad, keep, send, c ^ plane, opt)
    keep[3 ^ plane, 0:HALF, :] = okeep[...]
    send[3 ^ plane, 0:HALF, :] = osend[...]
    q_sum = jnp.sum(dproj[:, 0:D].astype(F32), axis=0, keepdims=True)
    v_sum = jnp.sum(dproj[:, 2 * D : 3 * D].astype(F32), axis=0, keepdims=True)
    rows = jnp.concatenate(
        [
            q_sum,
            v_sum,
            usums[4:5, :],
            usums[0:4, :],
            dsums[0:1, :],
            usums[5:7, :],
            dsums[1:3, :],
            jnp.zeros((4, D), F32),
        ],
        axis=0,
    ).astype(BF16)
    for c in range(4):
        keep[c, HALF : HALF + 16, :] = rows
        send[c, HALF : HALF + 16, :] = rows
    igrad[...] = (nt(dproj[...], wfull[...]) + dfirst[...]).astype(BF16)


def input_backward(place, tokens, parts, dfirst, okeep, osend, dsums, usums, w_own, w_other):
    return call(
        input_kernel,
        [(1, place), (0, tokens)]
        + [(0, a) for a in tuple(parts) + (dfirst, okeep, osend, dsums, usums, w_own, w_other)],
        [((4, HALF + 16, D), BF16), ((4, HALF + 16, D), BF16), ((WIN, D), BF16)],
        [
            pltpu.VMEM((D, 3 * D), BF16),
            pltpu.VMEM((WIN, 3 * D), BF16),
            pltpu.VMEM((D, D), F32),
        ],
        flops=4 * WIN * D * 3 * D,
        name="input_backward",
    )


def flips(axis, size, bits):
    return [(i, i ^ bits) for i in range(size)]


def swap(value, axis, size, bits):
    return lax.ppermute(value, axis, flips(axis, size, bits))


def bit_groups(size):
    bits = size.bit_length() - 1
    return [(s, 1 << min(2, bits - s)) for s in range(0, bits, 2)]


def pair_sum_kernel(keep, other, *outs):
    for r, out in enumerate(outs):
        out[...] = (keep[r].astype(F32) + other[r].astype(F32)).astype(BF16)


def plane_sum_kernel(place, a, b, c, d, *rest):
    outs, scr = rest[:4], rest[4]
    z = place[3]
    scr[...] = (a[...].astype(F32) + b[...].astype(F32)) + (
        c[...].astype(F32) + d[...].astype(F32)
    )
    for k, out in enumerate(outs):
        out[0:48, :] = scr[aligned(48 * (z ^ k), 48, 16), :].astype(BF16)
        if out.shape[0] > 48:
            out[48:64, :] = scr[HALF : HALF + 16, :].astype(BF16)


def line_sum_kernel(a, b, c, d, out):
    out[...] = (
        (a[...].astype(F32) + b[...].astype(F32)) + (c[...].astype(F32) + d[...].astype(F32))
    ).astype(BF16)


def reduce_rows(place, keep, send, n):
    rows = keep.shape[1]
    piece = rows - 3 * 48
    groups = bit_groups(n)
    other = swap(send, "opt", 2, 1)
    mine = call(
        pair_sum_kernel,
        [(0, keep), (0, other)],
        [((rows, D), BF16)] * 4,
        name="pair_sum",
    )
    got = [mine[0]] + [swap(mine[r], "dp", n, r << groups[0][0]) for r in (1, 2, 3)]
    pieces = call(
        plane_sum_kernel,
        [(1, place)] + [(0, a) for a in got],
        [((piece, D), BF16)] * 4,
        [pltpu.VMEM((rows, D), F32)],
        name="plane_sum",
    )
    got = [pieces[0]] + [swap(pieces[k], "dp", n, k << groups[1][0]) for k in (1, 2, 3)]
    final = call(line_sum_kernel, [(0, a) for a in got], [((piece, D), BF16)], name="line_sum")[0]
    for shift, size in groups[2:]:
        for b in range(size.bit_length() - 1):
            final = final + swap(final, "dp", n, 1 << (shift + b))
    return final


def spread_rows(final, n):
    groups = bit_groups(n)
    own = final[0:48]
    line = jnp.stack([own] + [swap(own, "dp", n, k << groups[1][0]) for k in (1, 2, 3)])
    return [line] + [swap(line, "dp", n, r << groups[0][0]) for r in (1, 2, 3)]


def squares_kernel(place, a, b, c, out):
    def fold(ref):
        v = ref[0:48, :].astype(F32)
        v = v * v
        s = jnp.sum(v.reshape(6, 8, D), axis=0)
        return s[:, 0:128] + s[:, 128:256] + s[:, 256:384]

    v = a[48:64, :].astype(F32)
    row = iota((16, D), 0)
    low_row = 6 * place[0]
    once = (row >= low_row) & (row < low_row + 6) & (place[2] == 0)
    v = jnp.where(once, v * v, 0.0)
    s = v[0:8] + v[8:16]
    out[...] = fold(a) + fold(b) + fold(c) + (s[:, 0:128] + s[:, 128:256] + s[:, 256:384])


def sum_all(value, n):
    value = value + swap(value, "opt", 2, 1)
    for shift, size in bit_groups(n):
        got = [value] + [swap(value, "dp", n, k << shift) for k in range(1, size)]
        while len(got) > 1:
            got = [got[i] + got[i + 1] for i in range(0, len(got), 2)]
        value = got[0]
    return value


def adamw(parameter, first_state, second, clipped, rate):
    first_new = BETA_ONE * first_state + (1.0 - BETA_ONE) * clipped
    second_new = BETA_TWO * second + (1.0 - BETA_TWO) * clipped * clipped
    direction = (first_new * (1.0 / (1.0 - BETA_ONE**STEP))) / (
        jnp.sqrt(second_new * (1.0 / (1.0 - BETA_TWO**STEP))) + ADAM_EPS
    )
    return parameter - rate * (direction + DECAY_RATE * parameter), first_new, second_new


def adamw_kernel(
    place, squares, vgrad, w, m, v, pv, pm, pq, *rest,
):
    blocks, (nw, nm, nv, nlow, npv, npm, npq, norm, gscr) = rest[:12], rest[12:]
    step = pl.program_id(0)
    opt, z = place[0], place[3]
    total = jnp.sum(jnp.sum(squares[...], axis=1, keepdims=True), axis=0, keepdims=True)
    grad_norm = jnp.sqrt(total)
    factor = jnp.minimum(1.0, CLIP_NORM / (grad_norm + 1e-06))
    for t, block in enumerate(blocks):

        @pl.when(step == t)
        def load(block=block):
            for k in range(4):
                gscr[aligned(48 * (z ^ k), 48, 16), :] = block[k].astype(F32)

    nw_new, nm_new, nv_new = adamw(w[...], m[...], v[...], gscr[...] * factor, LEARN_RATE)
    nw[...] = nw_new
    nm[...] = nm_new
    nv[...] = nv_new
    nlow[...] = nw_new.astype(BF16)

    @pl.when(step == 0)
    def small():
        norm[...] = grad_norm
        g = vgrad[48:64, :].astype(F32)
        g = jnp.where(opt == 0, g[0:6], g[6:12])
        a, b, c = adamw(pv[...], pm[...], pq[...], g * factor, VECTOR_RATE)
        npv[...] = a
        npm[...] = b
        npq[...] = c


def update(place, squares, vgrad, w, m, v, pv, pm, pq, blocks):
    def column(step, place):
        return (0, (step // 4) * 4 + (lax.rem(step, 4) ^ place[1]))

    wide = pl.BlockSpec((HALF, D), column)

    def whole(a):
        zeros = (0,) * a.ndim
        return pl.BlockSpec(a.shape, lambda step, place: zeros)

    shapes = [
        jax.ShapeDtypeStruct(w.shape, F32),
        jax.ShapeDtypeStruct(w.shape, F32),
        jax.ShapeDtypeStruct(w.shape, F32),
        jax.ShapeDtypeStruct(w.shape, BF16),
        jax.ShapeDtypeStruct(pv.shape, F32),
        jax.ShapeDtypeStruct(pv.shape, F32),
        jax.ShapeDtypeStruct(pv.shape, F32),
        jax.ShapeDtypeStruct((1, 1), F32),
    ]
    return pl.pallas_call(
        adamw_kernel,
        grid_spec=pltpu.PrefetchScalarGridSpec(
            num_scalar_prefetch=1,
            grid=(12,),
            in_specs=[whole(squares), whole(vgrad), wide, wide, wide, whole(pv), whole(pm), whole(pq)]
            + [whole(b) for b in blocks],
            out_specs=[wide, wide, wide, wide, whole(pv), whole(pv), whole(pv), whole(shapes[-1])],
            scratch_shapes=[pltpu.VMEM((HALF, D), F32)],
        ),
        out_shape=shapes,
        compiler_params=pltpu.CompilerParams(vmem_limit_bytes=40 << 20),
        cost_estimate=pl.CostEstimate(flops=20 * w.size, bytes_accessed=26 * w.size, transcendentals=0),
        name="adamw",
    )(place, squares, vgrad, w, m, v, pv, pm, pq, *blocks)


def shards(
    n,
    tokens,
    lengths,
    query_index,
    doc_index,
    targets,
    weights,
    first_moment,
    second_moment,
    vectors,
    vec_first,
    vec_second,
):
    opt = lax.axis_index("opt")
    me = lax.axis_index("dp")
    place = jnp.stack([opt, me & 3, me, (me >> 2) & 3]).astype(jnp.int32)
    lengths = lengths.reshape(SEGS)
    chosen = jnp.concatenate([query_index, doc_index])

    extra = jnp.pad(vectors, ((0, 10), (0, 2 * D)))
    w_own = jnp.concatenate([weights[:, : 3 * D], extra], axis=0).astype(BF16)
    w_other = swap(w_own, "opt", 2, 1)
    wo_own = weights[:, 3 * D : 4 * D].astype(BF16)
    wu_own = weights[:, 4 * D : 4 * D + FF].astype(BF16)
    wd_own = weights[:, 4 * D + FF :].astype(BF16)
    wo = (wo_own, swap(wo_own, "opt", 2, 1))
    wu = (wu_own, swap(wu_own, "opt", 2, 1))
    wd = (wd_own, swap(wd_own, "opt", 2, 1))

    proj, att, lse, segc, segr, vec = attend(place, lengths, tokens, w_own, w_other)
    xhat1, inv1, hlow, act, slope, xhat2, inv2, unit, uscale = mlp(
        place, lengths, chosen, targets, att, tokens, segr, vec, wo + wu + wd
    )
    stack = (unit + swap(unit, "opt", 2, 1))[None]
    groups = bit_groups(n)
    for shift, size in groups:
        pieces = [stack] + [swap(stack, "dp", n, k << shift) for k in range(1, size)]
        if (shift, size) != groups[-1]:
            stack = jnp.concatenate(pieces, axis=0)
    dsec, dup, dkeep, dsend, dsums = down_backward(
        n, place, lengths, chosen, segc, uscale, (xhat2, inv2, act, slope), vec, wd, pieces
    )
    down_final = reduce_rows(place, dkeep, dsend, n)
    dfirst, datt, delta, ukeep, usend, okeep, osend, usums = up_backward(
        place, dup, dsec, hlow, xhat1, inv1, att, vec, wu + wo
    )
    up_final = reduce_rows(place, ukeep, usend, n)
    parts = [heads_backward(g, proj, datt, lse, delta, segc, segr) for g in range(3)]
    akeep, asend, igrad = input_backward(
        place, tokens, parts, dfirst, okeep, osend, dsums, usums, w_own, w_other
    )
    low_final = reduce_rows(place, akeep, asend, n)
    blocks = spread_rows(low_final, n) + spread_rows(up_final, n) + spread_rows(down_final, n)
    squares = call(
        squares_kernel,
        [(1, place), (0, low_final), (0, up_final), (0, down_final)],
        [((8, 128), F32)],
        name="squares",
    )[0]
    squares = sum_all(squares, n)

    iother = swap(igrad, "opt", 2, 1)
    lower = jnp.where(opt == 0, igrad, iother)
    upper = jnp.where(opt == 0, iother, igrad)
    input_grad = jnp.concatenate(
        [lower[:OFF], lower[OFF:] + upper[: WIN - OFF], upper[WIN - OFF :]], axis=0
    )
    nw, nm, nv, nlow, npv, npm, npq, norm = update(
        place, squares, low_final, weights, first_moment, second_moment,
        vectors, vec_first, vec_second, blocks,
    )
    return (norm.reshape(()), input_grad, nw, nm, nv, nlow, npv, npm, npq)


def solution(mesh):
    rows = P("opt", None)
    in_specs = (P("dp", None), P("dp", None), P("dp"), P("dp"), P("dp")) + (rows,) * 6
    out_specs = (P(), P("dp", None)) + (rows,) * 7
    n = mesh.shape["dp"]
    return jax.shard_map(
        functools.partial(shards, n),
        mesh=mesh,
        in_specs=in_specs,
        out_specs=out_specs,
        check_vma=False,
    )
```

```python
import functools

import jax
import jax.numpy as jnp
from jax import lax
from jax.experimental import pallas as pl
from jax.experimental.pallas import tpu as pltpu
from jax.sharding import PartitionSpec as P

D = 384
HEADS = 12
HD = 32
FF = 1536
SEQ = 1024
SEGS = 16
PAIRS = 8
STEP = 10

WIN = 576
OFF = SEQ - WIN
PAD = 640
BLOCK = 128
BANDS = tuple((q, max(0, q - 128), min(WIN, q + 256)) for q in range(0, WIN, BLOCK))
BAND_ROWS = tuple(sum(b[2] - b[1] for b in BANDS[:i]) for i in range(len(BANDS) + 1))
ROWS = 64

LN_EPS = 1e-06
POOL_EPS = 1e-06
SCORE_SCALE = 50.0
CLIP_NORM = 0.001
BETA_ONE = 0.9
BETA_TWO = 0.98
ADAM_EPS = 1e-08
LEARN_RATE = 0.05
VECTOR_RATE = 0.3
DECAY_RATE = 0.01
NEG_BIG = -1e30
HALF = D // 2
EXP2_SCALE = HD ** (-0.5) * 1.4426950408889634

F32 = jnp.float32
BF16 = jnp.bfloat16
VMEM = pl.BlockSpec(memory_space=pltpu.VMEM)
SMEM = pl.BlockSpec(memory_space=pltpu.SMEM)
ANY = pl.BlockSpec(memory_space=pl.ANY)


def nn(a, b):
    return jnp.dot(a, b, preferred_element_type=F32)


def nt(a, b):
    return lax.dot_general(a, b, (((1,), (1,)), ((), ())), preferred_element_type=F32)


def tn(a, b):
    return lax.dot_general(a, b, (((0,), (0,)), ((), ())), preferred_element_type=F32)


def exact(a, b, dims):
    return lax.dot_general(
        a, b, (dims, ((), ())), precision=lax.Precision.HIGHEST, preferred_element_type=F32
    )


def iota(shape, axis):
    return lax.broadcasted_iota(jnp.int32, shape, axis)


def low_pair(value):
    high = value.astype(BF16)
    return high, (value - high.astype(F32)).astype(BF16)


def aligned(start, size, unit):
    return pl.ds(pl.multiple_of(start, unit), size)


def assemble(dst, own, other, opt):
    dst[aligned(HALF * opt, HALF, 64), :] = own[0:HALF, :]
    dst[aligned(HALF * (1 - opt), HALF, 64), :] = other[0:HALF, :]


def call(kernel, ins, outs, scratch=(), micros=0, name=None, vmem=24, after=()):
    specs = [SMEM if s else VMEM for s, _ in ins] + [ANY] * len(after)
    count = len(ins)

    def body(*refs):
        kernel(*refs[:count], *refs[count + len(after) :])

    shapes = [jax.ShapeDtypeStruct(s, d) for s, d in outs]
    moved = sum(a.size * a.dtype.itemsize for _, a in ins)
    moved += sum(s.size * s.dtype.itemsize for s in shapes)
    return pl.pallas_call(
        body,
        out_shape=shapes,
        in_specs=specs,
        out_specs=[VMEM] * len(shapes),
        scratch_shapes=list(scratch),
        compiler_params=pltpu.CompilerParams(vmem_limit_bytes=vmem << 20),
        cost_estimate=pl.CostEstimate(
            flops=micros * 1100000000, bytes_accessed=moved, transcendentals=0
        ),
        name=name,
    )(*[a for _, a in ins], *after)


def head_stack(rows):
    lane_head = iota(rows.shape, 1) // HD
    zero = jnp.zeros_like(rows)
    return jnp.concatenate([jnp.where(lane_head == j, rows, zero) for j in range(4)], axis=0)


def attend_kernel(
    place, lengths, tokens, w_own, w_other, proj, att, lse, segc, segr, vec, wfull, bias, vt
):
    opt = place[0]
    assemble(wfull, w_own, w_other, opt)
    mine = w_own[HALF : HALF + 16, 0:D].astype(F32)
    others = w_other[HALF : HALF + 16, 0:D].astype(F32)
    first = opt == 0
    vec[0:6, :] = jnp.where(first, mine, others)[0:6]
    vec[6:12, :] = jnp.where(first, others, mine)[0:6]
    vec[12:16, :] = jnp.zeros((4, D), F32)

    pos_col = iota((WIN, 128), 0) + OFF * opt
    pos_row = iota((8, PAD), 1) + OFF * opt
    seg_col = jnp.zeros((WIN, 128), jnp.int32)
    seg_row = jnp.zeros((8, PAD), jnp.int32)
    bound = jnp.int32(0)
    for s in range(SEGS):
        bound = bound + lengths[s]
        seg_col = seg_col + (pos_col >= bound).astype(jnp.int32)
        seg_row = seg_row + (pos_row >= bound).astype(jnp.int32)
    segc[...] = seg_col
    segr[...] = seg_row
    for i, (q0, k0, k1) in enumerate(BANDS):
        bias[BAND_ROWS[i] : BAND_ROWS[i + 1], :] = jnp.where(
            segc[k0:k1, :] == segr[0:1, q0 : q0 + BLOCK], 0.0, NEG_BIG
        )

    x = tokens[aligned(OFF * opt, WIN, 64), :]
    for c in range(3):
        acc = nn(x, wfull[:, c * D : (c + 1) * D])
        if c != 1:
            acc = acc + vec[(0 if c == 0 else 1) : (1 if c == 0 else 2), :]
        proj[0:WIN, c * D : (c + 1) * D] = acc.astype(BF16)
    proj[WIN:PAD, :] = jnp.zeros((PAD - WIN, 3 * D), BF16)

    def group(g, carry):
        def lanes(part):
            return aligned(part * D + 128 * g, 128, 128)

        for t in range(PAD // 128):
            vt[:, 128 * t : 128 * t + 128] = (
                proj[128 * t : 128 * t + 128, lanes(2)].astype(F32).T.astype(BF16)
            )
        for i, (q0, k0, k1) in enumerate(BANDS):
            stack = head_stack(proj[q0 : q0 + BLOCK, lanes(0)])
            st = nt(proj[k0:k1, lanes(1)], stack)
            outs = []
            for j in range(4):
                t = (
                    st[:, j * BLOCK : (j + 1) * BLOCK] * EXP2_SCALE
                    + bias[BAND_ROWS[i] : BAND_ROWS[i + 1], :]
                )
                peak = jnp.max(t, axis=0, keepdims=True)
                powers = jnp.exp2(t - peak)
                total = jnp.sum(powers, axis=0, keepdims=True)
                lse[g, j : j + 1, q0 : q0 + BLOCK] = peak + jnp.log2(total)
                o = nn(vt[j * HD : (j + 1) * HD, k0:k1], powers.astype(BF16))
                outs.append(o * (1.0 / total))
            rows = min(BLOCK, WIN - q0)
            att[q0 : q0 + rows, aligned(128 * g, 128, 128)] = (
                jnp.concatenate(outs, axis=0).T[0:rows].astype(BF16)
            )
        return carry

    lax.fori_loop(0, 3, group, 0)


def attend(place, lengths, tokens, w_own, w_other):
    return call(
        attend_kernel,
        [(1, place), (1, lengths), (0, tokens), (0, w_own), (0, w_other)],
        [
            ((PAD, 3 * D), BF16),
            ((WIN, D), BF16),
            ((3, 4, PAD), F32),
            ((WIN, 128), jnp.int32),
            ((8, PAD), jnp.int32),
            ((16, D), F32),
        ],
        [
            pltpu.VMEM((D, 3 * D), BF16),
            pltpu.VMEM((BAND_ROWS[-1], 128), F32),
            pltpu.VMEM((128, PAD), BF16),
        ],
        micros=8,
        name="attend",
    )


def owned(place, lengths, segment):
    bound = jnp.int32(0)
    count = jnp.int32(0)
    for s in range(SEGS):
        bound = bound + lengths[s]
        count = count + (bound <= WIN).astype(jnp.int32)
    low_side = (segment < count).astype(jnp.int32)
    return low_side == (place[0] == 0).astype(jnp.int32)


def mlp_kernel(
    place, lengths, chosen, att, tokens, segr, vec, wo_own, wo_other, wu_own, wu_other,
    wd_own, wd_other, xhat1, inv1, hlow, act, slope, xhat2, inv2, unit, uscale,
    wo, wu, wd, tmp, hid, ench, encl,
):
    opt = place[0]
    assemble(wo, wo_own, wo_other, opt)
    assemble(wu, wu_own, wu_other, opt)
    assemble(wd, wd_own, wd_other, opt)
    tmp[...] = nn(att[...], wo[...])

    def first_norm(i, carry):
        r = aligned(i * ROWS, ROWS, ROWS)
        x = tokens[aligned(OFF * opt + i * ROWS, ROWS, ROWS), :].astype(F32)
        v = tmp[r, :] + vec[2:3, :] + x
        centred = v - jnp.mean(v, axis=1, keepdims=True)
        inverse = lax.rsqrt(jnp.mean(centred * centred, axis=1, keepdims=True) + LN_EPS)
        normed = centred * inverse
        xhat1[r, :] = normed
        inv1[r, :] = jnp.broadcast_to(inverse, (ROWS, 128))
        h = normed * vec[8:9, :] + vec[9:10, :]
        hid[r, :] = h
        hlow[r, :] = h.astype(BF16)
        return carry

    lax.fori_loop(0, WIN // ROWS, first_norm, 0)

    for c in range(4):
        cols = slice(c * D, (c + 1) * D)
        tmp[...] = nn(hlow[...], wu[:, cols])

        def gelu(i, carry, cols=cols, c=c):
            r = aligned(i * ROWS, ROWS, ROWS)
            u = tmp[r, :] + vec[3 + c : 4 + c, :]
            half = lax.erf(u * 0.7071067811865476) * 0.5 + 0.5
            act[r, cols] = (u * half).astype(BF16)
            slope[r, cols] = half + u * jnp.exp(-0.5 * u * u) * 0.3989422804014327
            return carry

        lax.fori_loop(0, WIN // ROWS, gelu, 0)

    tmp[...] = nt(act[...], wd[...])

    def second_norm(i, carry):
        r = aligned(i * ROWS, ROWS, ROWS)
        v = tmp[r, :] + vec[7:8, :] + hid[r, :]
        centred = v - jnp.mean(v, axis=1, keepdims=True)
        inverse = lax.rsqrt(jnp.mean(centred * centred, axis=1, keepdims=True) + LN_EPS)
        normed = centred * inverse
        xhat2[r, :] = normed
        inv2[r, :] = jnp.broadcast_to(inverse, (ROWS, 128))
        high, rest = low_pair(normed * vec[10:11, :] + vec[11:12, :])
        ench[r, :] = high
        encl[r, :] = rest
        return carry

    lax.fori_loop(0, WIN // ROWS, second_norm, 0)

    seg = segr[0:1, 0:WIN]
    row_id = iota((2 * PAIRS, WIN), 0)
    wanted = jnp.zeros((2 * PAIRS, WIN), jnp.int32)
    for j in range(2 * PAIRS):
        wanted = jnp.where(row_id == j, chosen[j], wanted)
    mask = owned(place, lengths, jnp.broadcast_to(seg, (2 * PAIRS, WIN)))
    onehot = jnp.where((wanted == seg) & mask, 1.0, 0.0)
    count = jnp.maximum(jnp.sum(onehot, axis=1, keepdims=True), 1.0)
    hot = onehot.astype(BF16)
    pooled = (nn(hot, ench[...]) + nn(hot, encl[...])) / count
    inverse_len = lax.rsqrt(jnp.sum(pooled * pooled, axis=1, keepdims=True) + POOL_EPS)
    unit[...] = pooled * inverse_len
    uscale[...] = jnp.broadcast_to(inverse_len / count, (2 * PAIRS, 128))


def mlp(place, lengths, chosen, att, tokens, segr, vec, halves):
    return call(
        mlp_kernel,
        [(1, place), (1, lengths), (1, chosen), (0, att), (0, tokens), (0, segr), (0, vec)]
        + [(0, h) for h in halves],
        [
            ((WIN, D), F32),
            ((WIN, 128), F32),
            ((WIN, D), BF16),
            ((WIN, FF), BF16),
            ((WIN, FF), F32),
            ((WIN, D), F32),
            ((WIN, 128), F32),
            ((2 * PAIRS, D), F32),
            ((2 * PAIRS, 128), F32),
        ],
        [
            pltpu.VMEM((D, D), BF16),
            pltpu.VMEM((D, FF), BF16),
            pltpu.VMEM((D, FF), BF16),
            pltpu.VMEM((WIN, D), F32),
            pltpu.VMEM((WIN, D), F32),
            pltpu.VMEM((WIN, D), BF16),
            pltpu.VMEM((WIN, D), BF16),
        ],
        micros=10,
        name="mlp",
    )


def turned(chunk):
    return (chunk & 1) * 2 + (chunk >> 1)


def split_rows(grad, keep, send, chunk, place):
    opt = place[0]
    straight = chunk ^ place[1]
    mine = jnp.where(opt == 0, straight, turned(straight))
    theirs = jnp.where(opt == 0, turned(straight), straight)
    keep[mine, 0:HALF, :] = grad[aligned(HALF * opt, HALF, 64), :].astype(BF16)
    send[theirs, 0:HALF, :] = grad[aligned(HALF * (1 - opt), HALF, 64), :].astype(BF16)


def column_sums(value):
    return jnp.sum(value.reshape(ROWS // 8, 8, D), axis=0)


def norm_backward(grad_at, normed_ref, inverse_ref, gain, out, low_out, sums, at):
    def block(i, carry):
        scale_sum, shift_sum, bias_sum = carry
        r = aligned(i * ROWS, ROWS, ROWS)
        g = grad_at(r)
        normed = normed_ref[r, :]
        scaled = g * gain
        inner = (
            scaled
            - jnp.mean(scaled, axis=1, keepdims=True)
            - normed * jnp.mean(scaled * normed, axis=1, keepdims=True)
        ) * inverse_ref[r, 0:1]
        out[r, :] = inner
        low_out[r, :] = inner.astype(BF16)
        return (
            scale_sum + column_sums(g * normed),
            shift_sum + column_sums(g),
            bias_sum + column_sums(inner),
        )

    zero = jnp.zeros((8, D), F32)
    scale_sum, shift_sum, bias_sum = lax.fori_loop(0, WIN // ROWS, block, (zero, zero, zero))
    sums[at : at + 1, :] = jnp.sum(bias_sum, axis=0, keepdims=True)
    sums[at + 1 : at + 2, :] = jnp.sum(scale_sum, axis=0, keepdims=True)
    sums[at + 2 : at + 3, :] = jnp.sum(shift_sum, axis=0, keepdims=True)


def down_kernel(
    count, place, lengths, chosen, marks, units, segc, uscale, xhat2, inv2, act, vec, *rest
):
    pieces, (dsec, dlow, keep, send, sums, queries, docs, grad) = rest[:-8], rest[-8:]
    me = place[2]
    per = pieces[0].shape[0]
    for p, piece in enumerate(pieces):
        for j in range(per):
            r = slice((p * per + j) * PAIRS, (p * per + j + 1) * PAIRS)
            both = piece[j].astype(F32)
            queries[r, :] = both[0:PAIRS]
            docs[r, :] = both[PAIRS : 2 * PAIRS]
    total = count * PAIRS
    q = queries[...].astype(BF16)
    d = docs[...].astype(BF16)
    logits = SCORE_SCALE * nt(q, d)
    peak = jnp.max(logits, axis=1, keepdims=True)
    powers = jnp.exp(logits - peak)
    soft = powers / jnp.sum(powers, axis=1, keepdims=True)
    col = iota((total, total), 1)
    doc_id = ((col // PAIRS) ^ me) * PAIRS + lax.rem(col, PAIRS)
    hit = marks[:, 0:1] == doc_id
    d_logits = (soft - jnp.where(hit, 1.0, 0.0)) * (SCORE_SCALE / total)
    high, rest_low = low_pair(d_logits[0:PAIRS, :])
    d_q = nn(high, d) + nn(rest_low, d)
    high, rest_low = low_pair(d_logits[:, 0:128].T[0:PAIRS, :])
    d_d = nn(high, q) + nn(rest_low, q)
    d_units = jnp.concatenate([d_q, d_d], axis=0)
    u = units[...]
    d_pool = uscale[:, 0:1] * (d_units - u * jnp.sum(u * d_units, axis=1, keepdims=True))
    lane = iota((8, 2 * PAIRS), 1)
    wanted = jnp.zeros((8, 2 * PAIRS), jnp.int32)
    for j in range(2 * PAIRS):
        wanted = jnp.where(lane == j, chosen[j], wanted)
    seg = segc[:, 0 : 2 * PAIRS]
    mask = owned(place, lengths, seg)
    hot = jnp.where((seg == wanted[0:1, :]) & mask, 1.0, 0.0).astype(BF16)
    high, rest_low = low_pair(d_pool)
    dsec[...] = nn(hot, high) + nn(hot, rest_low)
    norm_backward(lambda r: dsec[r, :], xhat2, inv2, vec[10:11, :], dsec, dlow, sums, 0)
    sums[3:8, :] = jnp.zeros((5, D), F32)
    for c in range(4):
        grad[...] = tn(dlow[...], act[:, c * D : (c + 1) * D])
        split_rows(grad, keep, send, c, place)


def down_backward(count, place, lengths, chosen, marks, units, segc, uscale, saved, vec, pieces):
    total = count * PAIRS
    return call(
        functools.partial(down_kernel, count),
        [(1, place), (1, lengths), (1, chosen), (0, marks), (0, units), (0, segc), (0, uscale)]
        + [(0, s) for s in saved]
        + [(0, vec)]
        + [(0, p) for p in pieces],
        [
            ((WIN, D), F32),
            ((WIN, D), BF16),
            ((4, HALF, D), BF16),
            ((4, HALF, D), BF16),
            ((8, D), F32),
        ],
        [
            pltpu.VMEM((total, D), F32),
            pltpu.VMEM((total, D), F32),
            pltpu.VMEM((D, D), F32),
        ],
        micros=4,
        name="down_backward",
    )


def up_kernel(place, dlow, slope, hlow, wd_own, wd_other, dup, keep, send, sums, wd, grad):
    opt = place[0]
    assemble(wd, wd_own, wd_other, opt)
    for c in range(4):
        cols = slice(c * D, (c + 1) * D)
        part = (nn(dlow[...], wd[:, cols]) * slope[:, cols]).astype(BF16)
        dup[:, cols] = part
        sums[c : c + 1, :] = jnp.sum(part.astype(F32), axis=0, keepdims=True)
        grad[...] = tn(hlow[...], dup[:, cols])
        split_rows(grad, keep, send, c, place)


def up_backward(place, dlow, slope, hlow, halves, after):
    return call(
        up_kernel,
        [(1, place)] + [(0, a) for a in (dlow, slope, hlow) + tuple(halves)],
        [((WIN, FF), BF16), ((4, HALF, D), BF16), ((4, HALF, D), BF16), ((4, D), F32)],
        [pltpu.VMEM((D, FF), BF16), pltpu.VMEM((D, D), F32)],
        micros=3,
        name="up_backward",
        after=after,
    )


def first_kernel(
    place, dup, dsec, xhat1, inv1, att, vec, wu_own, wu_other, wo_own, wo_other,
    dfirst, datt, delta, okeep, osend, sums, wu, wo, grad, dlow,
):
    opt = place[0]
    assemble(wu, wu_own, wu_other, opt)
    assemble(wo, wo_own, wo_other, opt)
    dfirst[...] = nt(dup[...], wu[...])
    norm_backward(
        lambda r: dfirst[r, :] + dsec[r, :], xhat1, inv1, vec[8:9, :], dfirst, dlow, sums, 0
    )
    sums[3:8, :] = jnp.zeros((5, D), F32)
    grad[...] = tn(att[...], dlow[...])
    okeep[...] = grad[aligned(HALF * opt, HALF, 64), :].astype(BF16)
    osend[...] = grad[aligned(HALF * (1 - opt), HALF, 64), :].astype(BF16)
    da = nt(dlow[...], wo[...]).astype(BF16)
    datt[0:WIN, :] = da
    datt[WIN:PAD, :] = jnp.zeros((PAD - WIN, D), BF16)
    high, rest = low_pair(da.astype(F32) * att[...].astype(F32))
    heads = (iota((16, D), 1) // HD == iota((16, D), 0)).astype(F32).astype(BF16)
    delta[:, 0:WIN] = nt(heads, high) + nt(heads, rest)
    delta[:, WIN:PAD] = jnp.zeros((16, PAD - WIN), F32)


def first_backward(place, dup, dsec, xhat1, inv1, att, vec, halves, after):
    return call(
        first_kernel,
        [(1, place)] + [(0, a) for a in (dup, dsec, xhat1, inv1, att, vec) + tuple(halves)],
        [
            ((WIN, D), F32),
            ((PAD, D), BF16),
            ((16, PAD), F32),
            ((HALF, D), BF16),
            ((HALF, D), BF16),
            ((8, D), F32),
        ],
        [
            pltpu.VMEM((D, FF), BF16),
            pltpu.VMEM((D, D), BF16),
            pltpu.VMEM((D, D), F32),
            pltpu.VMEM((WIN, D), BF16),
        ],
        micros=3,
        name="first_backward",
        after=after,
    )


def heads_kernel(g, proj, datt, lse, delta, segc, segr, dproj, kt, dk, dv):
    def lanes(part):
        return slice(part * D + 128 * g, part * D + 128 * g + 128)

    for t in range(PAD // 128):
        kt[:, 128 * t : 128 * t + 128] = (
            proj[128 * t : 128 * t + 128, lanes(1)].astype(F32).T.astype(BF16)
        )
    dk[...] = jnp.zeros_like(dk)
    dv[...] = jnp.zeros_like(dv)
    for q0, k0, k1 in BANDS:
        qs = head_stack(proj[q0 : q0 + BLOCK, lanes(0)])
        gs = head_stack(datt[q0 : q0 + BLOCK, lanes(0)])
        st = nt(proj[k0:k1, lanes(1)], qs)
        dp = nt(proj[k0:k1, lanes(2)], gs)
        same = segc[k0:k1, :] == segr[0:1, q0 : q0 + BLOCK]
        bias = jnp.where(same, 0.0, NEG_BIG)
        probs, d_scores, dq = [], [], []
        for j in range(4):
            cols = slice(j * BLOCK, (j + 1) * BLOCK)
            prob = jnp.exp2(st[:, cols] * EXP2_SCALE + bias - lse[g, j : j + 1, q0 : q0 + BLOCK])
            ds = prob * (dp[:, cols] - delta[4 * g + j : 4 * g + j + 1, q0 : q0 + BLOCK])
            ds = ds.astype(BF16)
            probs.append(prob.astype(BF16))
            d_scores.append(ds)
            dq.append(nn(kt[j * HD : (j + 1) * HD, k0:k1], ds))
        dv[k0:k1, :] += nn(jnp.concatenate(probs, axis=1), gs)
        dk[k0:k1, :] += nn(jnp.concatenate(d_scores, axis=1), qs)
        rows = min(BLOCK, WIN - q0)
        dqs = jnp.concatenate(dq, axis=0).T[0:rows] * HD ** (-0.5)
        dproj[q0 : q0 + rows, 0:128] = dqs.astype(BF16)
    dproj[:, 128:256] = (dk[...] * HD ** (-0.5)).astype(BF16)
    dproj[:, 256:384] = dv[...].astype(BF16)


def heads_backward(g, proj, datt, lse, delta, segc, segr, after):
    return call(
        functools.partial(heads_kernel, g),
        [(0, a) for a in (proj, datt, lse, delta, segc, segr)],
        [((WIN, D), BF16)],
        [
            pltpu.VMEM((128, PAD), BF16),
            pltpu.VMEM((WIN, 128), F32),
            pltpu.VMEM((WIN, 128), F32),
        ],
        micros=3,
        name="heads_backward",
        after=after,
    )[0]


def input_kernel(
    place, tokens, dp0, dp1, dp2, dfirst, okeep, osend, dsums, usums, fsums, w_own, w_other,
    keep, send, igrad, wfull, dproj, grad,
):
    opt, plane = place[0], place[1]
    assemble(wfull, w_own, w_other, opt)
    for g, part in enumerate((dp0, dp1, dp2)):
        for c in range(3):
            dproj[:, c * D + 128 * g : c * D + 128 * g + 128] = part[:, 128 * c : 128 * c + 128]
    x = tokens[aligned(OFF * opt, WIN, 64), :]
    for c in range(3):
        grad[...] = tn(x, dproj[:, c * D : (c + 1) * D])
        split_rows(grad, keep, send, c, place)
    straight = 3 ^ plane
    keep[jnp.where(opt == 0, straight, turned(straight)), 0:HALF, :] = okeep[...]
    send[jnp.where(opt == 0, turned(straight), straight), 0:HALF, :] = osend[...]
    q_sum = jnp.sum(dproj[:, 0:D].astype(F32), axis=0, keepdims=True)
    v_sum = jnp.sum(dproj[:, 2 * D : 3 * D].astype(F32), axis=0, keepdims=True)
    rows = jnp.concatenate(
        [
            q_sum,
            v_sum,
            fsums[0:1, :],
            usums[0:4, :],
            dsums[0:1, :],
            fsums[1:3, :],
            dsums[1:3, :],
            jnp.zeros((4, D), F32),
        ],
        axis=0,
    ).astype(BF16)
    for c in range(4):
        keep[c, HALF : HALF + 16, :] = rows
        send[c, HALF : HALF + 16, :] = rows
    igrad[...] = (nt(dproj[...], wfull[...]) + dfirst[...]).astype(BF16)


def input_backward(place, tokens, parts, dfirst, okeep, osend, sums, w_own, w_other, after):
    return call(
        input_kernel,
        [(1, place), (0, tokens)]
        + [(0, a) for a in tuple(parts) + (dfirst, okeep, osend) + sums + (w_own, w_other)],
        [((4, HALF + 16, D), BF16), ((4, HALF + 16, D), BF16), ((WIN, D), BF16)],
        [
            pltpu.VMEM((D, 3 * D), BF16),
            pltpu.VMEM((WIN, 3 * D), BF16),
            pltpu.VMEM((D, D), F32),
        ],
        micros=3,
        name="input_backward",
        after=after,
    )


def flips(axis, size, bits):
    return [(i, i ^ bits) for i in range(size)]


def swap(value, axis, size, bits):
    return lax.ppermute(value, axis, flips(axis, size, bits))


def bit_groups(size):
    bits = size.bit_length() - 1
    return [(s, 1 << min(2, bits - s)) for s in range(0, bits, 2)]


def cross(value, n, first):
    pairs = []
    for i in range(n):
        for core in range(2):
            bit = 1 if (core == 0) == first else 2
            pairs.append((2 * i + core, 2 * (i ^ bit) + core))
    return lax.ppermute(value, ("dp", "opt"), pairs)


def added(a, b):
    return (a.astype(F32) + b.astype(F32)).astype(BF16)


def pair_sum_kernel(keep, other, stay, go):
    for half in range(2):
        stay[half] = added(keep[2 * half], other[2 * half])
        go[half] = added(keep[2 * half + 1], other[2 * half + 1])


def first_sum_kernel(stay, other, keep, send):
    keep[...] = added(stay[0], other[0])
    send[...] = added(stay[1], other[1])


def second_sum_kernel(place, keep, other, *rest):
    outs, scr = rest[:4], rest[4]
    z = place[3]
    scr[...] = keep[...].astype(F32) + other[...].astype(F32)
    for k, out in enumerate(outs):
        out[0:48, :] = scr[aligned(48 * (z ^ k), 48, 16), :].astype(BF16)
        if out.shape[0] > 48:
            out[48:64, :] = scr[HALF : HALF + 16, :].astype(BF16)


def line_sum_kernel(a, b, c, d, out):
    out[...] = (
        (a[...].astype(F32) + b[...].astype(F32)) + (c[...].astype(F32) + d[...].astype(F32))
    ).astype(BF16)


def pair_sum(keep, other):
    half = ((2,) + keep.shape[1:], BF16)
    return call(pair_sum_kernel, [(0, keep), (0, other)], [half, half], name="pair_sum", vmem=8)


def first_sum(stay, other):
    one = (stay.shape[1:], BF16)
    return call(first_sum_kernel, [(0, stay), (0, other)], [one, one], name="first_sum", vmem=8)


def second_sum(place, keep, other):
    rows = keep.shape[0]
    return call(
        second_sum_kernel,
        [(1, place), (0, keep), (0, other)],
        [((rows - 3 * 48, D), BF16)] * 4,
        [pltpu.VMEM((rows, D), F32)],
        name="second_sum",
        vmem=8,
    )


def line_swaps(values, n):
    shift = bit_groups(n)[1][0]
    return [swap(values[k], "dp", n, k << shift) for k in (1, 2, 3)]


def line_sum(mine, got, n):
    final = call(
        line_sum_kernel,
        [(0, a) for a in [mine] + got],
        [(mine.shape, BF16)],
        name="line_sum",
        vmem=8,
    )[0]
    for shift, size in bit_groups(n)[2:]:
        for b in range(size.bit_length() - 1):
            final = final + swap(final, "dp", n, 1 << (shift + b))
    return final


def squares_kernel(place, a, b, c, out):
    def fold(ref):
        v = ref[0:48, :].astype(F32)
        v = v * v
        s = jnp.sum(v.reshape(6, 8, D), axis=0)
        return s[:, 0:128] + s[:, 128:256] + s[:, 256:384]

    v = a[48:64, :].astype(F32)
    row = iota((16, D), 0)
    low_row = 6 * place[0]
    once = (row >= low_row) & (row < low_row + 6) & (place[2] == 0)
    v = jnp.where(once, v * v, 0.0)
    s = v[0:8] + v[8:16]
    out[...] = fold(a) + fold(b) + fold(c) + (s[:, 0:128] + s[:, 128:256] + s[:, 256:384])


def sum_all(value, n):
    value = value + swap(value, "opt", 2, 1)
    for shift, size in bit_groups(n):
        got = [value] + [swap(value, "dp", n, k << shift) for k in range(1, size)]
        while len(got) > 1:
            got = [got[i] + got[i + 1] for i in range(0, len(got), 2)]
        value = got[0]
    return value


def adamw(parameter, first_state, second, clipped, rate):
    first_new = BETA_ONE * first_state + (1.0 - BETA_ONE) * clipped
    second_new = BETA_TWO * second + (1.0 - BETA_TWO) * clipped * clipped
    direction = (first_new * (1.0 / (1.0 - BETA_ONE**STEP))) / (
        jnp.sqrt(second_new * (1.0 / (1.0 - BETA_TWO**STEP))) + ADAM_EPS
    )
    return parameter - rate * (direction + DECAY_RATE * parameter), first_new, second_new


def adamw_kernel(place, squares, vgrad, w, m, v, pv, pm, pq, *rest):
    blocks, rest = rest[:12], rest[12:]
    outs, (npv, npm, npq, norm), scrs, (gscr, sems) = rest[:4], rest[4:8], rest[8:12], rest[12:]
    opt, z = place[0], place[3]
    total = jnp.sum(jnp.sum(squares[...], axis=1, keepdims=True), axis=0, keepdims=True)
    grad_norm = jnp.sqrt(total)
    factor = jnp.minimum(1.0, CLIP_NORM / (grad_norm + 1e-06))
    norm[...] = grad_norm
    g = vgrad[48:64, :].astype(F32)
    g = jnp.where(opt == 0, g[0:6], g[6:12])
    a, b, c = adamw(pv[...], pm[...], pq[...], g * factor, VECTOR_RATE)
    npv[...] = a
    npm[...] = b
    npq[...] = c
    copies = []
    for t, block in enumerate(blocks):
        at = aligned(D * (4 * (t // 4) + place[4 + t % 4]), D, 128)
        for k in range(4):
            gscr[aligned(48 * (z ^ k), 48, 16), :] = block[k].astype(F32)

        def rows(i, carry, at=at):
            r = aligned(i * 16, 16, 16)
            new_w, new_m, new_v = adamw(
                w[r, at], m[r, at], v[r, at], gscr[r, :] * factor, LEARN_RATE
            )
            for scr, value in zip(scrs, (new_w, new_m, new_v, new_w.astype(BF16))):
                scr[r, at] = value
            return carry

        lax.fori_loop(0, HALF // 16, rows, 0)
        for i, (scr, out) in enumerate(zip(scrs, outs)):
            copy = pltpu.make_async_copy(scr.at[:, at], out.at[:, at], sems.at[t, i])
            copy.start()
            copies.append(copy)
    for copy in copies:
        copy.wait()


def update(place, squares, vgrad, w, m, v, pv, pm, pq, blocks):
    ins = (squares, vgrad, w, m, v, pv, pm, pq) + tuple(blocks)
    shapes = [(w.shape, F32)] * 3 + [(w.shape, BF16)] + [(pv.shape, F32)] * 3 + [((1, 1), F32)]
    return pl.pallas_call(
        adamw_kernel,
        out_shape=[jax.ShapeDtypeStruct(s, d) for s, d in shapes],
        in_specs=[SMEM] + [VMEM] * len(ins),
        out_specs=[ANY] * 4 + [VMEM] * 4,
        scratch_shapes=[
            pltpu.VMEM(w.shape, F32),
            pltpu.VMEM(w.shape, F32),
            pltpu.VMEM(w.shape, F32),
            pltpu.VMEM(w.shape, BF16),
            pltpu.VMEM((HALF, D), F32),
            pltpu.SemaphoreType.DMA((12, 4)),
        ],
        compiler_params=pltpu.CompilerParams(vmem_limit_bytes=20 << 20),
        cost_estimate=pl.CostEstimate(
            flops=4000000000, bytes_accessed=26 * w.size, transcendentals=0
        ),
        name="adamw",
    )(place, *ins)


def shards(
    n,
    tokens,
    lengths,
    query_index,
    doc_index,
    targets,
    weights,
    first_moment,
    second_moment,
    vectors,
    vec_first,
    vec_second,
):
    opt = lax.axis_index("opt")
    me = lax.axis_index("dp")
    plane = me & 3
    columns = [jnp.where(opt == 0, plane ^ r, plane ^ turned(r)) for r in range(4)]
    place = jnp.stack([opt, plane, me, (me >> 2) & 3] + columns).astype(jnp.int32)
    lengths = lengths.reshape(SEGS)
    chosen = jnp.concatenate([query_index, doc_index])
    groups = bit_groups(n)

    extra = jnp.pad(vectors, ((0, 10), (0, 2 * D)))
    w_own = jnp.concatenate([weights[:, : 3 * D], extra], axis=0).astype(BF16)
    w_other = swap(w_own, "opt", 2, 1)
    wo_own = weights[:, 3 * D : 4 * D].astype(BF16)
    wu_own = weights[:, 4 * D : 4 * D + FF].astype(BF16)
    wd_own = weights[:, 4 * D + FF :].astype(BF16)
    wo = (wo_own, swap(wo_own, "opt", 2, 1))
    wu = (wu_own, swap(wu_own, "opt", 2, 1))
    wd = (wd_own, swap(wd_own, "opt", 2, 1))
    marks = targets[None]
    for shift, size in groups:
        marks = jnp.concatenate(
            [marks] + [swap(marks, "dp", n, k << shift) for k in range(1, size)], axis=0
        )
    marks = jnp.broadcast_to(marks.reshape(n * PAIRS, 1), (n * PAIRS, 128))

    proj, att, lse, segc, segr, vec = attend(place, lengths, tokens, w_own, w_other)
    xhat1, inv1, hlow, act, slope, xhat2, inv2, unit, uscale = mlp(
        place, lengths, chosen, att, tokens, segr, vec, wo + wu + wd
    )
    units = unit + swap(unit, "opt", 2, 1)
    stack = units.astype(BF16)[None]
    for shift, size in groups:
        pieces = [stack] + [swap(stack, "dp", n, k << shift) for k in range(1, size)]
        if (shift, size) != groups[-1]:
            stack = jnp.concatenate(pieces, axis=0)
    dsec, dlow, keep, send, dsums = down_backward(
        n, place, lengths, chosen, marks, units, segc, uscale, (xhat2, inv2, act), vec, pieces
    )
    d_other = swap(send, "opt", 2, 1)
    dup, ukeep, usend, usums = up_backward(place, dlow, slope, hlow, wd, [])
    u_other = swap(usend, "opt", 2, 1)
    stay, go = pair_sum(keep, d_other)
    d_other = cross(go, n, True)
    dfirst, datt, delta, okeep, osend, fsums = first_backward(
        place, dup, dsec, xhat1, inv1, att, vec, wu + wo, [stay]
    )
    keep, send = first_sum(stay, d_other)
    d_other = cross(send, n, False)
    ustay, go = pair_sum(ukeep, u_other)
    u_other = cross(go, n, True)
    heads = (proj, datt, lse, delta, segc, segr)
    part0 = heads_backward(0, *heads, [keep, ustay])
    d_parts = second_sum(place, keep, d_other)
    d_got = line_swaps(d_parts, n)
    ukeep, send = first_sum(ustay, u_other)
    u_other = cross(send, n, False)
    part1 = heads_backward(1, *heads, [d_parts[0], ukeep, part0])
    down_final = line_sum(d_parts[0], d_got, n)
    d_line = line_swaps([down_final] * 4, n)
    u_parts = second_sum(place, ukeep, u_other)
    u_got = line_swaps(u_parts, n)
    part2 = heads_backward(2, *heads, [down_final, u_parts[0], part1])
    d_line = jnp.stack([down_final] + d_line)
    d_plane = cross(d_line, n, False)
    up_final = line_sum(u_parts[0], u_got, n)
    u_line = line_swaps([up_final] * 4, n)
    keep, send, igrad = input_backward(
        place, tokens, (part0, part1, part2), dfirst, okeep, osend, (dsums, usums, fsums), w_own,
        w_other, [d_line, up_final],
    )
    a_other = swap(send, "opt", 2, 1)
    d_plane = jnp.stack([d_line, d_plane])
    d_far = cross(d_plane, n, True)
    u_line = jnp.stack([up_final] + u_line)
    u_plane = cross(u_line, n, False)
    stay, go = pair_sum(keep, a_other)
    a_other = cross(go, n, True)
    iother = swap(igrad, "opt", 2, 1)
    keep, send = first_sum(stay, a_other)
    a_other = cross(send, n, False)
    u_plane = jnp.stack([u_line, u_plane])
    u_far = cross(u_plane, n, True)
    a_parts = second_sum(place, keep, a_other)
    low_final = line_sum(a_parts[0], line_swaps(a_parts, n), n)
    own = low_final[0:48]
    a_line = jnp.stack([own] + line_swaps([own] * 4, n))
    squares = call(
        squares_kernel,
        [(1, place), (0, low_final), (0, up_final), (0, down_final)],
        [((8, 128), F32)],
        name="squares",
        vmem=8,
    )[0]
    squares = sum_all(squares, n)
    a_plane = jnp.stack([a_line, cross(a_line, n, False)])
    a_far = cross(a_plane, n, True)
    blocks = []
    for near, far in ((a_plane, a_far), (u_plane, u_far), (d_plane, d_far)):
        blocks += [near[0], far[0], near[1], far[1]]

    lower = jnp.where(opt == 0, igrad, iother)
    upper = jnp.where(opt == 0, iother, igrad)
    input_grad = jnp.concatenate(
        [lower[:OFF], lower[OFF:] + upper[: WIN - OFF], upper[WIN - OFF :]], axis=0
    )
    nw, nm, nv, nlow, npv, npm, npq, norm = update(
        place, squares, low_final, weights, first_moment, second_moment,
        vectors, vec_first, vec_second, blocks,
    )
    return (norm.reshape(()), input_grad, nw, nm, nv, nlow, npv, npm, npq)


def solution(mesh):
    rows = P("opt", None)
    in_specs = (P("dp", None), P("dp", None), P("dp"), P("dp"), P("dp")) + (rows,) * 6
    out_specs = (P(), P("dp", None)) + (rows,) * 7
    n = mesh.shape["dp"]
    return jax.shard_map(
        functools.partial(shards, n),
        mesh=mesh,
        in_specs=in_specs,
        out_specs=out_specs,
        check_vma=False,
    )
```

```python
import functools

import jax
import jax.numpy as jnp
from jax import lax
from jax.experimental import pallas as pl
from jax.experimental.pallas import tpu as pltpu
from jax.sharding import PartitionSpec as P

D = 384
HEADS = 12
HD = 32
FF = 1536
SEQ = 1024
SEGS = 16
PAIRS = 8
STEP = 10

WIN = 576
OFF = SEQ - WIN
PAD = 640
BLOCK = 128
BANDS = tuple((q, max(0, q - 128), min(WIN, q + 256)) for q in range(0, WIN, BLOCK))
BAND_ROWS = tuple(sum(b[2] - b[1] for b in BANDS[:i]) for i in range(len(BANDS) + 1))
ROWS = 64

LN_EPS = 1e-06
POOL_EPS = 1e-06
SCORE_SCALE = 50.0
CLIP_NORM = 0.001
BETA_ONE = 0.9
BETA_TWO = 0.98
ADAM_EPS = 1e-08
LEARN_RATE = 0.05
VECTOR_RATE = 0.3
DECAY_RATE = 0.01
NEG_BIG = -1e30
HALF = D // 2
EXP2_SCALE = HD ** (-0.5) * 1.4426950408889634

F32 = jnp.float32
BF16 = jnp.bfloat16
VMEM = pl.BlockSpec(memory_space=pltpu.VMEM)
SMEM = pl.BlockSpec(memory_space=pltpu.SMEM)
ANY = pl.BlockSpec(memory_space=pl.ANY)


def nn(a, b):
    return jnp.dot(a, b, preferred_element_type=F32)


def nt(a, b):
    return lax.dot_general(a, b, (((1,), (1,)), ((), ())), preferred_element_type=F32)


def tn(a, b):
    return lax.dot_general(a, b, (((0,), (0,)), ((), ())), preferred_element_type=F32)


def exact(a, b, dims):
    return lax.dot_general(
        a, b, (dims, ((), ())), precision=lax.Precision.HIGHEST, preferred_element_type=F32
    )


def iota(shape, axis):
    return lax.broadcasted_iota(jnp.int32, shape, axis)


def low_pair(value):
    high = value.astype(BF16)
    return high, (value - high.astype(F32)).astype(BF16)


def aligned(start, size, unit):
    return pl.ds(pl.multiple_of(start, unit), size)


def assemble(dst, own, other, opt):
    dst[aligned(HALF * opt, HALF, 64), :] = own[0:HALF, :]
    dst[aligned(HALF * (1 - opt), HALF, 64), :] = other[0:HALF, :]


def call(kernel, ins, outs, scratch=(), micros=0, name=None, vmem=12, after=()):
    specs = [SMEM if s else VMEM for s, _ in ins] + [ANY] * len(after)
    count = len(ins)

    def body(*refs):
        kernel(*refs[:count], *refs[count + len(after) :])

    shapes = [jax.ShapeDtypeStruct(s, d) for s, d in outs]
    moved = sum(a.size * a.dtype.itemsize for _, a in ins)
    moved += sum(s.size * s.dtype.itemsize for s in shapes)
    return pl.pallas_call(
        body,
        out_shape=shapes,
        in_specs=specs,
        out_specs=[VMEM] * len(shapes),
        scratch_shapes=list(scratch),
        compiler_params=pltpu.CompilerParams(vmem_limit_bytes=vmem << 20),
        cost_estimate=pl.CostEstimate(
            flops=micros * 1100000000, bytes_accessed=moved, transcendentals=0
        ),
        name=name,
    )(*[a for _, a in ins], *after)


def head_stack(rows):
    lane_head = iota(rows.shape, 1) // HD
    zero = jnp.zeros_like(rows)
    return jnp.concatenate([jnp.where(lane_head == j, rows, zero) for j in range(4)], axis=0)


def attend_kernel(
    place, lengths, tokens, w_own, w_other, proj, att, lse, segc, segr, vec, wfull, bias, vt
):
    opt = place[0]
    assemble(wfull, w_own, w_other, opt)
    mine = w_own[HALF : HALF + 16, 0:D].astype(F32)
    others = w_other[HALF : HALF + 16, 0:D].astype(F32)
    first = opt == 0
    vec[0:6, :] = jnp.where(first, mine, others)[0:6]
    vec[6:12, :] = jnp.where(first, others, mine)[0:6]
    vec[12:16, :] = jnp.zeros((4, D), F32)

    pos_col = iota((WIN, 128), 0) + OFF * opt
    pos_row = iota((8, PAD), 1) + OFF * opt
    seg_col = jnp.zeros((WIN, 128), jnp.int32)
    seg_row = jnp.zeros((8, PAD), jnp.int32)
    bound = jnp.int32(0)
    for s in range(SEGS):
        bound = bound + lengths[s]
        seg_col = seg_col + (pos_col >= bound).astype(jnp.int32)
        seg_row = seg_row + (pos_row >= bound).astype(jnp.int32)
    segc[...] = seg_col
    segr[...] = seg_row
    for i, (q0, k0, k1) in enumerate(BANDS):
        bias[BAND_ROWS[i] : BAND_ROWS[i + 1], :] = jnp.where(
            segc[k0:k1, :] == segr[0:1, q0 : q0 + BLOCK], 0.0, NEG_BIG
        )

    x = tokens[aligned(OFF * opt, WIN, 64), :]
    for c in range(3):
        acc = nn(x, wfull[:, c * D : (c + 1) * D])
        if c != 1:
            acc = acc + vec[(0 if c == 0 else 1) : (1 if c == 0 else 2), :]
        proj[0:WIN, c * D : (c + 1) * D] = acc.astype(BF16)
    proj[WIN:PAD, :] = jnp.zeros((PAD - WIN, 3 * D), BF16)

    def group(g, carry):
        def lanes(part):
            return aligned(part * D + 128 * g, 128, 128)

        for t in range(PAD // 128):
            vt[:, 128 * t : 128 * t + 128] = (
                proj[128 * t : 128 * t + 128, lanes(2)].astype(F32).T.astype(BF16)
            )
        for i, (q0, k0, k1) in enumerate(BANDS):
            stack = head_stack(proj[q0 : q0 + BLOCK, lanes(0)])
            st = nt(proj[k0:k1, lanes(1)], stack)
            outs = []
            for j in range(4):
                t = (
                    st[:, j * BLOCK : (j + 1) * BLOCK] * EXP2_SCALE
                    + bias[BAND_ROWS[i] : BAND_ROWS[i + 1], :]
                )
                peak = jnp.max(t, axis=0, keepdims=True)
                powers = jnp.exp2(t - peak)
                total = jnp.sum(powers, axis=0, keepdims=True)
                lse[g, j : j + 1, q0 : q0 + BLOCK] = peak + jnp.log2(total)
                o = nn(vt[j * HD : (j + 1) * HD, k0:k1], powers.astype(BF16))
                outs.append(o * (1.0 / total))
            rows = min(BLOCK, WIN - q0)
            att[q0 : q0 + rows, aligned(128 * g, 128, 128)] = (
                jnp.concatenate(outs, axis=0).T[0:rows].astype(BF16)
            )
        return carry

    lax.fori_loop(0, 3, group, 0)


def attend(place, lengths, tokens, w_own, w_other):
    return call(
        attend_kernel,
        [(1, place), (1, lengths), (0, tokens), (0, w_own), (0, w_other)],
        [
            ((PAD, 3 * D), BF16),
            ((WIN, D), BF16),
            ((3, 4, PAD), F32),
            ((WIN, 128), jnp.int32),
            ((8, PAD), jnp.int32),
            ((16, D), F32),
        ],
        [
            pltpu.VMEM((D, 3 * D), BF16),
            pltpu.VMEM((BAND_ROWS[-1], 128), F32),
            pltpu.VMEM((128, PAD), BF16),
        ],
        micros=8,
        name="attend",
    )


def owned(place, lengths, segment):
    bound = jnp.int32(0)
    count = jnp.int32(0)
    for s in range(SEGS):
        bound = bound + lengths[s]
        count = count + (bound <= WIN).astype(jnp.int32)
    low_side = (segment < count).astype(jnp.int32)
    return low_side == (place[0] == 0).astype(jnp.int32)


def mlp_kernel(
    place, lengths, chosen, att, tokens, segr, vec, wo_own, wo_other, wu_own, wu_other,
    wd_own, wd_other, xhat1, inv1, hlow, act, slope, xhat2, inv2, unit, uscale,
    wo, wu, wd, tmp, hid, ench, encl,
):
    opt = place[0]
    assemble(wo, wo_own, wo_other, opt)
    assemble(wu, wu_own, wu_other, opt)
    assemble(wd, wd_own, wd_other, opt)
    tmp[...] = nn(att[...], wo[...])

    def first_norm(i, carry):
        r = aligned(i * ROWS, ROWS, ROWS)
        x = tokens[aligned(OFF * opt + i * ROWS, ROWS, ROWS), :].astype(F32)
        v = tmp[r, :] + vec[2:3, :] + x
        centred = v - jnp.mean(v, axis=1, keepdims=True)
        inverse = lax.rsqrt(jnp.mean(centred * centred, axis=1, keepdims=True) + LN_EPS)
        normed = centred * inverse
        xhat1[r, :] = normed
        inv1[r, :] = jnp.broadcast_to(inverse, (ROWS, 128))
        h = normed * vec[8:9, :] + vec[9:10, :]
        hid[r, :] = h
        hlow[r, :] = h.astype(BF16)
        return carry

    lax.fori_loop(0, WIN // ROWS, first_norm, 0)

    for c in range(4):
        cols = slice(c * D, (c + 1) * D)
        tmp[...] = nn(hlow[...], wu[:, cols])

        def gelu(i, carry, cols=cols, c=c):
            r = aligned(i * ROWS, ROWS, ROWS)
            u = tmp[r, :] + vec[3 + c : 4 + c, :]
            half = lax.erf(u * 0.7071067811865476) * 0.5 + 0.5
            act[r, cols] = (u * half).astype(BF16)
            slope[r, cols] = half + u * jnp.exp(-0.5 * u * u) * 0.3989422804014327
            return carry

        lax.fori_loop(0, WIN // ROWS, gelu, 0)

    tmp[...] = nt(act[...], wd[...])

    def second_norm(i, carry):
        r = aligned(i * ROWS, ROWS, ROWS)
        v = tmp[r, :] + vec[7:8, :] + hid[r, :]
        centred = v - jnp.mean(v, axis=1, keepdims=True)
        inverse = lax.rsqrt(jnp.mean(centred * centred, axis=1, keepdims=True) + LN_EPS)
        normed = centred * inverse
        xhat2[r, :] = normed
        inv2[r, :] = jnp.broadcast_to(inverse, (ROWS, 128))
        high, rest = low_pair(normed * vec[10:11, :] + vec[11:12, :])
        ench[r, :] = high
        encl[r, :] = rest
        return carry

    lax.fori_loop(0, WIN // ROWS, second_norm, 0)

    seg = segr[0:1, 0:WIN]
    row_id = iota((2 * PAIRS, WIN), 0)
    wanted = jnp.zeros((2 * PAIRS, WIN), jnp.int32)
    for j in range(2 * PAIRS):
        wanted = jnp.where(row_id == j, chosen[j], wanted)
    mask = owned(place, lengths, jnp.broadcast_to(seg, (2 * PAIRS, WIN)))
    onehot = jnp.where((wanted == seg) & mask, 1.0, 0.0)
    count = jnp.maximum(jnp.sum(onehot, axis=1, keepdims=True), 1.0)
    hot = onehot.astype(BF16)
    pooled = (nn(hot, ench[...]) + nn(hot, encl[...])) / count
    inverse_len = lax.rsqrt(jnp.sum(pooled * pooled, axis=1, keepdims=True) + POOL_EPS)
    unit[...] = pooled * inverse_len
    uscale[...] = jnp.broadcast_to(inverse_len / count, (2 * PAIRS, 128))


def mlp(place, lengths, chosen, att, tokens, segr, vec, halves):
    return call(
        mlp_kernel,
        [(1, place), (1, lengths), (1, chosen), (0, att), (0, tokens), (0, segr), (0, vec)]
        + [(0, h) for h in halves],
        [
            ((WIN, D), F32),
            ((WIN, 128), F32),
            ((WIN, D), BF16),
            ((WIN, FF), BF16),
            ((WIN, FF), F32),
            ((WIN, D), F32),
            ((WIN, 128), F32),
            ((2 * PAIRS, D), F32),
            ((2 * PAIRS, 128), F32),
        ],
        [
            pltpu.VMEM((D, D), BF16),
            pltpu.VMEM((D, FF), BF16),
            pltpu.VMEM((D, FF), BF16),
            pltpu.VMEM((WIN, D), F32),
            pltpu.VMEM((WIN, D), F32),
            pltpu.VMEM((WIN, D), BF16),
            pltpu.VMEM((WIN, D), BF16),
        ],
        micros=10,
        name="mlp",
    )


def split_rows(grad, keep, send, chunk, opt):
    keep[chunk, 0:HALF, :] = grad[aligned(HALF * opt, HALF, 64), :].astype(BF16)
    send[chunk, 0:HALF, :] = grad[aligned(HALF * (1 - opt), HALF, 64), :].astype(BF16)


def column_sums(value):
    return jnp.sum(value.reshape(ROWS // 8, 8, D), axis=0)


def norm_backward(grad_at, normed_ref, inverse_ref, gain, out, low_out, sums, at):
    def block(i, carry):
        scale_sum, shift_sum, bias_sum = carry
        r = aligned(i * ROWS, ROWS, ROWS)
        g = grad_at(r)
        normed = normed_ref[r, :]
        scaled = g * gain
        inner = (
            scaled
            - jnp.mean(scaled, axis=1, keepdims=True)
            - normed * jnp.mean(scaled * normed, axis=1, keepdims=True)
        ) * inverse_ref[r, 0:1]
        out[r, :] = inner
        low_out[r, :] = inner.astype(BF16)
        return (
            scale_sum + column_sums(g * normed),
            shift_sum + column_sums(g),
            bias_sum + column_sums(inner),
        )

    zero = jnp.zeros((8, D), F32)
    scale_sum, shift_sum, bias_sum = lax.fori_loop(0, WIN // ROWS, block, (zero, zero, zero))
    sums[at : at + 1, :] = jnp.sum(bias_sum, axis=0, keepdims=True)
    sums[at + 1 : at + 2, :] = jnp.sum(scale_sum, axis=0, keepdims=True)
    sums[at + 2 : at + 3, :] = jnp.sum(shift_sum, axis=0, keepdims=True)


def down_kernel(
    count, place, lengths, chosen, marks, units, segc, uscale, xhat2, inv2, act, vec, *rest
):
    stack, dsec, dlow, keep, send, sums, queries, docs, grad, dlog = rest
    opt, me = place[0], place[1]
    for j in range(count):
        r = slice(j * PAIRS, (j + 1) * PAIRS)
        both = stack[j].astype(F32)
        queries[r, :] = both[0:PAIRS]
        docs[r, :] = both[PAIRS : 2 * PAIRS]
    total = count * PAIRS
    q = queries[...].astype(BF16)
    d = docs[...].astype(BF16)
    logits = SCORE_SCALE * nt(q, d)
    peak = jnp.max(logits, axis=1, keepdims=True)
    powers = jnp.exp(logits - peak)
    soft = powers / jnp.sum(powers, axis=1, keepdims=True)
    col = iota((total, total), 1)
    hit = marks[:, 0:1] == col
    d_logits = (soft - jnp.where(hit, 1.0, 0.0)) * (SCORE_SCALE / total)
    dlog[...] = d_logits
    mine = aligned(me * PAIRS, PAIRS, PAIRS)
    high, rest_low = low_pair(dlog[mine, :])
    d_q = nn(high, d) + nn(rest_low, d)
    dlog[...] = d_logits.T
    high, rest_low = low_pair(dlog[mine, :])
    d_d = nn(high, q) + nn(rest_low, q)
    d_units = jnp.concatenate([d_q, d_d], axis=0)
    u = units[...]
    d_pool = uscale[:, 0:1] * (d_units - u * jnp.sum(u * d_units, axis=1, keepdims=True))
    lane = iota((8, 2 * PAIRS), 1)
    wanted = jnp.zeros((8, 2 * PAIRS), jnp.int32)
    for j in range(2 * PAIRS):
        wanted = jnp.where(lane == j, chosen[j], wanted)
    seg = segc[:, 0 : 2 * PAIRS]
    mask = owned(place, lengths, seg)
    hot = jnp.where((seg == wanted[0:1, :]) & mask, 1.0, 0.0).astype(BF16)
    high, rest_low = low_pair(d_pool)
    dsec[...] = nn(hot, high) + nn(hot, rest_low)
    norm_backward(lambda r: dsec[r, :], xhat2, inv2, vec[10:11, :], dsec, dlow, sums, 0)
    sums[3:8, :] = jnp.zeros((5, D), F32)
    for c in range(4):
        grad[...] = tn(dlow[...], act[:, c * D : (c + 1) * D])
        split_rows(grad, keep, send, c, opt)


def down_backward(count, place, lengths, chosen, marks, units, segc, uscale, saved, vec, stack):
    total = count * PAIRS
    return call(
        functools.partial(down_kernel, count),
        [(1, place), (1, lengths), (1, chosen), (0, marks), (0, units), (0, segc), (0, uscale)]
        + [(0, s) for s in saved]
        + [(0, vec), (0, stack)],
        [
            ((WIN, D), F32),
            ((WIN, D), BF16),
            ((4, HALF, D), BF16),
            ((4, HALF, D), BF16),
            ((8, D), F32),
        ],
        [
            pltpu.VMEM((total, D), F32),
            pltpu.VMEM((total, D), F32),
            pltpu.VMEM((D, D), F32),
            pltpu.VMEM((total, total), F32),
        ],
        micros=4,
        name="down_backward",
    )


def up_kernel(place, dlow, slope, hlow, wd_own, wd_other, dup, keep, send, sums, wd, grad):
    opt = place[0]
    assemble(wd, wd_own, wd_other, opt)
    for c in range(4):
        cols = slice(c * D, (c + 1) * D)
        part = (nn(dlow[...], wd[:, cols]) * slope[:, cols]).astype(BF16)
        dup[:, cols] = part
        sums[c : c + 1, :] = jnp.sum(part.astype(F32), axis=0, keepdims=True)
        grad[...] = tn(hlow[...], dup[:, cols])
        split_rows(grad, keep, send, c, opt)


def up_backward(place, dlow, slope, hlow, halves, after):
    return call(
        up_kernel,
        [(1, place)] + [(0, a) for a in (dlow, slope, hlow) + tuple(halves)],
        [((WIN, FF), BF16), ((4, HALF, D), BF16), ((4, HALF, D), BF16), ((4, D), F32)],
        [pltpu.VMEM((D, FF), BF16), pltpu.VMEM((D, D), F32)],
        micros=3,
        name="up_backward",
        after=after,
    )


def first_kernel(
    place, dup, dsec, xhat1, inv1, att, vec, wu_own, wu_other, wo_own, wo_other,
    dfirst, datt, delta, okeep, osend, sums, wu, wo, grad, dlow,
):
    opt = place[0]
    assemble(wu, wu_own, wu_other, opt)
    assemble(wo, wo_own, wo_other, opt)
    dfirst[...] = nt(dup[...], wu[...])
    norm_backward(
        lambda r: dfirst[r, :] + dsec[r, :], xhat1, inv1, vec[8:9, :], dfirst, dlow, sums, 0
    )
    sums[3:8, :] = jnp.zeros((5, D), F32)
    grad[...] = tn(att[...], dlow[...])
    okeep[...] = grad[aligned(HALF * opt, HALF, 64), :].astype(BF16)
    osend[...] = grad[aligned(HALF * (1 - opt), HALF, 64), :].astype(BF16)
    da = nt(dlow[...], wo[...]).astype(BF16)
    datt[0:WIN, :] = da
    datt[WIN:PAD, :] = jnp.zeros((PAD - WIN, D), BF16)
    high, rest = low_pair(da.astype(F32) * att[...].astype(F32))
    heads = (iota((16, D), 1) // HD == iota((16, D), 0)).astype(F32).astype(BF16)
    delta[:, 0:WIN] = nt(heads, high) + nt(heads, rest)
    delta[:, WIN:PAD] = jnp.zeros((16, PAD - WIN), F32)


def first_backward(place, dup, dsec, xhat1, inv1, att, vec, halves, after):
    return call(
        first_kernel,
        [(1, place)] + [(0, a) for a in (dup, dsec, xhat1, inv1, att, vec) + tuple(halves)],
        [
            ((WIN, D), F32),
            ((PAD, D), BF16),
            ((16, PAD), F32),
            ((HALF, D), BF16),
            ((HALF, D), BF16),
            ((8, D), F32),
        ],
        [
            pltpu.VMEM((D, FF), BF16),
            pltpu.VMEM((D, D), BF16),
            pltpu.VMEM((D, D), F32),
            pltpu.VMEM((WIN, D), BF16),
        ],
        micros=3,
        name="first_backward",
        after=after,
    )


def heads_kernel(g, proj, datt, lse, delta, segc, segr, dproj, kt, dk, dv):
    def lanes(part):
        return slice(part * D + 128 * g, part * D + 128 * g + 128)

    for t in range(PAD // 128):
        kt[:, 128 * t : 128 * t + 128] = (
            proj[128 * t : 128 * t + 128, lanes(1)].astype(F32).T.astype(BF16)
        )
    dk[...] = jnp.zeros_like(dk)
    dv[...] = jnp.zeros_like(dv)
    for q0, k0, k1 in BANDS:
        qs = head_stack(proj[q0 : q0 + BLOCK, lanes(0)])
        gs = head_stack(datt[q0 : q0 + BLOCK, lanes(0)])
        st = nt(proj[k0:k1, lanes(1)], qs)
        dp = nt(proj[k0:k1, lanes(2)], gs)
        same = segc[k0:k1, :] == segr[0:1, q0 : q0 + BLOCK]
        bias = jnp.where(same, 0.0, NEG_BIG)
        probs, d_scores, dq = [], [], []
        for j in range(4):
            cols = slice(j * BLOCK, (j + 1) * BLOCK)
            prob = jnp.exp2(st[:, cols] * EXP2_SCALE + bias - lse[g, j : j + 1, q0 : q0 + BLOCK])
            ds = prob * (dp[:, cols] - delta[4 * g + j : 4 * g + j + 1, q0 : q0 + BLOCK])
            ds = ds.astype(BF16)
            probs.append(prob.astype(BF16))
            d_scores.append(ds)
            dq.append(nn(kt[j * HD : (j + 1) * HD, k0:k1], ds))
        dv[k0:k1, :] += nn(jnp.concatenate(probs, axis=1), gs)
        dk[k0:k1, :] += nn(jnp.concatenate(d_scores, axis=1), qs)
        rows = min(BLOCK, WIN - q0)
        dqs = jnp.concatenate(dq, axis=0).T[0:rows] * HD ** (-0.5)
        dproj[q0 : q0 + rows, 0:128] = dqs.astype(BF16)
    dproj[:, 128:256] = (dk[...] * HD ** (-0.5)).astype(BF16)
    dproj[:, 256:384] = dv[...].astype(BF16)


def heads_backward(g, proj, datt, lse, delta, segc, segr, after):
    return call(
        functools.partial(heads_kernel, g),
        [(0, a) for a in (proj, datt, lse, delta, segc, segr)],
        [((WIN, D), BF16)],
        [
            pltpu.VMEM((128, PAD), BF16),
            pltpu.VMEM((WIN, 128), F32),
            pltpu.VMEM((WIN, 128), F32),
        ],
        micros=3,
        name="heads_backward",
        after=after,
    )[0]


def input_kernel(
    place, tokens, dp0, dp1, dp2, dfirst, okeep, osend, dsums, usums, fsums, w_own, w_other,
    keep, send, igrad, wfull, dproj, grad,
):
    opt = place[0]
    assemble(wfull, w_own, w_other, opt)
    for g, part in enumerate((dp0, dp1, dp2)):
        for c in range(3):
            dproj[:, c * D + 128 * g : c * D + 128 * g + 128] = part[:, 128 * c : 128 * c + 128]
    x = tokens[aligned(OFF * opt, WIN, 64), :]
    for c in range(3):
        grad[...] = tn(x, dproj[:, c * D : (c + 1) * D])
        split_rows(grad, keep, send, c, opt)
    keep[3, 0:HALF, :] = okeep[...]
    send[3, 0:HALF, :] = osend[...]
    q_sum = jnp.sum(dproj[:, 0:D].astype(F32), axis=0, keepdims=True)
    v_sum = jnp.sum(dproj[:, 2 * D : 3 * D].astype(F32), axis=0, keepdims=True)
    rows = jnp.concatenate(
        [
            q_sum,
            v_sum,
            fsums[0:1, :],
            usums[0:4, :],
            dsums[0:1, :],
            fsums[1:3, :],
            dsums[1:3, :],
            jnp.zeros((4, D), F32),
        ],
        axis=0,
    ).astype(BF16)
    for c in range(4):
        keep[c, HALF : HALF + 16, :] = rows
        send[c, HALF : HALF + 16, :] = rows
    igrad[...] = (nt(dproj[...], wfull[...]) + dfirst[...]).astype(BF16)


def input_backward(place, tokens, parts, dfirst, okeep, osend, sums, w_own, w_other, after):
    return call(
        input_kernel,
        [(1, place), (0, tokens)]
        + [(0, a) for a in tuple(parts) + (dfirst, okeep, osend) + sums + (w_own, w_other)],
        [((4, HALF + 16, D), BF16), ((4, HALF + 16, D), BF16), ((WIN, D), BF16)],
        [
            pltpu.VMEM((D, 3 * D), BF16),
            pltpu.VMEM((WIN, 3 * D), BF16),
            pltpu.VMEM((D, D), F32),
        ],
        micros=3,
        name="input_backward",
        after=after,
    )


def pair(value):
    return lax.ppermute(value, "opt", [(0, 1), (1, 0)])


def trade(value, n, shift, size):
    groups = None
    if size < n:
        stride = 1 << shift
        groups = [
            [low + k * stride for k in range(size)] for low in range(n) if (low // stride) % size == 0
        ]
    return lax.all_to_all(value, "dp", 0, 0, axis_index_groups=groups, tiled=True)


def gather(value, n, shift, size):
    return trade(jnp.broadcast_to(value[None], (size,) + value.shape), n, shift, size)


def added(a, b):
    return (a.astype(F32) + b.astype(F32)).astype(BF16)


def summed(parts):
    return jnp.sum(parts.astype(F32), axis=0)


def line_pieces(plane):
    pieces = plane[:HALF].reshape(4, HALF // 4, D)
    if plane.shape[0] > HALF:
        extra = jnp.broadcast_to(plane[None, HALF:], (4, plane.shape[0] - HALF, D))
        pieces = jnp.concatenate([pieces, extra], axis=1)
    return pieces


def rest_sum(final, n):
    shift = 4
    while (1 << shift) < n:
        final = added(final, lax.ppermute(final, "dp", [(i, i ^ (1 << shift)) for i in range(n)]))
        shift += 1
    return final


def square_sum(value):
    value = value.astype(F32)
    return jnp.sum(value * value)


def adamw(parameter, first_state, second, clipped, rate):
    first_new = BETA_ONE * first_state + (1.0 - BETA_ONE) * clipped
    second_new = BETA_TWO * second + (1.0 - BETA_TWO) * clipped * clipped
    direction = (first_new * (1.0 / (1.0 - BETA_ONE**STEP))) / (
        jnp.sqrt(second_new * (1.0 / (1.0 - BETA_TWO**STEP))) + ADAM_EPS
    )
    return parameter - rate * (direction + DECAY_RATE * parameter), first_new, second_new


def adamw_kernel(place, squares, vgrad, w, m, v, pv, pm, pq, *rest):
    parts, rest = rest[:3], rest[3:]
    outs, (npv, npm, npq, norm), scrs, sems = rest[:4], rest[4:8], rest[8:12], rest[12]
    opt = place[0]
    grad_norm = jnp.sqrt(squares[...])
    factor = jnp.minimum(1.0, CLIP_NORM / (grad_norm + 1e-06))
    norm[...] = grad_norm
    g = vgrad[...].astype(F32)
    g = jnp.where(opt == 0, g[0:6], g[6:12])
    a, b, c = adamw(pv[...], pm[...], pq[...], g * factor, VECTOR_RATE)
    npv[...] = a
    npm[...] = b
    npq[...] = c
    copies = []
    for t in range(12):
        at = slice(D * t, D * t + D)
        part = parts[t // 4]

        def rows(i, carry, at=at, part=part, t=t):
            for k in range(4):
                r = aligned(48 * k + i * 16, 16, 16)
                g = part[t % 4, k, aligned(i * 16, 16, 16), :].astype(F32)
                new_w, new_m, new_v = adamw(w[r, at], m[r, at], v[r, at], g * factor, LEARN_RATE)
                for scr, value in zip(scrs, (new_w, new_m, new_v, new_w.astype(BF16))):
                    scr[r, at] = value
            return carry

        lax.fori_loop(0, 3, rows, 0)
        for i, (scr, out) in enumerate(zip(scrs, outs)):
            copy = pltpu.make_async_copy(scr.at[:, at], out.at[:, at], sems.at[t, i])
            copy.start()
            copies.append(copy)
    for copy in copies:
        copy.wait()


def update(place, squares, vgrad, w, m, v, pv, pm, pq, parts):
    ins = (squares, vgrad, w, m, v, pv, pm, pq) + tuple(parts)
    shapes = [(w.shape, F32)] * 3 + [(w.shape, BF16)] + [(pv.shape, F32)] * 3 + [((1, 1), F32)]
    return pl.pallas_call(
        adamw_kernel,
        out_shape=[jax.ShapeDtypeStruct(s, d) for s, d in shapes],
        in_specs=[SMEM] + [VMEM] * len(ins),
        out_specs=[ANY] * 4 + [VMEM] * 4,
        scratch_shapes=[
            pltpu.VMEM(w.shape, F32),
            pltpu.VMEM(w.shape, F32),
            pltpu.VMEM(w.shape, F32),
            pltpu.VMEM(w.shape, BF16),
            pltpu.SemaphoreType.DMA((12, 4)),
        ],
        compiler_params=pltpu.CompilerParams(vmem_limit_bytes=16 << 20),
        cost_estimate=pl.CostEstimate(
            flops=4000000000, bytes_accessed=26 * w.size, transcendentals=0
        ),
        name="adamw",
    )(place, *ins)


def shards(
    n,
    tokens,
    lengths,
    query_index,
    doc_index,
    targets,
    weights,
    first_moment,
    second_moment,
    vectors,
    vec_first,
    vec_second,
):
    opt = lax.axis_index("opt")
    me = lax.axis_index("dp")
    place = jnp.stack([opt, me]).astype(jnp.int32)
    lengths = lengths.reshape(SEGS)
    chosen = jnp.concatenate([query_index, doc_index])

    extra = jnp.pad(vectors, ((0, 10), (0, 2 * D)))
    w_own = jnp.concatenate([weights[:, : 3 * D], extra], axis=0).astype(BF16)
    w_other = pair(w_own)
    wo_own = weights[:, 3 * D : 4 * D].astype(BF16)
    wu_own = weights[:, 4 * D : 4 * D + FF].astype(BF16)
    wd_own = weights[:, 4 * D + FF :].astype(BF16)
    wo = (wo_own, pair(wo_own))
    wu = (wu_own, pair(wu_own))
    wd = (wd_own, pair(wd_own))
    marks = gather(targets, n, 0, n)
    marks = jnp.broadcast_to(marks.reshape(n * PAIRS, 1), (n * PAIRS, 128))

    proj, att, lse, segc, segr, vec = attend(place, lengths, tokens, w_own, w_other)
    xhat1, inv1, hlow, act, slope, xhat2, inv2, unit, uscale = mlp(
        place, lengths, chosen, att, tokens, segr, vec, wo + wu + wd
    )
    units = unit + pair(unit)
    stack = gather(units.astype(BF16), n, 0, n)
    plane, line = (n, 0, 4), (n, 2, 4)
    dsec, dlow, keep, send, dsums = down_backward(
        n, place, lengths, chosen, marks, units, segc, uscale, (xhat2, inv2, act), vec, stack
    )
    down = pair(send)
    dup, ukeep, usend, usums = up_backward(place, dlow, slope, hlow, wd, [])
    up = pair(usend)
    down = added(keep, down)
    dfirst, datt, delta, okeep, osend, fsums = first_backward(
        place, dup, dsec, xhat1, inv1, att, vec, wu + wo, [down]
    )
    down = line_pieces(summed(trade(down, *plane)).astype(BF16))
    up = added(ukeep, up)
    heads = (proj, datt, lse, delta, segc, segr)
    part0 = heads_backward(0, *heads, [down, up])
    down = rest_sum(summed(trade(down, *line)).astype(BF16), n)
    up = line_pieces(summed(trade(up, *plane)).astype(BF16))
    part1 = heads_backward(1, *heads, [down, up, part0])
    squares = square_sum(down)
    down = gather(down, *line)
    up = rest_sum(summed(trade(up, *line)).astype(BF16), n)
    part2 = heads_backward(2, *heads, [down, up, part1])
    squares = squares + square_sum(up)
    down = gather(down, *plane)
    up = gather(up, *line)
    keep, send, igrad = input_backward(
        place, tokens, (part0, part1, part2), dfirst, okeep, osend, (dsums, usums, fsums), w_own,
        w_other, [down, up],
    )
    low = pair(send)
    up = gather(up, *plane)
    iother = pair(igrad)
    low = added(keep, low)
    low = line_pieces(summed(trade(low, *plane)).astype(BF16))
    low = rest_sum(summed(trade(low, *line)).astype(BF16), n)
    vgrad = low[HALF // 4 :]
    low = low[: HALF // 4]
    squares = squares + square_sum(low)
    own_rows = lax.dynamic_slice_in_dim(vgrad, opt * 6, 6, 0)
    squares = squares + jnp.where(me == 0, square_sum(own_rows), 0.0)
    squares = jnp.sum(gather(squares.reshape(1, 1), n, 0, n), axis=0)
    squares = squares + pair(squares)
    low = gather(gather(low, *line), *plane)

    lower = jnp.where(opt == 0, igrad, iother)
    upper = jnp.where(opt == 0, iother, igrad)
    input_grad = jnp.concatenate(
        [lower[:OFF], lower[OFF:] + upper[: WIN - OFF], upper[WIN - OFF :]], axis=0
    )
    nw, nm, nv, nlow, npv, npm, npq, norm = update(
        place, squares, vgrad, weights, first_moment, second_moment,
        vectors, vec_first, vec_second, (low, up, down),
    )
    return (norm.reshape(()), input_grad, nw, nm, nv, nlow, npv, npm, npq)


def solution(mesh):
    rows = P("opt", None)
    in_specs = (P("dp", None), P("dp", None), P("dp"), P("dp"), P("dp")) + (rows,) * 6
    out_specs = (P(), P("dp", None)) + (rows,) * 7
    n = mesh.shape["dp"]
    return jax.shard_map(
        functools.partial(shards, n),
        mesh=mesh,
        in_specs=in_specs,
        out_specs=out_specs,
        check_vma=False,
    )
```

```python
import functools

import jax
import jax.numpy as jnp
from jax import lax
from jax.experimental import pallas as pl
from jax.experimental.pallas import tpu as pltpu
from jax.sharding import PartitionSpec as P

D = 384
HEADS = 12
HD = 32
FF = 1536
SEQ = 1024
SEGS = 16
PAIRS = 8
STEP = 10

WIN = 576
OFF = SEQ - WIN
PAD = 640
BLOCK = 128
BANDS = tuple((q, max(0, q - 128), min(WIN, q + 256)) for q in range(0, WIN, BLOCK))
BAND_ROWS = tuple(sum(b[2] - b[1] for b in BANDS[:i]) for i in range(len(BANDS) + 1))
ROWS = 64

LN_EPS = 1e-06
POOL_EPS = 1e-06
SCORE_SCALE = 50.0
CLIP_NORM = 0.001
BETA_ONE = 0.9
BETA_TWO = 0.98
ADAM_EPS = 1e-08
LEARN_RATE = 0.05
VECTOR_RATE = 0.3
DECAY_RATE = 0.01
NEG_BIG = -1e30
HALF = D // 2
CHUNK = HALF // 4
EXP2_SCALE = HD ** (-0.5) * 1.4426950408889634

F32 = jnp.float32
BF16 = jnp.bfloat16
VMEM = pl.BlockSpec(memory_space=pltpu.VMEM)
SMEM = pl.BlockSpec(memory_space=pltpu.SMEM)
ANY = pl.BlockSpec(memory_space=pl.ANY)


def nn(a, b):
    return jnp.dot(a, b, preferred_element_type=F32)


def nt(a, b):
    return lax.dot_general(a, b, (((1,), (1,)), ((), ())), preferred_element_type=F32)


def tn(a, b):
    return lax.dot_general(a, b, (((0,), (0,)), ((), ())), preferred_element_type=F32)


def exact(a, b, dims):
    return lax.dot_general(
        a, b, (dims, ((), ())), precision=lax.Precision.HIGHEST, preferred_element_type=F32
    )


def iota(shape, axis):
    return lax.broadcasted_iota(jnp.int32, shape, axis)


def low_pair(value):
    high = value.astype(BF16)
    return high, (value - high.astype(F32)).astype(BF16)


def aligned(start, size, unit):
    return pl.ds(pl.multiple_of(start, unit), size)


def assemble(dst, own, other, opt):
    dst[aligned(HALF * opt, HALF, 64), :] = own[0:HALF, :]
    dst[aligned(HALF * (1 - opt), HALF, 64), :] = other[0:HALF, :]


def call(kernel, ins, outs, scratch=(), micros=0, name=None, vmem=12, after=()):
    specs = [SMEM if s else VMEM for s, _ in ins] + [ANY] * len(after)
    count = len(ins)

    def body(*refs):
        kernel(*refs[:count], *refs[count + len(after) :])

    shapes = [jax.ShapeDtypeStruct(s, d) for s, d in outs]
    moved = sum(a.size * a.dtype.itemsize for _, a in ins)
    moved += sum(s.size * s.dtype.itemsize for s in shapes)
    return pl.pallas_call(
        body,
        out_shape=shapes,
        in_specs=specs,
        out_specs=[VMEM] * len(shapes),
        scratch_shapes=list(scratch),
        compiler_params=pltpu.CompilerParams(vmem_limit_bytes=vmem << 20),
        cost_estimate=pl.CostEstimate(
            flops=micros * 1100000000, bytes_accessed=moved, transcendentals=0
        ),
        name=name,
    )(*[a for _, a in ins], *after)


def head_stack(rows):
    lane_head = iota(rows.shape, 1) // HD
    zero = jnp.zeros_like(rows)
    return jnp.concatenate([jnp.where(lane_head == j, rows, zero) for j in range(4)], axis=0)


def attend_kernel(
    place, lengths, tokens, w_own, w_other, proj, att, lse, segc, segr, vec, wfull, bias, vt
):
    opt = place[0]
    assemble(wfull, w_own, w_other, opt)
    mine = w_own[HALF : HALF + 16, 0:D].astype(F32)
    others = w_other[HALF : HALF + 16, 0:D].astype(F32)
    first = opt == 0
    vec[0:6, :] = jnp.where(first, mine, others)[0:6]
    vec[6:12, :] = jnp.where(first, others, mine)[0:6]
    vec[12:16, :] = jnp.zeros((4, D), F32)

    pos_col = iota((WIN, 128), 0) + OFF * opt
    pos_row = iota((8, PAD), 1) + OFF * opt
    seg_col = jnp.zeros((WIN, 128), jnp.int32)
    seg_row = jnp.zeros((8, PAD), jnp.int32)
    bound = jnp.int32(0)
    for s in range(SEGS):
        bound = bound + lengths[s]
        seg_col = seg_col + (pos_col >= bound).astype(jnp.int32)
        seg_row = seg_row + (pos_row >= bound).astype(jnp.int32)
    segc[...] = seg_col
    segr[...] = seg_row
    for i, (q0, k0, k1) in enumerate(BANDS):
        bias[BAND_ROWS[i] : BAND_ROWS[i + 1], :] = jnp.where(
            segc[k0:k1, :] == segr[0:1, q0 : q0 + BLOCK], 0.0, NEG_BIG
        )

    x = tokens[aligned(OFF * opt, WIN, 64), :]
    for c in range(3):
        acc = nn(x, wfull[:, c * D : (c + 1) * D])
        if c != 1:
            acc = acc + vec[(0 if c == 0 else 1) : (1 if c == 0 else 2), :]
        proj[0:WIN, c * D : (c + 1) * D] = acc.astype(BF16)
    proj[WIN:PAD, :] = jnp.zeros((PAD - WIN, 3 * D), BF16)

    def group(g, carry):
        def lanes(part):
            return aligned(part * D + 128 * g, 128, 128)

        for t in range(PAD // 128):
            vt[:, 128 * t : 128 * t + 128] = (
                proj[128 * t : 128 * t + 128, lanes(2)].astype(F32).T.astype(BF16)
            )
        for i, (q0, k0, k1) in enumerate(BANDS):
            stack = head_stack(proj[q0 : q0 + BLOCK, lanes(0)])
            st = nt(proj[k0:k1, lanes(1)], stack)
            outs = []
            for j in range(4):
                t = (
                    st[:, j * BLOCK : (j + 1) * BLOCK] * EXP2_SCALE
                    + bias[BAND_ROWS[i] : BAND_ROWS[i + 1], :]
                )
                peak = jnp.max(t, axis=0, keepdims=True)
                powers = jnp.exp2(t - peak)
                total = jnp.sum(powers, axis=0, keepdims=True)
                lse[g, j : j + 1, q0 : q0 + BLOCK] = peak + jnp.log2(total)
                o = nn(vt[j * HD : (j + 1) * HD, k0:k1], powers.astype(BF16))
                outs.append(o * (1.0 / total))
            rows = min(BLOCK, WIN - q0)
            att[q0 : q0 + rows, aligned(128 * g, 128, 128)] = (
                jnp.concatenate(outs, axis=0).T[0:rows].astype(BF16)
            )
        return carry

    lax.fori_loop(0, 3, group, 0)


def attend(place, lengths, tokens, w_own, w_other):
    return call(
        attend_kernel,
        [(1, place), (1, lengths), (0, tokens), (0, w_own), (0, w_other)],
        [
            ((PAD, 3 * D), BF16),
            ((WIN, D), BF16),
            ((3, 4, PAD), F32),
            ((WIN, 128), jnp.int32),
            ((8, PAD), jnp.int32),
            ((16, D), F32),
        ],
        [
            pltpu.VMEM((D, 3 * D), BF16),
            pltpu.VMEM((BAND_ROWS[-1], 128), F32),
            pltpu.VMEM((128, PAD), BF16),
        ],
        micros=8,
        name="attend",
    )


def owned(place, lengths, segment):
    bound = jnp.int32(0)
    count = jnp.int32(0)
    for s in range(SEGS):
        bound = bound + lengths[s]
        count = count + (bound <= WIN).astype(jnp.int32)
    low_side = (segment < count).astype(jnp.int32)
    return low_side == (place[0] == 0).astype(jnp.int32)


def mlp_kernel(
    place, lengths, chosen, att, tokens, segr, vec, wo_own, wo_other, wu_own, wu_other,
    wd_own, wd_other, xhat1, inv1, hlow, act, slope, xhat2, inv2, unit, uscale,
    wo, wu, wd, tmp, hid, ench, encl,
):
    opt = place[0]
    assemble(wo, wo_own, wo_other, opt)
    assemble(wu, wu_own, wu_other, opt)
    assemble(wd, wd_own, wd_other, opt)
    tmp[...] = nn(att[...], wo[...])

    def first_norm(i, carry):
        r = aligned(i * ROWS, ROWS, ROWS)
        x = tokens[aligned(OFF * opt + i * ROWS, ROWS, ROWS), :].astype(F32)
        v = tmp[r, :] + vec[2:3, :] + x
        centred = v - jnp.mean(v, axis=1, keepdims=True)
        inverse = lax.rsqrt(jnp.mean(centred * centred, axis=1, keepdims=True) + LN_EPS)
        normed = centred * inverse
        xhat1[r, :] = normed
        inv1[r, :] = jnp.broadcast_to(inverse, (ROWS, 128))
        h = normed * vec[8:9, :] + vec[9:10, :]
        hid[r, :] = h
        hlow[r, :] = h.astype(BF16)
        return carry

    lax.fori_loop(0, WIN // ROWS, first_norm, 0)

    for c in range(4):
        cols = slice(c * D, (c + 1) * D)
        tmp[...] = nn(hlow[...], wu[:, cols])

        def gelu(i, carry, cols=cols, c=c):
            r = aligned(i * ROWS, ROWS, ROWS)
            u = tmp[r, :] + vec[3 + c : 4 + c, :]
            half = lax.erf(u * 0.7071067811865476) * 0.5 + 0.5
            act[r, cols] = (u * half).astype(BF16)
            slope[r, cols] = half + u * jnp.exp(-0.5 * u * u) * 0.3989422804014327
            return carry

        lax.fori_loop(0, WIN // ROWS, gelu, 0)

    tmp[...] = nt(act[...], wd[...])

    def second_norm(i, carry):
        r = aligned(i * ROWS, ROWS, ROWS)
        v = tmp[r, :] + vec[7:8, :] + hid[r, :]
        centred = v - jnp.mean(v, axis=1, keepdims=True)
        inverse = lax.rsqrt(jnp.mean(centred * centred, axis=1, keepdims=True) + LN_EPS)
        normed = centred * inverse
        xhat2[r, :] = normed
        inv2[r, :] = jnp.broadcast_to(inverse, (ROWS, 128))
        high, rest = low_pair(normed * vec[10:11, :] + vec[11:12, :])
        ench[r, :] = high
        encl[r, :] = rest
        return carry

    lax.fori_loop(0, WIN // ROWS, second_norm, 0)

    seg = segr[0:1, 0:WIN]
    row_id = iota((2 * PAIRS, WIN), 0)
    wanted = jnp.zeros((2 * PAIRS, WIN), jnp.int32)
    for j in range(2 * PAIRS):
        wanted = jnp.where(row_id == j, chosen[j], wanted)
    mask = owned(place, lengths, jnp.broadcast_to(seg, (2 * PAIRS, WIN)))
    onehot = jnp.where((wanted == seg) & mask, 1.0, 0.0)
    count = jnp.maximum(jnp.sum(onehot, axis=1, keepdims=True), 1.0)
    hot = onehot.astype(BF16)
    pooled = (nn(hot, ench[...]) + nn(hot, encl[...])) / count
    inverse_len = lax.rsqrt(jnp.sum(pooled * pooled, axis=1, keepdims=True) + POOL_EPS)
    unit[...] = pooled * inverse_len
    uscale[...] = jnp.broadcast_to(inverse_len / count, (2 * PAIRS, 128))


def mlp(place, lengths, chosen, att, tokens, segr, vec, halves):
    return call(
        mlp_kernel,
        [(1, place), (1, lengths), (1, chosen), (0, att), (0, tokens), (0, segr), (0, vec)]
        + [(0, h) for h in halves],
        [
            ((WIN, D), F32),
            ((WIN, 128), F32),
            ((WIN, D), BF16),
            ((WIN, FF), BF16),
            ((WIN, FF), F32),
            ((WIN, D), F32),
            ((WIN, 128), F32),
            ((2 * PAIRS, D), F32),
            ((2 * PAIRS, 128), F32),
        ],
        [
            pltpu.VMEM((D, D), BF16),
            pltpu.VMEM((D, FF), BF16),
            pltpu.VMEM((D, FF), BF16),
            pltpu.VMEM((WIN, D), F32),
            pltpu.VMEM((WIN, D), F32),
            pltpu.VMEM((WIN, D), BF16),
            pltpu.VMEM((WIN, D), BF16),
        ],
        micros=10,
        name="mlp",
    )


def turned(chunk):
    return (chunk & 1) * 2 + (chunk >> 1)


def split_rows(grad, keep, send, place, cols):
    opt = place[0]
    for c in range(4):
        straight = c ^ place[1]
        mine = jnp.where(opt == 0, straight, turned(straight))
        theirs = jnp.where(opt == 0, turned(straight), straight)
        keep[mine, 0:CHUNK, cols] = grad[aligned(HALF * opt + CHUNK * c, CHUNK, 16), :].astype(BF16)
        send[theirs, 0:CHUNK, cols] = grad[
            aligned(HALF * (1 - opt) + CHUNK * c, CHUNK, 16), :
        ].astype(BF16)


def column_sums(value):
    return jnp.sum(value.reshape(ROWS // 8, 8, D), axis=0)


def norm_backward(grad_at, normed_ref, inverse_ref, gain, out, low_out, sums, at):
    def block(i, carry):
        scale_sum, shift_sum, bias_sum = carry
        r = aligned(i * ROWS, ROWS, ROWS)
        g = grad_at(r)
        normed = normed_ref[r, :]
        scaled = g * gain
        inner = (
            scaled
            - jnp.mean(scaled, axis=1, keepdims=True)
            - normed * jnp.mean(scaled * normed, axis=1, keepdims=True)
        ) * inverse_ref[r, 0:1]
        out[r, :] = inner
        low_out[r, :] = inner.astype(BF16)
        return (
            scale_sum + column_sums(g * normed),
            shift_sum + column_sums(g),
            bias_sum + column_sums(inner),
        )

    zero = jnp.zeros((8, D), F32)
    scale_sum, shift_sum, bias_sum = lax.fori_loop(0, WIN // ROWS, block, (zero, zero, zero))
    sums[at : at + 1, :] = jnp.sum(bias_sum, axis=0, keepdims=True)
    sums[at + 1 : at + 2, :] = jnp.sum(scale_sum, axis=0, keepdims=True)
    sums[at + 2 : at + 3, :] = jnp.sum(shift_sum, axis=0, keepdims=True)


def down_kernel(
    count, place, lengths, chosen, units, segc, uscale, xhat2, inv2, act, vec, *rest
):
    pieces, (dsec, dlow, keep, send, sums, queries, docs, marks, grad) = rest[:-9], rest[-9:]
    me = place[2]
    per = pieces[0].shape[0]
    for p, piece in enumerate(pieces):
        for j in range(per):
            r = slice((p * per + j) * PAIRS, (p * per + j + 1) * PAIRS)
            both = piece[j].astype(F32)
            queries[r, :] = both[0:PAIRS, 0:D]
            docs[r, :] = both[PAIRS : 2 * PAIRS, 0:D]
            marks[r, :] = both[0:PAIRS, D : D + 128]
    total = count * PAIRS
    q = queries[...].astype(BF16)
    d = docs[...].astype(BF16)
    logits = SCORE_SCALE * nt(q, d)
    peak = jnp.max(logits, axis=1, keepdims=True)
    powers = jnp.exp(logits - peak)
    soft = powers / jnp.sum(powers, axis=1, keepdims=True)
    col = iota((total, total), 1)
    doc_id = ((col // PAIRS) ^ me) * PAIRS + lax.rem(col, PAIRS)
    hit = (marks[:, 0:1] * 32.0 + marks[:, 64:65]).astype(jnp.int32) == doc_id
    d_logits = (soft - jnp.where(hit, 1.0, 0.0)) * (SCORE_SCALE / total)
    high, rest_low = low_pair(d_logits[0:PAIRS, :])
    d_q = nn(high, d) + nn(rest_low, d)
    high, rest_low = low_pair(d_logits[:, 0:128].T[0:PAIRS, :])
    d_d = nn(high, q) + nn(rest_low, q)
    d_units = jnp.concatenate([d_q, d_d], axis=0)
    u = units[...]
    d_pool = uscale[:, 0:1] * (d_units - u * jnp.sum(u * d_units, axis=1, keepdims=True))
    lane = iota((8, 2 * PAIRS), 1)
    wanted = jnp.zeros((8, 2 * PAIRS), jnp.int32)
    for j in range(2 * PAIRS):
        wanted = jnp.where(lane == j, chosen[j], wanted)
    seg = segc[:, 0 : 2 * PAIRS]
    mask = owned(place, lengths, seg)
    hot = jnp.where((seg == wanted[0:1, :]) & mask, 1.0, 0.0).astype(BF16)
    high, rest_low = low_pair(d_pool)
    dsec[...] = nn(hot, high) + nn(hot, rest_low)
    norm_backward(lambda r: dsec[r, :], xhat2, inv2, vec[10:11, :], dsec, dlow, sums, 0)
    sums[3:8, :] = jnp.zeros((5, D), F32)
    for c in range(4):
        cols = slice(c * D, (c + 1) * D)
        grad[...] = tn(dlow[...], act[:, cols])
        split_rows(grad, keep, send, place, cols)


def down_backward(count, place, lengths, chosen, units, segc, uscale, saved, vec, pieces):
    total = count * PAIRS
    return call(
        functools.partial(down_kernel, count),
        [(1, place), (1, lengths), (1, chosen), (0, units), (0, segc), (0, uscale)]
        + [(0, s) for s in saved]
        + [(0, vec)]
        + [(0, p) for p in pieces],
        [
            ((WIN, D), F32),
            ((WIN, D), BF16),
            ((4, CHUNK, FF), BF16),
            ((4, CHUNK, FF), BF16),
            ((8, D), F32),
        ],
        [
            pltpu.VMEM((total, D), F32),
            pltpu.VMEM((total, D), F32),
            pltpu.VMEM((total, 128), F32),
            pltpu.VMEM((D, D), F32),
        ],
        micros=4,
        name="down_backward",
    )


def up_kernel(place, dlow, slope, hlow, wd_own, wd_other, dup, keep, send, sums, wd, grad):
    opt = place[0]
    assemble(wd, wd_own, wd_other, opt)
    for c in range(4):
        cols = slice(c * D, (c + 1) * D)
        part = (nn(dlow[...], wd[:, cols]) * slope[:, cols]).astype(BF16)
        dup[:, cols] = part
        sums[c : c + 1, :] = jnp.sum(part.astype(F32), axis=0, keepdims=True)
        grad[...] = tn(hlow[...], dup[:, cols])
        split_rows(grad, keep, send, place, cols)


def up_backward(place, dlow, slope, hlow, halves, after):
    return call(
        up_kernel,
        [(1, place)] + [(0, a) for a in (dlow, slope, hlow) + tuple(halves)],
        [((WIN, FF), BF16), ((4, CHUNK, FF), BF16), ((4, CHUNK, FF), BF16), ((4, D), F32)],
        [pltpu.VMEM((D, FF), BF16), pltpu.VMEM((D, D), F32)],
        micros=3,
        name="up_backward",
        after=after,
    )


def first_kernel(
    place, dup, dsec, xhat1, inv1, att, vec, wu_own, wu_other, wo_own, wo_other,
    dfirst, datt, delta, okeep, osend, sums, wu, wo, grad, dlow,
):
    opt = place[0]
    assemble(wu, wu_own, wu_other, opt)
    assemble(wo, wo_own, wo_other, opt)
    dfirst[...] = nt(dup[...], wu[...])
    norm_backward(
        lambda r: dfirst[r, :] + dsec[r, :], xhat1, inv1, vec[8:9, :], dfirst, dlow, sums, 0
    )
    sums[3:8, :] = jnp.zeros((5, D), F32)
    grad[...] = tn(att[...], dlow[...])
    split_rows(grad, okeep, osend, place, slice(0, D))
    da = nt(dlow[...], wo[...]).astype(BF16)
    datt[0:WIN, :] = da
    datt[WIN:PAD, :] = jnp.zeros((PAD - WIN, D), BF16)
    high, rest = low_pair(da.astype(F32) * att[...].astype(F32))
    heads = (iota((16, D), 1) // HD == iota((16, D), 0)).astype(F32).astype(BF16)
    delta[:, 0:WIN] = nt(heads, high) + nt(heads, rest)
    delta[:, WIN:PAD] = jnp.zeros((16, PAD - WIN), F32)


def first_backward(place, dup, dsec, xhat1, inv1, att, vec, halves, after):
    return call(
        first_kernel,
        [(1, place)] + [(0, a) for a in (dup, dsec, xhat1, inv1, att, vec) + tuple(halves)],
        [
            ((WIN, D), F32),
            ((PAD, D), BF16),
            ((16, PAD), F32),
            ((4, CHUNK, D), BF16),
            ((4, CHUNK, D), BF16),
            ((8, D), F32),
        ],
        [
            pltpu.VMEM((D, FF), BF16),
            pltpu.VMEM((D, D), BF16),
            pltpu.VMEM((D, D), F32),
            pltpu.VMEM((WIN, D), BF16),
        ],
        micros=3,
        name="first_backward",
        after=after,
    )


def heads_kernel(g, place, tokens, proj, datt, lse, delta, segc, segr, *rest):
    rest, (dproj, keep, send, sums, kt, dk, dv, grad) = rest[:-8], rest[-8:]

    def lanes(part):
        return slice(part * D + 128 * g, part * D + 128 * g + 128)

    for t in range(PAD // 128):
        kt[:, 128 * t : 128 * t + 128] = (
            proj[128 * t : 128 * t + 128, lanes(1)].astype(F32).T.astype(BF16)
        )
    dk[...] = jnp.zeros_like(dk)
    dv[...] = jnp.zeros_like(dv)
    for q0, k0, k1 in BANDS:
        qs = head_stack(proj[q0 : q0 + BLOCK, lanes(0)])
        gs = head_stack(datt[q0 : q0 + BLOCK, lanes(0)])
        st = nt(proj[k0:k1, lanes(1)], qs)
        dp = nt(proj[k0:k1, lanes(2)], gs)
        same = segc[k0:k1, :] == segr[0:1, q0 : q0 + BLOCK]
        bias = jnp.where(same, 0.0, NEG_BIG)
        probs, d_scores, dq = [], [], []
        for j in range(4):
            cols = slice(j * BLOCK, (j + 1) * BLOCK)
            prob = jnp.exp2(st[:, cols] * EXP2_SCALE + bias - lse[g, j : j + 1, q0 : q0 + BLOCK])
            ds = prob * (dp[:, cols] - delta[4 * g + j : 4 * g + j + 1, q0 : q0 + BLOCK])
            ds = ds.astype(BF16)
            probs.append(prob.astype(BF16))
            d_scores.append(ds)
            dq.append(nn(kt[j * HD : (j + 1) * HD, k0:k1], ds))
        dv[k0:k1, :] += nn(jnp.concatenate(probs, axis=1), gs)
        dk[k0:k1, :] += nn(jnp.concatenate(d_scores, axis=1), qs)
        rows = min(BLOCK, WIN - q0)
        dqs = jnp.concatenate(dq, axis=0).T[0:rows] * HD ** (-0.5)
        dproj[q0 : q0 + rows, 0:128] = dqs.astype(BF16)
    dproj[:, 128:256] = (dk[...] * HD ** (-0.5)).astype(BF16)
    dproj[:, 256:384] = dv[...].astype(BF16)
    grad[...] = tn(tokens[aligned(OFF * place[0], WIN, 64), :], dproj[...])
    q_sum = jnp.sum(dproj[:, 0:128].astype(F32), axis=0, keepdims=True)
    v_sum = jnp.sum(dproj[:, 256:384].astype(F32), axis=0, keepdims=True)
    sums[0:1, :] = q_sum
    sums[1:2, :] = v_sum
    sums[2:8, :] = jnp.zeros((6, 128), F32)
    if g == 1:
        okeep, osend, zkeep, zsend = rest
        for dst, o, z in ((keep, okeep, zkeep), (send, osend, zsend)):
            dst[:, :, 0:D] = o[...]
            dst[:, :, D : 2 * D] = z[...]
        split_rows(grad, keep, send, place, slice(2 * D, 3 * D))
    else:
        split_rows(grad, keep, send, place, slice(0, D))
    if g == 2:
        dsums, usums, fsums, zero, one = rest
        rows = jnp.concatenate(
            [
                jnp.concatenate([zero[0:1], one[0:1], q_sum], axis=1),
                jnp.concatenate([zero[1:2], one[1:2], v_sum], axis=1),
                fsums[0:1, :],
                usums[0:4, :],
                dsums[0:1, :],
                fsums[1:3, :],
                dsums[1:3, :],
                jnp.zeros((4, D), F32),
            ],
            axis=0,
        ).astype(BF16)
        for c in range(4):
            keep[c, CHUNK : CHUNK + 16, :] = rows
            send[c, CHUNK : CHUNK + 16, :] = rows


def heads_backward(g, place, ins, more, after):
    part = ((4, CHUNK + (16 if g == 2 else 0), 3 * D if g == 1 else D), BF16)
    return call(
        functools.partial(heads_kernel, g),
        [(1, place)] + [(0, a) for a in tuple(ins) + tuple(more)],
        [((WIN, D), BF16), part, part, ((8, 128), F32)],
        [
            pltpu.VMEM((128, PAD), BF16),
            pltpu.VMEM((WIN, 128), F32),
            pltpu.VMEM((WIN, 128), F32),
            pltpu.VMEM((D, D), F32),
        ],
        micros=3,
        name="heads_backward",
        after=after,
    )


def input_kernel(place, dp0, dp1, dp2, dfirst, w_own, w_other, igrad, wfull, dproj):
    assemble(wfull, w_own, w_other, place[0])
    for g, part in enumerate((dp0, dp1, dp2)):
        for c in range(3):
            dproj[:, c * D + 128 * g : c * D + 128 * g + 128] = part[:, 128 * c : 128 * c + 128]
    igrad[...] = (nt(dproj[...], wfull[...]) + dfirst[...]).astype(BF16)


def input_backward(place, parts, dfirst, w_own, w_other, after):
    return call(
        input_kernel,
        [(1, place)] + [(0, a) for a in tuple(parts) + (dfirst, w_own, w_other)],
        [((WIN, D), BF16)],
        [pltpu.VMEM((D, 3 * D), BF16), pltpu.VMEM((WIN, 3 * D), BF16)],
        micros=2,
        name="input_backward",
        after=after,
    )[0]


def flips(axis, size, bits):
    return [(i, i ^ bits) for i in range(size)]


def swap(value, axis, size, bits):
    return lax.ppermute(value, axis, flips(axis, size, bits))


def bit_groups(size):
    bits = size.bit_length() - 1
    return [(s, 1 << min(2, bits - s)) for s in range(0, bits, 2)]


def cross(value, n, first):
    pairs = []
    for i in range(n):
        for core in range(2):
            bit = 1 if (core == 0) == first else 2
            pairs.append((2 * i + core, 2 * (i ^ bit) + core))
    return lax.ppermute(value, ("dp", "opt"), pairs)


def added(a, b):
    return (a.astype(F32) + b.astype(F32)).astype(BF16)


def pack_kernel(place, targets, unit, other, units, packed):
    both = unit[...] + other[...]
    units[...] = both
    row = iota((2 * PAIRS, 128), 0)
    marks = jnp.zeros((2 * PAIRS, 128), jnp.int32)
    for j in range(PAIRS):
        marks = jnp.where(row == j, targets[j], marks)
    marks = jnp.where(iota((2 * PAIRS, 128), 1) < 64, marks >> 5, marks & 31)
    packed[0, :, 0:D] = both.astype(BF16)
    packed[0, :, D : D + 128] = marks.astype(F32).astype(BF16)


def pack(place, targets, unit, other):
    return call(
        pack_kernel,
        [(1, place), (1, targets), (0, unit), (0, other)],
        [(unit.shape, F32), ((1, 2 * PAIRS, D + 128), BF16)],
        name="pack",
        vmem=4,
    )


def join_kernel(*refs):
    ins, out = refs[:-1], refs[-1]
    at = 0
    for ref in ins:
        out[at : at + ref.shape[0]] = ref[...]
        at += ref.shape[0]


def join(parts):
    rows = sum(p.shape[0] for p in parts)
    return call(
        join_kernel,
        [(0, p) for p in parts],
        [((rows,) + parts[0].shape[1:], parts[0].dtype)],
        name="join",
        vmem=4,
    )[0]


def pair_sum_kernel(keep, other, stay, go):
    for half in range(2):
        stay[half] = added(keep[2 * half], other[2 * half])
        go[half] = added(keep[2 * half + 1], other[2 * half + 1])


def first_sum_kernel(stay, other, keep, send):
    keep[0] = added(stay[0], other[0])
    send[0] = added(stay[1], other[1])


def last_sum_kernel(keep, other, out):
    out[...] = added(keep[...], other[...])


class Part:
    def __init__(self, keep, send, n):
        self.n = n
        self.keep = keep
        self.other = swap(send, "opt", 2, 1)

    def first(self):
        half = ((2,) + self.keep.shape[1:], BF16)
        self.keep, go = call(
            pair_sum_kernel,
            [(0, self.keep), (0, self.other)],
            [half, half],
            name="pair_sum",
            vmem=4,
        )
        self.other = cross(go, self.n, True)
        return self.keep

    def second(self):
        one = ((1,) + self.keep.shape[1:], BF16)
        self.keep, go = call(
            first_sum_kernel,
            [(0, self.keep), (0, self.other)],
            [one, one],
            name="first_sum",
            vmem=4,
        )
        self.other = cross(go, self.n, False)
        return self.keep

    def add(self):
        self.keep = call(
            last_sum_kernel,
            [(0, self.keep), (0, self.other)],
            [(self.keep.shape, BF16)],
            name="last_sum",
            vmem=4,
        )[0]
        return self.keep

    def line(self, bit):
        self.add()
        self.other = swap(self.keep, "dp", self.n, bit)
        return self.keep

    def ready(self):
        bit = 16
        while bit < self.n:
            self.line(bit)
            bit *= 2
        return self.add()

    def near(self, chunk):
        self.keep = chunk
        self.other = cross(chunk, self.n, False)

    def far(self):
        self.keep = join([self.keep, self.other])
        self.other = cross(self.keep, self.n, True)
        return self.keep

    def whole(self):
        return self.keep, self.other


def squares_kernel(place, *refs):
    parts, vgrad, out = refs[:-2], refs[-2], refs[-1]
    acc = jnp.zeros((8, 128), F32)
    for part in parts:
        for k in range(part.shape[0]):
            for c in range(part.shape[2] // 128):
                v = part[k, :, 128 * c : 128 * c + 128].astype(F32)
                acc = acc + jnp.sum((v * v).reshape(CHUNK // 8, 8, 128), axis=0)
    if vgrad is not None:
        v = vgrad[0, CHUNK : CHUNK + 16, :].astype(F32)
        row = iota((16, D), 0)
        low_row = 6 * place[0]
        v = jnp.where((row >= low_row) & (row < low_row + 6), v * v, 0.0)
        s = v[0:8] + v[8:16]
        acc = acc + (s[:, 0:128] + s[:, 128:256] + s[:, 256:384])
    out[...] = acc


def total_kernel(a, b, c, d, out):
    out[...] = (a[...] + b[...]) + (c[...] + d[...])


def squares(place, parts, vgrad=None):
    ins = [(1, place)] + [(0, p) for p in parts]
    kernel = squares_kernel
    if vgrad is not None:
        ins.append((0, vgrad))
    else:

        def kernel(place, *refs):
            squares_kernel(place, *refs[:-1], None, refs[-1])

    return call(kernel, ins, [((8, 128), F32)], name="squares", vmem=4)[0]


def adamw(parameter, first_state, second, clipped, rate):
    first_new = BETA_ONE * first_state + (1.0 - BETA_ONE) * clipped
    second_new = BETA_TWO * second + (1.0 - BETA_TWO) * clipped * clipped
    direction = (first_new * (1.0 / (1.0 - BETA_ONE**STEP))) / (
        jnp.sqrt(second_new * (1.0 / (1.0 - BETA_TWO**STEP))) + ADAM_EPS
    )
    return parameter - rate * (direction + DECAY_RATE * parameter), first_new, second_new


SPANS = (
    ((0, FF, 4 * D + FF),),
    ((0, FF, 4 * D),),
    ((0, D, 3 * D),) + tuple((D + D * g + 128 * c, 128, D * c + 128 * g) for g in range(2) for c in range(3)),
    tuple((128 * c, 128, D * c + 256) for c in range(3)),
)


def adamw_kernel(place, *refs):
    sums, refs = refs[:2], refs[2:]
    (vgrad, w, m, v, pv, pm, pq), refs = refs[:7], refs[7:]
    parts, refs = refs[:8], refs[8:]
    outs, (npv, npm, npq, norm), scrs, sems = refs[:4], refs[4:8], refs[8:12], refs[12]
    opt = place[0]
    total = sums[0][...] + sums[1][...]
    total = jnp.sum(jnp.sum(total, axis=1, keepdims=True), axis=0, keepdims=True)
    grad_norm = jnp.sqrt(total)
    factor = jnp.minimum(1.0, CLIP_NORM / (grad_norm + 1e-06))
    norm[...] = grad_norm
    g = vgrad[0, CHUNK : CHUNK + 16, :].astype(F32)
    g = jnp.where(opt == 0, g[0:6], g[6:12])
    a, b, c = adamw(pv[...], pm[...], pq[...], g * factor, VECTOR_RATE)
    npv[...] = a
    npm[...] = b
    npq[...] = c
    copies = []
    for r in range(4):
        base = CHUNK * place[4 + r]

        def rows(i, carry, r=r, base=base):
            at = aligned(base + i * 16, 16, 16)
            for p, spans in enumerate(SPANS):
                part = parts[2 * p + r % 2]
                for source, width, column in spans:
                    for k in range(0, width, 384):
                        size = min(384, width - k)
                        cols = slice(column + k, column + k + size)
                        g = part[
                            r // 2, aligned(i * 16, 16, 16), source + k : source + k + size
                        ].astype(F32)
                        new = adamw(w[at, cols], m[at, cols], v[at, cols], g * factor, LEARN_RATE)
                        for scr, value in zip(scrs, new + (new[0].astype(BF16),)):
                            scr[at, cols] = value
            return carry

        lax.fori_loop(0, CHUNK // 16, rows, 0)
        at = aligned(base, CHUNK, 16)
        for i, (scr, out) in enumerate(zip(scrs, outs)):
            copy = pltpu.make_async_copy(scr.at[at, :], out.at[at, :], sems.at[r, i])
            copy.start()
            copies.append(copy)
    for copy in copies:
        copy.wait()


def update(place, sums, vgrad, w, m, v, pv, pm, pq, parts):
    ins = tuple(sums) + (vgrad, w, m, v, pv, pm, pq) + tuple(parts)
    shapes = [(w.shape, F32)] * 3 + [(w.shape, BF16)] + [(pv.shape, F32)] * 3 + [((1, 1), F32)]
    return pl.pallas_call(
        adamw_kernel,
        out_shape=[jax.ShapeDtypeStruct(s, d) for s, d in shapes],
        in_specs=[SMEM] + [VMEM] * len(ins),
        out_specs=[ANY] * 4 + [VMEM] * 4,
        scratch_shapes=[
            pltpu.VMEM(w.shape, F32),
            pltpu.VMEM(w.shape, F32),
            pltpu.VMEM(w.shape, F32),
            pltpu.VMEM(w.shape, BF16),
            pltpu.SemaphoreType.DMA((4, 4)),
        ],
        compiler_params=pltpu.CompilerParams(vmem_limit_bytes=16 << 20),
        cost_estimate=pl.CostEstimate(
            flops=4000000000, bytes_accessed=26 * w.size, transcendentals=0
        ),
        name="adamw",
    )(place, *ins)


def shards(
    n,
    tokens,
    lengths,
    query_index,
    doc_index,
    targets,
    weights,
    first_moment,
    second_moment,
    vectors,
    vec_first,
    vec_second,
):
    opt = lax.axis_index("opt")
    me = lax.axis_index("dp")
    plane = me & 3
    columns = [jnp.where(opt == 0, plane ^ r, plane ^ turned(r)) for r in range(4)]
    place = jnp.stack([opt, plane, me, (me >> 2) & 3] + columns).astype(jnp.int32)
    lengths = lengths.reshape(SEGS)
    chosen = jnp.concatenate([query_index, doc_index])
    groups = bit_groups(n)

    extra = jnp.pad(vectors, ((0, 10), (0, 2 * D)))
    w_own = jnp.concatenate([weights[:, : 3 * D], extra], axis=0).astype(BF16)
    w_other = swap(w_own, "opt", 2, 1)
    wo_own = weights[:, 3 * D : 4 * D].astype(BF16)
    wu_own = weights[:, 4 * D : 4 * D + FF].astype(BF16)
    wd_own = weights[:, 4 * D + FF :].astype(BF16)
    wo = (wo_own, swap(wo_own, "opt", 2, 1))
    wu = (wu_own, swap(wu_own, "opt", 2, 1))
    wd = (wd_own, swap(wd_own, "opt", 2, 1))
    proj, att, lse, segc, segr, vec = attend(place, lengths, tokens, w_own, w_other)
    xhat1, inv1, hlow, act, slope, xhat2, inv2, unit, uscale = mlp(
        place, lengths, chosen, att, tokens, segr, vec, wo + wu + wd
    )
    units, stack = pack(place, targets, unit, swap(unit, "opt", 2, 1))
    for shift, size in groups:
        pieces = [stack] + [swap(stack, "dp", n, k << shift) for k in range(1, size)]
        if (shift, size) != groups[-1]:
            stack = join(pieces)
    dsec, dlow, keep, send, dsums = down_backward(
        n, place, lengths, chosen, units, segc, uscale, (xhat2, inv2, act), vec, pieces
    )
    down = Part(keep, send, n)
    dup, keep, send, usums = up_backward(place, dlow, slope, hlow, wd, [])
    up = Part(keep, send, n)
    dfirst, datt, delta, okeep, osend, fsums = first_backward(
        place, dup, dsec, xhat1, inv1, att, vec, wu + wo, [down.first()]
    )
    ties = [down.second(), up.first()]
    ins = (tokens, proj, datt, lse, delta, segc, segr)
    part0, zkeep, zsend, sums0 = heads_backward(0, place, ins, (), ties)
    ties = [down.line(4), up.second()]
    part1, keep, send, sums1 = heads_backward(
        1, place, ins, (okeep, osend, zkeep, zsend), ties + [part0]
    )
    low = Part(keep, send, n)
    ties = [down.line(8), up.line(4)]
    part2, keep, send, _ = heads_backward(
        2, place, ins, (dsums, usums, fsums, sums0, sums1), ties + [part1]
    )
    last = Part(keep, send, n)
    chunk = down.ready()
    down.near(chunk)
    ties = [chunk, up.line(8), low.first()]
    igrad = input_backward(place, (part0, part1, part2), dfirst, w_own, w_other, ties)
    last.first()
    low.second()
    down.far()
    up.near(up.ready())
    iother = swap(igrad, "opt", 2, 1)
    low.line(4)
    last.second()
    up.far()
    low.line(8)
    last.line(4)
    low.near(low.ready())
    last.line(8)
    low.far()
    chunk = last.ready()
    last.near(chunk[:, :CHUNK])
    last.far()
    pieces = down.whole() + up.whole() + low.whole() + last.whole()
    sums = [squares(place, p.whole()) for p in (down, up, low)]
    mine = squares(place, last.whole(), chunk)
    mine = call(
        total_kernel, [(0, s) for s in sums + [mine]], [((8, 128), F32)], name="total", vmem=4
    )[0]
    sums = [mine, swap(mine, "opt", 2, 1)]

    lower = jnp.where(opt == 0, igrad, iother)
    upper = jnp.where(opt == 0, iother, igrad)
    input_grad = jnp.concatenate(
        [lower[:OFF], lower[OFF:] + upper[: WIN - OFF], upper[WIN - OFF :]], axis=0
    )
    nw, nm, nv, nlow, npv, npm, npq, norm = update(
        place, sums, chunk, weights, first_moment, second_moment,
        vectors, vec_first, vec_second, pieces,
    )
    return (norm.reshape(()), input_grad, nw, nm, nv, nlow, npv, npm, npq)


def solution(mesh):
    rows = P("opt", None)
    in_specs = (P("dp", None), P("dp", None), P("dp"), P("dp"), P("dp")) + (rows,) * 6
    out_specs = (P(), P("dp", None)) + (rows,) * 7
    n = mesh.shape["dp"]
    return jax.shard_map(
        functools.partial(shards, n),
        mesh=mesh,
        in_specs=in_specs,
        out_specs=out_specs,
        check_vma=False,
    )
```

```python
import functools

import jax
import jax.numpy as jnp
from jax import lax
from jax.experimental import pallas as pl
from jax.experimental.pallas import tpu as pltpu
from jax.sharding import PartitionSpec as P

D = 384
HEADS = 12
HD = 32
FF = 1536
SEQ = 1024
SEGS = 16
PAIRS = 8
STEP = 10

WIN = 576
OFF = SEQ - WIN
PAD = 640
BLOCK = 128
BANDS = tuple((q, max(0, q - 128), min(WIN, q + 256)) for q in range(0, WIN, BLOCK))
BAND_ROWS = tuple(sum(b[2] - b[1] for b in BANDS[:i]) for i in range(len(BANDS) + 1))
ROWS = 64

LN_EPS = 1e-06
POOL_EPS = 1e-06
SCORE_SCALE = 50.0
CLIP_NORM = 0.001
BETA_ONE = 0.9
BETA_TWO = 0.98
ADAM_EPS = 1e-08
LEARN_RATE = 0.05
VECTOR_RATE = 0.3
DECAY_RATE = 0.01
NEG_BIG = -1e30
HALF = D // 2
CHUNK = HALF // 4
EXP2_SCALE = HD ** (-0.5) * 1.4426950408889634

F32 = jnp.float32
BF16 = jnp.bfloat16
VMEM = pl.BlockSpec(memory_space=pltpu.VMEM)
SMEM = pl.BlockSpec(memory_space=pltpu.SMEM)
ANY = pl.BlockSpec(memory_space=pl.ANY)
HBM = pl.BlockSpec(memory_space=pltpu.HBM)


def nn(a, b):
    return jnp.dot(a, b, preferred_element_type=F32)


def nt(a, b):
    return lax.dot_general(a, b, (((1,), (1,)), ((), ())), preferred_element_type=F32)


def tn(a, b):
    return lax.dot_general(a, b, (((0,), (0,)), ((), ())), preferred_element_type=F32)


def exact(a, b, dims):
    return lax.dot_general(
        a, b, (dims, ((), ())), precision=lax.Precision.HIGHEST, preferred_element_type=F32
    )


def iota(shape, axis):
    return lax.broadcasted_iota(jnp.int32, shape, axis)


def low_pair(value):
    high = value.astype(BF16)
    return high, (value - high.astype(F32)).astype(BF16)


def aligned(start, size, unit):
    return pl.ds(pl.multiple_of(start, unit), size)


def assemble(dst, own, other, opt):
    dst[aligned(HALF * opt, HALF, 64), :] = own[0:HALF, :]
    dst[aligned(HALF * (1 - opt), HALF, 64), :] = other[0:HALF, :]


def call(kernel, ins, outs, scratch=(), micros=0, name=None, vmem=12, after=()):
    specs = [SMEM if s else VMEM for s, _ in ins] + [ANY] * len(after)
    count = len(ins)

    def body(*refs):
        kernel(*refs[:count], *refs[count + len(after) :])

    shapes = [jax.ShapeDtypeStruct(s, d) for s, d in outs]
    moved = sum(a.size * a.dtype.itemsize for _, a in ins)
    moved += sum(s.size * s.dtype.itemsize for s in shapes)
    return pl.pallas_call(
        body,
        out_shape=shapes,
        in_specs=specs,
        out_specs=[VMEM] * len(shapes),
        scratch_shapes=list(scratch),
        compiler_params=pltpu.CompilerParams(vmem_limit_bytes=vmem << 20),
        cost_estimate=pl.CostEstimate(
            flops=micros * 1100000000, bytes_accessed=moved, transcendentals=0
        ),
        name=name,
    )(*[a for _, a in ins], *after)


def first_cast_kernel(weights, vectors, out, buffer, rows, sems):
    copies = [
        pltpu.make_async_copy(weights.at[:, 0 : 3 * D], buffer, sems.at[0]),
        pltpu.make_async_copy(vectors, rows, sems.at[1]),
    ]
    for copy in copies:
        copy.start()
    out[HALF : HALF + 16, :] = jnp.zeros((16, 3 * D), BF16)
    copies[1].wait()
    block = jnp.concatenate([rows[...], jnp.zeros((10, D), F32)], axis=0)
    out[HALF : HALF + 16, 0:D] = block.astype(BF16)
    copies[0].wait()
    out[0:HALF, :] = buffer[...].astype(BF16)


def first_cast(weights, vectors):
    return pl.pallas_call(
        first_cast_kernel,
        out_shape=jax.ShapeDtypeStruct((HALF + 16, 3 * D), BF16),
        in_specs=[HBM, HBM],
        out_specs=VMEM,
        scratch_shapes=[
            pltpu.VMEM((HALF, 3 * D), F32),
            pltpu.VMEM((6, D), F32),
            pltpu.SemaphoreType.DMA((2,)),
        ],
        compiler_params=pltpu.CompilerParams(vmem_limit_bytes=57 << 20),
        name="first_cast",
    )(weights, vectors)


def cast_kernel(weights, after, wo, wu, wd, buffer, sems):
    spans = ((0, D, wo), (D, FF, wu), (D + FF, FF, wd))
    copies = []
    for i, (at, size, _) in enumerate(spans):
        copies.append(
            pltpu.make_async_copy(
                weights.at[:, 3 * D + at : 3 * D + at + size], buffer.at[:, at : at + size], sems.at[i]
            )
        )
        copies[-1].start()
    for copy, (at, size, out) in zip(copies, spans):
        copy.wait()
        out[...] = buffer[:, at : at + size].astype(BF16)


def cast(weights, after):
    return pl.pallas_call(
        cast_kernel,
        out_shape=[jax.ShapeDtypeStruct((HALF, c), BF16) for c in (D, FF, FF)],
        in_specs=[HBM, ANY],
        out_specs=[VMEM] * 3,
        scratch_shapes=[pltpu.VMEM((HALF, D + 2 * FF), F32), pltpu.SemaphoreType.DMA((3,))],
        compiler_params=pltpu.CompilerParams(vmem_limit_bytes=57 << 20),
        name="cast",
    )(weights, after)


def head_stack(rows):
    lane_head = iota(rows.shape, 1) // HD
    zero = jnp.zeros_like(rows)
    return jnp.concatenate([jnp.where(lane_head == j, rows, zero) for j in range(4)], axis=0)


def attend_kernel(
    place, lengths, tokens, w_own, w_other, proj, att, lse, segc, segr, vec, wfull, bias, vt
):
    opt = place[0]
    assemble(wfull, w_own, w_other, opt)
    mine = w_own[HALF : HALF + 16, 0:D].astype(F32)
    others = w_other[HALF : HALF + 16, 0:D].astype(F32)
    first = opt == 0
    vec[0:6, :] = jnp.where(first, mine, others)[0:6]
    vec[6:12, :] = jnp.where(first, others, mine)[0:6]
    vec[12:16, :] = jnp.zeros((4, D), F32)

    pos_col = iota((WIN, 128), 0) + OFF * opt
    pos_row = iota((8, PAD), 1) + OFF * opt
    seg_col = jnp.zeros((WIN, 128), jnp.int32)
    seg_row = jnp.zeros((8, PAD), jnp.int32)
    bound = jnp.int32(0)
    for s in range(SEGS):
        bound = bound + lengths[s]
        seg_col = seg_col + (pos_col >= bound).astype(jnp.int32)
        seg_row = seg_row + (pos_row >= bound).astype(jnp.int32)
    segc[...] = seg_col
    segr[...] = seg_row
    for i, (q0, k0, k1) in enumerate(BANDS):
        bias[BAND_ROWS[i] : BAND_ROWS[i + 1], :] = jnp.where(
            segc[k0:k1, :] == segr[0:1, q0 : q0 + BLOCK], 0.0, NEG_BIG
        )

    x = tokens[aligned(OFF * opt, WIN, 64), :]
    for c in range(3):
        acc = nn(x, wfull[:, c * D : (c + 1) * D])
        if c != 1:
            acc = acc + vec[(0 if c == 0 else 1) : (1 if c == 0 else 2), :]
        proj[0:WIN, c * D : (c + 1) * D] = acc.astype(BF16)
    proj[WIN:PAD, :] = jnp.zeros((PAD - WIN, 3 * D), BF16)

    def group(g, carry):
        def lanes(part):
            return aligned(part * D + 128 * g, 128, 128)

        for t in range(PAD // 128):
            vt[:, 128 * t : 128 * t + 128] = (
                proj[128 * t : 128 * t + 128, lanes(2)].astype(F32).T.astype(BF16)
            )
        for i, (q0, k0, k1) in enumerate(BANDS):
            stack = head_stack(proj[q0 : q0 + BLOCK, lanes(0)])
            st = nt(proj[k0:k1, lanes(1)], stack)
            outs = []
            for j in range(4):
                t = (
                    st[:, j * BLOCK : (j + 1) * BLOCK] * EXP2_SCALE
                    + bias[BAND_ROWS[i] : BAND_ROWS[i + 1], :]
                )
                peak = jnp.max(t, axis=0, keepdims=True)
                powers = jnp.exp2(t - peak)
                total = jnp.sum(powers, axis=0, keepdims=True)
                lse[g, j : j + 1, q0 : q0 + BLOCK] = peak + jnp.log2(total)
                o = nn(vt[j * HD : (j + 1) * HD, k0:k1], powers.astype(BF16))
                outs.append(o * (1.0 / total))
            rows = min(BLOCK, WIN - q0)
            att[q0 : q0 + rows, aligned(128 * g, 128, 128)] = (
                jnp.concatenate(outs, axis=0).T[0:rows].astype(BF16)
            )
        return carry

    lax.fori_loop(0, 3, group, 0)


def attend(place, lengths, tokens, w_own, w_other):
    return call(
        attend_kernel,
        [(1, place), (1, lengths), (0, tokens), (0, w_own), (0, w_other)],
        [
            ((PAD, 3 * D), BF16),
            ((WIN, D), BF16),
            ((3, 4, PAD), F32),
            ((WIN, 128), jnp.int32),
            ((8, PAD), jnp.int32),
            ((16, D), F32),
        ],
        [
            pltpu.VMEM((D, 3 * D), BF16),
            pltpu.VMEM((BAND_ROWS[-1], 128), F32),
            pltpu.VMEM((128, PAD), BF16),
        ],
        micros=8,
        name="attend",
    )


def owned(place, lengths, segment):
    bound = jnp.int32(0)
    count = jnp.int32(0)
    for s in range(SEGS):
        bound = bound + lengths[s]
        count = count + (bound <= WIN).astype(jnp.int32)
    low_side = (segment < count).astype(jnp.int32)
    return low_side == (place[0] == 0).astype(jnp.int32)


def mlp_kernel(
    place, lengths, chosen, att, tokens, segr, vec, wo_own, wo_other, wu_own, wu_other,
    wd_own, wd_other, xhat1, inv1, hlow, act, slope, xhat2, inv2, unit, uscale,
    wo, wu, wd, tmp, hid, ench, encl,
):
    opt = place[0]
    assemble(wo, wo_own, wo_other, opt)
    assemble(wu, wu_own, wu_other, opt)
    assemble(wd, wd_own, wd_other, opt)
    tmp[...] = nn(att[...], wo[...])

    def first_norm(i, carry):
        r = aligned(i * ROWS, ROWS, ROWS)
        x = tokens[aligned(OFF * opt + i * ROWS, ROWS, ROWS), :].astype(F32)
        v = tmp[r, :] + vec[2:3, :] + x
        centred = v - jnp.mean(v, axis=1, keepdims=True)
        inverse = lax.rsqrt(jnp.mean(centred * centred, axis=1, keepdims=True) + LN_EPS)
        normed = centred * inverse
        xhat1[r, :] = normed
        inv1[r, :] = jnp.broadcast_to(inverse, (ROWS, 128))
        h = normed * vec[8:9, :] + vec[9:10, :]
        hid[r, :] = h
        hlow[r, :] = h.astype(BF16)
        return carry

    lax.fori_loop(0, WIN // ROWS, first_norm, 0)

    for c in range(4):
        cols = slice(c * D, (c + 1) * D)
        tmp[...] = nn(hlow[...], wu[:, cols])

        def gelu(i, carry, cols=cols, c=c):
            r = aligned(i * ROWS, ROWS, ROWS)
            u = tmp[r, :] + vec[3 + c : 4 + c, :]
            half = lax.erf(u * 0.7071067811865476) * 0.5 + 0.5
            act[r, cols] = (u * half).astype(BF16)
            slope[r, cols] = half + u * jnp.exp(-0.5 * u * u) * 0.3989422804014327
            return carry

        lax.fori_loop(0, WIN // ROWS, gelu, 0)

    tmp[...] = nt(act[...], wd[...])

    def second_norm(i, carry):
        r = aligned(i * ROWS, ROWS, ROWS)
        v = tmp[r, :] + vec[7:8, :] + hid[r, :]
        centred = v - jnp.mean(v, axis=1, keepdims=True)
        inverse = lax.rsqrt(jnp.mean(centred * centred, axis=1, keepdims=True) + LN_EPS)
        normed = centred * inverse
        xhat2[r, :] = normed
        inv2[r, :] = jnp.broadcast_to(inverse, (ROWS, 128))
        high, rest = low_pair(normed * vec[10:11, :] + vec[11:12, :])
        ench[r, :] = high
        encl[r, :] = rest
        return carry

    lax.fori_loop(0, WIN // ROWS, second_norm, 0)

    seg = segr[0:1, 0:WIN]
    row_id = iota((2 * PAIRS, WIN), 0)
    wanted = jnp.zeros((2 * PAIRS, WIN), jnp.int32)
    for j in range(2 * PAIRS):
        wanted = jnp.where(row_id == j, chosen[j], wanted)
    mask = owned(place, lengths, jnp.broadcast_to(seg, (2 * PAIRS, WIN)))
    onehot = jnp.where((wanted == seg) & mask, 1.0, 0.0)
    count = jnp.maximum(jnp.sum(onehot, axis=1, keepdims=True), 1.0)
    hot = onehot.astype(BF16)
    pooled = (nn(hot, ench[...]) + nn(hot, encl[...])) / count
    inverse_len = lax.rsqrt(jnp.sum(pooled * pooled, axis=1, keepdims=True) + POOL_EPS)
    unit[...] = pooled * inverse_len
    uscale[...] = jnp.broadcast_to(inverse_len / count, (2 * PAIRS, 128))


def mlp(place, lengths, chosen, att, tokens, segr, vec, halves):
    return call(
        mlp_kernel,
        [(1, place), (1, lengths), (1, chosen), (0, att), (0, tokens), (0, segr), (0, vec)]
        + [(0, h) for h in halves],
        [
            ((WIN, D), F32),
            ((WIN, 128), F32),
            ((WIN, D), BF16),
            ((WIN, FF), BF16),
            ((WIN, FF), F32),
            ((WIN, D), F32),
            ((WIN, 128), F32),
            ((2 * PAIRS, D), F32),
            ((2 * PAIRS, 128), F32),
        ],
        [
            pltpu.VMEM((D, D), BF16),
            pltpu.VMEM((D, FF), BF16),
            pltpu.VMEM((D, FF), BF16),
            pltpu.VMEM((WIN, D), F32),
            pltpu.VMEM((WIN, D), F32),
            pltpu.VMEM((WIN, D), BF16),
            pltpu.VMEM((WIN, D), BF16),
        ],
        micros=10,
        name="mlp",
    )


def turned(chunk):
    return (chunk & 1) * 2 + (chunk >> 1)


def split_rows(grad, keep, send, place, cols, stepwise=False):
    opt = place[0]
    for c in range(4):
        straight = c ^ place[1]
        mine = theirs = straight
        if stepwise:
            mine = jnp.where(opt == 0, straight, turned(straight))
            theirs = jnp.where(opt == 0, turned(straight), straight)
        keep[mine, 0:CHUNK, cols] = grad[aligned(HALF * opt + CHUNK * c, CHUNK, 16), :].astype(BF16)
        send[theirs, 0:CHUNK, cols] = grad[
            aligned(HALF * (1 - opt) + CHUNK * c, CHUNK, 16), :
        ].astype(BF16)


def column_sums(value):
    return jnp.sum(value.reshape(ROWS // 8, 8, D), axis=0)


def norm_backward(grad_at, normed_ref, inverse_ref, gain, out, low_out, sums, at):
    def block(i, carry):
        scale_sum, shift_sum, bias_sum = carry
        r = aligned(i * ROWS, ROWS, ROWS)
        g = grad_at(r)
        normed = normed_ref[r, :]
        scaled = g * gain
        inner = (
            scaled
            - jnp.mean(scaled, axis=1, keepdims=True)
            - normed * jnp.mean(scaled * normed, axis=1, keepdims=True)
        ) * inverse_ref[r, 0:1]
        out[r, :] = inner
        low_out[r, :] = inner.astype(BF16)
        return (
            scale_sum + column_sums(g * normed),
            shift_sum + column_sums(g),
            bias_sum + column_sums(inner),
        )

    zero = jnp.zeros((8, D), F32)
    scale_sum, shift_sum, bias_sum = lax.fori_loop(0, WIN // ROWS, block, (zero, zero, zero))
    sums[at : at + 1, :] = jnp.sum(bias_sum, axis=0, keepdims=True)
    sums[at + 1 : at + 2, :] = jnp.sum(scale_sum, axis=0, keepdims=True)
    sums[at + 2 : at + 3, :] = jnp.sum(shift_sum, axis=0, keepdims=True)


def down_kernel(
    count, order, place, lengths, chosen, units, segc, uscale, xhat2, inv2, act, vec, *rest
):
    pieces, (dsec, dlow, keep, send, sums, queries, docs, marks, grad) = rest[:-9], rest[-9:]
    me = place[2]
    per = pieces[0].shape[0]
    for p, piece in enumerate(pieces):
        for j in range(per):
            at = order[p * per + j]
            r = slice(at * PAIRS, (at + 1) * PAIRS)
            both = piece[j].astype(F32)
            queries[r, :] = both[0:PAIRS, 0:D]
            docs[r, :] = both[PAIRS : 2 * PAIRS, 0:D]
            marks[r, :] = both[0:PAIRS, D : D + 128]
    total = count * PAIRS
    q = queries[...].astype(BF16)
    d = docs[...].astype(BF16)
    logits = SCORE_SCALE * nt(q, d)
    peak = jnp.max(logits, axis=1, keepdims=True)
    powers = jnp.exp(logits - peak)
    soft = powers / jnp.sum(powers, axis=1, keepdims=True)
    col = iota((total, total), 1)
    doc_id = ((col // PAIRS) ^ me) * PAIRS + lax.rem(col, PAIRS)
    hit = (marks[:, 0:1] * 32.0 + marks[:, 64:65]).astype(jnp.int32) == doc_id
    d_logits = (soft - jnp.where(hit, 1.0, 0.0)) * (SCORE_SCALE / total)
    high, rest_low = low_pair(d_logits[0:PAIRS, :])
    d_q = nn(high, d) + nn(rest_low, d)
    high, rest_low = low_pair(d_logits[:, 0:128].T[0:PAIRS, :])
    d_d = nn(high, q) + nn(rest_low, q)
    d_units = jnp.concatenate([d_q, d_d], axis=0)
    u = units[...]
    d_pool = uscale[:, 0:1] * (d_units - u * jnp.sum(u * d_units, axis=1, keepdims=True))
    lane = iota((8, 2 * PAIRS), 1)
    wanted = jnp.zeros((8, 2 * PAIRS), jnp.int32)
    for j in range(2 * PAIRS):
        wanted = jnp.where(lane == j, chosen[j], wanted)
    seg = segc[:, 0 : 2 * PAIRS]
    mask = owned(place, lengths, seg)
    hot = jnp.where((seg == wanted[0:1, :]) & mask, 1.0, 0.0).astype(BF16)
    high, rest_low = low_pair(d_pool)
    dsec[...] = nn(hot, high) + nn(hot, rest_low)
    norm_backward(lambda r: dsec[r, :], xhat2, inv2, vec[10:11, :], dsec, dlow, sums, 0)
    sums[3:8, :] = jnp.zeros((5, D), F32)
    for c in range(4):
        cols = slice(c * D, (c + 1) * D)
        grad[...] = tn(dlow[...], act[:, cols])
        split_rows(grad, keep, send, place, cols, True)


def down_backward(count, order, place, lengths, chosen, units, segc, uscale, saved, vec, pieces):
    total = count * PAIRS
    return call(
        functools.partial(down_kernel, count, order),
        [(1, place), (1, lengths), (1, chosen), (0, units), (0, segc), (0, uscale)]
        + [(0, s) for s in saved]
        + [(0, vec)]
        + [(0, p) for p in pieces],
        [
            ((WIN, D), F32),
            ((WIN, D), BF16),
            ((4, CHUNK, FF), BF16),
            ((4, CHUNK, FF), BF16),
            ((8, D), F32),
        ],
        [
            pltpu.VMEM((total, D), F32),
            pltpu.VMEM((total, D), F32),
            pltpu.VMEM((total, 128), F32),
            pltpu.VMEM((D, D), F32),
        ],
        micros=4,
        name="down_backward",
    )


def up_kernel(place, dlow, slope, hlow, wd_own, wd_other, dup, keep, send, sums, wd, grad):
    opt = place[0]
    assemble(wd, wd_own, wd_other, opt)
    for c in range(4):
        cols = slice(c * D, (c + 1) * D)
        part = (nn(dlow[...], wd[:, cols]) * slope[:, cols]).astype(BF16)
        dup[:, cols] = part
        sums[c : c + 1, :] = jnp.sum(part.astype(F32), axis=0, keepdims=True)
        grad[...] = tn(hlow[...], dup[:, cols])
        split_rows(grad, keep, send, place, cols, True)


def up_backward(place, dlow, slope, hlow, halves, after):
    return call(
        up_kernel,
        [(1, place)] + [(0, a) for a in (dlow, slope, hlow) + tuple(halves)],
        [((WIN, FF), BF16), ((4, CHUNK, FF), BF16), ((4, CHUNK, FF), BF16), ((4, D), F32)],
        [pltpu.VMEM((D, FF), BF16), pltpu.VMEM((D, D), F32)],
        micros=3,
        name="up_backward",
        after=after,
    )


def first_kernel(
    place, dup, dsec, xhat1, inv1, att, vec, wu_own, wu_other, wo_own, wo_other,
    dfirst, datt, delta, okeep, osend, sums, wu, wo, grad, dlow,
):
    opt = place[0]
    assemble(wu, wu_own, wu_other, opt)
    assemble(wo, wo_own, wo_other, opt)
    dfirst[...] = nt(dup[...], wu[...])
    norm_backward(
        lambda r: dfirst[r, :] + dsec[r, :], xhat1, inv1, vec[8:9, :], dfirst, dlow, sums, 0
    )
    sums[3:8, :] = jnp.zeros((5, D), F32)
    grad[...] = tn(att[...], dlow[...])
    split_rows(grad, okeep, osend, place, slice(0, D))
    da = nt(dlow[...], wo[...]).astype(BF16)
    datt[0:WIN, :] = da
    datt[WIN:PAD, :] = jnp.zeros((PAD - WIN, D), BF16)
    high, rest = low_pair(da.astype(F32) * att[...].astype(F32))
    heads = (iota((16, D), 1) // HD == iota((16, D), 0)).astype(F32).astype(BF16)
    delta[:, 0:WIN] = nt(heads, high) + nt(heads, rest)
    delta[:, WIN:PAD] = jnp.zeros((16, PAD - WIN), F32)


def first_backward(place, dup, dsec, xhat1, inv1, att, vec, halves, after):
    return call(
        first_kernel,
        [(1, place)] + [(0, a) for a in (dup, dsec, xhat1, inv1, att, vec) + tuple(halves)],
        [
            ((WIN, D), F32),
            ((PAD, D), BF16),
            ((16, PAD), F32),
            ((4, CHUNK, D), BF16),
            ((4, CHUNK, D), BF16),
            ((8, D), F32),
        ],
        [
            pltpu.VMEM((D, FF), BF16),
            pltpu.VMEM((D, D), BF16),
            pltpu.VMEM((D, D), F32),
            pltpu.VMEM((WIN, D), BF16),
        ],
        micros=3,
        name="first_backward",
        after=after,
    )


def heads_kernel(g, place, tokens, proj, datt, lse, delta, segc, segr, *rest):
    rest, (dproj, keep, send, sums, kt, dk, dv, grad, ktmp, stmp) = rest[:-10], rest[-10:]

    def lanes(part):
        return slice(part * D + 128 * g, part * D + 128 * g + 128)

    for t in range(PAD // 128):
        kt[:, 128 * t : 128 * t + 128] = (
            proj[128 * t : 128 * t + 128, lanes(1)].astype(F32).T.astype(BF16)
        )
    dk[...] = jnp.zeros_like(dk)
    dv[...] = jnp.zeros_like(dv)
    for q0, k0, k1 in BANDS:
        qs = head_stack(proj[q0 : q0 + BLOCK, lanes(0)])
        gs = head_stack(datt[q0 : q0 + BLOCK, lanes(0)])
        st = nt(proj[k0:k1, lanes(1)], qs)
        dp = nt(proj[k0:k1, lanes(2)], gs)
        same = segc[k0:k1, :] == segr[0:1, q0 : q0 + BLOCK]
        bias = jnp.where(same, 0.0, NEG_BIG)
        probs, d_scores, dq = [], [], []
        for j in range(4):
            cols = slice(j * BLOCK, (j + 1) * BLOCK)
            prob = jnp.exp2(st[:, cols] * EXP2_SCALE + bias - lse[g, j : j + 1, q0 : q0 + BLOCK])
            ds = prob * (dp[:, cols] - delta[4 * g + j : 4 * g + j + 1, q0 : q0 + BLOCK])
            ds = ds.astype(BF16)
            probs.append(prob.astype(BF16))
            d_scores.append(ds)
            dq.append(nn(kt[j * HD : (j + 1) * HD, k0:k1], ds))
        dv[k0:k1, :] += nn(jnp.concatenate(probs, axis=1), gs)
        dk[k0:k1, :] += nn(jnp.concatenate(d_scores, axis=1), qs)
        rows = min(BLOCK, WIN - q0)
        dqs = jnp.concatenate(dq, axis=0).T[0:rows] * HD ** (-0.5)
        dproj[q0 : q0 + rows, 0:128] = dqs.astype(BF16)
    dproj[:, 128:256] = (dk[...] * HD ** (-0.5)).astype(BF16)
    dproj[:, 256:384] = dv[...].astype(BF16)
    grad[...] = tn(tokens[aligned(OFF * place[0], WIN, 64), :], dproj[...])
    q_sum = jnp.sum(dproj[:, 0:128].astype(F32), axis=0, keepdims=True)
    v_sum = jnp.sum(dproj[:, 256:384].astype(F32), axis=0, keepdims=True)
    sums[0:1, :] = q_sum
    sums[1:2, :] = v_sum
    sums[2:8, :] = jnp.zeros((6, 128), F32)
    if g < 2:
        split_rows(grad, keep, send, place, slice(0, D))
        return
    parts, (dsums, usums, fsums, zero, one) = rest[:6], rest[6:]
    split_rows(grad, ktmp, stmp, place, slice(0, D))
    for dst, own, (zpart, opart, tpart) in (
        (keep, parts[0], (parts[2], parts[4], ktmp)),
        (send, parts[1], (parts[3], parts[5], stmp)),
    ):
        dst[:, :, 3 * D : 4 * D] = own[...]
        for h, part in enumerate((zpart, opart, tpart)):
            for c in range(3):
                dst[:, :, D * c + 128 * h : D * c + 128 * h + 128] = part[
                    :, :, 128 * c : 128 * c + 128
                ]
    rows = jnp.concatenate(
        [
            jnp.concatenate([zero[0:1], one[0:1], q_sum], axis=1),
            jnp.concatenate([zero[1:2], one[1:2], v_sum], axis=1),
            fsums[0:1, :],
            usums[0:4, :],
            dsums[0:1, :],
            fsums[1:3, :],
            dsums[1:3, :],
            jnp.zeros((4, D), F32),
        ],
        axis=0,
    ).astype(BF16)
    for c in range(4):
        for j in range(3):
            block = rows[:, 128 * j : 128 * j + 128]
            keep[c, 16 * j : 16 * j + 16, 4 * D : 4 * D + 128] = block
            send[c, 16 * j : 16 * j + 16, 4 * D : 4 * D + 128] = block


def heads_backward(g, place, ins, more, after):
    part = ((4, CHUNK, 4 * D + 128 if g == 2 else D), BF16)
    return call(
        functools.partial(heads_kernel, g),
        [(1, place)] + [(0, a) for a in tuple(ins) + tuple(more)],
        [((WIN, D), BF16), part, part, ((8, 128), F32)],
        [
            pltpu.VMEM((128, PAD), BF16),
            pltpu.VMEM((WIN, 128), F32),
            pltpu.VMEM((WIN, 128), F32),
            pltpu.VMEM((D, D), F32),
            pltpu.VMEM((4, CHUNK, D), BF16),
            pltpu.VMEM((4, CHUNK, D), BF16),
        ],
        micros=3,
        name="heads_backward",
        after=after,
    )


def input_kernel(place, dp0, dp1, dp2, dfirst, w_own, w_other, igrad, wfull, dproj):
    assemble(wfull, w_own, w_other, place[0])
    for g, part in enumerate((dp0, dp1, dp2)):
        for c in range(3):
            dproj[:, c * D + 128 * g : c * D + 128 * g + 128] = part[:, 128 * c : 128 * c + 128]
    igrad[...] = (nt(dproj[...], wfull[...]) + dfirst[...]).astype(BF16)


def input_backward(place, parts, dfirst, w_own, w_other, after):
    return call(
        input_kernel,
        [(1, place)] + [(0, a) for a in tuple(parts) + (dfirst, w_own, w_other)],
        [((WIN, D), BF16)],
        [pltpu.VMEM((D, 3 * D), BF16), pltpu.VMEM((WIN, 3 * D), BF16)],
        micros=2,
        name="input_backward",
        after=after,
    )[0]


def flips(axis, size, bits):
    return [(i, i ^ bits) for i in range(size)]


def swap(value, axis, size, bits):
    return lax.ppermute(value, axis, flips(axis, size, bits))


def bit_groups(size):
    bits = size.bit_length() - 1
    return [(s, 1 << min(2, bits - s)) for s in range(0, bits, 2)]


def cross(value, n, first):
    pairs = []
    for i in range(n):
        for core in range(2):
            bit = 1 if (core == 0) == first else 2
            pairs.append((2 * i + core, 2 * (i ^ bit) + core))
    return lax.ppermute(value, ("dp", "opt"), pairs)


def added(a, b):
    return (a.astype(F32) + b.astype(F32)).astype(BF16)


def pack_kernel(place, targets, unit, other, units, packed):
    both = unit[...] + other[...]
    units[...] = both
    row = iota((2 * PAIRS, 128), 0)
    marks = jnp.zeros((2 * PAIRS, 128), jnp.int32)
    for j in range(PAIRS):
        marks = jnp.where(row == j, targets[j], marks)
    marks = jnp.where(iota((2 * PAIRS, 128), 1) < 64, marks >> 5, marks & 31)
    packed[0, :, 0:D] = both.astype(BF16)
    packed[0, :, D : D + 128] = marks.astype(F32).astype(BF16)


def pack(place, targets, unit, other):
    return call(
        pack_kernel,
        [(1, place), (1, targets), (0, unit), (0, other)],
        [(unit.shape, F32), ((1, 2 * PAIRS, D + 128), BF16)],
        name="pack",
        vmem=4,
    )


def join_kernel(*refs):
    ins, out = refs[:-1], refs[-1]
    at = 0
    for ref in ins:
        out[at : at + ref.shape[0]] = ref[...]
        at += ref.shape[0]


def join(parts):
    rows = sum(p.shape[0] for p in parts)
    return call(
        join_kernel,
        [(0, p) for p in parts],
        [((rows,) + parts[0].shape[1:], parts[0].dtype)],
        name="join",
        vmem=4,
    )[0]


def pair_sum_kernel(keep, other, stay, go):
    for half in range(2):
        stay[half] = added(keep[2 * half], other[2 * half])
        go[half] = added(keep[2 * half + 1], other[2 * half + 1])


def pair_sum(keep, other, after=()):
    half = ((2,) + keep.shape[1:], BF16)
    return call(pair_sum_kernel, [(0, keep), (0, other)], [half, half], name="pair_sum", vmem=4, after=after)


def first_sum_kernel(stay, other, keep, send):
    keep[...] = added(stay[0], other[0])
    send[...] = added(stay[1], other[1])


def first_sum(stay, other, after=()):
    one = (stay.shape[1:], BF16)
    return call(first_sum_kernel, [(0, stay), (0, other)], [one, one], name="first_sum", vmem=4, after=after)


def second_sum_kernel(place, dk, do, uk, uo, *outs):
    for k, out in enumerate(outs):
        cols = aligned(D * (place[3] ^ k), D, 128)
        out[0] = added(dk[:, cols], do[:, cols])
        out[1] = added(uk[:, cols], uo[:, cols])


def second_sum(place, parts, after):
    return call(
        second_sum_kernel,
        [(1, place)] + [(0, p) for p in parts],
        [((2, CHUNK, D), BF16)] * 4,
        name="second_sum",
        vmem=4,
        after=after,
    )


def core_sum_kernel(keep, other, *outs):
    for r, out in enumerate(outs):
        out[...] = added(keep[r], other[r])


def core_sum(keep, other, after=()):
    one = (keep.shape[1:], BF16)
    return call(core_sum_kernel, [(0, keep), (0, other)], [one] * 4, name="core_sum", vmem=4, after=after)


def total_of(refs, *at):
    a, b, c, d = (ref[at].astype(F32) for ref in refs)
    return ((a + b) + (c + d)).astype(BF16)


def plane_sum_kernel(place, *refs):
    ins, outs = refs[:4], refs[4:]
    rows = slice(0, CHUNK)
    extra = total_of(ins, rows, slice(4 * D, 4 * D + 128))
    for k, out in enumerate(outs):
        out[:, 0:D] = total_of(ins, rows, aligned(D * (place[3] ^ k), D, 128))
        out[:, D : D + 128] = extra


def plane_sum(place, parts, after=()):
    return call(
        plane_sum_kernel,
        [(1, place)] + [(0, p) for p in parts],
        [((CHUNK, D + 128), BF16)] * 4,
        name="plane_sum",
        vmem=4,
        after=after,
    )


def line_sum_kernel(a, b, c, d, *outs):
    refs = (a, b, c, d)
    if len(outs) == 1:
        outs[0][...] = total_of(refs, slice(0, 2))
    else:
        rows = slice(0, CHUNK)
        outs[0][...] = total_of(refs, rows, slice(0, D))
        outs[1][...] = total_of(refs, rows, slice(D, D + 128))


def line_sum(parts, after=()):
    outs = [((2, CHUNK, D), BF16)]
    if len(parts[0].shape) == 2:
        outs = [((CHUNK, D), BF16), ((CHUNK, 128), BF16)]
    return call(line_sum_kernel, [(0, p) for p in parts], outs, name="line_sum", vmem=4, after=after)


def rest_sum(value, n):
    bit = 16
    while bit < n:
        other = swap(value, "dp", n, bit)
        value = (value.astype(F32) + other.astype(F32)).astype(BF16)
        bit *= 2
    return value


def trades(values, n, shift):
    return [values[0]] + [swap(values[k], "dp", n, k << shift) for k in (1, 2, 3)]


def join_kernel(*refs):
    ins, out = refs[:-1], refs[-1]
    for i, ref in enumerate(ins):
        out[i] = ref[...]


def join(parts, after=()):
    return call(
        join_kernel,
        [(0, p) for p in parts],
        [((len(parts),) + parts[0].shape, parts[0].dtype)],
        name="join",
        vmem=4,
        after=after,
    )[0]


def pack_kernel(place, targets, unit, other, units, packed):
    both = unit[...] + other[...]
    units[...] = both
    row = iota((2 * PAIRS, 128), 0)
    marks = jnp.zeros((2 * PAIRS, 128), jnp.int32)
    for j in range(PAIRS):
        marks = jnp.where(row == j, targets[j], marks)
    marks = jnp.where(iota((2 * PAIRS, 128), 1) < 64, marks >> 5, marks & 31)
    packed[:, 0:D] = both.astype(BF16)
    packed[:, D : D + 128] = marks.astype(F32).astype(BF16)


def pack(place, targets, unit, other):
    return call(
        pack_kernel,
        [(1, place), (1, targets), (0, unit), (0, other)],
        [(unit.shape, F32), ((2 * PAIRS, D + 128), BF16)],
        name="pack",
        vmem=4,
    )


def squares_of(parts):
    acc = jnp.zeros((8, D), F32)
    for part in parts:
        flat = part.reshape(-1, CHUNK, D)
        for k in range(flat.shape[0]):
            v = flat[k].astype(F32)
            acc = acc + jnp.sum((v * v).reshape(CHUNK // 8, 8, D), axis=0)
    return acc[:, 0:128] + acc[:, 128:256] + acc[:, 256:384]


def wide_squares_kernel(*refs):
    refs[-1][...] = squares_of(refs[:-1])


def squares_kernel(place, *refs):
    parts, (vgrad, before, out) = refs[:-3], refs[-3:]
    acc = squares_of(parts) + before[...]
    row = iota((16, 128), 0)
    low_row = 6 * place[0]
    mine = (row >= low_row) & (row < low_row + 6)
    for j in range(3):
        v = jnp.where(mine, vgrad[16 * j : 16 * j + 16, :].astype(F32), 0.0)
        v = v * v
        acc = acc + (v[0:8] + v[8:16])
    out[...] = acc


def squares(place, parts, vgrad=None, before=None, after=()):
    ins = [(0, p) for p in parts]
    kernel = wide_squares_kernel
    if before is not None:
        ins = [(1, place)] + ins + [(0, vgrad), (0, before)]
        kernel = squares_kernel
    return call(kernel, ins, [((8, 128), F32)], name="squares", vmem=4, after=after)[0]


def merge_kernel(place, igrad, other, out):
    @pl.when(place[0] == 0)
    def low_core():
        out[0:OFF, :] = igrad[0:OFF, :]
        out[OFF:WIN, :] = added(igrad[OFF:WIN, :], other[0 : WIN - OFF, :])
        out[WIN:SEQ, :] = other[WIN - OFF : WIN, :]

    @pl.when(place[0] != 0)
    def high_core():
        out[0:OFF, :] = other[0:OFF, :]
        out[OFF:WIN, :] = added(other[OFF:WIN, :], igrad[0 : WIN - OFF, :])
        out[WIN:SEQ, :] = igrad[WIN - OFF : WIN, :]


def merge(place, igrad, other, after):
    return call(
        merge_kernel,
        [(1, place), (0, igrad), (0, other)],
        [((SEQ, D), BF16)],
        micros=1,
        name="merge",
        vmem=4,
        after=after,
    )[0]


def adamw(parameter, first_state, second, clipped, rate):
    first_new = BETA_ONE * first_state + (1.0 - BETA_ONE) * clipped
    second_new = BETA_TWO * second + (1.0 - BETA_TWO) * clipped * clipped
    direction = (first_new * (1.0 / (1.0 - BETA_ONE**STEP))) / (
        jnp.sqrt(second_new * (1.0 / (1.0 - BETA_TWO**STEP))) + ADAM_EPS
    )
    return parameter - rate * (direction + DECAY_RATE * parameter), first_new, second_new


def adamw_kernel(place, *refs):
    sums, refs = refs[:2], refs[2:]
    (vgrad, w, m, v, pv, pm, pq), refs = refs[:7], refs[7:]
    wide, low, refs = refs[:2], refs[2:6], refs[6:]
    outs, (npv, npm, npq, norm), scrs, sems = refs[:4], refs[4:8], refs[8:12], refs[12]
    opt = place[0]
    total = sums[0][...] + sums[1][...]
    total = jnp.sum(jnp.sum(total, axis=1, keepdims=True), axis=0, keepdims=True)
    grad_norm = jnp.sqrt(total)
    factor = jnp.minimum(1.0, CLIP_NORM / (grad_norm + 1e-06))
    norm[...] = grad_norm
    for j in range(3):
        cols = slice(128 * j, 128 * j + 128)
        g = vgrad[16 * j : 16 * j + 16, :].astype(F32)
        g = jnp.where(opt == 0, g[0:6], g[6:12])
        a, b, c = adamw(pv[:, cols], pm[:, cols], pq[:, cols], g * factor, VECTOR_RATE)
        npv[:, cols] = a
        npm[:, cols] = b
        npq[:, cols] = c
    copies = []

    def block(grad, rows, cols):
        new = adamw(w[rows, cols], m[rows, cols], v[rows, cols], grad * factor, LEARN_RATE)
        for scr, value in zip(scrs, new + (new[0].astype(BF16),)):
            scr[rows, cols] = value

    def send(step, base, cols):
        rows = aligned(base, CHUNK, 16)
        for i, (scr, out) in enumerate(zip(scrs, outs)):
            copy = pltpu.make_async_copy(scr.at[rows, cols], out.at[rows, cols], sems.at[step, i])
            copy.start()
            copies.append(copy)

    for r in range(4):
        base = CHUNK * place[4 + r]

        def wide_rows(i, carry, r=r, base=base):
            rows = aligned(base + i * 16, 16, 16)
            for k in range(4):
                at = D * (place[3] ^ k)
                for p in range(2):
                    grad = wide[r % 2][r // 2, k, p, aligned(i * 16, 16, 16), :].astype(F32)
                    block(grad, rows, aligned((4 * D + FF if p == 0 else 4 * D) + at, D, 128))
            return carry

        lax.fori_loop(0, CHUNK // 16, wide_rows, 0)
        send(2 * r, base, slice(4 * D, 4 * D + 2 * FF))
        base = CHUNK * (place[1] ^ r)

        def low_rows(i, carry, r=r, base=base):
            rows = aligned(base + i * 16, 16, 16)
            for k in range(4):
                grad = low[r][k, aligned(i * 16, 16, 16), :].astype(F32)
                block(grad, rows, aligned(D * (place[3] ^ k), D, 128))
            return carry

        lax.fori_loop(0, CHUNK // 16, low_rows, 0)
        send(2 * r + 1, base, slice(0, 4 * D))
    for copy in copies:
        copy.wait()


def update(place, sums, vgrad, w, m, v, pv, pm, pq, parts):
    ins = tuple(sums) + (vgrad, w, m, v, pv, pm, pq) + tuple(parts)
    shapes = [(w.shape, F32)] * 3 + [(w.shape, BF16)] + [(pv.shape, F32)] * 3 + [((1, 1), F32)]
    return pl.pallas_call(
        adamw_kernel,
        out_shape=[jax.ShapeDtypeStruct(s, d) for s, d in shapes],
        in_specs=[SMEM] + [VMEM] * len(ins),
        out_specs=[ANY] * 4 + [VMEM] * 4,
        scratch_shapes=[
            pltpu.VMEM(w.shape, F32),
            pltpu.VMEM(w.shape, F32),
            pltpu.VMEM(w.shape, F32),
            pltpu.VMEM(w.shape, BF16),
            pltpu.SemaphoreType.DMA((8, 4)),
        ],
        compiler_params=pltpu.CompilerParams(vmem_limit_bytes=16 << 20),
        cost_estimate=pl.CostEstimate(
            flops=4000000000, bytes_accessed=26 * w.size, transcendentals=0
        ),
        name="adamw",
    )(place, *ins)


def shards(
    n,
    tokens,
    lengths,
    query_index,
    doc_index,
    targets,
    weights,
    first_moment,
    second_moment,
    vectors,
    vec_first,
    vec_second,
):
    opt = lax.axis_index("opt")
    me = lax.axis_index("dp")
    plane = me & 3
    columns = [jnp.where(opt == 0, plane ^ r, plane ^ turned(r)) for r in range(4)]
    place = jnp.stack([opt, plane, me, (me >> 2) & 3] + columns).astype(jnp.int32)
    lengths = lengths.reshape(SEGS)
    chosen = jnp.concatenate([query_index, doc_index])
    groups = bit_groups(n)

    w_own = first_cast(weights, vectors)
    w_other = swap(w_own, "opt", 2, 1)
    wo_own, wu_own, wd_own = cast(weights, w_own)
    wo = (wo_own, swap(wo_own, "opt", 2, 1))
    wu = (wu_own, swap(wu_own, "opt", 2, 1))
    wd = (wd_own, swap(wd_own, "opt", 2, 1))

    proj, att, lse, segc, segr, vec = attend(place, lengths, tokens, w_own, w_other)
    xhat1, inv1, hlow, act, slope, xhat2, inv2, unit, uscale = mlp(
        place, lengths, chosen, att, tokens, segr, vec, wo + wu + wd
    )
    units, packed = pack(place, targets, unit, swap(unit, "opt", 2, 1))
    groups = bit_groups(n)
    order = [0]
    stack = packed
    for i, (shift, size) in enumerate(groups[1:] + groups[:1]):
        pieces = [stack] + [swap(stack, "dp", n, k << shift) for k in range(1, size)]
        order = [o | (k << shift) for k in range(size) for o in order]
        if i < len(groups) - 1:
            stack = join(pieces).reshape(-1, 2 * PAIRS, D + 128)
    dsec, dlow, keep, send, dsums = down_backward(
        n, order, place, lengths, chosen, units, segc, uscale, (xhat2, inv2, act), vec, pieces
    )
    other = swap(send, "opt", 2, 1)
    dup, ukeep, usend, usums = up_backward(place, dlow, slope, hlow, wd, [])
    stay, go = pair_sum(keep, other, [dup])
    other = cross(go, n, True)
    uother = swap(usend, "opt", 2, 1)
    dfirst, datt, delta, okeep, osend, fsums = first_backward(
        place, dup, dsec, xhat1, inv1, att, vec, wu + wo, [stay]
    )
    dkeep, go = first_sum(stay, other, [dfirst])
    dother = cross(go, n, False)
    ustay, go = pair_sum(ukeep, uother, [dfirst])
    uother = cross(go, n, True)
    ins = (tokens, proj, datt, lse, delta, segc, segr)
    part0, keep0, send0, sums0 = heads_backward(0, place, ins, (), [dkeep, ustay])
    ukeep, go = first_sum(ustay, uother, [part0])
    uother = cross(go, n, False)
    part1, keep1, send1, sums1 = heads_backward(1, place, ins, (), [ukeep, part0])
    wide = second_sum(place, (dkeep, dother, ukeep, uother), [part1])
    got = trades(wide, n, 2)
    part2, keep, send, _ = heads_backward(
        2, place, ins,
        (okeep, osend, keep0, send0, keep1, send1, dsums, usums, fsums, sums0, sums1),
        [wide[0], part1],
    )
    wide = rest_sum(line_sum(got, [part2])[0], n)
    send, wide = lax.optimization_barrier((send, wide))
    other = swap(send, "opt", 2, 1)
    got = trades([wide] * 4, n, 2)
    low = core_sum(keep, other)
    low_got = trades(low, n, 0)
    igrad = input_backward(place, (part0, part1, part2), dfirst, w_own, w_other, [low[0]])
    iother = swap(igrad, "opt", 2, 1)
    low = plane_sum(place, low_got, [igrad])
    low_got = trades(low, n, 2)
    wide = join(got, [low[0]])
    other = cross(wide, n, False)
    low, vgrad = line_sum(low_got)
    low, vgrad = rest_sum(low, n), rest_sum(vgrad, n)
    low_got = trades([low] * 4, n, 2)
    wide = join([wide, other], [low])
    wide = (wide, cross(wide, n, True))
    input_grad = merge(place, igrad, iother, [wide[0]])
    low = join(low_got)
    low = trades([low] * 4, n, 0)
    sums = squares(place, low, vgrad, squares(place, wide, after=[low[0]]))
    sums = (sums, swap(sums, "opt", 2, 1))
    pieces = wide + tuple(low)
    nw, nm, nv, nlow, npv, npm, npq, norm = update(
        place, sums, vgrad, weights, first_moment, second_moment,
        vectors, vec_first, vec_second, pieces,
    )
    return (norm.reshape(()), input_grad, nw, nm, nv, nlow, npv, npm, npq)


def solution(mesh):
    rows = P("opt", None)
    in_specs = (P("dp", None), P("dp", None), P("dp"), P("dp"), P("dp")) + (rows,) * 6
    out_specs = (P(), P("dp", None)) + (rows,) * 7
    n = mesh.shape["dp"]
    return jax.shard_map(
        functools.partial(shards, n),
        mesh=mesh,
        in_specs=in_specs,
        out_specs=out_specs,
        check_vma=False,
    )
```

```python
import functools

import jax
import jax.numpy as jnp
from jax import lax
from jax.experimental import pallas as pl
from jax.experimental.pallas import tpu as pltpu
from jax.sharding import PartitionSpec as P

D = 384
HEADS = 12
HD = 32
FF = 1536
SEQ = 1024
SEGS = 16
PAIRS = 8
STEP = 10

WIN = 576
OFF = SEQ - WIN
PAD = 640
BLOCK = 128
BANDS = tuple((q, max(0, q - 128), min(WIN, q + 256)) for q in range(0, WIN, BLOCK))
BAND_ROWS = tuple(sum(b[2] - b[1] for b in BANDS[:i]) for i in range(len(BANDS) + 1))
ROWS = 64

LN_EPS = 1e-06
POOL_EPS = 1e-06
SCORE_SCALE = 50.0
CLIP_NORM = 0.001
BETA_ONE = 0.9
BETA_TWO = 0.98
ADAM_EPS = 1e-08
LEARN_RATE = 0.05
VECTOR_RATE = 0.3
DECAY_RATE = 0.01
NEG_BIG = -1e30
HALF = D // 2
CHUNK = HALF // 4
EXP2_SCALE = HD ** (-0.5) * 1.4426950408889634

F32 = jnp.float32
BF16 = jnp.bfloat16
VMEM = pl.BlockSpec(memory_space=pltpu.VMEM)
SMEM = pl.BlockSpec(memory_space=pltpu.SMEM)
ANY = pl.BlockSpec(memory_space=pl.ANY)


def nn(a, b):
    return jnp.dot(a, b, preferred_element_type=F32)


def nt(a, b):
    return lax.dot_general(a, b, (((1,), (1,)), ((), ())), preferred_element_type=F32)


def tn(a, b):
    return lax.dot_general(a, b, (((0,), (0,)), ((), ())), preferred_element_type=F32)


def exact(a, b, dims):
    return lax.dot_general(
        a, b, (dims, ((), ())), precision=lax.Precision.HIGHEST, preferred_element_type=F32
    )


def iota(shape, axis):
    return lax.broadcasted_iota(jnp.int32, shape, axis)


def low_pair(value):
    high = value.astype(BF16)
    return high, (value - high.astype(F32)).astype(BF16)


def aligned(start, size, unit):
    return pl.ds(pl.multiple_of(start, unit), size)


def assemble(dst, own, other, opt):
    dst[aligned(HALF * opt, HALF, 64), :] = own[0:HALF, :]
    dst[aligned(HALF * (1 - opt), HALF, 64), :] = other[0:HALF, :]


def call(kernel, ins, outs, scratch=(), micros=0, name=None, vmem=12, after=()):
    specs = [SMEM if s else VMEM for s, _ in ins] + [ANY] * len(after)
    count = len(ins)

    def body(*refs):
        kernel(*refs[:count], *refs[count + len(after) :])

    shapes = [jax.ShapeDtypeStruct(s, d) for s, d in outs]
    moved = sum(a.size * a.dtype.itemsize for _, a in ins)
    moved += sum(s.size * s.dtype.itemsize for s in shapes)
    return pl.pallas_call(
        body,
        out_shape=shapes,
        in_specs=specs,
        out_specs=[VMEM] * len(shapes),
        scratch_shapes=list(scratch),
        compiler_params=pltpu.CompilerParams(vmem_limit_bytes=vmem << 20),
        cost_estimate=pl.CostEstimate(
            flops=micros * 1100000000, bytes_accessed=moved, transcendentals=0
        ),
        name=name,
    )(*[a for _, a in ins], *after)


def head_stack(rows):
    lane_head = iota(rows.shape, 1) // HD
    zero = jnp.zeros_like(rows)
    return jnp.concatenate([jnp.where(lane_head == j, rows, zero) for j in range(4)], axis=0)


def attend_kernel(
    place, lengths, tokens, w_own, w_other, proj, att, lse, segc, segr, vec, wfull, bias, vt
):
    opt = place[0]
    assemble(wfull, w_own, w_other, opt)
    mine = w_own[HALF : HALF + 16, 0:D].astype(F32)
    others = w_other[HALF : HALF + 16, 0:D].astype(F32)
    first = opt == 0
    vec[0:6, :] = jnp.where(first, mine, others)[0:6]
    vec[6:12, :] = jnp.where(first, others, mine)[0:6]
    vec[12:16, :] = jnp.zeros((4, D), F32)

    pos_col = iota((WIN, 128), 0) + OFF * opt
    pos_row = iota((8, PAD), 1) + OFF * opt
    seg_col = jnp.zeros((WIN, 128), jnp.int32)
    seg_row = jnp.zeros((8, PAD), jnp.int32)
    bound = jnp.int32(0)
    for s in range(SEGS):
        bound = bound + lengths[s]
        seg_col = seg_col + (pos_col >= bound).astype(jnp.int32)
        seg_row = seg_row + (pos_row >= bound).astype(jnp.int32)
    segc[...] = seg_col
    segr[...] = seg_row
    for i, (q0, k0, k1) in enumerate(BANDS):
        bias[BAND_ROWS[i] : BAND_ROWS[i + 1], :] = jnp.where(
            segc[k0:k1, :] == segr[0:1, q0 : q0 + BLOCK], 0.0, NEG_BIG
        )

    x = tokens[aligned(OFF * opt, WIN, 64), :]
    for c in range(3):
        acc = nn(x, wfull[:, c * D : (c + 1) * D])
        if c != 1:
            acc = acc + vec[(0 if c == 0 else 1) : (1 if c == 0 else 2), :]
        proj[0:WIN, c * D : (c + 1) * D] = acc.astype(BF16)
    proj[WIN:PAD, :] = jnp.zeros((PAD - WIN, 3 * D), BF16)

    def group(g, carry):
        def lanes(part):
            return aligned(part * D + 128 * g, 128, 128)

        for t in range(PAD // 128):
            vt[:, 128 * t : 128 * t + 128] = (
                proj[128 * t : 128 * t + 128, lanes(2)].astype(F32).T.astype(BF16)
            )
        for i, (q0, k0, k1) in enumerate(BANDS):
            stack = head_stack(proj[q0 : q0 + BLOCK, lanes(0)])
            st = nt(proj[k0:k1, lanes(1)], stack)
            outs = []
            for j in range(4):
                t = (
                    st[:, j * BLOCK : (j + 1) * BLOCK] * EXP2_SCALE
                    + bias[BAND_ROWS[i] : BAND_ROWS[i + 1], :]
                )
                peak = jnp.max(t, axis=0, keepdims=True)
                powers = jnp.exp2(t - peak)
                total = jnp.sum(powers, axis=0, keepdims=True)
                lse[g, j : j + 1, q0 : q0 + BLOCK] = peak + jnp.log2(total)
                o = nn(vt[j * HD : (j + 1) * HD, k0:k1], powers.astype(BF16))
                outs.append(o * (1.0 / total))
            rows = min(BLOCK, WIN - q0)
            att[q0 : q0 + rows, aligned(128 * g, 128, 128)] = (
                jnp.concatenate(outs, axis=0).T[0:rows].astype(BF16)
            )
        return carry

    lax.fori_loop(0, 3, group, 0)


def attend(place, lengths, tokens, w_own, w_other):
    return call(
        attend_kernel,
        [(1, place), (1, lengths), (0, tokens), (0, w_own), (0, w_other)],
        [
            ((PAD, 3 * D), BF16),
            ((WIN, D), BF16),
            ((3, 4, PAD), F32),
            ((WIN, 128), jnp.int32),
            ((8, PAD), jnp.int32),
            ((16, D), F32),
        ],
        [
            pltpu.VMEM((D, 3 * D), BF16),
            pltpu.VMEM((BAND_ROWS[-1], 128), F32),
            pltpu.VMEM((128, PAD), BF16),
        ],
        micros=8,
        name="attend",
    )


def owned(place, lengths, segment):
    bound = jnp.int32(0)
    count = jnp.int32(0)
    for s in range(SEGS):
        bound = bound + lengths[s]
        count = count + (bound <= WIN).astype(jnp.int32)
    low_side = (segment < count).astype(jnp.int32)
    return low_side == (place[0] == 0).astype(jnp.int32)


def mlp_kernel(
    place, lengths, chosen, att, tokens, segr, vec, wo_own, wo_other, wu_own, wu_other,
    wd_own, wd_other, xhat1, inv1, hlow, act, slope, xhat2, inv2, unit, uscale,
    wo, wu, wd, tmp, hid, ench, encl,
):
    opt = place[0]
    assemble(wo, wo_own, wo_other, opt)
    assemble(wu, wu_own, wu_other, opt)
    assemble(wd, wd_own, wd_other, opt)
    tmp[...] = nn(att[...], wo[...])

    def first_norm(i, carry):
        r = aligned(i * ROWS, ROWS, ROWS)
        x = tokens[aligned(OFF * opt + i * ROWS, ROWS, ROWS), :].astype(F32)
        v = tmp[r, :] + vec[2:3, :] + x
        centred = v - jnp.mean(v, axis=1, keepdims=True)
        inverse = lax.rsqrt(jnp.mean(centred * centred, axis=1, keepdims=True) + LN_EPS)
        normed = centred * inverse
        xhat1[r, :] = normed
        inv1[r, :] = jnp.broadcast_to(inverse, (ROWS, 128))
        h = normed * vec[8:9, :] + vec[9:10, :]
        hid[r, :] = h
        hlow[r, :] = h.astype(BF16)
        return carry

    lax.fori_loop(0, WIN // ROWS, first_norm, 0)

    for c in range(4):
        cols = slice(c * D, (c + 1) * D)
        tmp[...] = nn(hlow[...], wu[:, cols])

        def gelu(i, carry, cols=cols, c=c):
            r = aligned(i * ROWS, ROWS, ROWS)
            u = tmp[r, :] + vec[3 + c : 4 + c, :]
            half = lax.erf(u * 0.7071067811865476) * 0.5 + 0.5
            act[r, cols] = (u * half).astype(BF16)
            slope[r, cols] = half + u * jnp.exp(-0.5 * u * u) * 0.3989422804014327
            return carry

        lax.fori_loop(0, WIN // ROWS, gelu, 0)

    tmp[...] = nt(act[...], wd[...])

    def second_norm(i, carry):
        r = aligned(i * ROWS, ROWS, ROWS)
        v = tmp[r, :] + vec[7:8, :] + hid[r, :]
        centred = v - jnp.mean(v, axis=1, keepdims=True)
        inverse = lax.rsqrt(jnp.mean(centred * centred, axis=1, keepdims=True) + LN_EPS)
        normed = centred * inverse
        xhat2[r, :] = normed
        inv2[r, :] = jnp.broadcast_to(inverse, (ROWS, 128))
        high, rest = low_pair(normed * vec[10:11, :] + vec[11:12, :])
        ench[r, :] = high
        encl[r, :] = rest
        return carry

    lax.fori_loop(0, WIN // ROWS, second_norm, 0)

    seg = segr[0:1, 0:WIN]
    row_id = iota((2 * PAIRS, WIN), 0)
    wanted = jnp.zeros((2 * PAIRS, WIN), jnp.int32)
    for j in range(2 * PAIRS):
        wanted = jnp.where(row_id == j, chosen[j], wanted)
    mask = owned(place, lengths, jnp.broadcast_to(seg, (2 * PAIRS, WIN)))
    onehot = jnp.where((wanted == seg) & mask, 1.0, 0.0)
    count = jnp.maximum(jnp.sum(onehot, axis=1, keepdims=True), 1.0)
    hot = onehot.astype(BF16)
    pooled = (nn(hot, ench[...]) + nn(hot, encl[...])) / count
    inverse_len = lax.rsqrt(jnp.sum(pooled * pooled, axis=1, keepdims=True) + POOL_EPS)
    unit[...] = pooled * inverse_len
    uscale[...] = jnp.broadcast_to(inverse_len / count, (2 * PAIRS, 128))


def mlp(place, lengths, chosen, att, tokens, segr, vec, halves):
    return call(
        mlp_kernel,
        [(1, place), (1, lengths), (1, chosen), (0, att), (0, tokens), (0, segr), (0, vec)]
        + [(0, h) for h in halves],
        [
            ((WIN, D), F32),
            ((WIN, 128), F32),
            ((WIN, D), BF16),
            ((WIN, FF), BF16),
            ((WIN, FF), F32),
            ((WIN, D), F32),
            ((WIN, 128), F32),
            ((2 * PAIRS, D), F32),
            ((2 * PAIRS, 128), F32),
        ],
        [
            pltpu.VMEM((D, D), BF16),
            pltpu.VMEM((D, FF), BF16),
            pltpu.VMEM((D, FF), BF16),
            pltpu.VMEM((WIN, D), F32),
            pltpu.VMEM((WIN, D), F32),
            pltpu.VMEM((WIN, D), BF16),
            pltpu.VMEM((WIN, D), BF16),
        ],
        micros=10,
        name="mlp",
    )


def turned(chunk):
    return (chunk & 1) * 2 + (chunk >> 1)


def split_rows(grad, keep, send, place, *at):
    opt = place[0]
    for c in range(4):
        straight = c ^ place[1]
        mine = jnp.where(opt == 0, straight, turned(straight))
        theirs = jnp.where(opt == 0, turned(straight), straight)
        keep[(mine,) + at] = grad[aligned(HALF * opt + CHUNK * c, CHUNK, 16), :].astype(BF16)
        send[(theirs,) + at] = grad[aligned(HALF * (1 - opt) + CHUNK * c, CHUNK, 16), :].astype(BF16)


def column_sums(value):
    return jnp.sum(value.reshape(ROWS // 8, 8, D), axis=0)


def norm_backward(grad_at, normed_ref, inverse_ref, gain, out, low_out, sums, at):
    def block(i, carry):
        scale_sum, shift_sum, bias_sum = carry
        r = aligned(i * ROWS, ROWS, ROWS)
        g = grad_at(r)
        normed = normed_ref[r, :]
        scaled = g * gain
        inner = (
            scaled
            - jnp.mean(scaled, axis=1, keepdims=True)
            - normed * jnp.mean(scaled * normed, axis=1, keepdims=True)
        ) * inverse_ref[r, 0:1]
        out[r, :] = inner
        low_out[r, :] = inner.astype(BF16)
        return (
            scale_sum + column_sums(g * normed),
            shift_sum + column_sums(g),
            bias_sum + column_sums(inner),
        )

    zero = jnp.zeros((8, D), F32)
    scale_sum, shift_sum, bias_sum = lax.fori_loop(0, WIN // ROWS, block, (zero, zero, zero))
    sums[at : at + 1, :] = jnp.sum(bias_sum, axis=0, keepdims=True)
    sums[at + 1 : at + 2, :] = jnp.sum(scale_sum, axis=0, keepdims=True)
    sums[at + 2 : at + 3, :] = jnp.sum(shift_sum, axis=0, keepdims=True)


def down_kernel(
    count, order, place, lengths, chosen, units, segc, uscale, xhat2, inv2, act, vec, *rest
):
    pieces, (dsec, dlow, keep, send, sums, queries, docs, marks, grad) = rest[:-9], rest[-9:]
    me = place[2]
    per = pieces[0].shape[0]
    for p, piece in enumerate(pieces):
        for j in range(per):
            at = order[p * per + j]
            r = slice(at * PAIRS, (at + 1) * PAIRS)
            both = piece[j].astype(F32)
            queries[r, :] = both[0:PAIRS, 0:D]
            docs[r, :] = both[PAIRS : 2 * PAIRS, 0:D]
            marks[r, :] = both[0:PAIRS, D : D + 128]
    total = count * PAIRS
    q = queries[...].astype(BF16)
    d = docs[...].astype(BF16)
    logits = SCORE_SCALE * nt(q, d)
    peak = jnp.max(logits, axis=1, keepdims=True)
    powers = jnp.exp(logits - peak)
    soft = powers / jnp.sum(powers, axis=1, keepdims=True)
    col = iota((total, total), 1)
    doc_id = ((col // PAIRS) ^ me) * PAIRS + lax.rem(col, PAIRS)
    hit = (marks[:, 0:1] * 32.0 + marks[:, 64:65]).astype(jnp.int32) == doc_id
    d_logits = (soft - jnp.where(hit, 1.0, 0.0)) * (SCORE_SCALE / total)
    high, rest_low = low_pair(d_logits[0:PAIRS, :])
    d_q = nn(high, d) + nn(rest_low, d)
    high, rest_low = low_pair(d_logits[:, 0:128].T[0:PAIRS, :])
    d_d = nn(high, q) + nn(rest_low, q)
    d_units = jnp.concatenate([d_q, d_d], axis=0)
    u = units[...]
    d_pool = uscale[:, 0:1] * (d_units - u * jnp.sum(u * d_units, axis=1, keepdims=True))
    lane = iota((8, 2 * PAIRS), 1)
    wanted = jnp.zeros((8, 2 * PAIRS), jnp.int32)
    for j in range(2 * PAIRS):
        wanted = jnp.where(lane == j, chosen[j], wanted)
    seg = segc[:, 0 : 2 * PAIRS]
    mask = owned(place, lengths, seg)
    hot = jnp.where((seg == wanted[0:1, :]) & mask, 1.0, 0.0).astype(BF16)
    high, rest_low = low_pair(d_pool)
    dsec[...] = nn(hot, high) + nn(hot, rest_low)
    norm_backward(lambda r: dsec[r, :], xhat2, inv2, vec[10:11, :], dsec, dlow, sums, 0)
    sums[3:8, :] = jnp.zeros((5, D), F32)
    for c in range(4):
        cols = slice(c * D, (c + 1) * D)
        grad[...] = tn(dlow[...], act[:, cols])
        split_rows(grad, keep, send, place, c)


def down_backward(count, order, place, lengths, chosen, units, segc, uscale, saved, vec, pieces):
    total = count * PAIRS
    return call(
        functools.partial(down_kernel, count, order),
        [(1, place), (1, lengths), (1, chosen), (0, units), (0, segc), (0, uscale)]
        + [(0, s) for s in saved]
        + [(0, vec)]
        + [(0, p) for p in pieces],
        [
            ((WIN, D), F32),
            ((WIN, D), BF16),
            ((4, 4, CHUNK, D), BF16),
            ((4, 4, CHUNK, D), BF16),
            ((8, D), F32),
        ],
        [
            pltpu.VMEM((total, D), F32),
            pltpu.VMEM((total, D), F32),
            pltpu.VMEM((total, 128), F32),
            pltpu.VMEM((D, D), F32),
        ],
        micros=4,
        name="down_backward",
    )


def up_kernel(place, dlow, slope, hlow, wd_own, wd_other, dup, keep, send, sums, wd, grad):
    opt = place[0]
    assemble(wd, wd_own, wd_other, opt)
    for c in range(4):
        cols = slice(c * D, (c + 1) * D)
        part = (nn(dlow[...], wd[:, cols]) * slope[:, cols]).astype(BF16)
        dup[:, cols] = part
        sums[c : c + 1, :] = jnp.sum(part.astype(F32), axis=0, keepdims=True)
        grad[...] = tn(hlow[...], dup[:, cols])
        split_rows(grad, keep, send, place, c)


def up_backward(place, dlow, slope, hlow, halves, after):
    return call(
        up_kernel,
        [(1, place)] + [(0, a) for a in (dlow, slope, hlow) + tuple(halves)],
        [((WIN, FF), BF16), ((4, 4, CHUNK, D), BF16), ((4, 4, CHUNK, D), BF16), ((4, D), F32)],
        [pltpu.VMEM((D, FF), BF16), pltpu.VMEM((D, D), F32)],
        micros=3,
        name="up_backward",
        after=after,
    )


def first_kernel(
    place, dup, dsec, xhat1, inv1, att, vec, wu_own, wu_other, wo_own, wo_other,
    dfirst, datt, delta, okeep, osend, sums, wu, wo, grad, dlow,
):
    opt = place[0]
    assemble(wu, wu_own, wu_other, opt)
    assemble(wo, wo_own, wo_other, opt)
    dfirst[...] = nt(dup[...], wu[...])
    norm_backward(
        lambda r: dfirst[r, :] + dsec[r, :], xhat1, inv1, vec[8:9, :], dfirst, dlow, sums, 0
    )
    sums[3:8, :] = jnp.zeros((5, D), F32)
    grad[...] = tn(att[...], dlow[...])
    split_rows(grad, okeep, osend, place)
    da = nt(dlow[...], wo[...]).astype(BF16)
    datt[0:WIN, :] = da
    datt[WIN:PAD, :] = jnp.zeros((PAD - WIN, D), BF16)
    high, rest = low_pair(da.astype(F32) * att[...].astype(F32))
    heads = (iota((16, D), 1) // HD == iota((16, D), 0)).astype(F32).astype(BF16)
    delta[:, 0:WIN] = nt(heads, high) + nt(heads, rest)
    delta[:, WIN:PAD] = jnp.zeros((16, PAD - WIN), F32)


def first_backward(place, dup, dsec, xhat1, inv1, att, vec, halves, after):
    return call(
        first_kernel,
        [(1, place)] + [(0, a) for a in (dup, dsec, xhat1, inv1, att, vec) + tuple(halves)],
        [
            ((WIN, D), F32),
            ((PAD, D), BF16),
            ((16, PAD), F32),
            ((4, CHUNK, D), BF16),
            ((4, CHUNK, D), BF16),
            ((8, D), F32),
        ],
        [
            pltpu.VMEM((D, FF), BF16),
            pltpu.VMEM((D, D), BF16),
            pltpu.VMEM((D, D), F32),
            pltpu.VMEM((WIN, D), BF16),
        ],
        micros=3,
        name="first_backward",
        after=after,
    )


def heads_kernel(g, place, tokens, proj, datt, lse, delta, segc, segr, *rest):
    rest, (dproj, keep, send, sums, kt, dk, dv, grad, ktmp, stmp) = rest[:-10], rest[-10:]

    def lanes(part):
        return slice(part * D + 128 * g, part * D + 128 * g + 128)

    for t in range(PAD // 128):
        kt[:, 128 * t : 128 * t + 128] = (
            proj[128 * t : 128 * t + 128, lanes(1)].astype(F32).T.astype(BF16)
        )
    dk[...] = jnp.zeros_like(dk)
    dv[...] = jnp.zeros_like(dv)
    for q0, k0, k1 in BANDS:
        qs = head_stack(proj[q0 : q0 + BLOCK, lanes(0)])
        gs = head_stack(datt[q0 : q0 + BLOCK, lanes(0)])
        st = nt(proj[k0:k1, lanes(1)], qs)
        dp = nt(proj[k0:k1, lanes(2)], gs)
        same = segc[k0:k1, :] == segr[0:1, q0 : q0 + BLOCK]
        bias = jnp.where(same, 0.0, NEG_BIG)
        probs, d_scores, dq = [], [], []
        for j in range(4):
            cols = slice(j * BLOCK, (j + 1) * BLOCK)
            prob = jnp.exp2(st[:, cols] * EXP2_SCALE + bias - lse[g, j : j + 1, q0 : q0 + BLOCK])
            ds = prob * (dp[:, cols] - delta[4 * g + j : 4 * g + j + 1, q0 : q0 + BLOCK])
            ds = ds.astype(BF16)
            probs.append(prob.astype(BF16))
            d_scores.append(ds)
            dq.append(nn(kt[j * HD : (j + 1) * HD, k0:k1], ds))
        dv[k0:k1, :] += nn(jnp.concatenate(probs, axis=1), gs)
        dk[k0:k1, :] += nn(jnp.concatenate(d_scores, axis=1), qs)
        rows = min(BLOCK, WIN - q0)
        dqs = jnp.concatenate(dq, axis=0).T[0:rows] * HD ** (-0.5)
        dproj[q0 : q0 + rows, 0:128] = dqs.astype(BF16)
    dproj[:, 128:256] = (dk[...] * HD ** (-0.5)).astype(BF16)
    dproj[:, 256:384] = dv[...].astype(BF16)
    grad[...] = tn(tokens[aligned(OFF * place[0], WIN, 64), :], dproj[...])
    q_sum = jnp.sum(dproj[:, 0:128].astype(F32), axis=0, keepdims=True)
    v_sum = jnp.sum(dproj[:, 256:384].astype(F32), axis=0, keepdims=True)
    sums[0:1, :] = q_sum
    sums[1:2, :] = v_sum
    sums[2:8, :] = jnp.zeros((6, 128), F32)
    if g < 2:
        split_rows(grad, keep, send, place)
        return
    parts, (dsums, usums, fsums, zero, one) = rest[:4], rest[4:]
    split_rows(grad, ktmp, stmp, place)
    for dst, blocks in (
        (keep, (parts[0], parts[2], ktmp)),
        (send, (parts[1], parts[3], stmp)),
    ):
        for h, part in enumerate(blocks):
            for c in range(3):
                dst[:, :, D * c + 128 * h : D * c + 128 * h + 128] = part[
                    :, :, 128 * c : 128 * c + 128
                ]
    rows = jnp.concatenate(
        [
            jnp.concatenate([zero[0:1], one[0:1], q_sum], axis=1),
            jnp.concatenate([zero[1:2], one[1:2], v_sum], axis=1),
            fsums[0:1, :],
            usums[0:4, :],
            dsums[0:1, :],
            fsums[1:3, :],
            dsums[1:3, :],
            jnp.zeros((4, D), F32),
        ],
        axis=0,
    ).astype(BF16)
    for c in range(4):
        for j in range(3):
            block = rows[:, 128 * j : 128 * j + 128]
            keep[c, 16 * j : 16 * j + 16, 3 * D : 3 * D + 128] = block
            send[c, 16 * j : 16 * j + 16, 3 * D : 3 * D + 128] = block


def heads_backward(g, place, ins, more, after):
    part = ((4, CHUNK, 3 * D + 128 if g == 2 else D), BF16)
    return call(
        functools.partial(heads_kernel, g),
        [(1, place)] + [(0, a) for a in tuple(ins) + tuple(more)],
        [((WIN, D), BF16), part, part, ((8, 128), F32)],
        [
            pltpu.VMEM((128, PAD), BF16),
            pltpu.VMEM((WIN, 128), F32),
            pltpu.VMEM((WIN, 128), F32),
            pltpu.VMEM((D, D), F32),
            pltpu.VMEM((4, CHUNK, D), BF16),
            pltpu.VMEM((4, CHUNK, D), BF16),
        ],
        micros=3,
        name="heads_backward",
        after=after,
    )


def input_kernel(place, dp0, dp1, dp2, dfirst, w_own, w_other, igrad, wfull, dproj):
    assemble(wfull, w_own, w_other, place[0])
    for g, part in enumerate((dp0, dp1, dp2)):
        for c in range(3):
            dproj[:, c * D + 128 * g : c * D + 128 * g + 128] = part[:, 128 * c : 128 * c + 128]
    igrad[...] = (nt(dproj[...], wfull[...]) + dfirst[...]).astype(BF16)


def input_backward(place, parts, dfirst, w_own, w_other, after):
    return call(
        input_kernel,
        [(1, place)] + [(0, a) for a in tuple(parts) + (dfirst, w_own, w_other)],
        [((WIN, D), BF16)],
        [pltpu.VMEM((D, 3 * D), BF16), pltpu.VMEM((WIN, 3 * D), BF16)],
        micros=2,
        name="input_backward",
        after=after,
    )[0]


def flips(axis, size, bits):
    return [(i, i ^ bits) for i in range(size)]


def pair(value):
    return swap(value, "opt", 2, 1)


def swap(value, axis, size, bits):
    return lax.ppermute(value, axis, flips(axis, size, bits))


def bit_groups(size):
    bits = size.bit_length() - 1
    return [(s, 1 << min(2, bits - s)) for s in range(0, bits, 2)]


def cross(value, n, first):
    pairs = []
    for i in range(n):
        for core in range(2):
            bit = 1 if (core == 0) == first else 2
            pairs.append((2 * i + core, 2 * (i ^ bit) + core))
    return lax.ppermute(value, ("dp", "opt"), pairs)


def added(a, b):
    return (a.astype(F32) + b.astype(F32)).astype(BF16)


def pack_kernel(place, targets, unit, other, units, packed):
    both = unit[...] + other[...]
    units[...] = both
    row = iota((2 * PAIRS, 128), 0)
    marks = jnp.zeros((2 * PAIRS, 128), jnp.int32)
    for j in range(PAIRS):
        marks = jnp.where(row == j, targets[j], marks)
    marks = jnp.where(iota((2 * PAIRS, 128), 1) < 64, marks >> 5, marks & 31)
    packed[0, :, 0:D] = both.astype(BF16)
    packed[0, :, D : D + 128] = marks.astype(F32).astype(BF16)


def pack(place, targets, unit, other):
    return call(
        pack_kernel,
        [(1, place), (1, targets), (0, unit), (0, other)],
        [(unit.shape, F32), ((1, 2 * PAIRS, D + 128), BF16)],
        name="pack",
        vmem=4,
    )


def join_kernel(*refs):
    ins, out = refs[:-1], refs[-1]
    at = 0
    for ref in ins:
        out[at : at + ref.shape[0]] = ref[...]
        at += ref.shape[0]


def join(parts):
    rows = sum(p.shape[0] for p in parts)
    return call(
        join_kernel,
        [(0, p) for p in parts],
        [((rows,) + parts[0].shape[1:], parts[0].dtype)],
        name="join",
        vmem=4,
    )[0]


def down_pair_kernel(keep, other, stay, go):
    for half in range(2):
        stay[half] = added(keep[2 * half], other[2 * half])
        go[half] = added(keep[2 * half + 1], other[2 * half + 1])


def down_pair(keep, other, after=()):
    half = ((2,) + keep.shape[1:], BF16)
    return call(
        down_pair_kernel, [(0, keep), (0, other)], [half, half], name="pair_sum", vmem=4, after=after
    )


def up_pair_kernel(keep, other, okeep, oother, stay, go):
    for half in range(2):
        stay[half, 0:4] = added(keep[2 * half], other[2 * half])
        stay[half, 4] = added(okeep[2 * half], oother[2 * half])
        go[half, 0:4] = added(keep[2 * half + 1], other[2 * half + 1])
        go[half, 4] = added(okeep[2 * half + 1], oother[2 * half + 1])


def up_pair(parts, after):
    half = ((2, 5, CHUNK, D), BF16)
    return call(
        up_pair_kernel, [(0, p) for p in parts], [half, half], name="up_pair", vmem=4, after=after
    )


def wide_first_kernel(dstay, dother, ustay, uother, keep, send):
    for i, out in enumerate((keep, send)):
        out[0:4] = added(dstay[i], dother[i])
        out[4:9] = added(ustay[i], uother[i])


def wide_first(parts, after):
    one = ((9, CHUNK, D), BF16)
    return call(
        wide_first_kernel, [(0, p) for p in parts], [one, one], name="wide_first", vmem=4, after=after
    )


def wide_second_kernel(place, keep, other, mine, send):
    z = place[3]
    for p in range(2):
        for i, bits in enumerate((0, 2)):
            mine[2 * p + i] = added(keep[4 * p + (z ^ bits)], other[4 * p + (z ^ bits)])
            send[2 * p + i] = added(keep[4 * p + (z ^ bits ^ 1)], other[4 * p + (z ^ bits ^ 1)])
    whole = added(keep[8], other[8])
    mine[4] = whole
    send[4] = whole


def wide_second(place, keep, other, after):
    one = ((5, CHUNK, D), BF16)
    return call(
        wide_second_kernel,
        [(1, place), (0, keep), (0, other)],
        [one, one],
        name="wide_second",
        vmem=4,
        after=after,
    )


def wide_third_kernel(keep, other, mine, send):
    for p in range(2):
        mine[p] = added(keep[2 * p], other[2 * p])
        send[p] = added(keep[2 * p + 1], other[2 * p + 1])
    whole = added(keep[4], other[4])
    mine[2] = whole
    send[2] = whole


def wide_third(keep, other, after):
    one = ((3, CHUNK, D), BF16)
    return call(
        wide_third_kernel, [(0, keep), (0, other)], [one, one], name="wide_third", vmem=4, after=after
    )


def wide_last_kernel(keep, other, pair, single):
    pair[...] = added(keep[0:2], other[0:2])
    single[0] = added(keep[2], other[2])


def wide_last(keep, other, after):
    return call(
        wide_last_kernel,
        [(0, keep), (0, other)],
        [((2, CHUNK, D), BF16), ((1, CHUNK, D), BF16)],
        name="wide_last",
        vmem=4,
        after=after,
    )


def low_first_kernel(stay, other, keep, send):
    keep[...] = added(stay[0], other[0])
    send[...] = added(stay[1], other[1])


def low_first(stay, other, after=()):
    one = (stay.shape[1:], BF16)
    return call(
        low_first_kernel, [(0, stay), (0, other)], [one, one], name="low_first", vmem=4, after=after
    )


def low_next_kernel(keep, other, out):
    out[...] = added(keep[...], other[...])


def low_next(keep, other, after=()):
    return call(
        low_next_kernel,
        [(0, keep), (0, other)],
        [(keep.shape, BF16)],
        name="low_next",
        vmem=4,
        after=after,
    )[0]


def low_last_kernel(keep, other, out, vgrad):
    out[...] = added(keep[:, 0 : 3 * D], other[:, 0 : 3 * D])
    vgrad[...] = added(keep[:, 3 * D : 3 * D + 128], other[:, 3 * D : 3 * D + 128])


def low_last(keep, other):
    return call(
        low_last_kernel,
        [(0, keep), (0, other)],
        [((CHUNK, 3 * D), BF16), ((CHUNK, 128), BF16)],
        name="low_last",
        vmem=4,
    )


def chain_kernel(*refs):
    ins, out = refs[:-1], refs[-1]
    at = 0
    for ref in ins:
        flat = ref.reshape(-1, CHUNK, D)
        out[at : at + flat.shape[0]] = flat[...]
        at += flat.shape[0]


def chain(parts, after=()):
    count = sum(p.size for p in parts) // (CHUNK * D)
    return call(
        chain_kernel,
        [(0, p) for p in parts],
        [((count, CHUNK, D), BF16)],
        name="chain",
        vmem=4,
        after=after,
    )[0]


def rest_sum(value, n):
    bit = 16
    while bit < n:
        other = swap(value, "dp", n, bit)
        value = (value.astype(F32) + other.astype(F32)).astype(BF16)
        bit *= 2
    return value


def join_kernel(*refs):
    ins, out = refs[:-1], refs[-1]
    at = 0
    for ref in ins:
        out[at : at + ref.shape[0]] = ref[...]
        at += ref.shape[0]


def join(parts):
    rows = sum(p.shape[0] for p in parts)
    return call(
        join_kernel,
        [(0, p) for p in parts],
        [((rows,) + parts[0].shape[1:], parts[0].dtype)],
        name="join",
        vmem=4,
    )[0]


def down_pair_kernel(keep, other, stay, go):
    for half in range(2):
        stay[half] = added(keep[2 * half], other[2 * half])
        go[half] = added(keep[2 * half + 1], other[2 * half + 1])


def down_pair(keep, other, after=()):
    half = ((2,) + keep.shape[1:], BF16)
    return call(
        down_pair_kernel, [(0, keep), (0, other)], [half, half], name="pair_sum", vmem=4, after=after
    )


def up_pair_kernel(keep, other, okeep, oother, stay, go):
    for half in range(2):
        stay[half, 0:4] = added(keep[2 * half], other[2 * half])
        stay[half, 4] = added(okeep[2 * half], oother[2 * half])
        go[half, 0:4] = added(keep[2 * half + 1], other[2 * half + 1])
        go[half, 4] = added(okeep[2 * half + 1], oother[2 * half + 1])


def up_pair(parts, after):
    half = ((2, 5, CHUNK, D), BF16)
    return call(
        up_pair_kernel, [(0, p) for p in parts], [half, half], name="up_pair", vmem=4, after=after
    )


def wide_first_kernel(dstay, dother, ustay, uother, keep, send):
    for i, out in enumerate((keep, send)):
        out[0:4] = added(dstay[i], dother[i])
        out[4:9] = added(ustay[i], uother[i])


def wide_first(parts, after):
    one = ((9, CHUNK, D), BF16)
    return call(
        wide_first_kernel, [(0, p) for p in parts], [one, one], name="wide_first", vmem=4, after=after
    )


def wide_second_kernel(place, keep, other, mine, send):
    z = place[3]
    for p in range(2):
        for i, bits in enumerate((0, 2)):
            mine[2 * p + i] = added(keep[4 * p + (z ^ bits)], other[4 * p + (z ^ bits)])
            send[2 * p + i] = added(keep[4 * p + (z ^ bits ^ 1)], other[4 * p + (z ^ bits ^ 1)])
    whole = added(keep[8], other[8])
    mine[4] = whole
    send[4] = whole


def wide_second(place, keep, other, after):
    one = ((5, CHUNK, D), BF16)
    return call(
        wide_second_kernel,
        [(1, place), (0, keep), (0, other)],
        [one, one],
        name="wide_second",
        vmem=4,
        after=after,
    )


def wide_third_kernel(keep, other, mine, send):
    for p in range(2):
        mine[p] = added(keep[2 * p], other[2 * p])
        send[p] = added(keep[2 * p + 1], other[2 * p + 1])
    whole = added(keep[4], other[4])
    mine[2] = whole
    send[2] = whole


def wide_third(keep, other, after):
    one = ((3, CHUNK, D), BF16)
    return call(
        wide_third_kernel, [(0, keep), (0, other)], [one, one], name="wide_third", vmem=4, after=after
    )


def wide_last_kernel(keep, other, pair, single):
    pair[...] = added(keep[0:2], other[0:2])
    single[0] = added(keep[2], other[2])


def wide_last(keep, other, after):
    return call(
        wide_last_kernel,
        [(0, keep), (0, other)],
        [((2, CHUNK, D), BF16), ((1, CHUNK, D), BF16)],
        name="wide_last",
        vmem=4,
        after=after,
    )


def low_first_kernel(stay, other, keep, send):
    keep[...] = added(stay[0], other[0])
    send[...] = added(stay[1], other[1])


def low_first(stay, other, after=()):
    one = (stay.shape[1:], BF16)
    return call(
        low_first_kernel, [(0, stay), (0, other)], [one, one], name="low_first", vmem=4, after=after
    )


def low_next_kernel(keep, other, out):
    out[...] = added(keep[...], other[...])


def low_next(keep, other, after=()):
    return call(
        low_next_kernel,
        [(0, keep), (0, other)],
        [(keep.shape, BF16)],
        name="low_next",
        vmem=4,
        after=after,
    )[0]


def low_last_kernel(keep, other, out, vgrad):
    out[...] = added(keep[:, 0 : 3 * D], other[:, 0 : 3 * D])
    vgrad[...] = added(keep[:, 3 * D : 3 * D + 128], other[:, 3 * D : 3 * D + 128])


def low_last(keep, other):
    return call(
        low_last_kernel,
        [(0, keep), (0, other)],
        [((CHUNK, 3 * D), BF16), ((CHUNK, 128), BF16)],
        name="low_last",
        vmem=4,
    )


def chain_kernel(*refs):
    ins, out = refs[:-1], refs[-1]
    at = 0
    for ref in ins:
        flat = ref.reshape(-1, CHUNK, D)
        out[at : at + flat.shape[0]] = flat[...]
        at += flat.shape[0]


def chain(parts, after=()):
    count = sum(p.size for p in parts) // (CHUNK * D)
    return call(
        chain_kernel,
        [(0, p) for p in parts],
        [((count, CHUNK, D), BF16)],
        name="chain",
        vmem=4,
        after=after,
    )[0]


def rest_sum(value, n):
    bit = 16
    while bit < n:
        other = swap(value, "dp", n, bit)
        value = (value.astype(F32) + other.astype(F32)).astype(BF16)
        bit *= 2
    return value


def trades(values, n, shift):
    return [values[0]] + [swap(values[k], "dp", n, k << shift) for k in (1, 2, 3)]


def join_kernel(*refs):
    ins, out = refs[:-1], refs[-1]
    for i, ref in enumerate(ins):
        out[i] = ref[...]


def join(parts, after=()):
    return call(
        join_kernel,
        [(0, p) for p in parts],
        [((len(parts),) + parts[0].shape, parts[0].dtype)],
        name="join",
        vmem=4,
        after=after,
    )[0]


def pack_kernel(place, targets, unit, other, units, packed):
    both = unit[...] + other[...]
    units[...] = both
    row = iota((2 * PAIRS, 128), 0)
    marks = jnp.zeros((2 * PAIRS, 128), jnp.int32)
    for j in range(PAIRS):
        marks = jnp.where(row == j, targets[j], marks)
    marks = jnp.where(iota((2 * PAIRS, 128), 1) < 64, marks >> 5, marks & 31)
    packed[:, 0:D] = both.astype(BF16)
    packed[:, D : D + 128] = marks.astype(F32).astype(BF16)


def pack(place, targets, unit, other):
    return call(
        pack_kernel,
        [(1, place), (1, targets), (0, unit), (0, other)],
        [(unit.shape, F32), ((2 * PAIRS, D + 128), BF16)],
        name="pack",
        vmem=4,
    )


def squares_of(parts):
    acc = jnp.zeros((8, D), F32)
    for part in parts:
        flat = part.reshape(-1, CHUNK, part.shape[-1])
        for k in range(flat.shape[0]):
            for c in range(0, part.shape[-1], D):
                v = flat[k, :, c : c + D].astype(F32)
                acc = acc + jnp.sum((v * v).reshape(CHUNK // 8, 8, D), axis=0)
    return acc[:, 0:128] + acc[:, 128:256] + acc[:, 256:384]


def wide_squares_kernel(*refs):
    refs[-1][...] = squares_of(refs[:-1])


def squares_kernel(place, *refs):
    parts, (vgrad, before, out) = refs[:-3], refs[-3:]
    acc = squares_of(parts) + before[...]
    row = iota((16, 128), 0)
    low_row = 6 * place[0]
    mine = (row >= low_row) & (row < low_row + 6)
    for j in range(3):
        v = jnp.where(mine, vgrad[16 * j : 16 * j + 16, :].astype(F32), 0.0)
        v = v * v
        acc = acc + (v[0:8] + v[8:16])
    out[...] = acc


def squares(place, parts, vgrad=None, before=None, after=()):
    ins = [(0, p) for p in parts]
    kernel = wide_squares_kernel
    if before is not None:
        ins = [(1, place)] + ins + [(0, vgrad), (0, before)]
        kernel = squares_kernel
    return call(kernel, ins, [((8, 128), F32)], name="squares", vmem=4, after=after)[0]


def merge_kernel(place, igrad, other, out):
    @pl.when(place[0] == 0)
    def low_core():
        out[0:OFF, :] = igrad[0:OFF, :]
        out[OFF:WIN, :] = added(igrad[OFF:WIN, :], other[0 : WIN - OFF, :])
        out[WIN:SEQ, :] = other[WIN - OFF : WIN, :]

    @pl.when(place[0] != 0)
    def high_core():
        out[0:OFF, :] = other[0:OFF, :]
        out[OFF:WIN, :] = added(other[OFF:WIN, :], igrad[0 : WIN - OFF, :])
        out[WIN:SEQ, :] = igrad[WIN - OFF : WIN, :]


def merge(place, igrad, other, after):
    return call(
        merge_kernel,
        [(1, place), (0, igrad), (0, other)],
        [((SEQ, D), BF16)],
        micros=1,
        name="merge",
        vmem=4,
        after=after,
    )[0]


def adamw(parameter, first_state, second, clipped, rate):
    first_new = BETA_ONE * first_state + (1.0 - BETA_ONE) * clipped
    second_new = BETA_TWO * second + (1.0 - BETA_TWO) * clipped * clipped
    direction = (first_new * (1.0 / (1.0 - BETA_ONE**STEP))) / (
        jnp.sqrt(second_new * (1.0 / (1.0 - BETA_TWO**STEP))) + ADAM_EPS
    )
    return parameter - rate * (direction + DECAY_RATE * parameter), first_new, second_new


def adamw_kernel(place, *refs):
    sums, refs = refs[:2], refs[2:]
    (vgrad, w, m, v, pv, pm, pq), refs = refs[:7], refs[7:]
    wide, low, refs = refs[:2], refs[2:4], refs[4:]
    outs, (npv, npm, npq, norm), scrs, sems = refs[:4], refs[4:8], refs[8:12], refs[12]
    opt = place[0]
    total = sums[0][...] + sums[1][...]
    total = jnp.sum(jnp.sum(total, axis=1, keepdims=True), axis=0, keepdims=True)
    grad_norm = jnp.sqrt(total)
    factor = jnp.minimum(1.0, CLIP_NORM / (grad_norm + 1e-06))
    norm[...] = grad_norm
    for j in range(3):
        cols = slice(128 * j, 128 * j + 128)
        g = vgrad[16 * j : 16 * j + 16, :].astype(F32)
        g = jnp.where(opt == 0, g[0:6], g[6:12])
        a, b, c = adamw(pv[:, cols], pm[:, cols], pq[:, cols], g * factor, VECTOR_RATE)
        npv[:, cols] = a
        npm[:, cols] = b
        npq[:, cols] = c
    copies = []

    def block(grad, rows, cols):
        new = adamw(w[rows, cols], m[rows, cols], v[rows, cols], grad * factor, LEARN_RATE)
        for scr, value in zip(scrs, new + (new[0].astype(BF16),)):
            scr[rows, cols] = value

    for r in range(4):
        base = CHUNK * place[4 + r]
        wide_part, low_part = wide[r % 2], low[r % 2]

        def rows_of(i, carry, r=r, base=base, wide_part=wide_part, low_part=low_part):
            rows = aligned(base + i * 16, 16, 16)
            here = aligned(i * 16, 16, 16)
            for j, bits in enumerate((0, 2, 1, 3)):
                at = D * (place[3] ^ bits)
                for p, start in enumerate((4 * D + FF, 4 * D)):
                    grad = wide_part[r // 2, 2 * j + p, here, :].astype(F32)
                    block(grad, rows, aligned(start + at, D, 128))
            grad = wide_part[r // 2, 8, here, :].astype(F32)
            block(grad, rows, slice(3 * D, 4 * D))
            for c in range(3):
                grad = low_part[r // 2, here, D * c : D * c + D].astype(F32)
                block(grad, rows, slice(D * c, D * c + D))
            return carry

        lax.fori_loop(0, CHUNK // 16, rows_of, 0)
        rows = aligned(base, CHUNK, 16)
        for i, (scr, out) in enumerate(zip(scrs, outs)):
            copy = pltpu.make_async_copy(scr.at[rows, :], out.at[rows, :], sems.at[r, i])
            copy.start()
            copies.append(copy)
    for copy in copies:
        copy.wait()


def update(place, sums, vgrad, w, m, v, pv, pm, pq, parts):
    ins = tuple(sums) + (vgrad, w, m, v, pv, pm, pq) + tuple(parts)
    shapes = [(w.shape, F32)] * 3 + [(w.shape, BF16)] + [(pv.shape, F32)] * 3 + [((1, 1), F32)]
    return pl.pallas_call(
        adamw_kernel,
        out_shape=[jax.ShapeDtypeStruct(s, d) for s, d in shapes],
        in_specs=[SMEM] + [VMEM] * len(ins),
        out_specs=[ANY] * 4 + [VMEM] * 4,
        scratch_shapes=[
            pltpu.VMEM(w.shape, F32),
            pltpu.VMEM(w.shape, F32),
            pltpu.VMEM(w.shape, F32),
            pltpu.VMEM(w.shape, BF16),
            pltpu.SemaphoreType.DMA((4, 4)),
        ],
        compiler_params=pltpu.CompilerParams(vmem_limit_bytes=16 << 20),
        cost_estimate=pl.CostEstimate(
            flops=4000000000, bytes_accessed=26 * w.size, transcendentals=0
        ),
        name="adamw",
    )(place, *ins)


def shards(
    n,
    tokens,
    lengths,
    query_index,
    doc_index,
    targets,
    weights,
    first_moment,
    second_moment,
    vectors,
    vec_first,
    vec_second,
):
    opt = lax.axis_index("opt")
    me = lax.axis_index("dp")
    plane = me & 3
    columns = [jnp.where(opt == 0, plane ^ r, plane ^ turned(r)) for r in range(4)]
    place = jnp.stack([opt, plane, me, (me >> 2) & 3] + columns).astype(jnp.int32)
    lengths = lengths.reshape(SEGS)
    chosen = jnp.concatenate([query_index, doc_index])
    groups = bit_groups(n)

    extra = jnp.pad(vectors, ((0, 10), (0, 2 * D)))
    w_own = jnp.concatenate([weights[:, : 3 * D], extra], axis=0).astype(BF16)
    w_other = pair(w_own)
    later, w_own = lax.optimization_barrier((weights, w_own))
    wo_own = later[:, 3 * D : 4 * D].astype(BF16)
    wu_own = later[:, 4 * D : 4 * D + FF].astype(BF16)
    wd_own = later[:, 4 * D + FF :].astype(BF16)
    wo = (wo_own, pair(wo_own))
    wu = (wu_own, pair(wu_own))
    wd = (wd_own, pair(wd_own))

    proj, att, lse, segc, segr, vec = attend(place, lengths, tokens, w_own, w_other)
    xhat1, inv1, hlow, act, slope, xhat2, inv2, unit, uscale = mlp(
        place, lengths, chosen, att, tokens, segr, vec, wo + wu + wd
    )
    units, packed = pack(place, targets, unit, swap(unit, "opt", 2, 1))
    groups = bit_groups(n)
    order = [0]
    stack = packed
    for i, (shift, size) in enumerate(groups[1:] + groups[:1]):
        pieces = [stack] + [swap(stack, "dp", n, k << shift) for k in range(1, size)]
        order = [o | (k << shift) for k in range(size) for o in order]
        if i < len(groups) - 1:
            stack = join(pieces).reshape(-1, 2 * PAIRS, D + 128)
    dsec, dlow, keep, send, dsums = down_backward(
        n, order, place, lengths, chosen, units, segc, uscale, (xhat2, inv2, act), vec, pieces
    )
    other = pair(send)
    dup, ukeep, usend, usums = up_backward(place, dlow, slope, hlow, wd, [])
    dstay, go = down_pair(keep, other, [dup])
    dother = cross(go, n, True)
    uother = pair(usend)
    dfirst, datt, delta, okeep, osend, fsums = first_backward(
        place, dup, dsec, xhat1, inv1, att, vec, wu + wo, [dstay]
    )
    ustay, go = up_pair((ukeep, uother, okeep, pair(osend)), [dfirst, dother])
    uother = cross(go, n, True)
    ins = (tokens, proj, datt, lse, delta, segc, segr)
    part0, keep0, send0, sums0 = heads_backward(0, place, ins, (), [ustay])
    wide, go = wide_first((dstay, dother, ustay, uother), [part0])
    wother = cross(go, n, False)
    part1, keep1, send1, sums1 = heads_backward(1, place, ins, (), [wide, part0])
    wide, go = wide_second(place, wide, wother, [part1])
    wother = swap(go, "dp", n, 4)
    part2, keep, send, _ = heads_backward(
        2, place, ins, (keep0, send0, keep1, send1, dsums, usums, fsums, sums0, sums1), [wide, part1]
    )
    wide, go = wide_third(wide, wother, [part2])
    send, wide, go = lax.optimization_barrier((send, wide, go))
    other = pair(send)
    wother = swap(go, "dp", n, 8)
    igrad = input_backward(place, (part0, part1, part2), dfirst, w_own, w_other, [wide])
    low, go = down_pair(keep, other, [igrad])
    other = cross(go, n, True)
    wide, single = wide_last(wide, wother, [low])
    wide, single = rest_sum(wide, n), rest_sum(single, n)
    wother = swap(wide, "dp", n, 8)
    iother = pair(igrad)
    low, go = low_first(low, other, [wide])
    other = cross(go, n, False)
    wide = chain([wide, wother], [low])
    wother = swap(wide, "dp", n, 4)
    low = low_next(low, other, [wide])
    other = swap(low, "dp", n, 4)
    wide = chain([wide, wother, single], [low])
    wother = cross(wide, n, False)
    low = low_next(low, other, [wide])
    other = swap(low, "dp", n, 8)
    wide = join([wide, wother], [low])
    wide = (wide, cross(wide, n, True))
    input_grad = merge(place, igrad, iother, [wide[0]])
    low, vgrad = low_last(low, other)
    low, vgrad = rest_sum(low, n), rest_sum(vgrad, n)
    low = join([low, cross(low, n, False)])
    low = (low, cross(low, n, True))
    sums = squares(place, low, vgrad, squares(place, wide, after=[low[0]]))
    sums = (sums, pair(sums))
    pieces = wide + low
    nw, nm, nv, nlow, npv, npm, npq, norm = update(
        place, sums, vgrad, weights, first_moment, second_moment,
        vectors, vec_first, vec_second, pieces,
    )
    return (norm.reshape(()), input_grad, nw, nm, nv, nlow, npv, npm, npq)


def solution(mesh):
    rows = P("opt", None)
    in_specs = (P("dp", None), P("dp", None), P("dp"), P("dp"), P("dp")) + (rows,) * 6
    out_specs = (P(), P("dp", None)) + (rows,) * 7
    n = mesh.shape["dp"]
    return jax.shard_map(
        functools.partial(shards, n),
        mesh=mesh,
        in_specs=in_specs,
        out_specs=out_specs,
        check_vma=False,
    )
```

```python
import functools

import jax
import jax.numpy as jnp
from jax import lax
from jax.experimental import pallas as pl
from jax.experimental.pallas import tpu as pltpu
from jax.sharding import PartitionSpec as P

D = 384
HEADS = 12
HD = 32
FF = 1536
SEQ = 1024
SEGS = 16
PAIRS = 8
STEP = 10

WIN = 576
OFF = SEQ - WIN
PAD = 640
BLOCK = 128
BANDS = tuple((q, max(0, q - 128), min(WIN, q + 256)) for q in range(0, WIN, BLOCK))
BAND_ROWS = tuple(sum(b[2] - b[1] for b in BANDS[:i]) for i in range(len(BANDS) + 1))
ROWS = 64

LN_EPS = 1e-06
POOL_EPS = 1e-06
SCORE_SCALE = 50.0
CLIP_NORM = 0.001
BETA_ONE = 0.9
BETA_TWO = 0.98
ADAM_EPS = 1e-08
LEARN_RATE = 0.05
VECTOR_RATE = 0.3
DECAY_RATE = 0.01
NEG_BIG = -1e30
HALF = D // 2
CHUNK = HALF // 4
EXP2_SCALE = HD ** (-0.5) * 1.4426950408889634

F32 = jnp.float32
BF16 = jnp.bfloat16
VMEM = pl.BlockSpec(memory_space=pltpu.VMEM)
SMEM = pl.BlockSpec(memory_space=pltpu.SMEM)
ANY = pl.BlockSpec(memory_space=pl.ANY)


def nn(a, b):
    return jnp.dot(a, b, preferred_element_type=F32)


def nt(a, b):
    return lax.dot_general(a, b, (((1,), (1,)), ((), ())), preferred_element_type=F32)


def tn(a, b):
    return lax.dot_general(a, b, (((0,), (0,)), ((), ())), preferred_element_type=F32)


def exact(a, b, dims):
    return lax.dot_general(
        a, b, (dims, ((), ())), precision=lax.Precision.HIGHEST, preferred_element_type=F32
    )


def iota(shape, axis):
    return lax.broadcasted_iota(jnp.int32, shape, axis)


def low_pair(value):
    high = value.astype(BF16)
    return high, (value - high.astype(F32)).astype(BF16)


def aligned(start, size, unit):
    return pl.ds(pl.multiple_of(start, unit), size)


def assemble(dst, own, other, opt):
    dst[aligned(HALF * opt, HALF, 64), :] = own[0:HALF, :]
    dst[aligned(HALF * (1 - opt), HALF, 64), :] = other[0:HALF, :]


def call(kernel, ins, outs, scratch=(), micros=5, name=None, vmem=12, after=()):
    specs = [SMEM if s else VMEM for s, _ in ins] + [ANY] * len(after)
    count = len(ins)

    def body(*refs):
        kernel(*refs[:count], *refs[count + len(after) :])

    shapes = [jax.ShapeDtypeStruct(s, d) for s, d in outs]
    moved = sum(a.size * a.dtype.itemsize for _, a in ins)
    moved += sum(s.size * s.dtype.itemsize for s in shapes)
    return pl.pallas_call(
        body,
        out_shape=shapes,
        in_specs=specs,
        out_specs=[VMEM] * len(shapes),
        scratch_shapes=list(scratch),
        compiler_params=pltpu.CompilerParams(vmem_limit_bytes=vmem << 20),
        cost_estimate=pl.CostEstimate(
            flops=micros * 1100000000, bytes_accessed=moved, transcendentals=0
        ),
        name=name,
    )(*[a for _, a in ins], *after)


def head_stack(rows):
    lane_head = iota(rows.shape, 1) // HD
    zero = jnp.zeros_like(rows)
    return jnp.concatenate([jnp.where(lane_head == j, rows, zero) for j in range(4)], axis=0)


def attend_kernel(
    place, lengths, tokens, w_own, w_other, proj, att, lse, segc, segr, vec, wfull, bias, vt
):
    opt = place[0]
    assemble(wfull, w_own, w_other, opt)
    mine = w_own[HALF : HALF + 16, 0:D].astype(F32)
    others = w_other[HALF : HALF + 16, 0:D].astype(F32)
    first = opt == 0
    vec[0:6, :] = jnp.where(first, mine, others)[0:6]
    vec[6:12, :] = jnp.where(first, others, mine)[0:6]
    vec[12:16, :] = jnp.zeros((4, D), F32)

    pos_col = iota((WIN, 128), 0) + OFF * opt
    pos_row = iota((8, PAD), 1) + OFF * opt
    seg_col = jnp.zeros((WIN, 128), jnp.int32)
    seg_row = jnp.zeros((8, PAD), jnp.int32)
    bound = jnp.int32(0)
    for s in range(SEGS):
        bound = bound + lengths[s]
        seg_col = seg_col + (pos_col >= bound).astype(jnp.int32)
        seg_row = seg_row + (pos_row >= bound).astype(jnp.int32)
    segc[...] = seg_col
    segr[...] = seg_row
    for i, (q0, k0, k1) in enumerate(BANDS):
        bias[BAND_ROWS[i] : BAND_ROWS[i + 1], :] = jnp.where(
            segc[k0:k1, :] == segr[0:1, q0 : q0 + BLOCK], 0.0, NEG_BIG
        )

    x = tokens[aligned(OFF * opt, WIN, 64), :]
    for c in range(3):
        acc = nn(x, wfull[:, c * D : (c + 1) * D])
        if c != 1:
            acc = acc + vec[(0 if c == 0 else 1) : (1 if c == 0 else 2), :]
        proj[0:WIN, c * D : (c + 1) * D] = acc.astype(BF16)
    proj[WIN:PAD, :] = jnp.zeros((PAD - WIN, 3 * D), BF16)

    def group(g, carry):
        def lanes(part):
            return aligned(part * D + 128 * g, 128, 128)

        for t in range(PAD // 128):
            vt[:, 128 * t : 128 * t + 128] = (
                proj[128 * t : 128 * t + 128, lanes(2)].astype(F32).T.astype(BF16)
            )
        for i, (q0, k0, k1) in enumerate(BANDS):
            stack = head_stack(proj[q0 : q0 + BLOCK, lanes(0)])
            st = nt(proj[k0:k1, lanes(1)], stack)
            outs = []
            for j in range(4):
                t = (
                    st[:, j * BLOCK : (j + 1) * BLOCK] * EXP2_SCALE
                    + bias[BAND_ROWS[i] : BAND_ROWS[i + 1], :]
                )
                peak = jnp.max(t, axis=0, keepdims=True)
                powers = jnp.exp2(t - peak)
                total = jnp.sum(powers, axis=0, keepdims=True)
                lse[g, j : j + 1, q0 : q0 + BLOCK] = peak + jnp.log2(total)
                o = nn(vt[j * HD : (j + 1) * HD, k0:k1], powers.astype(BF16))
                outs.append(o * (1.0 / total))
            rows = min(BLOCK, WIN - q0)
            att[q0 : q0 + rows, aligned(128 * g, 128, 128)] = (
                jnp.concatenate(outs, axis=0).T[0:rows].astype(BF16)
            )
        return carry

    lax.fori_loop(0, 3, group, 0)


def attend(place, lengths, tokens, w_own, w_other):
    return call(
        attend_kernel,
        [(1, place), (1, lengths), (0, tokens), (0, w_own), (0, w_other)],
        [
            ((PAD, 3 * D), BF16),
            ((WIN, D), BF16),
            ((3, 4, PAD), F32),
            ((WIN, 128), jnp.int32),
            ((8, PAD), jnp.int32),
            ((16, D), F32),
        ],
        [
            pltpu.VMEM((D, 3 * D), BF16),
            pltpu.VMEM((BAND_ROWS[-1], 128), F32),
            pltpu.VMEM((128, PAD), BF16),
        ],
        micros=8,
        name="attend",
    )


def owned(place, lengths, segment):
    bound = jnp.int32(0)
    count = jnp.int32(0)
    for s in range(SEGS):
        bound = bound + lengths[s]
        count = count + (bound <= WIN).astype(jnp.int32)
    low_side = (segment < count).astype(jnp.int32)
    return low_side == (place[0] == 0).astype(jnp.int32)


def mlp_kernel(
    place, lengths, chosen, att, tokens, segr, vec, wo_own, wo_other, wu_own, wu_other,
    wd_own, wd_other, xhat1, inv1, hlow, act, slope, xhat2, inv2, unit, uscale,
    wo, wu, wd, tmp, hid, ench, encl,
):
    opt = place[0]
    assemble(wo, wo_own, wo_other, opt)
    assemble(wu, wu_own, wu_other, opt)
    assemble(wd, wd_own, wd_other, opt)
    tmp[...] = nn(att[...], wo[...])

    def first_norm(i, carry):
        r = aligned(i * ROWS, ROWS, ROWS)
        x = tokens[aligned(OFF * opt + i * ROWS, ROWS, ROWS), :].astype(F32)
        v = tmp[r, :] + vec[2:3, :] + x
        centred = v - jnp.mean(v, axis=1, keepdims=True)
        inverse = lax.rsqrt(jnp.mean(centred * centred, axis=1, keepdims=True) + LN_EPS)
        normed = centred * inverse
        xhat1[r, :] = normed
        inv1[r, :] = jnp.broadcast_to(inverse, (ROWS, 128))
        h = normed * vec[8:9, :] + vec[9:10, :]
        hid[r, :] = h
        hlow[r, :] = h.astype(BF16)
        return carry

    lax.fori_loop(0, WIN // ROWS, first_norm, 0)

    for c in range(4):
        cols = slice(c * D, (c + 1) * D)
        tmp[...] = nn(hlow[...], wu[:, cols])

        def gelu(i, carry, cols=cols, c=c):
            r = aligned(i * ROWS, ROWS, ROWS)
            u = tmp[r, :] + vec[3 + c : 4 + c, :]
            half = lax.erf(u * 0.7071067811865476) * 0.5 + 0.5
            act[r, cols] = (u * half).astype(BF16)
            slope[r, cols] = half + u * jnp.exp(-0.5 * u * u) * 0.3989422804014327
            return carry

        lax.fori_loop(0, WIN // ROWS, gelu, 0)

    tmp[...] = nt(act[...], wd[...])

    def second_norm(i, carry):
        r = aligned(i * ROWS, ROWS, ROWS)
        v = tmp[r, :] + vec[7:8, :] + hid[r, :]
        centred = v - jnp.mean(v, axis=1, keepdims=True)
        inverse = lax.rsqrt(jnp.mean(centred * centred, axis=1, keepdims=True) + LN_EPS)
        normed = centred * inverse
        xhat2[r, :] = normed
        inv2[r, :] = jnp.broadcast_to(inverse, (ROWS, 128))
        high, rest = low_pair(normed * vec[10:11, :] + vec[11:12, :])
        ench[r, :] = high
        encl[r, :] = rest
        return carry

    lax.fori_loop(0, WIN // ROWS, second_norm, 0)

    seg = segr[0:1, 0:WIN]
    row_id = iota((2 * PAIRS, WIN), 0)
    wanted = jnp.zeros((2 * PAIRS, WIN), jnp.int32)
    for j in range(2 * PAIRS):
        wanted = jnp.where(row_id == j, chosen[j], wanted)
    mask = owned(place, lengths, jnp.broadcast_to(seg, (2 * PAIRS, WIN)))
    onehot = jnp.where((wanted == seg) & mask, 1.0, 0.0)
    count = jnp.maximum(jnp.sum(onehot, axis=1, keepdims=True), 1.0)
    hot = onehot.astype(BF16)
    pooled = (nn(hot, ench[...]) + nn(hot, encl[...])) / count
    inverse_len = lax.rsqrt(jnp.sum(pooled * pooled, axis=1, keepdims=True) + POOL_EPS)
    unit[...] = pooled * inverse_len
    uscale[...] = jnp.broadcast_to(inverse_len / count, (2 * PAIRS, 128))


def mlp(place, lengths, chosen, att, tokens, segr, vec, halves):
    return call(
        mlp_kernel,
        [(1, place), (1, lengths), (1, chosen), (0, att), (0, tokens), (0, segr), (0, vec)]
        + [(0, h) for h in halves],
        [
            ((WIN, D), F32),
            ((WIN, 128), F32),
            ((WIN, D), BF16),
            ((WIN, FF), BF16),
            ((WIN, FF), F32),
            ((WIN, D), F32),
            ((WIN, 128), F32),
            ((2 * PAIRS, D), F32),
            ((2 * PAIRS, 128), F32),
        ],
        [
            pltpu.VMEM((D, D), BF16),
            pltpu.VMEM((D, FF), BF16),
            pltpu.VMEM((D, FF), BF16),
            pltpu.VMEM((WIN, D), F32),
            pltpu.VMEM((WIN, D), F32),
            pltpu.VMEM((WIN, D), BF16),
            pltpu.VMEM((WIN, D), BF16),
        ],
        micros=10,
        name="mlp",
    )


def turned(chunk):
    return (chunk & 1) * 2 + (chunk >> 1)


def split_rows(grad, keep, send, place, *at):
    opt = place[0]
    for c in range(4):
        straight = c ^ place[1]
        mine = jnp.where(opt == 0, straight, turned(straight))
        theirs = jnp.where(opt == 0, turned(straight), straight)
        keep[(mine,) + at] = grad[aligned(HALF * opt + CHUNK * c, CHUNK, 16), :].astype(BF16)
        send[(theirs,) + at] = grad[aligned(HALF * (1 - opt) + CHUNK * c, CHUNK, 16), :].astype(BF16)


def column_sums(value):
    return jnp.sum(value.reshape(ROWS // 8, 8, D), axis=0)


def norm_backward(grad_at, normed_ref, inverse_ref, gain, out, low_out, sums, at):
    def block(i, carry):
        scale_sum, shift_sum, bias_sum = carry
        r = aligned(i * ROWS, ROWS, ROWS)
        g = grad_at(r)
        normed = normed_ref[r, :]
        scaled = g * gain
        inner = (
            scaled
            - jnp.mean(scaled, axis=1, keepdims=True)
            - normed * jnp.mean(scaled * normed, axis=1, keepdims=True)
        ) * inverse_ref[r, 0:1]
        out[r, :] = inner
        low_out[r, :] = inner.astype(BF16)
        return (
            scale_sum + column_sums(g * normed),
            shift_sum + column_sums(g),
            bias_sum + column_sums(inner),
        )

    zero = jnp.zeros((8, D), F32)
    scale_sum, shift_sum, bias_sum = lax.fori_loop(0, WIN // ROWS, block, (zero, zero, zero))
    sums[at : at + 1, :] = jnp.sum(bias_sum, axis=0, keepdims=True)
    sums[at + 1 : at + 2, :] = jnp.sum(scale_sum, axis=0, keepdims=True)
    sums[at + 2 : at + 3, :] = jnp.sum(shift_sum, axis=0, keepdims=True)


def down_kernel(
    count, order, place, lengths, chosen, units, segc, uscale, xhat2, inv2, act, vec, *rest
):
    pieces, (dsec, dlow, keep, send, sums, queries, docs, marks, grad) = rest[:-9], rest[-9:]
    me = place[2]
    per = pieces[0].shape[0]
    for p, piece in enumerate(pieces):
        for j in range(per):
            at = order[p * per + j]
            r = slice(at * PAIRS, (at + 1) * PAIRS)
            both = piece[j].astype(F32)
            queries[r, :] = both[0:PAIRS, 0:D]
            docs[r, :] = both[PAIRS : 2 * PAIRS, 0:D]
            marks[r, :] = both[0:PAIRS, D : D + 128]
    total = count * PAIRS
    q = queries[...].astype(BF16)
    d = docs[...].astype(BF16)
    logits = SCORE_SCALE * nt(q, d)
    peak = jnp.max(logits, axis=1, keepdims=True)
    powers = jnp.exp(logits - peak)
    soft = powers / jnp.sum(powers, axis=1, keepdims=True)
    col = iota((total, total), 1)
    doc_id = ((col // PAIRS) ^ me) * PAIRS + lax.rem(col, PAIRS)
    hit = (marks[:, 0:1] * 32.0 + marks[:, 64:65]).astype(jnp.int32) == doc_id
    d_logits = (soft - jnp.where(hit, 1.0, 0.0)) * (SCORE_SCALE / total)
    high, rest_low = low_pair(d_logits[0:PAIRS, :])
    d_q = nn(high, d) + nn(rest_low, d)
    high, rest_low = low_pair(d_logits[:, 0:128].T[0:PAIRS, :])
    d_d = nn(high, q) + nn(rest_low, q)
    d_units = jnp.concatenate([d_q, d_d], axis=0)
    u = units[...]
    d_pool = uscale[:, 0:1] * (d_units - u * jnp.sum(u * d_units, axis=1, keepdims=True))
    lane = iota((8, 2 * PAIRS), 1)
    wanted = jnp.zeros((8, 2 * PAIRS), jnp.int32)
    for j in range(2 * PAIRS):
        wanted = jnp.where(lane == j, chosen[j], wanted)
    seg = segc[:, 0 : 2 * PAIRS]
    mask = owned(place, lengths, seg)
    hot = jnp.where((seg == wanted[0:1, :]) & mask, 1.0, 0.0).astype(BF16)
    high, rest_low = low_pair(d_pool)
    dsec[...] = nn(hot, high) + nn(hot, rest_low)
    norm_backward(lambda r: dsec[r, :], xhat2, inv2, vec[10:11, :], dsec, dlow, sums, 0)
    sums[3:8, :] = jnp.zeros((5, D), F32)
    for c in range(4):
        cols = slice(c * D, (c + 1) * D)
        grad[...] = tn(dlow[...], act[:, cols])
        split_rows(grad, keep, send, place, c)


def down_backward(count, order, place, lengths, chosen, units, segc, uscale, saved, vec, pieces):
    total = count * PAIRS
    return call(
        functools.partial(down_kernel, count, order),
        [(1, place), (1, lengths), (1, chosen), (0, units), (0, segc), (0, uscale)]
        + [(0, s) for s in saved]
        + [(0, vec)]
        + [(0, p) for p in pieces],
        [
            ((WIN, D), F32),
            ((WIN, D), BF16),
            ((4, 4, CHUNK, D), BF16),
            ((4, 4, CHUNK, D), BF16),
            ((8, D), F32),
        ],
        [
            pltpu.VMEM((total, D), F32),
            pltpu.VMEM((total, D), F32),
            pltpu.VMEM((total, 128), F32),
            pltpu.VMEM((D, D), F32),
        ],
        micros=4,
        name="down_backward",
    )


def up_kernel(place, dlow, slope, hlow, wd_own, wd_other, dup, keep, send, sums, wd, grad):
    opt = place[0]
    assemble(wd, wd_own, wd_other, opt)
    for c in range(4):
        cols = slice(c * D, (c + 1) * D)
        part = (nn(dlow[...], wd[:, cols]) * slope[:, cols]).astype(BF16)
        dup[:, cols] = part
        sums[c : c + 1, :] = jnp.sum(part.astype(F32), axis=0, keepdims=True)
        grad[...] = tn(hlow[...], dup[:, cols])
        split_rows(grad, keep, send, place, c)


def up_backward(place, dlow, slope, hlow, halves, after):
    return call(
        up_kernel,
        [(1, place)] + [(0, a) for a in (dlow, slope, hlow) + tuple(halves)],
        [((WIN, FF), BF16), ((4, 4, CHUNK, D), BF16), ((4, 4, CHUNK, D), BF16), ((4, D), F32)],
        [pltpu.VMEM((D, FF), BF16), pltpu.VMEM((D, D), F32)],
        micros=3,
        name="up_backward",
        after=after,
    )


def first_kernel(
    place, dup, dsec, xhat1, inv1, att, vec, wu_own, wu_other, wo_own, wo_other,
    dfirst, datt, delta, okeep, osend, sums, wu, wo, grad, dlow,
):
    opt = place[0]
    assemble(wu, wu_own, wu_other, opt)
    assemble(wo, wo_own, wo_other, opt)
    dfirst[...] = nt(dup[...], wu[...])
    norm_backward(
        lambda r: dfirst[r, :] + dsec[r, :], xhat1, inv1, vec[8:9, :], dfirst, dlow, sums, 0
    )
    sums[3:8, :] = jnp.zeros((5, D), F32)
    grad[...] = tn(att[...], dlow[...])
    split_rows(grad, okeep, osend, place)
    da = nt(dlow[...], wo[...]).astype(BF16)
    datt[0:WIN, :] = da
    datt[WIN:PAD, :] = jnp.zeros((PAD - WIN, D), BF16)
    high, rest = low_pair(da.astype(F32) * att[...].astype(F32))
    heads = (iota((16, D), 1) // HD == iota((16, D), 0)).astype(F32).astype(BF16)
    delta[:, 0:WIN] = nt(heads, high) + nt(heads, rest)
    delta[:, WIN:PAD] = jnp.zeros((16, PAD - WIN), F32)


def first_backward(place, dup, dsec, xhat1, inv1, att, vec, halves, after):
    return call(
        first_kernel,
        [(1, place)] + [(0, a) for a in (dup, dsec, xhat1, inv1, att, vec) + tuple(halves)],
        [
            ((WIN, D), F32),
            ((PAD, D), BF16),
            ((16, PAD), F32),
            ((4, CHUNK, D), BF16),
            ((4, CHUNK, D), BF16),
            ((8, D), F32),
        ],
        [
            pltpu.VMEM((D, FF), BF16),
            pltpu.VMEM((D, D), BF16),
            pltpu.VMEM((D, D), F32),
            pltpu.VMEM((WIN, D), BF16),
        ],
        micros=3,
        name="first_backward",
        after=after,
    )


def heads_kernel(g, place, tokens, proj, datt, lse, delta, segc, segr, *rest):
    rest, (dproj, keep, send, sums, kt, dk, dv, grad, ktmp, stmp) = rest[:-10], rest[-10:]

    def lanes(part):
        return slice(part * D + 128 * g, part * D + 128 * g + 128)

    for t in range(PAD // 128):
        kt[:, 128 * t : 128 * t + 128] = (
            proj[128 * t : 128 * t + 128, lanes(1)].astype(F32).T.astype(BF16)
        )
    dk[...] = jnp.zeros_like(dk)
    dv[...] = jnp.zeros_like(dv)
    for q0, k0, k1 in BANDS:
        qs = head_stack(proj[q0 : q0 + BLOCK, lanes(0)])
        gs = head_stack(datt[q0 : q0 + BLOCK, lanes(0)])
        st = nt(proj[k0:k1, lanes(1)], qs)
        dp = nt(proj[k0:k1, lanes(2)], gs)
        same = segc[k0:k1, :] == segr[0:1, q0 : q0 + BLOCK]
        bias = jnp.where(same, 0.0, NEG_BIG)
        probs, d_scores, dq = [], [], []
        for j in range(4):
            cols = slice(j * BLOCK, (j + 1) * BLOCK)
            prob = jnp.exp2(st[:, cols] * EXP2_SCALE + bias - lse[g, j : j + 1, q0 : q0 + BLOCK])
            ds = prob * (dp[:, cols] - delta[4 * g + j : 4 * g + j + 1, q0 : q0 + BLOCK])
            ds = ds.astype(BF16)
            probs.append(prob.astype(BF16))
            d_scores.append(ds)
            dq.append(nn(kt[j * HD : (j + 1) * HD, k0:k1], ds))
        dv[k0:k1, :] += nn(jnp.concatenate(probs, axis=1), gs)
        dk[k0:k1, :] += nn(jnp.concatenate(d_scores, axis=1), qs)
        rows = min(BLOCK, WIN - q0)
        dqs = jnp.concatenate(dq, axis=0).T[0:rows] * HD ** (-0.5)
        dproj[q0 : q0 + rows, 0:128] = dqs.astype(BF16)
    dproj[:, 128:256] = (dk[...] * HD ** (-0.5)).astype(BF16)
    dproj[:, 256:384] = dv[...].astype(BF16)
    grad[...] = tn(tokens[aligned(OFF * place[0], WIN, 64), :], dproj[...])
    q_sum = jnp.sum(dproj[:, 0:128].astype(F32), axis=0, keepdims=True)
    v_sum = jnp.sum(dproj[:, 256:384].astype(F32), axis=0, keepdims=True)
    sums[0:1, :] = q_sum
    sums[1:2, :] = v_sum
    sums[2:8, :] = jnp.zeros((6, 128), F32)
    if g < 2:
        split_rows(grad, keep, send, place)
        return
    parts, (dsums, usums, fsums, zero, one) = rest[:4], rest[4:]
    split_rows(grad, ktmp, stmp, place)
    for dst, blocks in (
        (keep, (parts[0], parts[2], ktmp)),
        (send, (parts[1], parts[3], stmp)),
    ):
        for h, part in enumerate(blocks):
            for c in range(3):
                dst[:, :, D * c + 128 * h : D * c + 128 * h + 128] = part[
                    :, :, 128 * c : 128 * c + 128
                ]
    rows = jnp.concatenate(
        [
            jnp.concatenate([zero[0:1], one[0:1], q_sum], axis=1),
            jnp.concatenate([zero[1:2], one[1:2], v_sum], axis=1),
            fsums[0:1, :],
            usums[0:4, :],
            dsums[0:1, :],
            fsums[1:3, :],
            dsums[1:3, :],
            jnp.zeros((4, D), F32),
        ],
        axis=0,
    ).astype(BF16)
    for c in range(4):
        for j in range(3):
            block = rows[:, 128 * j : 128 * j + 128]
            keep[c, 16 * j : 16 * j + 16, 3 * D : 3 * D + 128] = block
            send[c, 16 * j : 16 * j + 16, 3 * D : 3 * D + 128] = block


def heads_backward(g, place, ins, more, after):
    part = ((4, CHUNK, 3 * D + 128 if g == 2 else D), BF16)
    return call(
        functools.partial(heads_kernel, g),
        [(1, place)] + [(0, a) for a in tuple(ins) + tuple(more)],
        [((WIN, D), BF16), part, part, ((8, 128), F32)],
        [
            pltpu.VMEM((128, PAD), BF16),
            pltpu.VMEM((WIN, 128), F32),
            pltpu.VMEM((WIN, 128), F32),
            pltpu.VMEM((D, D), F32),
            pltpu.VMEM((4, CHUNK, D), BF16),
            pltpu.VMEM((4, CHUNK, D), BF16),
        ],
        micros=3,
        name="heads_backward",
        after=after,
    )


def input_kernel(place, dp0, dp1, dp2, dfirst, w_own, w_other, igrad, wfull, dproj):
    assemble(wfull, w_own, w_other, place[0])
    for g, part in enumerate((dp0, dp1, dp2)):
        for c in range(3):
            dproj[:, c * D + 128 * g : c * D + 128 * g + 128] = part[:, 128 * c : 128 * c + 128]
    igrad[...] = (nt(dproj[...], wfull[...]) + dfirst[...]).astype(BF16)


def input_backward(place, parts, dfirst, w_own, w_other, after):
    return call(
        input_kernel,
        [(1, place)] + [(0, a) for a in tuple(parts) + (dfirst, w_own, w_other)],
        [((WIN, D), BF16)],
        [pltpu.VMEM((D, 3 * D), BF16), pltpu.VMEM((WIN, 3 * D), BF16)],
        micros=2,
        name="input_backward",
        after=after,
    )[0]


def flips(axis, size, bits):
    return [(i, i ^ bits) for i in range(size)]


def pair(value):
    return swap(value, "opt", 2, 1)


def swap(value, axis, size, bits):
    return lax.ppermute(value, axis, flips(axis, size, bits))


def bit_groups(size):
    bits = size.bit_length() - 1
    return [(s, 1 << min(2, bits - s)) for s in range(0, bits, 2)]


def cross(value, n, first):
    pairs = []
    for i in range(n):
        for core in range(2):
            bit = 1 if (core == 0) == first else 2
            pairs.append((2 * i + core, 2 * (i ^ bit) + core))
    return lax.ppermute(value, ("dp", "opt"), pairs)


def added(a, b):
    return (a.astype(F32) + b.astype(F32)).astype(BF16)


def pack_kernel(place, targets, unit, other, units, packed):
    both = unit[...] + other[...]
    units[...] = both
    row = iota((2 * PAIRS, 128), 0)
    marks = jnp.zeros((2 * PAIRS, 128), jnp.int32)
    for j in range(PAIRS):
        marks = jnp.where(row == j, targets[j], marks)
    marks = jnp.where(iota((2 * PAIRS, 128), 1) < 64, marks >> 5, marks & 31)
    packed[0, :, 0:D] = both.astype(BF16)
    packed[0, :, D : D + 128] = marks.astype(F32).astype(BF16)


def pack(place, targets, unit, other):
    return call(
        pack_kernel,
        [(1, place), (1, targets), (0, unit), (0, other)],
        [(unit.shape, F32), ((1, 2 * PAIRS, D + 128), BF16)],
        name="pack",
        vmem=4,
    )


def join_kernel(*refs):
    ins, out = refs[:-1], refs[-1]
    at = 0
    for ref in ins:
        out[at : at + ref.shape[0]] = ref[...]
        at += ref.shape[0]


def join(parts):
    rows = sum(p.shape[0] for p in parts)
    return call(
        join_kernel,
        [(0, p) for p in parts],
        [((rows,) + parts[0].shape[1:], parts[0].dtype)],
        name="join",
        vmem=4,
    )[0]


def down_pair_kernel(keep, other, stay, go):
    for half in range(2):
        stay[half] = added(keep[2 * half], other[2 * half])
        go[half] = added(keep[2 * half + 1], other[2 * half + 1])


def down_pair(keep, other, after=()):
    half = ((2,) + keep.shape[1:], BF16)
    return call(
        down_pair_kernel, [(0, keep), (0, other)], [half, half], name="pair_sum", vmem=4, after=after
    )


def up_pair_kernel(keep, other, okeep, oother, stay, go):
    for half in range(2):
        stay[half, 0:4] = added(keep[2 * half], other[2 * half])
        stay[half, 4] = added(okeep[2 * half], oother[2 * half])
        go[half, 0:4] = added(keep[2 * half + 1], other[2 * half + 1])
        go[half, 4] = added(okeep[2 * half + 1], oother[2 * half + 1])


def up_pair(parts, after):
    half = ((2, 5, CHUNK, D), BF16)
    return call(
        up_pair_kernel, [(0, p) for p in parts], [half, half], name="up_pair", vmem=4, after=after
    )


def wide_first_kernel(dstay, dother, ustay, uother, keep, send):
    for i, out in enumerate((keep, send)):
        out[0:4] = added(dstay[i], dother[i])
        out[4:9] = added(ustay[i], uother[i])


def wide_first(parts, after):
    one = ((9, CHUNK, D), BF16)
    return call(
        wide_first_kernel, [(0, p) for p in parts], [one, one], name="wide_first", vmem=4, after=after
    )


def wide_second_kernel(place, keep, other, mine, send):
    z = place[3]
    for p in range(2):
        for i, bits in enumerate((0, 2)):
            mine[2 * p + i] = added(keep[4 * p + (z ^ bits)], other[4 * p + (z ^ bits)])
            send[2 * p + i] = added(keep[4 * p + (z ^ bits ^ 1)], other[4 * p + (z ^ bits ^ 1)])
    whole = added(keep[8], other[8])
    mine[4] = whole
    send[4] = whole


def wide_second(place, keep, other, after):
    one = ((5, CHUNK, D), BF16)
    return call(
        wide_second_kernel,
        [(1, place), (0, keep), (0, other)],
        [one, one],
        name="wide_second",
        vmem=4,
        after=after,
    )


def wide_third_kernel(keep, other, mine, send):
    for p in range(2):
        mine[p] = added(keep[2 * p], other[2 * p])
        send[p] = added(keep[2 * p + 1], other[2 * p + 1])
    whole = added(keep[4], other[4])
    mine[2] = whole
    send[2] = whole


def wide_third(keep, other, after):
    one = ((3, CHUNK, D), BF16)
    return call(
        wide_third_kernel, [(0, keep), (0, other)], [one, one], name="wide_third", vmem=4, after=after
    )


def wide_last_kernel(keep, other, pair, single):
    pair[...] = added(keep[0:2], other[0:2])
    single[0] = added(keep[2], other[2])


def wide_last(keep, other, after):
    return call(
        wide_last_kernel,
        [(0, keep), (0, other)],
        [((2, CHUNK, D), BF16), ((1, CHUNK, D), BF16)],
        name="wide_last",
        vmem=4,
        after=after,
    )


def low_first_kernel(stay, other, keep, send):
    keep[...] = added(stay[0], other[0])
    send[...] = added(stay[1], other[1])


def low_first(stay, other, after=()):
    one = (stay.shape[1:], BF16)
    return call(
        low_first_kernel, [(0, stay), (0, other)], [one, one], name="low_first", vmem=4, after=after
    )


def low_next_kernel(keep, other, out):
    out[...] = added(keep[...], other[...])


def low_next(keep, other, after=()):
    return call(
        low_next_kernel,
        [(0, keep), (0, other)],
        [(keep.shape, BF16)],
        name="low_next",
        vmem=4,
        after=after,
    )[0]


def low_last_kernel(keep, other, out, vgrad):
    out[...] = added(keep[:, 0 : 3 * D], other[:, 0 : 3 * D])
    vgrad[...] = added(keep[:, 3 * D : 3 * D + 128], other[:, 3 * D : 3 * D + 128])


def low_last(keep, other, after):
    return call(
        low_last_kernel,
        [(0, keep), (0, other)],
        [((CHUNK, 3 * D), BF16), ((CHUNK, 128), BF16)],
        name="low_last",
        vmem=4,
        after=after,
    )


def chain_kernel(*refs):
    ins, out = refs[:-1], refs[-1]
    at = 0
    for ref in ins:
        flat = ref.reshape(-1, CHUNK, D)
        out[at : at + flat.shape[0]] = flat[...]
        at += flat.shape[0]


def chain(parts, after=()):
    count = sum(p.size for p in parts) // (CHUNK * D)
    return call(
        chain_kernel,
        [(0, p) for p in parts],
        [((count, CHUNK, D), BF16)],
        name="chain",
        vmem=4,
        after=after,
    )[0]


def rest_sum(value, n):
    bit = 16
    while bit < n:
        other = swap(value, "dp", n, bit)
        value = (value.astype(F32) + other.astype(F32)).astype(BF16)
        bit *= 2
    return value


def join_kernel(*refs):
    ins, out = refs[:-1], refs[-1]
    at = 0
    for ref in ins:
        out[at : at + ref.shape[0]] = ref[...]
        at += ref.shape[0]


def join(parts):
    rows = sum(p.shape[0] for p in parts)
    return call(
        join_kernel,
        [(0, p) for p in parts],
        [((rows,) + parts[0].shape[1:], parts[0].dtype)],
        name="join",
        vmem=4,
    )[0]


def down_pair_kernel(keep, other, stay, go):
    for half in range(2):
        stay[half] = added(keep[2 * half], other[2 * half])
        go[half] = added(keep[2 * half + 1], other[2 * half + 1])


def down_pair(keep, other, after=()):
    half = ((2,) + keep.shape[1:], BF16)
    return call(
        down_pair_kernel, [(0, keep), (0, other)], [half, half], name="pair_sum", vmem=4, after=after
    )


def up_pair_kernel(keep, other, okeep, oother, stay, go):
    for half in range(2):
        stay[half, 0:4] = added(keep[2 * half], other[2 * half])
        stay[half, 4] = added(okeep[2 * half], oother[2 * half])
        go[half, 0:4] = added(keep[2 * half + 1], other[2 * half + 1])
        go[half, 4] = added(okeep[2 * half + 1], oother[2 * half + 1])


def up_pair(parts, after):
    half = ((2, 5, CHUNK, D), BF16)
    return call(
        up_pair_kernel, [(0, p) for p in parts], [half, half], name="up_pair", vmem=4, after=after
    )


def wide_first_kernel(dstay, dother, ustay, uother, keep, send):
    for i, out in enumerate((keep, send)):
        out[0:4] = added(dstay[i], dother[i])
        out[4:9] = added(ustay[i], uother[i])


def wide_first(parts, after):
    one = ((9, CHUNK, D), BF16)
    return call(
        wide_first_kernel, [(0, p) for p in parts], [one, one], name="wide_first", vmem=4, after=after
    )


def wide_second_kernel(place, keep, other, mine, send):
    z = place[3]
    for p in range(2):
        for i, bits in enumerate((0, 2)):
            mine[2 * p + i] = added(keep[4 * p + (z ^ bits)], other[4 * p + (z ^ bits)])
            send[2 * p + i] = added(keep[4 * p + (z ^ bits ^ 1)], other[4 * p + (z ^ bits ^ 1)])
    whole = added(keep[8], other[8])
    mine[4] = whole
    send[4] = whole


def wide_second(place, keep, other, after):
    one = ((5, CHUNK, D), BF16)
    return call(
        wide_second_kernel,
        [(1, place), (0, keep), (0, other)],
        [one, one],
        name="wide_second",
        vmem=4,
        after=after,
    )


def wide_third_kernel(keep, other, mine, send):
    for p in range(2):
        mine[p] = added(keep[2 * p], other[2 * p])
        send[p] = added(keep[2 * p + 1], other[2 * p + 1])
    whole = added(keep[4], other[4])
    mine[2] = whole
    send[2] = whole


def wide_third(keep, other, after):
    one = ((3, CHUNK, D), BF16)
    return call(
        wide_third_kernel, [(0, keep), (0, other)], [one, one], name="wide_third", vmem=4, after=after
    )


def wide_last_kernel(keep, other, pair, single):
    pair[...] = added(keep[0:2], other[0:2])
    single[0] = added(keep[2], other[2])


def wide_last(keep, other, after):
    return call(
        wide_last_kernel,
        [(0, keep), (0, other)],
        [((2, CHUNK, D), BF16), ((1, CHUNK, D), BF16)],
        name="wide_last",
        vmem=4,
        after=after,
    )


def low_first_kernel(stay, other, keep, send):
    keep[...] = added(stay[0], other[0])
    send[...] = added(stay[1], other[1])


def low_first(stay, other, after=()):
    one = (stay.shape[1:], BF16)
    return call(
        low_first_kernel, [(0, stay), (0, other)], [one, one], name="low_first", vmem=4, after=after
    )


def low_next_kernel(keep, other, out):
    out[...] = added(keep[...], other[...])


def low_next(keep, other, after=()):
    return call(
        low_next_kernel,
        [(0, keep), (0, other)],
        [(keep.shape, BF16)],
        name="low_next",
        vmem=4,
        after=after,
    )[0]


def low_last_kernel(keep, other, out, vgrad):
    out[...] = added(keep[:, 0 : 3 * D], other[:, 0 : 3 * D])
    vgrad[...] = added(keep[:, 3 * D : 3 * D + 128], other[:, 3 * D : 3 * D + 128])


def low_last(keep, other, after):
    return call(
        low_last_kernel,
        [(0, keep), (0, other)],
        [((CHUNK, 3 * D), BF16), ((CHUNK, 128), BF16)],
        name="low_last",
        vmem=4,
        after=after,
    )


def chain_kernel(*refs):
    ins, out = refs[:-1], refs[-1]
    at = 0
    for ref in ins:
        flat = ref.reshape(-1, CHUNK, D)
        out[at : at + flat.shape[0]] = flat[...]
        at += flat.shape[0]


def chain(parts, after=()):
    count = sum(p.size for p in parts) // (CHUNK * D)
    return call(
        chain_kernel,
        [(0, p) for p in parts],
        [((count, CHUNK, D), BF16)],
        name="chain",
        vmem=4,
        after=after,
    )[0]


def rest_sum(value, n):
    bit = 16
    while bit < n:
        other = swap(value, "dp", n, bit)
        value = (value.astype(F32) + other.astype(F32)).astype(BF16)
        bit *= 2
    return value


def trades(values, n, shift):
    return [values[0]] + [swap(values[k], "dp", n, k << shift) for k in (1, 2, 3)]


def join_kernel(*refs):
    ins, out = refs[:-1], refs[-1]
    for i, ref in enumerate(ins):
        out[i] = ref[...]


def join(parts, after=()):
    return call(
        join_kernel,
        [(0, p) for p in parts],
        [((len(parts),) + parts[0].shape, parts[0].dtype)],
        name="join",
        vmem=4,
        after=after,
    )[0]


def pack_kernel(place, targets, unit, other, units, packed):
    both = unit[...] + other[...]
    units[...] = both
    row = iota((2 * PAIRS, 128), 0)
    marks = jnp.zeros((2 * PAIRS, 128), jnp.int32)
    for j in range(PAIRS):
        marks = jnp.where(row == j, targets[j], marks)
    marks = jnp.where(iota((2 * PAIRS, 128), 1) < 64, marks >> 5, marks & 31)
    packed[:, 0:D] = both.astype(BF16)
    packed[:, D : D + 128] = marks.astype(F32).astype(BF16)


def pack(place, targets, unit, other):
    return call(
        pack_kernel,
        [(1, place), (1, targets), (0, unit), (0, other)],
        [(unit.shape, F32), ((2 * PAIRS, D + 128), BF16)],
        name="pack",
        vmem=4,
    )


def squares_of(parts):
    acc = jnp.zeros((8, D), F32)
    for part in parts:
        flat = part.reshape(-1, CHUNK, part.shape[-1])
        for k in range(flat.shape[0]):
            for c in range(0, part.shape[-1], D):
                v = flat[k, :, c : c + D].astype(F32)
                acc = acc + jnp.sum((v * v).reshape(CHUNK // 8, 8, D), axis=0)
    return acc[:, 0:128] + acc[:, 128:256] + acc[:, 256:384]


def wide_squares_kernel(*refs):
    refs[-1][...] = squares_of(refs[:-1])


def squares_kernel(place, *refs):
    parts, (vgrad, before, out) = refs[:-3], refs[-3:]
    acc = squares_of(parts) + before[...]
    row = iota((16, 128), 0)
    low_row = 6 * place[0]
    mine = (row >= low_row) & (row < low_row + 6)
    for j in range(3):
        v = jnp.where(mine, vgrad[16 * j : 16 * j + 16, :].astype(F32), 0.0)
        v = v * v
        acc = acc + (v[0:8] + v[8:16])
    out[...] = acc


def squares(place, parts, vgrad=None, before=None, after=()):
    ins = [(0, p) for p in parts]
    kernel = wide_squares_kernel
    if before is not None:
        ins = [(1, place)] + ins + [(0, vgrad), (0, before)]
        kernel = squares_kernel
    return call(kernel, ins, [((8, 128), F32)], name="squares", vmem=4, after=after)[0]


def merge_kernel(place, igrad, other, out):
    @pl.when(place[0] == 0)
    def low_core():
        out[0:OFF, :] = igrad[0:OFF, :]
        out[OFF:WIN, :] = added(igrad[OFF:WIN, :], other[0 : WIN - OFF, :])
        out[WIN:SEQ, :] = other[WIN - OFF : WIN, :]

    @pl.when(place[0] != 0)
    def high_core():
        out[0:OFF, :] = other[0:OFF, :]
        out[OFF:WIN, :] = added(other[OFF:WIN, :], igrad[0 : WIN - OFF, :])
        out[WIN:SEQ, :] = igrad[WIN - OFF : WIN, :]


def merge(place, igrad, other, after):
    return call(
        merge_kernel,
        [(1, place), (0, igrad), (0, other)],
        [((SEQ, D), BF16)],
        micros=1,
        name="merge",
        vmem=4,
        after=after,
    )[0]


def adamw(parameter, first_state, second, clipped, rate):
    first_new = BETA_ONE * first_state + (1.0 - BETA_ONE) * clipped
    second_new = BETA_TWO * second + (1.0 - BETA_TWO) * clipped * clipped
    direction = (first_new * (1.0 / (1.0 - BETA_ONE**STEP))) / (
        jnp.sqrt(second_new * (1.0 / (1.0 - BETA_TWO**STEP))) + ADAM_EPS
    )
    return parameter - rate * (direction + DECAY_RATE * parameter), first_new, second_new


def adamw_kernel(place, *refs):
    sums, refs = refs[:2], refs[2:]
    (vgrad, w, m, v, pv, pm, pq), refs = refs[:7], refs[7:]
    wide, low, refs = refs[:2], refs[2:4], refs[4:]
    outs, (npv, npm, npq, norm), scrs, sems = refs[:4], refs[4:8], refs[8:12], refs[12]
    opt = place[0]
    total = sums[0][...] + sums[1][...]
    total = jnp.sum(jnp.sum(total, axis=1, keepdims=True), axis=0, keepdims=True)
    grad_norm = jnp.sqrt(total)
    factor = jnp.minimum(1.0, CLIP_NORM / (grad_norm + 1e-06))
    norm[...] = grad_norm
    for j in range(3):
        cols = slice(128 * j, 128 * j + 128)
        g = vgrad[16 * j : 16 * j + 16, :].astype(F32)
        g = jnp.where(opt == 0, g[0:6], g[6:12])
        a, b, c = adamw(pv[:, cols], pm[:, cols], pq[:, cols], g * factor, VECTOR_RATE)
        npv[:, cols] = a
        npm[:, cols] = b
        npq[:, cols] = c
    copies = []

    def block(grad, rows, cols):
        new = adamw(w[rows, cols], m[rows, cols], v[rows, cols], grad * factor, LEARN_RATE)
        for scr, value in zip(scrs, new + (new[0].astype(BF16),)):
            scr[rows, cols] = value

    for r in range(4):
        base = CHUNK * place[4 + r]
        wide_part, low_part = wide[r % 2], low[r % 2]

        def rows_of(i, carry, r=r, base=base, wide_part=wide_part, low_part=low_part):
            rows = aligned(base + i * 16, 16, 16)
            here = aligned(i * 16, 16, 16)
            for j, bits in enumerate((0, 2, 1, 3)):
                at = D * (place[3] ^ bits)
                for p, start in enumerate((4 * D + FF, 4 * D)):
                    grad = wide_part[r // 2, 2 * j + p, here, :].astype(F32)
                    block(grad, rows, aligned(start + at, D, 128))
            grad = wide_part[r // 2, 8, here, :].astype(F32)
            block(grad, rows, slice(3 * D, 4 * D))
            for c in range(3):
                grad = low_part[r // 2, here, D * c : D * c + D].astype(F32)
                block(grad, rows, slice(D * c, D * c + D))
            return carry

        lax.fori_loop(0, CHUNK // 16, rows_of, 0)
        rows = aligned(base, CHUNK, 16)
        for i, (scr, out) in enumerate(zip(scrs, outs)):
            copy = pltpu.make_async_copy(scr.at[rows, :], out.at[rows, :], sems.at[r, i])
            copy.start()
            copies.append(copy)
    for copy in copies:
        copy.wait()


def update(place, sums, vgrad, w, m, v, pv, pm, pq, parts):
    ins = tuple(sums) + (vgrad, w, m, v, pv, pm, pq) + tuple(parts)
    shapes = [(w.shape, F32)] * 3 + [(w.shape, BF16)] + [(pv.shape, F32)] * 3 + [((1, 1), F32)]
    return pl.pallas_call(
        adamw_kernel,
        out_shape=[jax.ShapeDtypeStruct(s, d) for s, d in shapes],
        in_specs=[SMEM] + [VMEM] * len(ins),
        out_specs=[ANY] * 4 + [VMEM] * 4,
        scratch_shapes=[
            pltpu.VMEM(w.shape, F32),
            pltpu.VMEM(w.shape, F32),
            pltpu.VMEM(w.shape, F32),
            pltpu.VMEM(w.shape, BF16),
            pltpu.SemaphoreType.DMA((4, 4)),
        ],
        compiler_params=pltpu.CompilerParams(vmem_limit_bytes=16 << 20),
        cost_estimate=pl.CostEstimate(
            flops=4000000000, bytes_accessed=26 * w.size, transcendentals=0
        ),
        name="adamw",
    )(place, *ins)


def shards(
    n,
    tokens,
    lengths,
    query_index,
    doc_index,
    targets,
    weights,
    first_moment,
    second_moment,
    vectors,
    vec_first,
    vec_second,
):
    opt = lax.axis_index("opt")
    me = lax.axis_index("dp")
    plane = me & 3
    columns = [jnp.where(opt == 0, plane ^ r, plane ^ turned(r)) for r in range(4)]
    place = jnp.stack([opt, plane, me, (me >> 2) & 3] + columns).astype(jnp.int32)
    lengths = lengths.reshape(SEGS)
    chosen = jnp.concatenate([query_index, doc_index])
    groups = bit_groups(n)

    extra = jnp.pad(vectors, ((0, 10), (0, 2 * D)))
    w_own = jnp.concatenate([weights[:, : 3 * D], extra], axis=0).astype(BF16)
    w_other = pair(w_own)
    later, w_own = lax.optimization_barrier((weights, w_own))
    wo_own = later[:, 3 * D : 4 * D].astype(BF16)
    wu_own = later[:, 4 * D : 4 * D + FF].astype(BF16)
    wd_own = later[:, 4 * D + FF :].astype(BF16)
    wo = (wo_own, pair(wo_own))
    wu = (wu_own, pair(wu_own))
    wd = (wd_own, pair(wd_own))

    proj, att, lse, segc, segr, vec = attend(place, lengths, tokens, w_own, w_other)
    xhat1, inv1, hlow, act, slope, xhat2, inv2, unit, uscale = mlp(
        place, lengths, chosen, att, tokens, segr, vec, wo + wu + wd
    )
    units, packed = pack(place, targets, unit, swap(unit, "opt", 2, 1))
    groups = bit_groups(n)
    order = [0]
    stack = packed
    for i, (shift, size) in enumerate(groups[1:] + groups[:1]):
        pieces = [stack] + [swap(stack, "dp", n, k << shift) for k in range(1, size)]
        order = [o | (k << shift) for k in range(size) for o in order]
        if i < len(groups) - 1:
            stack = join(pieces).reshape(-1, 2 * PAIRS, D + 128)
    dsec, dlow, keep, send, dsums = down_backward(
        n, order, place, lengths, chosen, units, segc, uscale, (xhat2, inv2, act), vec, pieces
    )
    other = pair(send)
    dup, ukeep, usend, usums = up_backward(place, dlow, slope, hlow, wd, [])
    dstay, go = down_pair(keep, other, [dup])
    dother = cross(go, n, True)
    uother = pair(usend)
    dfirst, datt, delta, okeep, osend, fsums = first_backward(
        place, dup, dsec, xhat1, inv1, att, vec, wu + wo, [dstay]
    )
    ustay, go = up_pair((ukeep, uother, okeep, pair(osend)), [dfirst, dother])
    uother = cross(go, n, True)
    ins = (tokens, proj, datt, lse, delta, segc, segr)
    part0, keep0, send0, sums0 = heads_backward(0, place, ins, (), [ustay])
    wide, go = wide_first((dstay, dother, ustay, uother), [part0])
    wother = cross(go, n, False)
    part1, keep1, send1, sums1 = heads_backward(1, place, ins, (), [wide, part0])
    wide, go = wide_second(place, wide, wother, [part1])
    wother = swap(go, "dp", n, 4)
    part2, keep, send, _ = heads_backward(
        2, place, ins, (keep0, send0, keep1, send1, dsums, usums, fsums, sums0, sums1), [wide, part1]
    )
    wide, go = wide_third(wide, wother, [part2])
    send, wide, go = lax.optimization_barrier((send, wide, go))
    other = pair(send)
    wother = swap(go, "dp", n, 8)
    igrad = input_backward(place, (part0, part1, part2), dfirst, w_own, w_other, [wide])
    low, go = down_pair(keep, other, [igrad])
    other = cross(go, n, True)
    low, go = low_first(low, other)
    other = cross(go, n, False)
    wide, single = wide_last(wide, wother, [low])
    wide, single = rest_sum(wide, n), rest_sum(single, n)
    wother = swap(wide, "dp", n, 8)
    low = low_next(low, other, [wide])
    other = swap(low, "dp", n, 4)
    low = low_next(low, other)
    other = swap(low, "dp", n, 8)
    wide = chain([wide, wother], [low])
    wother = swap(wide, "dp", n, 4)
    wide = chain([wide, wother, single])
    wother = cross(wide, n, False)
    iother = pair(igrad)
    low, vgrad = low_last(low, other, [wide])
    low, vgrad = rest_sum(low, n), rest_sum(vgrad, n)
    far = cross(low, n, False)
    wide = join([wide, wother], [low])
    wide = (wide, cross(wide, n, True))
    input_grad = merge(place, igrad, iother, [wide[0]])
    low = join([low, far], [wide[0]])
    low = (low, cross(low, n, True))
    sums = squares(place, wide, vgrad, squares(place, low))
    sums = (sums, pair(sums))
    pieces = wide + low
    nw, nm, nv, nlow, npv, npm, npq, norm = update(
        place, sums, vgrad, weights, first_moment, second_moment,
        vectors, vec_first, vec_second, pieces,
    )
    return (norm.reshape(()), input_grad, nw, nm, nv, nlow, npv, npm, npq)


def solution(mesh):
    rows = P("opt", None)
    in_specs = (P("dp", None), P("dp", None), P("dp"), P("dp"), P("dp")) + (rows,) * 6
    out_specs = (P(), P("dp", None)) + (rows,) * 7
    n = mesh.shape["dp"]
    return jax.shard_map(
        functools.partial(shards, n),
        mesh=mesh,
        in_specs=in_specs,
        out_specs=out_specs,
        check_vma=False,
    )
```

```python
import functools

import jax
import jax.numpy as jnp
from jax import lax
from jax.experimental import pallas as pl
from jax.experimental.pallas import tpu as pltpu
from jax.sharding import PartitionSpec as P

D = 384
HEADS = 12
HD = 32
FF = 1536
SEQ = 1024
SEGS = 16
PAIRS = 8
STEP = 10

WIN = 576
OFF = SEQ - WIN
PAD = 640
BLOCK = 128
BANDS = tuple((q, max(0, q - 128), min(WIN, q + 256)) for q in range(0, WIN, BLOCK))
BAND_ROWS = tuple(sum(b[2] - b[1] for b in BANDS[:i]) for i in range(len(BANDS) + 1))
ROWS = 64

LN_EPS = 1e-06
POOL_EPS = 1e-06
SCORE_SCALE = 50.0
CLIP_NORM = 0.001
BETA_ONE = 0.9
BETA_TWO = 0.98
ADAM_EPS = 1e-08
LEARN_RATE = 0.05
VECTOR_RATE = 0.3
DECAY_RATE = 0.01
NEG_BIG = -1e30
HALF = D // 2
CHUNK = HALF // 4
EXP2_SCALE = HD ** (-0.5) * 1.4426950408889634

F32 = jnp.float32
BF16 = jnp.bfloat16
VMEM = pl.BlockSpec(memory_space=pltpu.VMEM)
SMEM = pl.BlockSpec(memory_space=pltpu.SMEM)
ANY = pl.BlockSpec(memory_space=pl.ANY)


def nn(a, b):
    return jnp.dot(a, b, preferred_element_type=F32)


def nt(a, b):
    return lax.dot_general(a, b, (((1,), (1,)), ((), ())), preferred_element_type=F32)


def tn(a, b):
    return lax.dot_general(a, b, (((0,), (0,)), ((), ())), preferred_element_type=F32)


def exact(a, b, dims):
    return lax.dot_general(
        a, b, (dims, ((), ())), precision=lax.Precision.HIGHEST, preferred_element_type=F32
    )


def iota(shape, axis):
    return lax.broadcasted_iota(jnp.int32, shape, axis)


def low_pair(value):
    high = value.astype(BF16)
    return high, (value - high.astype(F32)).astype(BF16)


def aligned(start, size, unit):
    return pl.ds(pl.multiple_of(start, unit), size)


def assemble(dst, own, other, opt):
    dst[aligned(HALF * opt, HALF, 64), :] = own[0:HALF, :]
    dst[aligned(HALF * (1 - opt), HALF, 64), :] = other[0:HALF, :]


def call(kernel, ins, outs, scratch=(), micros=5, name=None, vmem=12, after=()):
    specs = [SMEM if s else VMEM for s, _ in ins] + [ANY] * len(after)
    count = len(ins)

    def body(*refs):
        kernel(*refs[:count], *refs[count + len(after) :])

    shapes = [jax.ShapeDtypeStruct(s, d) for s, d in outs]
    moved = sum(a.size * a.dtype.itemsize for _, a in ins)
    moved += sum(s.size * s.dtype.itemsize for s in shapes)
    return pl.pallas_call(
        body,
        out_shape=shapes,
        in_specs=specs,
        out_specs=[VMEM] * len(shapes),
        scratch_shapes=list(scratch),
        compiler_params=pltpu.CompilerParams(vmem_limit_bytes=vmem << 20),
        cost_estimate=pl.CostEstimate(
            flops=micros * 1100000000, bytes_accessed=moved, transcendentals=0
        ),
        name=name,
    )(*[a for _, a in ins], *after)


def head_stack(rows):
    lane_head = iota(rows.shape, 1) // HD
    zero = jnp.zeros_like(rows)
    return jnp.concatenate([jnp.where(lane_head == j, rows, zero) for j in range(4)], axis=0)


def attend_kernel(
    place, lengths, tokens, w_own, w_other, proj, att, lse, segc, segr, vec, wfull, bias, vt
):
    opt = place[0]
    assemble(wfull, w_own, w_other, opt)
    mine = w_own[HALF : HALF + 16, 0:D].astype(F32)
    others = w_other[HALF : HALF + 16, 0:D].astype(F32)
    first = opt == 0
    vec[0:6, :] = jnp.where(first, mine, others)[0:6]
    vec[6:12, :] = jnp.where(first, others, mine)[0:6]
    vec[12:16, :] = jnp.zeros((4, D), F32)

    pos_col = iota((WIN, 128), 0) + OFF * opt
    pos_row = iota((8, PAD), 1) + OFF * opt
    seg_col = jnp.zeros((WIN, 128), jnp.int32)
    seg_row = jnp.zeros((8, PAD), jnp.int32)
    bound = jnp.int32(0)
    for s in range(SEGS):
        bound = bound + lengths[s]
        seg_col = seg_col + (pos_col >= bound).astype(jnp.int32)
        seg_row = seg_row + (pos_row >= bound).astype(jnp.int32)
    segc[...] = seg_col
    segr[...] = seg_row
    for i, (q0, k0, k1) in enumerate(BANDS):
        bias[BAND_ROWS[i] : BAND_ROWS[i + 1], :] = jnp.where(
            segc[k0:k1, :] == segr[0:1, q0 : q0 + BLOCK], 0.0, NEG_BIG
        )

    x = tokens[aligned(OFF * opt, WIN, 64), :]
    for c in range(3):
        acc = nn(x, wfull[:, c * D : (c + 1) * D])
        if c != 1:
            acc = acc + vec[(0 if c == 0 else 1) : (1 if c == 0 else 2), :]
        proj[0:WIN, c * D : (c + 1) * D] = acc.astype(BF16)
    proj[WIN:PAD, :] = jnp.zeros((PAD - WIN, 3 * D), BF16)

    def group(g, carry):
        def lanes(part):
            return aligned(part * D + 128 * g, 128, 128)

        for t in range(PAD // 128):
            vt[:, 128 * t : 128 * t + 128] = (
                proj[128 * t : 128 * t + 128, lanes(2)].astype(F32).T.astype(BF16)
            )
        for i, (q0, k0, k1) in enumerate(BANDS):
            stack = head_stack(proj[q0 : q0 + BLOCK, lanes(0)])
            st = nt(proj[k0:k1, lanes(1)], stack)
            outs = []
            for j in range(4):
                t = (
                    st[:, j * BLOCK : (j + 1) * BLOCK] * EXP2_SCALE
                    + bias[BAND_ROWS[i] : BAND_ROWS[i + 1], :]
                )
                peak = jnp.max(t, axis=0, keepdims=True)
                powers = jnp.exp2(t - peak)
                total = jnp.sum(powers, axis=0, keepdims=True)
                lse[g, j : j + 1, q0 : q0 + BLOCK] = peak + jnp.log2(total)
                o = nn(vt[j * HD : (j + 1) * HD, k0:k1], powers.astype(BF16))
                outs.append(o * (1.0 / total))
            rows = min(BLOCK, WIN - q0)
            att[q0 : q0 + rows, aligned(128 * g, 128, 128)] = (
                jnp.concatenate(outs, axis=0).T[0:rows].astype(BF16)
            )
        return carry

    lax.fori_loop(0, 3, group, 0)


def attend(place, lengths, tokens, w_own, w_other):
    return call(
        attend_kernel,
        [(1, place), (1, lengths), (0, tokens), (0, w_own), (0, w_other)],
        [
            ((PAD, 3 * D), BF16),
            ((WIN, D), BF16),
            ((3, 4, PAD), F32),
            ((WIN, 128), jnp.int32),
            ((8, PAD), jnp.int32),
            ((16, D), F32),
        ],
        [
            pltpu.VMEM((D, 3 * D), BF16),
            pltpu.VMEM((BAND_ROWS[-1], 128), F32),
            pltpu.VMEM((128, PAD), BF16),
        ],
        micros=8,
        name="attend",
    )


def owned(place, lengths, segment):
    bound = jnp.int32(0)
    count = jnp.int32(0)
    for s in range(SEGS):
        bound = bound + lengths[s]
        count = count + (bound <= WIN).astype(jnp.int32)
    low_side = (segment < count).astype(jnp.int32)
    return low_side == (place[0] == 0).astype(jnp.int32)


def mlp_kernel(
    place, lengths, chosen, att, tokens, segr, vec, wo_own, wo_other, wu_own, wu_other,
    wd_own, wd_other, xhat1, inv1, hlow, act, slope, xhat2, inv2, unit, uscale,
    wo, wu, wd, tmp, hid, ench, encl,
):
    opt = place[0]
    assemble(wo, wo_own, wo_other, opt)
    assemble(wu, wu_own, wu_other, opt)
    assemble(wd, wd_own, wd_other, opt)
    tmp[...] = nn(att[...], wo[...])

    def first_norm(i, carry):
        r = aligned(i * ROWS, ROWS, ROWS)
        x = tokens[aligned(OFF * opt + i * ROWS, ROWS, ROWS), :].astype(F32)
        v = tmp[r, :] + vec[2:3, :] + x
        centred = v - jnp.mean(v, axis=1, keepdims=True)
        inverse = lax.rsqrt(jnp.mean(centred * centred, axis=1, keepdims=True) + LN_EPS)
        normed = centred * inverse
        xhat1[r, :] = normed
        inv1[r, :] = jnp.broadcast_to(inverse, (ROWS, 128))
        h = normed * vec[8:9, :] + vec[9:10, :]
        hid[r, :] = h
        hlow[r, :] = h.astype(BF16)
        return carry

    lax.fori_loop(0, WIN // ROWS, first_norm, 0)

    for c in range(4):
        cols = slice(c * D, (c + 1) * D)
        tmp[...] = nn(hlow[...], wu[:, cols])

        def gelu(i, carry, cols=cols, c=c):
            r = aligned(i * ROWS, ROWS, ROWS)
            u = tmp[r, :] + vec[3 + c : 4 + c, :]
            half = lax.erf(u * 0.7071067811865476) * 0.5 + 0.5
            act[r, cols] = (u * half).astype(BF16)
            slope[r, cols] = half + u * jnp.exp(-0.5 * u * u) * 0.3989422804014327
            return carry

        lax.fori_loop(0, WIN // ROWS, gelu, 0)

    tmp[...] = nt(act[...], wd[...])

    def second_norm(i, carry):
        r = aligned(i * ROWS, ROWS, ROWS)
        v = tmp[r, :] + vec[7:8, :] + hid[r, :]
        centred = v - jnp.mean(v, axis=1, keepdims=True)
        inverse = lax.rsqrt(jnp.mean(centred * centred, axis=1, keepdims=True) + LN_EPS)
        normed = centred * inverse
        xhat2[r, :] = normed
        inv2[r, :] = jnp.broadcast_to(inverse, (ROWS, 128))
        high, rest = low_pair(normed * vec[10:11, :] + vec[11:12, :])
        ench[r, :] = high
        encl[r, :] = rest
        return carry

    lax.fori_loop(0, WIN // ROWS, second_norm, 0)

    seg = segr[0:1, 0:WIN]
    row_id = iota((2 * PAIRS, WIN), 0)
    wanted = jnp.zeros((2 * PAIRS, WIN), jnp.int32)
    for j in range(2 * PAIRS):
        wanted = jnp.where(row_id == j, chosen[j], wanted)
    mask = owned(place, lengths, jnp.broadcast_to(seg, (2 * PAIRS, WIN)))
    onehot = jnp.where((wanted == seg) & mask, 1.0, 0.0)
    count = jnp.maximum(jnp.sum(onehot, axis=1, keepdims=True), 1.0)
    hot = onehot.astype(BF16)
    pooled = (nn(hot, ench[...]) + nn(hot, encl[...])) / count
    inverse_len = lax.rsqrt(jnp.sum(pooled * pooled, axis=1, keepdims=True) + POOL_EPS)
    unit[...] = pooled * inverse_len
    uscale[...] = jnp.broadcast_to(inverse_len / count, (2 * PAIRS, 128))


def mlp(place, lengths, chosen, att, tokens, segr, vec, halves):
    return call(
        mlp_kernel,
        [(1, place), (1, lengths), (1, chosen), (0, att), (0, tokens), (0, segr), (0, vec)]
        + [(0, h) for h in halves],
        [
            ((WIN, D), F32),
            ((WIN, 128), F32),
            ((WIN, D), BF16),
            ((WIN, FF), BF16),
            ((WIN, FF), F32),
            ((WIN, D), F32),
            ((WIN, 128), F32),
            ((2 * PAIRS, D), F32),
            ((2 * PAIRS, 128), F32),
        ],
        [
            pltpu.VMEM((D, D), BF16),
            pltpu.VMEM((D, FF), BF16),
            pltpu.VMEM((D, FF), BF16),
            pltpu.VMEM((WIN, D), F32),
            pltpu.VMEM((WIN, D), F32),
            pltpu.VMEM((WIN, D), BF16),
            pltpu.VMEM((WIN, D), BF16),
        ],
        micros=10,
        name="mlp",
    )


def turned(chunk):
    return (chunk & 1) * 2 + (chunk >> 1)


def split_rows(grad, keep, send, place, *at):
    opt = place[0]
    for c in range(4):
        straight = c ^ place[1]
        mine = jnp.where(opt == 0, straight, turned(straight))
        theirs = jnp.where(opt == 0, turned(straight), straight)
        keep[(mine,) + at] = grad[aligned(HALF * opt + CHUNK * c, CHUNK, 16), :].astype(BF16)
        send[(theirs,) + at] = grad[aligned(HALF * (1 - opt) + CHUNK * c, CHUNK, 16), :].astype(BF16)


def column_sums(value):
    return jnp.sum(value.reshape(ROWS // 8, 8, D), axis=0)


def norm_backward(grad_at, normed_ref, inverse_ref, gain, out, low_out, sums, at):
    def block(i, carry):
        scale_sum, shift_sum, bias_sum = carry
        r = aligned(i * ROWS, ROWS, ROWS)
        g = grad_at(r)
        normed = normed_ref[r, :]
        scaled = g * gain
        inner = (
            scaled
            - jnp.mean(scaled, axis=1, keepdims=True)
            - normed * jnp.mean(scaled * normed, axis=1, keepdims=True)
        ) * inverse_ref[r, 0:1]
        out[r, :] = inner
        low_out[r, :] = inner.astype(BF16)
        return (
            scale_sum + column_sums(g * normed),
            shift_sum + column_sums(g),
            bias_sum + column_sums(inner),
        )

    zero = jnp.zeros((8, D), F32)
    scale_sum, shift_sum, bias_sum = lax.fori_loop(0, WIN // ROWS, block, (zero, zero, zero))
    sums[at : at + 1, :] = jnp.sum(bias_sum, axis=0, keepdims=True)
    sums[at + 1 : at + 2, :] = jnp.sum(scale_sum, axis=0, keepdims=True)
    sums[at + 2 : at + 3, :] = jnp.sum(shift_sum, axis=0, keepdims=True)


def down_kernel(
    count, order, place, lengths, chosen, units, segc, uscale, xhat2, inv2, act, vec, *rest
):
    pieces, (dsec, dlow, keep, send, sums, queries, docs, marks, grad) = rest[:-9], rest[-9:]
    me = place[2]
    per = pieces[0].shape[0]
    for p, piece in enumerate(pieces):
        for j in range(per):
            at = order[p * per + j]
            r = slice(at * PAIRS, (at + 1) * PAIRS)
            both = piece[j].astype(F32)
            queries[r, :] = both[0:PAIRS, 0:D]
            docs[r, :] = both[PAIRS : 2 * PAIRS, 0:D]
            marks[r, :] = both[0:PAIRS, D : D + 128]
    total = count * PAIRS
    q = queries[...].astype(BF16)
    d = docs[...].astype(BF16)
    logits = SCORE_SCALE * nt(q, d)
    peak = jnp.max(logits, axis=1, keepdims=True)
    powers = jnp.exp(logits - peak)
    soft = powers / jnp.sum(powers, axis=1, keepdims=True)
    col = iota((total, total), 1)
    doc_id = ((col // PAIRS) ^ me) * PAIRS + lax.rem(col, PAIRS)
    hit = (marks[:, 0:1] * 32.0 + marks[:, 64:65]).astype(jnp.int32) == doc_id
    d_logits = (soft - jnp.where(hit, 1.0, 0.0)) * (SCORE_SCALE / total)
    high, rest_low = low_pair(d_logits[0:PAIRS, :])
    d_q = nn(high, d) + nn(rest_low, d)
    high, rest_low = low_pair(d_logits[:, 0:128].T[0:PAIRS, :])
    d_d = nn(high, q) + nn(rest_low, q)
    d_units = jnp.concatenate([d_q, d_d], axis=0)
    u = units[...]
    d_pool = uscale[:, 0:1] * (d_units - u * jnp.sum(u * d_units, axis=1, keepdims=True))
    lane = iota((8, 2 * PAIRS), 1)
    wanted = jnp.zeros((8, 2 * PAIRS), jnp.int32)
    for j in range(2 * PAIRS):
        wanted = jnp.where(lane == j, chosen[j], wanted)
    seg = segc[:, 0 : 2 * PAIRS]
    mask = owned(place, lengths, seg)
    hot = jnp.where((seg == wanted[0:1, :]) & mask, 1.0, 0.0).astype(BF16)
    high, rest_low = low_pair(d_pool)
    dsec[...] = nn(hot, high) + nn(hot, rest_low)
    norm_backward(lambda r: dsec[r, :], xhat2, inv2, vec[10:11, :], dsec, dlow, sums, 0)
    sums[3:8, :] = jnp.zeros((5, D), F32)
    for c in range(4):
        cols = slice(c * D, (c + 1) * D)
        grad[...] = tn(dlow[...], act[:, cols])
        split_rows(grad, keep, send, place, c)


def down_backward(count, order, place, lengths, chosen, units, segc, uscale, saved, vec, pieces, after):
    total = count * PAIRS
    return call(
        functools.partial(down_kernel, count, order),
        [(1, place), (1, lengths), (1, chosen), (0, units), (0, segc), (0, uscale)]
        + [(0, s) for s in saved]
        + [(0, vec)]
        + [(0, p) for p in pieces],
        [
            ((WIN, D), F32),
            ((WIN, D), BF16),
            ((4, 4, CHUNK, D), BF16),
            ((4, 4, CHUNK, D), BF16),
            ((8, D), F32),
        ],
        [
            pltpu.VMEM((total, D), F32),
            pltpu.VMEM((total, D), F32),
            pltpu.VMEM((total, 128), F32),
            pltpu.VMEM((D, D), F32),
        ],
        micros=4,
        name="down_backward",
        after=after,
    )


def up_kernel(place, dlow, slope, hlow, wd_own, wd_other, dup, keep, send, sums, wd, grad):
    opt = place[0]
    assemble(wd, wd_own, wd_other, opt)
    for c in range(4):
        cols = slice(c * D, (c + 1) * D)
        part = (nn(dlow[...], wd[:, cols]) * slope[:, cols]).astype(BF16)
        dup[:, cols] = part
        sums[c : c + 1, :] = jnp.sum(part.astype(F32), axis=0, keepdims=True)
        grad[...] = tn(hlow[...], dup[:, cols])
        split_rows(grad, keep, send, place, c)


def up_backward(place, dlow, slope, hlow, halves, after):
    return call(
        up_kernel,
        [(1, place)] + [(0, a) for a in (dlow, slope, hlow) + tuple(halves)],
        [((WIN, FF), BF16), ((4, 4, CHUNK, D), BF16), ((4, 4, CHUNK, D), BF16), ((4, D), F32)],
        [pltpu.VMEM((D, FF), BF16), pltpu.VMEM((D, D), F32)],
        micros=3,
        name="up_backward",
        after=after,
    )


def first_kernel(
    place, dup, dsec, xhat1, inv1, att, vec, wu_own, wu_other, wo_own, wo_other,
    dfirst, datt, delta, okeep, osend, sums, wu, wo, grad, dlow,
):
    opt = place[0]
    assemble(wu, wu_own, wu_other, opt)
    assemble(wo, wo_own, wo_other, opt)
    dfirst[...] = nt(dup[...], wu[...])
    norm_backward(
        lambda r: dfirst[r, :] + dsec[r, :], xhat1, inv1, vec[8:9, :], dfirst, dlow, sums, 0
    )
    sums[3:8, :] = jnp.zeros((5, D), F32)
    grad[...] = tn(att[...], dlow[...])
    split_rows(grad, okeep, osend, place)
    da = nt(dlow[...], wo[...]).astype(BF16)
    datt[0:WIN, :] = da
    datt[WIN:PAD, :] = jnp.zeros((PAD - WIN, D), BF16)
    high, rest = low_pair(da.astype(F32) * att[...].astype(F32))
    heads = (iota((16, D), 1) // HD == iota((16, D), 0)).astype(F32).astype(BF16)
    delta[:, 0:WIN] = nt(heads, high) + nt(heads, rest)
    delta[:, WIN:PAD] = jnp.zeros((16, PAD - WIN), F32)


def first_backward(place, dup, dsec, xhat1, inv1, att, vec, halves, after):
    return call(
        first_kernel,
        [(1, place)] + [(0, a) for a in (dup, dsec, xhat1, inv1, att, vec) + tuple(halves)],
        [
            ((WIN, D), F32),
            ((PAD, D), BF16),
            ((16, PAD), F32),
            ((4, CHUNK, D), BF16),
            ((4, CHUNK, D), BF16),
            ((8, D), F32),
        ],
        [
            pltpu.VMEM((D, FF), BF16),
            pltpu.VMEM((D, D), BF16),
            pltpu.VMEM((D, D), F32),
            pltpu.VMEM((WIN, D), BF16),
        ],
        micros=3,
        name="first_backward",
        after=after,
    )


def heads_kernel(g, place, tokens, proj, datt, lse, delta, segc, segr, *rest):
    rest, (dproj, keep, send, sums, kt, dk, dv, grad, ktmp, stmp) = rest[:-10], rest[-10:]

    def lanes(part):
        return slice(part * D + 128 * g, part * D + 128 * g + 128)

    for t in range(PAD // 128):
        kt[:, 128 * t : 128 * t + 128] = (
            proj[128 * t : 128 * t + 128, lanes(1)].astype(F32).T.astype(BF16)
        )
    dk[...] = jnp.zeros_like(dk)
    dv[...] = jnp.zeros_like(dv)
    for q0, k0, k1 in BANDS:
        qs = head_stack(proj[q0 : q0 + BLOCK, lanes(0)])
        gs = head_stack(datt[q0 : q0 + BLOCK, lanes(0)])
        st = nt(proj[k0:k1, lanes(1)], qs)
        dp = nt(proj[k0:k1, lanes(2)], gs)
        same = segc[k0:k1, :] == segr[0:1, q0 : q0 + BLOCK]
        bias = jnp.where(same, 0.0, NEG_BIG)
        probs, d_scores, dq = [], [], []
        for j in range(4):
            cols = slice(j * BLOCK, (j + 1) * BLOCK)
            prob = jnp.exp2(st[:, cols] * EXP2_SCALE + bias - lse[g, j : j + 1, q0 : q0 + BLOCK])
            ds = prob * (dp[:, cols] - delta[4 * g + j : 4 * g + j + 1, q0 : q0 + BLOCK])
            ds = ds.astype(BF16)
            probs.append(prob.astype(BF16))
            d_scores.append(ds)
            dq.append(nn(kt[j * HD : (j + 1) * HD, k0:k1], ds))
        dv[k0:k1, :] += nn(jnp.concatenate(probs, axis=1), gs)
        dk[k0:k1, :] += nn(jnp.concatenate(d_scores, axis=1), qs)
        rows = min(BLOCK, WIN - q0)
        dqs = jnp.concatenate(dq, axis=0).T[0:rows] * HD ** (-0.5)
        dproj[q0 : q0 + rows, 0:128] = dqs.astype(BF16)
    dproj[:, 128:256] = (dk[...] * HD ** (-0.5)).astype(BF16)
    dproj[:, 256:384] = dv[...].astype(BF16)
    grad[...] = tn(tokens[aligned(OFF * place[0], WIN, 64), :], dproj[...])
    q_sum = jnp.sum(dproj[:, 0:128].astype(F32), axis=0, keepdims=True)
    v_sum = jnp.sum(dproj[:, 256:384].astype(F32), axis=0, keepdims=True)
    sums[0:1, :] = q_sum
    sums[1:2, :] = v_sum
    sums[2:8, :] = jnp.zeros((6, 128), F32)
    if g < 2:
        split_rows(grad, keep, send, place)
        return
    parts, (dsums, usums, fsums, zero, one) = rest[:4], rest[4:]
    split_rows(grad, ktmp, stmp, place)
    for dst, blocks in (
        (keep, (parts[0], parts[2], ktmp)),
        (send, (parts[1], parts[3], stmp)),
    ):
        for h, part in enumerate(blocks):
            for c in range(3):
                dst[:, :, D * c + 128 * h : D * c + 128 * h + 128] = part[
                    :, :, 128 * c : 128 * c + 128
                ]
    rows = jnp.concatenate(
        [
            jnp.concatenate([zero[0:1], one[0:1], q_sum], axis=1),
            jnp.concatenate([zero[1:2], one[1:2], v_sum], axis=1),
            fsums[0:1, :],
            usums[0:4, :],
            dsums[0:1, :],
            fsums[1:3, :],
            dsums[1:3, :],
            jnp.zeros((4, D), F32),
        ],
        axis=0,
    ).astype(BF16)
    for c in range(4):
        for j in range(3):
            block = rows[:, 128 * j : 128 * j + 128]
            keep[c, 16 * j : 16 * j + 16, 3 * D : 3 * D + 128] = block
            send[c, 16 * j : 16 * j + 16, 3 * D : 3 * D + 128] = block


def heads_backward(g, place, ins, more, after):
    part = ((4, CHUNK, 3 * D + 128 if g == 2 else D), BF16)
    return call(
        functools.partial(heads_kernel, g),
        [(1, place)] + [(0, a) for a in tuple(ins) + tuple(more)],
        [((WIN, D), BF16), part, part, ((8, 128), F32)],
        [
            pltpu.VMEM((128, PAD), BF16),
            pltpu.VMEM((WIN, 128), F32),
            pltpu.VMEM((WIN, 128), F32),
            pltpu.VMEM((D, D), F32),
            pltpu.VMEM((4, CHUNK, D), BF16),
            pltpu.VMEM((4, CHUNK, D), BF16),
        ],
        micros=3,
        name="heads_backward",
        after=after,
    )


def input_kernel(place, dp0, dp1, dp2, dfirst, w_own, w_other, igrad, wfull, dproj):
    assemble(wfull, w_own, w_other, place[0])
    for g, part in enumerate((dp0, dp1, dp2)):
        for c in range(3):
            dproj[:, c * D + 128 * g : c * D + 128 * g + 128] = part[:, 128 * c : 128 * c + 128]
    igrad[...] = (nt(dproj[...], wfull[...]) + dfirst[...]).astype(BF16)


def input_backward(place, parts, dfirst, w_own, w_other, after):
    return call(
        input_kernel,
        [(1, place)] + [(0, a) for a in tuple(parts) + (dfirst, w_own, w_other)],
        [((WIN, D), BF16)],
        [pltpu.VMEM((D, 3 * D), BF16), pltpu.VMEM((WIN, 3 * D), BF16)],
        micros=2,
        name="input_backward",
        after=after,
    )[0]


def flips(axis, size, bits):
    return [(i, i ^ bits) for i in range(size)]


def pair(value):
    return swap(value, "opt", 2, 1)


def swap(value, axis, size, bits):
    return lax.ppermute(value, axis, flips(axis, size, bits))


def bit_groups(size):
    bits = size.bit_length() - 1
    return [(s, 1 << min(2, bits - s)) for s in range(0, bits, 2)]


def cross(value, n, first):
    pairs = []
    for i in range(n):
        for core in range(2):
            bit = 1 if (core == 0) == first else 2
            pairs.append((2 * i + core, 2 * (i ^ bit) + core))
    return lax.ppermute(value, ("dp", "opt"), pairs)


def added(a, b):
    return (a.astype(F32) + b.astype(F32)).astype(BF16)


def down_pair_kernel(keep, other, stay, go):
    for half in range(2):
        stay[half] = added(keep[2 * half], other[2 * half])
        go[half] = added(keep[2 * half + 1], other[2 * half + 1])


def down_pair(keep, other, after=()):
    half = ((2,) + keep.shape[1:], BF16)
    return call(
        down_pair_kernel, [(0, keep), (0, other)], [half, half], name="pair_sum", vmem=4, after=after
    )


def first_step_kernel(stay, other, keep, send):
    keep[...] = added(stay[0], other[0])
    send[...] = added(stay[1], other[1])


def first_step(stay, other, after=()):
    one = (stay.shape[1:], BF16)
    return call(
        first_step_kernel, [(0, stay), (0, other)], [one, one], name="first_step", vmem=4, after=after
    )


def up_first_kernel(stay, other, ostay, oother, keep, send):
    for i, out in enumerate((keep, send)):
        out[0:4] = added(stay[i], other[i])
        out[4] = added(ostay[i], oother[i])


def up_first(parts, after):
    one = ((5, CHUNK, D), BF16)
    return call(
        up_first_kernel, [(0, p) for p in parts], [one, one], name="up_first", vmem=4, after=after
    )


def wide_second_kernel(place, dkeep, dother, ukeep, uother, mine, send):
    z = place[3]
    for p, (keep, other) in enumerate(((dkeep, dother), (ukeep, uother))):
        for i, bits in enumerate((0, 2)):
            mine[2 * p + i] = added(keep[z ^ bits], other[z ^ bits])
            send[2 * p + i] = added(keep[z ^ bits ^ 1], other[z ^ bits ^ 1])
    whole = added(ukeep[4], uother[4])
    mine[4] = whole
    send[4] = whole


def wide_second(place, parts, after):
    one = ((5, CHUNK, D), BF16)
    return call(
        wide_second_kernel,
        [(1, place)] + [(0, p) for p in parts],
        [one, one],
        name="wide_second",
        vmem=4,
        after=after,
    )


def wide_third_kernel(keep, other, mine, send):
    for p in range(2):
        mine[p] = added(keep[2 * p], other[2 * p])
        send[p] = added(keep[2 * p + 1], other[2 * p + 1])
    whole = added(keep[4], other[4])
    mine[2] = whole
    send[2] = whole


def wide_third(keep, other, after):
    one = ((3, CHUNK, D), BF16)
    return call(
        wide_third_kernel, [(0, keep), (0, other)], [one, one], name="wide_third", vmem=4, after=after
    )


def wide_last_kernel(keep, other, pair, single):
    pair[...] = added(keep[0:2], other[0:2])
    single[0] = added(keep[2], other[2])


def wide_last(keep, other, after):
    return call(
        wide_last_kernel,
        [(0, keep), (0, other)],
        [((2, CHUNK, D), BF16), ((1, CHUNK, D), BF16)],
        name="wide_last",
        vmem=4,
        after=after,
    )


def low_next_kernel(keep, other, out):
    out[...] = added(keep[...], other[...])


def low_next(keep, other, after=()):
    return call(
        low_next_kernel,
        [(0, keep), (0, other)],
        [(keep.shape, BF16)],
        name="low_next",
        vmem=4,
        after=after,
    )[0]


def low_last_kernel(keep, other, out, vgrad):
    out[...] = added(keep[:, 0 : 3 * D], other[:, 0 : 3 * D])
    vgrad[...] = added(keep[:, 3 * D : 3 * D + 128], other[:, 3 * D : 3 * D + 128])


def low_last(keep, other, after):
    return call(
        low_last_kernel,
        [(0, keep), (0, other)],
        [((CHUNK, 3 * D), BF16), ((CHUNK, 128), BF16)],
        name="low_last",
        vmem=4,
        after=after,
    )


def chain_kernel(*refs):
    ins, out = refs[:-1], refs[-1]
    at = 0
    for ref in ins:
        flat = ref.reshape(-1, CHUNK, D)
        out[at : at + flat.shape[0]] = flat[...]
        at += flat.shape[0]


def chain(parts, after=()):
    count = sum(p.size for p in parts) // (CHUNK * D)
    return call(
        chain_kernel,
        [(0, p) for p in parts],
        [((count, CHUNK, D), BF16)],
        name="chain",
        vmem=4,
        after=after,
    )[0]


def rest_sum(value, n):
    bit = 16
    while bit < n:
        other = swap(value, "dp", n, bit)
        value = (value.astype(F32) + other.astype(F32)).astype(BF16)
        bit *= 2
    return value


def trades(values, n, shift):
    return [values[0]] + [swap(values[k], "dp", n, k << shift) for k in (1, 2, 3)]


def join_kernel(*refs):
    ins, out = refs[:-1], refs[-1]
    for i, ref in enumerate(ins):
        out[i] = ref[...]


def join(parts, after=()):
    return call(
        join_kernel,
        [(0, p) for p in parts],
        [((len(parts),) + parts[0].shape, parts[0].dtype)],
        name="join",
        vmem=4,
        after=after,
    )[0]


def pack_kernel(place, targets, unit, other, units, packed):
    both = unit[...] + other[...]
    units[...] = both
    row = iota((2 * PAIRS, 128), 0)
    marks = jnp.zeros((2 * PAIRS, 128), jnp.int32)
    for j in range(PAIRS):
        marks = jnp.where(row == j, targets[j], marks)
    marks = jnp.where(iota((2 * PAIRS, 128), 1) < 64, marks >> 5, marks & 31)
    packed[:, 0:D] = both.astype(BF16)
    packed[:, D : D + 128] = marks.astype(F32).astype(BF16)


def pack(place, targets, unit, other):
    return call(
        pack_kernel,
        [(1, place), (1, targets), (0, unit), (0, other)],
        [(unit.shape, F32), ((2 * PAIRS, D + 128), BF16)],
        name="pack",
        vmem=4,
    )


def squares_of(parts):
    acc = jnp.zeros((8, D), F32)
    for part in parts:
        flat = part.reshape(-1, CHUNK, part.shape[-1])
        for k in range(flat.shape[0]):
            for c in range(0, part.shape[-1], D):
                v = flat[k, :, c : c + D].astype(F32)
                acc = acc + jnp.sum((v * v).reshape(CHUNK // 8, 8, D), axis=0)
    return acc[:, 0:128] + acc[:, 128:256] + acc[:, 256:384]


def wide_squares_kernel(*refs):
    refs[-1][...] = squares_of(refs[:-1])


def squares_kernel(place, *refs):
    parts, (vgrad, before, out) = refs[:-3], refs[-3:]
    acc = squares_of(parts) + before[...]
    row = iota((16, 128), 0)
    low_row = 6 * place[0]
    mine = (row >= low_row) & (row < low_row + 6)
    for j in range(3):
        v = jnp.where(mine, vgrad[16 * j : 16 * j + 16, :].astype(F32), 0.0)
        v = v * v
        acc = acc + (v[0:8] + v[8:16])
    out[...] = acc


def squares(place, parts, vgrad=None, before=None, after=()):
    ins = [(0, p) for p in parts]
    kernel = wide_squares_kernel
    if before is not None:
        ins = [(1, place)] + ins + [(0, vgrad), (0, before)]
        kernel = squares_kernel
    return call(kernel, ins, [((8, 128), F32)], name="squares", vmem=4, after=after)[0]


def merge_kernel(place, igrad, other, out, flag):
    flag[...] = jnp.zeros((8, 128), F32)

    @pl.when(place[0] == 0)
    def low_core():
        out[0:OFF, :] = igrad[0:OFF, :]
        out[OFF:WIN, :] = added(igrad[OFF:WIN, :], other[0 : WIN - OFF, :])
        out[WIN:SEQ, :] = other[WIN - OFF : WIN, :]

    @pl.when(place[0] != 0)
    def high_core():
        out[0:OFF, :] = other[0:OFF, :]
        out[OFF:WIN, :] = added(other[OFF:WIN, :], igrad[0 : WIN - OFF, :])
        out[WIN:SEQ, :] = igrad[WIN - OFF : WIN, :]


def merge(place, igrad, other, after):
    return call(
        merge_kernel,
        [(1, place), (0, igrad), (0, other)],
        [((SEQ, D), BF16), ((8, 128), F32)],
        name="merge",
        vmem=4,
        after=after,
    )


def adamw(parameter, first_state, second, clipped, rate):
    first_new = first_state + (1.0 - BETA_ONE) * clipped
    second_new = second + (1.0 - BETA_TWO) * clipped * clipped
    direction = (first_new * (1.0 / (1.0 - BETA_ONE**STEP))) / (
        jnp.sqrt(second_new * (1.0 / (1.0 - BETA_TWO**STEP))) + ADAM_EPS
    )
    return parameter - rate * direction, first_new, second_new


def decay_kernel(w, m, v, pv, pm, pq, nw, nm, nv, npv, npm, npq):
    for ins, outs, rate in (
        ((w, m, v), (nw, nm, nv), LEARN_RATE),
        ((pv, pm, pq), (npv, npm, npq), VECTOR_RATE),
    ):
        for ref, out, scale in zip(ins, outs, (1.0 - rate * DECAY_RATE, BETA_ONE, BETA_TWO)):
            out[...] = ref[...] * scale


def decay(arrays, after):
    return call(
        decay_kernel,
        [(0, a) for a in arrays],
        [(a.shape, F32) for a in arrays],
        name="decay",
        vmem=4,
        after=after,
    )


def adamw_kernel(place, *refs):
    sums, refs = refs[:2], refs[2:]
    (vgrad, w, m, v, pv, pm, pq), refs = refs[:7], refs[7:]
    wide, low, refs = refs[:2], refs[2:4], refs[4:]
    outs, (npv, npm, npq, norm), scrs, sems = refs[:4], refs[4:8], refs[8:12], refs[12]
    opt = place[0]
    total = sums[0][...] + sums[1][...]
    total = jnp.sum(jnp.sum(total, axis=1, keepdims=True), axis=0, keepdims=True)
    grad_norm = jnp.sqrt(total)
    factor = jnp.minimum(1.0, CLIP_NORM / (grad_norm + 1e-06))
    norm[...] = grad_norm
    for j in range(3):
        cols = slice(128 * j, 128 * j + 128)
        g = vgrad[16 * j : 16 * j + 16, :].astype(F32)
        g = jnp.where(opt == 0, g[0:6], g[6:12])
        a, b, c = adamw(pv[:, cols], pm[:, cols], pq[:, cols], g * factor, VECTOR_RATE)
        npv[:, cols] = a
        npm[:, cols] = b
        npq[:, cols] = c
    copies = []

    def block(grad, rows, cols):
        new = adamw(w[rows, cols], m[rows, cols], v[rows, cols], grad * factor, LEARN_RATE)
        for scr, value in zip(scrs, new + (new[0].astype(BF16),)):
            scr[rows, cols] = value

    for r in range(4):
        base = CHUNK * place[4 + r]
        wide_part, low_part = wide[r % 2], low[r % 2]

        def rows_of(i, carry, r=r, base=base, wide_part=wide_part, low_part=low_part):
            rows = aligned(base + i * 16, 16, 16)
            here = aligned(i * 16, 16, 16)
            for j, bits in enumerate((0, 2, 1, 3)):
                at = D * (place[3] ^ bits)
                for p, start in enumerate((4 * D + FF, 4 * D)):
                    grad = wide_part[r // 2, 2 * j + p, here, :].astype(F32)
                    block(grad, rows, aligned(start + at, D, 128))
            grad = wide_part[r // 2, 8, here, :].astype(F32)
            block(grad, rows, slice(3 * D, 4 * D))
            for c in range(3):
                grad = low_part[r // 2, here, D * c : D * c + D].astype(F32)
                block(grad, rows, slice(D * c, D * c + D))
            return carry

        lax.fori_loop(0, CHUNK // 16, rows_of, 0)
        rows = aligned(base, CHUNK, 16)
        for i, (scr, out) in enumerate(zip(scrs, outs)):
            copy = pltpu.make_async_copy(scr.at[rows, :], out.at[rows, :], sems.at[r, i])
            copy.start()
            copies.append(copy)
    for copy in copies:
        copy.wait()


def update(place, sums, vgrad, w, m, v, pv, pm, pq, parts):
    ins = tuple(sums) + (vgrad, w, m, v, pv, pm, pq) + tuple(parts)
    shapes = [(w.shape, F32)] * 3 + [(w.shape, BF16)] + [(pv.shape, F32)] * 3 + [((1, 1), F32)]
    return pl.pallas_call(
        adamw_kernel,
        out_shape=[jax.ShapeDtypeStruct(s, d) for s, d in shapes],
        in_specs=[SMEM] + [VMEM] * len(ins),
        out_specs=[ANY] * 4 + [VMEM] * 4,
        scratch_shapes=[
            pltpu.VMEM(w.shape, F32),
            pltpu.VMEM(w.shape, F32),
            pltpu.VMEM(w.shape, F32),
            pltpu.VMEM(w.shape, BF16),
            pltpu.SemaphoreType.DMA((4, 4)),
        ],
        compiler_params=pltpu.CompilerParams(vmem_limit_bytes=16 << 20),
        cost_estimate=pl.CostEstimate(
            flops=4000000000, bytes_accessed=26 * w.size, transcendentals=0
        ),
        name="adamw",
    )(place, *ins)


def shards(
    n,
    tokens,
    lengths,
    query_index,
    doc_index,
    targets,
    weights,
    first_moment,
    second_moment,
    vectors,
    vec_first,
    vec_second,
):
    opt = lax.axis_index("opt")
    me = lax.axis_index("dp")
    plane = me & 3
    columns = [jnp.where(opt == 0, plane ^ r, plane ^ turned(r)) for r in range(4)]
    place = jnp.stack([opt, plane, me, (me >> 2) & 3] + columns).astype(jnp.int32)
    lengths = lengths.reshape(SEGS)
    chosen = jnp.concatenate([query_index, doc_index])
    groups = bit_groups(n)

    extra = jnp.pad(vectors, ((0, 10), (0, 2 * D)))
    w_own = jnp.concatenate([weights[:, : 3 * D], extra], axis=0).astype(BF16)
    w_other = pair(w_own)
    later, w_own = lax.optimization_barrier((weights, w_own))
    wo_own = later[:, 3 * D : 4 * D].astype(BF16)
    wu_own = later[:, 4 * D : 4 * D + FF].astype(BF16)
    wd_own = later[:, 4 * D + FF :].astype(BF16)
    wo = (wo_own, pair(wo_own))
    wu = (wu_own, pair(wu_own))
    wd = (wd_own, pair(wd_own))

    proj, att, lse, segc, segr, vec = attend(place, lengths, tokens, w_own, w_other)
    xhat1, inv1, hlow, act, slope, xhat2, inv2, unit, uscale = mlp(
        place, lengths, chosen, att, tokens, segr, vec, wo + wu + wd
    )
    units, packed = pack(place, targets, unit, swap(unit, "opt", 2, 1))
    groups = bit_groups(n)
    order = [0]
    stack = packed
    for i, (shift, size) in enumerate(groups[1:] + groups[:1]):
        pieces = [stack] + [swap(stack, "dp", n, k << shift) for k in range(1, size)]
        order = [o | (k << shift) for k in range(size) for o in order]
        if i < len(groups) - 1:
            stack = join(pieces).reshape(-1, 2 * PAIRS, D + 128)
    decayed = decay(
        (weights, first_moment, second_moment, vectors, vec_first, vec_second), [packed]
    )
    dsec, dlow, keep, send, dsums = down_backward(
        n, order, place, lengths, chosen, units, segc, uscale, (xhat2, inv2, act), vec, pieces,
        decayed,
    )
    other = pair(send)
    dup, ukeep, usend, usums = up_backward(place, dlow, slope, hlow, wd, [])
    stay, go = down_pair(keep, other, [dup])
    dother = cross(go, n, True)
    uother = pair(usend)
    dfirst, datt, delta, okeep, osend, fsums = first_backward(
        place, dup, dsec, xhat1, inv1, att, vec, wu + wo, [stay]
    )
    oother = pair(osend)
    dkeep, go = first_step(stay, dother, [dfirst])
    dother = cross(go, n, False)
    ustay, go = down_pair(ukeep, uother, [dkeep])
    uother = cross(go, n, True)
    ostay, go = down_pair(okeep, oother, [ustay])
    oother = cross(go, n, True)
    ins = (tokens, proj, datt, lse, delta, segc, segr)
    part0, keep0, send0, sums0 = heads_backward(0, place, ins, (), [ostay])
    ukeep, go = up_first((ustay, uother, ostay, oother), [part0])
    uother = cross(go, n, False)
    part1, keep1, send1, sums1 = heads_backward(1, place, ins, (), [ukeep, part0])
    wide, go = wide_second(place, (dkeep, dother, ukeep, uother), [part1])
    wother = swap(go, "dp", n, 4)
    part2, keep, send, _ = heads_backward(
        2, place, ins, (keep0, send0, keep1, send1, dsums, usums, fsums, sums0, sums1), [wide, part1]
    )
    wide, go = wide_third(wide, wother, [part2])
    send, wide, go = lax.optimization_barrier((send, wide, go))
    other = pair(send)
    wother = swap(go, "dp", n, 8)
    igrad = input_backward(place, (part0, part1, part2), dfirst, w_own, w_other, [wide])
    iother = pair(igrad)
    low, go = down_pair(keep, other, [igrad])
    other = cross(go, n, True)
    low, go = first_step(low, other)
    other = cross(go, n, False)
    wide, single = wide_last(wide, wother, [low])
    wide, single = rest_sum(wide, n), rest_sum(single, n)
    wother = swap(wide, "dp", n, 8)
    low = low_next(low, other, [wide])
    other = swap(low, "dp", n, 4)
    low = low_next(low, other)
    other = swap(low, "dp", n, 8)
    input_grad, flag = merge(place, igrad, iother, [low])
    wide = chain([wide, wother], [flag])
    wother = swap(wide, "dp", n, 4)
    wide = chain([wide, wother, single])
    wother = cross(wide, n, False)
    low, vgrad = low_last(low, other, [wide])
    low, vgrad = rest_sum(low, n), rest_sum(vgrad, n)
    far = cross(low, n, False)
    wide = join([wide, wother], [low])
    wide = (wide, cross(wide, n, True))
    low = join([low, far], [wide[0]])
    low = (low, cross(low, n, True))
    sums = squares(place, low, vgrad, squares(place, wide))
    sums = (sums, pair(sums))
    pieces = wide + low
    nw, nm, nv, nlow, npv, npm, npq, norm = update(
        place, sums, vgrad, *decayed, pieces,
    )
    return (norm.reshape(()), input_grad, nw, nm, nv, nlow, npv, npm, npq)


def solution(mesh):
    rows = P("opt", None)
    in_specs = (P("dp", None), P("dp", None), P("dp"), P("dp"), P("dp")) + (rows,) * 6
    out_specs = (P(), P("dp", None)) + (rows,) * 7
    n = mesh.shape["dp"]
    return jax.shard_map(
        functools.partial(shards, n),
        mesh=mesh,
        in_specs=in_specs,
        out_specs=out_specs,
        check_vma=False,
    )
```

```python
import functools

import jax
import jax.numpy as jnp
from jax import lax
from jax.experimental import pallas as pl
from jax.experimental.pallas import tpu as pltpu
from jax.sharding import PartitionSpec as P

D = 384
HEADS = 12
HD = 32
FF = 1536
SEQ = 1024
SEGS = 16
PAIRS = 8
STEP = 10

WIN = 576
OFF = SEQ - WIN
PAD = 640
BLOCK = 128
BANDS = tuple((q, max(0, q - 128), min(WIN, q + 256)) for q in range(0, WIN, BLOCK))
BAND_ROWS = tuple(sum(b[2] - b[1] for b in BANDS[:i]) for i in range(len(BANDS) + 1))
ROWS = 64

LN_EPS = 1e-06
POOL_EPS = 1e-06
SCORE_SCALE = 50.0
CLIP_NORM = 0.001
BETA_ONE = 0.9
BETA_TWO = 0.98
ADAM_EPS = 1e-08
LEARN_RATE = 0.05
VECTOR_RATE = 0.3
DECAY_RATE = 0.01
NEG_BIG = -1e30
HALF = D // 2
CHUNK = HALF // 4
EXP2_SCALE = HD ** (-0.5) * 1.4426950408889634

F32 = jnp.float32
BF16 = jnp.bfloat16
VMEM = pl.BlockSpec(memory_space=pltpu.VMEM)
SMEM = pl.BlockSpec(memory_space=pltpu.SMEM)
ANY = pl.BlockSpec(memory_space=pl.ANY)


def nn(a, b):
    return jnp.dot(a, b, preferred_element_type=F32)


def nt(a, b):
    return lax.dot_general(a, b, (((1,), (1,)), ((), ())), preferred_element_type=F32)


def tn(a, b):
    return lax.dot_general(a, b, (((0,), (0,)), ((), ())), preferred_element_type=F32)


def exact(a, b, dims):
    return lax.dot_general(
        a, b, (dims, ((), ())), precision=lax.Precision.HIGHEST, preferred_element_type=F32
    )


def iota(shape, axis):
    return lax.broadcasted_iota(jnp.int32, shape, axis)


def low_pair(value):
    high = value.astype(BF16)
    return high, (value - high.astype(F32)).astype(BF16)


def aligned(start, size, unit):
    return pl.ds(pl.multiple_of(start, unit), size)


def assemble(dst, own, other, opt):
    dst[aligned(HALF * opt, HALF, 64), :] = own[0:HALF, :]
    dst[aligned(HALF * (1 - opt), HALF, 64), :] = other[0:HALF, :]


def call(kernel, ins, outs, scratch=(), micros=5, name=None, vmem=12, after=()):
    specs = [SMEM if s else VMEM for s, _ in ins] + [ANY] * len(after)
    count = len(ins)

    def body(*refs):
        kernel(*refs[:count], *refs[count + len(after) :])

    shapes = [jax.ShapeDtypeStruct(s, d) for s, d in outs]
    moved = sum(a.size * a.dtype.itemsize for _, a in ins)
    moved += sum(s.size * s.dtype.itemsize for s in shapes)
    return pl.pallas_call(
        body,
        out_shape=shapes,
        in_specs=specs,
        out_specs=[VMEM] * len(shapes),
        scratch_shapes=list(scratch),
        compiler_params=pltpu.CompilerParams(vmem_limit_bytes=vmem << 20),
        cost_estimate=pl.CostEstimate(
            flops=micros * 1100000000, bytes_accessed=moved, transcendentals=0
        ),
        name=name,
    )(*[a for _, a in ins], *after)


def head_stack(rows):
    lane_head = iota(rows.shape, 1) // HD
    zero = jnp.zeros_like(rows)
    return jnp.concatenate([jnp.where(lane_head == j, rows, zero) for j in range(4)], axis=0)


def attend_kernel(
    place, lengths, tokens, w_own, w_other, proj, att, lse, segc, segr, vec, wfull, bias, vt
):
    opt = place[0]
    assemble(wfull, w_own, w_other, opt)
    mine = w_own[HALF : HALF + 16, 0:D].astype(F32)
    others = w_other[HALF : HALF + 16, 0:D].astype(F32)
    first = opt == 0
    vec[0:6, :] = jnp.where(first, mine, others)[0:6]
    vec[6:12, :] = jnp.where(first, others, mine)[0:6]
    vec[12:16, :] = jnp.zeros((4, D), F32)

    pos_col = iota((WIN, 128), 0) + OFF * opt
    pos_row = iota((8, PAD), 1) + OFF * opt
    seg_col = jnp.zeros((WIN, 128), jnp.int32)
    seg_row = jnp.zeros((8, PAD), jnp.int32)
    bound = jnp.int32(0)
    for s in range(SEGS):
        bound = bound + lengths[s]
        seg_col = seg_col + (pos_col >= bound).astype(jnp.int32)
        seg_row = seg_row + (pos_row >= bound).astype(jnp.int32)
    segc[...] = seg_col
    segr[...] = seg_row
    for i, (q0, k0, k1) in enumerate(BANDS):
        bias[BAND_ROWS[i] : BAND_ROWS[i + 1], :] = jnp.where(
            segc[k0:k1, :] == segr[0:1, q0 : q0 + BLOCK], 0.0, NEG_BIG
        )

    x = tokens[aligned(OFF * opt, WIN, 64), :]
    for c in range(3):
        acc = nn(x, wfull[:, c * D : (c + 1) * D])
        if c != 1:
            acc = acc + vec[(0 if c == 0 else 1) : (1 if c == 0 else 2), :]
        proj[0:WIN, c * D : (c + 1) * D] = acc.astype(BF16)
    proj[WIN:PAD, :] = jnp.zeros((PAD - WIN, 3 * D), BF16)

    def group(g, carry):
        def lanes(part):
            return aligned(part * D + 128 * g, 128, 128)

        for t in range(PAD // 128):
            vt[:, 128 * t : 128 * t + 128] = (
                proj[128 * t : 128 * t + 128, lanes(2)].astype(F32).T.astype(BF16)
            )
        for i, (q0, k0, k1) in enumerate(BANDS):
            stack = head_stack(proj[q0 : q0 + BLOCK, lanes(0)])
            st = nt(proj[k0:k1, lanes(1)], stack)
            outs = []
            for j in range(4):
                t = (
                    st[:, j * BLOCK : (j + 1) * BLOCK] * EXP2_SCALE
                    + bias[BAND_ROWS[i] : BAND_ROWS[i + 1], :]
                )
                peak = jnp.max(t, axis=0, keepdims=True)
                powers = jnp.exp2(t - peak)
                total = jnp.sum(powers, axis=0, keepdims=True)
                lse[g, j : j + 1, q0 : q0 + BLOCK] = peak + jnp.log2(total)
                o = nn(vt[j * HD : (j + 1) * HD, k0:k1], powers.astype(BF16))
                outs.append(o * (1.0 / total))
            rows = min(BLOCK, WIN - q0)
            att[q0 : q0 + rows, aligned(128 * g, 128, 128)] = (
                jnp.concatenate(outs, axis=0).T[0:rows].astype(BF16)
            )
        return carry

    lax.fori_loop(0, 3, group, 0)


def attend(place, lengths, tokens, w_own, w_other):
    return call(
        attend_kernel,
        [(1, place), (1, lengths), (0, tokens), (0, w_own), (0, w_other)],
        [
            ((PAD, 3 * D), BF16),
            ((WIN, D), BF16),
            ((3, 4, PAD), F32),
            ((WIN, 128), jnp.int32),
            ((8, PAD), jnp.int32),
            ((16, D), F32),
        ],
        [
            pltpu.VMEM((D, 3 * D), BF16),
            pltpu.VMEM((BAND_ROWS[-1], 128), F32),
            pltpu.VMEM((128, PAD), BF16),
        ],
        micros=8,
        name="attend",
    )


def owned(place, lengths, segment):
    bound = jnp.int32(0)
    count = jnp.int32(0)
    for s in range(SEGS):
        bound = bound + lengths[s]
        count = count + (bound <= WIN).astype(jnp.int32)
    low_side = (segment < count).astype(jnp.int32)
    return low_side == (place[0] == 0).astype(jnp.int32)


def mlp_kernel(
    place, lengths, chosen, att, tokens, segr, vec, wo_own, wo_other, wu_own, wu_other,
    wd_own, wd_other, xhat1, inv1, hlow, act, slope, xhat2, inv2, unit, uscale,
    wo, wu, wd, tmp, hid, ench, encl,
):
    opt = place[0]
    assemble(wo, wo_own, wo_other, opt)
    assemble(wu, wu_own, wu_other, opt)
    assemble(wd, wd_own, wd_other, opt)
    tmp[...] = nn(att[...], wo[...])

    def first_norm(i, carry):
        r = aligned(i * ROWS, ROWS, ROWS)
        x = tokens[aligned(OFF * opt + i * ROWS, ROWS, ROWS), :].astype(F32)
        v = tmp[r, :] + vec[2:3, :] + x
        centred = v - jnp.mean(v, axis=1, keepdims=True)
        inverse = lax.rsqrt(jnp.mean(centred * centred, axis=1, keepdims=True) + LN_EPS)
        normed = centred * inverse
        xhat1[r, :] = normed
        inv1[r, :] = jnp.broadcast_to(inverse, (ROWS, 128))
        h = normed * vec[8:9, :] + vec[9:10, :]
        hid[r, :] = h
        hlow[r, :] = h.astype(BF16)
        return carry

    lax.fori_loop(0, WIN // ROWS, first_norm, 0)

    for c in range(4):
        cols = slice(c * D, (c + 1) * D)
        tmp[...] = nn(hlow[...], wu[:, cols])

        def gelu(i, carry, cols=cols, c=c):
            r = aligned(i * ROWS, ROWS, ROWS)
            u = tmp[r, :] + vec[3 + c : 4 + c, :]
            half = lax.erf(u * 0.7071067811865476) * 0.5 + 0.5
            act[r, cols] = (u * half).astype(BF16)
            slope[r, cols] = half + u * jnp.exp(-0.5 * u * u) * 0.3989422804014327
            return carry

        lax.fori_loop(0, WIN // ROWS, gelu, 0)

    tmp[...] = nt(act[...], wd[...])

    def second_norm(i, carry):
        r = aligned(i * ROWS, ROWS, ROWS)
        v = tmp[r, :] + vec[7:8, :] + hid[r, :]
        centred = v - jnp.mean(v, axis=1, keepdims=True)
        inverse = lax.rsqrt(jnp.mean(centred * centred, axis=1, keepdims=True) + LN_EPS)
        normed = centred * inverse
        xhat2[r, :] = normed
        inv2[r, :] = jnp.broadcast_to(inverse, (ROWS, 128))
        high, rest = low_pair(normed * vec[10:11, :] + vec[11:12, :])
        ench[r, :] = high
        encl[r, :] = rest
        return carry

    lax.fori_loop(0, WIN // ROWS, second_norm, 0)

    seg = segr[0:1, 0:WIN]
    row_id = iota((2 * PAIRS, WIN), 0)
    wanted = jnp.zeros((2 * PAIRS, WIN), jnp.int32)
    for j in range(2 * PAIRS):
        wanted = jnp.where(row_id == j, chosen[j], wanted)
    mask = owned(place, lengths, jnp.broadcast_to(seg, (2 * PAIRS, WIN)))
    onehot = jnp.where((wanted == seg) & mask, 1.0, 0.0)
    count = jnp.maximum(jnp.sum(onehot, axis=1, keepdims=True), 1.0)
    hot = onehot.astype(BF16)
    pooled = (nn(hot, ench[...]) + nn(hot, encl[...])) / count
    inverse_len = lax.rsqrt(jnp.sum(pooled * pooled, axis=1, keepdims=True) + POOL_EPS)
    unit[...] = pooled * inverse_len
    uscale[...] = jnp.broadcast_to(inverse_len / count, (2 * PAIRS, 128))


def mlp(place, lengths, chosen, att, tokens, segr, vec, halves):
    return call(
        mlp_kernel,
        [(1, place), (1, lengths), (1, chosen), (0, att), (0, tokens), (0, segr), (0, vec)]
        + [(0, h) for h in halves],
        [
            ((WIN, D), F32),
            ((WIN, 128), F32),
            ((WIN, D), BF16),
            ((WIN, FF), BF16),
            ((WIN, FF), F32),
            ((WIN, D), F32),
            ((WIN, 128), F32),
            ((2 * PAIRS, D), F32),
            ((2 * PAIRS, 128), F32),
        ],
        [
            pltpu.VMEM((D, D), BF16),
            pltpu.VMEM((D, FF), BF16),
            pltpu.VMEM((D, FF), BF16),
            pltpu.VMEM((WIN, D), F32),
            pltpu.VMEM((WIN, D), F32),
            pltpu.VMEM((WIN, D), BF16),
            pltpu.VMEM((WIN, D), BF16),
        ],
        micros=10,
        name="mlp",
    )


def split_rows(grad, keep, send, place, *at):
    opt = place[0]
    for c in range(4):
        index = (c ^ place[1],) + at
        keep[index] = grad[aligned(HALF * opt + CHUNK * c, CHUNK, 16), :].astype(BF16)
        send[index] = grad[aligned(HALF * (1 - opt) + CHUNK * c, CHUNK, 16), :].astype(BF16)


def column_sums(value):
    return jnp.sum(value.reshape(ROWS // 8, 8, D), axis=0)


def norm_backward(grad_at, normed_ref, inverse_ref, gain, out, low_out, sums, at):
    def block(i, carry):
        scale_sum, shift_sum, bias_sum = carry
        r = aligned(i * ROWS, ROWS, ROWS)
        g = grad_at(r)
        normed = normed_ref[r, :]
        scaled = g * gain
        inner = (
            scaled
            - jnp.mean(scaled, axis=1, keepdims=True)
            - normed * jnp.mean(scaled * normed, axis=1, keepdims=True)
        ) * inverse_ref[r, 0:1]
        out[r, :] = inner
        low_out[r, :] = inner.astype(BF16)
        return (
            scale_sum + column_sums(g * normed),
            shift_sum + column_sums(g),
            bias_sum + column_sums(inner),
        )

    zero = jnp.zeros((8, D), F32)
    scale_sum, shift_sum, bias_sum = lax.fori_loop(0, WIN // ROWS, block, (zero, zero, zero))
    sums[at : at + 1, :] = jnp.sum(bias_sum, axis=0, keepdims=True)
    sums[at + 1 : at + 2, :] = jnp.sum(scale_sum, axis=0, keepdims=True)
    sums[at + 2 : at + 3, :] = jnp.sum(shift_sum, axis=0, keepdims=True)


def down_kernel(
    count, order, place, lengths, chosen, units, segc, uscale, xhat2, inv2, act, vec, *rest
):
    pieces, (dsec, dlow, keep, send, sums, queries, docs, marks, grad) = rest[:-9], rest[-9:]
    me = place[2]
    per = pieces[0].shape[0]
    for p, piece in enumerate(pieces):
        for j in range(per):
            at = order[p * per + j]
            r = slice(at * PAIRS, (at + 1) * PAIRS)
            both = piece[j].astype(F32)
            queries[r, :] = both[0:PAIRS, 0:D]
            docs[r, :] = both[PAIRS : 2 * PAIRS, 0:D]
            marks[r, :] = both[0:PAIRS, D : D + 128]
    total = count * PAIRS
    q = queries[...].astype(BF16)
    d = docs[...].astype(BF16)
    logits = SCORE_SCALE * nt(q, d)
    peak = jnp.max(logits, axis=1, keepdims=True)
    powers = jnp.exp(logits - peak)
    soft = powers / jnp.sum(powers, axis=1, keepdims=True)
    col = iota((total, total), 1)
    doc_id = ((col // PAIRS) ^ me) * PAIRS + lax.rem(col, PAIRS)
    hit = (marks[:, 0:1] * 32.0 + marks[:, 64:65]).astype(jnp.int32) == doc_id
    d_logits = (soft - jnp.where(hit, 1.0, 0.0)) * (SCORE_SCALE / total)
    high, rest_low = low_pair(d_logits[0:PAIRS, :])
    d_q = nn(high, d) + nn(rest_low, d)
    high, rest_low = low_pair(d_logits[:, 0:128].T[0:PAIRS, :])
    d_d = nn(high, q) + nn(rest_low, q)
    d_units = jnp.concatenate([d_q, d_d], axis=0)
    u = units[...]
    d_pool = uscale[:, 0:1] * (d_units - u * jnp.sum(u * d_units, axis=1, keepdims=True))
    lane = iota((8, 2 * PAIRS), 1)
    wanted = jnp.zeros((8, 2 * PAIRS), jnp.int32)
    for j in range(2 * PAIRS):
        wanted = jnp.where(lane == j, chosen[j], wanted)
    seg = segc[:, 0 : 2 * PAIRS]
    mask = owned(place, lengths, seg)
    hot = jnp.where((seg == wanted[0:1, :]) & mask, 1.0, 0.0).astype(BF16)
    high, rest_low = low_pair(d_pool)
    dsec[...] = nn(hot, high) + nn(hot, rest_low)
    norm_backward(lambda r: dsec[r, :], xhat2, inv2, vec[10:11, :], dsec, dlow, sums, 0)
    sums[3:8, :] = jnp.zeros((5, D), F32)
    for c in range(4):
        cols = slice(c * D, (c + 1) * D)
        grad[...] = tn(dlow[...], act[:, cols])
        split_rows(grad, keep, send, place, c)


def down_backward(count, order, place, lengths, chosen, units, segc, uscale, saved, vec, pieces, after):
    total = count * PAIRS
    return call(
        functools.partial(down_kernel, count, order),
        [(1, place), (1, lengths), (1, chosen), (0, units), (0, segc), (0, uscale)]
        + [(0, s) for s in saved]
        + [(0, vec)]
        + [(0, p) for p in pieces],
        [
            ((WIN, D), F32),
            ((WIN, D), BF16),
            ((4, 4, CHUNK, D), BF16),
            ((4, 4, CHUNK, D), BF16),
            ((8, D), F32),
        ],
        [
            pltpu.VMEM((total, D), F32),
            pltpu.VMEM((total, D), F32),
            pltpu.VMEM((total, 128), F32),
            pltpu.VMEM((D, D), F32),
        ],
        micros=4,
        name="down_backward",
        after=after,
    )


def up_kernel(place, dlow, slope, hlow, wd_own, wd_other, dup, keep, send, sums, wd, grad):
    opt = place[0]
    assemble(wd, wd_own, wd_other, opt)
    for c in range(4):
        cols = slice(c * D, (c + 1) * D)
        part = (nn(dlow[...], wd[:, cols]) * slope[:, cols]).astype(BF16)
        dup[:, cols] = part
        sums[c : c + 1, :] = jnp.sum(part.astype(F32), axis=0, keepdims=True)
        grad[...] = tn(hlow[...], dup[:, cols])
        split_rows(grad, keep, send, place, c)


def up_backward(place, dlow, slope, hlow, halves, after):
    return call(
        up_kernel,
        [(1, place)] + [(0, a) for a in (dlow, slope, hlow) + tuple(halves)],
        [((WIN, FF), BF16), ((4, 4, CHUNK, D), BF16), ((4, 4, CHUNK, D), BF16), ((4, D), F32)],
        [pltpu.VMEM((D, FF), BF16), pltpu.VMEM((D, D), F32)],
        micros=3,
        name="up_backward",
        after=after,
    )


def first_kernel(
    place, dup, dsec, xhat1, inv1, att, vec, wu_own, wu_other, wo_own, wo_other,
    dfirst, datt, delta, okeep, osend, sums, wu, wo, grad, dlow,
):
    opt = place[0]
    assemble(wu, wu_own, wu_other, opt)
    assemble(wo, wo_own, wo_other, opt)
    dfirst[...] = nt(dup[...], wu[...])
    norm_backward(
        lambda r: dfirst[r, :] + dsec[r, :], xhat1, inv1, vec[8:9, :], dfirst, dlow, sums, 0
    )
    sums[3:8, :] = jnp.zeros((5, D), F32)
    grad[...] = tn(att[...], dlow[...])
    split_rows(grad, okeep, osend, place)
    da = nt(dlow[...], wo[...]).astype(BF16)
    datt[0:WIN, :] = da
    datt[WIN:PAD, :] = jnp.zeros((PAD - WIN, D), BF16)
    high, rest = low_pair(da.astype(F32) * att[...].astype(F32))
    heads = (iota((16, D), 1) // HD == iota((16, D), 0)).astype(F32).astype(BF16)
    delta[:, 0:WIN] = nt(heads, high) + nt(heads, rest)
    delta[:, WIN:PAD] = jnp.zeros((16, PAD - WIN), F32)


def first_backward(place, dup, dsec, xhat1, inv1, att, vec, halves, after):
    return call(
        first_kernel,
        [(1, place)] + [(0, a) for a in (dup, dsec, xhat1, inv1, att, vec) + tuple(halves)],
        [
            ((WIN, D), F32),
            ((PAD, D), BF16),
            ((16, PAD), F32),
            ((4, CHUNK, D), BF16),
            ((4, CHUNK, D), BF16),
            ((8, D), F32),
        ],
        [
            pltpu.VMEM((D, FF), BF16),
            pltpu.VMEM((D, D), BF16),
            pltpu.VMEM((D, D), F32),
            pltpu.VMEM((WIN, D), BF16),
        ],
        micros=3,
        name="first_backward",
        after=after,
    )


def heads_kernel(g, place, tokens, proj, datt, lse, delta, segc, segr, *rest):
    rest, (dproj, keep, send, sums, kt, dk, dv, grad, ktmp, stmp) = rest[:-10], rest[-10:]

    def lanes(part):
        return slice(part * D + 128 * g, part * D + 128 * g + 128)

    for t in range(PAD // 128):
        kt[:, 128 * t : 128 * t + 128] = (
            proj[128 * t : 128 * t + 128, lanes(1)].astype(F32).T.astype(BF16)
        )
    dk[...] = jnp.zeros_like(dk)
    dv[...] = jnp.zeros_like(dv)
    for q0, k0, k1 in BANDS:
        qs = head_stack(proj[q0 : q0 + BLOCK, lanes(0)])
        gs = head_stack(datt[q0 : q0 + BLOCK, lanes(0)])
        st = nt(proj[k0:k1, lanes(1)], qs)
        dp = nt(proj[k0:k1, lanes(2)], gs)
        same = segc[k0:k1, :] == segr[0:1, q0 : q0 + BLOCK]
        bias = jnp.where(same, 0.0, NEG_BIG)
        probs, d_scores, dq = [], [], []
        for j in range(4):
            cols = slice(j * BLOCK, (j + 1) * BLOCK)
            prob = jnp.exp2(st[:, cols] * EXP2_SCALE + bias - lse[g, j : j + 1, q0 : q0 + BLOCK])
            ds = prob * (dp[:, cols] - delta[4 * g + j : 4 * g + j + 1, q0 : q0 + BLOCK])
            ds = ds.astype(BF16)
            probs.append(prob.astype(BF16))
            d_scores.append(ds)
            dq.append(nn(kt[j * HD : (j + 1) * HD, k0:k1], ds))
        dv[k0:k1, :] += nn(jnp.concatenate(probs, axis=1), gs)
        dk[k0:k1, :] += nn(jnp.concatenate(d_scores, axis=1), qs)
        rows = min(BLOCK, WIN - q0)
        dqs = jnp.concatenate(dq, axis=0).T[0:rows] * HD ** (-0.5)
        dproj[q0 : q0 + rows, 0:128] = dqs.astype(BF16)
    dproj[:, 128:256] = (dk[...] * HD ** (-0.5)).astype(BF16)
    dproj[:, 256:384] = dv[...].astype(BF16)
    grad[...] = tn(tokens[aligned(OFF * place[0], WIN, 64), :], dproj[...])
    q_sum = jnp.sum(dproj[:, 0:128].astype(F32), axis=0, keepdims=True)
    v_sum = jnp.sum(dproj[:, 256:384].astype(F32), axis=0, keepdims=True)
    sums[0:1, :] = q_sum
    sums[1:2, :] = v_sum
    sums[2:8, :] = jnp.zeros((6, 128), F32)
    if g < 2:
        split_rows(grad, keep, send, place)
        return
    parts, (dsums, usums, fsums, zero, one) = rest[:4], rest[4:]
    split_rows(grad, ktmp, stmp, place)
    for dst, blocks in (
        (keep, (parts[0], parts[2], ktmp)),
        (send, (parts[1], parts[3], stmp)),
    ):
        for h, part in enumerate(blocks):
            for c in range(3):
                dst[:, :, D * c + 128 * h : D * c + 128 * h + 128] = part[
                    :, :, 128 * c : 128 * c + 128
                ]
    rows = jnp.concatenate(
        [
            jnp.concatenate([zero[0:1], one[0:1], q_sum], axis=1),
            jnp.concatenate([zero[1:2], one[1:2], v_sum], axis=1),
            fsums[0:1, :],
            usums[0:4, :],
            dsums[0:1, :],
            fsums[1:3, :],
            dsums[1:3, :],
            jnp.zeros((4, D), F32),
        ],
        axis=0,
    ).astype(BF16)
    for c in range(4):
        for j in range(3):
            block = rows[:, 128 * j : 128 * j + 128]
            keep[c, 16 * j : 16 * j + 16, 3 * D : 3 * D + 128] = block
            send[c, 16 * j : 16 * j + 16, 3 * D : 3 * D + 128] = block


def heads_backward(g, place, ins, more, after):
    part = ((4, CHUNK, 3 * D + 128 if g == 2 else D), BF16)
    return call(
        functools.partial(heads_kernel, g),
        [(1, place)] + [(0, a) for a in tuple(ins) + tuple(more)],
        [((WIN, D), BF16), part, part, ((8, 128), F32)],
        [
            pltpu.VMEM((128, PAD), BF16),
            pltpu.VMEM((WIN, 128), F32),
            pltpu.VMEM((WIN, 128), F32),
            pltpu.VMEM((D, D), F32),
            pltpu.VMEM((4, CHUNK, D), BF16),
            pltpu.VMEM((4, CHUNK, D), BF16),
        ],
        micros=3,
        name="heads_backward",
        after=after,
    )


def input_kernel(place, dp0, dp1, dp2, dfirst, w_own, w_other, igrad, wfull, dproj):
    assemble(wfull, w_own, w_other, place[0])
    for g, part in enumerate((dp0, dp1, dp2)):
        for c in range(3):
            dproj[:, c * D + 128 * g : c * D + 128 * g + 128] = part[:, 128 * c : 128 * c + 128]
    igrad[...] = (nt(dproj[...], wfull[...]) + dfirst[...]).astype(BF16)


def input_backward(place, parts, dfirst, w_own, w_other, after):
    return call(
        input_kernel,
        [(1, place)] + [(0, a) for a in tuple(parts) + (dfirst, w_own, w_other)],
        [((WIN, D), BF16)],
        [pltpu.VMEM((D, 3 * D), BF16), pltpu.VMEM((WIN, 3 * D), BF16)],
        micros=2,
        name="input_backward",
        after=after,
    )[0]


def flips(axis, size, bits):
    return [(i, i ^ bits) for i in range(size)]


def pair(value):
    return swap(value, "opt", 2, 1)


def swap(value, axis, size, bits):
    return lax.ppermute(value, axis, flips(axis, size, bits))


def bit_groups(size):
    bits = size.bit_length() - 1
    return [(s, 1 << min(2, bits - s)) for s in range(0, bits, 2)]


def trades(values, n, shift):
    return [values[0]] + [swap(values[k], "dp", n, k << shift) for k in (1, 2, 3)]


def added(a, b):
    return (a.astype(F32) + b.astype(F32)).astype(BF16)


def core_sum_kernel(*refs):
    ins, outs = refs[:-4], refs[-4:]
    for r, out in enumerate(outs):
        if len(ins) == 2:
            out[...] = added(ins[0][r], ins[1][r])
        else:
            out[0:4] = added(ins[0][r], ins[1][r])
            out[4] = added(ins[2][r], ins[3][r])


def core_sum(parts, after):
    shape = parts[0].shape[1:]
    if len(parts) == 4:
        shape = (5,) + shape[1:]
    return call(
        core_sum_kernel, [(0, p) for p in parts], [(shape, BF16)] * 4, name="core_sum", vmem=4, after=after
    )


def total_of(refs, at):
    a, b, c, d = (ref[at].astype(F32) for ref in refs)
    return ((a + b) + (c + d)).astype(BF16)


def down_plane_kernel(a, b, c, d, out):
    out[...] = (a[...].astype(F32) + b[...].astype(F32)) + (c[...].astype(F32) + d[...].astype(F32))


def down_plane_sum(parts, after):
    return call(
        down_plane_kernel,
        [(0, p) for p in parts],
        [(parts[0].shape, F32)],
        name="down_plane_sum",
        vmem=4,
        after=after,
    )[0]


def wide_plane_kernel(place, down, *refs):
    up, outs = refs[:4], refs[4:]
    single = total_of(up, 4)
    for k, out in enumerate(outs):
        out[0] = down[place[3] ^ k].astype(BF16)
        out[1] = total_of(up, place[3] ^ k)
        out[2] = single


def wide_plane_sum(place, parts, after):
    return call(
        wide_plane_kernel,
        [(1, place)] + [(0, p) for p in parts],
        [((3, CHUNK, D), BF16)] * 4,
        name="wide_plane_sum",
        vmem=4,
        after=after,
    )


def wide_line_kernel(a, b, c, d, pair_out, single):
    refs = (a, b, c, d)
    pair_out[...] = total_of(refs, slice(0, 2))
    single[...] = total_of(refs, slice(2, 3))


def wide_line_sum(parts, after):
    return call(
        wide_line_kernel,
        [(0, p) for p in parts],
        [((2, CHUNK, D), BF16), ((1, CHUNK, D), BF16)],
        name="wide_line_sum",
        vmem=4,
        after=after,
    )


def low_plane_kernel(a, b, c, d, out):
    out[...] = total_of((a, b, c, d), slice(None))


def low_plane_sum(parts, after=()):
    return call(
        low_plane_kernel,
        [(0, p) for p in parts],
        [(parts[0].shape, BF16)],
        name="low_plane_sum",
        vmem=4,
        after=after,
    )[0]


def low_next_kernel(keep, other, out):
    out[...] = added(keep[...], other[...])


def low_next(keep, other, after=()):
    return call(
        low_next_kernel,
        [(0, keep), (0, other)],
        [(keep.shape, BF16)],
        name="low_next",
        vmem=4,
        after=after,
    )[0]


def low_last_kernel(keep, other, out, vgrad):
    out[...] = added(keep[:, 0 : 3 * D], other[:, 0 : 3 * D])
    vgrad[...] = added(keep[:, 3 * D : 3 * D + 128], other[:, 3 * D : 3 * D + 128])


def low_last(keep, other, after):
    return call(
        low_last_kernel,
        [(0, keep), (0, other)],
        [((CHUNK, 3 * D), BF16), ((CHUNK, 128), BF16)],
        name="low_last",
        vmem=4,
        after=after,
    )


def chain_kernel(*refs):
    ins, out = refs[:-1], refs[-1]
    at = 0
    for ref in ins:
        flat = ref.reshape(-1, CHUNK, D)
        out[at : at + flat.shape[0]] = flat[...]
        at += flat.shape[0]


def chain(parts, after=()):
    count = sum(p.size for p in parts) // (CHUNK * D)
    return call(
        chain_kernel,
        [(0, p) for p in parts],
        [((count, CHUNK, D), BF16)],
        name="chain",
        vmem=4,
        after=after,
    )[0]


def rest_sum(value, n):
    bit = 16
    while bit < n:
        other = swap(value, "dp", n, bit)
        value = (value.astype(F32) + other.astype(F32)).astype(BF16)
        bit *= 2
    return value


def join_kernel(*refs):
    ins, out = refs[:-1], refs[-1]
    for i, ref in enumerate(ins):
        out[i] = ref[...]


def join(parts, after=()):
    return call(
        join_kernel,
        [(0, p) for p in parts],
        [((len(parts),) + parts[0].shape, parts[0].dtype)],
        name="join",
        vmem=4,
        after=after,
    )[0]


def pack_kernel(place, targets, unit, other, units, packed):
    both = unit[...] + other[...]
    units[...] = both
    row = iota((2 * PAIRS, 128), 0)
    marks = jnp.zeros((2 * PAIRS, 128), jnp.int32)
    for j in range(PAIRS):
        marks = jnp.where(row == j, targets[j], marks)
    marks = jnp.where(iota((2 * PAIRS, 128), 1) < 64, marks >> 5, marks & 31)
    packed[:, 0:D] = both.astype(BF16)
    packed[:, D : D + 128] = marks.astype(F32).astype(BF16)


def pack(place, targets, unit, other):
    return call(
        pack_kernel,
        [(1, place), (1, targets), (0, unit), (0, other)],
        [(unit.shape, F32), ((2 * PAIRS, D + 128), BF16)],
        name="pack",
        vmem=4,
    )


def squares_of(parts):
    acc = jnp.zeros((8, D), F32)
    for part in parts:
        flat = part.reshape(-1, CHUNK, part.shape[-1])
        for k in range(flat.shape[0]):
            for c in range(0, part.shape[-1], D):
                v = flat[k, :, c : c + D].astype(F32)
                acc = acc + jnp.sum((v * v).reshape(CHUNK // 8, 8, D), axis=0)
    return acc[:, 0:128] + acc[:, 128:256] + acc[:, 256:384]


def wide_squares_kernel(*refs):
    refs[-1][...] = squares_of(refs[:-1])


def squares_kernel(place, *refs):
    parts, (vgrad, before, out) = refs[:-3], refs[-3:]
    acc = squares_of(parts) + before[...]
    row = iota((16, 128), 0)
    low_row = 6 * place[0]
    mine = (row >= low_row) & (row < low_row + 6)
    for j in range(3):
        v = jnp.where(mine, vgrad[16 * j : 16 * j + 16, :].astype(F32), 0.0)
        v = v * v
        acc = acc + (v[0:8] + v[8:16])
    out[...] = acc


def squares(place, parts, vgrad=None, before=None, after=()):
    ins = [(0, p) for p in parts]
    kernel = wide_squares_kernel
    if before is not None:
        ins = [(1, place)] + ins + [(0, vgrad), (0, before)]
        kernel = squares_kernel
    return call(kernel, ins, [((8, 128), F32)], name="squares", vmem=4, after=after)[0]


def merge_kernel(place, igrad, other, out, flag):
    flag[...] = jnp.zeros((8, 128), F32)

    @pl.when(place[0] == 0)
    def low_core():
        out[0:OFF, :] = igrad[0:OFF, :]
        out[OFF:WIN, :] = added(igrad[OFF:WIN, :], other[0 : WIN - OFF, :])
        out[WIN:SEQ, :] = other[WIN - OFF : WIN, :]

    @pl.when(place[0] != 0)
    def high_core():
        out[0:OFF, :] = other[0:OFF, :]
        out[OFF:WIN, :] = added(other[OFF:WIN, :], igrad[0 : WIN - OFF, :])
        out[WIN:SEQ, :] = igrad[WIN - OFF : WIN, :]


def merge(place, igrad, other, after):
    return call(
        merge_kernel,
        [(1, place), (0, igrad), (0, other)],
        [((SEQ, D), BF16), ((8, 128), F32)],
        name="merge",
        vmem=4,
        after=after,
    )


def adamw(parameter, first_state, second, clipped, rate):
    first_new = first_state + (1.0 - BETA_ONE) * clipped
    second_new = second + (1.0 - BETA_TWO) * clipped * clipped
    direction = (first_new * (1.0 / (1.0 - BETA_ONE**STEP))) / (
        jnp.sqrt(second_new * (1.0 / (1.0 - BETA_TWO**STEP))) + ADAM_EPS
    )
    return parameter - rate * direction, first_new, second_new


def decay_kernel(w, m, v, pv, pm, pq, nw, nm, nv, npv, npm, npq):
    for ins, outs, rate in (
        ((w, m, v), (nw, nm, nv), LEARN_RATE),
        ((pv, pm, pq), (npv, npm, npq), VECTOR_RATE),
    ):
        for ref, out, scale in zip(ins, outs, (1.0 - rate * DECAY_RATE, BETA_ONE, BETA_TWO)):
            out[...] = ref[...] * scale


def decay(arrays, after):
    return call(
        decay_kernel,
        [(0, a) for a in arrays],
        [(a.shape, F32) for a in arrays],
        name="decay",
        vmem=4,
        after=after,
    )


def adamw_kernel(place, *refs):
    sums, refs = refs[:2], refs[2:]
    (vgrad, w, m, v, pv, pm, pq), refs = refs[:7], refs[7:]
    wide, low, refs = refs[:4], refs[4:8], refs[8:]
    outs, (npv, npm, npq, norm), scrs, sems = refs[:4], refs[4:8], refs[8:12], refs[12]
    opt = place[0]
    total = sums[0][...] + sums[1][...]
    total = jnp.sum(jnp.sum(total, axis=1, keepdims=True), axis=0, keepdims=True)
    grad_norm = jnp.sqrt(total)
    factor = jnp.minimum(1.0, CLIP_NORM / (grad_norm + 1e-06))
    norm[...] = grad_norm
    for j in range(3):
        cols = slice(128 * j, 128 * j + 128)
        g = vgrad[16 * j : 16 * j + 16, :].astype(F32)
        g = jnp.where(opt == 0, g[0:6], g[6:12])
        a, b, c = adamw(pv[:, cols], pm[:, cols], pq[:, cols], g * factor, VECTOR_RATE)
        npv[:, cols] = a
        npm[:, cols] = b
        npq[:, cols] = c
    copies = []

    def block(grad, rows, cols):
        new = adamw(w[rows, cols], m[rows, cols], v[rows, cols], grad * factor, LEARN_RATE)
        for scr, value in zip(scrs, new + (new[0].astype(BF16),)):
            scr[rows, cols] = value

    for r in range(4):
        base = CHUNK * (place[1] ^ r)

        def rows_of(i, carry, r=r, base=base):
            rows = aligned(base + i * 16, 16, 16)
            here = aligned(i * 16, 16, 16)
            for k in range(4):
                at = D * (place[3] ^ k)
                for p, start in enumerate((4 * D + FF, 4 * D)):
                    grad = wide[r][2 * k + p, here, :].astype(F32)
                    block(grad, rows, aligned(start + at, D, 128))
            grad = wide[r][8, here, :].astype(F32)
            block(grad, rows, slice(3 * D, 4 * D))
            for c in range(3):
                grad = low[r][here, D * c : D * c + D].astype(F32)
                block(grad, rows, slice(D * c, D * c + D))
            return carry

        lax.fori_loop(0, CHUNK // 16, rows_of, 0)
        rows = aligned(base, CHUNK, 16)
        for i, (scr, out) in enumerate(zip(scrs, outs)):
            copy = pltpu.make_async_copy(scr.at[rows, :], out.at[rows, :], sems.at[r, i])
            copy.start()
            copies.append(copy)
    for copy in copies:
        copy.wait()


def update(place, sums, vgrad, w, m, v, pv, pm, pq, parts):
    ins = tuple(sums) + (vgrad, w, m, v, pv, pm, pq) + tuple(parts)
    shapes = [(w.shape, F32)] * 3 + [(w.shape, BF16)] + [(pv.shape, F32)] * 3 + [((1, 1), F32)]
    return pl.pallas_call(
        adamw_kernel,
        out_shape=[jax.ShapeDtypeStruct(s, d) for s, d in shapes],
        in_specs=[SMEM] + [VMEM] * len(ins),
        out_specs=[ANY] * 4 + [VMEM] * 4,
        scratch_shapes=[
            pltpu.VMEM(w.shape, F32),
            pltpu.VMEM(w.shape, F32),
            pltpu.VMEM(w.shape, F32),
            pltpu.VMEM(w.shape, BF16),
            pltpu.SemaphoreType.DMA((4, 4)),
        ],
        compiler_params=pltpu.CompilerParams(vmem_limit_bytes=16 << 20),
        cost_estimate=pl.CostEstimate(
            flops=4000000000, bytes_accessed=26 * w.size, transcendentals=0
        ),
        name="adamw",
    )(place, *ins)


def shards(
    n,
    tokens,
    lengths,
    query_index,
    doc_index,
    targets,
    weights,
    first_moment,
    second_moment,
    vectors,
    vec_first,
    vec_second,
):
    opt = lax.axis_index("opt")
    me = lax.axis_index("dp")
    place = jnp.stack([opt, me & 3, me, (me >> 2) & 3]).astype(jnp.int32)
    lengths = lengths.reshape(SEGS)
    chosen = jnp.concatenate([query_index, doc_index])
    groups = bit_groups(n)

    extra = jnp.pad(vectors, ((0, 10), (0, 2 * D)))
    w_own = jnp.concatenate([weights[:, : 3 * D], extra], axis=0).astype(BF16)
    w_other = pair(w_own)
    later, w_own = lax.optimization_barrier((weights, w_own))
    wo_own = later[:, 3 * D : 4 * D].astype(BF16)
    wu_own = later[:, 4 * D : 4 * D + FF].astype(BF16)
    wd_own = later[:, 4 * D + FF :].astype(BF16)
    wo = (wo_own, pair(wo_own))
    wu = (wu_own, pair(wu_own))
    wd = (wd_own, pair(wd_own))

    proj, att, lse, segc, segr, vec = attend(place, lengths, tokens, w_own, w_other)
    xhat1, inv1, hlow, act, slope, xhat2, inv2, unit, uscale = mlp(
        place, lengths, chosen, att, tokens, segr, vec, wo + wu + wd
    )
    units, packed = pack(place, targets, unit, swap(unit, "opt", 2, 1))
    groups = bit_groups(n)
    order = [0]
    stack = packed
    for i, (shift, size) in enumerate(groups[1:] + groups[:1]):
        pieces = [stack] + [swap(stack, "dp", n, k << shift) for k in range(1, size)]
        order = [o | (k << shift) for k in range(size) for o in order]
        if i < len(groups) - 1:
            stack = join(pieces).reshape(-1, 2 * PAIRS, D + 128)
    decayed = decay(
        (weights, first_moment, second_moment, vectors, vec_first, vec_second), [packed]
    )
    dsec, dlow, keep, send, dsums = down_backward(
        n, order, place, lengths, chosen, units, segc, uscale, (xhat2, inv2, act), vec, pieces,
        decayed,
    )
    other = pair(send)
    dup, ukeep, usend, usums = up_backward(place, dlow, slope, hlow, wd, [])
    down = core_sum((keep, other), [dup])
    down_got = trades(down, n, 0)
    uother = pair(usend)
    dfirst, datt, delta, okeep, osend, fsums = first_backward(
        place, dup, dsec, xhat1, inv1, att, vec, wu + wo, [down[0]]
    )
    oother = pair(osend)
    down = down_plane_sum(down_got, [dfirst])
    up = core_sum((ukeep, uother, okeep, oother), [down])
    up_got = trades(up, n, 0)
    ins = (tokens, proj, datt, lse, delta, segc, segr)
    part0, keep0, send0, sums0 = heads_backward(0, place, ins, (), [up[0]])
    part1, keep1, send1, sums1 = heads_backward(1, place, ins, (), [part0])
    wide = wide_plane_sum(place, [down] + up_got, [part1])
    wide_got = trades(wide, n, 2)
    part2, keep, send, _ = heads_backward(
        2, place, ins, (keep0, send0, keep1, send1, dsums, usums, fsums, sums0, sums1),
        [wide[0], part1],
    )
    wide, single = wide_line_sum(wide_got, [part2])
    send, wide, single = lax.optimization_barrier((send, wide, single))
    other = pair(send)
    igrad = input_backward(place, (part0, part1, part2), dfirst, w_own, w_other, [wide])
    iother = pair(igrad)
    low = core_sum((keep, other), [igrad])
    low_got = trades(low, n, 0)
    low, wide, single = lax.optimization_barrier((low[0], wide, single))
    wide, single = rest_sum(wide, n), rest_sum(single, n)
    wide_got = trades([wide] * 4, n, 2)
    low = low_plane_sum(low_got, [low])
    other = swap(low, "dp", n, 4)
    wide = chain(wide_got + [single], [low])
    wide = trades([wide] * 4, n, 0)
    low = low_next(low, other, [wide[0]])
    other = swap(low, "dp", n, 8)
    input_grad, flag = merge(place, igrad, iother, [low])
    low, vgrad = low_last(low, other, [flag])
    low, vgrad = rest_sum(low, n), rest_sum(vgrad, n)
    low = trades([low] * 4, n, 0)
    sums = squares(place, low, vgrad, squares(place, wide, after=[low[0]]))
    sums = (sums, pair(sums))
    pieces = tuple(wide) + tuple(low)
    nw, nm, nv, nlow, npv, npm, npq, norm = update(
        place, sums, vgrad, *decayed, pieces,
    )
    return (norm.reshape(()), input_grad, nw, nm, nv, nlow, npv, npm, npq)


def solution(mesh):
    rows = P("opt", None)
    in_specs = (P("dp", None), P("dp", None), P("dp"), P("dp"), P("dp")) + (rows,) * 6
    out_specs = (P(), P("dp", None)) + (rows,) * 7
    n = mesh.shape["dp"]
    return jax.shard_map(
        functools.partial(shards, n),
        mesh=mesh,
        in_specs=in_specs,
        out_specs=out_specs,
        check_vma=False,
    )
```

```python
import functools

import jax
import jax.numpy as jnp
from jax import lax
from jax.experimental import pallas as pl
from jax.experimental.pallas import tpu as pltpu
from jax.sharding import PartitionSpec as P

D = 384
HEADS = 12
HD = 32
FF = 1536
SEQ = 1024
SEGS = 16
PAIRS = 8
STEP = 10

WIN = 576
OFF = SEQ - WIN
PAD = 640
BLOCK = 128
BANDS = tuple((q, max(0, q - 128), min(WIN, q + 256)) for q in range(0, WIN, BLOCK))
BAND_ROWS = tuple(sum(b[2] - b[1] for b in BANDS[:i]) for i in range(len(BANDS) + 1))
ROWS = 64
WIDE_ROWS = 192
LOG2E = 1.4426950408889634

LN_EPS = 1e-06
POOL_EPS = 1e-06
SCORE_SCALE = 50.0
CLIP_NORM = 0.001
BETA_ONE = 0.9
BETA_TWO = 0.98
ADAM_EPS = 1e-08
LEARN_RATE = 0.05
VECTOR_RATE = 0.3
DECAY_RATE = 0.01
NEG_BIG = -1e30
HALF = D // 2
CHUNK = HALF // 4
EXP2_SCALE = HD ** (-0.5) * 1.4426950408889634

F32 = jnp.float32
BF16 = jnp.bfloat16
VMEM = pl.BlockSpec(memory_space=pltpu.VMEM)
SMEM = pl.BlockSpec(memory_space=pltpu.SMEM)
ANY = pl.BlockSpec(memory_space=pl.ANY)


def nn(a, b):
    return jnp.dot(a, b, preferred_element_type=F32)


def nt(a, b):
    return lax.dot_general(a, b, (((1,), (1,)), ((), ())), preferred_element_type=F32)


def tn(a, b):
    return lax.dot_general(a, b, (((0,), (0,)), ((), ())), preferred_element_type=F32)


def exact(a, b, dims):
    return lax.dot_general(
        a, b, (dims, ((), ())), precision=lax.Precision.HIGHEST, preferred_element_type=F32
    )


def iota(shape, axis):
    return lax.broadcasted_iota(jnp.int32, shape, axis)


def low_pair(value):
    high = value.astype(BF16)
    return high, (value - high.astype(F32)).astype(BF16)


def aligned(start, size, unit):
    return pl.ds(pl.multiple_of(start, unit), size)


def assemble(dst, own, other, opt):
    dst[aligned(HALF * opt, HALF, 64), :] = own[0:HALF, :]
    dst[aligned(HALF * (1 - opt), HALF, 64), :] = other[0:HALF, :]


def call(kernel, ins, outs, scratch=(), micros=5, name=None, vmem=12, after=()):
    specs = [SMEM if s else VMEM for s, _ in ins] + [ANY] * len(after)
    count = len(ins)

    def body(*refs):
        kernel(*refs[:count], *refs[count + len(after) :])

    shapes = [jax.ShapeDtypeStruct(s, d) for s, d in outs]
    moved = sum(a.size * a.dtype.itemsize for _, a in ins)
    moved += sum(s.size * s.dtype.itemsize for s in shapes)
    return pl.pallas_call(
        body,
        out_shape=shapes,
        in_specs=specs,
        out_specs=[VMEM] * len(shapes),
        scratch_shapes=list(scratch),
        compiler_params=pltpu.CompilerParams(vmem_limit_bytes=vmem << 20),
        cost_estimate=pl.CostEstimate(
            flops=micros * 1100000000, bytes_accessed=moved, transcendentals=0
        ),
        name=name,
    )(*[a for _, a in ins], *after)


def head_stack(rows):
    lane_head = iota(rows.shape, 1) // HD
    zero = jnp.zeros_like(rows)
    return jnp.concatenate([jnp.where(lane_head == j, rows, zero) for j in range(4)], axis=0)


def attend_kernel(
    place, lengths, tokens, w_own, w_other, v_own, v_other,
    proj, att, lse, segc, segr, vec, wfull, bias, vt,
):
    opt = place[0]
    assemble(wfull, w_own, w_other, opt)
    mine = v_own[...].astype(BF16).astype(F32)
    others = v_other[...].astype(BF16).astype(F32)
    first = opt == 0
    vec[0:6, :] = jnp.where(first, mine, others)
    vec[6:12, :] = jnp.where(first, others, mine)
    vec[12:16, :] = jnp.zeros((4, D), F32)

    pos_col = iota((WIN, 128), 0) + OFF * opt
    pos_row = iota((8, PAD), 1) + OFF * opt
    seg_col = jnp.zeros((WIN, 128), jnp.int32)
    seg_row = jnp.zeros((8, PAD), jnp.int32)
    bound = jnp.int32(0)
    for s in range(SEGS):
        bound = bound + lengths[s]
        seg_col = seg_col + (pos_col >= bound).astype(jnp.int32)
        seg_row = seg_row + (pos_row >= bound).astype(jnp.int32)
    segc[...] = seg_col
    segr[...] = seg_row
    for i, (q0, k0, k1) in enumerate(BANDS):
        bias[BAND_ROWS[i] : BAND_ROWS[i + 1], :] = jnp.where(
            segc[k0:k1, :] == segr[0:1, q0 : q0 + BLOCK], 0.0, NEG_BIG
        )

    x = tokens[aligned(OFF * opt, WIN, 64), :]
    for c in range(3):
        acc = nn(x, wfull[:, c * D : (c + 1) * D])
        if c != 1:
            acc = acc + vec[(0 if c == 0 else 1) : (1 if c == 0 else 2), :]
        proj[0:WIN, c * D : (c + 1) * D] = acc.astype(BF16)
    proj[WIN:PAD, :] = jnp.zeros((PAD - WIN, 3 * D), BF16)

    def group(g, carry):
        def lanes(part):
            return aligned(part * D + 128 * g, 128, 128)

        for t in range(PAD // 128):
            vt[:, 128 * t : 128 * t + 128] = (
                proj[128 * t : 128 * t + 128, lanes(2)].astype(F32).T.astype(BF16)
            )
        for i, (q0, k0, k1) in enumerate(BANDS):
            stack = head_stack(proj[q0 : q0 + BLOCK, lanes(0)])
            st = nt(proj[k0:k1, lanes(1)], stack)
            outs = []
            for j in range(4):
                t = (
                    st[:, j * BLOCK : (j + 1) * BLOCK] * EXP2_SCALE
                    + bias[BAND_ROWS[i] : BAND_ROWS[i + 1], :]
                )
                peak = jnp.max(t, axis=0, keepdims=True)
                powers = jnp.exp2(t - peak)
                total = jnp.sum(powers, axis=0, keepdims=True)
                lse[g, j : j + 1, q0 : q0 + BLOCK] = peak + jnp.log2(total)
                o = nn(vt[j * HD : (j + 1) * HD, k0:k1], powers.astype(BF16))
                outs.append(o * (1.0 / total))
            rows = min(BLOCK, WIN - q0)
            att[q0 : q0 + rows, aligned(128 * g, 128, 128)] = (
                jnp.concatenate(outs, axis=0).T[0:rows].astype(BF16)
            )
        return carry

    lax.fori_loop(0, 3, group, 0)


def attend(place, lengths, tokens, w_own, w_other, v_own, v_other):
    return call(
        attend_kernel,
        [(1, place), (1, lengths)] + [(0, a) for a in (tokens, w_own, w_other, v_own, v_other)],
        [
            ((PAD, 3 * D), BF16),
            ((WIN, D), BF16),
            ((3, 4, PAD), F32),
            ((WIN, 128), jnp.int32),
            ((8, PAD), jnp.int32),
            ((16, D), F32),
        ],
        [
            pltpu.VMEM((D, 3 * D), BF16),
            pltpu.VMEM((BAND_ROWS[-1], 128), F32),
            pltpu.VMEM((128, PAD), BF16),
        ],
        micros=8,
        name="attend",
    )


def owned(place, lengths, segment):
    bound = jnp.int32(0)
    count = jnp.int32(0)
    for s in range(SEGS):
        bound = bound + lengths[s]
        count = count + (bound <= WIN).astype(jnp.int32)
    low_side = (segment < count).astype(jnp.int32)
    return low_side == (place[0] == 0).astype(jnp.int32)


def bias_of(vec, c):
    first, last = 256 * c, 256 * c + 256
    parts = []
    while first < last:
        row, col = divmod(first, D)
        size = min(D - col, last - first)
        parts.append(vec[3 + row : 4 + row, col : col + size])
        first += size
    return parts[0] if len(parts) == 1 else jnp.concatenate(parts, axis=1)


def mlp_kernel(
    place, lengths, chosen, att, tokens, segr, vec, wo_own, wo_other, wu_own, wu_other,
    wd_own, wd_other, xhat1, inv1, hlow, act, slope, xhat2, inv2, unit, uscale,
    wo, wu, wd, ench, encl,
):
    opt = place[0]
    assemble(wo, wo_own, wo_other, opt)
    assemble(wu, wu_own, wu_other, opt)
    assemble(wd, wd_own, wd_other, opt)

    def norm(v):
        centred = v - jnp.mean(v, axis=1, keepdims=True)
        inverse = lax.rsqrt(jnp.mean(centred * centred, axis=1, keepdims=True) + LN_EPS)
        return centred * inverse, inverse

    def block(i, carry):
        r = aligned(i * WIDE_ROWS, WIDE_ROWS, 64)
        x = tokens[aligned(OFF * opt + i * WIDE_ROWS, WIDE_ROWS, 64), :].astype(F32)
        normed, inverse = norm(nn(att[r, :], wo[...]) + vec[2:3, :] + x)
        xhat1[r, :] = normed
        inv1[r, :] = jnp.broadcast_to(inverse, (WIDE_ROWS, 128))
        h = normed * vec[8:9, :] + vec[9:10, :]
        low = h.astype(BF16)
        hlow[r, :] = low
        for c in range(6):
            cols = slice(c * 256, (c + 1) * 256)
            u = nn(low, wu[:, cols]) + bias_of(vec, c)
            half = lax.erf(u * 0.7071067811865476) * 0.5 + 0.5
            act[r, cols] = (u * half).astype(BF16)
            slope[r, cols] = half + u * jnp.exp2(u * u * (-0.5 * LOG2E)) * 0.3989422804014327
        normed, inverse = norm(nt(act[r, :], wd[...]) + vec[7:8, :] + h)
        xhat2[r, :] = normed
        inv2[r, :] = jnp.broadcast_to(inverse, (WIDE_ROWS, 128))
        high, rest = low_pair(normed * vec[10:11, :] + vec[11:12, :])
        ench[r, :] = high
        encl[r, :] = rest
        return carry

    lax.fori_loop(0, WIN // WIDE_ROWS, block, 0)

    seg = segr[0:1, 0:WIN]
    row_id = iota((2 * PAIRS, WIN), 0)
    wanted = jnp.zeros((2 * PAIRS, WIN), jnp.int32)
    for j in range(2 * PAIRS):
        wanted = jnp.where(row_id == j, chosen[j], wanted)
    mask = owned(place, lengths, jnp.broadcast_to(seg, (2 * PAIRS, WIN)))
    onehot = jnp.where((wanted == seg) & mask, 1.0, 0.0)
    count = jnp.maximum(jnp.sum(onehot, axis=1, keepdims=True), 1.0)
    hot = onehot.astype(BF16)
    pooled = (nn(hot, ench[...]) + nn(hot, encl[...])) / count
    inverse_len = lax.rsqrt(jnp.sum(pooled * pooled, axis=1, keepdims=True) + POOL_EPS)
    unit[...] = pooled * inverse_len
    uscale[...] = jnp.broadcast_to(inverse_len / count, (2 * PAIRS, 128))


def mlp(place, lengths, chosen, att, tokens, segr, vec, halves):
    return call(
        mlp_kernel,
        [(1, place), (1, lengths), (1, chosen), (0, att), (0, tokens), (0, segr), (0, vec)]
        + [(0, h) for h in halves],
        [
            ((WIN, D), F32),
            ((WIN, 128), F32),
            ((WIN, D), BF16),
            ((WIN, FF), BF16),
            ((WIN, FF), F32),
            ((WIN, D), F32),
            ((WIN, 128), F32),
            ((2 * PAIRS, D), F32),
            ((2 * PAIRS, 128), F32),
        ],
        [
            pltpu.VMEM((D, D), BF16),
            pltpu.VMEM((D, FF), BF16),
            pltpu.VMEM((D, FF), BF16),
            pltpu.VMEM((WIN, D), BF16),
            pltpu.VMEM((WIN, D), BF16),
        ],
        micros=10,
        name="mlp",
    )


def split_rows(grad, keep, send, place, *at):
    opt = place[0]
    for c in range(4):
        index = (c ^ place[1],) + at
        keep[index] = grad[aligned(HALF * opt + CHUNK * c, CHUNK, 16), :].astype(BF16)
        send[index] = grad[aligned(HALF * (1 - opt) + CHUNK * c, CHUNK, 16), :].astype(BF16)


def column_sums(value):
    return jnp.sum(value.reshape(-1, 8, D), axis=0)


def norm_backward(grad_at, normed_ref, inverse_ref, gain, out, low_out, sums, at, step=ROWS):
    def block(i, carry):
        scale_sum, shift_sum, bias_sum = carry
        r = aligned(i * step, step, 64)
        g = grad_at(r)
        normed = normed_ref[r, :]
        scaled = g * gain
        inner = (
            scaled
            - jnp.mean(scaled, axis=1, keepdims=True)
            - normed * jnp.mean(scaled * normed, axis=1, keepdims=True)
        ) * inverse_ref[r, 0:1]
        out[r, :] = inner
        low_out[r, :] = inner.astype(BF16)
        return (
            scale_sum + column_sums(g * normed),
            shift_sum + column_sums(g),
            bias_sum + column_sums(inner),
        )

    zero = jnp.zeros((8, D), F32)
    scale_sum, shift_sum, bias_sum = lax.fori_loop(0, WIN // step, block, (zero, zero, zero))
    sums[at : at + 1, :] = jnp.sum(bias_sum, axis=0, keepdims=True)
    sums[at + 1 : at + 2, :] = jnp.sum(scale_sum, axis=0, keepdims=True)
    sums[at + 2 : at + 3, :] = jnp.sum(shift_sum, axis=0, keepdims=True)


def down_kernel(
    count, order, place, lengths, chosen, units, segc, uscale, xhat2, inv2, act, vec, *rest
):
    pieces, (dsec, dlow, keep, send, sums, queries, docs, marks, grad) = rest[:-9], rest[-9:]
    me = place[2]
    per = pieces[0].shape[0]
    for p, piece in enumerate(pieces):
        for j in range(per):
            at = order[p * per + j]
            r = slice(at * PAIRS, (at + 1) * PAIRS)
            both = piece[j].astype(F32)
            queries[r, :] = both[0:PAIRS, 0:D]
            docs[r, :] = both[PAIRS : 2 * PAIRS, 0:D]
            marks[r, :] = both[0:PAIRS, D : D + 128]
    total = count * PAIRS
    q = queries[...].astype(BF16)
    d = docs[...].astype(BF16)
    logits = SCORE_SCALE * nt(q, d)
    peak = jnp.max(logits, axis=1, keepdims=True)
    powers = jnp.exp(logits - peak)
    soft = powers / jnp.sum(powers, axis=1, keepdims=True)
    col = iota((total, total), 1)
    doc_id = ((col // PAIRS) ^ me) * PAIRS + lax.rem(col, PAIRS)
    hit = (marks[:, 0:1] * 32.0 + marks[:, 64:65]).astype(jnp.int32) == doc_id
    d_logits = (soft - jnp.where(hit, 1.0, 0.0)) * (SCORE_SCALE / total)
    high, rest_low = low_pair(d_logits[0:PAIRS, :])
    d_q = nn(high, d) + nn(rest_low, d)
    high, rest_low = low_pair(d_logits[:, 0:128].T[0:PAIRS, :])
    d_d = nn(high, q) + nn(rest_low, q)
    d_units = jnp.concatenate([d_q, d_d], axis=0)
    u = units[...]
    d_pool = uscale[:, 0:1] * (d_units - u * jnp.sum(u * d_units, axis=1, keepdims=True))
    lane = iota((8, 2 * PAIRS), 1)
    wanted = jnp.zeros((8, 2 * PAIRS), jnp.int32)
    for j in range(2 * PAIRS):
        wanted = jnp.where(lane == j, chosen[j], wanted)
    seg = segc[:, 0 : 2 * PAIRS]
    mask = owned(place, lengths, seg)
    hot = jnp.where((seg == wanted[0:1, :]) & mask, 1.0, 0.0).astype(BF16)
    high, rest_low = low_pair(d_pool)
    dsec[...] = nn(hot, high) + nn(hot, rest_low)
    norm_backward(lambda r: dsec[r, :], xhat2, inv2, vec[10:11, :], dsec, dlow, sums, 0)
    sums[3:8, :] = jnp.zeros((5, D), F32)
    for c in range(3):
        cols = slice(c * 512, (c + 1) * 512)
        grad[:, cols] = tn(dlow[...], act[:, cols])
    for c in range(4):
        split_rows(grad.at[:, c * D : (c + 1) * D], keep, send, place, c)


def down_backward(count, order, place, lengths, chosen, units, segc, uscale, saved, vec, pieces, after):
    total = count * PAIRS
    return call(
        functools.partial(down_kernel, count, order),
        [(1, place), (1, lengths), (1, chosen), (0, units), (0, segc), (0, uscale)]
        + [(0, s) for s in saved]
        + [(0, vec)]
        + [(0, p) for p in pieces],
        [
            ((WIN, D), F32),
            ((WIN, D), BF16),
            ((4, 4, CHUNK, D), BF16),
            ((4, 4, CHUNK, D), BF16),
            ((8, D), F32),
        ],
        [
            pltpu.VMEM((total, D), F32),
            pltpu.VMEM((total, D), F32),
            pltpu.VMEM((total, 128), F32),
            pltpu.VMEM((D, FF), F32),
        ],
        micros=4,
        name="down_backward",
        after=after,
    )


def up_kernel(place, dlow, slope, hlow, wd_own, wd_other, dup, keep, send, sums, wd, grad):
    opt = place[0]
    assemble(wd, wd_own, wd_other, opt)
    for c in range(3):
        cols = slice(c * 512, (c + 1) * 512)
        part = (nn(dlow[...], wd[:, cols]) * slope[:, cols]).astype(BF16)
        dup[:, cols] = part
        column_sum = jnp.sum(part.astype(F32), axis=0, keepdims=True)
        for j in range(4):
            at = 512 * c + 128 * j
            sums[at // D : at // D + 1, at % D : at % D + 128] = column_sum[:, 128 * j : 128 * j + 128]
        grad[:, cols] = tn(hlow[...], dup[:, cols])
    for c in range(4):
        split_rows(grad.at[:, c * D : (c + 1) * D], keep, send, place, c)


def up_backward(place, dlow, slope, hlow, halves, after):
    return call(
        up_kernel,
        [(1, place)] + [(0, a) for a in (dlow, slope, hlow) + tuple(halves)],
        [((WIN, FF), BF16), ((4, 4, CHUNK, D), BF16), ((4, 4, CHUNK, D), BF16), ((4, D), F32)],
        [pltpu.VMEM((D, FF), BF16), pltpu.VMEM((D, FF), F32)],
        micros=3,
        name="up_backward",
        after=after,
    )


def first_kernel(
    place, dup, dsec, xhat1, inv1, att, vec, wu_own, wu_other, wo_own, wo_other,
    dfirst, datt, delta, okeep, osend, sums, wu, wo, grad, dlow,
):
    opt = place[0]
    assemble(wu, wu_own, wu_other, opt)
    assemble(wo, wo_own, wo_other, opt)
    norm_backward(
        lambda r: nt(dup[r, :], wu[...]) + dsec[r, :],
        xhat1, inv1, vec[8:9, :], dfirst, dlow, sums, 0, WIDE_ROWS,
    )
    sums[3:8, :] = jnp.zeros((5, D), F32)
    grad[...] = tn(att[...], dlow[...])
    split_rows(grad, okeep, osend, place)
    da = nt(dlow[...], wo[...]).astype(BF16)
    datt[0:WIN, :] = da
    datt[WIN:PAD, :] = jnp.zeros((PAD - WIN, D), BF16)
    high, rest = low_pair(da.astype(F32) * att[...].astype(F32))
    heads = (iota((16, D), 1) // HD == iota((16, D), 0)).astype(F32).astype(BF16)
    delta[:, 0:WIN] = nt(heads, high) + nt(heads, rest)
    delta[:, WIN:PAD] = jnp.zeros((16, PAD - WIN), F32)


def first_backward(place, dup, dsec, xhat1, inv1, att, vec, halves, after):
    return call(
        first_kernel,
        [(1, place)] + [(0, a) for a in (dup, dsec, xhat1, inv1, att, vec) + tuple(halves)],
        [
            ((WIN, D), F32),
            ((PAD, D), BF16),
            ((16, PAD), F32),
            ((4, CHUNK, D), BF16),
            ((4, CHUNK, D), BF16),
            ((8, D), F32),
        ],
        [
            pltpu.VMEM((D, FF), BF16),
            pltpu.VMEM((D, D), BF16),
            pltpu.VMEM((D, D), F32),
            pltpu.VMEM((WIN, D), BF16),
        ],
        micros=3,
        name="first_backward",
        after=after,
    )


def heads_kernel(g, place, tokens, proj, datt, lse, delta, segc, segr, *rest):
    rest, (dproj, keep, send, sums, kt, dk, dv, grad, ktmp, stmp) = rest[:-10], rest[-10:]

    def lanes(part):
        return slice(part * D + 128 * g, part * D + 128 * g + 128)

    for t in range(PAD // 128):
        kt[:, 128 * t : 128 * t + 128] = (
            proj[128 * t : 128 * t + 128, lanes(1)].astype(F32).T.astype(BF16)
        )
    dk[...] = jnp.zeros_like(dk)
    dv[...] = jnp.zeros_like(dv)
    for q0, k0, k1 in BANDS:
        qs = head_stack(proj[q0 : q0 + BLOCK, lanes(0)])
        gs = head_stack(datt[q0 : q0 + BLOCK, lanes(0)])
        st = nt(proj[k0:k1, lanes(1)], qs)
        dp = nt(proj[k0:k1, lanes(2)], gs)
        same = segc[k0:k1, :] == segr[0:1, q0 : q0 + BLOCK]
        bias = jnp.where(same, 0.0, NEG_BIG)
        probs, d_scores, dq = [], [], []
        for j in range(4):
            cols = slice(j * BLOCK, (j + 1) * BLOCK)
            prob = jnp.exp2(st[:, cols] * EXP2_SCALE + bias - lse[g, j : j + 1, q0 : q0 + BLOCK])
            ds = prob * (dp[:, cols] - delta[4 * g + j : 4 * g + j + 1, q0 : q0 + BLOCK])
            ds = ds.astype(BF16)
            probs.append(prob.astype(BF16))
            d_scores.append(ds)
            dq.append(nn(kt[j * HD : (j + 1) * HD, k0:k1], ds))
        dv[k0:k1, :] += nn(jnp.concatenate(probs, axis=1), gs)
        dk[k0:k1, :] += nn(jnp.concatenate(d_scores, axis=1), qs)
        rows = min(BLOCK, WIN - q0)
        dqs = jnp.concatenate(dq, axis=0).T[0:rows] * HD ** (-0.5)
        dproj[q0 : q0 + rows, 0:128] = dqs.astype(BF16)
    dproj[:, 128:256] = (dk[...] * HD ** (-0.5)).astype(BF16)
    dproj[:, 256:384] = dv[...].astype(BF16)
    grad[...] = tn(tokens[aligned(OFF * place[0], WIN, 64), :], dproj[...])
    q_sum = jnp.sum(dproj[:, 0:128].astype(F32), axis=0, keepdims=True)
    v_sum = jnp.sum(dproj[:, 256:384].astype(F32), axis=0, keepdims=True)
    sums[0:1, :] = q_sum
    sums[1:2, :] = v_sum
    sums[2:8, :] = jnp.zeros((6, 128), F32)
    if g < 2:
        split_rows(grad, keep, send, place)
        return
    parts, (dsums, usums, fsums, zero, one) = rest[:4], rest[4:]
    split_rows(grad, ktmp, stmp, place)
    for dst, blocks in (
        (keep, (parts[0], parts[2], ktmp)),
        (send, (parts[1], parts[3], stmp)),
    ):
        for h, part in enumerate(blocks):
            for c in range(3):
                dst[:, :, D * c + 128 * h : D * c + 128 * h + 128] = part[
                    :, :, 128 * c : 128 * c + 128
                ]
    rows = jnp.concatenate(
        [
            jnp.concatenate([zero[0:1], one[0:1], q_sum], axis=1),
            jnp.concatenate([zero[1:2], one[1:2], v_sum], axis=1),
            fsums[0:1, :],
            usums[0:4, :],
            dsums[0:1, :],
            fsums[1:3, :],
            dsums[1:3, :],
            jnp.zeros((4, D), F32),
        ],
        axis=0,
    ).astype(BF16)
    for c in range(4):
        for j in range(3):
            block = rows[:, 128 * j : 128 * j + 128]
            keep[c, 16 * j : 16 * j + 16, 3 * D : 3 * D + 128] = block
            send[c, 16 * j : 16 * j + 16, 3 * D : 3 * D + 128] = block


def heads_backward(g, place, ins, more, after):
    part = ((4, CHUNK, 3 * D + 128 if g == 2 else D), BF16)
    return call(
        functools.partial(heads_kernel, g),
        [(1, place)] + [(0, a) for a in tuple(ins) + tuple(more)],
        [((WIN, D), BF16), part, part, ((8, 128), F32)],
        [
            pltpu.VMEM((128, PAD), BF16),
            pltpu.VMEM((WIN, 128), F32),
            pltpu.VMEM((WIN, 128), F32),
            pltpu.VMEM((D, D), F32),
            pltpu.VMEM((4, CHUNK, D), BF16),
            pltpu.VMEM((4, CHUNK, D), BF16),
        ],
        micros=3,
        name="heads_backward",
        after=after,
    )


def input_kernel(place, dp0, dp1, dp2, dfirst, w_own, w_other, igrad, wfull, dproj):
    assemble(wfull, w_own, w_other, place[0])
    for g, part in enumerate((dp0, dp1, dp2)):
        for c in range(3):
            dproj[:, c * D + 128 * g : c * D + 128 * g + 128] = part[:, 128 * c : 128 * c + 128]
    igrad[...] = (nt(dproj[...], wfull[...]) + dfirst[...]).astype(BF16)


def input_backward(place, parts, dfirst, w_own, w_other, after):
    return call(
        input_kernel,
        [(1, place)] + [(0, a) for a in tuple(parts) + (dfirst, w_own, w_other)],
        [((WIN, D), BF16)],
        [pltpu.VMEM((D, 3 * D), BF16), pltpu.VMEM((WIN, 3 * D), BF16)],
        micros=2,
        name="input_backward",
        after=after,
    )[0]


def flips(axis, size, bits):
    return [(i, i ^ bits) for i in range(size)]


def pair(value):
    return swap(value, "opt", 2, 1)


def swap(value, axis, size, bits):
    return lax.ppermute(value, axis, flips(axis, size, bits))


def bit_groups(size):
    bits = size.bit_length() - 1
    return [(s, 1 << min(2, bits - s)) for s in range(0, bits, 2)]


def trades(values, n, shift):
    return [values[0]] + [swap(values[k], "dp", n, k << shift) for k in (1, 2, 3)]


def added(a, b):
    return (a.astype(F32) + b.astype(F32)).astype(BF16)


def core_sum_kernel(*refs):
    ins, outs = refs[:-4], refs[-4:]
    for r, out in enumerate(outs):
        if len(ins) == 2:
            out[...] = added(ins[0][r], ins[1][r])
        else:
            out[0:4] = added(ins[0][r], ins[1][r])
            out[4] = added(ins[2][r], ins[3][r])


def core_sum(parts, after):
    shape = parts[0].shape[1:]
    if len(parts) == 4:
        shape = (5,) + shape[1:]
    return call(
        core_sum_kernel, [(0, p) for p in parts], [(shape, BF16)] * 4, name="core_sum", vmem=4, after=after
    )


def total_of(refs, at):
    a, b, c, d = (ref[at].astype(F32) for ref in refs)
    return ((a + b) + (c + d)).astype(BF16)


def down_plane_kernel(a, b, c, d, out):
    out[...] = (a[...].astype(F32) + b[...].astype(F32)) + (c[...].astype(F32) + d[...].astype(F32))


def down_plane_sum(parts, after):
    return call(
        down_plane_kernel,
        [(0, p) for p in parts],
        [(parts[0].shape, F32)],
        name="down_plane_sum",
        vmem=4,
        after=after,
    )[0]


def wide_plane_kernel(place, down, *refs):
    up, outs = refs[:4], refs[4:]
    single = total_of(up, 4)
    for k, out in enumerate(outs):
        out[0] = down[place[3] ^ k].astype(BF16)
        out[1] = total_of(up, place[3] ^ k)
        out[2] = single


def wide_plane_sum(place, parts, after):
    return call(
        wide_plane_kernel,
        [(1, place)] + [(0, p) for p in parts],
        [((3, CHUNK, D), BF16)] * 4,
        name="wide_plane_sum",
        vmem=4,
        after=after,
    )


def wide_line_kernel(a, b, c, d, pair_out, single):
    refs = (a, b, c, d)
    pair_out[...] = total_of(refs, slice(0, 2))
    single[...] = total_of(refs, slice(2, 3))


def wide_line_sum(parts, after):
    return call(
        wide_line_kernel,
        [(0, p) for p in parts],
        [((2, CHUNK, D), BF16), ((1, CHUNK, D), BF16)],
        name="wide_line_sum",
        vmem=4,
        after=after,
    )


def low_plane_kernel(a, b, c, d, out):
    out[...] = total_of((a, b, c, d), slice(None))


def low_plane_sum(parts, after=()):
    return call(
        low_plane_kernel,
        [(0, p) for p in parts],
        [(parts[0].shape, BF16)],
        name="low_plane_sum",
        vmem=4,
        after=after,
    )[0]


def low_next_kernel(keep, other, out):
    out[...] = added(keep[...], other[...])


def low_next(keep, other, after=()):
    return call(
        low_next_kernel,
        [(0, keep), (0, other)],
        [(keep.shape, BF16)],
        name="low_next",
        vmem=4,
        after=after,
    )[0]


def low_last_kernel(keep, other, out, vgrad):
    out[...] = added(keep[:, 0 : 3 * D], other[:, 0 : 3 * D])
    vgrad[...] = added(keep[:, 3 * D : 3 * D + 128], other[:, 3 * D : 3 * D + 128])


def low_last(keep, other, after):
    return call(
        low_last_kernel,
        [(0, keep), (0, other)],
        [((CHUNK, 3 * D), BF16), ((CHUNK, 128), BF16)],
        name="low_last",
        vmem=4,
        after=after,
    )


def chain_kernel(*refs):
    ins, out = refs[:-1], refs[-1]
    at = 0
    for ref in ins:
        flat = ref.reshape(-1, CHUNK, D)
        out[at : at + flat.shape[0]] = flat[...]
        at += flat.shape[0]


def chain(parts, after=()):
    count = sum(p.size for p in parts) // (CHUNK * D)
    return call(
        chain_kernel,
        [(0, p) for p in parts],
        [((count, CHUNK, D), BF16)],
        name="chain",
        vmem=4,
        after=after,
    )[0]


def rest_sum(value, n):
    bit = 16
    while bit < n:
        other = swap(value, "dp", n, bit)
        value = (value.astype(F32) + other.astype(F32)).astype(BF16)
        bit *= 2
    return value


def join_kernel(*refs):
    ins, out = refs[:-1], refs[-1]
    for i, ref in enumerate(ins):
        out[i] = ref[...]


def join(parts, after=()):
    return call(
        join_kernel,
        [(0, p) for p in parts],
        [((len(parts),) + parts[0].shape, parts[0].dtype)],
        name="join",
        vmem=4,
        after=after,
    )[0]


def pack_kernel(place, targets, unit, other, units, packed):
    both = unit[...] + other[...]
    units[...] = both
    row = iota((2 * PAIRS, 128), 0)
    marks = jnp.zeros((2 * PAIRS, 128), jnp.int32)
    for j in range(PAIRS):
        marks = jnp.where(row == j, targets[j], marks)
    marks = jnp.where(iota((2 * PAIRS, 128), 1) < 64, marks >> 5, marks & 31)
    packed[:, 0:D] = both.astype(BF16)
    packed[:, D : D + 128] = marks.astype(F32).astype(BF16)


def pack(place, targets, unit, other):
    return call(
        pack_kernel,
        [(1, place), (1, targets), (0, unit), (0, other)],
        [(unit.shape, F32), ((2 * PAIRS, D + 128), BF16)],
        name="pack",
        vmem=4,
    )


def squares_of(parts):
    acc = jnp.zeros((8, D), F32)
    for part in parts:
        flat = part.reshape(-1, CHUNK, part.shape[-1])
        for k in range(flat.shape[0]):
            for c in range(0, part.shape[-1], D):
                v = flat[k, :, c : c + D].astype(F32)
                acc = acc + jnp.sum((v * v).reshape(CHUNK // 8, 8, D), axis=0)
    return acc[:, 0:128] + acc[:, 128:256] + acc[:, 256:384]


def wide_squares_kernel(*refs):
    refs[-1][...] = squares_of(refs[:-1])


def squares_kernel(place, *refs):
    parts, (vgrad, before, out) = refs[:-3], refs[-3:]
    acc = squares_of(parts) + before[...]
    row = iota((16, 128), 0)
    low_row = 6 * place[0]
    mine = (row >= low_row) & (row < low_row + 6)
    for j in range(3):
        v = jnp.where(mine, vgrad[16 * j : 16 * j + 16, :].astype(F32), 0.0)
        v = v * v
        acc = acc + (v[0:8] + v[8:16])
    out[...] = acc


def squares(place, parts, vgrad=None, before=None, after=()):
    ins = [(0, p) for p in parts]
    kernel = wide_squares_kernel
    if before is not None:
        ins = [(1, place)] + ins + [(0, vgrad), (0, before)]
        kernel = squares_kernel
    return call(kernel, ins, [((8, 128), F32)], name="squares", vmem=4, after=after)[0]


def merge_kernel(place, igrad, other, out, flag):
    flag[...] = jnp.zeros((8, 128), F32)

    @pl.when(place[0] == 0)
    def low_core():
        out[0:OFF, :] = igrad[0:OFF, :]
        out[OFF:WIN, :] = added(igrad[OFF:WIN, :], other[0 : WIN - OFF, :])
        out[WIN:SEQ, :] = other[WIN - OFF : WIN, :]

    @pl.when(place[0] != 0)
    def high_core():
        out[0:OFF, :] = other[0:OFF, :]
        out[OFF:WIN, :] = added(other[OFF:WIN, :], igrad[0 : WIN - OFF, :])
        out[WIN:SEQ, :] = igrad[WIN - OFF : WIN, :]


def merge(place, igrad, other, after):
    return call(
        merge_kernel,
        [(1, place), (0, igrad), (0, other)],
        [((SEQ, D), BF16), ((8, 128), F32)],
        name="merge",
        vmem=4,
        after=after,
    )


def adamw(parameter, first_state, second, clipped, rate):
    first_new = first_state + (1.0 - BETA_ONE) * clipped
    second_new = second + (1.0 - BETA_TWO) * clipped * clipped
    root = (1.0 - BETA_TWO**STEP) ** 0.5
    below = pl.reciprocal(second_new * lax.rsqrt(second_new) + ADAM_EPS * root)
    scale = rate * root / (1.0 - BETA_ONE**STEP)
    return parameter - scale * (first_new * below), first_new, second_new


def decay_kernel(w, m, v, pv, pm, pq, nw, nm, nv, npv, npm, npq):
    for ins, outs, rate in (
        ((w, m, v), (nw, nm, nv), LEARN_RATE),
        ((pv, pm, pq), (npv, npm, npq), VECTOR_RATE),
    ):
        for ref, out, scale in zip(ins, outs, (1.0 - rate * DECAY_RATE, BETA_ONE, BETA_TWO)):
            out[...] = ref[...] * scale


def decay(arrays, after):
    return call(
        decay_kernel,
        [(0, a) for a in arrays],
        [(a.shape, F32) for a in arrays],
        name="decay",
        vmem=4,
        after=after,
    )


def adamw_kernel(place, *refs):
    sums, refs = refs[:2], refs[2:]
    (vgrad, w, m, v, pv, pm, pq), refs = refs[:7], refs[7:]
    wide, low, refs = refs[:4], refs[4:8], refs[8:]
    outs, (npv, npm, npq, norm), scrs, sems = refs[:4], refs[4:8], refs[8:12], refs[12]
    opt = place[0]
    total = sums[0][...] + sums[1][...]
    total = jnp.sum(jnp.sum(total, axis=1, keepdims=True), axis=0, keepdims=True)
    grad_norm = jnp.sqrt(total)
    factor = jnp.minimum(1.0, CLIP_NORM / (grad_norm + 1e-06))
    norm[...] = grad_norm
    for j in range(3):
        cols = slice(128 * j, 128 * j + 128)
        g = vgrad[16 * j : 16 * j + 16, :].astype(F32)
        g = jnp.where(opt == 0, g[0:6], g[6:12])
        a, b, c = adamw(pv[:, cols], pm[:, cols], pq[:, cols], g * factor, VECTOR_RATE)
        npv[:, cols] = a
        npm[:, cols] = b
        npq[:, cols] = c
    copies = []

    def block(grad, rows, cols):
        new = adamw(w[rows, cols], m[rows, cols], v[rows, cols], grad * factor, LEARN_RATE)
        for scr, value in zip(scrs, new + (new[0].astype(BF16),)):
            scr[rows, cols] = value

    for r in range(4):
        base = CHUNK * (place[1] ^ r)

        def rows_of(i, carry, r=r, base=base):
            rows = aligned(base + i * 16, 16, 16)
            here = aligned(i * 16, 16, 16)
            for k in range(4):
                at = D * (place[3] ^ k)
                for p, start in enumerate((4 * D + FF, 4 * D)):
                    grad = wide[r][2 * k + p, here, :].astype(F32)
                    block(grad, rows, aligned(start + at, D, 128))
            grad = wide[r][8, here, :].astype(F32)
            block(grad, rows, slice(3 * D, 4 * D))
            for c in range(3):
                grad = low[r][here, D * c : D * c + D].astype(F32)
                block(grad, rows, slice(D * c, D * c + D))
            return carry

        lax.fori_loop(0, CHUNK // 16, rows_of, 0)
        rows = aligned(base, CHUNK, 16)
        for i, (scr, out) in enumerate(zip(scrs, outs)):
            copy = pltpu.make_async_copy(scr.at[rows, :], out.at[rows, :], sems.at[r, i])
            copy.start()
            copies.append(copy)
    for copy in copies:
        copy.wait()


def update(place, sums, vgrad, w, m, v, pv, pm, pq, parts):
    ins = tuple(sums) + (vgrad, w, m, v, pv, pm, pq) + tuple(parts)
    shapes = [(w.shape, F32)] * 3 + [(w.shape, BF16)] + [(pv.shape, F32)] * 3 + [((1, 1), F32)]
    return pl.pallas_call(
        adamw_kernel,
        out_shape=[jax.ShapeDtypeStruct(s, d) for s, d in shapes],
        in_specs=[SMEM] + [VMEM] * len(ins),
        out_specs=[ANY] * 4 + [VMEM] * 4,
        scratch_shapes=[
            pltpu.VMEM(w.shape, F32),
            pltpu.VMEM(w.shape, F32),
            pltpu.VMEM(w.shape, F32),
            pltpu.VMEM(w.shape, BF16),
            pltpu.SemaphoreType.DMA((4, 4)),
        ],
        compiler_params=pltpu.CompilerParams(vmem_limit_bytes=16 << 20),
        cost_estimate=pl.CostEstimate(
            flops=4000000000, bytes_accessed=26 * w.size, transcendentals=0
        ),
        name="adamw",
    )(place, *ins)


def shards(
    n,
    tokens,
    lengths,
    query_index,
    doc_index,
    targets,
    weights,
    first_moment,
    second_moment,
    vectors,
    vec_first,
    vec_second,
):
    opt = lax.axis_index("opt")
    me = lax.axis_index("dp")
    place = jnp.stack([opt, me & 3, me, (me >> 2) & 3]).astype(jnp.int32)
    lengths = lengths.reshape(SEGS)
    chosen = jnp.concatenate([query_index, doc_index])
    groups = bit_groups(n)

    w_own = weights[:, : 3 * D].astype(BF16)
    w_other = pair(w_own)
    v_other = pair(vectors)
    later, w_own = lax.optimization_barrier((weights, w_own))
    wo_own = later[:, 3 * D : 4 * D].astype(BF16)
    wu_own = later[:, 4 * D : 4 * D + FF].astype(BF16)
    wd_own = later[:, 4 * D + FF :].astype(BF16)
    wo = (wo_own, pair(wo_own))
    wu = (wu_own, pair(wu_own))
    wd = (wd_own, pair(wd_own))

    proj, att, lse, segc, segr, vec = attend(
        place, lengths, tokens, w_own, w_other, vectors, v_other
    )
    xhat1, inv1, hlow, act, slope, xhat2, inv2, unit, uscale = mlp(
        place, lengths, chosen, att, tokens, segr, vec, wo + wu + wd
    )
    units, packed = pack(place, targets, unit, swap(unit, "opt", 2, 1))
    groups = bit_groups(n)
    order = [0]
    stack = packed
    for i, (shift, size) in enumerate(groups[1:] + groups[:1]):
        pieces = [stack] + [swap(stack, "dp", n, k << shift) for k in range(1, size)]
        order = [o | (k << shift) for k in range(size) for o in order]
        if i < len(groups) - 1:
            stack = join(pieces).reshape(-1, 2 * PAIRS, D + 128)
    decayed = decay(
        (weights, first_moment, second_moment, vectors, vec_first, vec_second), [packed]
    )
    dsec, dlow, keep, send, dsums = down_backward(
        n, order, place, lengths, chosen, units, segc, uscale, (xhat2, inv2, act), vec, pieces,
        decayed,
    )
    other = pair(send)
    dup, ukeep, usend, usums = up_backward(place, dlow, slope, hlow, wd, [])
    down = core_sum((keep, other), [dup])
    down_got = trades(down, n, 0)
    uother = pair(usend)
    dfirst, datt, delta, okeep, osend, fsums = first_backward(
        place, dup, dsec, xhat1, inv1, att, vec, wu + wo, [down[0]]
    )
    oother = pair(osend)
    down = down_plane_sum(down_got, [dfirst])
    up = core_sum((ukeep, uother, okeep, oother), [down])
    up_got = trades(up, n, 0)
    ins = (tokens, proj, datt, lse, delta, segc, segr)
    part0, keep0, send0, sums0 = heads_backward(0, place, ins, (), [up[0]])
    part1, keep1, send1, sums1 = heads_backward(1, place, ins, (), [part0])
    wide = wide_plane_sum(place, [down] + up_got, [part1])
    wide_got = trades(wide, n, 2)
    part2, keep, send, _ = heads_backward(
        2, place, ins, (keep0, send0, keep1, send1, dsums, usums, fsums, sums0, sums1),
        [wide[0], part1],
    )
    wide, single = wide_line_sum(wide_got, [part2])
    send, wide, single = lax.optimization_barrier((send, wide, single))
    other = pair(send)
    igrad = input_backward(place, (part0, part1, part2), dfirst, w_own, w_other, [wide])
    iother = pair(igrad)
    low = core_sum((keep, other), [igrad])
    low_got = trades(low, n, 0)
    low, wide, single = lax.optimization_barrier((low[0], wide, single))
    wide, single = rest_sum(wide, n), rest_sum(single, n)
    wide_got = trades([wide] * 4, n, 2)
    low = low_plane_sum(low_got, [low])
    other = swap(low, "dp", n, 4)
    wide = chain(wide_got + [single], [low])
    wide = trades([wide] * 4, n, 0)
    low = low_next(low, other, [wide[0]])
    other = swap(low, "dp", n, 8)
    input_grad, flag = merge(place, igrad, iother, [low])
    low, vgrad = low_last(low, other, [flag])
    low, vgrad = rest_sum(low, n), rest_sum(vgrad, n)
    low = trades([low] * 4, n, 0)
    sums = squares(place, low, vgrad, squares(place, wide, after=[low[0]]))
    sums = (sums, pair(sums))
    pieces = tuple(wide) + tuple(low)
    nw, nm, nv, nlow, npv, npm, npq, norm = update(
        place, sums, vgrad, *decayed, pieces,
    )
    return (norm.reshape(()), input_grad, nw, nm, nv, nlow, npv, npm, npq)


def solution(mesh):
    rows = P("opt", None)
    in_specs = (P("dp", None), P("dp", None), P("dp"), P("dp"), P("dp")) + (rows,) * 6
    out_specs = (P(), P("dp", None)) + (rows,) * 7
    n = mesh.shape["dp"]
    return jax.shard_map(
        functools.partial(shards, n),
        mesh=mesh,
        in_specs=in_specs,
        out_specs=out_specs,
        check_vma=False,
    )
```

```python
import functools

import jax
import jax.numpy as jnp
from jax import lax
from jax.experimental import pallas as pl
from jax.experimental.pallas import tpu as pltpu
from jax.sharding import PartitionSpec as P

D = 384
HEADS = 12
HD = 32
FF = 1536
SEQ = 1024
SEGS = 16
PAIRS = 8
STEP = 10

WIN = 576
OFF = SEQ - WIN
PAD = 640
BLOCK = 128
BANDS = tuple((q, max(0, q - 128), min(WIN, q + 256)) for q in range(0, WIN, BLOCK))
BAND_ROWS = tuple(sum(b[2] - b[1] for b in BANDS[:i]) for i in range(len(BANDS) + 1))
ROWS = 64
WIDE_ROWS = 192
LOG2E = 1.4426950408889634

LN_EPS = 1e-06
POOL_EPS = 1e-06
SCORE_SCALE = 50.0
CLIP_NORM = 0.001
BETA_ONE = 0.9
BETA_TWO = 0.98
ADAM_EPS = 1e-08
LEARN_RATE = 0.05
VECTOR_RATE = 0.3
DECAY_RATE = 0.01
NEG_BIG = -1e30
HALF = D // 2
CHUNK = HALF // 4
EXP2_SCALE = HD ** (-0.5) * 1.4426950408889634

F32 = jnp.float32
BF16 = jnp.bfloat16
VMEM = pl.BlockSpec(memory_space=pltpu.VMEM)
SMEM = pl.BlockSpec(memory_space=pltpu.SMEM)
ANY = pl.BlockSpec(memory_space=pl.ANY)


def nn(a, b):
    return jnp.dot(a, b, preferred_element_type=F32)


def nt(a, b):
    return lax.dot_general(a, b, (((1,), (1,)), ((), ())), preferred_element_type=F32)


def tn(a, b):
    return lax.dot_general(a, b, (((0,), (0,)), ((), ())), preferred_element_type=F32)


def exact(a, b, dims):
    return lax.dot_general(
        a, b, (dims, ((), ())), precision=lax.Precision.HIGHEST, preferred_element_type=F32
    )


def iota(shape, axis):
    return lax.broadcasted_iota(jnp.int32, shape, axis)


def low_pair(value):
    high = value.astype(BF16)
    return high, (value - high.astype(F32)).astype(BF16)


def aligned(start, size, unit):
    return pl.ds(pl.multiple_of(start, unit), size)


def assemble(dst, own, other, opt):
    dst[aligned(HALF * opt, HALF, 64), :] = own[0:HALF, :]
    dst[aligned(HALF * (1 - opt), HALF, 64), :] = other[0:HALF, :]


class Place:
    def __getitem__(self, i):
        if i == 0:
            return lax.axis_index("opt")
        me = lax.axis_index("dp")
        return (me & 3, me, (me >> 2) & 3)[i - 1]


def call(kernel, ins, outs, scratch=(), micros=5, name=None, vmem=12, after=()):
    if ins[0][1] is None:
        kernel = functools.partial(kernel, Place())
        ins = ins[1:]
    specs = [SMEM if s else VMEM for s, _ in ins] + [ANY] * len(after)
    count = len(ins)

    def body(*refs):
        kernel(*refs[:count], *refs[count + len(after) :])

    shapes = [jax.ShapeDtypeStruct(s, d) for s, d in outs]
    moved = sum(a.size * a.dtype.itemsize for _, a in ins)
    moved += sum(s.size * s.dtype.itemsize for s in shapes)
    return pl.pallas_call(
        body,
        out_shape=shapes,
        in_specs=specs,
        out_specs=[VMEM] * len(shapes),
        scratch_shapes=list(scratch),
        compiler_params=pltpu.CompilerParams(vmem_limit_bytes=vmem << 20),
        cost_estimate=pl.CostEstimate(
            flops=micros * 1100000000, bytes_accessed=moved, transcendentals=0
        ),
        name=name,
    )(*[a for _, a in ins], *after)


def head_stack(rows):
    lane_head = iota(rows.shape, 1) // HD
    zero = jnp.zeros_like(rows)
    return jnp.concatenate([jnp.where(lane_head == j, rows, zero) for j in range(4)], axis=0)


def attend_kernel(
    place, lengths, query_index, doc_index, targets, tokens, w_own, w_other, v_own, v_other,
    proj, att, lse, segc, segr, ownc, ownr, wanted, marks, vec, wfull, bias, vt,
):
    opt = place[0]
    assemble(wfull, w_own, w_other, opt)
    mine = v_own[...].astype(BF16).astype(F32)
    others = v_other[...].astype(BF16).astype(F32)
    first = opt == 0
    vec[0:6, :] = jnp.where(first, mine, others)
    vec[6:12, :] = jnp.where(first, others, mine)
    vec[12:16, :] = jnp.zeros((4, D), F32)

    position = iota((8, PAD), 1) + OFF * opt
    segment = jnp.zeros((8, PAD), jnp.int32)
    bound = jnp.int32(0)
    low_count = jnp.int32(0)
    for s in range(SEGS):
        bound = bound + lengths[s]
        segment = segment + (position >= bound).astype(jnp.int32)
        low_count = low_count + (bound <= WIN).astype(jnp.int32)
    mine = (segment < low_count).astype(jnp.int32) == (opt == 0).astype(jnp.int32)
    owned = jnp.where(mine, segment, -1)
    segr[...] = segment
    ownr[...] = owned
    for value, out in ((segment, segc), (owned, ownc)):
        value = value.astype(F32)
        for t in range(PAD // 128):
            rows = min(128, WIN - 128 * t)
            turned = jnp.broadcast_to(value[0:1, 128 * t : 128 * t + 128], (128, 128)).T
            out[128 * t : 128 * t + rows, :] = turned[0:rows].astype(jnp.int32)
    row, col = iota((2 * PAIRS, 128), 0), iota((2 * PAIRS, 128), 1)
    by_row = jnp.zeros((2 * PAIRS, 128), jnp.int32)
    by_col = jnp.zeros((2 * PAIRS, 128), jnp.int32)
    mark = jnp.zeros((2 * PAIRS, 128), jnp.int32)
    for j in range(PAIRS):
        mark = jnp.where(row == j, targets[j], mark)
        for at, index in ((j, query_index), (PAIRS + j, doc_index)):
            by_row = jnp.where(row == at, index[j], by_row)
            by_col = jnp.where(col == at, index[j], by_col)
    wanted[0] = by_row
    wanted[1] = by_col
    marks[...] = jnp.where(col < 64, mark >> 5, mark & 31).astype(F32).astype(BF16)
    for i, (q0, k0, k1) in enumerate(BANDS):
        bias[BAND_ROWS[i] : BAND_ROWS[i + 1], :] = jnp.where(
            segc[k0:k1, :] == segr[0:1, q0 : q0 + BLOCK], 0.0, NEG_BIG
        )

    x = tokens[aligned(OFF * opt, WIN, 64), :]
    for c in range(3):
        acc = nn(x, wfull[:, c * D : (c + 1) * D])
        if c != 1:
            acc = acc + vec[(0 if c == 0 else 1) : (1 if c == 0 else 2), :]
        proj[0:WIN, c * D : (c + 1) * D] = acc.astype(BF16)
    proj[WIN:PAD, :] = jnp.zeros((PAD - WIN, 3 * D), BF16)

    def group(g, carry):
        def lanes(part):
            return aligned(part * D + 128 * g, 128, 128)

        for t in range(PAD // 128):
            vt[:, 128 * t : 128 * t + 128] = (
                proj[128 * t : 128 * t + 128, lanes(2)].astype(F32).T.astype(BF16)
            )
        for i, (q0, k0, k1) in enumerate(BANDS):
            stack = head_stack(proj[q0 : q0 + BLOCK, lanes(0)])
            st = nt(proj[k0:k1, lanes(1)], stack)
            outs = []
            for j in range(4):
                t = (
                    st[:, j * BLOCK : (j + 1) * BLOCK] * EXP2_SCALE
                    + bias[BAND_ROWS[i] : BAND_ROWS[i + 1], :]
                )
                peak = jnp.max(t, axis=0, keepdims=True)
                powers = jnp.exp2(t - peak)
                total = jnp.sum(powers, axis=0, keepdims=True)
                lse[g, j : j + 1, q0 : q0 + BLOCK] = peak + jnp.log2(total)
                o = nn(vt[j * HD : (j + 1) * HD, k0:k1], powers.astype(BF16))
                outs.append(o * (1.0 / total))
            rows = min(BLOCK, WIN - q0)
            att[q0 : q0 + rows, aligned(128 * g, 128, 128)] = (
                jnp.concatenate(outs, axis=0).T[0:rows].astype(BF16)
            )
        return carry

    lax.fori_loop(0, 3, group, 0)


def attend(place, scalars, arrays):
    return call(
        attend_kernel,
        [(1, place)] + [(1, a) for a in scalars] + [(0, a) for a in arrays],
        [
            ((PAD, 3 * D), BF16),
            ((WIN, D), BF16),
            ((3, 4, PAD), F32),
            ((WIN, 128), jnp.int32),
            ((8, PAD), jnp.int32),
            ((WIN, 128), jnp.int32),
            ((8, PAD), jnp.int32),
            ((2, 2 * PAIRS, 128), jnp.int32),
            ((2 * PAIRS, 128), BF16),
            ((16, D), F32),
        ],
        [
            pltpu.VMEM((D, 3 * D), BF16),
            pltpu.VMEM((BAND_ROWS[-1], 128), F32),
            pltpu.VMEM((128, PAD), BF16),
        ],
        micros=8,
        name="attend",
    )


def bias_of(vec, c):
    first, last = 256 * c, 256 * c + 256
    parts = []
    while first < last:
        row, col = divmod(first, D)
        size = min(D - col, last - first)
        parts.append(vec[3 + row : 4 + row, col : col + size])
        first += size
    return parts[0] if len(parts) == 1 else jnp.concatenate(parts, axis=1)


def mlp_kernel(
    place, wanted, att, tokens, ownr, vec, wo_own, wo_other, wu_own, wu_other,
    wd_own, wd_other, xhat1, inv1, hlow, act, slope, xhat2, inv2, unit, uscale,
    wo, wu, wd, ench, encl,
):
    opt = place[0]
    assemble(wo, wo_own, wo_other, opt)
    assemble(wu, wu_own, wu_other, opt)
    assemble(wd, wd_own, wd_other, opt)

    def norm(v):
        centred = v - jnp.mean(v, axis=1, keepdims=True)
        inverse = lax.rsqrt(jnp.mean(centred * centred, axis=1, keepdims=True) + LN_EPS)
        return centred * inverse, inverse

    def block(i, carry):
        r = aligned(i * WIDE_ROWS, WIDE_ROWS, 64)
        x = tokens[aligned(OFF * opt + i * WIDE_ROWS, WIDE_ROWS, 64), :].astype(F32)
        normed, inverse = norm(nn(att[r, :], wo[...]) + vec[2:3, :] + x)
        xhat1[r, :] = normed
        inv1[r, :] = jnp.broadcast_to(inverse, (WIDE_ROWS, 128))
        h = normed * vec[8:9, :] + vec[9:10, :]
        low = h.astype(BF16)
        hlow[r, :] = low
        for c in range(6):
            cols = slice(c * 256, (c + 1) * 256)
            u = nn(low, wu[:, cols]) + bias_of(vec, c)
            half = lax.erf(u * 0.7071067811865476) * 0.5 + 0.5
            act[r, cols] = (u * half).astype(BF16)
            slope[r, cols] = half + u * jnp.exp2(u * u * (-0.5 * LOG2E)) * 0.3989422804014327
        normed, inverse = norm(nt(act[r, :], wd[...]) + vec[7:8, :] + h)
        xhat2[r, :] = normed
        inv2[r, :] = jnp.broadcast_to(inverse, (WIDE_ROWS, 128))
        high, rest = low_pair(normed * vec[10:11, :] + vec[11:12, :])
        ench[r, :] = high
        encl[r, :] = rest
        return carry

    lax.fori_loop(0, WIN // WIDE_ROWS, block, 0)

    onehot = jnp.where(wanted[0, :, 0:1] == ownr[0:1, 0:WIN], 1.0, 0.0)
    count = jnp.maximum(jnp.sum(onehot, axis=1, keepdims=True), 1.0)
    hot = onehot.astype(BF16)
    pooled = (nn(hot, ench[...]) + nn(hot, encl[...])) / count
    inverse_len = lax.rsqrt(jnp.sum(pooled * pooled, axis=1, keepdims=True) + POOL_EPS)
    unit[...] = pooled * inverse_len
    uscale[...] = jnp.broadcast_to(inverse_len / count, (2 * PAIRS, 128))


def mlp(place, wanted, att, tokens, ownr, vec, halves):
    return call(
        mlp_kernel,
        [(1, place), (0, wanted), (0, att), (0, tokens), (0, ownr), (0, vec)]
        + [(0, h) for h in halves],
        [
            ((WIN, D), F32),
            ((WIN, 128), F32),
            ((WIN, D), BF16),
            ((WIN, FF), BF16),
            ((WIN, FF), F32),
            ((WIN, D), F32),
            ((WIN, 128), F32),
            ((2 * PAIRS, D), F32),
            ((2 * PAIRS, 128), F32),
        ],
        [
            pltpu.VMEM((D, D), BF16),
            pltpu.VMEM((D, FF), BF16),
            pltpu.VMEM((D, FF), BF16),
            pltpu.VMEM((WIN, D), BF16),
            pltpu.VMEM((WIN, D), BF16),
        ],
        micros=10,
        name="mlp",
    )


def split_rows(grad, keep, send, place, *at):
    opt = place[0]
    for c in range(4):
        index = (c ^ place[1],) + at
        keep[index] = grad[aligned(HALF * opt + CHUNK * c, CHUNK, 16), :].astype(BF16)
        send[index] = grad[aligned(HALF * (1 - opt) + CHUNK * c, CHUNK, 16), :].astype(BF16)


def column_sums(value):
    return jnp.sum(value.reshape(-1, 8, D), axis=0)


def norm_backward(grad_at, normed_ref, inverse_ref, gain, out, low_out, sums, at, step=ROWS):
    def block(i, carry):
        scale_sum, shift_sum, bias_sum = carry
        r = aligned(i * step, step, 64)
        g = grad_at(r)
        normed = normed_ref[r, :]
        scaled = g * gain
        inner = (
            scaled
            - jnp.mean(scaled, axis=1, keepdims=True)
            - normed * jnp.mean(scaled * normed, axis=1, keepdims=True)
        ) * inverse_ref[r, 0:1]
        out[r, :] = inner
        low_out[r, :] = inner.astype(BF16)
        return (
            scale_sum + column_sums(g * normed),
            shift_sum + column_sums(g),
            bias_sum + column_sums(inner),
        )

    zero = jnp.zeros((8, D), F32)
    scale_sum, shift_sum, bias_sum = lax.fori_loop(0, WIN // step, block, (zero, zero, zero))
    sums[at : at + 1, :] = jnp.sum(bias_sum, axis=0, keepdims=True)
    sums[at + 1 : at + 2, :] = jnp.sum(scale_sum, axis=0, keepdims=True)
    sums[at + 2 : at + 3, :] = jnp.sum(shift_sum, axis=0, keepdims=True)


def down_kernel(
    place, count, order, wanted, units, ownc, uscale, xhat2, inv2, act, vec, *rest
):
    pieces, (dsec, dlow, keep, send, sums, queries, docs, marks, grad) = rest[:-9], rest[-9:]
    me = place[2]
    per = pieces[0].shape[0]
    for p, piece in enumerate(pieces):
        for j in range(per):
            at = order[p * per + j]
            r = slice(at * PAIRS, (at + 1) * PAIRS)
            both = piece[j].astype(F32)
            queries[r, :] = both[0:PAIRS, 0:D]
            docs[r, :] = both[PAIRS : 2 * PAIRS, 0:D]
            marks[r, :] = both[0:PAIRS, D : D + 128]
    total = count * PAIRS
    q = queries[...].astype(BF16)
    d = docs[...].astype(BF16)
    logits = SCORE_SCALE * nt(q, d)
    peak = jnp.max(logits, axis=1, keepdims=True)
    powers = jnp.exp(logits - peak)
    soft = powers / jnp.sum(powers, axis=1, keepdims=True)
    col = iota((total, total), 1)
    doc_id = ((col // PAIRS) ^ me) * PAIRS + lax.rem(col, PAIRS)
    hit = (marks[:, 0:1] * 32.0 + marks[:, 64:65]).astype(jnp.int32) == doc_id
    d_logits = (soft - jnp.where(hit, 1.0, 0.0)) * (SCORE_SCALE / total)
    high, rest_low = low_pair(d_logits[0:PAIRS, :])
    d_q = nn(high, d) + nn(rest_low, d)
    high, rest_low = low_pair(d_logits[:, 0:128].T[0:PAIRS, :])
    d_d = nn(high, q) + nn(rest_low, q)
    d_units = jnp.concatenate([d_q, d_d], axis=0)
    u = units[...]
    d_pool = uscale[:, 0:1] * (d_units - u * jnp.sum(u * d_units, axis=1, keepdims=True))
    hot = jnp.where(ownc[:, 0 : 2 * PAIRS] == wanted[1, 0:1, 0 : 2 * PAIRS], 1.0, 0.0).astype(BF16)
    high, rest_low = low_pair(d_pool)
    dsec[...] = nn(hot, high) + nn(hot, rest_low)
    norm_backward(lambda r: dsec[r, :], xhat2, inv2, vec[10:11, :], dsec, dlow, sums, 0)
    sums[3:8, :] = jnp.zeros((5, D), F32)
    for c in range(3):
        cols = slice(c * 512, (c + 1) * 512)
        grad[:, cols] = tn(dlow[...], act[:, cols])
    for c in range(4):
        split_rows(grad.at[:, c * D : (c + 1) * D], keep, send, place, c)


def down_backward(count, order, place, wanted, units, ownc, uscale, saved, vec, pieces, after):
    total = count * PAIRS
    return call(
        lambda place, *refs: down_kernel(place, count, order, *refs),
        [(1, place), (0, wanted), (0, units), (0, ownc), (0, uscale)]
        + [(0, s) for s in saved]
        + [(0, vec)]
        + [(0, p) for p in pieces],
        [
            ((WIN, D), F32),
            ((WIN, D), BF16),
            ((4, 4, CHUNK, D), BF16),
            ((4, 4, CHUNK, D), BF16),
            ((8, D), F32),
        ],
        [
            pltpu.VMEM((total, D), F32),
            pltpu.VMEM((total, D), F32),
            pltpu.VMEM((total, 128), F32),
            pltpu.VMEM((D, FF), F32),
        ],
        micros=4,
        name="down_backward",
        after=after,
    )


def up_kernel(place, dlow, slope, hlow, wd_own, wd_other, dup, keep, send, sums, wd, grad):
    opt = place[0]
    assemble(wd, wd_own, wd_other, opt)
    for c in range(3):
        cols = slice(c * 512, (c + 1) * 512)
        part = (nn(dlow[...], wd[:, cols]) * slope[:, cols]).astype(BF16)
        dup[:, cols] = part
        column_sum = jnp.sum(part.astype(F32), axis=0, keepdims=True)
        for j in range(4):
            at = 512 * c + 128 * j
            sums[at // D : at // D + 1, at % D : at % D + 128] = column_sum[:, 128 * j : 128 * j + 128]
        grad[:, cols] = tn(hlow[...], dup[:, cols])
    for c in range(4):
        split_rows(grad.at[:, c * D : (c + 1) * D], keep, send, place, c)


def up_backward(place, dlow, slope, hlow, halves, after):
    return call(
        up_kernel,
        [(1, place)] + [(0, a) for a in (dlow, slope, hlow) + tuple(halves)],
        [((WIN, FF), BF16), ((4, 4, CHUNK, D), BF16), ((4, 4, CHUNK, D), BF16), ((4, D), F32)],
        [pltpu.VMEM((D, FF), BF16), pltpu.VMEM((D, FF), F32)],
        micros=3,
        name="up_backward",
        after=after,
    )


def first_kernel(
    place, dup, dsec, xhat1, inv1, att, vec, wu_own, wu_other, wo_own, wo_other,
    dfirst, datt, delta, okeep, osend, sums, wu, wo, grad, dlow,
):
    opt = place[0]
    assemble(wu, wu_own, wu_other, opt)
    assemble(wo, wo_own, wo_other, opt)
    norm_backward(
        lambda r: nt(dup[r, :], wu[...]) + dsec[r, :],
        xhat1, inv1, vec[8:9, :], dfirst, dlow, sums, 0, WIDE_ROWS,
    )
    sums[3:8, :] = jnp.zeros((5, D), F32)
    grad[...] = tn(att[...], dlow[...])
    split_rows(grad, okeep, osend, place)
    da = nt(dlow[...], wo[...]).astype(BF16)
    datt[0:WIN, :] = da
    datt[WIN:PAD, :] = jnp.zeros((PAD - WIN, D), BF16)
    high, rest = low_pair(da.astype(F32) * att[...].astype(F32))
    heads = (iota((16, D), 1) // HD == iota((16, D), 0)).astype(F32).astype(BF16)
    delta[:, 0:WIN] = nt(heads, high) + nt(heads, rest)
    delta[:, WIN:PAD] = jnp.zeros((16, PAD - WIN), F32)


def first_backward(place, dup, dsec, xhat1, inv1, att, vec, halves, after):
    return call(
        first_kernel,
        [(1, place)] + [(0, a) for a in (dup, dsec, xhat1, inv1, att, vec) + tuple(halves)],
        [
            ((WIN, D), F32),
            ((PAD, D), BF16),
            ((16, PAD), F32),
            ((4, CHUNK, D), BF16),
            ((4, CHUNK, D), BF16),
            ((8, D), F32),
        ],
        [
            pltpu.VMEM((D, FF), BF16),
            pltpu.VMEM((D, D), BF16),
            pltpu.VMEM((D, D), F32),
            pltpu.VMEM((WIN, D), BF16),
        ],
        micros=3,
        name="first_backward",
        after=after,
    )


def heads_kernel(place, g, tokens, proj, datt, lse, delta, segc, segr, *rest):
    rest, (dproj, keep, send, sums, kt, dk, dv, grad, ktmp, stmp) = rest[:-10], rest[-10:]

    def lanes(part):
        return slice(part * D + 128 * g, part * D + 128 * g + 128)

    for t in range(PAD // 128):
        kt[:, 128 * t : 128 * t + 128] = (
            proj[128 * t : 128 * t + 128, lanes(1)].astype(F32).T.astype(BF16)
        )
    dk[...] = jnp.zeros_like(dk)
    dv[...] = jnp.zeros_like(dv)
    for q0, k0, k1 in BANDS:
        qs = head_stack(proj[q0 : q0 + BLOCK, lanes(0)])
        gs = head_stack(datt[q0 : q0 + BLOCK, lanes(0)])
        st = nt(proj[k0:k1, lanes(1)], qs)
        dp = nt(proj[k0:k1, lanes(2)], gs)
        same = segc[k0:k1, :] == segr[0:1, q0 : q0 + BLOCK]
        bias = jnp.where(same, 0.0, NEG_BIG)
        probs, d_scores, dq = [], [], []
        for j in range(4):
            cols = slice(j * BLOCK, (j + 1) * BLOCK)
            prob = jnp.exp2(st[:, cols] * EXP2_SCALE + bias - lse[g, j : j + 1, q0 : q0 + BLOCK])
            ds = prob * (dp[:, cols] - delta[4 * g + j : 4 * g + j + 1, q0 : q0 + BLOCK])
            ds = ds.astype(BF16)
            probs.append(prob.astype(BF16))
            d_scores.append(ds)
            dq.append(nn(kt[j * HD : (j + 1) * HD, k0:k1], ds))
        dv[k0:k1, :] += nn(jnp.concatenate(probs, axis=1), gs)
        dk[k0:k1, :] += nn(jnp.concatenate(d_scores, axis=1), qs)
        rows = min(BLOCK, WIN - q0)
        dqs = jnp.concatenate(dq, axis=0).T[0:rows] * HD ** (-0.5)
        dproj[q0 : q0 + rows, 0:128] = dqs.astype(BF16)
    dproj[:, 128:256] = (dk[...] * HD ** (-0.5)).astype(BF16)
    dproj[:, 256:384] = dv[...].astype(BF16)
    grad[...] = tn(tokens[aligned(OFF * place[0], WIN, 64), :], dproj[...])
    q_sum = jnp.sum(dproj[:, 0:128].astype(F32), axis=0, keepdims=True)
    v_sum = jnp.sum(dproj[:, 256:384].astype(F32), axis=0, keepdims=True)
    sums[0:1, :] = q_sum
    sums[1:2, :] = v_sum
    sums[2:8, :] = jnp.zeros((6, 128), F32)
    if g < 2:
        split_rows(grad, keep, send, place)
        return
    parts, (dsums, usums, fsums, zero, one) = rest[:6], rest[6:]
    split_rows(grad, ktmp, stmp, place)
    for dst, out_part, blocks in (
        (keep, parts[0], (parts[2], parts[4], ktmp)),
        (send, parts[1], (parts[3], parts[5], stmp)),
    ):
        dst[:, :, 3 * D : 4 * D] = out_part[...]
        for h, part in enumerate(blocks):
            for c in range(3):
                dst[:, :, D * c + 128 * h : D * c + 128 * h + 128] = part[
                    :, :, 128 * c : 128 * c + 128
                ]
    rows = jnp.concatenate(
        [
            jnp.concatenate([zero[0:1], one[0:1], q_sum], axis=1),
            jnp.concatenate([zero[1:2], one[1:2], v_sum], axis=1),
            fsums[0:1, :],
            usums[0:4, :],
            dsums[0:1, :],
            fsums[1:3, :],
            dsums[1:3, :],
            jnp.zeros((4, D), F32),
        ],
        axis=0,
    ).astype(BF16)
    for c in range(4):
        for j in range(3):
            block = rows[:, 128 * j : 128 * j + 128]
            keep[c, 16 * j : 16 * j + 16, 4 * D : 4 * D + 128] = block
            send[c, 16 * j : 16 * j + 16, 4 * D : 4 * D + 128] = block


def heads_backward(g, place, ins, more, after):
    part = ((4, CHUNK, 4 * D + 128 if g == 2 else D), BF16)
    return call(
        lambda place, *refs: heads_kernel(place, g, *refs),
        [(1, place)] + [(0, a) for a in tuple(ins) + tuple(more)],
        [((WIN, D), BF16), part, part, ((8, 128), F32)],
        [
            pltpu.VMEM((128, PAD), BF16),
            pltpu.VMEM((WIN, 128), F32),
            pltpu.VMEM((WIN, 128), F32),
            pltpu.VMEM((D, D), F32),
            pltpu.VMEM((4, CHUNK, D), BF16),
            pltpu.VMEM((4, CHUNK, D), BF16),
        ],
        micros=3,
        name="heads_backward",
        after=after,
    )


def input_kernel(place, dp0, dp1, dp2, dfirst, w_own, w_other, igrad, wfull, dproj):
    assemble(wfull, w_own, w_other, place[0])
    for g, part in enumerate((dp0, dp1, dp2)):
        for c in range(3):
            dproj[:, c * D + 128 * g : c * D + 128 * g + 128] = part[:, 128 * c : 128 * c + 128]
    igrad[...] = (nt(dproj[...], wfull[...]) + dfirst[...]).astype(BF16)


def input_backward(place, parts, dfirst, w_own, w_other, after):
    return call(
        input_kernel,
        [(1, place)] + [(0, a) for a in tuple(parts) + (dfirst, w_own, w_other)],
        [((WIN, D), BF16)],
        [pltpu.VMEM((D, 3 * D), BF16), pltpu.VMEM((WIN, 3 * D), BF16)],
        micros=2,
        name="input_backward",
        after=after,
    )[0]


def flips(axis, size, bits):
    return [(i, i ^ bits) for i in range(size)]


def pair(value):
    return swap(value, "opt", 2, 1)


def swap(value, axis, size, bits):
    return lax.ppermute(value, axis, flips(axis, size, bits))


def bit_groups(size):
    bits = size.bit_length() - 1
    return [(s, 1 << min(2, bits - s)) for s in range(0, bits, 2)]


def trades(values, n, shift):
    return [values[0]] + [swap(values[k], "dp", n, k << shift) for k in (1, 2, 3)]


def added(a, b):
    return (a.astype(F32) + b.astype(F32)).astype(BF16)


def core_sum_kernel(*refs):
    ins, outs = refs[:-4], refs[-4:]
    for r, out in enumerate(outs):
        if len(ins) == 2:
            out[...] = added(ins[0][r], ins[1][r])
        else:
            out[0:4] = added(ins[0][r], ins[1][r])
            out[4:8] = added(ins[2][r], ins[3][r])


def core_sum(parts, after):
    shape = parts[0].shape[1:]
    if len(parts) == 4:
        shape = (8,) + shape[1:]
    return call(
        core_sum_kernel, [(0, p) for p in parts], [(shape, BF16)] * 4, name="core_sum", vmem=4, after=after
    )


def total_of(refs, at):
    a, b, c, d = (ref[at].astype(F32) for ref in refs)
    return ((a + b) + (c + d)).astype(BF16)


def wide_plane_kernel(place, *refs):
    ins, (mine, send) = refs[:4], refs[4:]
    z = place[3]
    for i, bits in enumerate((0, 2)):
        for p in range(2):
            mine[2 * i + p] = total_of(ins, 4 * p + (z ^ bits))
            send[2 * i + p] = total_of(ins, 4 * p + (z ^ bits ^ 1))


def wide_plane_sum(place, parts, after):
    return call(
        wide_plane_kernel,
        [(1, place)] + [(0, p) for p in parts],
        [((4, CHUNK, D), BF16)] * 2,
        name="wide_plane_sum",
        vmem=4,
        after=after,
    )


def wide_half_kernel(keep, other, mine, send):
    mine[...] = added(keep[0:2], other[0:2])
    send[...] = added(keep[2:4], other[2:4])


def wide_half(keep, other, after):
    return call(
        wide_half_kernel,
        [(0, keep), (0, other)],
        [((2, CHUNK, D), BF16)] * 2,
        name="wide_half",
        vmem=4,
        after=after,
    )


def low_plane_kernel(a, b, c, d, out):
    out[...] = total_of((a, b, c, d), slice(None))


def low_plane_sum(parts, after=()):
    return call(
        low_plane_kernel,
        [(0, p) for p in parts],
        [(parts[0].shape, BF16)],
        name="low_plane_sum",
        vmem=4,
        after=after,
    )[0]


def low_next_kernel(keep, other, out):
    out[...] = added(keep[...], other[...])


def low_next(keep, other, after=()):
    return call(
        low_next_kernel,
        [(0, keep), (0, other)],
        [(keep.shape, BF16)],
        name="low_next",
        vmem=4,
        after=after,
    )[0]


def low_last_kernel(keep, other, out, vgrad):
    out[...] = added(keep[:, 0 : 4 * D], other[:, 0 : 4 * D])
    vgrad[...] = added(keep[:, 4 * D : 4 * D + 128], other[:, 4 * D : 4 * D + 128])


def low_last(keep, other, after):
    return call(
        low_last_kernel,
        [(0, keep), (0, other)],
        [((CHUNK, 4 * D), BF16), ((CHUNK, 128), BF16)],
        name="low_last",
        vmem=4,
        after=after,
    )


def chain_kernel(*refs):
    ins, out = refs[:-1], refs[-1]
    at = 0
    for ref in ins:
        flat = ref.reshape(-1, CHUNK, D)
        out[at : at + flat.shape[0]] = flat[...]
        at += flat.shape[0]


def chain(parts, after=()):
    count = sum(p.size for p in parts) // (CHUNK * D)
    return call(
        chain_kernel,
        [(0, p) for p in parts],
        [((count, CHUNK, D), BF16)],
        name="chain",
        vmem=4,
        after=after,
    )[0]


def rest_sum(value, n):
    bit = 16
    while bit < n:
        other = swap(value, "dp", n, bit)
        value = (value.astype(F32) + other.astype(F32)).astype(BF16)
        bit *= 2
    return value


def join_kernel(*refs):
    ins, out = refs[:-1], refs[-1]
    for i, ref in enumerate(ins):
        out[i] = ref[...]


def join(parts, after=()):
    return call(
        join_kernel,
        [(0, p) for p in parts],
        [((len(parts),) + parts[0].shape, parts[0].dtype)],
        name="join",
        vmem=4,
        after=after,
    )[0]


def pack_kernel(marks, unit, other, units, packed):
    both = unit[...] + other[...]
    units[...] = both
    packed[:, 0:D] = both.astype(BF16)
    packed[:, D : D + 128] = marks[...]


def pack(marks, unit, other):
    return call(
        pack_kernel,
        [(0, marks), (0, unit), (0, other)],
        [(unit.shape, F32), ((2 * PAIRS, D + 128), BF16)],
        name="pack",
        vmem=4,
    )


def squares_of(parts):
    acc = jnp.zeros((8, D), F32)
    for part in parts:
        flat = part.reshape(-1, CHUNK, part.shape[-1])
        for k in range(flat.shape[0]):
            for c in range(0, part.shape[-1], D):
                v = flat[k, :, c : c + D].astype(F32)
                acc = acc + jnp.sum((v * v).reshape(CHUNK // 8, 8, D), axis=0)
    return acc[:, 0:128] + acc[:, 128:256] + acc[:, 256:384]


def wide_squares_kernel(*refs):
    refs[-1][...] = squares_of(refs[:-1])


def squares_kernel(place, *refs):
    parts, (vgrad, before, out) = refs[:-3], refs[-3:]
    acc = squares_of(parts) + before[...]
    row = iota((16, 128), 0)
    low_row = 6 * place[0]
    mine = (row >= low_row) & (row < low_row + 6)
    for j in range(3):
        v = jnp.where(mine, vgrad[16 * j : 16 * j + 16, :].astype(F32), 0.0)
        v = v * v
        acc = acc + (v[0:8] + v[8:16])
    out[...] = acc


def squares(place, parts, vgrad=None, before=None, after=()):
    ins = [(0, p) for p in parts]
    kernel = wide_squares_kernel
    if before is not None:
        ins = [(1, place)] + ins + [(0, vgrad), (0, before)]
        kernel = squares_kernel
    return call(kernel, ins, [((8, 128), F32)], name="squares", vmem=4, after=after)[0]


def merge_kernel(place, igrad, other, out, flag):
    flag[...] = jnp.zeros((8, 128), F32)

    @pl.when(place[0] == 0)
    def low_core():
        out[0:OFF, :] = igrad[0:OFF, :]
        out[OFF:WIN, :] = added(igrad[OFF:WIN, :], other[0 : WIN - OFF, :])
        out[WIN:SEQ, :] = other[WIN - OFF : WIN, :]

    @pl.when(place[0] != 0)
    def high_core():
        out[0:OFF, :] = other[0:OFF, :]
        out[OFF:WIN, :] = added(other[OFF:WIN, :], igrad[0 : WIN - OFF, :])
        out[WIN:SEQ, :] = igrad[WIN - OFF : WIN, :]


def merge(place, igrad, other, after):
    return call(
        merge_kernel,
        [(1, place), (0, igrad), (0, other)],
        [((SEQ, D), BF16), ((8, 128), F32)],
        name="merge",
        vmem=4,
        after=after,
    )


def adamw(parameter, first_state, second, clipped, rate):
    first_new = first_state + (1.0 - BETA_ONE) * clipped
    second_new = second + (1.0 - BETA_TWO) * clipped * clipped
    root = (1.0 - BETA_TWO**STEP) ** 0.5
    below = pl.reciprocal(second_new * lax.rsqrt(second_new) + ADAM_EPS * root)
    scale = rate * root / (1.0 - BETA_ONE**STEP)
    return parameter - scale * (first_new * below), first_new, second_new


def decay_kernel(w, m, v, pv, pm, pq, nw, nm, nv, npv, npm, npq):
    for ins, outs, rate in (
        ((w, m, v), (nw, nm, nv), LEARN_RATE),
        ((pv, pm, pq), (npv, npm, npq), VECTOR_RATE),
    ):
        for ref, out, scale in zip(ins, outs, (1.0 - rate * DECAY_RATE, BETA_ONE, BETA_TWO)):
            out[...] = ref[...] * scale


def decay(arrays, after):
    return call(
        decay_kernel,
        [(0, a) for a in arrays],
        [(a.shape, F32) for a in arrays],
        name="decay",
        vmem=4,
        after=after,
    )


def adamw_kernel(*refs):
    place = Place()
    sums, refs = refs[:2], refs[2:]
    (vgrad, w, m, v, pv, pm, pq), refs = refs[:7], refs[7:]
    wide, low, refs = refs[:4], refs[4:8], refs[8:]
    outs, (npv, npm, npq, norm), scrs, sems = refs[:4], refs[4:8], refs[8:12], refs[12]
    opt = place[0]
    total = sums[0][...] + sums[1][...]
    total = jnp.sum(jnp.sum(total, axis=1, keepdims=True), axis=0, keepdims=True)
    grad_norm = jnp.sqrt(total)
    factor = jnp.minimum(1.0, CLIP_NORM / (grad_norm + 1e-06))
    norm[...] = grad_norm
    for j in range(3):
        cols = slice(128 * j, 128 * j + 128)
        g = vgrad[16 * j : 16 * j + 16, :].astype(F32)
        g = jnp.where(opt == 0, g[0:6], g[6:12])
        a, b, c = adamw(pv[:, cols], pm[:, cols], pq[:, cols], g * factor, VECTOR_RATE)
        npv[:, cols] = a
        npm[:, cols] = b
        npq[:, cols] = c

    def block(grad, rows, cols):
        new = adamw(w[rows, cols], m[rows, cols], v[rows, cols], grad * factor, LEARN_RATE)
        for scr, value in zip(scrs, new + (new[0].astype(BF16),)):
            scr[rows, cols] = value

    def copies(r, i):
        rows = aligned(CHUNK * (place[1] ^ r) + i * 16, 16, 16)
        return [
            pltpu.make_async_copy(scr.at[rows, :], out.at[rows, :], sems.at[3 * r + i, j])
            for j, (scr, out) in enumerate(zip(scrs, outs))
        ]

    for r in range(4):

        def step(i, carry, r=r):
            rows = aligned(CHUNK * (place[1] ^ r) + i * 16, 16, 16)
            here = aligned(i * 16, 16, 16)
            for j, bits in enumerate((0, 2, 1, 3)):
                at = D * (place[3] ^ bits)
                for p, start in enumerate((4 * D + FF, 4 * D)):
                    grad = wide[r][2 * j + p, here, :].astype(F32)
                    block(grad, rows, aligned(start + at, D, 128))
            for c in range(4):
                grad = low[r][here, D * c : D * c + D].astype(F32)
                block(grad, rows, slice(D * c, D * c + D))
            for copy in copies(r, i):
                copy.start()
            return carry

        lax.fori_loop(0, CHUNK // 16, step, 0)
    for r in range(4):

        def finish(i, carry, r=r):
            for copy in copies(r, i):
                copy.wait()
            return carry

        lax.fori_loop(0, CHUNK // 16, finish, 0)


def update(place, sums, vgrad, w, m, v, pv, pm, pq, parts):
    ins = tuple(sums) + (vgrad, w, m, v, pv, pm, pq) + tuple(parts)
    shapes = [(w.shape, F32)] * 3 + [(w.shape, BF16)] + [(pv.shape, F32)] * 3 + [((1, 1), F32)]
    return pl.pallas_call(
        adamw_kernel,
        out_shape=[jax.ShapeDtypeStruct(s, d) for s, d in shapes],
        in_specs=[VMEM] * len(ins),
        out_specs=[ANY] * 4 + [VMEM] * 4,
        scratch_shapes=[
            pltpu.VMEM(w.shape, F32),
            pltpu.VMEM(w.shape, F32),
            pltpu.VMEM(w.shape, F32),
            pltpu.VMEM(w.shape, BF16),
            pltpu.SemaphoreType.DMA((12, 4)),
        ],
        compiler_params=pltpu.CompilerParams(vmem_limit_bytes=16 << 20),
        cost_estimate=pl.CostEstimate(
            flops=4000000000, bytes_accessed=26 * w.size, transcendentals=0
        ),
        name="adamw",
    )(*ins)


def shards(
    n,
    tokens,
    lengths,
    query_index,
    doc_index,
    targets,
    weights,
    first_moment,
    second_moment,
    vectors,
    vec_first,
    vec_second,
):
    place = None
    lengths = lengths.reshape(SEGS)
    groups = bit_groups(n)

    w_own = weights[:, : 3 * D].astype(BF16)
    w_other = pair(w_own)
    v_other = pair(vectors)
    later, w_own = lax.optimization_barrier((weights, w_own))
    wo_own = later[:, 3 * D : 4 * D].astype(BF16)
    wu_own = later[:, 4 * D : 4 * D + FF].astype(BF16)
    wd_own = later[:, 4 * D + FF :].astype(BF16)
    wo = (wo_own, pair(wo_own))
    wu = (wu_own, pair(wu_own))
    wd = (wd_own, pair(wd_own))

    proj, att, lse, segc, segr, ownc, ownr, wanted, marks, vec = attend(
        place, (lengths, query_index, doc_index, targets), (tokens, w_own, w_other, vectors, v_other)
    )
    xhat1, inv1, hlow, act, slope, xhat2, inv2, unit, uscale = mlp(
        place, wanted, att, tokens, ownr, vec, wo + wu + wd
    )
    units, packed = pack(marks, unit, pair(unit))
    groups = bit_groups(n)
    order = [0]
    stack = packed
    for i, (shift, size) in enumerate(groups[1:] + groups[:1]):
        pieces = [stack] + [swap(stack, "dp", n, k << shift) for k in range(1, size)]
        order = [o | (k << shift) for k in range(size) for o in order]
        if i < len(groups) - 1:
            stack = join(pieces).reshape(-1, 2 * PAIRS, D + 128)
    decayed = decay(
        (weights, first_moment, second_moment, vectors, vec_first, vec_second), [packed]
    )
    dsec, dlow, keep, send, dsums = down_backward(
        n, order, place, wanted, units, ownc, uscale, (xhat2, inv2, act), vec, pieces,
        decayed,
    )
    other = pair(send)
    dup, ukeep, usend, usums = up_backward(place, dlow, slope, hlow, wd, [])
    usend, other = lax.optimization_barrier((usend, other))
    wide = core_sum((keep, other, ukeep, pair(usend)), [dup])
    wide_got = trades(wide, n, 0)
    dfirst, datt, delta, okeep, osend, fsums = first_backward(
        place, dup, dsec, xhat1, inv1, att, vec, wu + wo, [wide[0]]
    )
    ins = (tokens, proj, datt, lse, delta, segc, segr)
    part0, keep0, send0, sums0 = heads_backward(0, place, ins, (), [])
    wide, go = wide_plane_sum(place, wide_got, [part0])
    other = swap(go, "dp", n, 4)
    part1, keep1, send1, sums1 = heads_backward(1, place, ins, (), [wide])
    wide, go = wide_half(wide, other, [part1])
    wother = swap(go, "dp", n, 8)
    part2, keep, send, _ = heads_backward(
        2, place, ins,
        (okeep, osend, keep0, send0, keep1, send1, dsums, usums, fsums, sums0, sums1),
        [wide, part1],
    )
    wide = low_next(wide, wother, [part2])
    send, wide = lax.optimization_barrier((send, wide))
    other = pair(send)
    wide = rest_sum(wide, n)
    wother = swap(wide, "dp", n, 8)
    igrad = input_backward(place, (part0, part1, part2), dfirst, w_own, w_other, [wide])
    iother = pair(igrad)
    low = core_sum((keep, other), [igrad])
    low_got = trades(low, n, 0)
    wide = chain([wide, wother], [low[0]])
    wother = swap(wide, "dp", n, 4)
    low = low_plane_sum(low_got, [wide])
    other = swap(low, "dp", n, 4)
    wide = chain([wide, wother], [low])
    wide = trades([wide] * 4, n, 0)
    low = low_next(low, other, [wide[0]])
    other = swap(low, "dp", n, 8)
    input_grad, flag = merge(place, igrad, iother, [low])
    low, vgrad = low_last(low, other, [flag])
    low, vgrad = rest_sum(low, n), rest_sum(vgrad, n)
    low = trades([low] * 4, n, 0)
    sums = squares(place, low, vgrad, squares(place, wide, after=[low[0]]))
    sums = (sums, pair(sums))
    pieces = tuple(wide) + tuple(low)
    nw, nm, nv, nlow, npv, npm, npq, norm = update(
        place, sums, vgrad, *decayed, pieces,
    )
    return (norm.reshape(()), input_grad, nw, nm, nv, nlow, npv, npm, npq)


def solution(mesh):
    rows = P("opt", None)
    in_specs = (P("dp", None), P("dp", None), P("dp"), P("dp"), P("dp")) + (rows,) * 6
    out_specs = (P(), P("dp", None)) + (rows,) * 7
    n = mesh.shape["dp"]
    return jax.shard_map(
        functools.partial(shards, n),
        mesh=mesh,
        in_specs=in_specs,
        out_specs=out_specs,
        check_vma=False,
    )
```

```python
import functools

import jax
import jax.numpy as jnp
from jax import lax
from jax.experimental import pallas as pl
from jax.experimental.pallas import tpu as pltpu
from jax.sharding import PartitionSpec as P

D = 384
HEADS = 12
HD = 32
FF = 1536
SEQ = 1024
SEGS = 16
PAIRS = 8
STEP = 10

WIN = 576
OFF = SEQ - WIN
PAD = 640
BLOCK = 128
BANDS = tuple((q, max(0, q - 128), min(WIN, q + 256)) for q in range(0, WIN, BLOCK))
BAND_ROWS = tuple(sum(b[2] - b[1] for b in BANDS[:i]) for i in range(len(BANDS) + 1))
ROWS = 64
WIDE_ROWS = 192
LOG2E = 1.4426950408889634

LN_EPS = 1e-06
POOL_EPS = 1e-06
SCORE_SCALE = 50.0
CLIP_NORM = 0.001
BETA_ONE = 0.9
BETA_TWO = 0.98
ADAM_EPS = 1e-08
LEARN_RATE = 0.05
VECTOR_RATE = 0.3
DECAY_RATE = 0.01
NEG_BIG = -1e30
HALF = D // 2
CHUNK = HALF // 4
EXP2_SCALE = HD ** (-0.5) * 1.4426950408889634

F32 = jnp.float32
BF16 = jnp.bfloat16
VMEM = pl.BlockSpec(memory_space=pltpu.VMEM)
SMEM = pl.BlockSpec(memory_space=pltpu.SMEM)
ANY = pl.BlockSpec(memory_space=pl.ANY)


def nn(a, b):
    return jnp.dot(a, b, preferred_element_type=F32)


def nt(a, b):
    return lax.dot_general(a, b, (((1,), (1,)), ((), ())), preferred_element_type=F32)


def tn(a, b):
    return lax.dot_general(a, b, (((0,), (0,)), ((), ())), preferred_element_type=F32)


def exact(a, b, dims):
    return lax.dot_general(
        a, b, (dims, ((), ())), precision=lax.Precision.HIGHEST, preferred_element_type=F32
    )


def iota(shape, axis):
    return lax.broadcasted_iota(jnp.int32, shape, axis)


def low_pair(value):
    high = value.astype(BF16)
    return high, (value - high.astype(F32)).astype(BF16)


def aligned(start, size, unit):
    return pl.ds(pl.multiple_of(start, unit), size)


def assemble(dst, own, other, opt):
    dst[aligned(HALF * opt, HALF, 64), :] = own[0:HALF, :]
    dst[aligned(HALF * (1 - opt), HALF, 64), :] = other[0:HALF, :]


class Place:
    def __getitem__(self, i):
        if i == 0:
            return lax.axis_index("opt")
        me = lax.axis_index("dp")
        return (me & 3, me, (me >> 2) & 3)[i - 1]


def call(kernel, ins, outs, scratch=(), micros=5, name=None, vmem=12, after=()):
    if ins[0][1] is None:
        kernel = functools.partial(kernel, Place())
        ins = ins[1:]
    specs = [SMEM if s else VMEM for s, _ in ins] + [ANY] * len(after)
    count = len(ins)

    def body(*refs):
        kernel(*refs[:count], *refs[count + len(after) :])

    shapes = [jax.ShapeDtypeStruct(s, d) for s, d in outs]
    moved = sum(a.size * a.dtype.itemsize for _, a in ins)
    moved += sum(s.size * s.dtype.itemsize for s in shapes)
    return pl.pallas_call(
        body,
        out_shape=shapes,
        in_specs=specs,
        out_specs=[VMEM] * len(shapes),
        scratch_shapes=list(scratch),
        compiler_params=pltpu.CompilerParams(vmem_limit_bytes=vmem << 20),
        cost_estimate=pl.CostEstimate(
            flops=micros * 1100000000, bytes_accessed=moved, transcendentals=0
        ),
        name=name,
    )(*[a for _, a in ins], *after)


def head_stack(rows):
    lane_head = iota(rows.shape, 1) // HD
    zero = jnp.zeros_like(rows)
    return jnp.concatenate([jnp.where(lane_head == j, rows, zero) for j in range(4)], axis=0)


def attend_kernel(
    place, lengths, query_index, doc_index, targets, tokens, w_own, w_other, v_own, v_other,
    proj, att, lse, segc, segr, ownc, ownr, wanted, marks, vec, wfull, bias, vt,
):
    opt = place[0]
    assemble(wfull, w_own, w_other, opt)
    mine = v_own[...].astype(BF16).astype(F32)
    others = v_other[...].astype(BF16).astype(F32)
    first = opt == 0
    vec[0:6, :] = jnp.where(first, mine, others)
    vec[6:12, :] = jnp.where(first, others, mine)
    vec[12:16, :] = jnp.zeros((4, D), F32)

    position = iota((8, PAD), 1) + OFF * opt
    segment = jnp.zeros((8, PAD), jnp.int32)
    bound = jnp.int32(0)
    low_count = jnp.int32(0)
    for s in range(SEGS):
        bound = bound + lengths[s]
        segment = segment + (position >= bound).astype(jnp.int32)
        low_count = low_count + (bound <= WIN).astype(jnp.int32)
    mine = (segment < low_count).astype(jnp.int32) == (opt == 0).astype(jnp.int32)
    owned = jnp.where(mine, segment, -1)
    segr[...] = segment
    ownr[...] = owned
    for value, out in ((segment, segc), (owned, ownc)):
        value = value.astype(F32)
        for t in range(PAD // 128):
            rows = min(128, WIN - 128 * t)
            turned = jnp.broadcast_to(value[0:1, 128 * t : 128 * t + 128], (128, 128)).T
            out[128 * t : 128 * t + rows, :] = turned[0:rows].astype(jnp.int32)
    row, col = iota((2 * PAIRS, 128), 0), iota((2 * PAIRS, 128), 1)
    by_row = jnp.zeros((2 * PAIRS, 128), jnp.int32)
    by_col = jnp.zeros((2 * PAIRS, 128), jnp.int32)
    mark = jnp.zeros((2 * PAIRS, 128), jnp.int32)
    for j in range(PAIRS):
        mark = jnp.where(row == j, targets[j], mark)
        for at, index in ((j, query_index), (PAIRS + j, doc_index)):
            by_row = jnp.where(row == at, index[j], by_row)
            by_col = jnp.where(col == at, index[j], by_col)
    wanted[0] = by_row
    wanted[1] = by_col
    marks[...] = jnp.where(col < 64, mark >> 5, mark & 31).astype(F32).astype(BF16)
    for i, (q0, k0, k1) in enumerate(BANDS):
        bias[BAND_ROWS[i] : BAND_ROWS[i + 1], :] = jnp.where(
            segc[k0:k1, :] == segr[0:1, q0 : q0 + BLOCK], 0.0, NEG_BIG
        )

    x = tokens[aligned(OFF * opt, WIN, 64), :]
    for c in range(3):
        acc = nn(x, wfull[:, c * D : (c + 1) * D])
        if c != 1:
            acc = acc + vec[(0 if c == 0 else 1) : (1 if c == 0 else 2), :]
        proj[0:WIN, c * D : (c + 1) * D] = acc.astype(BF16)
    proj[WIN:PAD, :] = jnp.zeros((PAD - WIN, 3 * D), BF16)

    def group(g, carry):
        def lanes(part):
            return aligned(part * D + 128 * g, 128, 128)

        for t in range(PAD // 128):
            vt[:, 128 * t : 128 * t + 128] = (
                proj[128 * t : 128 * t + 128, lanes(2)].astype(F32).T.astype(BF16)
            )
        for i, (q0, k0, k1) in enumerate(BANDS):
            stack = head_stack(proj[q0 : q0 + BLOCK, lanes(0)])
            st = nt(proj[k0:k1, lanes(1)], stack)
            outs, probs, totals = [], [], []
            for j in range(4):
                t = (
                    st[:, j * BLOCK : (j + 1) * BLOCK] * EXP2_SCALE
                    + bias[BAND_ROWS[i] : BAND_ROWS[i + 1], :]
                )
                peak = jnp.max(t, axis=0, keepdims=True)
                powers = jnp.exp2(t - peak)
                total = jnp.sum(powers, axis=0, keepdims=True)
                lse[g, j : j + 1, q0 : q0 + BLOCK] = peak + jnp.log2(total)
                probs.append(powers.astype(BF16))
                totals.append(1.0 / total)
                if j % 2 == 1:
                    o = nn(vt[(j - 1) * HD : (j + 1) * HD, k0:k1], jnp.concatenate(probs[-2:], axis=1))
                    outs.append(o[0:HD, 0:BLOCK] * totals[-2])
                    outs.append(o[HD : 2 * HD, BLOCK : 2 * BLOCK] * totals[-1])
            rows = min(BLOCK, WIN - q0)
            att[q0 : q0 + rows, aligned(128 * g, 128, 128)] = (
                jnp.concatenate(outs, axis=0).T[0:rows].astype(BF16)
            )
        return carry

    lax.fori_loop(0, 3, group, 0)


def attend(place, scalars, arrays):
    return call(
        attend_kernel,
        [(1, place)] + [(1, a) for a in scalars] + [(0, a) for a in arrays],
        [
            ((PAD, 3 * D), BF16),
            ((WIN, D), BF16),
            ((3, 4, PAD), F32),
            ((WIN, 128), jnp.int32),
            ((8, PAD), jnp.int32),
            ((WIN, 128), jnp.int32),
            ((8, PAD), jnp.int32),
            ((2, 2 * PAIRS, 128), jnp.int32),
            ((2 * PAIRS, 128), BF16),
            ((16, D), F32),
            ((D, 3 * D), BF16),
        ],
        [
            pltpu.VMEM((BAND_ROWS[-1], 128), F32),
            pltpu.VMEM((128, PAD), BF16),
        ],
        micros=8,
        name="attend",
    )


def bias_of(vec, c):
    first, last = 256 * c, 256 * c + 256
    parts = []
    while first < last:
        row, col = divmod(first, D)
        size = min(D - col, last - first)
        parts.append(vec[3 + row : 4 + row, col : col + size])
        first += size
    return parts[0] if len(parts) == 1 else jnp.concatenate(parts, axis=1)


def mlp_kernel(
    place, wanted, att, tokens, ownr, vec, wo_own, wo_other, wu_own, wu_other,
    wd_own, wd_other, xhat1, inv1, hlow, act, slope, xhat2, inv2, unit, uscale, wo, wu, wd,
    ench, encl,
):
    opt = place[0]
    assemble(wo, wo_own, wo_other, opt)
    assemble(wu, wu_own, wu_other, opt)
    assemble(wd, wd_own, wd_other, opt)

    def norm(v):
        centred = v - jnp.mean(v, axis=1, keepdims=True)
        inverse = lax.rsqrt(jnp.mean(centred * centred, axis=1, keepdims=True) + LN_EPS)
        return centred * inverse, inverse

    def block(i, carry):
        r = aligned(i * WIDE_ROWS, WIDE_ROWS, 64)
        x = tokens[aligned(OFF * opt + i * WIDE_ROWS, WIDE_ROWS, 64), :].astype(F32)
        normed, inverse = norm(nn(att[r, :], wo[...]) + vec[2:3, :] + x)
        xhat1[r, :] = normed
        inv1[r, :] = jnp.broadcast_to(inverse, (WIDE_ROWS, 128))
        h = normed * vec[8:9, :] + vec[9:10, :]
        low = h.astype(BF16)
        hlow[r, :] = low
        for c in range(6):
            cols = slice(c * 256, (c + 1) * 256)
            u = nn(low, wu[:, cols]) + bias_of(vec, c)
            half = lax.erf(u * 0.7071067811865476) * 0.5 + 0.5
            act[r, cols] = (u * half).astype(BF16)
            slope[r, cols] = half + u * jnp.exp2(u * u * (-0.5 * LOG2E)) * 0.3989422804014327
        normed, inverse = norm(nt(act[r, :], wd[...]) + vec[7:8, :] + h)
        xhat2[r, :] = normed
        inv2[r, :] = jnp.broadcast_to(inverse, (WIDE_ROWS, 128))
        high, rest = low_pair(normed * vec[10:11, :] + vec[11:12, :])
        ench[r, :] = high
        encl[r, :] = rest
        return carry

    lax.fori_loop(0, WIN // WIDE_ROWS, block, 0)

    onehot = jnp.where(wanted[0, :, 0:1] == ownr[0:1, 0:WIN], 1.0, 0.0)
    count = jnp.maximum(jnp.sum(onehot, axis=1, keepdims=True), 1.0)
    hot = onehot.astype(BF16)
    pooled = (nn(hot, ench[...]) + nn(hot, encl[...])) / count
    inverse_len = lax.rsqrt(jnp.sum(pooled * pooled, axis=1, keepdims=True) + POOL_EPS)
    unit[...] = pooled * inverse_len
    uscale[...] = jnp.broadcast_to(inverse_len / count, (2 * PAIRS, 128))


def mlp(place, wanted, att, tokens, ownr, vec, halves):
    return call(
        mlp_kernel,
        [(1, place), (0, wanted), (0, att), (0, tokens), (0, ownr), (0, vec)]
        + [(0, h) for h in halves],
        [
            ((WIN, D), F32),
            ((WIN, 128), F32),
            ((WIN, D), BF16),
            ((WIN, FF), BF16),
            ((WIN, FF), F32),
            ((WIN, D), F32),
            ((WIN, 128), F32),
            ((2 * PAIRS, D), F32),
            ((2 * PAIRS, 128), F32),
            ((D, D), BF16),
            ((D, FF), BF16),
            ((D, FF), BF16),
        ],
        [
            pltpu.VMEM((WIN, D), BF16),
            pltpu.VMEM((WIN, D), BF16),
        ],
        micros=10,
        name="mlp",
    )


def split_rows(grad, keep, send, place, *at):
    opt = place[0]
    for c in range(4):
        index = (c ^ place[1],) + at
        keep[index] = grad[aligned(HALF * opt + CHUNK * c, CHUNK, 16), :].astype(BF16)
        send[index] = grad[aligned(HALF * (1 - opt) + CHUNK * c, CHUNK, 16), :].astype(BF16)


def column_sums(value):
    return jnp.sum(value.reshape(-1, 8, D), axis=0)


def norm_backward(grad_at, normed_ref, inverse_ref, gain, out, low_out, sums, at, step=ROWS):
    def block(i, carry):
        scale_sum, shift_sum, bias_sum = carry
        r = aligned(i * step, step, 64)
        g = grad_at(r)
        normed = normed_ref[r, :]
        scaled = g * gain
        inner = (
            scaled
            - jnp.mean(scaled, axis=1, keepdims=True)
            - normed * jnp.mean(scaled * normed, axis=1, keepdims=True)
        ) * inverse_ref[r, 0:1]
        out[r, :] = inner
        low_out[r, :] = inner.astype(BF16)
        return (
            scale_sum + column_sums(g * normed),
            shift_sum + column_sums(g),
            bias_sum + column_sums(inner),
        )

    zero = jnp.zeros((8, D), F32)
    scale_sum, shift_sum, bias_sum = lax.fori_loop(0, WIN // step, block, (zero, zero, zero))
    sums[at : at + 1, :] = jnp.sum(bias_sum, axis=0, keepdims=True)
    sums[at + 1 : at + 2, :] = jnp.sum(scale_sum, axis=0, keepdims=True)
    sums[at + 2 : at + 3, :] = jnp.sum(shift_sum, axis=0, keepdims=True)


def down_kernel(
    place, count, order, wanted, units, ownc, uscale, xhat2, inv2, act, vec, *rest
):
    pieces, (dsec, dlow, keep, send, sums, queries, docs, marks, grad) = rest[:-9], rest[-9:]
    me = place[2]
    per = pieces[0].shape[0]
    for p, piece in enumerate(pieces):
        for j in range(per):
            at = order[p * per + j]
            r = slice(at * PAIRS, (at + 1) * PAIRS)
            both = piece[j].astype(F32)
            queries[r, :] = both[0:PAIRS, 0:D]
            docs[r, :] = both[PAIRS : 2 * PAIRS, 0:D]
            marks[r, :] = both[0:PAIRS, D : D + 128]
    total = count * PAIRS
    q = queries[...].astype(BF16)
    d = docs[...].astype(BF16)
    logits = SCORE_SCALE * nt(q, d)
    peak = jnp.max(logits, axis=1, keepdims=True)
    powers = jnp.exp(logits - peak)
    soft = powers / jnp.sum(powers, axis=1, keepdims=True)
    col = iota((total, total), 1)
    doc_id = ((col // PAIRS) ^ me) * PAIRS + lax.rem(col, PAIRS)
    hit = (marks[:, 0:1] * 32.0 + marks[:, 64:65]).astype(jnp.int32) == doc_id
    d_logits = (soft - jnp.where(hit, 1.0, 0.0)) * (SCORE_SCALE / total)
    high, rest_low = low_pair(d_logits[0:PAIRS, :])
    d_q = nn(high, d) + nn(rest_low, d)
    high, rest_low = low_pair(d_logits[:, 0:128].T[0:PAIRS, :])
    d_d = nn(high, q) + nn(rest_low, q)
    d_units = jnp.concatenate([d_q, d_d], axis=0)
    u = units[...]
    d_pool = uscale[:, 0:1] * (d_units - u * jnp.sum(u * d_units, axis=1, keepdims=True))
    hot = jnp.where(ownc[:, 0 : 2 * PAIRS] == wanted[1, 0:1, 0 : 2 * PAIRS], 1.0, 0.0).astype(BF16)
    high, rest_low = low_pair(d_pool)
    dsec[...] = nn(hot, high) + nn(hot, rest_low)
    norm_backward(lambda r: dsec[r, :], xhat2, inv2, vec[10:11, :], dsec, dlow, sums, 0)
    sums[3:8, :] = jnp.zeros((5, D), F32)
    for c in range(3):
        cols = slice(c * 512, (c + 1) * 512)
        grad[:, cols] = tn(dlow[...], act[:, cols])
    for c in range(4):
        split_rows(grad.at[:, c * D : (c + 1) * D], keep, send, place, c)


def down_backward(count, order, place, wanted, units, ownc, uscale, saved, vec, pieces, after):
    total = count * PAIRS
    return call(
        lambda place, *refs: down_kernel(place, count, order, *refs),
        [(1, place), (0, wanted), (0, units), (0, ownc), (0, uscale)]
        + [(0, s) for s in saved]
        + [(0, vec)]
        + [(0, p) for p in pieces],
        [
            ((WIN, D), F32),
            ((WIN, D), BF16),
            ((4, 4, CHUNK, D), BF16),
            ((4, 4, CHUNK, D), BF16),
            ((8, D), F32),
        ],
        [
            pltpu.VMEM((total, D), F32),
            pltpu.VMEM((total, D), F32),
            pltpu.VMEM((total, 128), F32),
            pltpu.VMEM((D, FF), F32),
        ],
        micros=4,
        name="down_backward",
        after=after,
    )


def up_kernel(place, dlow, slope, hlow, wd, dup, keep, send, sums, grad):
    for c in range(3):
        cols = slice(c * 512, (c + 1) * 512)
        part = (nn(dlow[...], wd[:, cols]) * slope[:, cols]).astype(BF16)
        dup[:, cols] = part
        column_sum = jnp.sum(part.astype(F32), axis=0, keepdims=True)
        for j in range(4):
            at = 512 * c + 128 * j
            sums[at // D : at // D + 1, at % D : at % D + 128] = column_sum[:, 128 * j : 128 * j + 128]
        grad[:, cols] = tn(hlow[...], dup[:, cols])
    for c in range(4):
        split_rows(grad.at[:, c * D : (c + 1) * D], keep, send, place, c)


def up_backward(place, dlow, slope, hlow, wd, after):
    return call(
        up_kernel,
        [(1, place)] + [(0, a) for a in (dlow, slope, hlow, wd)],
        [((WIN, FF), BF16), ((4, 4, CHUNK, D), BF16), ((4, 4, CHUNK, D), BF16), ((4, D), F32)],
        [pltpu.VMEM((D, FF), F32)],
        micros=3,
        name="up_backward",
        after=after,
    )


def first_kernel(
    place, dup, dsec, xhat1, inv1, att, vec, wu, wo,
    dfirst, datt, delta, okeep, osend, sums, grad, dlow,
):
    norm_backward(
        lambda r: nt(dup[r, :], wu[...]) + dsec[r, :],
        xhat1, inv1, vec[8:9, :], dfirst, dlow, sums, 0, WIDE_ROWS,
    )
    sums[3:8, :] = jnp.zeros((5, D), F32)
    grad[...] = tn(att[...], dlow[...])
    split_rows(grad, okeep, osend, place)
    da = nt(dlow[...], wo[...]).astype(BF16)
    datt[0:WIN, :] = da
    datt[WIN:PAD, :] = jnp.zeros((PAD - WIN, D), BF16)
    high, rest = low_pair(da.astype(F32) * att[...].astype(F32))
    heads = (iota((16, D), 1) // HD == iota((16, D), 0)).astype(F32).astype(BF16)
    delta[:, 0:WIN] = nt(heads, high) + nt(heads, rest)
    delta[:, WIN:PAD] = jnp.zeros((16, PAD - WIN), F32)


def first_backward(place, dup, dsec, xhat1, inv1, att, vec, wu, wo, after):
    return call(
        first_kernel,
        [(1, place)] + [(0, a) for a in (dup, dsec, xhat1, inv1, att, vec, wu, wo)],
        [
            ((WIN, D), F32),
            ((PAD, D), BF16),
            ((16, PAD), F32),
            ((4, CHUNK, D), BF16),
            ((4, CHUNK, D), BF16),
            ((8, D), F32),
        ],
        [
            pltpu.VMEM((D, D), F32),
            pltpu.VMEM((WIN, D), BF16),
        ],
        micros=3,
        name="first_backward",
        after=after,
    )


def heads_kernel(place, g, tokens, proj, datt, lse, delta, segc, segr, *rest):
    rest, (dproj, keep, send, sums, kt, dk, dv, grad, ktmp, stmp) = rest[:-10], rest[-10:]

    def lanes(part):
        return slice(part * D + 128 * g, part * D + 128 * g + 128)

    for t in range(PAD // 128):
        kt[:, 128 * t : 128 * t + 128] = (
            proj[128 * t : 128 * t + 128, lanes(1)].astype(F32).T.astype(BF16)
        )
    dk[...] = jnp.zeros_like(dk)
    dv[...] = jnp.zeros_like(dv)
    for q0, k0, k1 in BANDS:
        qs = head_stack(proj[q0 : q0 + BLOCK, lanes(0)])
        gs = head_stack(datt[q0 : q0 + BLOCK, lanes(0)])
        st = nt(proj[k0:k1, lanes(1)], qs)
        dp = nt(proj[k0:k1, lanes(2)], gs)
        same = segc[k0:k1, :] == segr[0:1, q0 : q0 + BLOCK]
        bias = jnp.where(same, 0.0, NEG_BIG)
        probs, d_scores, dq = [], [], []
        for j in range(4):
            cols = slice(j * BLOCK, (j + 1) * BLOCK)
            prob = jnp.exp2(st[:, cols] * EXP2_SCALE + bias - lse[g, j : j + 1, q0 : q0 + BLOCK])
            ds = prob * (dp[:, cols] - delta[4 * g + j : 4 * g + j + 1, q0 : q0 + BLOCK])
            ds = ds.astype(BF16)
            probs.append(prob.astype(BF16))
            d_scores.append(ds)
            if j % 2 == 1:
                part = nn(
                    kt[(j - 1) * HD : (j + 1) * HD, k0:k1], jnp.concatenate(d_scores[-2:], axis=1)
                )
                dq.append(part[0:HD, 0:BLOCK])
                dq.append(part[HD : 2 * HD, BLOCK : 2 * BLOCK])
        dv[k0:k1, :] += nn(jnp.concatenate(probs, axis=1), gs)
        dk[k0:k1, :] += nn(jnp.concatenate(d_scores, axis=1), qs)
        rows = min(BLOCK, WIN - q0)
        dqs = jnp.concatenate(dq, axis=0).T[0:rows] * HD ** (-0.5)
        dproj[q0 : q0 + rows, 0:128] = dqs.astype(BF16)
    dproj[:, 128:256] = (dk[...] * HD ** (-0.5)).astype(BF16)
    dproj[:, 256:384] = dv[...].astype(BF16)
    grad[...] = tn(tokens[aligned(OFF * place[0], WIN, 64), :], dproj[...])
    q_sum = jnp.sum(dproj[:, 0:128].astype(F32), axis=0, keepdims=True)
    v_sum = jnp.sum(dproj[:, 256:384].astype(F32), axis=0, keepdims=True)
    sums[0:1, :] = q_sum
    sums[1:2, :] = v_sum
    sums[2:8, :] = jnp.zeros((6, 128), F32)
    if g < 2:
        split_rows(grad, keep, send, place)
        return
    parts, (dsums, usums, fsums, zero, one) = rest[:6], rest[6:]
    split_rows(grad, ktmp, stmp, place)
    for dst, out_part, blocks in (
        (keep, parts[0], (parts[2], parts[4], ktmp)),
        (send, parts[1], (parts[3], parts[5], stmp)),
    ):
        dst[:, :, 3 * D : 4 * D] = out_part[...]
        for h, part in enumerate(blocks):
            for c in range(3):
                dst[:, :, D * c + 128 * h : D * c + 128 * h + 128] = part[
                    :, :, 128 * c : 128 * c + 128
                ]
    rows = jnp.concatenate(
        [
            jnp.concatenate([zero[0:1], one[0:1], q_sum], axis=1),
            jnp.concatenate([zero[1:2], one[1:2], v_sum], axis=1),
            fsums[0:1, :],
            usums[0:4, :],
            dsums[0:1, :],
            fsums[1:3, :],
            dsums[1:3, :],
            jnp.zeros((4, D), F32),
        ],
        axis=0,
    ).astype(BF16)
    for c in range(4):
        for j in range(3):
            block = rows[:, 128 * j : 128 * j + 128]
            keep[c, 16 * j : 16 * j + 16, 4 * D : 4 * D + 128] = block
            send[c, 16 * j : 16 * j + 16, 4 * D : 4 * D + 128] = block


def heads_backward(g, place, ins, more, after):
    part = ((4, CHUNK, 4 * D + 128 if g == 2 else D), BF16)
    return call(
        lambda place, *refs: heads_kernel(place, g, *refs),
        [(1, place)] + [(0, a) for a in tuple(ins) + tuple(more)],
        [((WIN, D), BF16), part, part, ((8, 128), F32)],
        [
            pltpu.VMEM((128, PAD), BF16),
            pltpu.VMEM((WIN, 128), F32),
            pltpu.VMEM((WIN, 128), F32),
            pltpu.VMEM((D, D), F32),
            pltpu.VMEM((4, CHUNK, D), BF16),
            pltpu.VMEM((4, CHUNK, D), BF16),
        ],
        micros=3,
        name="heads_backward",
        after=after,
    )


def input_kernel(dp0, dp1, dp2, dfirst, wfull, igrad, dproj):
    for g, part in enumerate((dp0, dp1, dp2)):
        for c in range(3):
            dproj[:, c * D + 128 * g : c * D + 128 * g + 128] = part[:, 128 * c : 128 * c + 128]
    igrad[...] = (nt(dproj[...], wfull[...]) + dfirst[...]).astype(BF16)


def input_backward(parts, dfirst, wqkv, after):
    return call(
        input_kernel,
        [(0, a) for a in tuple(parts) + (dfirst, wqkv)],
        [((WIN, D), BF16)],
        [pltpu.VMEM((WIN, 3 * D), BF16)],
        micros=2,
        name="input_backward",
        after=after,
    )[0]


def flips(axis, size, bits):
    return [(i, i ^ bits) for i in range(size)]


def pair(value):
    return swap(value, "opt", 2, 1)


def swap(value, axis, size, bits):
    return lax.ppermute(value, axis, flips(axis, size, bits))


def bit_groups(size):
    bits = size.bit_length() - 1
    return [(s, 1 << min(2, bits - s)) for s in range(0, bits, 2)]


def trades(values, n, shift):
    return [values[0]] + [swap(values[k], "dp", n, k << shift) for k in (1, 2, 3)]


def added(a, b):
    return (a.astype(F32) + b.astype(F32)).astype(BF16)


def core_sum_kernel(keep, other, *outs):
    for r, out in enumerate(outs):
        out[...] = added(keep[r], other[r])


def core_sum(keep, other, after):
    return call(
        core_sum_kernel,
        [(0, keep), (0, other)],
        [(keep.shape[1:], BF16)] * 4,
        name="core_sum",
        vmem=4,
        after=after,
    )


def pair_sum_kernel(bit, keep, other, stay, go):
    for i, r in enumerate((0, 3 - bit)):
        stay[i] = added(keep[r], other[r])
        go[i] = added(keep[r + bit], other[r + bit])


def pair_sum(bit, keep, other, after):
    return call(
        functools.partial(pair_sum_kernel, bit),
        [(0, keep), (0, other)],
        [((2,) + keep.shape[1:], BF16)] * 2,
        name="pair_sum",
        vmem=4,
        after=after,
    )


def wide_step_kernel(down, dother, up, uother, dkeep, dsend, ukeep, usend):
    dkeep[...] = added(down[0], dother[0])
    dsend[...] = added(down[1], dother[1])
    ukeep[...] = added(up[0], uother[0])
    usend[...] = added(up[1], uother[1])


def wide_step(parts, after):
    return call(
        wide_step_kernel,
        [(0, p) for p in parts],
        [((4, CHUNK, D), BF16)] * 4,
        name="wide_step",
        vmem=4,
        after=after,
    )


def total_of(refs, at):
    a, b, c, d = (ref[at].astype(F32) for ref in refs)
    return ((a + b) + (c + d)).astype(BF16)


def wide_plane_kernel(place, down, dother, up, uother, mine, send):
    z = place[3]
    for p, (keep, other) in enumerate(((down, dother), (up, uother))):
        for i, bits in enumerate((0, 2)):
            mine[2 * i + p] = added(keep[z ^ bits], other[z ^ bits])
            send[2 * i + p] = added(keep[z ^ bits ^ 1], other[z ^ bits ^ 1])


def wide_plane_sum(place, parts, after):
    return call(
        wide_plane_kernel,
        [(1, place)] + [(0, p) for p in parts],
        [((4, CHUNK, D), BF16)] * 2,
        name="wide_plane_sum",
        vmem=4,
        after=after,
    )


def wide_half_kernel(keep, other, mine, send):
    mine[...] = added(keep[0:2], other[0:2])
    send[...] = added(keep[2:4], other[2:4])


def wide_half(keep, other, after):
    return call(
        wide_half_kernel,
        [(0, keep), (0, other)],
        [((2, CHUNK, D), BF16)] * 2,
        name="wide_half",
        vmem=4,
        after=after,
    )


def low_plane_kernel(a, b, c, d, out):
    out[...] = total_of((a, b, c, d), slice(None))


def low_plane_sum(parts, after=()):
    return call(
        low_plane_kernel,
        [(0, p) for p in parts],
        [(parts[0].shape, BF16)],
        name="low_plane_sum",
        vmem=4,
        after=after,
    )[0]


def low_next_kernel(keep, other, out):
    out[...] = added(keep[...], other[...])


def low_next(keep, other, after=()):
    return call(
        low_next_kernel,
        [(0, keep), (0, other)],
        [(keep.shape, BF16)],
        name="low_next",
        vmem=4,
        after=after,
    )[0]


def low_last_kernel(keep, other, out, vgrad):
    out[...] = added(keep[:, 0 : 4 * D], other[:, 0 : 4 * D])
    vgrad[...] = added(keep[:, 4 * D : 4 * D + 128], other[:, 4 * D : 4 * D + 128])


def low_last(keep, other, after):
    return call(
        low_last_kernel,
        [(0, keep), (0, other)],
        [((CHUNK, 4 * D), BF16), ((CHUNK, 128), BF16)],
        name="low_last",
        vmem=4,
        after=after,
    )


def chain_kernel(*refs):
    ins, out = refs[:-1], refs[-1]
    at = 0
    for ref in ins:
        flat = ref.reshape(-1, CHUNK, D)
        out[at : at + flat.shape[0]] = flat[...]
        at += flat.shape[0]


def chain(parts, after=()):
    count = sum(p.size for p in parts) // (CHUNK * D)
    return call(
        chain_kernel,
        [(0, p) for p in parts],
        [((count, CHUNK, D), BF16)],
        name="chain",
        vmem=4,
        after=after,
    )[0]


def rest_sum(value, n):
    bit = 16
    while bit < n:
        other = swap(value, "dp", n, bit)
        value = (value.astype(F32) + other.astype(F32)).astype(BF16)
        bit *= 2
    return value


def join_kernel(*refs):
    ins, out = refs[:-1], refs[-1]
    for i, ref in enumerate(ins):
        out[i] = ref[...]


def join(parts, after=()):
    return call(
        join_kernel,
        [(0, p) for p in parts],
        [((len(parts),) + parts[0].shape, parts[0].dtype)],
        name="join",
        vmem=4,
        after=after,
    )[0]


def pack_kernel(marks, unit, other, units, packed):
    both = unit[...] + other[...]
    units[...] = both
    packed[:, 0:D] = both.astype(BF16)
    packed[:, D : D + 128] = marks[...]


def pack(marks, unit, other):
    return call(
        pack_kernel,
        [(0, marks), (0, unit), (0, other)],
        [(unit.shape, F32), ((2 * PAIRS, D + 128), BF16)],
        name="pack",
        vmem=4,
    )


def squares_of(parts):
    acc = jnp.zeros((8, D), F32)
    for part in parts:
        flat = part.reshape(-1, CHUNK, part.shape[-1])
        for k in range(flat.shape[0]):
            for c in range(0, part.shape[-1], D):
                v = flat[k, :, c : c + D].astype(F32)
                acc = acc + jnp.sum((v * v).reshape(CHUNK // 8, 8, D), axis=0)
    return acc[:, 0:128] + acc[:, 128:256] + acc[:, 256:384]


def wide_squares_kernel(*refs):
    refs[-1][...] = squares_of(refs[:-1])


def squares_kernel(place, *refs):
    parts, (vgrad, before, out) = refs[:-3], refs[-3:]
    acc = squares_of(parts) + before[...]
    row = iota((16, 128), 0)
    low_row = 6 * place[0]
    mine = (row >= low_row) & (row < low_row + 6)
    for j in range(3):
        v = jnp.where(mine, vgrad[16 * j : 16 * j + 16, :].astype(F32), 0.0)
        v = v * v
        acc = acc + (v[0:8] + v[8:16])
    out[...] = acc


def squares(place, parts, vgrad=None, before=None, after=()):
    ins = [(0, p) for p in parts]
    kernel = wide_squares_kernel
    if before is not None:
        ins = [(1, place)] + ins + [(0, vgrad), (0, before)]
        kernel = squares_kernel
    return call(kernel, ins, [((8, 128), F32)], name="squares", vmem=4, after=after)[0]


def merge_kernel(place, igrad, other, out, flag):
    flag[...] = jnp.zeros((8, 128), F32)

    @pl.when(place[0] == 0)
    def low_core():
        out[0:OFF, :] = igrad[0:OFF, :]
        out[OFF:WIN, :] = added(igrad[OFF:WIN, :], other[0 : WIN - OFF, :])
        out[WIN:SEQ, :] = other[WIN - OFF : WIN, :]

    @pl.when(place[0] != 0)
    def high_core():
        out[0:OFF, :] = other[0:OFF, :]
        out[OFF:WIN, :] = added(other[OFF:WIN, :], igrad[0 : WIN - OFF, :])
        out[WIN:SEQ, :] = igrad[WIN - OFF : WIN, :]


def merge(place, igrad, other, after):
    return call(
        merge_kernel,
        [(1, place), (0, igrad), (0, other)],
        [((SEQ, D), BF16), ((8, 128), F32)],
        name="merge",
        vmem=4,
        after=after,
    )


def adamw(parameter, first_state, second, clipped, rate):
    first_new = first_state + (1.0 - BETA_ONE) * clipped
    second_new = second + (1.0 - BETA_TWO) * clipped * clipped
    root = (1.0 - BETA_TWO**STEP) ** 0.5
    below = pl.reciprocal(second_new * lax.rsqrt(second_new) + ADAM_EPS * root)
    scale = rate * root / (1.0 - BETA_ONE**STEP)
    return parameter - scale * (first_new * below), first_new, second_new


def decay_kernel(w, m, v, pv, pm, pq, nw, nm, nv, npv, npm, npq):
    for ins, outs, rate in (
        ((w, m, v), (nw, nm, nv), LEARN_RATE),
        ((pv, pm, pq), (npv, npm, npq), VECTOR_RATE),
    ):
        for ref, out, scale in zip(ins, outs, (1.0 - rate * DECAY_RATE, BETA_ONE, BETA_TWO)):
            out[...] = ref[...] * scale


def decay(arrays, after):
    return call(
        decay_kernel,
        [(0, a) for a in arrays],
        [(a.shape, F32) for a in arrays],
        name="decay",
        vmem=4,
        after=after,
    )


def adamw_kernel(*refs):
    place = Place()
    sums, refs = refs[:2], refs[2:]
    (vgrad, w, m, v, pv, pm, pq), refs = refs[:7], refs[7:]
    wide, low, refs = refs[:4], refs[4:8], refs[8:]
    outs, (npv, npm, npq, norm), scrs, sems = refs[:4], refs[4:8], refs[8:12], refs[12]
    opt = place[0]
    total = sums[0][...] + sums[1][...]
    total = jnp.sum(jnp.sum(total, axis=1, keepdims=True), axis=0, keepdims=True)
    grad_norm = jnp.sqrt(total)
    factor = jnp.minimum(1.0, CLIP_NORM / (grad_norm + 1e-06))
    norm[...] = grad_norm
    for j in range(3):
        cols = slice(128 * j, 128 * j + 128)
        g = vgrad[16 * j : 16 * j + 16, :].astype(F32)
        g = jnp.where(opt == 0, g[0:6], g[6:12])
        a, b, c = adamw(pv[:, cols], pm[:, cols], pq[:, cols], g * factor, VECTOR_RATE)
        npv[:, cols] = a
        npm[:, cols] = b
        npq[:, cols] = c

    def block(grad, rows, cols):
        new = adamw(w[rows, cols], m[rows, cols], v[rows, cols], grad * factor, LEARN_RATE)
        for scr, value in zip(scrs, new + (new[0].astype(BF16),)):
            scr[rows, cols] = value

    def copies(r, i):
        rows = aligned(CHUNK * (place[1] ^ r) + i * 16, 16, 16)
        return [
            pltpu.make_async_copy(scr.at[rows, :], out.at[rows, :], sems.at[3 * r + i, j])
            for j, (scr, out) in enumerate(zip(scrs, outs))
        ]

    for r in range(4):

        def step(i, carry, r=r):
            rows = aligned(CHUNK * (place[1] ^ r) + i * 16, 16, 16)
            here = aligned(i * 16, 16, 16)
            for j in range(4):
                at = D * (place[3] ^ j)
                for p, start in enumerate((4 * D + FF, 4 * D)):
                    grad = wide[r][2 * j + p, here, :].astype(F32)
                    block(grad, rows, aligned(start + at, D, 128))
            for c in range(4):
                grad = low[r][here, D * c : D * c + D].astype(F32)
                block(grad, rows, slice(D * c, D * c + D))
            for copy in copies(r, i):
                copy.start()
            return carry

        lax.fori_loop(0, CHUNK // 16, step, 0)
    for r in range(4):

        def finish(i, carry, r=r):
            for copy in copies(r, i):
                copy.wait()
            return carry

        lax.fori_loop(0, CHUNK // 16, finish, 0)


def update(place, sums, vgrad, w, m, v, pv, pm, pq, parts):
    ins = tuple(sums) + (vgrad, w, m, v, pv, pm, pq) + tuple(parts)
    shapes = [(w.shape, F32)] * 3 + [(w.shape, BF16)] + [(pv.shape, F32)] * 3 + [((1, 1), F32)]
    return pl.pallas_call(
        adamw_kernel,
        out_shape=[jax.ShapeDtypeStruct(s, d) for s, d in shapes],
        in_specs=[VMEM] * len(ins),
        out_specs=[ANY] * 4 + [VMEM] * 4,
        scratch_shapes=[
            pltpu.VMEM(w.shape, F32),
            pltpu.VMEM(w.shape, F32),
            pltpu.VMEM(w.shape, F32),
            pltpu.VMEM(w.shape, BF16),
            pltpu.SemaphoreType.DMA((12, 4)),
        ],
        compiler_params=pltpu.CompilerParams(vmem_limit_bytes=16 << 20),
        cost_estimate=pl.CostEstimate(
            flops=4000000000, bytes_accessed=26 * w.size, transcendentals=0
        ),
        name="adamw",
    )(*ins)


def shards(
    n,
    tokens,
    lengths,
    query_index,
    doc_index,
    targets,
    weights,
    first_moment,
    second_moment,
    vectors,
    vec_first,
    vec_second,
):
    place = None
    lengths = lengths.reshape(SEGS)
    groups = bit_groups(n)

    w_own = weights[:, : 3 * D].astype(BF16)
    w_other = pair(w_own)
    v_other = pair(vectors)
    later, w_own = lax.optimization_barrier((weights, w_own))
    wo_own = later[:, 3 * D : 4 * D].astype(BF16)
    wu_own = later[:, 4 * D : 4 * D + FF].astype(BF16)
    wd_own = later[:, 4 * D + FF :].astype(BF16)
    wo = (wo_own, pair(wo_own))
    wu = (wu_own, pair(wu_own))
    wd = (wd_own, pair(wd_own))

    proj, att, lse, segc, segr, ownc, ownr, wanted, marks, vec, wqkv = attend(
        place, (lengths, query_index, doc_index, targets), (tokens, w_own, w_other, vectors, v_other)
    )
    xhat1, inv1, hlow, act, slope, xhat2, inv2, unit, uscale, wo, wu, wd = mlp(
        place, wanted, att, tokens, ownr, vec, wo + wu + wd
    )
    units, packed = pack(marks, unit, pair(unit))
    groups = bit_groups(n)
    order = [0]
    stack = packed
    for i, (shift, size) in enumerate(groups[1:] + groups[:1]):
        pieces = [stack] + [swap(stack, "dp", n, k << shift) for k in range(1, size)]
        order = [o | (k << shift) for k in range(size) for o in order]
        if i < len(groups) - 1:
            stack = join(pieces).reshape(-1, 2 * PAIRS, D + 128)
    decayed = decay(
        (weights, first_moment, second_moment, vectors, vec_first, vec_second), [packed]
    )
    dsec, dlow, keep, send, dsums = down_backward(
        n, order, place, wanted, units, ownc, uscale, (xhat2, inv2, act), vec, pieces,
        decayed,
    )
    other = pair(send)
    dup, ukeep, usend, usums = up_backward(place, dlow, slope, hlow, wd, [])
    down, go = pair_sum(1, keep, other, [dup])
    dother = swap(go, "dp", n, 1)
    up, go = pair_sum(2, ukeep, pair(usend), [down])
    uother = swap(go, "dp", n, 2)
    dfirst, datt, delta, okeep, osend, fsums = first_backward(
        place, dup, dsec, xhat1, inv1, att, vec, wu, wo, [up]
    )
    ins = (tokens, proj, datt, lse, delta, segc, segr)
    part0, keep0, send0, sums0 = heads_backward(0, place, ins, (), [])
    down, dsend, up, usend = wide_step((down, dother, up, uother), [part0])
    dother, uother = swap(dsend, "dp", n, 2), swap(usend, "dp", n, 1)
    part1, keep1, send1, sums1 = heads_backward(1, place, ins, (), [down])
    wide, go = wide_plane_sum(place, (down, dother, up, uother), [part1])
    wother = swap(go, "dp", n, 4)
    part2, keep, send, _ = heads_backward(
        2, place, ins,
        (okeep, osend, keep0, send0, keep1, send1, dsums, usums, fsums, sums0, sums1),
        [wide, part1],
    )
    wide, go = wide_half(wide, wother, [part2])
    send, wide, go = lax.optimization_barrier((send, wide, go))
    wother = swap(go, "dp", n, 8)
    other = pair(send)
    igrad = input_backward((part0, part1, part2), dfirst, wqkv, [wide])
    iother = pair(igrad)
    low = core_sum(keep, other, [igrad])
    low_got = trades(low, n, 0)
    wide = rest_sum(low_next(wide, wother, [low[0]]), n)
    wide_got = trades([wide] * 4, n, 2)
    low = low_plane_sum(low_got, [wide])
    other = swap(low, "dp", n, 4)
    wide = chain(wide_got, [low])
    wide = trades([wide] * 4, n, 0)
    low = low_next(low, other, [wide[0]])
    other = swap(low, "dp", n, 8)
    input_grad, flag = merge(place, igrad, iother, [low])
    low, vgrad = low_last(low, other, [flag])
    low, vgrad = rest_sum(low, n), rest_sum(vgrad, n)
    low = trades([low] * 4, n, 0)
    sums = squares(place, low, vgrad, squares(place, wide, after=[low[0]]))
    sums = (sums, pair(sums))
    pieces = tuple(wide) + tuple(low)
    nw, nm, nv, nlow, npv, npm, npq, norm = update(
        place, sums, vgrad, *decayed, pieces,
    )
    return (norm.reshape(()), input_grad, nw, nm, nv, nlow, npv, npm, npq)


def solution(mesh):
    rows = P("opt", None)
    in_specs = (P("dp", None), P("dp", None), P("dp"), P("dp"), P("dp")) + (rows,) * 6
    out_specs = (P(), P("dp", None)) + (rows,) * 7
    n = mesh.shape["dp"]
    return jax.shard_map(
        functools.partial(shards, n),
        mesh=mesh,
        in_specs=in_specs,
        out_specs=out_specs,
        check_vma=False,
    )
```

```python
import functools

import jax
import jax.numpy as jnp
from jax import lax
from jax.experimental import pallas as pl
from jax.experimental.pallas import tpu as pltpu
from jax.sharding import PartitionSpec as P

D = 384
HEADS = 12
HD = 32
FF = 1536
SEQ = 1024
SEGS = 16
PAIRS = 8
STEP = 10

WIN = 576
OFF = SEQ - WIN
PAD = 640
BLOCK = 128
BANDS = tuple((q, max(0, q - 128), min(WIN, q + 256)) for q in range(0, WIN, BLOCK))
BAND_ROWS = tuple(sum(b[2] - b[1] for b in BANDS[:i]) for i in range(len(BANDS) + 1))
ROWS = 64
WIDE_ROWS = 192
LOG2E = 1.4426950408889634

LN_EPS = 1e-06
POOL_EPS = 1e-06
SCORE_SCALE = 50.0
CLIP_NORM = 0.001
BETA_ONE = 0.9
BETA_TWO = 0.98
ADAM_EPS = 1e-08
LEARN_RATE = 0.05
VECTOR_RATE = 0.3
DECAY_RATE = 0.01
NEG_BIG = -1e30
HALF = D // 2
CHUNK = HALF // 4
EXP2_SCALE = HD ** (-0.5) * 1.4426950408889634

F32 = jnp.float32
BF16 = jnp.bfloat16
VMEM = pl.BlockSpec(memory_space=pltpu.VMEM)
SMEM = pl.BlockSpec(memory_space=pltpu.SMEM)
ANY = pl.BlockSpec(memory_space=pl.ANY)


def nn(a, b):
    return jnp.dot(a, b, preferred_element_type=F32)


def nt(a, b):
    return lax.dot_general(a, b, (((1,), (1,)), ((), ())), preferred_element_type=F32)


def tn(a, b):
    return lax.dot_general(a, b, (((0,), (0,)), ((), ())), preferred_element_type=F32)


def exact(a, b, dims):
    return lax.dot_general(
        a, b, (dims, ((), ())), precision=lax.Precision.HIGHEST, preferred_element_type=F32
    )


def iota(shape, axis):
    return lax.broadcasted_iota(jnp.int32, shape, axis)


def low_pair(value):
    high = value.astype(BF16)
    return high, (value - high.astype(F32)).astype(BF16)


def aligned(start, size, unit):
    return pl.ds(pl.multiple_of(start, unit), size)


def assemble(dst, own, other, opt):
    dst[aligned(HALF * opt, HALF, 64), :] = own[0:HALF, :]
    dst[aligned(HALF * (1 - opt), HALF, 64), :] = other[0:HALF, :]


class Place:
    def __getitem__(self, i):
        if i == 0:
            return lax.axis_index("opt")
        me = lax.axis_index("dp")
        return (me & 3, me, (me >> 2) & 3)[i - 1]


def call(kernel, ins, outs, scratch=(), micros=5, name=None, vmem=12, after=()):
    if ins[0][1] is None:
        kernel = functools.partial(kernel, Place())
        ins = ins[1:]
    specs = [SMEM if s else VMEM for s, _ in ins] + [ANY] * len(after)
    count = len(ins)

    def body(*refs):
        kernel(*refs[:count], *refs[count + len(after) :])

    shapes = [jax.ShapeDtypeStruct(s, d) for s, d in outs]
    moved = sum(a.size * a.dtype.itemsize for _, a in ins)
    moved += sum(s.size * s.dtype.itemsize for s in shapes)
    return pl.pallas_call(
        body,
        out_shape=shapes,
        in_specs=specs,
        out_specs=[VMEM] * len(shapes),
        scratch_shapes=list(scratch),
        compiler_params=pltpu.CompilerParams(vmem_limit_bytes=vmem << 20),
        cost_estimate=pl.CostEstimate(
            flops=micros * 1100000000, bytes_accessed=moved, transcendentals=0
        ),
        name=name,
    )(*[a for _, a in ins], *after)


def head_stack(rows):
    lane_head = iota(rows.shape, 1) // HD
    zero = jnp.zeros_like(rows)
    return jnp.concatenate([jnp.where(lane_head == j, rows, zero) for j in range(4)], axis=0)


def attend_kernel(
    place, scalars, tokens, w_own, w_other, v_own, v_other,
    proj, att, inverse, kept, ownc, ownr, wanted, marks, vec, wfull, segc, segr, bias, vt,
):
    opt = place[0]
    assemble(wfull, w_own, w_other, opt)
    mine = v_own[...].astype(BF16).astype(F32)
    others = v_other[...].astype(BF16).astype(F32)
    first = opt == 0
    vec[0:6, :] = jnp.where(first, mine, others)
    vec[6:12, :] = jnp.where(first, others, mine)
    vec[12:16, :] = jnp.zeros((4, D), F32)

    position = iota((8, PAD), 1) + OFF * opt
    segment = jnp.zeros((8, PAD), jnp.int32)
    bound = jnp.int32(0)
    low_count = jnp.int32(0)
    for s in range(SEGS):
        bound = bound + scalars[s]
        segment = segment + (position >= bound).astype(jnp.int32)
        low_count = low_count + (bound <= WIN).astype(jnp.int32)
    mine = (segment < low_count).astype(jnp.int32) == (opt == 0).astype(jnp.int32)
    owned = jnp.where(mine, segment, -1)
    segr[...] = segment
    ownr[...] = owned
    for value, out in ((segment, segc), (owned, ownc)):
        value = value.astype(F32)
        for t in range(PAD // 128):
            rows = min(128, WIN - 128 * t)
            turned = jnp.broadcast_to(value[0:1, 128 * t : 128 * t + 128], (128, 128)).T
            out[128 * t : 128 * t + rows, :] = turned[0:rows].astype(jnp.int32)
    row, col = iota((2 * PAIRS, 128), 0), iota((2 * PAIRS, 128), 1)
    by_row = jnp.zeros((2 * PAIRS, 128), jnp.int32)
    by_col = jnp.zeros((2 * PAIRS, 128), jnp.int32)
    mark = jnp.zeros((2 * PAIRS, 128), jnp.int32)
    for j in range(PAIRS):
        mark = jnp.where(row == j, scalars[SEGS + 2 * PAIRS + j], mark)
        for at in (j, PAIRS + j):
            by_row = jnp.where(row == at, scalars[SEGS + at], by_row)
            by_col = jnp.where(col == at, scalars[SEGS + at], by_col)
    wanted[0] = by_row
    wanted[1] = by_col
    marks[...] = jnp.where(col < 64, mark >> 5, mark & 31).astype(F32).astype(BF16)
    for i, (q0, k0, k1) in enumerate(BANDS):
        bias[BAND_ROWS[i] : BAND_ROWS[i + 1], :] = jnp.where(
            segc[k0:k1, :] == segr[0:1, q0 : q0 + BLOCK], 0.0, NEG_BIG
        )

    x = tokens[aligned(OFF * opt, WIN, 64), :]
    bias_row = jnp.concatenate([vec[0:1, :], jnp.zeros((1, D), F32), vec[1:2, :]], axis=1)
    for first in range(0, 3 * D, 512):
        cols = slice(first, min(first + 512, 3 * D))
        proj[0:WIN, cols] = (nn(x, wfull[:, cols]) + bias_row[:, cols]).astype(BF16)
    proj[WIN:PAD, :] = jnp.zeros((PAD - WIN, 3 * D), BF16)

    def group(g, carry):
        def lanes(part):
            return aligned(part * D + 128 * g, 128, 128)

        for t in range(PAD // 128):
            vt[:, 128 * t : 128 * t + 128] = (
                proj[128 * t : 128 * t + 128, lanes(2)].astype(F32).T.astype(BF16)
            )
        for i, (q0, k0, k1) in enumerate(BANDS):
            stack = head_stack(proj[q0 : q0 + BLOCK, lanes(0)])
            st = nt(proj[k0:k1, lanes(1)], stack)
            outs, probs, totals = [], [], []
            for j in range(4):
                t = (
                    st[:, j * BLOCK : (j + 1) * BLOCK] * EXP2_SCALE
                    + bias[BAND_ROWS[i] : BAND_ROWS[i + 1], :]
                )
                peak = jnp.max(t, axis=0, keepdims=True)
                powers = jnp.exp2(t - peak)
                total = jnp.sum(powers, axis=0, keepdims=True)
                totals.append(1.0 / total)
                inverse[g, j : j + 1, q0 : q0 + BLOCK] = totals[-1]
                probs.append(powers.astype(BF16))
                kept[g, BAND_ROWS[i] : BAND_ROWS[i + 1], j * BLOCK : (j + 1) * BLOCK] = probs[-1]
                if j % 2 == 1:
                    o = nn(vt[(j - 1) * HD : (j + 1) * HD, k0:k1], jnp.concatenate(probs[-2:], axis=1))
                    outs.append(o[0:HD, 0:BLOCK] * totals[-2])
                    outs.append(o[HD : 2 * HD, BLOCK : 2 * BLOCK] * totals[-1])
            rows = min(BLOCK, WIN - q0)
            att[q0 : q0 + rows, aligned(128 * g, 128, 128)] = (
                jnp.concatenate(outs, axis=0).T[0:rows].astype(BF16)
            )
        return carry

    lax.fori_loop(0, 3, group, 0)


def attend(place, scalars, arrays):
    return call(
        attend_kernel,
        [(1, place), (1, scalars)] + [(0, a) for a in arrays],
        [
            ((PAD, 3 * D), BF16),
            ((WIN, D), BF16),
            ((3, 4, PAD), F32),
            ((3, BAND_ROWS[-1], 4 * BLOCK), BF16),
            ((WIN, 128), jnp.int32),
            ((8, PAD), jnp.int32),
            ((2, 2 * PAIRS, 128), jnp.int32),
            ((2 * PAIRS, 128), BF16),
            ((16, D), F32),
            ((D, 3 * D), BF16),
        ],
        [
            pltpu.VMEM((WIN, 128), jnp.int32),
            pltpu.VMEM((8, PAD), jnp.int32),
            pltpu.VMEM((BAND_ROWS[-1], 128), F32),
            pltpu.VMEM((128, PAD), BF16),
        ],
        micros=8,
        name="attend",
    )


def cast_kernel(weights, wo, wu, wd):
    wo[...] = weights[:, 3 * D : 4 * D].astype(BF16)
    wu[...] = weights[:, 4 * D : 4 * D + FF].astype(BF16)
    wd[...] = weights[:, 4 * D + FF : 4 * D + 2 * FF].astype(BF16)


def cast(weights, after):
    shapes = [((HALF, c), BF16) for c in (D, FF, FF)]
    return call(cast_kernel, [(0, weights)], shapes, name="cast", vmem=4, after=after)


def bias_of(vec, c):
    first, last = 256 * c, 256 * c + 256
    parts = []
    while first < last:
        row, col = divmod(first, D)
        size = min(D - col, last - first)
        parts.append(vec[3 + row : 4 + row, col : col + size])
        first += size
    return parts[0] if len(parts) == 1 else jnp.concatenate(parts, axis=1)


TAIL = (
    -0.11376862874824702, 0.44333253986048965, -0.3177007191690967, 0.3247801682810717,
    0.04569401949235749, 0.11766263932151709,
)


def normal_parts(u):
    bell = jnp.exp2(u * u * (-0.5 * LOG2E))
    t = pl.reciprocal(jnp.abs(u) * (0.39 * 0.7071067811865476) + 1.0)
    tail = TAIL[0]
    for coefficient in TAIL[1:]:
        tail = tail * t + coefficient
    tail = tail * t * bell
    return jnp.where(u < 0.0, tail, 1.0 - tail), bell


def mlp_kernel(
    place, wanted, att, tokens, ownr, vec, wo_own, wo_other, wu_own, wu_other,
    wd_own, wd_other, xhat1, inv1, hlow, act, slope, xhat2, inv2, unit, uscale, wo, wu, wd,
    ench, encl,
):
    opt = place[0]
    assemble(wo, wo_own, wo_other, opt)
    assemble(wu, wu_own, wu_other, opt)
    assemble(wd, wd_own, wd_other, opt)

    def norm(v):
        centred = v - jnp.mean(v, axis=1, keepdims=True)
        inverse = lax.rsqrt(jnp.mean(centred * centred, axis=1, keepdims=True) + LN_EPS)
        return centred * inverse, inverse

    def block(i, carry):
        r = aligned(i * WIDE_ROWS, WIDE_ROWS, 64)
        x = tokens[aligned(OFF * opt + i * WIDE_ROWS, WIDE_ROWS, 64), :].astype(F32)
        normed, inverse = norm(nn(att[r, :], wo[...]) + vec[2:3, :] + x)
        xhat1[r, :] = normed
        inv1[r, :] = jnp.broadcast_to(inverse, (WIDE_ROWS, 128))
        h = normed * vec[8:9, :] + vec[9:10, :]
        low = h.astype(BF16)
        hlow[r, :] = low
        for c in range(6):
            cols = slice(c * 256, (c + 1) * 256)
            u = nn(low, wu[:, cols]) + bias_of(vec, c)
            half, bell = normal_parts(u)
            act[r, cols] = (u * half).astype(BF16)
            slope[r, cols] = half + u * bell * 0.3989422804014327
        normed, inverse = norm(nt(act[r, :], wd[...]) + vec[7:8, :] + h)
        xhat2[r, :] = normed
        inv2[r, :] = jnp.broadcast_to(inverse, (WIDE_ROWS, 128))
        high, rest = low_pair(normed * vec[10:11, :] + vec[11:12, :])
        ench[r, :] = high
        encl[r, :] = rest
        return carry

    lax.fori_loop(0, WIN // WIDE_ROWS, block, 0)

    onehot = jnp.where(wanted[0, :, 0:1] == ownr[0:1, 0:WIN], 1.0, 0.0)
    count = jnp.maximum(jnp.sum(onehot, axis=1, keepdims=True), 1.0)
    hot = onehot.astype(BF16)
    pooled = (nn(hot, ench[...]) + nn(hot, encl[...])) / count
    inverse_len = lax.rsqrt(jnp.sum(pooled * pooled, axis=1, keepdims=True) + POOL_EPS)
    unit[...] = pooled * inverse_len
    uscale[...] = jnp.broadcast_to(inverse_len / count, (2 * PAIRS, 128))


def mlp(place, wanted, att, tokens, ownr, vec, halves):
    return call(
        mlp_kernel,
        [(1, place), (0, wanted), (0, att), (0, tokens), (0, ownr), (0, vec)]
        + [(0, h) for h in halves],
        [
            ((WIN, D), F32),
            ((WIN, 128), F32),
            ((WIN, D), BF16),
            ((WIN, FF), BF16),
            ((WIN, FF), F32),
            ((WIN, D), F32),
            ((WIN, 128), F32),
            ((2 * PAIRS, D), F32),
            ((2 * PAIRS, 128), F32),
            ((D, D), BF16),
            ((D, FF), BF16),
            ((D, FF), BF16),
        ],
        [
            pltpu.VMEM((WIN, D), BF16),
            pltpu.VMEM((WIN, D), BF16),
        ],
        micros=10,
        name="mlp",
    )


def split_rows(grad, keep, send, place, *at):
    opt = place[0]
    for c in range(4):
        index = (c ^ place[1],) + at
        keep[index] = grad[aligned(HALF * opt + CHUNK * c, CHUNK, 16), :].astype(BF16)
        send[index] = grad[aligned(HALF * (1 - opt) + CHUNK * c, CHUNK, 16), :].astype(BF16)


def column_sums(value):
    return jnp.sum(value.reshape(-1, 8, D), axis=0)


def norm_backward(grad_at, normed_ref, inverse_ref, gain, out, low_out, sums, at, step=ROWS):
    def block(i, carry):
        scale_sum, shift_sum, bias_sum = carry
        r = aligned(i * step, step, 64)
        g = grad_at(r)
        normed = normed_ref[r, :]
        scaled = g * gain
        inner = (
            scaled
            - jnp.mean(scaled, axis=1, keepdims=True)
            - normed * jnp.mean(scaled * normed, axis=1, keepdims=True)
        ) * inverse_ref[r, 0:1]
        out[r, :] = inner
        low_out[r, :] = inner.astype(BF16)
        return (
            scale_sum + column_sums(g * normed),
            shift_sum + column_sums(g),
            bias_sum + column_sums(inner),
        )

    zero = jnp.zeros((8, D), F32)
    scale_sum, shift_sum, bias_sum = lax.fori_loop(0, WIN // step, block, (zero, zero, zero))
    sums[at : at + 1, :] = jnp.sum(bias_sum, axis=0, keepdims=True)
    sums[at + 1 : at + 2, :] = jnp.sum(scale_sum, axis=0, keepdims=True)
    sums[at + 2 : at + 3, :] = jnp.sum(shift_sum, axis=0, keepdims=True)


def down_kernel(
    place, count, order, wanted, units, ownc, uscale, xhat2, inv2, act, vec, *rest
):
    pieces, (dsec, dlow, keep, send, sums, queries, docs, marks, grad) = rest[:-9], rest[-9:]
    me = place[2]
    per = pieces[0].shape[0]
    for p, piece in enumerate(pieces):
        for j in range(per):
            at = order[p * per + j]
            r = slice(at * PAIRS, (at + 1) * PAIRS)
            both = piece[j].astype(F32)
            queries[r, :] = both[0:PAIRS, 0:D]
            docs[r, :] = both[PAIRS : 2 * PAIRS, 0:D]
            marks[r, :] = both[0:PAIRS, D : D + 128]
    total = count * PAIRS
    q = queries[...].astype(BF16)
    d = docs[...].astype(BF16)
    logits = SCORE_SCALE * nt(q, d)
    peak = jnp.max(logits, axis=1, keepdims=True)
    powers = jnp.exp(logits - peak)
    soft = powers / jnp.sum(powers, axis=1, keepdims=True)
    col = iota((total, total), 1)
    doc_id = ((col // PAIRS) ^ me) * PAIRS + lax.rem(col, PAIRS)
    hit = (marks[:, 0:1] * 32.0 + marks[:, 64:65]).astype(jnp.int32) == doc_id
    d_logits = (soft - jnp.where(hit, 1.0, 0.0)) * (SCORE_SCALE / total)
    high, rest_low = low_pair(d_logits[0:PAIRS, :])
    d_q = nn(high, d) + nn(rest_low, d)
    high, rest_low = low_pair(d_logits[:, 0:128].T[0:PAIRS, :])
    d_d = nn(high, q) + nn(rest_low, q)
    d_units = jnp.concatenate([d_q, d_d], axis=0)
    u = units[...]
    d_pool = uscale[:, 0:1] * (d_units - u * jnp.sum(u * d_units, axis=1, keepdims=True))
    hot = jnp.where(ownc[:, 0 : 2 * PAIRS] == wanted[1, 0:1, 0 : 2 * PAIRS], 1.0, 0.0).astype(BF16)
    high, rest_low = low_pair(d_pool)
    dsec[...] = nn(hot, high) + nn(hot, rest_low)
    norm_backward(lambda r: dsec[r, :], xhat2, inv2, vec[10:11, :], dsec, dlow, sums, 0)
    sums[3:8, :] = jnp.zeros((5, D), F32)
    for c in range(3):
        cols = slice(c * 512, (c + 1) * 512)
        grad[:, cols] = tn(dlow[...], act[:, cols])
    for c in range(4):
        split_rows(grad.at[:, c * D : (c + 1) * D], keep, send, place, c)


def down_backward(count, order, place, wanted, units, ownc, uscale, saved, vec, pieces, after):
    total = count * PAIRS
    return call(
        lambda place, *refs: down_kernel(place, count, order, *refs),
        [(1, place), (0, wanted), (0, units), (0, ownc), (0, uscale)]
        + [(0, s) for s in saved]
        + [(0, vec)]
        + [(0, p) for p in pieces],
        [
            ((WIN, D), F32),
            ((WIN, D), BF16),
            ((4, 4, CHUNK, D), BF16),
            ((4, 4, CHUNK, D), BF16),
            ((8, D), F32),
        ],
        [
            pltpu.VMEM((total, D), F32),
            pltpu.VMEM((total, D), F32),
            pltpu.VMEM((total, 128), F32),
            pltpu.VMEM((D, FF), F32),
        ],
        micros=4,
        name="down_backward",
        after=after,
    )


def up_kernel(place, dlow, slope, hlow, wd, dup, keep, send, sums, grad):
    for c in range(3):
        cols = slice(c * 512, (c + 1) * 512)
        part = (nn(dlow[...], wd[:, cols]) * slope[:, cols]).astype(BF16)
        dup[:, cols] = part
        column_sum = jnp.sum(part.astype(F32), axis=0, keepdims=True)
        for j in range(4):
            at = 512 * c + 128 * j
            sums[at // D : at // D + 1, at % D : at % D + 128] = column_sum[:, 128 * j : 128 * j + 128]
        grad[:, cols] = tn(hlow[...], dup[:, cols])
    for c in range(4):
        split_rows(grad.at[:, c * D : (c + 1) * D], keep, send, place, c)


def up_backward(place, dlow, slope, hlow, wd, after):
    return call(
        up_kernel,
        [(1, place)] + [(0, a) for a in (dlow, slope, hlow, wd)],
        [((WIN, FF), BF16), ((4, 4, CHUNK, D), BF16), ((4, 4, CHUNK, D), BF16), ((4, D), F32)],
        [pltpu.VMEM((D, FF), F32)],
        micros=3,
        name="up_backward",
        after=after,
    )


def first_kernel(
    place, dup, dsec, xhat1, inv1, att, vec, wu, wo,
    dfirst, datt, delta, okeep, osend, sums, grad, dlow,
):
    norm_backward(
        lambda r: nt(dup[r, :], wu[...]) + dsec[r, :],
        xhat1, inv1, vec[8:9, :], dfirst, dlow, sums, 0, WIDE_ROWS,
    )
    sums[3:8, :] = jnp.zeros((5, D), F32)
    grad[...] = tn(att[...], dlow[...])
    split_rows(grad, okeep, osend, place)
    da = nt(dlow[...], wo[...]).astype(BF16)
    datt[0:WIN, :] = da
    datt[WIN:PAD, :] = jnp.zeros((PAD - WIN, D), BF16)
    high, rest = low_pair(da.astype(F32) * att[...].astype(F32))
    heads = (iota((16, D), 1) // HD == iota((16, D), 0)).astype(F32).astype(BF16)
    delta[:, 0:WIN] = nt(heads, high) + nt(heads, rest)
    delta[:, WIN:PAD] = jnp.zeros((16, PAD - WIN), F32)


def first_backward(place, dup, dsec, xhat1, inv1, att, vec, wu, wo, after):
    return call(
        first_kernel,
        [(1, place)] + [(0, a) for a in (dup, dsec, xhat1, inv1, att, vec, wu, wo)],
        [
            ((WIN, D), F32),
            ((PAD, D), BF16),
            ((16, PAD), F32),
            ((4, CHUNK, D), BF16),
            ((4, CHUNK, D), BF16),
            ((8, D), F32),
        ],
        [
            pltpu.VMEM((D, D), F32),
            pltpu.VMEM((WIN, D), BF16),
        ],
        micros=3,
        name="first_backward",
        after=after,
    )


def heads_kernel(place, g, tokens, proj, datt, inverse, kept, delta, *rest):
    rest, (dproj, keep, send, sums, kt, dk, dv, grad, ktmp, stmp) = rest[:-10], rest[-10:]

    def lanes(part):
        return slice(part * D + 128 * g, part * D + 128 * g + 128)

    for t in range(PAD // 128):
        kt[:, 128 * t : 128 * t + 128] = (
            proj[128 * t : 128 * t + 128, lanes(1)].astype(F32).T.astype(BF16)
        )
    dk[...] = jnp.zeros_like(dk)
    dv[...] = jnp.zeros_like(dv)
    for i, (q0, k0, k1) in enumerate(BANDS):
        qs = head_stack(proj[q0 : q0 + BLOCK, lanes(0)])
        gs = head_stack(datt[q0 : q0 + BLOCK, lanes(0)])
        dp = nt(proj[k0:k1, lanes(2)], gs)
        probs, d_scores, dq = [], [], []
        for j in range(4):
            cols = slice(j * BLOCK, (j + 1) * BLOCK)
            prob = kept[g, BAND_ROWS[i] : BAND_ROWS[i + 1], cols].astype(F32)
            prob = prob * inverse[g, j : j + 1, q0 : q0 + BLOCK]
            ds = prob * (dp[:, cols] - delta[4 * g + j : 4 * g + j + 1, q0 : q0 + BLOCK])
            ds = ds.astype(BF16)
            probs.append(prob.astype(BF16))
            d_scores.append(ds)
            if j % 2 == 1:
                part = nn(
                    kt[(j - 1) * HD : (j + 1) * HD, k0:k1], jnp.concatenate(d_scores[-2:], axis=1)
                )
                dq.append(part[0:HD, 0:BLOCK])
                dq.append(part[HD : 2 * HD, BLOCK : 2 * BLOCK])
        dv[k0:k1, :] += nn(jnp.concatenate(probs, axis=1), gs)
        dk[k0:k1, :] += nn(jnp.concatenate(d_scores, axis=1), qs)
        rows = min(BLOCK, WIN - q0)
        dqs = jnp.concatenate(dq, axis=0).T[0:rows] * HD ** (-0.5)
        dproj[q0 : q0 + rows, 0:128] = dqs.astype(BF16)
    dproj[:, 128:256] = (dk[...] * HD ** (-0.5)).astype(BF16)
    dproj[:, 256:384] = dv[...].astype(BF16)
    grad[...] = tn(tokens[aligned(OFF * place[0], WIN, 64), :], dproj[...])
    q_sum = jnp.sum(dproj[:, 0:128].astype(F32), axis=0, keepdims=True)
    v_sum = jnp.sum(dproj[:, 256:384].astype(F32), axis=0, keepdims=True)
    sums[0:1, :] = q_sum
    sums[1:2, :] = v_sum
    sums[2:8, :] = jnp.zeros((6, 128), F32)
    if g < 2:
        split_rows(grad, keep, send, place)
        return
    parts, (dsums, usums, fsums, zero, one) = rest[:6], rest[6:]
    split_rows(grad, ktmp, stmp, place)
    for dst, out_part, blocks in (
        (keep, parts[0], (parts[2], parts[4], ktmp)),
        (send, parts[1], (parts[3], parts[5], stmp)),
    ):
        dst[:, :, 3 * D : 4 * D] = out_part[...]
        for h, part in enumerate(blocks):
            for c in range(3):
                dst[:, :, D * c + 128 * h : D * c + 128 * h + 128] = part[
                    :, :, 128 * c : 128 * c + 128
                ]
    rows = jnp.concatenate(
        [
            jnp.concatenate([zero[0:1], one[0:1], q_sum], axis=1),
            jnp.concatenate([zero[1:2], one[1:2], v_sum], axis=1),
            fsums[0:1, :],
            usums[0:4, :],
            dsums[0:1, :],
            fsums[1:3, :],
            dsums[1:3, :],
            jnp.zeros((4, D), F32),
        ],
        axis=0,
    ).astype(BF16)
    for c in range(4):
        for j in range(3):
            block = rows[:, 128 * j : 128 * j + 128]
            keep[c, 16 * j : 16 * j + 16, 4 * D : 4 * D + 128] = block
            send[c, 16 * j : 16 * j + 16, 4 * D : 4 * D + 128] = block


def heads_backward(g, place, ins, more, after):
    part = ((4, CHUNK, 4 * D + 128 if g == 2 else D), BF16)
    return call(
        lambda place, *refs: heads_kernel(place, g, *refs),
        [(1, place)] + [(0, a) for a in tuple(ins) + tuple(more)],
        [((WIN, D), BF16), part, part, ((8, 128), F32)],
        [
            pltpu.VMEM((128, PAD), BF16),
            pltpu.VMEM((WIN, 128), F32),
            pltpu.VMEM((WIN, 128), F32),
            pltpu.VMEM((D, D), F32),
            pltpu.VMEM((4, CHUNK, D), BF16),
            pltpu.VMEM((4, CHUNK, D), BF16),
        ],
        micros=3,
        name="heads_backward",
        after=after,
    )


def input_kernel(dp0, dp1, dp2, dfirst, wfull, igrad, dproj):
    for g, part in enumerate((dp0, dp1, dp2)):
        for c in range(3):
            dproj[:, c * D + 128 * g : c * D + 128 * g + 128] = part[:, 128 * c : 128 * c + 128]
    igrad[...] = (nt(dproj[...], wfull[...]) + dfirst[...]).astype(BF16)


def input_backward(parts, dfirst, wqkv, after):
    return call(
        input_kernel,
        [(0, a) for a in tuple(parts) + (dfirst, wqkv)],
        [((WIN, D), BF16)],
        [pltpu.VMEM((WIN, 3 * D), BF16)],
        micros=2,
        name="input_backward",
        after=after,
    )[0]


def flips(axis, size, bits):
    return [(i, i ^ bits) for i in range(size)]


def pair(value):
    return swap(value, "opt", 2, 1)


def swap(value, axis, size, bits):
    return lax.ppermute(value, axis, flips(axis, size, bits))


def bit_groups(size):
    bits = size.bit_length() - 1
    return [(s, 1 << min(2, bits - s)) for s in range(0, bits, 2)]


def trades(values, n, shift):
    return [values[0]] + [swap(values[k], "dp", n, k << shift) for k in (1, 2, 3)]


def added(a, b):
    return (a.astype(F32) + b.astype(F32)).astype(BF16)


def core_sum_kernel(keep, other, *outs):
    for r, out in enumerate(outs):
        out[...] = added(keep[r], other[r])


def core_sum(keep, other, after):
    return call(
        core_sum_kernel,
        [(0, keep), (0, other)],
        [(keep.shape[1:], BF16)] * 4,
        name="core_sum",
        vmem=4,
        after=after,
    )


def pair_sum_kernel(bit, keep, other, stay, go):
    for i, r in enumerate((0, 3 - bit)):
        stay[i] = added(keep[r], other[r])
        go[i] = added(keep[r + bit], other[r + bit])


def pair_sum(bit, keep, other, after):
    return call(
        functools.partial(pair_sum_kernel, bit),
        [(0, keep), (0, other)],
        [((2,) + keep.shape[1:], BF16)] * 2,
        name="pair_sum",
        vmem=4,
        after=after,
    )


def wide_step_kernel(down, dother, up, uother, dkeep, dsend, ukeep, usend):
    dkeep[...] = added(down[0], dother[0])
    dsend[...] = added(down[1], dother[1])
    ukeep[...] = added(up[0], uother[0])
    usend[...] = added(up[1], uother[1])


def wide_step(parts, after):
    return call(
        wide_step_kernel,
        [(0, p) for p in parts],
        [((4, CHUNK, D), BF16)] * 4,
        name="wide_step",
        vmem=4,
        after=after,
    )


def total_of(refs, at):
    a, b, c, d = (ref[at].astype(F32) for ref in refs)
    return ((a + b) + (c + d)).astype(BF16)


def wide_plane_kernel(place, down, dother, up, uother, mine, send):
    z = place[3]
    for p, (keep, other) in enumerate(((down, dother), (up, uother))):
        for i, bits in enumerate((0, 2)):
            mine[2 * i + p] = added(keep[z ^ bits], other[z ^ bits])
            send[2 * i + p] = added(keep[z ^ bits ^ 1], other[z ^ bits ^ 1])


def wide_plane_sum(place, parts, after):
    return call(
        wide_plane_kernel,
        [(1, place)] + [(0, p) for p in parts],
        [((4, CHUNK, D), BF16)] * 2,
        name="wide_plane_sum",
        vmem=4,
        after=after,
    )


def wide_half_kernel(keep, other, mine, send):
    mine[...] = added(keep[0:2], other[0:2])
    send[...] = added(keep[2:4], other[2:4])


def wide_half(keep, other, after):
    return call(
        wide_half_kernel,
        [(0, keep), (0, other)],
        [((2, CHUNK, D), BF16)] * 2,
        name="wide_half",
        vmem=4,
        after=after,
    )


def low_plane_kernel(a, b, c, d, out):
    out[...] = total_of((a, b, c, d), slice(None))


def low_plane_sum(parts, after=()):
    return call(
        low_plane_kernel,
        [(0, p) for p in parts],
        [(parts[0].shape, BF16)],
        name="low_plane_sum",
        vmem=4,
        after=after,
    )[0]


def low_next_kernel(keep, other, out):
    out[...] = added(keep[...], other[...])


def low_next(keep, other, after=()):
    return call(
        low_next_kernel,
        [(0, keep), (0, other)],
        [(keep.shape, BF16)],
        name="low_next",
        vmem=4,
        after=after,
    )[0]


def low_last_kernel(keep, other, out, vgrad):
    out[...] = added(keep[:, 0 : 4 * D], other[:, 0 : 4 * D])
    vgrad[...] = added(keep[:, 4 * D : 4 * D + 128], other[:, 4 * D : 4 * D + 128])


def low_last(keep, other, after):
    return call(
        low_last_kernel,
        [(0, keep), (0, other)],
        [((CHUNK, 4 * D), BF16), ((CHUNK, 128), BF16)],
        name="low_last",
        vmem=4,
        after=after,
    )


def chain_kernel(*refs):
    ins, out = refs[:-1], refs[-1]
    at = 0
    for ref in ins:
        flat = ref.reshape(-1, CHUNK, D)
        out[at : at + flat.shape[0]] = flat[...]
        at += flat.shape[0]


def chain(parts, after=()):
    count = sum(p.size for p in parts) // (CHUNK * D)
    return call(
        chain_kernel,
        [(0, p) for p in parts],
        [((count, CHUNK, D), BF16)],
        name="chain",
        vmem=4,
        after=after,
    )[0]


def rest_sum(value, n):
    bit = 16
    while bit < n:
        other = swap(value, "dp", n, bit)
        value = (value.astype(F32) + other.astype(F32)).astype(BF16)
        bit *= 2
    return value


def join_kernel(*refs):
    ins, out = refs[:-1], refs[-1]
    for i, ref in enumerate(ins):
        out[i] = ref[...]


def join(parts, after=()):
    return call(
        join_kernel,
        [(0, p) for p in parts],
        [((len(parts),) + parts[0].shape, parts[0].dtype)],
        name="join",
        vmem=4,
        after=after,
    )[0]


def pack_kernel(marks, unit, other, units, packed):
    both = unit[...] + other[...]
    units[...] = both
    packed[:, 0:D] = both.astype(BF16)
    packed[:, D : D + 128] = marks[...]


def pack(marks, unit, other):
    return call(
        pack_kernel,
        [(0, marks), (0, unit), (0, other)],
        [(unit.shape, F32), ((2 * PAIRS, D + 128), BF16)],
        name="pack",
        vmem=4,
    )


def squares_of(parts):
    acc = jnp.zeros((8, D), F32)
    for part in parts:
        flat = part.reshape(-1, CHUNK, part.shape[-1])
        for k in range(flat.shape[0]):
            for c in range(0, part.shape[-1], D):
                v = flat[k, :, c : c + D].astype(F32)
                acc = acc + jnp.sum((v * v).reshape(CHUNK // 8, 8, D), axis=0)
    return acc[:, 0:128] + acc[:, 128:256] + acc[:, 256:384]


def wide_squares_kernel(*refs):
    refs[-1][...] = squares_of(refs[:-1])


def squares_kernel(place, *refs):
    parts, (vgrad, before, out) = refs[:-3], refs[-3:]
    acc = squares_of(parts) + before[...]
    row = iota((16, 128), 0)
    low_row = 6 * place[0]
    mine = (row >= low_row) & (row < low_row + 6)
    for j in range(3):
        v = jnp.where(mine, vgrad[16 * j : 16 * j + 16, :].astype(F32), 0.0)
        v = v * v
        acc = acc + (v[0:8] + v[8:16])
    out[...] = acc


def squares(place, parts, vgrad=None, before=None, after=()):
    ins = [(0, p) for p in parts]
    kernel = wide_squares_kernel
    if before is not None:
        ins = [(1, place)] + ins + [(0, vgrad), (0, before)]
        kernel = squares_kernel
    return call(kernel, ins, [((8, 128), F32)], name="squares", vmem=4, after=after)[0]


def merge_kernel(place, igrad, other, out, flag):
    flag[...] = jnp.zeros((8, 128), F32)

    @pl.when(place[0] == 0)
    def low_core():
        out[0:OFF, :] = igrad[0:OFF, :]
        out[OFF:WIN, :] = added(igrad[OFF:WIN, :], other[0 : WIN - OFF, :])
        out[WIN:SEQ, :] = other[WIN - OFF : WIN, :]

    @pl.when(place[0] != 0)
    def high_core():
        out[0:OFF, :] = other[0:OFF, :]
        out[OFF:WIN, :] = added(other[OFF:WIN, :], igrad[0 : WIN - OFF, :])
        out[WIN:SEQ, :] = igrad[WIN - OFF : WIN, :]


def merge(place, igrad, other, after):
    return call(
        merge_kernel,
        [(1, place), (0, igrad), (0, other)],
        [((SEQ, D), BF16), ((8, 128), F32)],
        name="merge",
        vmem=4,
        after=after,
    )


def adamw(parameter, first_state, second, clipped, rate):
    first_new = first_state + (1.0 - BETA_ONE) * clipped
    second_new = second + (1.0 - BETA_TWO) * clipped * clipped
    root = (1.0 - BETA_TWO**STEP) ** 0.5
    below = pl.reciprocal(second_new * lax.rsqrt(second_new) + ADAM_EPS * root)
    scale = rate * root / (1.0 - BETA_ONE**STEP)
    return parameter - scale * (first_new * below), first_new, second_new


def decay_kernel(w, m, v, pv, pm, pq, nw, nm, nv, npv, npm, npq):
    for ins, outs, rate in (
        ((w, m, v), (nw, nm, nv), LEARN_RATE),
        ((pv, pm, pq), (npv, npm, npq), VECTOR_RATE),
    ):
        for ref, out, scale in zip(ins, outs, (1.0 - rate * DECAY_RATE, BETA_ONE, BETA_TWO)):
            out[...] = ref[...] * scale


def decay(arrays, after):
    return call(
        decay_kernel,
        [(0, a) for a in arrays],
        [(a.shape, F32) for a in arrays],
        name="decay",
        vmem=4,
        after=after,
    )


def adamw_kernel(*refs):
    place = Place()
    sums, refs = refs[:2], refs[2:]
    (vgrad, w, m, v, pv, pm, pq), refs = refs[:7], refs[7:]
    wide, low, refs = refs[:4], refs[4:8], refs[8:]
    outs, (npv, npm, npq, norm), scrs, sems = refs[:4], refs[4:8], refs[8:12], refs[12]
    opt = place[0]
    total = sums[0][...] + sums[1][...]
    total = jnp.sum(jnp.sum(total, axis=1, keepdims=True), axis=0, keepdims=True)
    grad_norm = jnp.sqrt(total)
    factor = jnp.minimum(1.0, CLIP_NORM / (grad_norm + 1e-06))
    norm[...] = grad_norm
    for j in range(3):
        cols = slice(128 * j, 128 * j + 128)
        g = vgrad[16 * j : 16 * j + 16, :].astype(F32)
        g = jnp.where(opt == 0, g[0:6], g[6:12])
        a, b, c = adamw(pv[:, cols], pm[:, cols], pq[:, cols], g * factor, VECTOR_RATE)
        npv[:, cols] = a
        npm[:, cols] = b
        npq[:, cols] = c

    def block(grad, rows, cols):
        new = adamw(w[rows, cols], m[rows, cols], v[rows, cols], grad * factor, LEARN_RATE)
        for scr, value in zip(scrs, new + (new[0].astype(BF16),)):
            scr[rows, cols] = value

    def copies(r, i):
        rows = aligned(CHUNK * (place[1] ^ r) + i * 16, 16, 16)
        return [
            pltpu.make_async_copy(scr.at[rows, :], out.at[rows, :], sems.at[3 * r + i, j])
            for j, (scr, out) in enumerate(zip(scrs, outs))
        ]

    for r in range(4):

        def step(i, carry, r=r):
            rows = aligned(CHUNK * (place[1] ^ r) + i * 16, 16, 16)
            here = aligned(i * 16, 16, 16)
            for j in range(4):
                at = D * (place[3] ^ j)
                for p, start in enumerate((4 * D + FF, 4 * D)):
                    grad = wide[r][2 * j + p, here, :].astype(F32)
                    block(grad, rows, aligned(start + at, D, 128))
            for c in range(4):
                grad = low[r][here, D * c : D * c + D].astype(F32)
                block(grad, rows, slice(D * c, D * c + D))
            for copy in copies(r, i):
                copy.start()
            return carry

        lax.fori_loop(0, CHUNK // 16, step, 0)
    for r in range(4):

        def finish(i, carry, r=r):
            for copy in copies(r, i):
                copy.wait()
            return carry

        lax.fori_loop(0, CHUNK // 16, finish, 0)


def update(place, sums, vgrad, w, m, v, pv, pm, pq, parts):
    ins = tuple(sums) + (vgrad, w, m, v, pv, pm, pq) + tuple(parts)
    shapes = [(w.shape, F32)] * 3 + [(w.shape, BF16)] + [(pv.shape, F32)] * 3 + [((1, 1), F32)]
    return pl.pallas_call(
        adamw_kernel,
        out_shape=[jax.ShapeDtypeStruct(s, d) for s, d in shapes],
        in_specs=[VMEM] * len(ins),
        out_specs=[ANY] * 4 + [VMEM] * 4,
        scratch_shapes=[
            pltpu.VMEM(w.shape, F32),
            pltpu.VMEM(w.shape, F32),
            pltpu.VMEM(w.shape, F32),
            pltpu.VMEM(w.shape, BF16),
            pltpu.SemaphoreType.DMA((12, 4)),
        ],
        compiler_params=pltpu.CompilerParams(vmem_limit_bytes=16 << 20),
        cost_estimate=pl.CostEstimate(
            flops=4000000000, bytes_accessed=26 * w.size, transcendentals=0
        ),
        name="adamw",
    )(*ins)


def shards(
    n,
    tokens,
    lengths,
    query_index,
    doc_index,
    targets,
    weights,
    first_moment,
    second_moment,
    vectors,
    vec_first,
    vec_second,
):
    place = None
    scalars = jnp.concatenate([lengths.reshape(SEGS), query_index, doc_index, targets])
    groups = bit_groups(n)

    w_own = weights[:, : 3 * D].astype(BF16)
    w_other = pair(w_own)
    v_other = pair(vectors)
    wo_own, wu_own, wd_own = cast(weights, [w_own])
    wo = (wo_own, pair(wo_own))
    wu = (wu_own, pair(wu_own))
    wd = (wd_own, pair(wd_own))

    proj, att, inverse, kept, ownc, ownr, wanted, marks, vec, wqkv = attend(
        place, scalars, (tokens, w_own, w_other, vectors, v_other)
    )
    xhat1, inv1, hlow, act, slope, xhat2, inv2, unit, uscale, wo, wu, wd = mlp(
        place, wanted, att, tokens, ownr, vec, wo + wu + wd
    )
    units, packed = pack(marks, unit, pair(unit))
    groups = bit_groups(n)
    order = [0]
    stack = packed
    for i, (shift, size) in enumerate(groups[1:] + groups[:1]):
        pieces = [stack] + [swap(stack, "dp", n, k << shift) for k in range(1, size)]
        order = [o | (k << shift) for k in range(size) for o in order]
        if i < len(groups) - 1:
            stack = join(pieces).reshape(-1, 2 * PAIRS, D + 128)
    decayed = decay(
        (weights, first_moment, second_moment, vectors, vec_first, vec_second), [packed]
    )
    dsec, dlow, keep, send, dsums = down_backward(
        n, order, place, wanted, units, ownc, uscale, (xhat2, inv2, act), vec, pieces,
        decayed,
    )
    other = pair(send)
    dup, ukeep, usend, usums = up_backward(place, dlow, slope, hlow, wd, [])
    down, go = pair_sum(1, keep, other, [dup])
    dother = swap(go, "dp", n, 1)
    up, go = pair_sum(2, ukeep, pair(usend), [down])
    uother = swap(go, "dp", n, 2)
    dfirst, datt, delta, okeep, osend, fsums = first_backward(
        place, dup, dsec, xhat1, inv1, att, vec, wu, wo, [up]
    )
    ins = (tokens, proj, datt, inverse, kept, delta)
    part0, keep0, send0, sums0 = heads_backward(0, place, ins, (), [])
    down, dsend, up, usend = wide_step((down, dother, up, uother), [part0])
    dother, uother = swap(dsend, "dp", n, 2), swap(usend, "dp", n, 1)
    part1, keep1, send1, sums1 = heads_backward(1, place, ins, (), [down])
    wide, go = wide_plane_sum(place, (down, dother, up, uother), [part1])
    wother = swap(go, "dp", n, 4)
    part2, keep, send, _ = heads_backward(
        2, place, ins,
        (okeep, osend, keep0, send0, keep1, send1, dsums, usums, fsums, sums0, sums1),
        [wide, part1],
    )
    wide, go = wide_half(wide, wother, [part2])
    send, wide, go = lax.optimization_barrier((send, wide, go))
    wother = swap(go, "dp", n, 8)
    other = pair(send)
    igrad = input_backward((part0, part1, part2), dfirst, wqkv, [wide])
    iother = pair(igrad)
    low = core_sum(keep, other, [igrad])
    low_got = trades(low, n, 0)
    wide = rest_sum(low_next(wide, wother, [low[0]]), n)
    wide_got = trades([wide] * 4, n, 2)
    low = low_plane_sum(low_got, [wide])
    other = swap(low, "dp", n, 4)
    wide = chain(wide_got, [low])
    wide = trades([wide] * 4, n, 0)
    low = low_next(low, other, [wide[0]])
    other = swap(low, "dp", n, 8)
    input_grad, flag = merge(place, igrad, iother, [low])
    low, vgrad = low_last(low, other, [flag])
    low, vgrad = rest_sum(low, n), rest_sum(vgrad, n)
    low = trades([low] * 4, n, 0)
    sums = squares(place, low, vgrad, squares(place, wide, after=[low[0]]))
    sums = (sums, pair(sums))
    pieces = tuple(wide) + tuple(low)
    nw, nm, nv, nlow, npv, npm, npq, norm = update(
        place, sums, vgrad, *decayed, pieces,
    )
    return (norm.reshape(()), input_grad, nw, nm, nv, nlow, npv, npm, npq)


def solution(mesh):
    rows = P("opt", None)
    in_specs = (P("dp", None), P("dp", None), P("dp"), P("dp"), P("dp")) + (rows,) * 6
    out_specs = (P(), P("dp", None)) + (rows,) * 7
    n = mesh.shape["dp"]
    return jax.shard_map(
        functools.partial(shards, n),
        mesh=mesh,
        in_specs=in_specs,
        out_specs=out_specs,
        check_vma=False,
    )
```

```python
import functools

import jax
import jax.numpy as jnp
from jax import lax
from jax.experimental import pallas as pl
from jax.experimental.pallas import tpu as pltpu
from jax.sharding import PartitionSpec as P

D = 384
HEADS = 12
HD = 32
FF = 1536
SEQ = 1024
SEGS = 16
PAIRS = 8
STEP = 10

WIN = 576
OFF = SEQ - WIN
PAD = 640
BLOCK = 128
BANDS = tuple((q, max(0, q - 128), min(WIN, q + 256)) for q in range(0, WIN, BLOCK))
BAND_ROWS = tuple(sum(b[2] - b[1] for b in BANDS[:i]) for i in range(len(BANDS) + 1))
ROWS = 64
WIDE_ROWS = 192
LOG2E = 1.4426950408889634

LN_EPS = 1e-06
POOL_EPS = 1e-06
SCORE_SCALE = 50.0
CLIP_NORM = 0.001
BETA_ONE = 0.9
BETA_TWO = 0.98
ADAM_EPS = 1e-08
LEARN_RATE = 0.05
VECTOR_RATE = 0.3
DECAY_RATE = 0.01
NEG_BIG = -1e30
HALF = D // 2
CHUNK = HALF // 4
EXP2_SCALE = HD ** (-0.5) * 1.4426950408889634

F32 = jnp.float32
BF16 = jnp.bfloat16
VMEM = pl.BlockSpec(memory_space=pltpu.VMEM)
SMEM = pl.BlockSpec(memory_space=pltpu.SMEM)
ANY = pl.BlockSpec(memory_space=pl.ANY)


def nn(a, b):
    return jnp.dot(a, b, preferred_element_type=F32)


def nt(a, b):
    return lax.dot_general(a, b, (((1,), (1,)), ((), ())), preferred_element_type=F32)


def tn(a, b):
    return lax.dot_general(a, b, (((0,), (0,)), ((), ())), preferred_element_type=F32)


def exact(a, b, dims):
    return lax.dot_general(
        a, b, (dims, ((), ())), precision=lax.Precision.HIGHEST, preferred_element_type=F32
    )


def iota(shape, axis):
    return lax.broadcasted_iota(jnp.int32, shape, axis)


def low_pair(value):
    high = value.astype(BF16)
    return high, (value - high.astype(F32)).astype(BF16)


def aligned(start, size, unit):
    return pl.ds(pl.multiple_of(start, unit), size)


def assemble(dst, own, other, opt):
    dst[aligned(HALF * opt, HALF, 64), :] = own[0:HALF, :]
    dst[aligned(HALF * (1 - opt), HALF, 64), :] = other[0:HALF, :]


class Place:
    def __getitem__(self, i):
        if i == 0:
            return lax.axis_index("opt")
        me = lax.axis_index("dp")
        return (me & 3, me, (me >> 2) & 3)[i - 1]


def call(kernel, ins, outs, scratch=(), micros=5, name=None, vmem=12, after=()):
    if ins[0][1] is None:
        kernel = functools.partial(kernel, Place())
        ins = ins[1:]
    specs = [SMEM if s else VMEM for s, _ in ins] + [ANY] * len(after)
    count = len(ins)

    def body(*refs):
        kernel(*refs[:count], *refs[count + len(after) :])

    shapes = [jax.ShapeDtypeStruct(s, d) for s, d in outs]
    moved = sum(a.size * a.dtype.itemsize for _, a in ins)
    moved += sum(s.size * s.dtype.itemsize for s in shapes)
    return pl.pallas_call(
        body,
        out_shape=shapes,
        in_specs=specs,
        out_specs=[VMEM] * len(shapes),
        scratch_shapes=list(scratch),
        compiler_params=pltpu.CompilerParams(vmem_limit_bytes=vmem << 20),
        cost_estimate=pl.CostEstimate(
            flops=micros * 1100000000, bytes_accessed=moved, transcendentals=0
        ),
        name=name,
    )(*[a for _, a in ins], *after)


def head_stack(rows):
    lane_head = iota(rows.shape, 1) // HD
    zero = jnp.zeros_like(rows)
    return jnp.concatenate([jnp.where(lane_head == j, rows, zero) for j in range(4)], axis=0)


def attend_kernel(
    place, scalars, tokens, w_own, w_other, v_own, v_other,
    proj, att, lse, segc, segr, ownc, ownr, wanted, marks, vec, wfull, bias, vt,
):
    opt = place[0]
    assemble(wfull, w_own, w_other, opt)
    mine = v_own[...].astype(BF16).astype(F32)
    others = v_other[...].astype(BF16).astype(F32)
    first = opt == 0
    vec[0:6, :] = jnp.where(first, mine, others)
    vec[6:12, :] = jnp.where(first, others, mine)
    vec[12:16, :] = jnp.zeros((4, D), F32)

    position = iota((8, PAD), 1) + OFF * opt
    segment = jnp.zeros((8, PAD), jnp.int32)
    bound = jnp.int32(0)
    low_count = jnp.int32(0)
    for s in range(SEGS):
        bound = bound + scalars[s]
        segment = segment + (position >= bound).astype(jnp.int32)
        low_count = low_count + (bound <= WIN).astype(jnp.int32)
    mine = (segment < low_count).astype(jnp.int32) == (opt == 0).astype(jnp.int32)
    owned = jnp.where(mine, segment, -1)
    segr[...] = segment
    ownr[...] = owned
    for value, out in ((segment, segc), (owned, ownc)):
        value = value.astype(F32)
        for t in range(PAD // 128):
            rows = min(128, WIN - 128 * t)
            turned = jnp.broadcast_to(value[0:1, 128 * t : 128 * t + 128], (128, 128)).T
            out[128 * t : 128 * t + rows, :] = turned[0:rows].astype(jnp.int32)
    row, col = iota((2 * PAIRS, 128), 0), iota((2 * PAIRS, 128), 1)
    by_row = jnp.zeros((2 * PAIRS, 128), jnp.int32)
    by_col = jnp.zeros((2 * PAIRS, 128), jnp.int32)
    mark = jnp.zeros((2 * PAIRS, 128), jnp.int32)
    for j in range(PAIRS):
        mark = jnp.where(row == j, scalars[SEGS + 2 * PAIRS + j], mark)
        for at in (j, PAIRS + j):
            by_row = jnp.where(row == at, scalars[SEGS + at], by_row)
            by_col = jnp.where(col == at, scalars[SEGS + at], by_col)
    wanted[0] = by_row
    wanted[1] = by_col
    marks[...] = jnp.where(col < 64, mark >> 5, mark & 31).astype(F32).astype(BF16)
    for i, (q0, k0, k1) in enumerate(BANDS):
        bias[BAND_ROWS[i] : BAND_ROWS[i + 1], :] = jnp.where(
            segc[k0:k1, :] == segr[0:1, q0 : q0 + BLOCK], 0.0, NEG_BIG
        )

    x = tokens[aligned(OFF * opt, WIN, 64), :]
    bias_row = jnp.concatenate([vec[0:1, :], jnp.zeros((1, D), F32), vec[1:2, :]], axis=1)
    for first in range(0, 3 * D, 512):
        cols = slice(first, min(first + 512, 3 * D))
        proj[0:WIN, cols] = (nn(x, wfull[:, cols]) + bias_row[:, cols]).astype(BF16)
    proj[WIN:PAD, :] = jnp.zeros((PAD - WIN, 3 * D), BF16)

    def group(g, carry):
        def lanes(part):
            return aligned(part * D + 128 * g, 128, 128)

        for t in range(PAD // 128):
            vt[:, 128 * t : 128 * t + 128] = (
                proj[128 * t : 128 * t + 128, lanes(2)].astype(F32).T.astype(BF16)
            )
        for i, (q0, k0, k1) in enumerate(BANDS):
            stack = head_stack(proj[q0 : q0 + BLOCK, lanes(0)])
            st = nt(proj[k0:k1, lanes(1)], stack)
            outs, probs, totals = [], [], []
            for j in range(4):
                t = (
                    st[:, j * BLOCK : (j + 1) * BLOCK] * EXP2_SCALE
                    + bias[BAND_ROWS[i] : BAND_ROWS[i + 1], :]
                )
                peak = jnp.max(t, axis=0, keepdims=True)
                powers = jnp.exp2(t - peak)
                total = jnp.sum(powers, axis=0, keepdims=True)
                lse[g, j : j + 1, q0 : q0 + BLOCK] = peak + jnp.log2(total)
                probs.append(powers.astype(BF16))
                totals.append(1.0 / total)
                if j % 2 == 1:
                    o = nn(vt[(j - 1) * HD : (j + 1) * HD, k0:k1], jnp.concatenate(probs[-2:], axis=1))
                    outs.append(o[0:HD, 0:BLOCK] * totals[-2])
                    outs.append(o[HD : 2 * HD, BLOCK : 2 * BLOCK] * totals[-1])
            rows = min(BLOCK, WIN - q0)
            att[q0 : q0 + rows, aligned(128 * g, 128, 128)] = (
                jnp.concatenate(outs, axis=0).T[0:rows].astype(BF16)
            )
        return carry

    lax.fori_loop(0, 3, group, 0)


def attend(place, scalars, arrays):
    return call(
        attend_kernel,
        [(1, place), (1, scalars)] + [(0, a) for a in arrays],
        [
            ((PAD, 3 * D), BF16),
            ((WIN, D), BF16),
            ((3, 4, PAD), F32),
            ((WIN, 128), jnp.int32),
            ((8, PAD), jnp.int32),
            ((WIN, 128), jnp.int32),
            ((8, PAD), jnp.int32),
            ((2, 2 * PAIRS, 128), jnp.int32),
            ((2 * PAIRS, 128), BF16),
            ((16, D), F32),
            ((D, 3 * D), BF16),
        ],
        [
            pltpu.VMEM((BAND_ROWS[-1], 128), F32),
            pltpu.VMEM((128, PAD), BF16),
        ],
        micros=8,
        name="attend",
    )


def cast_kernel(weights, wq, wo, wu, wd, buffer, sems):
    spans = [(wq, 3 * D), (wo, D), (wu, FF), (wd, FF)]
    copies = [
        pltpu.make_async_copy(
            weights.at[:, i * D : (i + 1) * D], buffer.at[:, i * D : (i + 1) * D], sems.at[i]
        )
        for i in range(12)
    ]
    for copy in copies:
        copy.start()
    at = 0
    for out, width in spans:
        for part in range(width // D):
            copies[at].wait()
            out[:, part * D : (part + 1) * D] = buffer[:, at * D : (at + 1) * D].astype(BF16)
            at += 1


def cast(weights):
    return pl.pallas_call(
        cast_kernel,
        out_shape=[jax.ShapeDtypeStruct((HALF, c), BF16) for c in (3 * D, D, FF, FF)],
        in_specs=[ANY],
        out_specs=[VMEM] * 4,
        scratch_shapes=[pltpu.VMEM(weights.shape, F32), pltpu.SemaphoreType.DMA((12,))],
        compiler_params=pltpu.CompilerParams(vmem_limit_bytes=52 << 20),
        name="cast",
    )(weights)


def bias_of(vec, c):
    first, last = 256 * c, 256 * c + 256
    parts = []
    while first < last:
        row, col = divmod(first, D)
        size = min(D - col, last - first)
        parts.append(vec[3 + row : 4 + row, col : col + size])
        first += size
    return parts[0] if len(parts) == 1 else jnp.concatenate(parts, axis=1)


def mlp_kernel(
    place, wanted, att, tokens, ownr, vec, wo_own, wo_other, wu_own, wu_other,
    wd_own, wd_other, xhat1, inv1, hlow, act, up_proj, xhat2, inv2, unit, uscale, wo, wu, wd,
    ench, encl,
):
    opt = place[0]
    assemble(wo, wo_own, wo_other, opt)
    assemble(wu, wu_own, wu_other, opt)
    assemble(wd, wd_own, wd_other, opt)

    def norm(v):
        centred = v - jnp.mean(v, axis=1, keepdims=True)
        inverse = lax.rsqrt(jnp.mean(centred * centred, axis=1, keepdims=True) + LN_EPS)
        return centred * inverse, inverse

    def block(i, carry):
        r = aligned(i * WIDE_ROWS, WIDE_ROWS, 64)
        x = tokens[aligned(OFF * opt + i * WIDE_ROWS, WIDE_ROWS, 64), :].astype(F32)
        normed, inverse = norm(nn(att[r, :], wo[...]) + vec[2:3, :] + x)
        xhat1[r, :] = normed
        inv1[r, :] = jnp.broadcast_to(inverse, (WIDE_ROWS, 128))
        h = normed * vec[8:9, :] + vec[9:10, :]
        low = h.astype(BF16)
        hlow[r, :] = low
        for c in range(6):
            cols = slice(c * 256, (c + 1) * 256)
            u = nn(low, wu[:, cols]) + bias_of(vec, c)
            up_proj[r, cols] = u
            half = lax.erf(u * 0.7071067811865476) * 0.5 + 0.5
            act[r, cols] = (u * half).astype(BF16)
        normed, inverse = norm(nt(act[r, :], wd[...]) + vec[7:8, :] + h)
        xhat2[r, :] = normed
        inv2[r, :] = jnp.broadcast_to(inverse, (WIDE_ROWS, 128))
        high, rest = low_pair(normed * vec[10:11, :] + vec[11:12, :])
        ench[r, :] = high
        encl[r, :] = rest
        return carry

    lax.fori_loop(0, WIN // WIDE_ROWS, block, 0)

    onehot = jnp.where(wanted[0, :, 0:1] == ownr[0:1, 0:WIN], 1.0, 0.0)
    count = jnp.maximum(jnp.sum(onehot, axis=1, keepdims=True), 1.0)
    hot = onehot.astype(BF16)
    pooled = (nn(hot, ench[...]) + nn(hot, encl[...])) / count
    inverse_len = lax.rsqrt(jnp.sum(pooled * pooled, axis=1, keepdims=True) + POOL_EPS)
    unit[...] = pooled * inverse_len
    uscale[...] = jnp.broadcast_to(inverse_len / count, (2 * PAIRS, 128))


def slope_kernel(up_proj, out):
    def block(i, carry):
        r = aligned(i * 16, 16, 16)
        u = up_proj[r, :]
        half = lax.erf(u * 0.7071067811865476) * 0.5 + 0.5
        out[r, :] = half + u * jnp.exp2(u * u * (-0.5 * LOG2E)) * 0.3989422804014327
        return carry

    lax.fori_loop(0, WIN // 16, block, 0)


def slope_of(up_proj, after):
    return call(slope_kernel, [(0, up_proj)], [(up_proj.shape, F32)], name="slope", vmem=4, after=after)[0]


def mlp(place, wanted, att, tokens, ownr, vec, halves):
    return call(
        mlp_kernel,
        [(1, place), (0, wanted), (0, att), (0, tokens), (0, ownr), (0, vec)]
        + [(0, h) for h in halves],
        [
            ((WIN, D), F32),
            ((WIN, 128), F32),
            ((WIN, D), BF16),
            ((WIN, FF), BF16),
            ((WIN, FF), F32),
            ((WIN, D), F32),
            ((WIN, 128), F32),
            ((2 * PAIRS, D), F32),
            ((2 * PAIRS, 128), F32),
            ((D, D), BF16),
            ((D, FF), BF16),
            ((D, FF), BF16),
        ],
        [
            pltpu.VMEM((WIN, D), BF16),
            pltpu.VMEM((WIN, D), BF16),
        ],
        micros=10,
        name="mlp",
    )


def split_rows(grad, keep, send, place, *at):
    opt = place[0]
    for c in range(4):
        index = (c ^ place[1],) + at
        keep[index] = grad[aligned(HALF * opt + CHUNK * c, CHUNK, 16), :].astype(BF16)
        send[index] = grad[aligned(HALF * (1 - opt) + CHUNK * c, CHUNK, 16), :].astype(BF16)


def column_sums(value):
    return jnp.sum(value.reshape(-1, 8, D), axis=0)


def norm_backward(grad_at, normed_ref, inverse_ref, gain, out, low_out, sums, at, step=ROWS):
    def block(i, carry):
        scale_sum, shift_sum, bias_sum = carry
        r = aligned(i * step, step, 64)
        g = grad_at(r)
        normed = normed_ref[r, :]
        scaled = g * gain
        inner = (
            scaled
            - jnp.mean(scaled, axis=1, keepdims=True)
            - normed * jnp.mean(scaled * normed, axis=1, keepdims=True)
        ) * inverse_ref[r, 0:1]
        out[r, :] = inner
        low_out[r, :] = inner.astype(BF16)
        return (
            scale_sum + column_sums(g * normed),
            shift_sum + column_sums(g),
            bias_sum + column_sums(inner),
        )

    zero = jnp.zeros((8, D), F32)
    scale_sum, shift_sum, bias_sum = lax.fori_loop(0, WIN // step, block, (zero, zero, zero))
    sums[at : at + 1, :] = jnp.sum(bias_sum, axis=0, keepdims=True)
    sums[at + 1 : at + 2, :] = jnp.sum(scale_sum, axis=0, keepdims=True)
    sums[at + 2 : at + 3, :] = jnp.sum(shift_sum, axis=0, keepdims=True)


def down_kernel(
    place, count, order, wanted, units, ownc, uscale, xhat2, inv2, act, vec, *rest
):
    pieces, (dsec, dlow, keep, send, sums, queries, docs, marks, grad) = rest[:-9], rest[-9:]
    me = place[2]
    per = pieces[0].shape[0]
    for p, piece in enumerate(pieces):
        for j in range(per):
            at = order[p * per + j]
            r = slice(at * PAIRS, (at + 1) * PAIRS)
            both = piece[j].astype(F32)
            queries[r, :] = both[0:PAIRS, 0:D]
            docs[r, :] = both[PAIRS : 2 * PAIRS, 0:D]
            marks[r, :] = both[0:PAIRS, D : D + 128]
    total = count * PAIRS
    q = queries[...].astype(BF16)
    d = docs[...].astype(BF16)
    logits = SCORE_SCALE * nt(q, d)
    peak = jnp.max(logits, axis=1, keepdims=True)
    powers = jnp.exp(logits - peak)
    soft = powers / jnp.sum(powers, axis=1, keepdims=True)
    col = iota((total, total), 1)
    doc_id = ((col // PAIRS) ^ me) * PAIRS + lax.rem(col, PAIRS)
    hit = (marks[:, 0:1] * 32.0 + marks[:, 64:65]).astype(jnp.int32) == doc_id
    d_logits = (soft - jnp.where(hit, 1.0, 0.0)) * (SCORE_SCALE / total)
    high, rest_low = low_pair(d_logits[0:PAIRS, :])
    d_q = nn(high, d) + nn(rest_low, d)
    high, rest_low = low_pair(d_logits[:, 0:128].T[0:PAIRS, :])
    d_d = nn(high, q) + nn(rest_low, q)
    d_units = jnp.concatenate([d_q, d_d], axis=0)
    u = units[...]
    d_pool = uscale[:, 0:1] * (d_units - u * jnp.sum(u * d_units, axis=1, keepdims=True))
    hot = jnp.where(ownc[:, 0 : 2 * PAIRS] == wanted[1, 0:1, 0 : 2 * PAIRS], 1.0, 0.0).astype(BF16)
    high, rest_low = low_pair(d_pool)
    dsec[...] = nn(hot, high) + nn(hot, rest_low)
    norm_backward(lambda r: dsec[r, :], xhat2, inv2, vec[10:11, :], dsec, dlow, sums, 0)
    sums[3:8, :] = jnp.zeros((5, D), F32)
    for c in range(3):
        cols = slice(c * 512, (c + 1) * 512)
        grad[:, cols] = tn(dlow[...], act[:, cols])
    for c in range(4):
        split_rows(grad.at[:, c * D : (c + 1) * D], keep, send, place, c)


def down_backward(count, order, place, wanted, units, ownc, uscale, saved, vec, pieces, after):
    total = count * PAIRS
    return call(
        lambda place, *refs: down_kernel(place, count, order, *refs),
        [(1, place), (0, wanted), (0, units), (0, ownc), (0, uscale)]
        + [(0, s) for s in saved]
        + [(0, vec)]
        + [(0, p) for p in pieces],
        [
            ((WIN, D), F32),
            ((WIN, D), BF16),
            ((4, 4, CHUNK, D), BF16),
            ((4, 4, CHUNK, D), BF16),
            ((8, D), F32),
        ],
        [
            pltpu.VMEM((total, D), F32),
            pltpu.VMEM((total, D), F32),
            pltpu.VMEM((total, 128), F32),
            pltpu.VMEM((D, FF), F32),
        ],
        micros=4,
        name="down_backward",
        after=after,
    )


def up_kernel(place, dlow, slope, hlow, wd, dup, keep, send, sums, grad):
    for c in range(3):
        cols = slice(c * 512, (c + 1) * 512)
        part = (nn(dlow[...], wd[:, cols]) * slope[:, cols]).astype(BF16)
        dup[:, cols] = part
        column_sum = jnp.sum(part.astype(F32), axis=0, keepdims=True)
        for j in range(4):
            at = 512 * c + 128 * j
            sums[at // D : at // D + 1, at % D : at % D + 128] = column_sum[:, 128 * j : 128 * j + 128]
        grad[:, cols] = tn(hlow[...], dup[:, cols])
    for c in range(4):
        split_rows(grad.at[:, c * D : (c + 1) * D], keep, send, place, c)


def up_backward(place, dlow, slope, hlow, wd, after):
    return call(
        up_kernel,
        [(1, place)] + [(0, a) for a in (dlow, slope, hlow, wd)],
        [((WIN, FF), BF16), ((4, 4, CHUNK, D), BF16), ((4, 4, CHUNK, D), BF16), ((4, D), F32)],
        [pltpu.VMEM((D, FF), F32)],
        micros=3,
        name="up_backward",
        after=after,
    )


def first_kernel(
    place, dup, dsec, xhat1, inv1, att, vec, wu, wo,
    dfirst, datt, delta, okeep, osend, sums, grad, dlow,
):
    norm_backward(
        lambda r: nt(dup[r, :], wu[...]) + dsec[r, :],
        xhat1, inv1, vec[8:9, :], dfirst, dlow, sums, 0, WIDE_ROWS,
    )
    sums[3:8, :] = jnp.zeros((5, D), F32)
    grad[...] = tn(att[...], dlow[...])
    split_rows(grad, okeep, osend, place)
    da = nt(dlow[...], wo[...]).astype(BF16)
    datt[0:WIN, :] = da
    datt[WIN:PAD, :] = jnp.zeros((PAD - WIN, D), BF16)
    high, rest = low_pair(da.astype(F32) * att[...].astype(F32))
    heads = (iota((16, D), 1) // HD == iota((16, D), 0)).astype(F32).astype(BF16)
    delta[:, 0:WIN] = nt(heads, high) + nt(heads, rest)
    delta[:, WIN:PAD] = jnp.zeros((16, PAD - WIN), F32)


def first_backward(place, dup, dsec, xhat1, inv1, att, vec, wu, wo, after):
    return call(
        first_kernel,
        [(1, place)] + [(0, a) for a in (dup, dsec, xhat1, inv1, att, vec, wu, wo)],
        [
            ((WIN, D), F32),
            ((PAD, D), BF16),
            ((16, PAD), F32),
            ((4, CHUNK, D), BF16),
            ((4, CHUNK, D), BF16),
            ((8, D), F32),
        ],
        [
            pltpu.VMEM((D, D), F32),
            pltpu.VMEM((WIN, D), BF16),
        ],
        micros=3,
        name="first_backward",
        after=after,
    )


def heads_kernel(place, g, tokens, proj, datt, lse, delta, segc, segr, *rest):
    rest, (dproj, keep, send, sums, kt, dk, dv, grad, ktmp, stmp) = rest[:-10], rest[-10:]

    def lanes(part):
        return slice(part * D + 128 * g, part * D + 128 * g + 128)

    for t in range(PAD // 128):
        kt[:, 128 * t : 128 * t + 128] = (
            proj[128 * t : 128 * t + 128, lanes(1)].astype(F32).T.astype(BF16)
        )
    dk[...] = jnp.zeros_like(dk)
    dv[...] = jnp.zeros_like(dv)
    for q0, k0, k1 in BANDS:
        qs = head_stack(proj[q0 : q0 + BLOCK, lanes(0)])
        gs = head_stack(datt[q0 : q0 + BLOCK, lanes(0)])
        st = nt(proj[k0:k1, lanes(1)], qs)
        dp = nt(proj[k0:k1, lanes(2)], gs)
        same = segc[k0:k1, :] == segr[0:1, q0 : q0 + BLOCK]
        bias = jnp.where(same, 0.0, NEG_BIG)
        probs, d_scores, dq = [], [], []
        for j in range(4):
            cols = slice(j * BLOCK, (j + 1) * BLOCK)
            prob = jnp.exp2(st[:, cols] * EXP2_SCALE + bias - lse[g, j : j + 1, q0 : q0 + BLOCK])
            ds = prob * (dp[:, cols] - delta[4 * g + j : 4 * g + j + 1, q0 : q0 + BLOCK])
            ds = ds.astype(BF16)
            probs.append(prob.astype(BF16))
            d_scores.append(ds)
            if j % 2 == 1:
                part = nn(
                    kt[(j - 1) * HD : (j + 1) * HD, k0:k1], jnp.concatenate(d_scores[-2:], axis=1)
                )
                dq.append(part[0:HD, 0:BLOCK])
                dq.append(part[HD : 2 * HD, BLOCK : 2 * BLOCK])
        dv[k0:k1, :] += nn(jnp.concatenate(probs, axis=1), gs)
        dk[k0:k1, :] += nn(jnp.concatenate(d_scores, axis=1), qs)
        rows = min(BLOCK, WIN - q0)
        dqs = jnp.concatenate(dq, axis=0).T[0:rows] * HD ** (-0.5)
        dproj[q0 : q0 + rows, 0:128] = dqs.astype(BF16)
    dproj[:, 128:256] = (dk[...] * HD ** (-0.5)).astype(BF16)
    dproj[:, 256:384] = dv[...].astype(BF16)
    grad[...] = tn(tokens[aligned(OFF * place[0], WIN, 64), :], dproj[...])
    q_sum = jnp.sum(dproj[:, 0:128].astype(F32), axis=0, keepdims=True)
    v_sum = jnp.sum(dproj[:, 256:384].astype(F32), axis=0, keepdims=True)
    sums[0:1, :] = q_sum
    sums[1:2, :] = v_sum
    sums[2:8, :] = jnp.zeros((6, 128), F32)
    if g < 2:
        split_rows(grad, keep, send, place)
        return
    parts, (dsums, usums, fsums, zero, one) = rest[:6], rest[6:]
    split_rows(grad, ktmp, stmp, place)
    for dst, out_part, blocks in (
        (keep, parts[0], (parts[2], parts[4], ktmp)),
        (send, parts[1], (parts[3], parts[5], stmp)),
    ):
        dst[:, :, 3 * D : 4 * D] = out_part[...]
        for h, part in enumerate(blocks):
            for c in range(3):
                dst[:, :, D * c + 128 * h : D * c + 128 * h + 128] = part[
                    :, :, 128 * c : 128 * c + 128
                ]
    rows = jnp.concatenate(
        [
            jnp.concatenate([zero[0:1], one[0:1], q_sum], axis=1),
            jnp.concatenate([zero[1:2], one[1:2], v_sum], axis=1),
            fsums[0:1, :],
            usums[0:4, :],
            dsums[0:1, :],
            fsums[1:3, :],
            dsums[1:3, :],
            jnp.zeros((4, D), F32),
        ],
        axis=0,
    ).astype(BF16)
    for c in range(4):
        for j in range(3):
            block = rows[:, 128 * j : 128 * j + 128]
            keep[c, 16 * j : 16 * j + 16, 4 * D : 4 * D + 128] = block
            send[c, 16 * j : 16 * j + 16, 4 * D : 4 * D + 128] = block


def heads_backward(g, place, ins, more, after):
    part = ((4, CHUNK, 4 * D + 128 if g == 2 else D), BF16)
    return call(
        lambda place, *refs: heads_kernel(place, g, *refs),
        [(1, place)] + [(0, a) for a in tuple(ins) + tuple(more)],
        [((WIN, D), BF16), part, part, ((8, 128), F32)],
        [
            pltpu.VMEM((128, PAD), BF16),
            pltpu.VMEM((WIN, 128), F32),
            pltpu.VMEM((WIN, 128), F32),
            pltpu.VMEM((D, D), F32),
            pltpu.VMEM((4, CHUNK, D), BF16),
            pltpu.VMEM((4, CHUNK, D), BF16),
        ],
        micros=3,
        name="heads_backward",
        after=after,
    )


def input_kernel(dp0, dp1, dp2, dfirst, wfull, igrad, dproj):
    for g, part in enumerate((dp0, dp1, dp2)):
        for c in range(3):
            dproj[:, c * D + 128 * g : c * D + 128 * g + 128] = part[:, 128 * c : 128 * c + 128]
    igrad[...] = (nt(dproj[...], wfull[...]) + dfirst[...]).astype(BF16)


def input_backward(parts, dfirst, wqkv, after):
    return call(
        input_kernel,
        [(0, a) for a in tuple(parts) + (dfirst, wqkv)],
        [((WIN, D), BF16)],
        [pltpu.VMEM((WIN, 3 * D), BF16)],
        micros=2,
        name="input_backward",
        after=after,
    )[0]


def flips(axis, size, bits):
    return [(i, i ^ bits) for i in range(size)]


def pair(value):
    return swap(value, "opt", 2, 1)


def swap(value, axis, size, bits):
    return lax.ppermute(value, axis, flips(axis, size, bits))


def bit_groups(size):
    bits = size.bit_length() - 1
    return [(s, 1 << min(2, bits - s)) for s in range(0, bits, 2)]


def trades(values, n, shift):
    return [values[0]] + [swap(values[k], "dp", n, k << shift) for k in (1, 2, 3)]


def added(a, b):
    return (a.astype(F32) + b.astype(F32)).astype(BF16)


def core_sum_kernel(keep, other, *outs):
    for r, out in enumerate(outs):
        out[...] = added(keep[r], other[r])


def core_sum(keep, other, after):
    return call(
        core_sum_kernel,
        [(0, keep), (0, other)],
        [(keep.shape[1:], BF16)] * 4,
        name="core_sum",
        vmem=4,
        after=after,
    )


def pair_sum_kernel(bit, keep, other, stay, go):
    for i, r in enumerate((0, 3 - bit)):
        stay[i] = added(keep[r], other[r])
        go[i] = added(keep[r + bit], other[r + bit])


def pair_sum(bit, keep, other, after):
    return call(
        functools.partial(pair_sum_kernel, bit),
        [(0, keep), (0, other)],
        [((2,) + keep.shape[1:], BF16)] * 2,
        name="pair_sum",
        vmem=4,
        after=after,
    )


def wide_step_kernel(down, dother, up, uother, dkeep, dsend, ukeep, usend):
    dkeep[...] = added(down[0], dother[0])
    dsend[...] = added(down[1], dother[1])
    ukeep[...] = added(up[0], uother[0])
    usend[...] = added(up[1], uother[1])


def wide_step(parts, after):
    return call(
        wide_step_kernel,
        [(0, p) for p in parts],
        [((4, CHUNK, D), BF16)] * 4,
        name="wide_step",
        vmem=4,
        after=after,
    )


def total_of(refs, at):
    a, b, c, d = (ref[at].astype(F32) for ref in refs)
    return ((a + b) + (c + d)).astype(BF16)


def wide_plane_kernel(place, down, dother, up, uother, mine, send):
    z = place[3]
    for p, (keep, other) in enumerate(((down, dother), (up, uother))):
        for i, bits in enumerate((0, 2)):
            mine[2 * i + p] = added(keep[z ^ bits], other[z ^ bits])
            send[2 * i + p] = added(keep[z ^ bits ^ 1], other[z ^ bits ^ 1])


def wide_plane_sum(place, parts, after):
    return call(
        wide_plane_kernel,
        [(1, place)] + [(0, p) for p in parts],
        [((4, CHUNK, D), BF16)] * 2,
        name="wide_plane_sum",
        vmem=4,
        after=after,
    )


def wide_half_kernel(keep, other, mine, send):
    mine[...] = added(keep[0:2], other[0:2])
    send[...] = added(keep[2:4], other[2:4])


def wide_half(keep, other, after):
    return call(
        wide_half_kernel,
        [(0, keep), (0, other)],
        [((2, CHUNK, D), BF16)] * 2,
        name="wide_half",
        vmem=4,
        after=after,
    )


def low_plane_kernel(a, b, c, d, out):
    out[...] = total_of((a, b, c, d), slice(None))


def low_plane_sum(parts, after=()):
    return call(
        low_plane_kernel,
        [(0, p) for p in parts],
        [(parts[0].shape, BF16)],
        name="low_plane_sum",
        vmem=4,
        after=after,
    )[0]


def low_next_kernel(keep, other, out):
    out[...] = added(keep[...], other[...])


def low_next(keep, other, after=()):
    return call(
        low_next_kernel,
        [(0, keep), (0, other)],
        [(keep.shape, BF16)],
        name="low_next",
        vmem=4,
        after=after,
    )[0]


def low_last_kernel(keep, other, out, vgrad):
    out[...] = added(keep[:, 0 : 4 * D], other[:, 0 : 4 * D])
    vgrad[...] = added(keep[:, 4 * D : 4 * D + 128], other[:, 4 * D : 4 * D + 128])


def low_last(keep, other, after):
    return call(
        low_last_kernel,
        [(0, keep), (0, other)],
        [((CHUNK, 4 * D), BF16), ((CHUNK, 128), BF16)],
        name="low_last",
        vmem=4,
        after=after,
    )


def chain_kernel(*refs):
    ins, out = refs[:-1], refs[-1]
    at = 0
    for ref in ins:
        flat = ref.reshape(-1, CHUNK, D)
        out[at : at + flat.shape[0]] = flat[...]
        at += flat.shape[0]


def chain(parts, after=()):
    count = sum(p.size for p in parts) // (CHUNK * D)
    return call(
        chain_kernel,
        [(0, p) for p in parts],
        [((count, CHUNK, D), BF16)],
        name="chain",
        vmem=4,
        after=after,
    )[0]


def rest_sum(value, n):
    bit = 16
    while bit < n:
        other = swap(value, "dp", n, bit)
        value = (value.astype(F32) + other.astype(F32)).astype(BF16)
        bit *= 2
    return value


def join_kernel(*refs):
    ins, out = refs[:-1], refs[-1]
    for i, ref in enumerate(ins):
        out[i] = ref[...]


def join(parts, after=()):
    return call(
        join_kernel,
        [(0, p) for p in parts],
        [((len(parts),) + parts[0].shape, parts[0].dtype)],
        name="join",
        vmem=4,
        after=after,
    )[0]


def pack_kernel(marks, unit, other, units, packed):
    both = unit[...] + other[...]
    units[...] = both
    packed[:, 0:D] = both.astype(BF16)
    packed[:, D : D + 128] = marks[...]


def pack(marks, unit, other):
    return call(
        pack_kernel,
        [(0, marks), (0, unit), (0, other)],
        [(unit.shape, F32), ((2 * PAIRS, D + 128), BF16)],
        name="pack",
        vmem=4,
    )


def squares_of(parts):
    acc = jnp.zeros((8, D), F32)
    for part in parts:
        flat = part.reshape(-1, CHUNK, part.shape[-1])
        for k in range(flat.shape[0]):
            for c in range(0, part.shape[-1], D):
                v = flat[k, :, c : c + D].astype(F32)
                acc = acc + jnp.sum((v * v).reshape(CHUNK // 8, 8, D), axis=0)
    return acc[:, 0:128] + acc[:, 128:256] + acc[:, 256:384]


def wide_squares_kernel(*refs):
    refs[-1][...] = squares_of(refs[:-1])


def squares_kernel(place, *refs):
    parts, (vgrad, before, out) = refs[:-3], refs[-3:]
    acc = squares_of(parts) + before[...]
    row = iota((16, 128), 0)
    low_row = 6 * place[0]
    mine = (row >= low_row) & (row < low_row + 6)
    for j in range(3):
        v = jnp.where(mine, vgrad[16 * j : 16 * j + 16, :].astype(F32), 0.0)
        v = v * v
        acc = acc + (v[0:8] + v[8:16])
    out[...] = acc


def squares(place, parts, vgrad=None, before=None, after=()):
    ins = [(0, p) for p in parts]
    kernel = wide_squares_kernel
    if before is not None:
        ins = [(1, place)] + ins + [(0, vgrad), (0, before)]
        kernel = squares_kernel
    return call(kernel, ins, [((8, 128), F32)], name="squares", vmem=4, after=after)[0]


def merge_kernel(place, igrad, other, out, flag):
    flag[...] = jnp.zeros((8, 128), F32)

    @pl.when(place[0] == 0)
    def low_core():
        out[0:OFF, :] = igrad[0:OFF, :]
        out[OFF:WIN, :] = added(igrad[OFF:WIN, :], other[0 : WIN - OFF, :])
        out[WIN:SEQ, :] = other[WIN - OFF : WIN, :]

    @pl.when(place[0] != 0)
    def high_core():
        out[0:OFF, :] = other[0:OFF, :]
        out[OFF:WIN, :] = added(other[OFF:WIN, :], igrad[0 : WIN - OFF, :])
        out[WIN:SEQ, :] = igrad[WIN - OFF : WIN, :]


def merge(place, igrad, other, after):
    return call(
        merge_kernel,
        [(1, place), (0, igrad), (0, other)],
        [((SEQ, D), BF16), ((8, 128), F32)],
        name="merge",
        vmem=4,
        after=after,
    )


def adamw(parameter, first_state, second, clipped, rate):
    first_new = first_state + (1.0 - BETA_ONE) * clipped
    second_new = second + (1.0 - BETA_TWO) * clipped * clipped
    root = (1.0 - BETA_TWO**STEP) ** 0.5
    below = pl.reciprocal(second_new * lax.rsqrt(second_new) + ADAM_EPS * root)
    scale = rate * root / (1.0 - BETA_ONE**STEP)
    return parameter - scale * (first_new * below), first_new, second_new


def decay_kernel(w, m, v, pv, pm, pq, nw, nm, nv, npv, npm, npq):
    for ins, outs, rate in (
        ((w, m, v), (nw, nm, nv), LEARN_RATE),
        ((pv, pm, pq), (npv, npm, npq), VECTOR_RATE),
    ):
        for ref, out, scale in zip(ins, outs, (1.0 - rate * DECAY_RATE, BETA_ONE, BETA_TWO)):
            out[...] = ref[...] * scale


def decay(arrays, after):
    return call(
        decay_kernel,
        [(0, a) for a in arrays],
        [(a.shape, F32) for a in arrays],
        name="decay",
        vmem=4,
        after=after,
    )


def adamw_kernel(*refs):
    place = Place()
    sums, refs = refs[:2], refs[2:]
    (vgrad, w, m, v, pv, pm, pq), refs = refs[:7], refs[7:]
    wide, low, refs = refs[:4], refs[4:8], refs[8:]
    outs, (npv, npm, npq, norm), scrs, sems = refs[:4], refs[4:8], refs[8:12], refs[12]
    opt = place[0]
    total = sums[0][...] + sums[1][...]
    total = jnp.sum(jnp.sum(total, axis=1, keepdims=True), axis=0, keepdims=True)
    grad_norm = jnp.sqrt(total)
    factor = jnp.minimum(1.0, CLIP_NORM / (grad_norm + 1e-06))
    norm[...] = grad_norm
    for j in range(3):
        cols = slice(128 * j, 128 * j + 128)
        g = vgrad[16 * j : 16 * j + 16, :].astype(F32)
        g = jnp.where(opt == 0, g[0:6], g[6:12])
        a, b, c = adamw(pv[:, cols], pm[:, cols], pq[:, cols], g * factor, VECTOR_RATE)
        npv[:, cols] = a
        npm[:, cols] = b
        npq[:, cols] = c

    def block(grad, rows, cols):
        new = adamw(w[rows, cols], m[rows, cols], v[rows, cols], grad * factor, LEARN_RATE)
        for scr, value in zip(scrs, new + (new[0].astype(BF16),)):
            scr[rows, cols] = value

    def copies(r, i):
        rows = aligned(CHUNK * (place[1] ^ r) + i * 16, 16, 16)
        return [
            pltpu.make_async_copy(scr.at[rows, :], out.at[rows, :], sems.at[3 * r + i, j])
            for j, (scr, out) in enumerate(zip(scrs, outs))
        ]

    for r in range(4):

        def step(i, carry, r=r):
            rows = aligned(CHUNK * (place[1] ^ r) + i * 16, 16, 16)
            here = aligned(i * 16, 16, 16)
            for j in range(4):
                at = D * (place[3] ^ j)
                for p, start in enumerate((4 * D + FF, 4 * D)):
                    grad = wide[r][2 * j + p, here, :].astype(F32)
                    block(grad, rows, aligned(start + at, D, 128))
            for c in range(4):
                grad = low[r][here, D * c : D * c + D].astype(F32)
                block(grad, rows, slice(D * c, D * c + D))
            for copy in copies(r, i):
                copy.start()
            return carry

        lax.fori_loop(0, CHUNK // 16, step, 0)
    for r in range(4):

        def finish(i, carry, r=r):
            for copy in copies(r, i):
                copy.wait()
            return carry

        lax.fori_loop(0, CHUNK // 16, finish, 0)


def update(place, sums, vgrad, w, m, v, pv, pm, pq, parts):
    ins = tuple(sums) + (vgrad, w, m, v, pv, pm, pq) + tuple(parts)
    shapes = [(w.shape, F32)] * 3 + [(w.shape, BF16)] + [(pv.shape, F32)] * 3 + [((1, 1), F32)]
    return pl.pallas_call(
        adamw_kernel,
        out_shape=[jax.ShapeDtypeStruct(s, d) for s, d in shapes],
        in_specs=[VMEM] * len(ins),
        out_specs=[ANY] * 4 + [VMEM] * 4,
        scratch_shapes=[
            pltpu.VMEM(w.shape, F32),
            pltpu.VMEM(w.shape, F32),
            pltpu.VMEM(w.shape, F32),
            pltpu.VMEM(w.shape, BF16),
            pltpu.SemaphoreType.DMA((12, 4)),
        ],
        compiler_params=pltpu.CompilerParams(vmem_limit_bytes=16 << 20),
        cost_estimate=pl.CostEstimate(
            flops=4000000000, bytes_accessed=26 * w.size, transcendentals=0
        ),
        name="adamw",
    )(*ins)


def shards(
    n,
    tokens,
    lengths,
    query_index,
    doc_index,
    targets,
    weights,
    first_moment,
    second_moment,
    vectors,
    vec_first,
    vec_second,
):
    place = None
    scalars = jnp.concatenate([lengths.reshape(SEGS), query_index, doc_index, targets])
    groups = bit_groups(n)

    w_own, wo_own, wu_own, wd_own = cast(weights)
    w_other = pair(w_own)
    vectors_late, w_own = lax.optimization_barrier((vectors, w_own))
    v_other = pair(vectors_late)
    wo = (wo_own, pair(wo_own))
    wu = (wu_own, pair(wu_own))
    wd = (wd_own, pair(wd_own))

    proj, att, lse, segc, segr, ownc, ownr, wanted, marks, vec, wqkv = attend(
        place, scalars, (tokens, w_own, w_other, vectors, v_other)
    )
    xhat1, inv1, hlow, act, up_proj, xhat2, inv2, unit, uscale, wo, wu, wd = mlp(
        place, wanted, att, tokens, ownr, vec, wo + wu + wd
    )
    units, packed = pack(marks, unit, pair(unit))
    groups = bit_groups(n)
    order = [0]
    stack = packed
    for i, (shift, size) in enumerate(groups[1:] + groups[:1]):
        pieces = [stack] + [swap(stack, "dp", n, k << shift) for k in range(1, size)]
        order = [o | (k << shift) for k in range(size) for o in order]
        if i < len(groups) - 1:
            slope = slope_of(up_proj, [packed])
            stack = join(pieces, [slope]).reshape(-1, 2 * PAIRS, D + 128)
    decayed = decay(
        (weights, first_moment, second_moment, vectors, vec_first, vec_second), [packed]
    )
    dsec, dlow, keep, send, dsums = down_backward(
        n, order, place, wanted, units, ownc, uscale, (xhat2, inv2, act), vec, pieces,
        decayed,
    )
    other = pair(send)
    dup, ukeep, usend, usums = up_backward(place, dlow, slope, hlow, wd, [])
    down, go = pair_sum(1, keep, other, [dup])
    dother = swap(go, "dp", n, 1)
    up, go = pair_sum(2, ukeep, pair(usend), [down])
    uother = swap(go, "dp", n, 2)
    dfirst, datt, delta, okeep, osend, fsums = first_backward(
        place, dup, dsec, xhat1, inv1, att, vec, wu, wo, [up]
    )
    ins = (tokens, proj, datt, lse, delta, segc, segr)
    part0, keep0, send0, sums0 = heads_backward(0, place, ins, (), [])
    down, dsend, up, usend = wide_step((down, dother, up, uother), [part0])
    dother, uother = swap(dsend, "dp", n, 2), swap(usend, "dp", n, 1)
    part1, keep1, send1, sums1 = heads_backward(1, place, ins, (), [down])
    wide, go = wide_plane_sum(place, (down, dother, up, uother), [part1])
    wother = swap(go, "dp", n, 4)
    part2, keep, send, _ = heads_backward(
        2, place, ins,
        (okeep, osend, keep0, send0, keep1, send1, dsums, usums, fsums, sums0, sums1),
        [wide, part1],
    )
    wide, go = wide_half(wide, wother, [part2])
    send, wide, go = lax.optimization_barrier((send, wide, go))
    wother = swap(go, "dp", n, 8)
    other = pair(send)
    igrad = input_backward((part0, part1, part2), dfirst, wqkv, [wide])
    iother = pair(igrad)
    low = core_sum(keep, other, [igrad])
    low_got = trades(low, n, 0)
    wide = rest_sum(low_next(wide, wother, [low[0]]), n)
    wide_got = trades([wide] * 4, n, 2)
    low = low_plane_sum(low_got, [wide])
    other = swap(low, "dp", n, 4)
    wide = chain(wide_got, [low])
    wide = trades([wide] * 4, n, 0)
    low = low_next(low, other, [wide[0]])
    other = swap(low, "dp", n, 8)
    input_grad, flag = merge(place, igrad, iother, [low])
    low, vgrad = low_last(low, other, [flag])
    low, vgrad = rest_sum(low, n), rest_sum(vgrad, n)
    low = trades([low] * 4, n, 0)
    sums = squares(place, low, vgrad, squares(place, wide, after=[low[0]]))
    sums = (sums, pair(sums))
    pieces = tuple(wide) + tuple(low)
    nw, nm, nv, nlow, npv, npm, npq, norm = update(
        place, sums, vgrad, *decayed, pieces,
    )
    return (norm.reshape(()), input_grad, nw, nm, nv, nlow, npv, npm, npq)


def solution(mesh):
    rows = P("opt", None)
    in_specs = (P("dp", None), P("dp", None), P("dp"), P("dp"), P("dp")) + (rows,) * 6
    out_specs = (P(), P("dp", None)) + (rows,) * 7
    n = mesh.shape["dp"]
    return jax.shard_map(
        functools.partial(shards, n),
        mesh=mesh,
        in_specs=in_specs,
        out_specs=out_specs,
        check_vma=False,
    )
```

```python
import functools

import jax
import jax.numpy as jnp
from jax import lax
from jax.experimental import pallas as pl
from jax.experimental.pallas import tpu as pltpu
from jax.sharding import PartitionSpec as P

D = 384
HEADS = 12
HD = 32
FF = 1536
SEQ = 1024
SEGS = 16
PAIRS = 8
STEP = 10

WIN = 576
OFF = SEQ - WIN
PAD = 640
BLOCK = 128
BANDS = tuple((q, max(0, q - 128), min(WIN, q + 256)) for q in range(0, WIN, BLOCK))
BAND_ROWS = tuple(sum(b[2] - b[1] for b in BANDS[:i]) for i in range(len(BANDS) + 1))
ROWS = 64
WIDE_ROWS = 192
LOG2E = 1.4426950408889634

LN_EPS = 1e-06
POOL_EPS = 1e-06
SCORE_SCALE = 50.0
CLIP_NORM = 0.001
BETA_ONE = 0.9
BETA_TWO = 0.98
ADAM_EPS = 1e-08
LEARN_RATE = 0.05
VECTOR_RATE = 0.3
DECAY_RATE = 0.01
NEG_BIG = -1e30
HALF = D // 2
CHUNK = HALF // 4
EXP2_SCALE = HD ** (-0.5) * 1.4426950408889634

F32 = jnp.float32
BF16 = jnp.bfloat16
VMEM = pl.BlockSpec(memory_space=pltpu.VMEM)
SMEM = pl.BlockSpec(memory_space=pltpu.SMEM)
ANY = pl.BlockSpec(memory_space=pl.ANY)


def nn(a, b):
    return jnp.dot(a, b, preferred_element_type=F32)


def nt(a, b):
    return lax.dot_general(a, b, (((1,), (1,)), ((), ())), preferred_element_type=F32)


def tn(a, b):
    return lax.dot_general(a, b, (((0,), (0,)), ((), ())), preferred_element_type=F32)


def exact(a, b, dims):
    return lax.dot_general(
        a, b, (dims, ((), ())), precision=lax.Precision.HIGHEST, preferred_element_type=F32
    )


def iota(shape, axis):
    return lax.broadcasted_iota(jnp.int32, shape, axis)


def low_pair(value):
    high = value.astype(BF16)
    return high, (value - high.astype(F32)).astype(BF16)


def aligned(start, size, unit):
    return pl.ds(pl.multiple_of(start, unit), size)


def assemble(dst, own, other, opt):
    dst[aligned(HALF * opt, HALF, 64), :] = own[0:HALF, :]
    dst[aligned(HALF * (1 - opt), HALF, 64), :] = other[0:HALF, :]


class Place:
    def __getitem__(self, i):
        if i == 0:
            return lax.axis_index("opt")
        me = lax.axis_index("dp")
        return (me & 3, me, (me >> 2) & 3)[i - 1]


def call(kernel, ins, outs, scratch=(), micros=5, name=None, vmem=12, after=()):
    if ins[0][1] is None:
        kernel = functools.partial(kernel, Place())
        ins = ins[1:]
    specs = [SMEM if s else VMEM for s, _ in ins] + [ANY] * len(after)
    count = len(ins)

    def body(*refs):
        kernel(*refs[:count], *refs[count + len(after) :])

    shapes = [jax.ShapeDtypeStruct(s, d) for s, d in outs]
    moved = sum(a.size * a.dtype.itemsize for _, a in ins)
    moved += sum(s.size * s.dtype.itemsize for s in shapes)
    return pl.pallas_call(
        body,
        out_shape=shapes,
        in_specs=specs,
        out_specs=[VMEM] * len(shapes),
        scratch_shapes=list(scratch),
        compiler_params=pltpu.CompilerParams(vmem_limit_bytes=vmem << 20),
        cost_estimate=pl.CostEstimate(
            flops=micros * 1100000000, bytes_accessed=moved, transcendentals=0
        ),
        name=name,
    )(*[a for _, a in ins], *after)


def head_stack(rows):
    lane_head = iota(rows.shape, 1) // HD
    zero = jnp.zeros_like(rows)
    return jnp.concatenate([jnp.where(lane_head == j, rows, zero) for j in range(4)], axis=0)


def attend_kernel(
    place, scalars, tokens, w_own, w_other, v_own, v_other,
    proj, att, lse, segc, segr, ownc, ownr, wanted, marks, vec, wfull, bias, vt,
):
    opt = place[0]
    assemble(wfull, w_own, w_other, opt)
    mine = v_own[...].astype(BF16).astype(F32)
    others = v_other[...].astype(BF16).astype(F32)
    first = opt == 0
    vec[0:6, :] = jnp.where(first, mine, others)
    vec[6:12, :] = jnp.where(first, others, mine)
    vec[12:16, :] = jnp.zeros((4, D), F32)

    position = iota((8, PAD), 1) + OFF * opt
    segment = jnp.zeros((8, PAD), jnp.int32)
    bound = jnp.int32(0)
    low_count = jnp.int32(0)
    for s in range(SEGS):
        bound = bound + scalars[s]
        segment = segment + (position >= bound).astype(jnp.int32)
        low_count = low_count + (bound <= WIN).astype(jnp.int32)
    mine = (segment < low_count).astype(jnp.int32) == (opt == 0).astype(jnp.int32)
    owned = jnp.where(mine, segment, -1)
    segr[...] = segment
    ownr[...] = owned
    for value, out in ((segment, segc), (owned, ownc)):
        value = value.astype(F32)
        for t in range(PAD // 128):
            rows = min(128, WIN - 128 * t)
            turned = jnp.broadcast_to(value[0:1, 128 * t : 128 * t + 128], (128, 128)).T
            out[128 * t : 128 * t + rows, :] = turned[0:rows].astype(jnp.int32)
    row, col = iota((2 * PAIRS, 128), 0), iota((2 * PAIRS, 128), 1)
    by_row = jnp.zeros((2 * PAIRS, 128), jnp.int32)
    by_col = jnp.zeros((2 * PAIRS, 128), jnp.int32)
    mark = jnp.zeros((2 * PAIRS, 128), jnp.int32)
    for j in range(PAIRS):
        mark = jnp.where(row == j, scalars[SEGS + 2 * PAIRS + j], mark)
        for at in (j, PAIRS + j):
            by_row = jnp.where(row == at, scalars[SEGS + at], by_row)
            by_col = jnp.where(col == at, scalars[SEGS + at], by_col)
    wanted[0] = by_row
    wanted[1] = by_col
    marks[...] = jnp.where(col < 64, mark >> 5, mark & 31).astype(F32).astype(BF16)
    for i, (q0, k0, k1) in enumerate(BANDS):
        bias[BAND_ROWS[i] : BAND_ROWS[i + 1], :] = jnp.where(
            segc[k0:k1, :] == segr[0:1, q0 : q0 + BLOCK], 0.0, NEG_BIG
        )

    x = tokens[aligned(OFF * opt, WIN, 64), :]
    bias_row = jnp.concatenate([vec[0:1, :], jnp.zeros((1, D), F32), vec[1:2, :]], axis=1)
    for first in range(0, 3 * D, 512):
        cols = slice(first, min(first + 512, 3 * D))
        proj[0:WIN, cols] = (nn(x, wfull[:, cols]) + bias_row[:, cols]).astype(BF16)
    proj[WIN:PAD, :] = jnp.zeros((PAD - WIN, 3 * D), BF16)

    def group(g, carry):
        def lanes(part):
            return aligned(part * D + 128 * g, 128, 128)

        for t in range(PAD // 128):
            vt[:, 128 * t : 128 * t + 128] = (
                proj[128 * t : 128 * t + 128, lanes(2)].astype(F32).T.astype(BF16)
            )
        def scores(i):
            q0, k0, k1 = BANDS[i]
            return nt(proj[k0:k1, lanes(1)], head_stack(proj[q0 : q0 + BLOCK, lanes(0)]))

        coming = scores(0)
        for i, (q0, k0, k1) in enumerate(BANDS):
            st = coming
            if i + 1 < len(BANDS):
                coming = scores(i + 1)
            outs, probs, totals = [], [], []
            for j in range(4):
                t = (
                    st[:, j * BLOCK : (j + 1) * BLOCK] * EXP2_SCALE
                    + bias[BAND_ROWS[i] : BAND_ROWS[i + 1], :]
                )
                peak = jnp.max(t, axis=0, keepdims=True)
                powers = jnp.exp2(t - peak)
                total = jnp.sum(powers, axis=0, keepdims=True)
                lse[g, j : j + 1, q0 : q0 + BLOCK] = peak + jnp.log2(total)
                probs.append(powers.astype(BF16))
                totals.append(1.0 / total)
                if j % 2 == 1:
                    o = nn(vt[(j - 1) * HD : (j + 1) * HD, k0:k1], jnp.concatenate(probs[-2:], axis=1))
                    outs.append(o[0:HD, 0:BLOCK] * totals[-2])
                    outs.append(o[HD : 2 * HD, BLOCK : 2 * BLOCK] * totals[-1])
            rows = min(BLOCK, WIN - q0)
            att[q0 : q0 + rows, aligned(128 * g, 128, 128)] = (
                jnp.concatenate(outs, axis=0).T[0:rows].astype(BF16)
            )
        return carry

    lax.fori_loop(0, 3, group, 0)


def attend(place, scalars, arrays):
    return call(
        attend_kernel,
        [(1, place), (1, scalars)] + [(0, a) for a in arrays],
        [
            ((PAD, 3 * D), BF16),
            ((WIN, D), BF16),
            ((3, 4, PAD), F32),
            ((WIN, 128), jnp.int32),
            ((8, PAD), jnp.int32),
            ((WIN, 128), jnp.int32),
            ((8, PAD), jnp.int32),
            ((2, 2 * PAIRS, 128), jnp.int32),
            ((2 * PAIRS, 128), BF16),
            ((16, D), F32),
            ((D, 3 * D), BF16),
        ],
        [
            pltpu.VMEM((BAND_ROWS[-1], 128), F32),
            pltpu.VMEM((128, PAD), BF16),
        ],
        micros=8,
        name="attend",
    )


def cast_kernel(weights, wq, wo, wu, wd, buffer, sems):
    spans = [(wq, 3 * D), (wo, D), (wu, FF), (wd, FF)]
    copies = [
        pltpu.make_async_copy(
            weights.at[:, i * D : (i + 1) * D], buffer.at[:, i * D : (i + 1) * D], sems.at[i]
        )
        for i in range(12)
    ]
    for copy in copies:
        copy.start()
    at = 0
    for out, width in spans:
        for part in range(width // D):
            copies[at].wait()
            out[:, part * D : (part + 1) * D] = buffer[:, at * D : (at + 1) * D].astype(BF16)
            at += 1


def cast(weights):
    return pl.pallas_call(
        cast_kernel,
        out_shape=[jax.ShapeDtypeStruct((HALF, c), BF16) for c in (3 * D, D, FF, FF)],
        in_specs=[ANY],
        out_specs=[VMEM] * 4,
        scratch_shapes=[pltpu.VMEM(weights.shape, F32), pltpu.SemaphoreType.DMA((12,))],
        compiler_params=pltpu.CompilerParams(vmem_limit_bytes=52 << 20),
        name="cast",
    )(weights)


def bias_of(vec, c):
    first, last = 256 * c, 256 * c + 256
    parts = []
    while first < last:
        row, col = divmod(first, D)
        size = min(D - col, last - first)
        parts.append(vec[3 + row : 4 + row, col : col + size])
        first += size
    return parts[0] if len(parts) == 1 else jnp.concatenate(parts, axis=1)


def mlp_kernel(
    place, wanted, att, tokens, ownr, vec, wo_own, wo_other, wu_own, wu_other,
    wd_own, wd_other, xhat1, inv1, hlow, act, up_proj, xhat2, inv2, unit, uscale, wo, wu, wd,
    ench, encl,
):
    opt = place[0]
    assemble(wo, wo_own, wo_other, opt)
    assemble(wu, wu_own, wu_other, opt)
    assemble(wd, wd_own, wd_other, opt)

    def norm(v):
        centred = v - jnp.mean(v, axis=1, keepdims=True)
        inverse = lax.rsqrt(jnp.mean(centred * centred, axis=1, keepdims=True) + LN_EPS)
        return centred * inverse, inverse

    def block(i, carry):
        r = aligned(i * WIDE_ROWS, WIDE_ROWS, 64)
        x = tokens[aligned(OFF * opt + i * WIDE_ROWS, WIDE_ROWS, 64), :].astype(F32)
        normed, inverse = norm(nn(att[r, :], wo[...]) + vec[2:3, :] + x)
        xhat1[r, :] = normed
        inv1[r, :] = jnp.broadcast_to(inverse, (WIDE_ROWS, 128))
        h = normed * vec[8:9, :] + vec[9:10, :]
        low = h.astype(BF16)
        hlow[r, :] = low
        for c in range(6):
            cols = slice(c * 256, (c + 1) * 256)
            u = nn(low, wu[:, cols]) + bias_of(vec, c)
            up_proj[r, cols] = u
            half = lax.erf(u * 0.7071067811865476) * 0.5 + 0.5
            act[r, cols] = (u * half).astype(BF16)
        normed, inverse = norm(nt(act[r, :], wd[...]) + vec[7:8, :] + h)
        xhat2[r, :] = normed
        inv2[r, :] = jnp.broadcast_to(inverse, (WIDE_ROWS, 128))
        high, rest = low_pair(normed * vec[10:11, :] + vec[11:12, :])
        ench[r, :] = high
        encl[r, :] = rest
        return carry

    lax.fori_loop(0, WIN // WIDE_ROWS, block, 0)

    onehot = jnp.where(wanted[0, :, 0:1] == ownr[0:1, 0:WIN], 1.0, 0.0)
    count = jnp.maximum(jnp.sum(onehot, axis=1, keepdims=True), 1.0)
    hot = onehot.astype(BF16)
    pooled = (nn(hot, ench[...]) + nn(hot, encl[...])) / count
    inverse_len = lax.rsqrt(jnp.sum(pooled * pooled, axis=1, keepdims=True) + POOL_EPS)
    unit[...] = pooled * inverse_len
    uscale[...] = jnp.broadcast_to(inverse_len / count, (2 * PAIRS, 128))


def slope_kernel(up_proj, out):
    def block(i, carry):
        r = aligned(i * 16, 16, 16)
        u = up_proj[r, :]
        half = lax.erf(u * 0.7071067811865476) * 0.5 + 0.5
        out[r, :] = half + u * jnp.exp2(u * u * (-0.5 * LOG2E)) * 0.3989422804014327
        return carry

    lax.fori_loop(0, WIN // 16, block, 0)


def slope_of(up_proj, after):
    return call(slope_kernel, [(0, up_proj)], [(up_proj.shape, F32)], name="slope", vmem=4, after=after)[0]


def mlp(place, wanted, att, tokens, ownr, vec, halves):
    return call(
        mlp_kernel,
        [(1, place), (0, wanted), (0, att), (0, tokens), (0, ownr), (0, vec)]
        + [(0, h) for h in halves],
        [
            ((WIN, D), F32),
            ((WIN, 128), F32),
            ((WIN, D), BF16),
            ((WIN, FF), BF16),
            ((WIN, FF), F32),
            ((WIN, D), F32),
            ((WIN, 128), F32),
            ((2 * PAIRS, D), F32),
            ((2 * PAIRS, 128), F32),
            ((D, D), BF16),
            ((D, FF), BF16),
            ((D, FF), BF16),
        ],
        [
            pltpu.VMEM((WIN, D), BF16),
            pltpu.VMEM((WIN, D), BF16),
        ],
        micros=10,
        name="mlp",
    )


def split_rows(grad, keep, send, place, *at):
    opt = place[0]
    for c in range(4):
        index = (c ^ place[1],) + at
        keep[index] = grad[aligned(HALF * opt + CHUNK * c, CHUNK, 16), :].astype(BF16)
        send[index] = grad[aligned(HALF * (1 - opt) + CHUNK * c, CHUNK, 16), :].astype(BF16)


def column_sums(value):
    return jnp.sum(value.reshape(-1, 8, D), axis=0)


def norm_backward(grad_at, normed_ref, inverse_ref, gain, out, low_out, sums, at, step=ROWS):
    def block(i, carry):
        scale_sum, shift_sum, bias_sum = carry
        r = aligned(i * step, step, 64)
        g = grad_at(r)
        normed = normed_ref[r, :]
        scaled = g * gain
        inner = (
            scaled
            - jnp.mean(scaled, axis=1, keepdims=True)
            - normed * jnp.mean(scaled * normed, axis=1, keepdims=True)
        ) * inverse_ref[r, 0:1]
        out[r, :] = inner
        low_out[r, :] = inner.astype(BF16)
        return (
            scale_sum + column_sums(g * normed),
            shift_sum + column_sums(g),
            bias_sum + column_sums(inner),
        )

    zero = jnp.zeros((8, D), F32)
    scale_sum, shift_sum, bias_sum = lax.fori_loop(0, WIN // step, block, (zero, zero, zero))
    sums[at : at + 1, :] = jnp.sum(bias_sum, axis=0, keepdims=True)
    sums[at + 1 : at + 2, :] = jnp.sum(scale_sum, axis=0, keepdims=True)
    sums[at + 2 : at + 3, :] = jnp.sum(shift_sum, axis=0, keepdims=True)


def down_kernel(
    place, count, order, wanted, units, ownc, uscale, xhat2, inv2, act, vec, *rest
):
    pieces, (dsec, dlow, keep, send, sums, queries, docs, marks, grad) = rest[:-9], rest[-9:]
    me = place[2]
    per = pieces[0].shape[0]
    for p, piece in enumerate(pieces):
        for j in range(per):
            at = order[p * per + j]
            r = slice(at * PAIRS, (at + 1) * PAIRS)
            both = piece[j].astype(F32)
            queries[r, :] = both[0:PAIRS, 0:D]
            docs[r, :] = both[PAIRS : 2 * PAIRS, 0:D]
            marks[r, :] = both[0:PAIRS, D : D + 128]
    total = count * PAIRS
    q = queries[...].astype(BF16)
    d = docs[...].astype(BF16)
    logits = SCORE_SCALE * nt(q, d)
    peak = jnp.max(logits, axis=1, keepdims=True)
    powers = jnp.exp(logits - peak)
    soft = powers / jnp.sum(powers, axis=1, keepdims=True)
    col = iota((total, total), 1)
    doc_id = ((col // PAIRS) ^ me) * PAIRS + lax.rem(col, PAIRS)
    hit = (marks[:, 0:1] * 32.0 + marks[:, 64:65]).astype(jnp.int32) == doc_id
    d_logits = (soft - jnp.where(hit, 1.0, 0.0)) * (SCORE_SCALE / total)
    high, rest_low = low_pair(d_logits[0:PAIRS, :])
    d_q = nn(high, d) + nn(rest_low, d)
    high, rest_low = low_pair(d_logits[:, 0:128].T[0:PAIRS, :])
    d_d = nn(high, q) + nn(rest_low, q)
    d_units = jnp.concatenate([d_q, d_d], axis=0)
    u = units[...]
    d_pool = uscale[:, 0:1] * (d_units - u * jnp.sum(u * d_units, axis=1, keepdims=True))
    hot = jnp.where(ownc[:, 0 : 2 * PAIRS] == wanted[1, 0:1, 0 : 2 * PAIRS], 1.0, 0.0).astype(BF16)
    high, rest_low = low_pair(d_pool)
    dsec[...] = nn(hot, high) + nn(hot, rest_low)
    norm_backward(lambda r: dsec[r, :], xhat2, inv2, vec[10:11, :], dsec, dlow, sums, 0)
    sums[3:8, :] = jnp.zeros((5, D), F32)
    for c in range(3):
        cols = slice(c * 512, (c + 1) * 512)
        grad[:, cols] = tn(dlow[...], act[:, cols])
    for c in range(4):
        split_rows(grad.at[:, c * D : (c + 1) * D], keep, send, place, c)


def down_backward(count, order, place, wanted, units, ownc, uscale, saved, vec, pieces, after):
    total = count * PAIRS
    return call(
        lambda place, *refs: down_kernel(place, count, order, *refs),
        [(1, place), (0, wanted), (0, units), (0, ownc), (0, uscale)]
        + [(0, s) for s in saved]
        + [(0, vec)]
        + [(0, p) for p in pieces],
        [
            ((WIN, D), F32),
            ((WIN, D), BF16),
            ((4, 4, CHUNK, D), BF16),
            ((4, 4, CHUNK, D), BF16),
            ((8, D), F32),
        ],
        [
            pltpu.VMEM((total, D), F32),
            pltpu.VMEM((total, D), F32),
            pltpu.VMEM((total, 128), F32),
            pltpu.VMEM((D, FF), F32),
        ],
        micros=4,
        name="down_backward",
        after=after,
    )


def up_kernel(place, dlow, slope, hlow, wd, dup, keep, send, sums, grad):
    for c in range(3):
        cols = slice(c * 512, (c + 1) * 512)
        part = (nn(dlow[...], wd[:, cols]) * slope[:, cols]).astype(BF16)
        dup[:, cols] = part
        column_sum = jnp.sum(part.astype(F32), axis=0, keepdims=True)
        for j in range(4):
            at = 512 * c + 128 * j
            sums[at // D : at // D + 1, at % D : at % D + 128] = column_sum[:, 128 * j : 128 * j + 128]
        grad[:, cols] = tn(hlow[...], dup[:, cols])
    for c in range(4):
        split_rows(grad.at[:, c * D : (c + 1) * D], keep, send, place, c)


def up_backward(place, dlow, slope, hlow, wd, after):
    return call(
        up_kernel,
        [(1, place)] + [(0, a) for a in (dlow, slope, hlow, wd)],
        [((WIN, FF), BF16), ((4, 4, CHUNK, D), BF16), ((4, 4, CHUNK, D), BF16), ((4, D), F32)],
        [pltpu.VMEM((D, FF), F32)],
        micros=3,
        name="up_backward",
        after=after,
    )


def first_kernel(
    place, dup, dsec, xhat1, inv1, att, vec, wu, wo,
    dfirst, datt, delta, okeep, osend, sums, grad, dlow,
):
    norm_backward(
        lambda r: nt(dup[r, :], wu[...]) + dsec[r, :],
        xhat1, inv1, vec[8:9, :], dfirst, dlow, sums, 0, WIDE_ROWS,
    )
    sums[3:8, :] = jnp.zeros((5, D), F32)
    grad[...] = tn(att[...], dlow[...])
    split_rows(grad, okeep, osend, place)
    da = nt(dlow[...], wo[...]).astype(BF16)
    datt[0:WIN, :] = da
    datt[WIN:PAD, :] = jnp.zeros((PAD - WIN, D), BF16)
    high, rest = low_pair(da.astype(F32) * att[...].astype(F32))
    heads = (iota((16, D), 1) // HD == iota((16, D), 0)).astype(F32).astype(BF16)
    delta[:, 0:WIN] = nt(heads, high) + nt(heads, rest)
    delta[:, WIN:PAD] = jnp.zeros((16, PAD - WIN), F32)


def first_backward(place, dup, dsec, xhat1, inv1, att, vec, wu, wo, after):
    return call(
        first_kernel,
        [(1, place)] + [(0, a) for a in (dup, dsec, xhat1, inv1, att, vec, wu, wo)],
        [
            ((WIN, D), F32),
            ((PAD, D), BF16),
            ((16, PAD), F32),
            ((4, CHUNK, D), BF16),
            ((4, CHUNK, D), BF16),
            ((8, D), F32),
        ],
        [
            pltpu.VMEM((D, D), F32),
            pltpu.VMEM((WIN, D), BF16),
        ],
        micros=3,
        name="first_backward",
        after=after,
    )


def heads_kernel(place, g, tokens, proj, datt, lse, delta, segc, segr, *rest):
    rest, (dproj, keep, send, sums, kt, dk, dv, grad, ktmp, stmp) = rest[:-10], rest[-10:]

    def lanes(part):
        return slice(part * D + 128 * g, part * D + 128 * g + 128)

    for t in range(PAD // 128):
        kt[:, 128 * t : 128 * t + 128] = (
            proj[128 * t : 128 * t + 128, lanes(1)].astype(F32).T.astype(BF16)
        )
    dk[...] = jnp.zeros_like(dk)
    dv[...] = jnp.zeros_like(dv)
    for q0, k0, k1 in BANDS:
        qs = head_stack(proj[q0 : q0 + BLOCK, lanes(0)])
        gs = head_stack(datt[q0 : q0 + BLOCK, lanes(0)])
        st = nt(proj[k0:k1, lanes(1)], qs)
        dp = nt(proj[k0:k1, lanes(2)], gs)
        same = segc[k0:k1, :] == segr[0:1, q0 : q0 + BLOCK]
        bias = jnp.where(same, 0.0, NEG_BIG)
        probs, d_scores, dq = [], [], []
        for j in range(4):
            cols = slice(j * BLOCK, (j + 1) * BLOCK)
            prob = jnp.exp2(st[:, cols] * EXP2_SCALE + bias - lse[g, j : j + 1, q0 : q0 + BLOCK])
            ds = prob * (dp[:, cols] - delta[4 * g + j : 4 * g + j + 1, q0 : q0 + BLOCK])
            ds = ds.astype(BF16)
            probs.append(prob.astype(BF16))
            d_scores.append(ds)
            if j % 2 == 1:
                part = nn(
                    kt[(j - 1) * HD : (j + 1) * HD, k0:k1], jnp.concatenate(d_scores[-2:], axis=1)
                )
                dq.append(part[0:HD, 0:BLOCK])
                dq.append(part[HD : 2 * HD, BLOCK : 2 * BLOCK])
        dv[k0:k1, :] += nn(jnp.concatenate(probs, axis=1), gs)
        dk[k0:k1, :] += nn(jnp.concatenate(d_scores, axis=1), qs)
        rows = min(BLOCK, WIN - q0)
        dqs = jnp.concatenate(dq, axis=0).T[0:rows] * HD ** (-0.5)
        dproj[q0 : q0 + rows, 0:128] = dqs.astype(BF16)
    dproj[:, 128:256] = (dk[...] * HD ** (-0.5)).astype(BF16)
    dproj[:, 256:384] = dv[...].astype(BF16)
    grad[...] = tn(tokens[aligned(OFF * place[0], WIN, 64), :], dproj[...])
    q_sum = jnp.sum(dproj[:, 0:128].astype(F32), axis=0, keepdims=True)
    v_sum = jnp.sum(dproj[:, 256:384].astype(F32), axis=0, keepdims=True)
    sums[0:1, :] = q_sum
    sums[1:2, :] = v_sum
    sums[2:8, :] = jnp.zeros((6, 128), F32)
    if g < 2:
        split_rows(grad, keep, send, place)
        return
    parts, (dsums, usums, fsums, zero, one) = rest[:6], rest[6:]
    split_rows(grad, ktmp, stmp, place)
    for dst, out_part, blocks in (
        (keep, parts[0], (parts[2], parts[4], ktmp)),
        (send, parts[1], (parts[3], parts[5], stmp)),
    ):
        dst[:, :, 3 * D : 4 * D] = out_part[...]
        for h, part in enumerate(blocks):
            for c in range(3):
                dst[:, :, D * c + 128 * h : D * c + 128 * h + 128] = part[
                    :, :, 128 * c : 128 * c + 128
                ]
    rows = jnp.concatenate(
        [
            jnp.concatenate([zero[0:1], one[0:1], q_sum], axis=1),
            jnp.concatenate([zero[1:2], one[1:2], v_sum], axis=1),
            fsums[0:1, :],
            usums[0:4, :],
            dsums[0:1, :],
            fsums[1:3, :],
            dsums[1:3, :],
            jnp.zeros((4, D), F32),
        ],
        axis=0,
    ).astype(BF16)
    for c in range(4):
        for j in range(3):
            block = rows[:, 128 * j : 128 * j + 128]
            keep[c, 16 * j : 16 * j + 16, 4 * D : 4 * D + 128] = block
            send[c, 16 * j : 16 * j + 16, 4 * D : 4 * D + 128] = block


def heads_backward(g, place, ins, more, after):
    part = ((4, CHUNK, 4 * D + 128 if g == 2 else D), BF16)
    return call(
        lambda place, *refs: heads_kernel(place, g, *refs),
        [(1, place)] + [(0, a) for a in tuple(ins) + tuple(more)],
        [((WIN, D), BF16), part, part, ((8, 128), F32)],
        [
            pltpu.VMEM((128, PAD), BF16),
            pltpu.VMEM((WIN, 128), F32),
            pltpu.VMEM((WIN, 128), F32),
            pltpu.VMEM((D, D), F32),
            pltpu.VMEM((4, CHUNK, D), BF16),
            pltpu.VMEM((4, CHUNK, D), BF16),
        ],
        micros=3,
        name="heads_backward",
        after=after,
    )


def input_kernel(dp0, dp1, dp2, dfirst, wfull, igrad, dproj):
    for g, part in enumerate((dp0, dp1, dp2)):
        for c in range(3):
            dproj[:, c * D + 128 * g : c * D + 128 * g + 128] = part[:, 128 * c : 128 * c + 128]
    igrad[...] = (nt(dproj[...], wfull[...]) + dfirst[...]).astype(BF16)


def input_backward(parts, dfirst, wqkv, after):
    return call(
        input_kernel,
        [(0, a) for a in tuple(parts) + (dfirst, wqkv)],
        [((WIN, D), BF16)],
        [pltpu.VMEM((WIN, 3 * D), BF16)],
        micros=2,
        name="input_backward",
        after=after,
    )[0]


def flips(axis, size, bits):
    return [(i, i ^ bits) for i in range(size)]


def pair(value):
    return swap(value, "opt", 2, 1)


def swap(value, axis, size, bits):
    return lax.ppermute(value, axis, flips(axis, size, bits))


def bit_groups(size):
    bits = size.bit_length() - 1
    return [(s, 1 << min(2, bits - s)) for s in range(0, bits, 2)]


def trades(values, n, shift):
    return [values[0]] + [swap(values[k], "dp", n, k << shift) for k in (1, 2, 3)]


def added(a, b):
    return (a.astype(F32) + b.astype(F32)).astype(BF16)


def core_sum_kernel(keep, other, *outs):
    for r, out in enumerate(outs):
        out[...] = added(keep[r], other[r])


def core_sum(keep, other, after):
    return call(
        core_sum_kernel,
        [(0, keep), (0, other)],
        [(keep.shape[1:], BF16)] * 4,
        name="core_sum",
        vmem=4,
        after=after,
    )


def pair_sum_kernel(bit, keep, other, stay, go):
    for i, r in enumerate((0, 3 - bit)):
        stay[i] = added(keep[r], other[r])
        go[i] = added(keep[r + bit], other[r + bit])


def pair_sum(bit, keep, other, after):
    return call(
        functools.partial(pair_sum_kernel, bit),
        [(0, keep), (0, other)],
        [((2,) + keep.shape[1:], BF16)] * 2,
        name="pair_sum",
        vmem=4,
        after=after,
    )


def wide_step_kernel(down, dother, up, uother, dkeep, dsend, ukeep, usend):
    dkeep[...] = added(down[0], dother[0])
    dsend[...] = added(down[1], dother[1])
    ukeep[...] = added(up[0], uother[0])
    usend[...] = added(up[1], uother[1])


def wide_step(parts, after):
    return call(
        wide_step_kernel,
        [(0, p) for p in parts],
        [((4, CHUNK, D), BF16)] * 4,
        name="wide_step",
        vmem=4,
        after=after,
    )


def total_of(refs, at):
    a, b, c, d = (ref[at].astype(F32) for ref in refs)
    return ((a + b) + (c + d)).astype(BF16)


def wide_plane_kernel(place, down, dother, up, uother, mine, send):
    z = place[3]
    for p, (keep, other) in enumerate(((down, dother), (up, uother))):
        for i, bits in enumerate((0, 2)):
            mine[2 * i + p] = added(keep[z ^ bits], other[z ^ bits])
            send[2 * i + p] = added(keep[z ^ bits ^ 1], other[z ^ bits ^ 1])


def wide_plane_sum(place, parts, after):
    return call(
        wide_plane_kernel,
        [(1, place)] + [(0, p) for p in parts],
        [((4, CHUNK, D), BF16)] * 2,
        name="wide_plane_sum",
        vmem=4,
        after=after,
    )


def wide_half_kernel(keep, other, mine, send):
    mine[...] = added(keep[0:2], other[0:2])
    send[...] = added(keep[2:4], other[2:4])


def wide_half(keep, other, after):
    return call(
        wide_half_kernel,
        [(0, keep), (0, other)],
        [((2, CHUNK, D), BF16)] * 2,
        name="wide_half",
        vmem=4,
        after=after,
    )


def low_plane_kernel(a, b, c, d, out):
    out[...] = total_of((a, b, c, d), slice(None))


def low_plane_sum(parts, after=()):
    return call(
        low_plane_kernel,
        [(0, p) for p in parts],
        [(parts[0].shape, BF16)],
        name="low_plane_sum",
        vmem=4,
        after=after,
    )[0]


def low_next_kernel(keep, other, out):
    out[...] = added(keep[...], other[...])


def low_next(keep, other, after=()):
    return call(
        low_next_kernel,
        [(0, keep), (0, other)],
        [(keep.shape, BF16)],
        name="low_next",
        vmem=4,
        after=after,
    )[0]


def low_last_kernel(keep, other, out, vgrad):
    out[...] = added(keep[:, 0 : 4 * D], other[:, 0 : 4 * D])
    vgrad[...] = added(keep[:, 4 * D : 4 * D + 128], other[:, 4 * D : 4 * D + 128])


def low_last(keep, other, after):
    return call(
        low_last_kernel,
        [(0, keep), (0, other)],
        [((CHUNK, 4 * D), BF16), ((CHUNK, 128), BF16)],
        name="low_last",
        vmem=4,
        after=after,
    )


def chain_kernel(*refs):
    ins, out = refs[:-1], refs[-1]
    at = 0
    for ref in ins:
        flat = ref.reshape(-1, CHUNK, D)
        out[at : at + flat.shape[0]] = flat[...]
        at += flat.shape[0]


def chain(parts, after=()):
    count = sum(p.size for p in parts) // (CHUNK * D)
    return call(
        chain_kernel,
        [(0, p) for p in parts],
        [((count, CHUNK, D), BF16)],
        name="chain",
        vmem=4,
        after=after,
    )[0]


def rest_sum(value, n):
    bit = 16
    while bit < n:
        other = swap(value, "dp", n, bit)
        value = (value.astype(F32) + other.astype(F32)).astype(BF16)
        bit *= 2
    return value


def join_kernel(*refs):
    ins, out = refs[:-1], refs[-1]
    for i, ref in enumerate(ins):
        out[i] = ref[...]


def join(parts, after=()):
    return call(
        join_kernel,
        [(0, p) for p in parts],
        [((len(parts),) + parts[0].shape, parts[0].dtype)],
        name="join",
        vmem=4,
        after=after,
    )[0]


def pack_kernel(marks, unit, other, units, packed):
    both = unit[...] + other[...]
    units[...] = both
    packed[:, 0:D] = both.astype(BF16)
    packed[:, D : D + 128] = marks[...]


def pack(marks, unit, other):
    return call(
        pack_kernel,
        [(0, marks), (0, unit), (0, other)],
        [(unit.shape, F32), ((2 * PAIRS, D + 128), BF16)],
        name="pack",
        vmem=4,
    )


def squares_of(parts):
    acc = jnp.zeros((8, D), F32)
    for part in parts:
        flat = part.reshape(-1, CHUNK, part.shape[-1])
        for k in range(flat.shape[0]):
            for c in range(0, part.shape[-1], D):
                v = flat[k, :, c : c + D].astype(F32)
                acc = acc + jnp.sum((v * v).reshape(CHUNK // 8, 8, D), axis=0)
    return acc[:, 0:128] + acc[:, 128:256] + acc[:, 256:384]


def wide_squares_kernel(*refs):
    refs[-1][...] = squares_of(refs[:-1])


def squares_kernel(place, *refs):
    parts, (vgrad, before, out) = refs[:-3], refs[-3:]
    acc = squares_of(parts) + before[...]
    row = iota((16, 128), 0)
    low_row = 6 * place[0]
    mine = (row >= low_row) & (row < low_row + 6)
    for j in range(3):
        v = jnp.where(mine, vgrad[16 * j : 16 * j + 16, :].astype(F32), 0.0)
        v = v * v
        acc = acc + (v[0:8] + v[8:16])
    out[...] = acc


def squares(place, parts, vgrad=None, before=None, after=()):
    ins = [(0, p) for p in parts]
    kernel = wide_squares_kernel
    if before is not None:
        ins = [(1, place)] + ins + [(0, vgrad), (0, before)]
        kernel = squares_kernel
    return call(kernel, ins, [((8, 128), F32)], name="squares", vmem=4, after=after)[0]


def merge_kernel(place, igrad, other, out, flag):
    flag[...] = jnp.zeros((8, 128), F32)

    @pl.when(place[0] == 0)
    def low_core():
        out[0:OFF, :] = igrad[0:OFF, :]
        out[OFF:WIN, :] = added(igrad[OFF:WIN, :], other[0 : WIN - OFF, :])
        out[WIN:SEQ, :] = other[WIN - OFF : WIN, :]

    @pl.when(place[0] != 0)
    def high_core():
        out[0:OFF, :] = other[0:OFF, :]
        out[OFF:WIN, :] = added(other[OFF:WIN, :], igrad[0 : WIN - OFF, :])
        out[WIN:SEQ, :] = igrad[WIN - OFF : WIN, :]


def merge(place, igrad, other, after):
    return call(
        merge_kernel,
        [(1, place), (0, igrad), (0, other)],
        [((SEQ, D), BF16), ((8, 128), F32)],
        name="merge",
        vmem=4,
        after=after,
    )


def adamw(parameter, first_state, second, clipped, rate):
    first_new = first_state + (1.0 - BETA_ONE) * clipped
    second_new = second + (1.0 - BETA_TWO) * clipped * clipped
    root = (1.0 - BETA_TWO**STEP) ** 0.5
    below = pl.reciprocal(second_new * lax.rsqrt(second_new) + ADAM_EPS * root)
    scale = rate * root / (1.0 - BETA_ONE**STEP)
    return parameter - scale * (first_new * below), first_new, second_new


def decay_kernel(w, m, v, pv, pm, pq, nw, nm, nv, npv, npm, npq):
    for ins, outs, rate in (
        ((w, m, v), (nw, nm, nv), LEARN_RATE),
        ((pv, pm, pq), (npv, npm, npq), VECTOR_RATE),
    ):
        for ref, out, scale in zip(ins, outs, (1.0 - rate * DECAY_RATE, BETA_ONE, BETA_TWO)):
            out[...] = ref[...] * scale


def decay(arrays, after):
    return call(
        decay_kernel,
        [(0, a) for a in arrays],
        [(a.shape, F32) for a in arrays],
        name="decay",
        vmem=4,
        after=after,
    )


def adamw_kernel(*refs):
    place = Place()
    sums, refs = refs[:2], refs[2:]
    (vgrad, w, m, v, pv, pm, pq), refs = refs[:7], refs[7:]
    wide, low, refs = refs[:4], refs[4:8], refs[8:]
    outs, (npv, npm, npq, norm), scrs, sems = refs[:4], refs[4:8], refs[8:12], refs[12]
    opt = place[0]
    total = sums[0][...] + sums[1][...]
    total = jnp.sum(jnp.sum(total, axis=1, keepdims=True), axis=0, keepdims=True)
    grad_norm = jnp.sqrt(total)
    factor = jnp.minimum(1.0, CLIP_NORM / (grad_norm + 1e-06))
    norm[...] = grad_norm
    for j in range(3):
        cols = slice(128 * j, 128 * j + 128)
        g = vgrad[16 * j : 16 * j + 16, :].astype(F32)
        g = jnp.where(opt == 0, g[0:6], g[6:12])
        a, b, c = adamw(pv[:, cols], pm[:, cols], pq[:, cols], g * factor, VECTOR_RATE)
        npv[:, cols] = a
        npm[:, cols] = b
        npq[:, cols] = c

    def block(grad, rows, cols):
        new = adamw(w[rows, cols], m[rows, cols], v[rows, cols], grad * factor, LEARN_RATE)
        for scr, value in zip(scrs, new + (new[0].astype(BF16),)):
            scr[rows, cols] = value

    def copies(r, i):
        rows = aligned(CHUNK * (place[1] ^ r) + i * 16, 16, 16)
        return [
            pltpu.make_async_copy(scr.at[rows, :], out.at[rows, :], sems.at[3 * r + i, j])
            for j, (scr, out) in enumerate(zip(scrs, outs))
        ]

    for r in range(4):

        def step(i, carry, r=r):
            rows = aligned(CHUNK * (place[1] ^ r) + i * 16, 16, 16)
            here = aligned(i * 16, 16, 16)
            for j in range(4):
                at = D * (place[3] ^ j)
                if j < 2:
                    part, near = wide[r % 2], r // 2
                else:
                    part, near = wide[2 + r // 2], r % 2
                for p, start in enumerate((4 * D + FF, 4 * D)):
                    grad = part[near, j % 2, p, here, :].astype(F32)
                    block(grad, rows, aligned(start + at, D, 128))
            for c in range(4):
                grad = low[r][here, D * c : D * c + D].astype(F32)
                block(grad, rows, slice(D * c, D * c + D))
            for copy in copies(r, i):
                copy.start()
            return carry

        lax.fori_loop(0, CHUNK // 16, step, 0)
    for r in range(4):

        def finish(i, carry, r=r):
            for copy in copies(r, i):
                copy.wait()
            return carry

        lax.fori_loop(0, CHUNK // 16, finish, 0)


def update(place, sums, vgrad, w, m, v, pv, pm, pq, parts):
    ins = tuple(sums) + (vgrad, w, m, v, pv, pm, pq) + tuple(parts)
    shapes = [(w.shape, F32)] * 3 + [(w.shape, BF16)] + [(pv.shape, F32)] * 3 + [((1, 1), F32)]
    return pl.pallas_call(
        adamw_kernel,
        out_shape=[jax.ShapeDtypeStruct(s, d) for s, d in shapes],
        in_specs=[VMEM] * len(ins),
        out_specs=[ANY] * 4 + [VMEM] * 4,
        scratch_shapes=[
            pltpu.VMEM(w.shape, F32),
            pltpu.VMEM(w.shape, F32),
            pltpu.VMEM(w.shape, F32),
            pltpu.VMEM(w.shape, BF16),
            pltpu.SemaphoreType.DMA((12, 4)),
        ],
        compiler_params=pltpu.CompilerParams(vmem_limit_bytes=16 << 20),
        cost_estimate=pl.CostEstimate(
            flops=4000000000, bytes_accessed=26 * w.size, transcendentals=0
        ),
        name="adamw",
    )(*ins)


def shards(
    n,
    tokens,
    lengths,
    query_index,
    doc_index,
    targets,
    weights,
    first_moment,
    second_moment,
    vectors,
    vec_first,
    vec_second,
):
    place = None
    scalars = jnp.concatenate([lengths.reshape(SEGS), query_index, doc_index, targets])
    groups = bit_groups(n)

    w_own, wo_own, wu_own, wd_own = cast(weights)
    w_other = pair(w_own)
    vectors_late, w_own = lax.optimization_barrier((vectors, w_own))
    v_other = pair(vectors_late)
    wo = (wo_own, pair(wo_own))
    wu = (wu_own, pair(wu_own))
    wd = (wd_own, pair(wd_own))

    proj, att, lse, segc, segr, ownc, ownr, wanted, marks, vec, wqkv = attend(
        place, scalars, (tokens, w_own, w_other, vectors, v_other)
    )
    xhat1, inv1, hlow, act, up_proj, xhat2, inv2, unit, uscale, wo, wu, wd = mlp(
        place, wanted, att, tokens, ownr, vec, wo + wu + wd
    )
    units, packed = pack(marks, unit, pair(unit))
    groups = bit_groups(n)
    order = [0]
    stack = packed
    for i, (shift, size) in enumerate(groups[1:] + groups[:1]):
        pieces = [stack] + [swap(stack, "dp", n, k << shift) for k in range(1, size)]
        order = [o | (k << shift) for k in range(size) for o in order]
        if i < len(groups) - 1:
            slope = slope_of(up_proj, [packed])
            stack = join(pieces, [slope]).reshape(-1, 2 * PAIRS, D + 128)
    decayed = decay(
        (weights, first_moment, second_moment, vectors, vec_first, vec_second), [packed]
    )
    dsec, dlow, keep, send, dsums = down_backward(
        n, order, place, wanted, units, ownc, uscale, (xhat2, inv2, act), vec, pieces,
        decayed,
    )
    other = pair(send)
    dup, ukeep, usend, usums = up_backward(place, dlow, slope, hlow, wd, [])
    down, go = pair_sum(1, keep, other, [dup])
    dother = swap(go, "dp", n, 1)
    up, go = pair_sum(2, ukeep, pair(usend), [down])
    uother = swap(go, "dp", n, 2)
    dfirst, datt, delta, okeep, osend, fsums = first_backward(
        place, dup, dsec, xhat1, inv1, att, vec, wu, wo, [up]
    )
    ins = (tokens, proj, datt, lse, delta, segc, segr)
    part0, keep0, send0, sums0 = heads_backward(0, place, ins, (), [])
    down, dsend, up, usend = wide_step((down, dother, up, uother), [part0])
    dother, uother = swap(dsend, "dp", n, 2), swap(usend, "dp", n, 1)
    part1, keep1, send1, sums1 = heads_backward(1, place, ins, (), [down])
    wide, go = wide_plane_sum(place, (down, dother, up, uother), [part1])
    wother = swap(go, "dp", n, 4)
    part2, keep, send, _ = heads_backward(
        2, place, ins,
        (okeep, osend, keep0, send0, keep1, send1, dsums, usums, fsums, sums0, sums1),
        [wide, part1],
    )
    wide, go = wide_half(wide, wother, [part2])
    send, wide, go = lax.optimization_barrier((send, wide, go))
    wother = swap(go, "dp", n, 8)
    other = pair(send)
    igrad = input_backward((part0, part1, part2), dfirst, wqkv, [wide])
    iother = pair(igrad)
    low = core_sum(keep, other, [igrad])
    low_got = trades(low, n, 0)
    wide = rest_sum(low_next(wide, wother, [low[0]]), n)
    wide_got = trades([wide] * 4, n, 2)
    low = low_plane_sum(low_got, [wide])
    other = swap(low, "dp", n, 4)
    first, last = join(wide_got[:2], [low]), join(wide_got[2:], [low])
    first_near, last_near = swap(first, "dp", n, 2), swap(last, "dp", n, 1)
    low = low_next(low, other, [first, last])
    other = swap(low, "dp", n, 8)
    input_grad, flag = merge(place, igrad, iother, [low])
    first, last = join([first, first_near], [flag]), join([last, last_near], [flag])
    wide = (first, swap(first, "dp", n, 1), last, swap(last, "dp", n, 2))
    low, vgrad = low_last(low, other, [first, last])
    low, vgrad = rest_sum(low, n), rest_sum(vgrad, n)
    low = trades([low] * 4, n, 0)
    sums = squares(place, low, vgrad, squares(place, wide, after=[low[0]]))
    sums = (sums, pair(sums))
    pieces = tuple(wide) + tuple(low)
    nw, nm, nv, nlow, npv, npm, npq, norm = update(
        place, sums, vgrad, *decayed, pieces,
    )
    return (norm.reshape(()), input_grad, nw, nm, nv, nlow, npv, npm, npq)


def solution(mesh):
    rows = P("opt", None)
    in_specs = (P("dp", None), P("dp", None), P("dp"), P("dp"), P("dp")) + (rows,) * 6
    out_specs = (P(), P("dp", None)) + (rows,) * 7
    n = mesh.shape["dp"]
    return jax.shard_map(
        functools.partial(shards, n),
        mesh=mesh,
        in_specs=in_specs,
        out_specs=out_specs,
        check_vma=False,
    )
```

```python
import functools

import jax
import jax.numpy as jnp
from jax import lax
from jax.experimental import pallas as pl
from jax.experimental.pallas import tpu as pltpu
from jax.sharding import PartitionSpec as P

D = 384
HEADS = 12
HD = 32
FF = 1536
SEQ = 1024
SEGS = 16
PAIRS = 8
STEP = 10

WIN = 576
OFF = SEQ - WIN
PAD = 640
BLOCK = 128
BANDS = tuple((q, max(0, q - 128), min(WIN, q + 256)) for q in range(0, WIN, BLOCK))
BAND_ROWS = tuple(sum(b[2] - b[1] for b in BANDS[:i]) for i in range(len(BANDS) + 1))
ROWS = 64
WIDE_ROWS = 192
LOG2E = 1.4426950408889634

LN_EPS = 1e-06
POOL_EPS = 1e-06
SCORE_SCALE = 50.0
CLIP_NORM = 0.001
BETA_ONE = 0.9
BETA_TWO = 0.98
ADAM_EPS = 1e-08
LEARN_RATE = 0.05
VECTOR_RATE = 0.3
DECAY_RATE = 0.01
NEG_BIG = -1e30
HALF = D // 2
CHUNK = HALF // 4
EXP2_SCALE = HD ** (-0.5) * 1.4426950408889634

F32 = jnp.float32
BF16 = jnp.bfloat16
VMEM = pl.BlockSpec(memory_space=pltpu.VMEM)
SMEM = pl.BlockSpec(memory_space=pltpu.SMEM)
ANY = pl.BlockSpec(memory_space=pl.ANY)


def nn(a, b):
    return jnp.dot(a, b, preferred_element_type=F32)


def nt(a, b):
    return lax.dot_general(a, b, (((1,), (1,)), ((), ())), preferred_element_type=F32)


def tn(a, b):
    return lax.dot_general(a, b, (((0,), (0,)), ((), ())), preferred_element_type=F32)


def exact(a, b, dims):
    return lax.dot_general(
        a, b, (dims, ((), ())), precision=lax.Precision.HIGHEST, preferred_element_type=F32
    )


def iota(shape, axis):
    return lax.broadcasted_iota(jnp.int32, shape, axis)


def low_pair(value):
    high = value.astype(BF16)
    return high, (value - high.astype(F32)).astype(BF16)


def aligned(start, size, unit):
    return pl.ds(pl.multiple_of(start, unit), size)


def assemble(dst, own, other, opt):
    dst[aligned(HALF * opt, HALF, 64), :] = own[0:HALF, :]
    dst[aligned(HALF * (1 - opt), HALF, 64), :] = other[0:HALF, :]


class Place:
    def __getitem__(self, i):
        if i == 0:
            return lax.axis_index("opt")
        me = lax.axis_index("dp")
        return (me & 3, me, (me >> 2) & 3)[i - 1]


def call(kernel, ins, outs, scratch=(), micros=5, name=None, vmem=12, after=()):
    if ins[0][1] is None:
        kernel = functools.partial(kernel, Place())
        ins = ins[1:]
    specs = [SMEM if s else VMEM for s, _ in ins] + [ANY] * len(after)
    count = len(ins)

    def body(*refs):
        kernel(*refs[:count], *refs[count + len(after) :])

    shapes = [jax.ShapeDtypeStruct(s, d) for s, d in outs]
    moved = sum(a.size * a.dtype.itemsize for _, a in ins)
    moved += sum(s.size * s.dtype.itemsize for s in shapes)
    return pl.pallas_call(
        body,
        out_shape=shapes,
        in_specs=specs,
        out_specs=[VMEM] * len(shapes),
        scratch_shapes=list(scratch),
        compiler_params=pltpu.CompilerParams(vmem_limit_bytes=vmem << 20),
        cost_estimate=pl.CostEstimate(
            flops=micros * 1100000000, bytes_accessed=moved, transcendentals=0
        ),
        name=name,
    )(*[a for _, a in ins], *after)


def head_stack(rows):
    lane_head = iota(rows.shape, 1) // HD
    zero = jnp.zeros_like(rows)
    return jnp.concatenate([jnp.where(lane_head == j, rows, zero) for j in range(4)], axis=0)


def attend_kernel(
    place, scalars, tokens, w_own, w_other, v_own, v_other,
    proj, att, lse, segc, segr, ownc, ownr, wanted, marks, vec, wfull, bias, vt,
):
    opt = place[0]
    assemble(wfull, w_own, w_other, opt)
    mine = v_own[...].astype(BF16).astype(F32)
    others = v_other[...].astype(BF16).astype(F32)
    first = opt == 0
    vec[0:6, :] = jnp.where(first, mine, others)
    vec[6:12, :] = jnp.where(first, others, mine)
    vec[12:16, :] = jnp.zeros((4, D), F32)

    position = iota((8, PAD), 1) + OFF * opt
    segment = jnp.zeros((8, PAD), jnp.int32)
    bound = jnp.int32(0)
    low_count = jnp.int32(0)
    for s in range(SEGS):
        bound = bound + scalars[s]
        segment = segment + (position >= bound).astype(jnp.int32)
        low_count = low_count + (bound <= WIN).astype(jnp.int32)
    mine = (segment < low_count).astype(jnp.int32) == (opt == 0).astype(jnp.int32)
    owned = jnp.where(mine, segment, -1)
    segr[...] = segment
    ownr[...] = owned
    for value, out in ((segment, segc), (owned, ownc)):
        value = value.astype(F32)
        for t in range(PAD // 128):
            rows = min(128, WIN - 128 * t)
            turned = jnp.broadcast_to(value[0:1, 128 * t : 128 * t + 128], (128, 128)).T
            out[128 * t : 128 * t + rows, :] = turned[0:rows].astype(jnp.int32)
    row, col = iota((2 * PAIRS, 128), 0), iota((2 * PAIRS, 128), 1)
    by_row = jnp.zeros((2 * PAIRS, 128), jnp.int32)
    by_col = jnp.zeros((2 * PAIRS, 128), jnp.int32)
    mark = jnp.zeros((2 * PAIRS, 128), jnp.int32)
    for j in range(PAIRS):
        mark = jnp.where(row == j, scalars[SEGS + 2 * PAIRS + j], mark)
        for at in (j, PAIRS + j):
            by_row = jnp.where(row == at, scalars[SEGS + at], by_row)
            by_col = jnp.where(col == at, scalars[SEGS + at], by_col)
    wanted[0] = by_row
    wanted[1] = by_col
    marks[...] = jnp.where(col < 64, mark >> 5, mark & 31).astype(F32).astype(BF16)
    for i, (q0, k0, k1) in enumerate(BANDS):
        bias[BAND_ROWS[i] : BAND_ROWS[i + 1], :] = jnp.where(
            segc[k0:k1, :] == segr[0:1, q0 : q0 + BLOCK], 0.0, NEG_BIG
        )

    x = tokens[aligned(OFF * opt, WIN, 64), :]
    bias_row = jnp.concatenate([vec[0:1, :], jnp.zeros((1, D), F32), vec[1:2, :]], axis=1)
    for first in range(0, 3 * D, 512):
        cols = slice(first, min(first + 512, 3 * D))
        proj[0:WIN, cols] = (nn(x, wfull[:, cols]) + bias_row[:, cols]).astype(BF16)
    proj[WIN:PAD, :] = jnp.zeros((PAD - WIN, 3 * D), BF16)

    def group(g, carry):
        def lanes(part):
            return aligned(part * D + 128 * g, 128, 128)

        for t in range(PAD // 128):
            vt[:, 128 * t : 128 * t + 128] = (
                proj[128 * t : 128 * t + 128, lanes(2)].astype(F32).T.astype(BF16)
            )
        def scores(i):
            q0, k0, k1 = BANDS[i]
            return nt(proj[k0:k1, lanes(1)], head_stack(proj[q0 : q0 + BLOCK, lanes(0)]))

        coming = scores(0)
        for i, (q0, k0, k1) in enumerate(BANDS):
            st = coming
            if i + 1 < len(BANDS):
                coming = scores(i + 1)
            outs, probs, totals = [], [], []
            for j in range(4):
                t = (
                    st[:, j * BLOCK : (j + 1) * BLOCK] * EXP2_SCALE
                    + bias[BAND_ROWS[i] : BAND_ROWS[i + 1], :]
                )
                peak = jnp.max(t, axis=0, keepdims=True)
                powers = jnp.exp2(t - peak)
                total = jnp.sum(powers, axis=0, keepdims=True)
                lse[g, j : j + 1, q0 : q0 + BLOCK] = peak + jnp.log2(total)
                probs.append(powers.astype(BF16))
                totals.append(1.0 / total)
                if j % 2 == 1:
                    o = nn(vt[(j - 1) * HD : (j + 1) * HD, k0:k1], jnp.concatenate(probs[-2:], axis=1))
                    outs.append(o[0:HD, 0:BLOCK] * totals[-2])
                    outs.append(o[HD : 2 * HD, BLOCK : 2 * BLOCK] * totals[-1])
            rows = min(BLOCK, WIN - q0)
            att[q0 : q0 + rows, aligned(128 * g, 128, 128)] = (
                jnp.concatenate(outs, axis=0).T[0:rows].astype(BF16)
            )
        return carry

    lax.fori_loop(0, 3, group, 0)


def attend(place, scalars, arrays):
    return call(
        attend_kernel,
        [(1, place), (1, scalars)] + [(0, a) for a in arrays],
        [
            ((PAD, 3 * D), BF16),
            ((WIN, D), BF16),
            ((3, 4, PAD), F32),
            ((WIN, 128), jnp.int32),
            ((8, PAD), jnp.int32),
            ((WIN, 128), jnp.int32),
            ((8, PAD), jnp.int32),
            ((2, 2 * PAIRS, 128), jnp.int32),
            ((2 * PAIRS, 128), BF16),
            ((16, D), F32),
            ((D, 3 * D), BF16),
        ],
        [
            pltpu.VMEM((BAND_ROWS[-1], 128), F32),
            pltpu.VMEM((128, PAD), BF16),
        ],
        micros=8,
        name="attend",
    )


def cast_kernel(weights, wq, wo, wu, wd, buffer, sems):
    spans = [(wq, 3 * D), (wo, D), (wu, FF), (wd, FF)]
    copies = [
        pltpu.make_async_copy(
            weights.at[:, i * D : (i + 1) * D], buffer.at[:, i * D : (i + 1) * D], sems.at[i]
        )
        for i in range(12)
    ]
    for copy in copies:
        copy.start()
    at = 0
    for out, width in spans:
        for part in range(width // D):
            copies[at].wait()
            out[:, part * D : (part + 1) * D] = buffer[:, at * D : (at + 1) * D].astype(BF16)
            at += 1


def cast(weights):
    return pl.pallas_call(
        cast_kernel,
        out_shape=[jax.ShapeDtypeStruct((HALF, c), BF16) for c in (3 * D, D, FF, FF)],
        in_specs=[ANY],
        out_specs=[VMEM] * 4,
        scratch_shapes=[pltpu.VMEM(weights.shape, F32), pltpu.SemaphoreType.DMA((12,))],
        compiler_params=pltpu.CompilerParams(vmem_limit_bytes=52 << 20),
        name="cast",
    )(weights)


def bias_of(vec, c):
    first, last = 256 * c, 256 * c + 256
    parts = []
    while first < last:
        row, col = divmod(first, D)
        size = min(D - col, last - first)
        parts.append(vec[3 + row : 4 + row, col : col + size])
        first += size
    return parts[0] if len(parts) == 1 else jnp.concatenate(parts, axis=1)


def mlp_kernel(
    place, wanted, att, tokens, ownr, vec, wo_own, wo_other, wu_own, wu_other,
    wd_own, wd_other, xhat1, inv1, hlow, act, up_proj, xhat2, inv2, unit, uscale, wo, wu, wd,
    ench, encl,
):
    opt = place[0]
    assemble(wo, wo_own, wo_other, opt)
    assemble(wu, wu_own, wu_other, opt)
    assemble(wd, wd_own, wd_other, opt)

    def norm(v):
        centred = v - jnp.mean(v, axis=1, keepdims=True)
        inverse = lax.rsqrt(jnp.mean(centred * centred, axis=1, keepdims=True) + LN_EPS)
        return centred * inverse, inverse

    def block(i, carry):
        r = aligned(i * WIDE_ROWS, WIDE_ROWS, 64)
        x = tokens[aligned(OFF * opt + i * WIDE_ROWS, WIDE_ROWS, 64), :].astype(F32)
        normed, inverse = norm(nn(att[r, :], wo[...]) + vec[2:3, :] + x)
        xhat1[r, :] = normed
        inv1[r, :] = jnp.broadcast_to(inverse, (WIDE_ROWS, 128))
        h = normed * vec[8:9, :] + vec[9:10, :]
        low = h.astype(BF16)
        hlow[r, :] = low
        coming = nn(low, wu[:, 0:256])
        for c in range(6):
            cols = slice(c * 256, (c + 1) * 256)
            u = coming + bias_of(vec, c)
            if c < 5:
                coming = nn(low, wu[:, (c + 1) * 256 : (c + 2) * 256])
            up_proj[r, cols] = u
            half = lax.erf(u * 0.7071067811865476) * 0.5 + 0.5
            act[r, cols] = (u * half).astype(BF16)
        normed, inverse = norm(nt(act[r, :], wd[...]) + vec[7:8, :] + h)
        xhat2[r, :] = normed
        inv2[r, :] = jnp.broadcast_to(inverse, (WIDE_ROWS, 128))
        high, rest = low_pair(normed * vec[10:11, :] + vec[11:12, :])
        ench[r, :] = high
        encl[r, :] = rest
        return carry

    lax.fori_loop(0, WIN // WIDE_ROWS, block, 0)

    onehot = jnp.where(wanted[0, :, 0:1] == ownr[0:1, 0:WIN], 1.0, 0.0)
    count = jnp.maximum(jnp.sum(onehot, axis=1, keepdims=True), 1.0)
    hot = onehot.astype(BF16)
    pooled = (nn(hot, ench[...]) + nn(hot, encl[...])) / count
    inverse_len = lax.rsqrt(jnp.sum(pooled * pooled, axis=1, keepdims=True) + POOL_EPS)
    unit[...] = pooled * inverse_len
    uscale[...] = jnp.broadcast_to(inverse_len / count, (2 * PAIRS, 128))


def slope_kernel(up_proj, out):
    def block(i, carry):
        r = aligned(i * 16, 16, 16)
        u = up_proj[r, :]
        half = lax.erf(u * 0.7071067811865476) * 0.5 + 0.5
        out[r, :] = half + u * jnp.exp2(u * u * (-0.5 * LOG2E)) * 0.3989422804014327
        return carry

    lax.fori_loop(0, WIN // 16, block, 0)


def slope_of(up_proj, after):
    return call(slope_kernel, [(0, up_proj)], [(up_proj.shape, F32)], name="slope", vmem=4, after=after)[0]


def mlp(place, wanted, att, tokens, ownr, vec, halves):
    return call(
        mlp_kernel,
        [(1, place), (0, wanted), (0, att), (0, tokens), (0, ownr), (0, vec)]
        + [(0, h) for h in halves],
        [
            ((WIN, D), F32),
            ((WIN, 128), F32),
            ((WIN, D), BF16),
            ((WIN, FF), BF16),
            ((WIN, FF), F32),
            ((WIN, D), F32),
            ((WIN, 128), F32),
            ((2 * PAIRS, D), F32),
            ((2 * PAIRS, 128), F32),
            ((D, D), BF16),
            ((D, FF), BF16),
            ((D, FF), BF16),
        ],
        [
            pltpu.VMEM((WIN, D), BF16),
            pltpu.VMEM((WIN, D), BF16),
        ],
        micros=10,
        name="mlp",
    )


def split_rows(grad, keep, send, place, *at):
    opt = place[0]
    for c in range(4):
        index = (c ^ place[1],) + at
        keep[index] = grad[aligned(HALF * opt + CHUNK * c, CHUNK, 16), :].astype(BF16)
        send[index] = grad[aligned(HALF * (1 - opt) + CHUNK * c, CHUNK, 16), :].astype(BF16)


def column_sums(value):
    return jnp.sum(value.reshape(-1, 8, D), axis=0)


def norm_backward(grad_at, normed_ref, inverse_ref, gain, out, low_out, sums, at, step=ROWS):
    def block(i, carry):
        scale_sum, shift_sum, bias_sum = carry
        r = aligned(i * step, step, 64)
        g = grad_at(r)
        normed = normed_ref[r, :]
        scaled = g * gain
        inner = (
            scaled
            - jnp.mean(scaled, axis=1, keepdims=True)
            - normed * jnp.mean(scaled * normed, axis=1, keepdims=True)
        ) * inverse_ref[r, 0:1]
        out[r, :] = inner
        low_out[r, :] = inner.astype(BF16)
        return (
            scale_sum + column_sums(g * normed),
            shift_sum + column_sums(g),
            bias_sum + column_sums(inner),
        )

    zero = jnp.zeros((8, D), F32)
    scale_sum, shift_sum, bias_sum = lax.fori_loop(0, WIN // step, block, (zero, zero, zero))
    sums[at : at + 1, :] = jnp.sum(bias_sum, axis=0, keepdims=True)
    sums[at + 1 : at + 2, :] = jnp.sum(scale_sum, axis=0, keepdims=True)
    sums[at + 2 : at + 3, :] = jnp.sum(shift_sum, axis=0, keepdims=True)


def down_kernel(
    place, count, order, wanted, units, ownc, uscale, xhat2, inv2, act, vec, *rest
):
    pieces, (dsec, dlow, keep, send, sums, queries, docs, marks, grad) = rest[:-9], rest[-9:]
    me = place[2]
    per = pieces[0].shape[0]
    for p, piece in enumerate(pieces):
        for j in range(per):
            at = order[p * per + j]
            r = slice(at * PAIRS, (at + 1) * PAIRS)
            both = piece[j].astype(F32)
            queries[r, :] = both[0:PAIRS, 0:D]
            docs[r, :] = both[PAIRS : 2 * PAIRS, 0:D]
            marks[r, :] = both[0:PAIRS, D : D + 128]
    total = count * PAIRS
    q = queries[...].astype(BF16)
    d = docs[...].astype(BF16)
    logits = SCORE_SCALE * nt(q, d)
    peak = jnp.max(logits, axis=1, keepdims=True)
    powers = jnp.exp(logits - peak)
    soft = powers / jnp.sum(powers, axis=1, keepdims=True)
    col = iota((total, total), 1)
    doc_id = ((col // PAIRS) ^ me) * PAIRS + lax.rem(col, PAIRS)
    hit = (marks[:, 0:1] * 32.0 + marks[:, 64:65]).astype(jnp.int32) == doc_id
    d_logits = (soft - jnp.where(hit, 1.0, 0.0)) * (SCORE_SCALE / total)
    high, rest_low = low_pair(d_logits[0:PAIRS, :])
    d_q = nn(high, d) + nn(rest_low, d)
    high, rest_low = low_pair(d_logits[:, 0:128].T[0:PAIRS, :])
    d_d = nn(high, q) + nn(rest_low, q)
    d_units = jnp.concatenate([d_q, d_d], axis=0)
    u = units[...]
    d_pool = uscale[:, 0:1] * (d_units - u * jnp.sum(u * d_units, axis=1, keepdims=True))
    hot = jnp.where(ownc[:, 0 : 2 * PAIRS] == wanted[1, 0:1, 0 : 2 * PAIRS], 1.0, 0.0).astype(BF16)
    high, rest_low = low_pair(d_pool)
    dsec[...] = nn(hot, high) + nn(hot, rest_low)
    norm_backward(lambda r: dsec[r, :], xhat2, inv2, vec[10:11, :], dsec, dlow, sums, 0)
    sums[3:8, :] = jnp.zeros((5, D), F32)
    for c in range(3):
        cols = slice(c * 512, (c + 1) * 512)
        grad[:, cols] = tn(dlow[...], act[:, cols])
    for c in range(4):
        split_rows(grad.at[:, c * D : (c + 1) * D], keep, send, place, c)


def down_backward(count, order, place, wanted, units, ownc, uscale, saved, vec, pieces, after):
    total = count * PAIRS
    return call(
        lambda place, *refs: down_kernel(place, count, order, *refs),
        [(1, place), (0, wanted), (0, units), (0, ownc), (0, uscale)]
        + [(0, s) for s in saved]
        + [(0, vec)]
        + [(0, p) for p in pieces],
        [
            ((WIN, D), F32),
            ((WIN, D), BF16),
            ((4, 4, CHUNK, D), BF16),
            ((4, 4, CHUNK, D), BF16),
            ((8, D), F32),
        ],
        [
            pltpu.VMEM((total, D), F32),
            pltpu.VMEM((total, D), F32),
            pltpu.VMEM((total, 128), F32),
            pltpu.VMEM((D, FF), F32),
        ],
        micros=4,
        name="down_backward",
        after=after,
    )


def up_kernel(place, dlow, slope, hlow, wd, dup, keep, send, sums, grad):
    coming = nn(dlow[...], wd[:, 0:512])
    for c in range(3):
        cols = slice(c * 512, (c + 1) * 512)
        part = (coming * slope[:, cols]).astype(BF16)
        if c < 2:
            coming = nn(dlow[...], wd[:, (c + 1) * 512 : (c + 2) * 512])
        dup[:, cols] = part
        column_sum = jnp.sum(part.astype(F32), axis=0, keepdims=True)
        for j in range(4):
            at = 512 * c + 128 * j
            sums[at // D : at // D + 1, at % D : at % D + 128] = column_sum[:, 128 * j : 128 * j + 128]
        grad[:, cols] = tn(hlow[...], dup[:, cols])
    for c in range(4):
        split_rows(grad.at[:, c * D : (c + 1) * D], keep, send, place, c)


def up_backward(place, dlow, slope, hlow, wd, after):
    return call(
        up_kernel,
        [(1, place)] + [(0, a) for a in (dlow, slope, hlow, wd)],
        [((WIN, FF), BF16), ((4, 4, CHUNK, D), BF16), ((4, 4, CHUNK, D), BF16), ((4, D), F32)],
        [pltpu.VMEM((D, FF), F32)],
        micros=3,
        name="up_backward",
        after=after,
    )


def first_kernel(
    place, dup, dsec, xhat1, inv1, att, vec, wu, wo,
    dfirst, datt, delta, okeep, osend, sums, grad, dlow,
):
    steps = [slice(i, i + WIDE_ROWS) for i in range(0, WIN, WIDE_ROWS)]
    coming = nt(dup[steps[0], :], wu[...])
    gain = vec[8:9, :]
    totals = None
    for i, r in enumerate(steps):
        g = coming + dsec[r, :]
        if i + 1 < len(steps):
            coming = nt(dup[steps[i + 1], :], wu[...])
        normed = xhat1[r, :]
        scaled = g * gain
        inner = (
            scaled
            - jnp.mean(scaled, axis=1, keepdims=True)
            - normed * jnp.mean(scaled * normed, axis=1, keepdims=True)
        ) * inv1[r, 0:1]
        dfirst[r, :] = inner
        dlow[r, :] = inner.astype(BF16)
        new = [column_sums(inner), column_sums(g * normed), column_sums(g)]
        totals = new if totals is None else [a + b for a, b in zip(totals, new)]
    for i, total in enumerate(totals):
        sums[i : i + 1, :] = jnp.sum(total, axis=0, keepdims=True)
    sums[3:8, :] = jnp.zeros((5, D), F32)
    grad[...] = tn(att[...], dlow[...])
    split_rows(grad, okeep, osend, place)
    da = nt(dlow[...], wo[...]).astype(BF16)
    datt[0:WIN, :] = da
    datt[WIN:PAD, :] = jnp.zeros((PAD - WIN, D), BF16)
    high, rest = low_pair(da.astype(F32) * att[...].astype(F32))
    heads = (iota((16, D), 1) // HD == iota((16, D), 0)).astype(F32).astype(BF16)
    delta[:, 0:WIN] = nt(heads, high) + nt(heads, rest)
    delta[:, WIN:PAD] = jnp.zeros((16, PAD - WIN), F32)


def first_backward(place, dup, dsec, xhat1, inv1, att, vec, wu, wo, after):
    return call(
        first_kernel,
        [(1, place)] + [(0, a) for a in (dup, dsec, xhat1, inv1, att, vec, wu, wo)],
        [
            ((WIN, D), F32),
            ((PAD, D), BF16),
            ((16, PAD), F32),
            ((4, CHUNK, D), BF16),
            ((4, CHUNK, D), BF16),
            ((8, D), F32),
        ],
        [
            pltpu.VMEM((D, D), F32),
            pltpu.VMEM((WIN, D), BF16),
        ],
        micros=1,
        name="first_backward",
        after=after,
    )


def heads_kernel(place, g, tokens, proj, datt, lse, delta, segc, segr, *rest):
    rest, (dproj, keep, send, sums, kt, dk, dv, grad, ktmp, stmp) = rest[:-10], rest[-10:]

    def lanes(part):
        return slice(part * D + 128 * g, part * D + 128 * g + 128)

    for t in range(PAD // 128):
        kt[:, 128 * t : 128 * t + 128] = (
            proj[128 * t : 128 * t + 128, lanes(1)].astype(F32).T.astype(BF16)
        )
    dk[...] = jnp.zeros_like(dk)
    dv[...] = jnp.zeros_like(dv)

    def products(i):
        q0, k0, k1 = BANDS[i]
        qs = head_stack(proj[q0 : q0 + BLOCK, lanes(0)])
        gs = head_stack(datt[q0 : q0 + BLOCK, lanes(0)])
        return qs, gs, nt(proj[k0:k1, lanes(1)], qs), nt(proj[k0:k1, lanes(2)], gs)

    coming = products(0)
    for i, (q0, k0, k1) in enumerate(BANDS):
        qs, gs, st, dp = coming
        if i + 1 < len(BANDS):
            coming = products(i + 1)
        same = segc[k0:k1, :] == segr[0:1, q0 : q0 + BLOCK]
        bias = jnp.where(same, 0.0, NEG_BIG)
        probs, d_scores, dq = [], [], []
        for j in range(4):
            cols = slice(j * BLOCK, (j + 1) * BLOCK)
            prob = jnp.exp2(st[:, cols] * EXP2_SCALE + bias - lse[g, j : j + 1, q0 : q0 + BLOCK])
            ds = prob * (dp[:, cols] - delta[4 * g + j : 4 * g + j + 1, q0 : q0 + BLOCK])
            ds = ds.astype(BF16)
            probs.append(prob.astype(BF16))
            d_scores.append(ds)
            if j % 2 == 1:
                part = nn(
                    kt[(j - 1) * HD : (j + 1) * HD, k0:k1], jnp.concatenate(d_scores[-2:], axis=1)
                )
                dq.append(part[0:HD, 0:BLOCK])
                dq.append(part[HD : 2 * HD, BLOCK : 2 * BLOCK])
        dv[k0:k1, :] += nn(jnp.concatenate(probs, axis=1), gs)
        dk[k0:k1, :] += nn(jnp.concatenate(d_scores, axis=1), qs)
        rows = min(BLOCK, WIN - q0)
        dqs = jnp.concatenate(dq, axis=0).T[0:rows] * HD ** (-0.5)
        dproj[q0 : q0 + rows, 0:128] = dqs.astype(BF16)
    dproj[:, 128:256] = (dk[...] * HD ** (-0.5)).astype(BF16)
    dproj[:, 256:384] = dv[...].astype(BF16)
    grad[...] = tn(tokens[aligned(OFF * place[0], WIN, 64), :], dproj[...])
    q_sum = jnp.sum(dproj[:, 0:128].astype(F32), axis=0, keepdims=True)
    v_sum = jnp.sum(dproj[:, 256:384].astype(F32), axis=0, keepdims=True)
    sums[0:1, :] = q_sum
    sums[1:2, :] = v_sum
    sums[2:8, :] = jnp.zeros((6, 128), F32)
    if g < 2:
        split_rows(grad, keep, send, place)
        return
    parts, (dsums, usums, fsums, zero, one) = rest[:6], rest[6:]
    split_rows(grad, ktmp, stmp, place)
    for dst, out_part, blocks in (
        (keep, parts[0], (parts[2], parts[4], ktmp)),
        (send, parts[1], (parts[3], parts[5], stmp)),
    ):
        dst[:, :, 3 * D : 4 * D] = out_part[...]
        for h, part in enumerate(blocks):
            for c in range(3):
                dst[:, :, D * c + 128 * h : D * c + 128 * h + 128] = part[
                    :, :, 128 * c : 128 * c + 128
                ]
    rows = jnp.concatenate(
        [
            jnp.concatenate([zero[0:1], one[0:1], q_sum], axis=1),
            jnp.concatenate([zero[1:2], one[1:2], v_sum], axis=1),
            fsums[0:1, :],
            usums[0:4, :],
            dsums[0:1, :],
            fsums[1:3, :],
            dsums[1:3, :],
            jnp.zeros((4, D), F32),
        ],
        axis=0,
    ).astype(BF16)
    for c in range(4):
        for j in range(3):
            block = rows[:, 128 * j : 128 * j + 128]
            keep[c, 16 * j : 16 * j + 16, 4 * D : 4 * D + 128] = block
            send[c, 16 * j : 16 * j + 16, 4 * D : 4 * D + 128] = block


def heads_backward(g, place, ins, more, after):
    part = ((4, CHUNK, 4 * D + 128 if g == 2 else D), BF16)
    return call(
        lambda place, *refs: heads_kernel(place, g, *refs),
        [(1, place)] + [(0, a) for a in tuple(ins) + tuple(more)],
        [((WIN, D), BF16), part, part, ((8, 128), F32)],
        [
            pltpu.VMEM((128, PAD), BF16),
            pltpu.VMEM((WIN, 128), F32),
            pltpu.VMEM((WIN, 128), F32),
            pltpu.VMEM((D, D), F32),
            pltpu.VMEM((4, CHUNK, D), BF16),
            pltpu.VMEM((4, CHUNK, D), BF16),
        ],
        micros=1,
        name="heads_backward",
        after=after,
    )


def input_kernel(dp0, dp1, dp2, dfirst, wfull, igrad, dproj):
    for g, part in enumerate((dp0, dp1, dp2)):
        for c in range(3):
            dproj[:, c * D + 128 * g : c * D + 128 * g + 128] = part[:, 128 * c : 128 * c + 128]
    igrad[...] = (nt(dproj[...], wfull[...]) + dfirst[...]).astype(BF16)


def input_backward(parts, dfirst, wqkv, after):
    return call(
        input_kernel,
        [(0, a) for a in tuple(parts) + (dfirst, wqkv)],
        [((WIN, D), BF16)],
        [pltpu.VMEM((WIN, 3 * D), BF16)],
        micros=2,
        name="input_backward",
        after=after,
    )[0]


def flips(axis, size, bits):
    return [(i, i ^ bits) for i in range(size)]


def pair(value):
    return swap(value, "opt", 2, 1)


def swap(value, axis, size, bits):
    return lax.ppermute(value, axis, flips(axis, size, bits))


def bit_groups(size):
    bits = size.bit_length() - 1
    return [(s, 1 << min(2, bits - s)) for s in range(0, bits, 2)]


def trades(values, n, shift):
    return [values[0]] + [swap(values[k], "dp", n, k << shift) for k in (1, 2, 3)]


def added(a, b):
    return (a.astype(F32) + b.astype(F32)).astype(BF16)


def core_sum_kernel(keep, other, *outs):
    for r, out in enumerate(outs):
        out[...] = added(keep[r], other[r])


def core_sum(keep, other, after):
    return call(
        core_sum_kernel,
        [(0, keep), (0, other)],
        [(keep.shape[1:], BF16)] * 4,
        name="core_sum",
        vmem=4,
        after=after,
    )


def pair_sum_kernel(bit, keep, other, stay, go):
    for i, r in enumerate((0, 3 - bit)):
        stay[i] = added(keep[r], other[r])
        go[i] = added(keep[r + bit], other[r + bit])


def pair_sum(bit, keep, other, after):
    return call(
        functools.partial(pair_sum_kernel, bit),
        [(0, keep), (0, other)],
        [((2,) + keep.shape[1:], BF16)] * 2,
        name="pair_sum",
        vmem=4,
        after=after,
    )


def wide_step_kernel(down, dother, up, uother, dkeep, dsend, ukeep, usend):
    dkeep[...] = added(down[0], dother[0])
    dsend[...] = added(down[1], dother[1])
    ukeep[...] = added(up[0], uother[0])
    usend[...] = added(up[1], uother[1])


def wide_step(parts, after):
    return call(
        wide_step_kernel,
        [(0, p) for p in parts],
        [((4, CHUNK, D), BF16)] * 4,
        name="wide_step",
        vmem=4,
        after=after,
    )


def total_of(refs, at):
    a, b, c, d = (ref[at].astype(F32) for ref in refs)
    return ((a + b) + (c + d)).astype(BF16)


def wide_plane_kernel(place, down, dother, up, uother, mine, send):
    z = place[3]
    for p, (keep, other) in enumerate(((down, dother), (up, uother))):
        for i, bits in enumerate((0, 2)):
            mine[2 * i + p] = added(keep[z ^ bits], other[z ^ bits])
            send[2 * i + p] = added(keep[z ^ bits ^ 1], other[z ^ bits ^ 1])


def wide_plane_sum(place, parts, after):
    return call(
        wide_plane_kernel,
        [(1, place)] + [(0, p) for p in parts],
        [((4, CHUNK, D), BF16)] * 2,
        name="wide_plane_sum",
        vmem=4,
        after=after,
    )


def wide_half_kernel(keep, other, mine, send):
    mine[...] = added(keep[0:2], other[0:2])
    send[...] = added(keep[2:4], other[2:4])


def wide_half(keep, other, after):
    return call(
        wide_half_kernel,
        [(0, keep), (0, other)],
        [((2, CHUNK, D), BF16)] * 2,
        name="wide_half",
        vmem=4,
        after=after,
    )


def low_plane_kernel(a, b, c, d, out):
    out[...] = total_of((a, b, c, d), slice(None))


def low_plane_sum(parts, after=()):
    return call(
        low_plane_kernel,
        [(0, p) for p in parts],
        [(parts[0].shape, BF16)],
        name="low_plane_sum",
        vmem=4,
        after=after,
    )[0]


def low_next_kernel(keep, other, out):
    out[...] = added(keep[...], other[...])


def low_next(keep, other, after=()):
    return call(
        low_next_kernel,
        [(0, keep), (0, other)],
        [(keep.shape, BF16)],
        name="low_next",
        vmem=4,
        after=after,
    )[0]


def low_last_kernel(keep, other, out, vgrad):
    out[...] = added(keep[:, 0 : 4 * D], other[:, 0 : 4 * D])
    vgrad[...] = added(keep[:, 4 * D : 4 * D + 128], other[:, 4 * D : 4 * D + 128])


def low_last(keep, other, after):
    return call(
        low_last_kernel,
        [(0, keep), (0, other)],
        [((CHUNK, 4 * D), BF16), ((CHUNK, 128), BF16)],
        name="low_last",
        vmem=4,
        after=after,
    )


def chain_kernel(*refs):
    ins, out = refs[:-1], refs[-1]
    at = 0
    for ref in ins:
        flat = ref.reshape(-1, CHUNK, D)
        out[at : at + flat.shape[0]] = flat[...]
        at += flat.shape[0]


def chain(parts, after=()):
    count = sum(p.size for p in parts) // (CHUNK * D)
    return call(
        chain_kernel,
        [(0, p) for p in parts],
        [((count, CHUNK, D), BF16)],
        name="chain",
        vmem=4,
        after=after,
    )[0]


def rest_sum(value, n):
    bit = 16
    while bit < n:
        other = swap(value, "dp", n, bit)
        value = (value.astype(F32) + other.astype(F32)).astype(BF16)
        bit *= 2
    return value


def join_kernel(*refs):
    ins, out = refs[:-1], refs[-1]
    for i, ref in enumerate(ins):
        out[i] = ref[...]


def join(parts, after=()):
    return call(
        join_kernel,
        [(0, p) for p in parts],
        [((len(parts),) + parts[0].shape, parts[0].dtype)],
        name="join",
        vmem=4,
        after=after,
    )[0]


def pack_kernel(marks, unit, other, units, packed):
    both = unit[...] + other[...]
    units[...] = both
    packed[:, 0:D] = both.astype(BF16)
    packed[:, D : D + 128] = marks[...]


def pack(marks, unit, other):
    return call(
        pack_kernel,
        [(0, marks), (0, unit), (0, other)],
        [(unit.shape, F32), ((2 * PAIRS, D + 128), BF16)],
        name="pack",
        vmem=4,
    )


def squares_of(parts):
    acc = jnp.zeros((8, D), F32)
    for part in parts:
        flat = part.reshape(-1, CHUNK, part.shape[-1])
        for k in range(flat.shape[0]):
            for c in range(0, part.shape[-1], D):
                v = flat[k, :, c : c + D].astype(F32)
                acc = acc + jnp.sum((v * v).reshape(CHUNK // 8, 8, D), axis=0)
    return acc[:, 0:128] + acc[:, 128:256] + acc[:, 256:384]


def wide_squares_kernel(*refs):
    refs[-1][...] = squares_of(refs[:-1])


def squares_kernel(place, *refs):
    parts, (vgrad, before, out) = refs[:-3], refs[-3:]
    acc = squares_of(parts) + before[...]
    row = iota((16, 128), 0)
    low_row = 6 * place[0]
    mine = (row >= low_row) & (row < low_row + 6)
    for j in range(3):
        v = jnp.where(mine, vgrad[16 * j : 16 * j + 16, :].astype(F32), 0.0)
        v = v * v
        acc = acc + (v[0:8] + v[8:16])
    out[...] = acc


def squares(place, parts, vgrad=None, before=None, after=()):
    ins = [(0, p) for p in parts]
    kernel = wide_squares_kernel
    if before is not None:
        ins = [(1, place)] + ins + [(0, vgrad), (0, before)]
        kernel = squares_kernel
    return call(kernel, ins, [((8, 128), F32)], name="squares", vmem=4, after=after)[0]


def merge_kernel(place, igrad, other, out, flag):
    flag[...] = jnp.zeros((8, 128), F32)

    @pl.when(place[0] == 0)
    def low_core():
        out[0:OFF, :] = igrad[0:OFF, :]
        out[OFF:WIN, :] = added(igrad[OFF:WIN, :], other[0 : WIN - OFF, :])
        out[WIN:SEQ, :] = other[WIN - OFF : WIN, :]

    @pl.when(place[0] != 0)
    def high_core():
        out[0:OFF, :] = other[0:OFF, :]
        out[OFF:WIN, :] = added(other[OFF:WIN, :], igrad[0 : WIN - OFF, :])
        out[WIN:SEQ, :] = igrad[WIN - OFF : WIN, :]


def merge(place, igrad, other, after):
    return call(
        merge_kernel,
        [(1, place), (0, igrad), (0, other)],
        [((SEQ, D), BF16), ((8, 128), F32)],
        name="merge",
        vmem=4,
        after=after,
    )


def adamw(parameter, first_state, second, clipped, rate):
    first_new = first_state + (1.0 - BETA_ONE) * clipped
    second_new = second + (1.0 - BETA_TWO) * clipped * clipped
    root = (1.0 - BETA_TWO**STEP) ** 0.5
    below = pl.reciprocal(second_new * lax.rsqrt(second_new) + ADAM_EPS * root)
    scale = rate * root / (1.0 - BETA_ONE**STEP)
    return parameter - scale * (first_new * below), first_new, second_new


def decay_kernel(w, m, v, pv, pm, pq, nw, nm, nv, npv, npm, npq):
    for ins, outs, rate in (
        ((w, m, v), (nw, nm, nv), LEARN_RATE),
        ((pv, pm, pq), (npv, npm, npq), VECTOR_RATE),
    ):
        for ref, out, scale in zip(ins, outs, (1.0 - rate * DECAY_RATE, BETA_ONE, BETA_TWO)):
            out[...] = ref[...] * scale


def decay(arrays, after):
    return call(
        decay_kernel,
        [(0, a) for a in arrays],
        [(a.shape, F32) for a in arrays],
        name="decay",
        vmem=4,
        after=after,
    )


def adamw_kernel(*refs):
    place = Place()
    sums, refs = refs[:2], refs[2:]
    (vgrad, w, m, v, pv, pm, pq), refs = refs[:7], refs[7:]
    wide, low, refs = refs[:4], refs[4:8], refs[8:]
    outs, (npv, npm, npq, norm), scrs, sems = refs[:4], refs[4:8], refs[8:12], refs[12]
    opt = place[0]
    total = sums[0][...] + sums[1][...]
    total = jnp.sum(jnp.sum(total, axis=1, keepdims=True), axis=0, keepdims=True)
    grad_norm = jnp.sqrt(total)
    factor = jnp.minimum(1.0, CLIP_NORM / (grad_norm + 1e-06))
    norm[...] = grad_norm
    for j in range(3):
        cols = slice(128 * j, 128 * j + 128)
        g = vgrad[16 * j : 16 * j + 16, :].astype(F32)
        g = jnp.where(opt == 0, g[0:6], g[6:12])
        a, b, c = adamw(pv[:, cols], pm[:, cols], pq[:, cols], g * factor, VECTOR_RATE)
        npv[:, cols] = a
        npm[:, cols] = b
        npq[:, cols] = c

    def block(grad, rows, cols):
        new = adamw(w[rows, cols], m[rows, cols], v[rows, cols], grad * factor, LEARN_RATE)
        for scr, value in zip(scrs, new + (new[0].astype(BF16),)):
            scr[rows, cols] = value

    def copies(r, i):
        rows = aligned(CHUNK * (place[1] ^ r) + i * 16, 16, 16)
        return [
            pltpu.make_async_copy(scr.at[rows, :], out.at[rows, :], sems.at[3 * r + i, j])
            for j, (scr, out) in enumerate(zip(scrs, outs))
        ]

    for r in range(4):

        def step(i, carry, r=r):
            rows = aligned(CHUNK * (place[1] ^ r) + i * 16, 16, 16)
            here = aligned(i * 16, 16, 16)
            for j in range(4):
                at = D * (place[3] ^ j)
                for p, start in enumerate((4 * D + FF, 4 * D)):
                    grad = wide[r][2 * j + p, here, :].astype(F32)
                    block(grad, rows, aligned(start + at, D, 128))
            for c in range(4):
                grad = low[r][here, D * c : D * c + D].astype(F32)
                block(grad, rows, slice(D * c, D * c + D))
            for copy in copies(r, i):
                copy.start()
            return carry

        lax.fori_loop(0, CHUNK // 16, step, 0)
    for r in range(4):

        def finish(i, carry, r=r):
            for copy in copies(r, i):
                copy.wait()
            return carry

        lax.fori_loop(0, CHUNK // 16, finish, 0)


def update(place, sums, vgrad, w, m, v, pv, pm, pq, parts):
    ins = tuple(sums) + (vgrad, w, m, v, pv, pm, pq) + tuple(parts)
    shapes = [(w.shape, F32)] * 3 + [(w.shape, BF16)] + [(pv.shape, F32)] * 3 + [((1, 1), F32)]
    return pl.pallas_call(
        adamw_kernel,
        out_shape=[jax.ShapeDtypeStruct(s, d) for s, d in shapes],
        in_specs=[VMEM] * len(ins),
        out_specs=[ANY] * 4 + [VMEM] * 4,
        scratch_shapes=[
            pltpu.VMEM(w.shape, F32),
            pltpu.VMEM(w.shape, F32),
            pltpu.VMEM(w.shape, F32),
            pltpu.VMEM(w.shape, BF16),
            pltpu.SemaphoreType.DMA((12, 4)),
        ],
        compiler_params=pltpu.CompilerParams(vmem_limit_bytes=16 << 20),
        cost_estimate=pl.CostEstimate(
            flops=4000000000, bytes_accessed=26 * w.size, transcendentals=0
        ),
        name="adamw",
    )(*ins)


def shards(
    n,
    tokens,
    lengths,
    query_index,
    doc_index,
    targets,
    weights,
    first_moment,
    second_moment,
    vectors,
    vec_first,
    vec_second,
):
    place = None
    scalars = jnp.concatenate([lengths.reshape(SEGS), query_index, doc_index, targets])
    groups = bit_groups(n)

    w_own, wo_own, wu_own, wd_own = cast(weights)
    w_other = pair(w_own)
    vectors_late, w_own = lax.optimization_barrier((vectors, w_own))
    v_other = pair(vectors_late)
    wo = (wo_own, pair(wo_own))
    wu = (wu_own, pair(wu_own))
    wd = (wd_own, pair(wd_own))

    proj, att, lse, segc, segr, ownc, ownr, wanted, marks, vec, wqkv = attend(
        place, scalars, (tokens, w_own, w_other, vectors, v_other)
    )
    xhat1, inv1, hlow, act, up_proj, xhat2, inv2, unit, uscale, wo, wu, wd = mlp(
        place, wanted, att, tokens, ownr, vec, wo + wu + wd
    )
    units, packed = pack(marks, unit, pair(unit))
    groups = bit_groups(n)
    order = [0]
    stack = packed
    for i, (shift, size) in enumerate(groups[1:] + groups[:1]):
        pieces = [stack] + [swap(stack, "dp", n, k << shift) for k in range(1, size)]
        order = [o | (k << shift) for k in range(size) for o in order]
        if i < len(groups) - 1:
            slope = slope_of(up_proj, [packed])
            stack = join(pieces, [slope]).reshape(-1, 2 * PAIRS, D + 128)
    decayed = decay(
        (weights, first_moment, second_moment, vectors, vec_first, vec_second), [packed]
    )
    dsec, dlow, keep, send, dsums = down_backward(
        n, order, place, wanted, units, ownc, uscale, (xhat2, inv2, act), vec, pieces,
        decayed,
    )
    other = pair(send)
    dup, ukeep, usend, usums = up_backward(place, dlow, slope, hlow, wd, [])
    down, go = pair_sum(1, keep, other, [dup])
    dother = swap(go, "dp", n, 1)
    up, go = pair_sum(2, ukeep, pair(usend), [down])
    uother = swap(go, "dp", n, 2)
    dfirst, datt, delta, okeep, osend, fsums = first_backward(
        place, dup, dsec, xhat1, inv1, att, vec, wu, wo, [up]
    )
    ins = (tokens, proj, datt, lse, delta, segc, segr)
    part0, keep0, send0, sums0 = heads_backward(0, place, ins, (), [])
    down, dsend, up, usend = wide_step((down, dother, up, uother), [part0])
    dother, uother = swap(dsend, "dp", n, 2), swap(usend, "dp", n, 1)
    part1, keep1, send1, sums1 = heads_backward(1, place, ins, (), [down])
    wide, go = wide_plane_sum(place, (down, dother, up, uother), [part1])
    wother = swap(go, "dp", n, 4)
    part2, keep, send, _ = heads_backward(
        2, place, ins,
        (okeep, osend, keep0, send0, keep1, send1, dsums, usums, fsums, sums0, sums1),
        [wide, part1],
    )
    wide, go = wide_half(wide, wother, [part2])
    send, wide, go = lax.optimization_barrier((send, wide, go))
    wother = swap(go, "dp", n, 8)
    other = pair(send)
    igrad = input_backward((part0, part1, part2), dfirst, wqkv, [wide])
    iother = pair(igrad)
    low = core_sum(keep, other, [igrad])
    low_got = trades(low, n, 0)
    wide = rest_sum(low_next(wide, wother, [low[0]]), n)
    wide_got = trades([wide] * 4, n, 2)
    low = low_plane_sum(low_got, [wide])
    other = swap(low, "dp", n, 4)
    wide = chain(wide_got, [low])
    wide = trades([wide] * 4, n, 0)
    low = low_next(low, other, [wide[0]])
    other = swap(low, "dp", n, 8)
    input_grad, flag = merge(place, igrad, iother, [low])
    low, vgrad = low_last(low, other, [flag])
    low, vgrad = rest_sum(low, n), rest_sum(vgrad, n)
    low = trades([low] * 4, n, 0)
    sums = squares(place, low, vgrad, squares(place, wide, after=[low[0]]))
    sums = (sums, pair(sums))
    pieces = tuple(wide) + tuple(low)
    nw, nm, nv, nlow, npv, npm, npq, norm = update(
        place, sums, vgrad, *decayed, pieces,
    )
    return (norm.reshape(()), input_grad, nw, nm, nv, nlow, npv, npm, npq)


def solution(mesh):
    rows = P("opt", None)
    in_specs = (P("dp", None), P("dp", None), P("dp"), P("dp"), P("dp")) + (rows,) * 6
    out_specs = (P(), P("dp", None)) + (rows,) * 7
    n = mesh.shape["dp"]
    return jax.shard_map(
        functools.partial(shards, n),
        mesh=mesh,
        in_specs=in_specs,
        out_specs=out_specs,
        check_vma=False,
    )
```

```python
import functools

import jax
import jax.numpy as jnp
from jax import lax
from jax.experimental import pallas as pl
from jax.experimental.pallas import tpu as pltpu
from jax.sharding import PartitionSpec as P

D = 384
HEADS = 12
HD = 32
FF = 1536
SEQ = 1024
SEGS = 16
PAIRS = 8
STEP = 10

WIN = 576
OFF = SEQ - WIN
PAD = 640
BLOCK = 128
BANDS = tuple((q, max(0, q - 128), min(WIN, q + 256)) for q in range(0, WIN, BLOCK))
BAND_ROWS = tuple(sum(b[2] - b[1] for b in BANDS[:i]) for i in range(len(BANDS) + 1))
ROWS = 64
WIDE_ROWS = 192
LOG2E = 1.4426950408889634

LN_EPS = 1e-06
POOL_EPS = 1e-06
SCORE_SCALE = 50.0
CLIP_NORM = 0.001
BETA_ONE = 0.9
BETA_TWO = 0.98
ADAM_EPS = 1e-08
LEARN_RATE = 0.05
VECTOR_RATE = 0.3
DECAY_RATE = 0.01
NEG_BIG = -1e30
HALF = D // 2
CHUNK = HALF // 4
EXP2_SCALE = HD ** (-0.5) * 1.4426950408889634

F32 = jnp.float32
BF16 = jnp.bfloat16
VMEM = pl.BlockSpec(memory_space=pltpu.VMEM)
SMEM = pl.BlockSpec(memory_space=pltpu.SMEM)
ANY = pl.BlockSpec(memory_space=pl.ANY)


def nn(a, b):
    return jnp.dot(a, b, preferred_element_type=F32)


def nt(a, b):
    return lax.dot_general(a, b, (((1,), (1,)), ((), ())), preferred_element_type=F32)


def tn(a, b):
    return lax.dot_general(a, b, (((0,), (0,)), ((), ())), preferred_element_type=F32)


def exact(a, b, dims):
    return lax.dot_general(
        a, b, (dims, ((), ())), precision=lax.Precision.HIGHEST, preferred_element_type=F32
    )


def iota(shape, axis):
    return lax.broadcasted_iota(jnp.int32, shape, axis)


def low_pair(value):
    high = value.astype(BF16)
    return high, (value - high.astype(F32)).astype(BF16)


def aligned(start, size, unit):
    return pl.ds(pl.multiple_of(start, unit), size)


def assemble(dst, own, other, opt):
    dst[aligned(HALF * opt, HALF, 64), :] = own[0:HALF, :]
    dst[aligned(HALF * (1 - opt), HALF, 64), :] = other[0:HALF, :]


class Place:
    def __getitem__(self, i):
        if i == 0:
            return lax.axis_index("opt")
        me = lax.axis_index("dp")
        return (me & 3, me, (me >> 2) & 3)[i - 1]


def call(kernel, ins, outs, scratch=(), micros=5, name=None, vmem=12, after=()):
    if ins[0][1] is None:
        kernel = functools.partial(kernel, Place())
        ins = ins[1:]
    specs = [SMEM if s else VMEM for s, _ in ins] + [ANY] * len(after)
    count = len(ins)

    def body(*refs):
        kernel(*refs[:count], *refs[count + len(after) :])

    shapes = [jax.ShapeDtypeStruct(s, d) for s, d in outs]
    moved = sum(a.size * a.dtype.itemsize for _, a in ins)
    moved += sum(s.size * s.dtype.itemsize for s in shapes)
    return pl.pallas_call(
        body,
        out_shape=shapes,
        in_specs=specs,
        out_specs=[VMEM] * len(shapes),
        scratch_shapes=list(scratch),
        compiler_params=pltpu.CompilerParams(vmem_limit_bytes=vmem << 20),
        cost_estimate=pl.CostEstimate(
            flops=micros * 1100000000, bytes_accessed=moved, transcendentals=0
        ),
        name=name,
    )(*[a for _, a in ins], *after)


def head_stack(rows):
    lane_head = iota(rows.shape, 1) // HD
    zero = jnp.zeros_like(rows)
    return jnp.concatenate([jnp.where(lane_head == j, rows, zero) for j in range(4)], axis=0)


def attend_kernel(
    place, scalars, tokens, w_own, w_other, v_own, v_other,
    proj, att, lse, segc, segr, ownc, ownr, wanted, marks, vec, wfull, bias, vt,
):
    opt = place[0]
    assemble(wfull, w_own, w_other, opt)
    mine = v_own[...].astype(BF16).astype(F32)
    others = v_other[...].astype(BF16).astype(F32)
    first = opt == 0
    vec[0:6, :] = jnp.where(first, mine, others)
    vec[6:12, :] = jnp.where(first, others, mine)
    vec[12:16, :] = jnp.zeros((4, D), F32)

    position = iota((8, PAD), 1) + OFF * opt
    segment = jnp.zeros((8, PAD), jnp.int32)
    bound = jnp.int32(0)
    low_count = jnp.int32(0)
    for s in range(SEGS):
        bound = bound + scalars[s]
        segment = segment + (position >= bound).astype(jnp.int32)
        low_count = low_count + (bound <= WIN).astype(jnp.int32)
    mine = (segment < low_count).astype(jnp.int32) == (opt == 0).astype(jnp.int32)
    owned = jnp.where(mine, segment, -1)
    segr[...] = segment
    ownr[...] = owned
    for value, out in ((segment, segc), (owned, ownc)):
        value = value.astype(F32)
        for t in range(PAD // 128):
            rows = min(128, WIN - 128 * t)
            turned = jnp.broadcast_to(value[0:1, 128 * t : 128 * t + 128], (128, 128)).T
            out[128 * t : 128 * t + rows, :] = turned[0:rows].astype(jnp.int32)
    row, col = iota((2 * PAIRS, 128), 0), iota((2 * PAIRS, 128), 1)
    by_row = jnp.zeros((2 * PAIRS, 128), jnp.int32)
    by_col = jnp.zeros((2 * PAIRS, 128), jnp.int32)
    mark = jnp.zeros((2 * PAIRS, 128), jnp.int32)
    for j in range(PAIRS):
        mark = jnp.where(row == j, scalars[SEGS + 2 * PAIRS + j], mark)
        for at in (j, PAIRS + j):
            by_row = jnp.where(row == at, scalars[SEGS + at], by_row)
            by_col = jnp.where(col == at, scalars[SEGS + at], by_col)
    wanted[0] = by_row
    wanted[1] = by_col
    marks[...] = jnp.where(col < 64, mark >> 5, mark & 31).astype(F32).astype(BF16)
    for i, (q0, k0, k1) in enumerate(BANDS):
        bias[BAND_ROWS[i] : BAND_ROWS[i + 1], :] = jnp.where(
            segc[k0:k1, :] == segr[0:1, q0 : q0 + BLOCK], 0.0, NEG_BIG
        )

    x = tokens[aligned(OFF * opt, WIN, 64), :]
    bias_row = jnp.concatenate([vec[0:1, :], jnp.zeros((1, D), F32), vec[1:2, :]], axis=1)
    for first in range(0, 3 * D, 512):
        cols = slice(first, min(first + 512, 3 * D))
        proj[0:WIN, cols] = (nn(x, wfull[:, cols]) + bias_row[:, cols]).astype(BF16)
    proj[WIN:PAD, :] = jnp.zeros((PAD - WIN, 3 * D), BF16)

    def group(g, carry):
        def lanes(part):
            return aligned(part * D + 128 * g, 128, 128)

        for t in range(PAD // 128):
            vt[:, 128 * t : 128 * t + 128] = (
                proj[128 * t : 128 * t + 128, lanes(2)].astype(F32).T.astype(BF16)
            )
        def scores(i):
            q0, k0, k1 = BANDS[i]
            return nt(proj[k0:k1, lanes(1)], head_stack(proj[q0 : q0 + BLOCK, lanes(0)]))

        coming = scores(0)
        for i, (q0, k0, k1) in enumerate(BANDS):
            st = coming
            if i + 1 < len(BANDS):
                coming = scores(i + 1)
            outs, probs, totals = [], [], []
            for j in range(4):
                t = (
                    st[:, j * BLOCK : (j + 1) * BLOCK] * EXP2_SCALE
                    + bias[BAND_ROWS[i] : BAND_ROWS[i + 1], :]
                )
                peak = jnp.max(t, axis=0, keepdims=True)
                powers = jnp.exp2(t - peak)
                total = jnp.sum(powers, axis=0, keepdims=True)
                lse[g, j : j + 1, q0 : q0 + BLOCK] = peak + jnp.log2(total)
                probs.append(powers.astype(BF16))
                totals.append(1.0 / total)
                if j % 2 == 1:
                    o = nn(vt[(j - 1) * HD : (j + 1) * HD, k0:k1], jnp.concatenate(probs[-2:], axis=1))
                    outs.append(o[0:HD, 0:BLOCK] * totals[-2])
                    outs.append(o[HD : 2 * HD, BLOCK : 2 * BLOCK] * totals[-1])
            rows = min(BLOCK, WIN - q0)
            att[q0 : q0 + rows, aligned(128 * g, 128, 128)] = (
                jnp.concatenate(outs, axis=0).T[0:rows].astype(BF16)
            )
        return carry

    lax.fori_loop(0, 3, group, 0)


def attend(place, scalars, arrays):
    return call(
        attend_kernel,
        [(1, place), (1, scalars)] + [(0, a) for a in arrays],
        [
            ((PAD, 3 * D), BF16),
            ((WIN, D), BF16),
            ((3, 4, PAD), F32),
            ((WIN, 128), jnp.int32),
            ((8, PAD), jnp.int32),
            ((WIN, 128), jnp.int32),
            ((8, PAD), jnp.int32),
            ((2, 2 * PAIRS, 128), jnp.int32),
            ((2 * PAIRS, 128), BF16),
            ((16, D), F32),
            ((D, 3 * D), BF16),
        ],
        [
            pltpu.VMEM((BAND_ROWS[-1], 128), F32),
            pltpu.VMEM((128, PAD), BF16),
        ],
        micros=8,
        name="attend",
    )


def cast_kernel(weights, wq, wo, wu, wd, buffer, sems):
    spans = [(wq, 3 * D), (wo, D), (wu, FF), (wd, FF)]
    copies = [
        pltpu.make_async_copy(
            weights.at[:, i * D : (i + 1) * D], buffer.at[:, i * D : (i + 1) * D], sems.at[i]
        )
        for i in range(12)
    ]
    for copy in copies:
        copy.start()
    at = 0
    for out, width in spans:
        for part in range(width // D):
            copies[at].wait()
            out[:, part * D : (part + 1) * D] = buffer[:, at * D : (at + 1) * D].astype(BF16)
            at += 1


def cast(weights):
    return pl.pallas_call(
        cast_kernel,
        out_shape=[jax.ShapeDtypeStruct((HALF, c), BF16) for c in (3 * D, D, FF, FF)],
        in_specs=[ANY],
        out_specs=[VMEM] * 4,
        scratch_shapes=[pltpu.VMEM(weights.shape, F32), pltpu.SemaphoreType.DMA((12,))],
        compiler_params=pltpu.CompilerParams(vmem_limit_bytes=52 << 20),
        name="cast",
    )(weights)


def bias_of(vec, c):
    first, last = 256 * c, 256 * c + 256
    parts = []
    while first < last:
        row, col = divmod(first, D)
        size = min(D - col, last - first)
        parts.append(vec[3 + row : 4 + row, col : col + size])
        first += size
    return parts[0] if len(parts) == 1 else jnp.concatenate(parts, axis=1)


def mlp_kernel(
    place, wanted, att, tokens, ownr, vec, wo_own, wo_other, wu_own, wu_other,
    wd_own, wd_other, xhat1, inv1, hlow, act, up_proj, xhat2, inv2, unit, uscale, wo, wu, wd,
    ench, encl,
):
    opt = place[0]
    assemble(wo, wo_own, wo_other, opt)
    assemble(wu, wu_own, wu_other, opt)
    assemble(wd, wd_own, wd_other, opt)

    def norm(v):
        centred = v - jnp.mean(v, axis=1, keepdims=True)
        inverse = lax.rsqrt(jnp.mean(centred * centred, axis=1, keepdims=True) + LN_EPS)
        return centred * inverse, inverse

    def block(i, carry):
        r = aligned(i * WIDE_ROWS, WIDE_ROWS, 64)
        x = tokens[aligned(OFF * opt + i * WIDE_ROWS, WIDE_ROWS, 64), :].astype(F32)
        normed, inverse = norm(nn(att[r, :], wo[...]) + vec[2:3, :] + x)
        xhat1[r, :] = normed
        inv1[r, :] = jnp.broadcast_to(inverse, (WIDE_ROWS, 128))
        h = normed * vec[8:9, :] + vec[9:10, :]
        low = h.astype(BF16)
        hlow[r, :] = low
        coming = nn(low, wu[:, 0:256])
        for c in range(6):
            cols = slice(c * 256, (c + 1) * 256)
            u = coming + bias_of(vec, c)
            if c < 5:
                coming = nn(low, wu[:, (c + 1) * 256 : (c + 2) * 256])
            up_proj[r, cols] = u
            half = lax.erf(u * 0.7071067811865476) * 0.5 + 0.5
            act[r, cols] = (u * half).astype(BF16)
        normed, inverse = norm(nt(act[r, :], wd[...]) + vec[7:8, :] + h)
        xhat2[r, :] = normed
        inv2[r, :] = jnp.broadcast_to(inverse, (WIDE_ROWS, 128))
        high, rest = low_pair(normed * vec[10:11, :] + vec[11:12, :])
        ench[r, :] = high
        encl[r, :] = rest
        return carry

    lax.fori_loop(0, WIN // WIDE_ROWS, block, 0)

    onehot = jnp.where(wanted[0, :, 0:1] == ownr[0:1, 0:WIN], 1.0, 0.0)
    count = jnp.maximum(jnp.sum(onehot, axis=1, keepdims=True), 1.0)
    hot = onehot.astype(BF16)
    pooled = (nn(hot, ench[...]) + nn(hot, encl[...])) / count
    inverse_len = lax.rsqrt(jnp.sum(pooled * pooled, axis=1, keepdims=True) + POOL_EPS)
    unit[...] = pooled * inverse_len
    uscale[...] = jnp.broadcast_to(inverse_len / count, (2 * PAIRS, 128))


def slope_kernel(up_proj, out):
    def block(i, carry):
        r = aligned(i * 16, 16, 16)
        u = up_proj[r, :]
        half = lax.erf(u * 0.7071067811865476) * 0.5 + 0.5
        out[r, :] = half + u * jnp.exp2(u * u * (-0.5 * LOG2E)) * 0.3989422804014327
        return carry

    lax.fori_loop(0, WIN // 16, block, 0)


def slope_of(up_proj, after):
    return call(slope_kernel, [(0, up_proj)], [(up_proj.shape, F32)], name="slope", vmem=4, after=after)[0]


def mlp(place, wanted, att, tokens, ownr, vec, halves):
    return call(
        mlp_kernel,
        [(1, place), (0, wanted), (0, att), (0, tokens), (0, ownr), (0, vec)]
        + [(0, h) for h in halves],
        [
            ((WIN, D), F32),
            ((WIN, 128), F32),
            ((WIN, D), BF16),
            ((WIN, FF), BF16),
            ((WIN, FF), F32),
            ((WIN, D), F32),
            ((WIN, 128), F32),
            ((2 * PAIRS, D), F32),
            ((2 * PAIRS, 128), F32),
            ((D, D), BF16),
            ((D, FF), BF16),
            ((D, FF), BF16),
        ],
        [
            pltpu.VMEM((WIN, D), BF16),
            pltpu.VMEM((WIN, D), BF16),
        ],
        micros=10,
        name="mlp",
    )


def split_rows(grad, keep, send, place, *at):
    opt = place[0]
    for c in range(4):
        index = (c ^ place[1],) + at
        keep[index] = grad[aligned(HALF * opt + CHUNK * c, CHUNK, 16), :].astype(BF16)
        send[index] = grad[aligned(HALF * (1 - opt) + CHUNK * c, CHUNK, 16), :].astype(BF16)


def column_sums(value):
    return jnp.sum(value.reshape(-1, 8, D), axis=0)


def norm_backward(grad_at, normed_ref, inverse_ref, gain, out, low_out, sums, at, step=ROWS):
    def block(i, carry):
        scale_sum, shift_sum, bias_sum = carry
        r = aligned(i * step, step, 64)
        g = grad_at(r)
        normed = normed_ref[r, :]
        scaled = g * gain
        inner = (
            scaled
            - jnp.mean(scaled, axis=1, keepdims=True)
            - normed * jnp.mean(scaled * normed, axis=1, keepdims=True)
        ) * inverse_ref[r, 0:1]
        out[r, :] = inner
        low_out[r, :] = inner.astype(BF16)
        return (
            scale_sum + column_sums(g * normed),
            shift_sum + column_sums(g),
            bias_sum + column_sums(inner),
        )

    zero = jnp.zeros((8, D), F32)
    scale_sum, shift_sum, bias_sum = lax.fori_loop(0, WIN // step, block, (zero, zero, zero))
    sums[at : at + 1, :] = jnp.sum(bias_sum, axis=0, keepdims=True)
    sums[at + 1 : at + 2, :] = jnp.sum(scale_sum, axis=0, keepdims=True)
    sums[at + 2 : at + 3, :] = jnp.sum(shift_sum, axis=0, keepdims=True)


def down_kernel(
    place, count, order, wanted, units, ownc, uscale, xhat2, inv2, act, vec, *rest
):
    pieces, (dsec, dlow, keep, send, sums, queries, docs, marks, grad) = rest[:-9], rest[-9:]
    me = place[2]
    per = pieces[0].shape[0]
    for p, piece in enumerate(pieces):
        for j in range(per):
            at = order[p * per + j]
            r = slice(at * PAIRS, (at + 1) * PAIRS)
            both = piece[j].astype(F32)
            queries[r, :] = both[0:PAIRS, 0:D]
            docs[r, :] = both[PAIRS : 2 * PAIRS, 0:D]
            marks[r, :] = both[0:PAIRS, D : D + 128]
    total = count * PAIRS
    q = queries[...].astype(BF16)
    d = docs[...].astype(BF16)
    logits = SCORE_SCALE * nt(q, d)
    peak = jnp.max(logits, axis=1, keepdims=True)
    powers = jnp.exp(logits - peak)
    soft = powers / jnp.sum(powers, axis=1, keepdims=True)
    col = iota((total, total), 1)
    doc_id = ((col // PAIRS) ^ me) * PAIRS + lax.rem(col, PAIRS)
    hit = (marks[:, 0:1] * 32.0 + marks[:, 64:65]).astype(jnp.int32) == doc_id
    d_logits = (soft - jnp.where(hit, 1.0, 0.0)) * (SCORE_SCALE / total)
    high, rest_low = low_pair(d_logits[0:PAIRS, :])
    d_q = nn(high, d) + nn(rest_low, d)
    high, rest_low = low_pair(d_logits[:, 0:128].T[0:PAIRS, :])
    d_d = nn(high, q) + nn(rest_low, q)
    d_units = jnp.concatenate([d_q, d_d], axis=0)
    u = units[...]
    d_pool = uscale[:, 0:1] * (d_units - u * jnp.sum(u * d_units, axis=1, keepdims=True))
    hot = jnp.where(ownc[:, 0 : 2 * PAIRS] == wanted[1, 0:1, 0 : 2 * PAIRS], 1.0, 0.0).astype(BF16)
    high, rest_low = low_pair(d_pool)
    dsec[...] = nn(hot, high) + nn(hot, rest_low)
    norm_backward(lambda r: dsec[r, :], xhat2, inv2, vec[10:11, :], dsec, dlow, sums, 0)
    sums[3:8, :] = jnp.zeros((5, D), F32)
    for c in range(3):
        cols = slice(c * 512, (c + 1) * 512)
        grad[:, cols] = tn(dlow[...], act[:, cols])
    for c in range(4):
        split_rows(grad.at[:, c * D : (c + 1) * D], keep, send, place, c)


def down_backward(count, order, place, wanted, units, ownc, uscale, saved, vec, pieces, after):
    total = count * PAIRS
    return call(
        lambda place, *refs: down_kernel(place, count, order, *refs),
        [(1, place), (0, wanted), (0, units), (0, ownc), (0, uscale)]
        + [(0, s) for s in saved]
        + [(0, vec)]
        + [(0, p) for p in pieces],
        [
            ((WIN, D), F32),
            ((WIN, D), BF16),
            ((4, 4, CHUNK, D), BF16),
            ((4, 4, CHUNK, D), BF16),
            ((8, D), F32),
        ],
        [
            pltpu.VMEM((total, D), F32),
            pltpu.VMEM((total, D), F32),
            pltpu.VMEM((total, 128), F32),
            pltpu.VMEM((D, FF), F32),
        ],
        micros=4,
        name="down_backward",
        after=after,
    )


def up_kernel(place, dlow, slope, hlow, wd, dup, keep, send, sums, grad):
    coming = nn(dlow[...], wd[:, 0:512])
    for c in range(3):
        cols = slice(c * 512, (c + 1) * 512)
        part = (coming * slope[:, cols]).astype(BF16)
        if c < 2:
            coming = nn(dlow[...], wd[:, (c + 1) * 512 : (c + 2) * 512])
        dup[:, cols] = part
        column_sum = jnp.sum(part.astype(F32), axis=0, keepdims=True)
        for j in range(4):
            at = 512 * c + 128 * j
            sums[at // D : at // D + 1, at % D : at % D + 128] = column_sum[:, 128 * j : 128 * j + 128]
        grad[:, cols] = tn(hlow[...], dup[:, cols])
    for c in range(4):
        split_rows(grad.at[:, c * D : (c + 1) * D], keep, send, place, c)


def up_backward(place, dlow, slope, hlow, wd, after):
    return call(
        up_kernel,
        [(1, place)] + [(0, a) for a in (dlow, slope, hlow, wd)],
        [((WIN, FF), BF16), ((4, 4, CHUNK, D), BF16), ((4, 4, CHUNK, D), BF16), ((4, D), F32)],
        [pltpu.VMEM((D, FF), F32)],
        micros=3,
        name="up_backward",
        after=after,
    )


def first_kernel(
    place, dup, dsec, xhat1, inv1, att, vec, wu, wo,
    dfirst, datt, delta, okeep, osend, sums, grad, dlow,
):
    steps = [slice(i, i + WIDE_ROWS) for i in range(0, WIN, WIDE_ROWS)]
    coming = nt(dup[steps[0], :], wu[...])
    gain = vec[8:9, :]
    totals = None
    for i, r in enumerate(steps):
        g = coming + dsec[r, :]
        if i + 1 < len(steps):
            coming = nt(dup[steps[i + 1], :], wu[...])
        normed = xhat1[r, :]
        scaled = g * gain
        inner = (
            scaled
            - jnp.mean(scaled, axis=1, keepdims=True)
            - normed * jnp.mean(scaled * normed, axis=1, keepdims=True)
        ) * inv1[r, 0:1]
        dfirst[r, :] = inner
        dlow[r, :] = inner.astype(BF16)
        new = [column_sums(inner), column_sums(g * normed), column_sums(g)]
        totals = new if totals is None else [a + b for a, b in zip(totals, new)]
    for i, total in enumerate(totals):
        sums[i : i + 1, :] = jnp.sum(total, axis=0, keepdims=True)
    sums[3:8, :] = jnp.zeros((5, D), F32)
    grad[...] = tn(att[...], dlow[...])
    split_rows(grad, okeep, osend, place)
    da = nt(dlow[...], wo[...]).astype(BF16)
    datt[0:WIN, :] = da
    datt[WIN:PAD, :] = jnp.zeros((PAD - WIN, D), BF16)
    high, rest = low_pair(da.astype(F32) * att[...].astype(F32))
    heads = (iota((16, D), 1) // HD == iota((16, D), 0)).astype(F32).astype(BF16)
    delta[:, 0:WIN] = nt(heads, high) + nt(heads, rest)
    delta[:, WIN:PAD] = jnp.zeros((16, PAD - WIN), F32)


def first_backward(place, dup, dsec, xhat1, inv1, att, vec, wu, wo, after):
    return call(
        first_kernel,
        [(1, place)] + [(0, a) for a in (dup, dsec, xhat1, inv1, att, vec, wu, wo)],
        [
            ((WIN, D), F32),
            ((PAD, D), BF16),
            ((16, PAD), F32),
            ((4, CHUNK, D), BF16),
            ((4, CHUNK, D), BF16),
            ((8, D), F32),
        ],
        [
            pltpu.VMEM((D, D), F32),
            pltpu.VMEM((WIN, D), BF16),
        ],
        micros=1,
        name="first_backward",
        after=after,
    )


def heads_kernel(place, g, tokens, proj, datt, lse, delta, segc, segr, *rest):
    rest, (dproj, keep, send, sums, kt, dk, dv, grad, ktmp, stmp) = rest[:-10], rest[-10:]

    def lanes(part):
        return slice(part * D + 128 * g, part * D + 128 * g + 128)

    for t in range(PAD // 128):
        kt[:, 128 * t : 128 * t + 128] = (
            proj[128 * t : 128 * t + 128, lanes(1)].astype(F32).T.astype(BF16)
        )
    dk[...] = jnp.zeros_like(dk)
    dv[...] = jnp.zeros_like(dv)

    def products(i):
        q0, k0, k1 = BANDS[i]
        qs = head_stack(proj[q0 : q0 + BLOCK, lanes(0)])
        gs = head_stack(datt[q0 : q0 + BLOCK, lanes(0)])
        return qs, gs, nt(proj[k0:k1, lanes(1)], qs), nt(proj[k0:k1, lanes(2)], gs)

    coming = products(0)
    for i, (q0, k0, k1) in enumerate(BANDS):
        qs, gs, st, dp = coming
        if i + 1 < len(BANDS):
            coming = products(i + 1)
        same = segc[k0:k1, :] == segr[0:1, q0 : q0 + BLOCK]
        bias = jnp.where(same, 0.0, NEG_BIG)
        probs, d_scores, dq = [], [], []
        for j in range(4):
            cols = slice(j * BLOCK, (j + 1) * BLOCK)
            prob = jnp.exp2(st[:, cols] * EXP2_SCALE + bias - lse[g, j : j + 1, q0 : q0 + BLOCK])
            ds = prob * (dp[:, cols] - delta[4 * g + j : 4 * g + j + 1, q0 : q0 + BLOCK])
            ds = ds.astype(BF16)
            probs.append(prob.astype(BF16))
            d_scores.append(ds)
            if j % 2 == 1:
                part = nn(
                    kt[(j - 1) * HD : (j + 1) * HD, k0:k1], jnp.concatenate(d_scores[-2:], axis=1)
                )
                dq.append(part[0:HD, 0:BLOCK])
                dq.append(part[HD : 2 * HD, BLOCK : 2 * BLOCK])
        dv[k0:k1, :] += nn(jnp.concatenate(probs, axis=1), gs)
        dk[k0:k1, :] += nn(jnp.concatenate(d_scores, axis=1), qs)
        rows = min(BLOCK, WIN - q0)
        dqs = jnp.concatenate(dq, axis=0).T[0:rows] * HD ** (-0.5)
        dproj[q0 : q0 + rows, 0:128] = dqs.astype(BF16)
    dproj[:, 128:256] = (dk[...] * HD ** (-0.5)).astype(BF16)
    dproj[:, 256:384] = dv[...].astype(BF16)
    grad[...] = tn(tokens[aligned(OFF * place[0], WIN, 64), :], dproj[...])
    q_sum = jnp.sum(dproj[:, 0:128].astype(F32), axis=0, keepdims=True)
    v_sum = jnp.sum(dproj[:, 256:384].astype(F32), axis=0, keepdims=True)
    sums[0:1, :] = q_sum
    sums[1:2, :] = v_sum
    sums[2:8, :] = jnp.zeros((6, 128), F32)
    if g < 2:
        split_rows(grad, keep, send, place)
        return
    parts, (dsums, usums, fsums, zero, one) = rest[:6], rest[6:]
    split_rows(grad, ktmp, stmp, place)
    for dst, out_part, blocks in (
        (keep, parts[0], (parts[2], parts[4], ktmp)),
        (send, parts[1], (parts[3], parts[5], stmp)),
    ):
        dst[:, :, 3 * D : 4 * D] = out_part[...]
        for h, part in enumerate(blocks):
            for c in range(3):
                dst[:, :, D * c + 128 * h : D * c + 128 * h + 128] = part[
                    :, :, 128 * c : 128 * c + 128
                ]
    rows = jnp.concatenate(
        [
            jnp.concatenate([zero[0:1], one[0:1], q_sum], axis=1),
            jnp.concatenate([zero[1:2], one[1:2], v_sum], axis=1),
            fsums[0:1, :],
            usums[0:4, :],
            dsums[0:1, :],
            fsums[1:3, :],
            dsums[1:3, :],
            jnp.zeros((4, D), F32),
        ],
        axis=0,
    ).astype(BF16)
    for c in range(4):
        for j in range(3):
            block = rows[:, 128 * j : 128 * j + 128]
            keep[c, 16 * j : 16 * j + 16, 4 * D : 4 * D + 128] = block
            send[c, 16 * j : 16 * j + 16, 4 * D : 4 * D + 128] = block


def heads_backward(g, place, ins, more, after):
    part = ((4, CHUNK, 4 * D + 128 if g == 2 else D), BF16)
    return call(
        lambda place, *refs: heads_kernel(place, g, *refs),
        [(1, place)] + [(0, a) for a in tuple(ins) + tuple(more)],
        [((WIN, D), BF16), part, part, ((8, 128), F32)],
        [
            pltpu.VMEM((128, PAD), BF16),
            pltpu.VMEM((WIN, 128), F32),
            pltpu.VMEM((WIN, 128), F32),
            pltpu.VMEM((D, D), F32),
            pltpu.VMEM((4, CHUNK, D), BF16),
            pltpu.VMEM((4, CHUNK, D), BF16),
        ],
        micros=1,
        name="heads_backward",
        after=after,
    )


def input_kernel(dp0, dp1, dp2, dfirst, wfull, igrad, dproj):
    for g, part in enumerate((dp0, dp1, dp2)):
        for c in range(3):
            dproj[:, c * D + 128 * g : c * D + 128 * g + 128] = part[:, 128 * c : 128 * c + 128]
    igrad[...] = (nt(dproj[...], wfull[...]) + dfirst[...]).astype(BF16)


def input_backward(parts, dfirst, wqkv, after):
    return call(
        input_kernel,
        [(0, a) for a in tuple(parts) + (dfirst, wqkv)],
        [((WIN, D), BF16)],
        [pltpu.VMEM((WIN, 3 * D), BF16)],
        micros=2,
        name="input_backward",
        after=after,
    )[0]


def flips(axis, size, bits):
    return [(i, i ^ bits) for i in range(size)]


def pair(value):
    return swap(value, "opt", 2, 1)


def swap(value, axis, size, bits):
    return lax.ppermute(value, axis, flips(axis, size, bits))


def bit_groups(size):
    bits = size.bit_length() - 1
    return [(s, 1 << min(2, bits - s)) for s in range(0, bits, 2)]


def trades(values, n, shift):
    return [values[0]] + [swap(values[k], "dp", n, k << shift) for k in (1, 2, 3)]


def added(a, b):
    return (a.astype(F32) + b.astype(F32)).astype(BF16)


def core_sum_kernel(keep, other, *outs):
    for r, out in enumerate(outs):
        out[...] = added(keep[r], other[r])


def core_sum(keep, other, after):
    return call(
        core_sum_kernel,
        [(0, keep), (0, other)],
        [(keep.shape[1:], BF16)] * 4,
        name="core_sum",
        vmem=4,
        after=after,
    )


def pair_sum_kernel(bit, keep, other, stay, go):
    for i, r in enumerate((0, 3 - bit)):
        stay[i] = added(keep[r], other[r])
        go[i] = added(keep[r + bit], other[r + bit])


def pair_sum(bit, keep, other, after):
    return call(
        functools.partial(pair_sum_kernel, bit),
        [(0, keep), (0, other)],
        [((2,) + keep.shape[1:], BF16)] * 2,
        name="pair_sum",
        vmem=4,
        after=after,
    )


def wide_step_kernel(down, dother, up, uother, dkeep, dsend, ukeep, usend):
    dkeep[...] = added(down[0], dother[0])
    dsend[...] = added(down[1], dother[1])
    ukeep[...] = added(up[0], uother[0])
    usend[...] = added(up[1], uother[1])


def wide_step(parts, after):
    return call(
        wide_step_kernel,
        [(0, p) for p in parts],
        [((4, CHUNK, D), BF16)] * 4,
        name="wide_step",
        vmem=4,
        after=after,
    )


def total_of(refs, at):
    a, b, c, d = (ref[at].astype(F32) for ref in refs)
    return ((a + b) + (c + d)).astype(BF16)


def wide_plane_kernel(place, down, dother, up, uother, *outs):
    for k, out in enumerate(outs):
        at = place[3] ^ k
        out[0] = added(down[at], dother[at])
        out[1] = added(up[at], uother[at])


def wide_plane_sum(place, parts, after):
    return call(
        wide_plane_kernel,
        [(1, place)] + [(0, p) for p in parts],
        [((2, CHUNK, D), BF16)] * 4,
        name="wide_plane_sum",
        vmem=4,
        after=after,
    )


def low_plane_kernel(a, b, c, d, out):
    out[...] = total_of((a, b, c, d), slice(None))


def low_plane_sum(parts, after=()):
    return call(
        low_plane_kernel,
        [(0, p) for p in parts],
        [(parts[0].shape, BF16)],
        name="low_plane_sum",
        vmem=4,
        after=after,
    )[0]


def low_next_kernel(keep, other, out):
    out[...] = added(keep[...], other[...])


def low_next(keep, other, after=()):
    return call(
        low_next_kernel,
        [(0, keep), (0, other)],
        [(keep.shape, BF16)],
        name="low_next",
        vmem=4,
        after=after,
    )[0]


def low_last_kernel(keep, other, out, vgrad):
    out[...] = added(keep[:, 0 : 4 * D], other[:, 0 : 4 * D])
    vgrad[...] = added(keep[:, 4 * D : 4 * D + 128], other[:, 4 * D : 4 * D + 128])


def low_last(keep, other, after):
    return call(
        low_last_kernel,
        [(0, keep), (0, other)],
        [((CHUNK, 4 * D), BF16), ((CHUNK, 128), BF16)],
        name="low_last",
        vmem=4,
        after=after,
    )


def chain_kernel(*refs):
    ins, out = refs[:-1], refs[-1]
    at = 0
    for ref in ins:
        flat = ref.reshape(-1, CHUNK, D)
        out[at : at + flat.shape[0]] = flat[...]
        at += flat.shape[0]


def chain(parts, after=()):
    count = sum(p.size for p in parts) // (CHUNK * D)
    return call(
        chain_kernel,
        [(0, p) for p in parts],
        [((count, CHUNK, D), BF16)],
        name="chain",
        vmem=4,
        after=after,
    )[0]


def rest_sum(value, n):
    bit = 16
    while bit < n:
        other = swap(value, "dp", n, bit)
        value = (value.astype(F32) + other.astype(F32)).astype(BF16)
        bit *= 2
    return value


def join_kernel(*refs):
    ins, out = refs[:-1], refs[-1]
    for i, ref in enumerate(ins):
        out[i] = ref[...]


def join(parts, after=()):
    return call(
        join_kernel,
        [(0, p) for p in parts],
        [((len(parts),) + parts[0].shape, parts[0].dtype)],
        name="join",
        vmem=4,
        after=after,
    )[0]


def pack_kernel(marks, unit, other, units, packed):
    both = unit[...] + other[...]
    units[...] = both
    packed[:, 0:D] = both.astype(BF16)
    packed[:, D : D + 128] = marks[...]


def pack(marks, unit, other):
    return call(
        pack_kernel,
        [(0, marks), (0, unit), (0, other)],
        [(unit.shape, F32), ((2 * PAIRS, D + 128), BF16)],
        name="pack",
        vmem=4,
    )


def squares_of(parts):
    acc = jnp.zeros((8, D), F32)
    for part in parts:
        flat = part.reshape(-1, CHUNK, part.shape[-1])
        for k in range(flat.shape[0]):
            for c in range(0, part.shape[-1], D):
                v = flat[k, :, c : c + D].astype(F32)
                acc = acc + jnp.sum((v * v).reshape(CHUNK // 8, 8, D), axis=0)
    return acc[:, 0:128] + acc[:, 128:256] + acc[:, 256:384]


def wide_squares_kernel(*refs):
    refs[-1][...] = squares_of(refs[:-1])


def squares_kernel(place, *refs):
    parts, (vgrad, before, out) = refs[:-3], refs[-3:]
    acc = squares_of(parts) + before[...]
    row = iota((16, 128), 0)
    low_row = 6 * place[0]
    mine = (row >= low_row) & (row < low_row + 6)
    for j in range(3):
        v = jnp.where(mine, vgrad[16 * j : 16 * j + 16, :].astype(F32), 0.0)
        v = v * v
        acc = acc + (v[0:8] + v[8:16])
    out[...] = acc


def squares(place, parts, vgrad=None, before=None, after=()):
    ins = [(0, p) for p in parts]
    kernel = wide_squares_kernel
    if before is not None:
        ins = [(1, place)] + ins + [(0, vgrad), (0, before)]
        kernel = squares_kernel
    return call(kernel, ins, [((8, 128), F32)], name="squares", vmem=4, after=after)[0]


def merge_kernel(place, igrad, other, out, flag):
    flag[...] = jnp.zeros((8, 128), F32)

    @pl.when(place[0] == 0)
    def low_core():
        out[0:OFF, :] = igrad[0:OFF, :]
        out[OFF:WIN, :] = added(igrad[OFF:WIN, :], other[0 : WIN - OFF, :])
        out[WIN:SEQ, :] = other[WIN - OFF : WIN, :]

    @pl.when(place[0] != 0)
    def high_core():
        out[0:OFF, :] = other[0:OFF, :]
        out[OFF:WIN, :] = added(other[OFF:WIN, :], igrad[0 : WIN - OFF, :])
        out[WIN:SEQ, :] = igrad[WIN - OFF : WIN, :]


def merge(place, igrad, other, after):
    return call(
        merge_kernel,
        [(1, place), (0, igrad), (0, other)],
        [((SEQ, D), BF16), ((8, 128), F32)],
        name="merge",
        vmem=4,
        after=after,
    )


def adamw(parameter, first_state, second, clipped, rate):
    first_new = first_state + (1.0 - BETA_ONE) * clipped
    second_new = second + (1.0 - BETA_TWO) * clipped * clipped
    root = (1.0 - BETA_TWO**STEP) ** 0.5
    below = pl.reciprocal(second_new * lax.rsqrt(second_new) + ADAM_EPS * root)
    scale = rate * root / (1.0 - BETA_ONE**STEP)
    return parameter - scale * (first_new * below), first_new, second_new


def decay_kernel(w, m, v, pv, pm, pq, nw, nm, nv, npv, npm, npq):
    for ins, outs, rate in (
        ((w, m, v), (nw, nm, nv), LEARN_RATE),
        ((pv, pm, pq), (npv, npm, npq), VECTOR_RATE),
    ):
        for ref, out, scale in zip(ins, outs, (1.0 - rate * DECAY_RATE, BETA_ONE, BETA_TWO)):
            out[...] = ref[...] * scale


def decay(arrays, after):
    return call(
        decay_kernel,
        [(0, a) for a in arrays],
        [(a.shape, F32) for a in arrays],
        name="decay",
        vmem=4,
        after=after,
    )


def adamw_kernel(*refs):
    place = Place()
    sums, refs = refs[:2], refs[2:]
    (vgrad, w, m, v, pv, pm, pq), refs = refs[:7], refs[7:]
    wide, low, refs = refs[:4], refs[4:8], refs[8:]
    outs, (npv, npm, npq, norm), scrs, sems = refs[:4], refs[4:8], refs[8:12], refs[12]
    opt = place[0]
    total = sums[0][...] + sums[1][...]
    total = jnp.sum(jnp.sum(total, axis=1, keepdims=True), axis=0, keepdims=True)
    grad_norm = jnp.sqrt(total)
    factor = jnp.minimum(1.0, CLIP_NORM / (grad_norm + 1e-06))
    norm[...] = grad_norm
    for j in range(3):
        cols = slice(128 * j, 128 * j + 128)
        g = vgrad[16 * j : 16 * j + 16, :].astype(F32)
        g = jnp.where(opt == 0, g[0:6], g[6:12])
        a, b, c = adamw(pv[:, cols], pm[:, cols], pq[:, cols], g * factor, VECTOR_RATE)
        npv[:, cols] = a
        npm[:, cols] = b
        npq[:, cols] = c

    def block(grad, rows, cols):
        new = adamw(w[rows, cols], m[rows, cols], v[rows, cols], grad * factor, LEARN_RATE)
        for scr, value in zip(scrs, new + (new[0].astype(BF16),)):
            scr[rows, cols] = value

    def copies(r, i):
        rows = aligned(CHUNK * (place[1] ^ r) + i * 16, 16, 16)
        return [
            pltpu.make_async_copy(scr.at[rows, :], out.at[rows, :], sems.at[3 * r + i, j])
            for j, (scr, out) in enumerate(zip(scrs, outs))
        ]

    for r in range(4):

        def step(i, carry, r=r):
            rows = aligned(CHUNK * (place[1] ^ r) + i * 16, 16, 16)
            here = aligned(i * 16, 16, 16)
            for j in range(4):
                at = D * (place[3] ^ j)
                for p, start in enumerate((4 * D + FF, 4 * D)):
                    grad = wide[r][2 * j + p, here, :].astype(F32)
                    block(grad, rows, aligned(start + at, D, 128))
            for c in range(4):
                grad = low[r][here, D * c : D * c + D].astype(F32)
                block(grad, rows, slice(D * c, D * c + D))
            for copy in copies(r, i):
                copy.start()
            return carry

        lax.fori_loop(0, CHUNK // 16, step, 0)
    for r in range(4):

        def finish(i, carry, r=r):
            for copy in copies(r, i):
                copy.wait()
            return carry

        lax.fori_loop(0, CHUNK // 16, finish, 0)


def update(place, sums, vgrad, w, m, v, pv, pm, pq, parts):
    ins = tuple(sums) + (vgrad, w, m, v, pv, pm, pq) + tuple(parts)
    shapes = [(w.shape, F32)] * 3 + [(w.shape, BF16)] + [(pv.shape, F32)] * 3 + [((1, 1), F32)]
    return pl.pallas_call(
        adamw_kernel,
        out_shape=[jax.ShapeDtypeStruct(s, d) for s, d in shapes],
        in_specs=[VMEM] * len(ins),
        out_specs=[ANY] * 4 + [VMEM] * 4,
        scratch_shapes=[
            pltpu.VMEM(w.shape, F32),
            pltpu.VMEM(w.shape, F32),
            pltpu.VMEM(w.shape, F32),
            pltpu.VMEM(w.shape, BF16),
            pltpu.SemaphoreType.DMA((12, 4)),
        ],
        compiler_params=pltpu.CompilerParams(vmem_limit_bytes=16 << 20),
        cost_estimate=pl.CostEstimate(
            flops=4000000000, bytes_accessed=26 * w.size, transcendentals=0
        ),
        name="adamw",
    )(*ins)


def shards(
    n,
    tokens,
    lengths,
    query_index,
    doc_index,
    targets,
    weights,
    first_moment,
    second_moment,
    vectors,
    vec_first,
    vec_second,
):
    place = None
    scalars = jnp.concatenate([lengths.reshape(SEGS), query_index, doc_index, targets])
    groups = bit_groups(n)

    w_own, wo_own, wu_own, wd_own = cast(weights)
    w_other = pair(w_own)
    vectors_late, w_own = lax.optimization_barrier((vectors, w_own))
    v_other = pair(vectors_late)
    wo = (wo_own, pair(wo_own))
    wu = (wu_own, pair(wu_own))
    wd = (wd_own, pair(wd_own))

    proj, att, lse, segc, segr, ownc, ownr, wanted, marks, vec, wqkv = attend(
        place, scalars, (tokens, w_own, w_other, vectors, v_other)
    )
    xhat1, inv1, hlow, act, up_proj, xhat2, inv2, unit, uscale, wo, wu, wd = mlp(
        place, wanted, att, tokens, ownr, vec, wo + wu + wd
    )
    units, packed = pack(marks, unit, pair(unit))
    groups = bit_groups(n)
    order = [0]
    stack = packed
    for i, (shift, size) in enumerate(groups[1:] + groups[:1]):
        pieces = [stack] + [swap(stack, "dp", n, k << shift) for k in range(1, size)]
        order = [o | (k << shift) for k in range(size) for o in order]
        if i < len(groups) - 1:
            slope = slope_of(up_proj, [packed])
            stack = join(pieces, [slope]).reshape(-1, 2 * PAIRS, D + 128)
    decayed = decay(
        (weights, first_moment, second_moment, vectors, vec_first, vec_second), [packed]
    )
    dsec, dlow, keep, send, dsums = down_backward(
        n, order, place, wanted, units, ownc, uscale, (xhat2, inv2, act), vec, pieces,
        decayed,
    )
    other = pair(send)
    dup, ukeep, usend, usums = up_backward(place, dlow, slope, hlow, wd, [])
    down, go = pair_sum(1, keep, other, [dup])
    dother = swap(go, "dp", n, 1)
    up, go = pair_sum(2, ukeep, pair(usend), [down])
    uother = swap(go, "dp", n, 2)
    dfirst, datt, delta, okeep, osend, fsums = first_backward(
        place, dup, dsec, xhat1, inv1, att, vec, wu, wo, [up]
    )
    ins = (tokens, proj, datt, lse, delta, segc, segr)
    part0, keep0, send0, sums0 = heads_backward(0, place, ins, (), [])
    part1, keep1, send1, sums1 = heads_backward(1, place, ins, (), [part0])
    down, dsend, up, usend = wide_step((down, dother, up, uother), [part1])
    dother, uother = swap(dsend, "dp", n, 2), swap(usend, "dp", n, 1)
    part2, keep, send, _ = heads_backward(
        2, place, ins,
        (okeep, osend, keep0, send0, keep1, send1, dsums, usums, fsums, sums0, sums1),
        [down, part1],
    )
    other = pair(send)
    igrad = input_backward((part0, part1, part2), dfirst, wqkv, [part2])
    iother = pair(igrad)
    wide = wide_plane_sum(place, (down, dother, up, uother), [igrad])
    wide_got = trades(wide, n, 2)
    low = core_sum(keep, other, [wide[0]])
    low_got = trades(low, n, 0)
    wide = rest_sum(low_plane_sum(wide_got, [low[0]]), n)
    wide_got = trades([wide] * 4, n, 2)
    low = low_plane_sum(low_got, [wide])
    other = swap(low, "dp", n, 4)
    wide = chain(wide_got, [low])
    wide = trades([wide] * 4, n, 0)
    low = low_next(low, other, [wide[0]])
    other = swap(low, "dp", n, 8)
    input_grad, flag = merge(place, igrad, iother, [low])
    low, vgrad = low_last(low, other, [flag])
    low, vgrad = rest_sum(low, n), rest_sum(vgrad, n)
    low = trades([low] * 4, n, 0)
    sums = squares(place, low, vgrad, squares(place, wide, after=[low[0]]))
    sums = (sums, pair(sums))
    pieces = tuple(wide) + tuple(low)
    nw, nm, nv, nlow, npv, npm, npq, norm = update(
        place, sums, vgrad, *decayed, pieces,
    )
    return (norm.reshape(()), input_grad, nw, nm, nv, nlow, npv, npm, npq)


def solution(mesh):
    rows = P("opt", None)
    in_specs = (P("dp", None), P("dp", None), P("dp"), P("dp"), P("dp")) + (rows,) * 6
    out_specs = (P(), P("dp", None)) + (rows,) * 7
    n = mesh.shape["dp"]
    return jax.shard_map(
        functools.partial(shards, n),
        mesh=mesh,
        in_specs=in_specs,
        out_specs=out_specs,
        check_vma=False,
    )
```

```python
import functools

import jax
import jax.numpy as jnp
from jax import lax
from jax.experimental import pallas as pl
from jax.experimental.pallas import tpu as pltpu
from jax.sharding import PartitionSpec as P

D = 384
HEADS = 12
HD = 32
FF = 1536
SEQ = 1024
SEGS = 16
PAIRS = 8
STEP = 10

WIN = 576
OFF = SEQ - WIN
PAD = 640
BLOCK = 128
BANDS = tuple((q, max(0, q - 128), min(WIN, q + 256)) for q in range(0, WIN, BLOCK))
BAND_ROWS = tuple(sum(b[2] - b[1] for b in BANDS[:i]) for i in range(len(BANDS) + 1))
ROWS = 64
WIDE_ROWS = 192
LOG2E = 1.4426950408889634

LN_EPS = 1e-06
POOL_EPS = 1e-06
SCORE_SCALE = 50.0
CLIP_NORM = 0.001
BETA_ONE = 0.9
BETA_TWO = 0.98
ADAM_EPS = 1e-08
LEARN_RATE = 0.05
VECTOR_RATE = 0.3
DECAY_RATE = 0.01
NEG_BIG = -1e30
HALF = D // 2
CHUNK = HALF // 4
EXP2_SCALE = HD ** (-0.5) * 1.4426950408889634

F32 = jnp.float32
BF16 = jnp.bfloat16
VMEM = pl.BlockSpec(memory_space=pltpu.VMEM)
SMEM = pl.BlockSpec(memory_space=pltpu.SMEM)
ANY = pl.BlockSpec(memory_space=pl.ANY)


def nn(a, b):
    return jnp.dot(a, b, preferred_element_type=F32)


def nt(a, b):
    return lax.dot_general(a, b, (((1,), (1,)), ((), ())), preferred_element_type=F32)


def tn(a, b):
    return lax.dot_general(a, b, (((0,), (0,)), ((), ())), preferred_element_type=F32)


def exact(a, b, dims):
    return lax.dot_general(
        a, b, (dims, ((), ())), precision=lax.Precision.HIGHEST, preferred_element_type=F32
    )


def iota(shape, axis):
    return lax.broadcasted_iota(jnp.int32, shape, axis)


def low_pair(value):
    high = value.astype(BF16)
    return high, (value - high.astype(F32)).astype(BF16)


def aligned(start, size, unit):
    return pl.ds(pl.multiple_of(start, unit), size)


def assemble(dst, own, other, opt):
    dst[aligned(HALF * opt, HALF, 64), :] = own[0:HALF, :]
    dst[aligned(HALF * (1 - opt), HALF, 64), :] = other[0:HALF, :]


class Place:
    def __getitem__(self, i):
        if i == 0:
            return lax.axis_index("opt")
        me = lax.axis_index("dp")
        return (me & 3, me, (me >> 2) & 3)[i - 1]


def call(kernel, ins, outs, scratch=(), micros=5, name=None, vmem=12, after=()):
    if ins[0][1] is None:
        kernel = functools.partial(kernel, Place())
        ins = ins[1:]
    specs = [SMEM if s else VMEM for s, _ in ins] + [ANY] * len(after)
    count = len(ins)

    def body(*refs):
        kernel(*refs[:count], *refs[count + len(after) :])

    shapes = [jax.ShapeDtypeStruct(s, d) for s, d in outs]
    moved = sum(a.size * a.dtype.itemsize for _, a in ins)
    moved += sum(s.size * s.dtype.itemsize for s in shapes)
    return pl.pallas_call(
        body,
        out_shape=shapes,
        in_specs=specs,
        out_specs=[VMEM] * len(shapes),
        scratch_shapes=list(scratch),
        compiler_params=pltpu.CompilerParams(vmem_limit_bytes=vmem << 20),
        cost_estimate=pl.CostEstimate(
            flops=micros * 1100000000, bytes_accessed=moved, transcendentals=0
        ),
        name=name,
    )(*[a for _, a in ins], *after)


def head_stack(rows):
    lane_head = iota(rows.shape, 1) // HD
    zero = jnp.zeros_like(rows)
    return jnp.concatenate([jnp.where(lane_head == j, rows, zero) for j in range(4)], axis=0)


def attend_kernel(
    place, scalars, tokens, w_own, w_other, v_own, v_other,
    proj, att, lse, segc, segr, ownc, ownr, wanted, marks, vec, wfull, bias, vt,
):
    opt = place[0]
    assemble(wfull, w_own, w_other, opt)
    mine = v_own[...].astype(BF16).astype(F32)
    others = v_other[...].astype(BF16).astype(F32)
    first = opt == 0
    vec[0:6, :] = jnp.where(first, mine, others)
    vec[6:12, :] = jnp.where(first, others, mine)
    vec[12:16, :] = jnp.zeros((4, D), F32)

    position = iota((8, PAD), 1) + OFF * opt
    segment = jnp.zeros((8, PAD), jnp.int32)
    bound = jnp.int32(0)
    low_count = jnp.int32(0)
    for s in range(SEGS):
        bound = bound + scalars[s]
        segment = segment + (position >= bound).astype(jnp.int32)
        low_count = low_count + (bound <= WIN).astype(jnp.int32)
    mine = (segment < low_count).astype(jnp.int32) == (opt == 0).astype(jnp.int32)
    owned = jnp.where(mine, segment, -1)
    segr[...] = segment
    ownr[...] = owned
    for value, out in ((segment, segc), (owned, ownc)):
        value = value.astype(F32)
        for t in range(PAD // 128):
            rows = min(128, WIN - 128 * t)
            turned = jnp.broadcast_to(value[0:1, 128 * t : 128 * t + 128], (128, 128)).T
            out[128 * t : 128 * t + rows, :] = turned[0:rows].astype(jnp.int32)
    row, col = iota((2 * PAIRS, 128), 0), iota((2 * PAIRS, 128), 1)
    by_row = jnp.zeros((2 * PAIRS, 128), jnp.int32)
    by_col = jnp.zeros((2 * PAIRS, 128), jnp.int32)
    mark = jnp.zeros((2 * PAIRS, 128), jnp.int32)
    for j in range(PAIRS):
        mark = jnp.where(row == j, scalars[SEGS + 2 * PAIRS + j], mark)
        for at in (j, PAIRS + j):
            by_row = jnp.where(row == at, scalars[SEGS + at], by_row)
            by_col = jnp.where(col == at, scalars[SEGS + at], by_col)
    wanted[0] = by_row
    wanted[1] = by_col
    marks[...] = jnp.where(col < 64, mark >> 5, mark & 31).astype(F32).astype(BF16)
    for i, (q0, k0, k1) in enumerate(BANDS):
        bias[BAND_ROWS[i] : BAND_ROWS[i + 1], :] = jnp.where(
            segc[k0:k1, :] == segr[0:1, q0 : q0 + BLOCK], 0.0, NEG_BIG
        )

    x = tokens[aligned(OFF * opt, WIN, 64), :]
    bias_row = jnp.concatenate([vec[0:1, :], jnp.zeros((1, D), F32), vec[1:2, :]], axis=1)
    for first in range(0, 3 * D, 512):
        cols = slice(first, min(first + 512, 3 * D))
        proj[0:WIN, cols] = (nn(x, wfull[:, cols]) + bias_row[:, cols]).astype(BF16)
    proj[WIN:PAD, :] = jnp.zeros((PAD - WIN, 3 * D), BF16)

    def group(g, carry):
        def lanes(part):
            return aligned(part * D + 128 * g, 128, 128)

        for t in range(PAD // 128):
            vt[:, 128 * t : 128 * t + 128] = (
                proj[128 * t : 128 * t + 128, lanes(2)].astype(F32).T.astype(BF16)
            )
        def scores(i):
            q0, k0, k1 = BANDS[i]
            return nt(proj[k0:k1, lanes(1)], head_stack(proj[q0 : q0 + BLOCK, lanes(0)]))

        coming = scores(0)
        for i, (q0, k0, k1) in enumerate(BANDS):
            st = coming
            if i + 1 < len(BANDS):
                coming = scores(i + 1)
            outs, probs, totals = [], [], []
            for j in range(4):
                t = (
                    st[:, j * BLOCK : (j + 1) * BLOCK] * EXP2_SCALE
                    + bias[BAND_ROWS[i] : BAND_ROWS[i + 1], :]
                )
                peak = jnp.max(t, axis=0, keepdims=True)
                powers = jnp.exp2(t - peak)
                total = jnp.sum(powers, axis=0, keepdims=True)
                lse[g, j : j + 1, q0 : q0 + BLOCK] = peak + jnp.log2(total)
                probs.append(powers.astype(BF16))
                totals.append(1.0 / total)
                if j % 2 == 1:
                    o = nn(vt[(j - 1) * HD : (j + 1) * HD, k0:k1], jnp.concatenate(probs[-2:], axis=1))
                    outs.append(o[0:HD, 0:BLOCK] * totals[-2])
                    outs.append(o[HD : 2 * HD, BLOCK : 2 * BLOCK] * totals[-1])
            rows = min(BLOCK, WIN - q0)
            att[q0 : q0 + rows, aligned(128 * g, 128, 128)] = (
                jnp.concatenate(outs, axis=0).T[0:rows].astype(BF16)
            )
        return carry

    lax.fori_loop(0, 3, group, 0)


def attend(place, scalars, arrays):
    return call(
        attend_kernel,
        [(1, place), (1, scalars)] + [(0, a) for a in arrays],
        [
            ((PAD, 3 * D), BF16),
            ((WIN, D), BF16),
            ((3, 4, PAD), F32),
            ((WIN, 128), jnp.int32),
            ((8, PAD), jnp.int32),
            ((WIN, 128), jnp.int32),
            ((8, PAD), jnp.int32),
            ((2, 2 * PAIRS, 128), jnp.int32),
            ((2 * PAIRS, 128), BF16),
            ((16, D), F32),
            ((D, 3 * D), BF16),
        ],
        [
            pltpu.VMEM((BAND_ROWS[-1], 128), F32),
            pltpu.VMEM((128, PAD), BF16),
        ],
        micros=8,
        name="attend",
    )


def cast_kernel(weights, wq, wo, wu, wd, buffer, sems):
    spans = [(wq, 3 * D), (wo, D), (wu, FF), (wd, FF)]
    copies = [
        pltpu.make_async_copy(
            weights.at[:, i * D : (i + 1) * D], buffer.at[:, i * D : (i + 1) * D], sems.at[i]
        )
        for i in range(12)
    ]
    for copy in copies:
        copy.start()
    at = 0
    for out, width in spans:
        for part in range(width // D):
            copies[at].wait()
            out[:, part * D : (part + 1) * D] = buffer[:, at * D : (at + 1) * D].astype(BF16)
            at += 1


def cast(weights):
    return pl.pallas_call(
        cast_kernel,
        out_shape=[jax.ShapeDtypeStruct((HALF, c), BF16) for c in (3 * D, D, FF, FF)],
        in_specs=[ANY],
        out_specs=[VMEM] * 4,
        scratch_shapes=[pltpu.VMEM(weights.shape, F32), pltpu.SemaphoreType.DMA((12,))],
        compiler_params=pltpu.CompilerParams(vmem_limit_bytes=52 << 20),
        name="cast",
    )(weights)


def bias_of(vec, c):
    first, last = 256 * c, 256 * c + 256
    parts = []
    while first < last:
        row, col = divmod(first, D)
        size = min(D - col, last - first)
        parts.append(vec[3 + row : 4 + row, col : col + size])
        first += size
    return parts[0] if len(parts) == 1 else jnp.concatenate(parts, axis=1)


def mlp_kernel(
    place, wanted, att, tokens, ownr, vec, wo_own, wo_other, wu_own, wu_other,
    wd_own, wd_other, xhat1, inv1, hlow, act, up_proj, xhat2, inv2, unit, uscale, wo, wu, wd,
    ench, encl,
):
    opt = place[0]
    assemble(wo, wo_own, wo_other, opt)
    assemble(wu, wu_own, wu_other, opt)
    assemble(wd, wd_own, wd_other, opt)

    def norm(v):
        centred = v - jnp.mean(v, axis=1, keepdims=True)
        inverse = lax.rsqrt(jnp.mean(centred * centred, axis=1, keepdims=True) + LN_EPS)
        return centred * inverse, inverse

    def block(i, carry):
        r = aligned(i * WIDE_ROWS, WIDE_ROWS, 64)
        x = tokens[aligned(OFF * opt + i * WIDE_ROWS, WIDE_ROWS, 64), :].astype(F32)
        normed, inverse = norm(nn(att[r, :], wo[...]) + vec[2:3, :] + x)
        xhat1[r, :] = normed
        inv1[r, :] = jnp.broadcast_to(inverse, (WIDE_ROWS, 128))
        h = normed * vec[8:9, :] + vec[9:10, :]
        low = h.astype(BF16)
        hlow[r, :] = low
        coming = nn(low, wu[:, 0:256])
        for c in range(6):
            cols = slice(c * 256, (c + 1) * 256)
            u = coming + bias_of(vec, c)
            if c < 5:
                coming = nn(low, wu[:, (c + 1) * 256 : (c + 2) * 256])
            up_proj[r, cols] = u
            half = lax.erf(u * 0.7071067811865476) * 0.5 + 0.5
            act[r, cols] = (u * half).astype(BF16)
        normed, inverse = norm(nt(act[r, :], wd[...]) + vec[7:8, :] + h)
        xhat2[r, :] = normed
        inv2[r, :] = jnp.broadcast_to(inverse, (WIDE_ROWS, 128))
        high, rest = low_pair(normed * vec[10:11, :] + vec[11:12, :])
        ench[r, :] = high
        encl[r, :] = rest
        return carry

    lax.fori_loop(0, WIN // WIDE_ROWS, block, 0)

    onehot = jnp.where(wanted[0, :, 0:1] == ownr[0:1, 0:WIN], 1.0, 0.0)
    count = jnp.maximum(jnp.sum(onehot, axis=1, keepdims=True), 1.0)
    hot = onehot.astype(BF16)
    pooled = (nn(hot, ench[...]) + nn(hot, encl[...])) / count
    inverse_len = lax.rsqrt(jnp.sum(pooled * pooled, axis=1, keepdims=True) + POOL_EPS)
    unit[...] = pooled * inverse_len
    uscale[...] = jnp.broadcast_to(inverse_len / count, (2 * PAIRS, 128))


def slope_kernel(up_proj, out):
    def block(i, carry):
        r = aligned(i * 16, 16, 16)
        u = up_proj[r, :]
        half = lax.erf(u * 0.7071067811865476) * 0.5 + 0.5
        out[r, :] = half + u * jnp.exp2(u * u * (-0.5 * LOG2E)) * 0.3989422804014327
        return carry

    lax.fori_loop(0, WIN // 16, block, 0)


def slope_of(up_proj, after):
    return call(slope_kernel, [(0, up_proj)], [(up_proj.shape, F32)], name="slope", vmem=4, after=after)[0]


def mlp(place, wanted, att, tokens, ownr, vec, halves):
    return call(
        mlp_kernel,
        [(1, place), (0, wanted), (0, att), (0, tokens), (0, ownr), (0, vec)]
        + [(0, h) for h in halves],
        [
            ((WIN, D), F32),
            ((WIN, 128), F32),
            ((WIN, D), BF16),
            ((WIN, FF), BF16),
            ((WIN, FF), F32),
            ((WIN, D), F32),
            ((WIN, 128), F32),
            ((2 * PAIRS, D), F32),
            ((2 * PAIRS, 128), F32),
            ((D, D), BF16),
            ((D, FF), BF16),
            ((D, FF), BF16),
        ],
        [
            pltpu.VMEM((WIN, D), BF16),
            pltpu.VMEM((WIN, D), BF16),
        ],
        micros=10,
        name="mlp",
    )


def split_rows(grad, keep, send, place, *at):
    opt = place[0]
    for c in range(4):
        index = (c ^ place[1],) + at
        keep[index] = grad[aligned(HALF * opt + CHUNK * c, CHUNK, 16), :].astype(BF16)
        send[index] = grad[aligned(HALF * (1 - opt) + CHUNK * c, CHUNK, 16), :].astype(BF16)


def column_sums(value):
    return jnp.sum(value.reshape(-1, 8, D), axis=0)


def norm_backward(grad_at, normed_ref, inverse_ref, gain, out, low_out, sums, at, step=ROWS):
    def block(i, carry):
        scale_sum, shift_sum, bias_sum = carry
        r = aligned(i * step, step, 64)
        g = grad_at(r)
        normed = normed_ref[r, :]
        scaled = g * gain
        inner = (
            scaled
            - jnp.mean(scaled, axis=1, keepdims=True)
            - normed * jnp.mean(scaled * normed, axis=1, keepdims=True)
        ) * inverse_ref[r, 0:1]
        out[r, :] = inner
        low_out[r, :] = inner.astype(BF16)
        return (
            scale_sum + column_sums(g * normed),
            shift_sum + column_sums(g),
            bias_sum + column_sums(inner),
        )

    zero = jnp.zeros((8, D), F32)
    scale_sum, shift_sum, bias_sum = lax.fori_loop(0, WIN // step, block, (zero, zero, zero))
    sums[at : at + 1, :] = jnp.sum(bias_sum, axis=0, keepdims=True)
    sums[at + 1 : at + 2, :] = jnp.sum(scale_sum, axis=0, keepdims=True)
    sums[at + 2 : at + 3, :] = jnp.sum(shift_sum, axis=0, keepdims=True)


def down_kernel(
    place, count, order, wanted, units, ownc, uscale, xhat2, inv2, act, vec, *rest
):
    pieces, (dsec, dlow, keep, send, sums, queries, docs, marks, grad) = rest[:-9], rest[-9:]
    me = place[2]
    per = pieces[0].shape[0]
    for p, piece in enumerate(pieces):
        for j in range(per):
            at = order[p * per + j]
            r = slice(at * PAIRS, (at + 1) * PAIRS)
            both = piece[j].astype(F32)
            queries[r, :] = both[0:PAIRS, 0:D]
            docs[r, :] = both[PAIRS : 2 * PAIRS, 0:D]
            marks[r, :] = both[0:PAIRS, D : D + 128]
    total = count * PAIRS
    q = queries[...].astype(BF16)
    d = docs[...].astype(BF16)
    logits = SCORE_SCALE * nt(q, d)
    peak = jnp.max(logits, axis=1, keepdims=True)
    powers = jnp.exp(logits - peak)
    soft = powers / jnp.sum(powers, axis=1, keepdims=True)
    col = iota((total, total), 1)
    doc_id = ((col // PAIRS) ^ me) * PAIRS + lax.rem(col, PAIRS)
    hit = (marks[:, 0:1] * 32.0 + marks[:, 64:65]).astype(jnp.int32) == doc_id
    d_logits = (soft - jnp.where(hit, 1.0, 0.0)) * (SCORE_SCALE / total)
    high, rest_low = low_pair(d_logits[0:PAIRS, :])
    d_q = nn(high, d) + nn(rest_low, d)
    high, rest_low = low_pair(d_logits[:, 0:128].T[0:PAIRS, :])
    d_d = nn(high, q) + nn(rest_low, q)
    d_units = jnp.concatenate([d_q, d_d], axis=0)
    u = units[...]
    d_pool = uscale[:, 0:1] * (d_units - u * jnp.sum(u * d_units, axis=1, keepdims=True))
    hot = jnp.where(ownc[:, 0 : 2 * PAIRS] == wanted[1, 0:1, 0 : 2 * PAIRS], 1.0, 0.0).astype(BF16)
    high, rest_low = low_pair(d_pool)
    dsec[...] = nn(hot, high) + nn(hot, rest_low)
    norm_backward(lambda r: dsec[r, :], xhat2, inv2, vec[10:11, :], dsec, dlow, sums, 0)
    sums[3:8, :] = jnp.zeros((5, D), F32)
    for c in range(3):
        cols = slice(c * 512, (c + 1) * 512)
        grad[:, cols] = tn(dlow[...], act[:, cols])
    for c in range(4):
        split_rows(grad.at[:, c * D : (c + 1) * D], keep, send, place, c)


def down_backward(count, order, place, wanted, units, ownc, uscale, saved, vec, pieces, after):
    total = count * PAIRS
    return call(
        lambda place, *refs: down_kernel(place, count, order, *refs),
        [(1, place), (0, wanted), (0, units), (0, ownc), (0, uscale)]
        + [(0, s) for s in saved]
        + [(0, vec)]
        + [(0, p) for p in pieces],
        [
            ((WIN, D), F32),
            ((WIN, D), BF16),
            ((4, 4, CHUNK, D), BF16),
            ((4, 4, CHUNK, D), BF16),
            ((8, D), F32),
        ],
        [
            pltpu.VMEM((total, D), F32),
            pltpu.VMEM((total, D), F32),
            pltpu.VMEM((total, 128), F32),
            pltpu.VMEM((D, FF), F32),
        ],
        micros=4,
        name="down_backward",
        after=after,
    )


def up_kernel(place, dlow, slope, hlow, wd, dup, keep, send, sums, grad):
    coming = nn(dlow[...], wd[:, 0:512])
    for c in range(3):
        cols = slice(c * 512, (c + 1) * 512)
        part = (coming * slope[:, cols]).astype(BF16)
        if c < 2:
            coming = nn(dlow[...], wd[:, (c + 1) * 512 : (c + 2) * 512])
        dup[:, cols] = part
        column_sum = jnp.sum(part.astype(F32), axis=0, keepdims=True)
        for j in range(4):
            at = 512 * c + 128 * j
            sums[at // D : at // D + 1, at % D : at % D + 128] = column_sum[:, 128 * j : 128 * j + 128]
        grad[:, cols] = tn(hlow[...], dup[:, cols])
    for c in range(4):
        split_rows(grad.at[:, c * D : (c + 1) * D], keep, send, place, c)


def up_backward(place, dlow, slope, hlow, wd, after):
    return call(
        up_kernel,
        [(1, place)] + [(0, a) for a in (dlow, slope, hlow, wd)],
        [((WIN, FF), BF16), ((4, 4, CHUNK, D), BF16), ((4, 4, CHUNK, D), BF16), ((4, D), F32)],
        [pltpu.VMEM((D, FF), F32)],
        micros=3,
        name="up_backward",
        after=after,
    )


def first_kernel(
    place, dup, dsec, xhat1, inv1, att, vec, wu, wo,
    dfirst, datt, delta, okeep, osend, sums, grad, dlow,
):
    steps = [slice(i, i + WIDE_ROWS) for i in range(0, WIN, WIDE_ROWS)]
    coming = nt(dup[steps[0], :], wu[...])
    gain = vec[8:9, :]
    totals = None
    for i, r in enumerate(steps):
        g = coming + dsec[r, :]
        if i + 1 < len(steps):
            coming = nt(dup[steps[i + 1], :], wu[...])
        normed = xhat1[r, :]
        scaled = g * gain
        inner = (
            scaled
            - jnp.mean(scaled, axis=1, keepdims=True)
            - normed * jnp.mean(scaled * normed, axis=1, keepdims=True)
        ) * inv1[r, 0:1]
        dfirst[r, :] = inner
        dlow[r, :] = inner.astype(BF16)
        new = [column_sums(inner), column_sums(g * normed), column_sums(g)]
        totals = new if totals is None else [a + b for a, b in zip(totals, new)]
    for i, total in enumerate(totals):
        sums[i : i + 1, :] = jnp.sum(total, axis=0, keepdims=True)
    sums[3:8, :] = jnp.zeros((5, D), F32)
    grad[...] = tn(att[...], dlow[...])
    split_rows(grad, okeep, osend, place)
    da = nt(dlow[...], wo[...]).astype(BF16)
    datt[0:WIN, :] = da
    datt[WIN:PAD, :] = jnp.zeros((PAD - WIN, D), BF16)
    high, rest = low_pair(da.astype(F32) * att[...].astype(F32))
    heads = (iota((16, D), 1) // HD == iota((16, D), 0)).astype(F32).astype(BF16)
    delta[:, 0:WIN] = nt(heads, high) + nt(heads, rest)
    delta[:, WIN:PAD] = jnp.zeros((16, PAD - WIN), F32)


def first_backward(place, dup, dsec, xhat1, inv1, att, vec, wu, wo, after):
    return call(
        first_kernel,
        [(1, place)] + [(0, a) for a in (dup, dsec, xhat1, inv1, att, vec, wu, wo)],
        [
            ((WIN, D), F32),
            ((PAD, D), BF16),
            ((16, PAD), F32),
            ((4, CHUNK, D), BF16),
            ((4, CHUNK, D), BF16),
            ((8, D), F32),
        ],
        [
            pltpu.VMEM((D, D), F32),
            pltpu.VMEM((WIN, D), BF16),
        ],
        micros=1,
        name="first_backward",
        after=after,
    )


def heads_kernel(place, g, tokens, proj, datt, lse, delta, segc, segr, *rest):
    rest, (dproj, keep, send, sums, kt, dk, dv, grad, ktmp, stmp) = rest[:-10], rest[-10:]

    def lanes(part):
        return slice(part * D + 128 * g, part * D + 128 * g + 128)

    for t in range(PAD // 128):
        kt[:, 128 * t : 128 * t + 128] = (
            proj[128 * t : 128 * t + 128, lanes(1)].astype(F32).T.astype(BF16)
        )
    dk[...] = jnp.zeros_like(dk)
    dv[...] = jnp.zeros_like(dv)

    def products(i):
        q0, k0, k1 = BANDS[i]
        qs = head_stack(proj[q0 : q0 + BLOCK, lanes(0)])
        gs = head_stack(datt[q0 : q0 + BLOCK, lanes(0)])
        return qs, gs, nt(proj[k0:k1, lanes(1)], qs), nt(proj[k0:k1, lanes(2)], gs)

    coming = products(0)
    for i, (q0, k0, k1) in enumerate(BANDS):
        qs, gs, st, dp = coming
        if i + 1 < len(BANDS):
            coming = products(i + 1)
        same = segc[k0:k1, :] == segr[0:1, q0 : q0 + BLOCK]
        bias = jnp.where(same, 0.0, NEG_BIG)
        probs, d_scores, dq = [], [], []
        for j in range(4):
            cols = slice(j * BLOCK, (j + 1) * BLOCK)
            prob = jnp.exp2(st[:, cols] * EXP2_SCALE + bias - lse[g, j : j + 1, q0 : q0 + BLOCK])
            ds = prob * (dp[:, cols] - delta[4 * g + j : 4 * g + j + 1, q0 : q0 + BLOCK])
            ds = ds.astype(BF16)
            probs.append(prob.astype(BF16))
            d_scores.append(ds)
            if j % 2 == 1:
                part = nn(
                    kt[(j - 1) * HD : (j + 1) * HD, k0:k1], jnp.concatenate(d_scores[-2:], axis=1)
                )
                dq.append(part[0:HD, 0:BLOCK])
                dq.append(part[HD : 2 * HD, BLOCK : 2 * BLOCK])
        dv[k0:k1, :] += nn(jnp.concatenate(probs, axis=1), gs)
        dk[k0:k1, :] += nn(jnp.concatenate(d_scores, axis=1), qs)
        rows = min(BLOCK, WIN - q0)
        dqs = jnp.concatenate(dq, axis=0).T[0:rows] * HD ** (-0.5)
        dproj[q0 : q0 + rows, 0:128] = dqs.astype(BF16)
    dproj[:, 128:256] = (dk[...] * HD ** (-0.5)).astype(BF16)
    dproj[:, 256:384] = dv[...].astype(BF16)
    grad[...] = tn(tokens[aligned(OFF * place[0], WIN, 64), :], dproj[...])
    q_sum = jnp.sum(dproj[:, 0:128].astype(F32), axis=0, keepdims=True)
    v_sum = jnp.sum(dproj[:, 256:384].astype(F32), axis=0, keepdims=True)
    sums[0:1, :] = q_sum
    sums[1:2, :] = v_sum
    sums[2:8, :] = jnp.zeros((6, 128), F32)
    if g < 2:
        split_rows(grad, keep, send, place)
        return
    parts, (dsums, usums, fsums, zero, one) = rest[:6], rest[6:]
    split_rows(grad, ktmp, stmp, place)
    for dst, out_part, blocks in (
        (keep, parts[0], (parts[2], parts[4], ktmp)),
        (send, parts[1], (parts[3], parts[5], stmp)),
    ):
        dst[:, :, 3 * D : 4 * D] = out_part[...]
        for h, part in enumerate(blocks):
            for c in range(3):
                dst[:, :, D * c + 128 * h : D * c + 128 * h + 128] = part[
                    :, :, 128 * c : 128 * c + 128
                ]
    rows = jnp.concatenate(
        [
            jnp.concatenate([zero[0:1], one[0:1], q_sum], axis=1),
            jnp.concatenate([zero[1:2], one[1:2], v_sum], axis=1),
            fsums[0:1, :],
            usums[0:4, :],
            dsums[0:1, :],
            fsums[1:3, :],
            dsums[1:3, :],
            jnp.zeros((4, D), F32),
        ],
        axis=0,
    ).astype(BF16)
    for c in range(4):
        for j in range(3):
            block = rows[:, 128 * j : 128 * j + 128]
            keep[c, 16 * j : 16 * j + 16, 4 * D : 4 * D + 128] = block
            send[c, 16 * j : 16 * j + 16, 4 * D : 4 * D + 128] = block


def heads_backward(g, place, ins, more, after):
    part = ((4, CHUNK, 4 * D + 128 if g == 2 else D), BF16)
    return call(
        lambda place, *refs: heads_kernel(place, g, *refs),
        [(1, place)] + [(0, a) for a in tuple(ins) + tuple(more)],
        [((WIN, D), BF16), part, part, ((8, 128), F32)],
        [
            pltpu.VMEM((128, PAD), BF16),
            pltpu.VMEM((WIN, 128), F32),
            pltpu.VMEM((WIN, 128), F32),
            pltpu.VMEM((D, D), F32),
            pltpu.VMEM((4, CHUNK, D), BF16),
            pltpu.VMEM((4, CHUNK, D), BF16),
        ],
        micros=1,
        name="heads_backward",
        after=after,
    )


def input_kernel(dp0, dp1, dp2, dfirst, wfull, igrad, dproj):
    for g, part in enumerate((dp0, dp1, dp2)):
        for c in range(3):
            dproj[:, c * D + 128 * g : c * D + 128 * g + 128] = part[:, 128 * c : 128 * c + 128]
    igrad[...] = (nt(dproj[...], wfull[...]) + dfirst[...]).astype(BF16)


def input_backward(parts, dfirst, wqkv, after):
    return call(
        input_kernel,
        [(0, a) for a in tuple(parts) + (dfirst, wqkv)],
        [((WIN, D), BF16)],
        [pltpu.VMEM((WIN, 3 * D), BF16)],
        micros=2,
        name="input_backward",
        after=after,
    )[0]


def flips(axis, size, bits):
    return [(i, i ^ bits) for i in range(size)]


def pair(value):
    return swap(value, "opt", 2, 1)


def swap(value, axis, size, bits):
    return lax.ppermute(value, axis, flips(axis, size, bits))


def bit_groups(size):
    bits = size.bit_length() - 1
    return [(s, 1 << min(2, bits - s)) for s in range(0, bits, 2)]


def trades(values, n, shift):
    return [values[0]] + [swap(values[k], "dp", n, k << shift) for k in (1, 2, 3)]


def added(a, b):
    return (a.astype(F32) + b.astype(F32)).astype(BF16)


def core_sum_kernel(keep, other, *outs):
    for r, out in enumerate(outs):
        out[...] = added(keep[r], other[r])


def core_sum(keep, other, after):
    return call(
        core_sum_kernel,
        [(0, keep), (0, other)],
        [(keep.shape[1:], BF16)] * 4,
        name="core_sum",
        vmem=4,
        after=after,
    )


def pair_sum_kernel(bit, keep, other, stay, go):
    for i, r in enumerate((0, 3 - bit)):
        stay[i] = added(keep[r], other[r])
        go[i] = added(keep[r + bit], other[r + bit])


def pair_sum(bit, keep, other, after):
    return call(
        functools.partial(pair_sum_kernel, bit),
        [(0, keep), (0, other)],
        [((2,) + keep.shape[1:], BF16)] * 2,
        name="pair_sum",
        vmem=4,
        after=after,
    )


def wide_step_kernel(down, dother, up, uother, dkeep, dsend, ukeep, usend):
    dkeep[...] = added(down[0], dother[0])
    dsend[...] = added(down[1], dother[1])
    ukeep[...] = added(up[0], uother[0])
    usend[...] = added(up[1], uother[1])


def wide_step(parts, after):
    return call(
        wide_step_kernel,
        [(0, p) for p in parts],
        [((4, CHUNK, D), BF16)] * 4,
        name="wide_step",
        vmem=4,
        after=after,
    )


def total_of(refs, at):
    a, b, c, d = (ref[at].astype(F32) for ref in refs)
    return ((a + b) + (c + d)).astype(BF16)


def wide_plane_kernel(place, down, dother, up, uother, *outs):
    for k, out in enumerate(outs):
        at = place[3] ^ k
        out[0] = added(down[at], dother[at])
        out[1] = added(up[at], uother[at])


def wide_plane_sum(place, parts, after):
    return call(
        wide_plane_kernel,
        [(1, place)] + [(0, p) for p in parts],
        [((2, CHUNK, D), BF16)] * 4,
        name="wide_plane_sum",
        vmem=4,
        after=after,
    )


def low_plane_kernel(a, b, c, d, out):
    out[...] = total_of((a, b, c, d), slice(None))


def low_plane_sum(parts, after=()):
    return call(
        low_plane_kernel,
        [(0, p) for p in parts],
        [(parts[0].shape, BF16)],
        name="low_plane_sum",
        vmem=4,
        after=after,
    )[0]


def low_next_kernel(keep, other, out):
    out[...] = added(keep[...], other[...])


def low_next(keep, other, after=()):
    return call(
        low_next_kernel,
        [(0, keep), (0, other)],
        [(keep.shape, BF16)],
        name="low_next",
        vmem=4,
        after=after,
    )[0]


def low_last_kernel(keep, other, out, vgrad):
    out[...] = added(keep[:, 0 : 4 * D], other[:, 0 : 4 * D])
    vgrad[...] = added(keep[:, 4 * D : 4 * D + 128], other[:, 4 * D : 4 * D + 128])


def low_last(keep, other, after):
    return call(
        low_last_kernel,
        [(0, keep), (0, other)],
        [((CHUNK, 4 * D), BF16), ((CHUNK, 128), BF16)],
        name="low_last",
        vmem=4,
        after=after,
    )


def chain_kernel(*refs):
    ins, out = refs[:-1], refs[-1]
    at = 0
    for ref in ins:
        flat = ref.reshape(-1, CHUNK, D)
        out[at : at + flat.shape[0]] = flat[...]
        at += flat.shape[0]


def chain(parts, after=()):
    count = sum(p.size for p in parts) // (CHUNK * D)
    return call(
        chain_kernel,
        [(0, p) for p in parts],
        [((count, CHUNK, D), BF16)],
        name="chain",
        vmem=4,
        after=after,
    )[0]


def rest_sum(value, n):
    bit = 16
    while bit < n:
        other = swap(value, "dp", n, bit)
        value = (value.astype(F32) + other.astype(F32)).astype(BF16)
        bit *= 2
    return value


def join_kernel(*refs):
    ins, out = refs[:-1], refs[-1]
    for i, ref in enumerate(ins):
        out[i] = ref[...]


def join(parts, after=()):
    return call(
        join_kernel,
        [(0, p) for p in parts],
        [((len(parts),) + parts[0].shape, parts[0].dtype)],
        name="join",
        vmem=4,
        after=after,
    )[0]


def pack_kernel(marks, unit, other, units, packed):
    both = unit[...] + other[...]
    units[...] = both
    packed[:, 0:D] = both.astype(BF16)
    packed[:, D : D + 128] = marks[...]


def pack(marks, unit, other):
    return call(
        pack_kernel,
        [(0, marks), (0, unit), (0, other)],
        [(unit.shape, F32), ((2 * PAIRS, D + 128), BF16)],
        name="pack",
        vmem=4,
    )


def squares_of(parts):
    acc = jnp.zeros((8, D), F32)
    for part in parts:
        flat = part.reshape(-1, CHUNK, part.shape[-1])
        for k in range(flat.shape[0]):
            for c in range(0, part.shape[-1], D):
                v = flat[k, :, c : c + D].astype(F32)
                acc = acc + jnp.sum((v * v).reshape(CHUNK // 8, 8, D), axis=0)
    return acc[:, 0:128] + acc[:, 128:256] + acc[:, 256:384]


def wide_squares_kernel(*refs):
    refs[-1][...] = squares_of(refs[:-1])


def squares_kernel(place, *refs):
    parts, (vgrad, before, out) = refs[:-3], refs[-3:]
    acc = squares_of(parts) + before[...]
    row = iota((16, 128), 0)
    low_row = 6 * place[0]
    mine = (row >= low_row) & (row < low_row + 6)
    for j in range(3):
        v = jnp.where(mine, vgrad[16 * j : 16 * j + 16, :].astype(F32), 0.0)
        v = v * v
        acc = acc + (v[0:8] + v[8:16])
    out[...] = acc


def squares(place, parts, vgrad=None, before=None, after=()):
    ins = [(0, p) for p in parts]
    kernel = wide_squares_kernel
    if before is not None:
        ins = [(1, place)] + ins + [(0, vgrad), (0, before)]
        kernel = squares_kernel
    return call(kernel, ins, [((8, 128), F32)], name="squares", vmem=4, after=after)[0]


def merge_kernel(place, igrad, other, out, flag):
    flag[...] = jnp.zeros((8, 128), F32)

    @pl.when(place[0] == 0)
    def low_core():
        out[0:OFF, :] = igrad[0:OFF, :]
        out[OFF:WIN, :] = added(igrad[OFF:WIN, :], other[0 : WIN - OFF, :])
        out[WIN:SEQ, :] = other[WIN - OFF : WIN, :]

    @pl.when(place[0] != 0)
    def high_core():
        out[0:OFF, :] = other[0:OFF, :]
        out[OFF:WIN, :] = added(other[OFF:WIN, :], igrad[0 : WIN - OFF, :])
        out[WIN:SEQ, :] = igrad[WIN - OFF : WIN, :]


def merge(place, igrad, other, after):
    return call(
        merge_kernel,
        [(1, place), (0, igrad), (0, other)],
        [((SEQ, D), BF16), ((8, 128), F32)],
        name="merge",
        vmem=4,
        after=after,
    )


def adamw(parameter, first_state, second, clipped, rate):
    first_new = first_state + (1.0 - BETA_ONE) * clipped
    second_new = second + (1.0 - BETA_TWO) * clipped * clipped
    root = (1.0 - BETA_TWO**STEP) ** 0.5
    below = pl.reciprocal(second_new * lax.rsqrt(second_new) + ADAM_EPS * root)
    scale = rate * root / (1.0 - BETA_ONE**STEP)
    return parameter - scale * (first_new * below), first_new, second_new


def decay_kernel(w, m, v, pv, pm, pq, nw, nm, nv, npv, npm, npq):
    for ins, outs, rate in (
        ((w, m, v), (nw, nm, nv), LEARN_RATE),
        ((pv, pm, pq), (npv, npm, npq), VECTOR_RATE),
    ):
        for ref, out, scale in zip(ins, outs, (1.0 - rate * DECAY_RATE, BETA_ONE, BETA_TWO)):
            out[...] = ref[...] * scale


def decay(arrays, after):
    return call(
        decay_kernel,
        [(0, a) for a in arrays],
        [(a.shape, F32) for a in arrays],
        name="decay",
        vmem=4,
        after=after,
    )


def adamw_kernel(*refs):
    place = Place()
    sums, refs = refs[:2], refs[2:]
    (vgrad, w, m, v, pv, pm, pq), refs = refs[:7], refs[7:]
    wide, low, refs = refs[:4], refs[4:8], refs[8:]
    outs, (npv, npm, npq, norm), scrs, sems = refs[:4], refs[4:8], refs[8:12], refs[12]
    opt = place[0]
    total = sums[0][...] + sums[1][...]
    total = jnp.sum(jnp.sum(total, axis=1, keepdims=True), axis=0, keepdims=True)
    grad_norm = jnp.sqrt(total)
    factor = jnp.minimum(1.0, CLIP_NORM / (grad_norm + 1e-06))
    norm[...] = grad_norm
    for j in range(3):
        cols = slice(128 * j, 128 * j + 128)
        g = vgrad[16 * j : 16 * j + 16, :].astype(F32)
        g = jnp.where(opt == 0, g[0:6], g[6:12])
        a, b, c = adamw(pv[:, cols], pm[:, cols], pq[:, cols], g * factor, VECTOR_RATE)
        npv[:, cols] = a
        npm[:, cols] = b
        npq[:, cols] = c

    def block(grad, rows, cols):
        new = adamw(w[rows, cols], m[rows, cols], v[rows, cols], grad * factor, LEARN_RATE)
        for scr, value in zip(scrs, new + (new[0].astype(BF16),)):
            scr[rows, cols] = value

    def copies(r, i):
        rows = aligned(CHUNK * (place[1] ^ r) + i * 16, 16, 16)
        return [
            pltpu.make_async_copy(scr.at[rows, :], out.at[rows, :], sems.at[3 * r + i, j])
            for j, (scr, out) in enumerate(zip(scrs, outs))
        ]

    for r in range(4):

        def step(i, carry, r=r):
            rows = aligned(CHUNK * (place[1] ^ r) + i * 16, 16, 16)
            here = aligned(i * 16, 16, 16)
            for j in range(4):
                at = D * (place[3] ^ j)
                for p, start in enumerate((4 * D + FF, 4 * D)):
                    grad = wide[r][2 * j + p, here, :].astype(F32)
                    block(grad, rows, aligned(start + at, D, 128))
            for c in range(4):
                grad = low[r][here, D * c : D * c + D].astype(F32)
                block(grad, rows, slice(D * c, D * c + D))
            for copy in copies(r, i):
                copy.start()
            return carry

        lax.fori_loop(0, CHUNK // 16, step, 0)
    for r in range(4):

        def finish(i, carry, r=r):
            for copy in copies(r, i):
                copy.wait()
            return carry

        lax.fori_loop(0, CHUNK // 16, finish, 0)


def update(place, sums, vgrad, w, m, v, pv, pm, pq, parts):
    ins = tuple(sums) + (vgrad, w, m, v, pv, pm, pq) + tuple(parts)
    shapes = [(w.shape, F32)] * 3 + [(w.shape, BF16)] + [(pv.shape, F32)] * 3 + [((1, 1), F32)]
    return pl.pallas_call(
        adamw_kernel,
        out_shape=[jax.ShapeDtypeStruct(s, d) for s, d in shapes],
        in_specs=[VMEM] * len(ins),
        out_specs=[ANY] * 4 + [VMEM] * 4,
        scratch_shapes=[
            pltpu.VMEM(w.shape, F32),
            pltpu.VMEM(w.shape, F32),
            pltpu.VMEM(w.shape, F32),
            pltpu.VMEM(w.shape, BF16),
            pltpu.SemaphoreType.DMA((12, 4)),
        ],
        compiler_params=pltpu.CompilerParams(vmem_limit_bytes=16 << 20),
        cost_estimate=pl.CostEstimate(
            flops=4000000000, bytes_accessed=26 * w.size, transcendentals=0
        ),
        name="adamw",
    )(*ins)


def shards(
    n,
    tokens,
    lengths,
    query_index,
    doc_index,
    targets,
    weights,
    first_moment,
    second_moment,
    vectors,
    vec_first,
    vec_second,
):
    place = None
    scalars = jnp.concatenate([lengths.reshape(SEGS), query_index, doc_index, targets])
    groups = bit_groups(n)

    w_own, wo_own, wu_own, wd_own = cast(weights)
    w_other = pair(w_own)
    vectors_late, w_own = lax.optimization_barrier((vectors, w_own))
    v_other = pair(vectors_late)
    wo = (wo_own, pair(wo_own))
    wu = (wu_own, pair(wu_own))
    wd = (wd_own, pair(wd_own))

    proj, att, lse, segc, segr, ownc, ownr, wanted, marks, vec, wqkv = attend(
        place, scalars, (tokens, w_own, w_other, vectors, v_other)
    )
    xhat1, inv1, hlow, act, up_proj, xhat2, inv2, unit, uscale, wo, wu, wd = mlp(
        place, wanted, att, tokens, ownr, vec, wo + wu + wd
    )
    units, packed = pack(marks, unit, pair(unit))
    groups = bit_groups(n)
    order = [0]
    stack = packed
    for i, (shift, size) in enumerate(groups[1:] + groups[:1]):
        pieces = [stack] + [swap(stack, "dp", n, k << shift) for k in range(1, size)]
        order = [o | (k << shift) for k in range(size) for o in order]
        if i < len(groups) - 1:
            slope = slope_of(up_proj, [packed])
            stack = join(pieces, [slope]).reshape(-1, 2 * PAIRS, D + 128)
    decayed = decay(
        (weights, first_moment, second_moment, vectors, vec_first, vec_second), [packed]
    )
    dsec, dlow, keep, send, dsums = down_backward(
        n, order, place, wanted, units, ownc, uscale, (xhat2, inv2, act), vec, pieces,
        decayed,
    )
    other = pair(send)
    dup, ukeep, usend, usums = up_backward(place, dlow, slope, hlow, wd, [])
    down, go = pair_sum(1, keep, other, [dup])
    dother = swap(go, "dp", n, 1)
    up, go = pair_sum(2, ukeep, pair(usend), [down])
    uother = swap(go, "dp", n, 2)
    dfirst, datt, delta, okeep, osend, fsums = first_backward(
        place, dup, dsec, xhat1, inv1, att, vec, wu, wo, [up]
    )
    ins = (tokens, proj, datt, lse, delta, segc, segr)
    part0, keep0, send0, sums0 = heads_backward(0, place, ins, (), [])
    part1, keep1, send1, sums1 = heads_backward(1, place, ins, (), [part0])
    down, dsend, up, usend = wide_step((down, dother, up, uother), [part1])
    dother, uother = swap(dsend, "dp", n, 2), swap(usend, "dp", n, 1)
    part2, keep, send, _ = heads_backward(
        2, place, ins,
        (okeep, osend, keep0, send0, keep1, send1, dsums, usums, fsums, sums0, sums1),
        [down, part1],
    )
    other = pair(send)
    igrad = input_backward((part0, part1, part2), dfirst, wqkv, [part2])
    wide = wide_plane_sum(place, (down, dother, up, uother), [igrad])
    low = core_sum(keep, other, [wide[0]])
    low_got = trades(low, n, 0)
    wide, first = lax.optimization_barrier((wide, low[0]))
    wide_got = trades(wide, n, 2)
    low = low_plane_sum([first] + low_got[1:], [wide[0]])
    other = swap(low, "dp", n, 4)
    wide = rest_sum(low_plane_sum(wide_got, [low]), n)
    wide_got = trades([wide] * 4, n, 2)
    low = low_next(low, other, [wide])
    other = swap(low, "dp", n, 8)
    igrad, low = lax.optimization_barrier((igrad, low))
    iother = pair(igrad)
    wide = chain(wide_got, [low])
    wide = trades([wide] * 4, n, 0)
    input_grad, flag = merge(place, igrad, iother, [wide[0]])
    low, vgrad = low_last(low, other, [flag])
    low, vgrad = rest_sum(low, n), rest_sum(vgrad, n)
    low = trades([low] * 4, n, 0)
    sums = squares(place, low, vgrad, squares(place, wide, after=[low[0]]))
    sums = (sums, pair(sums))
    pieces = tuple(wide) + tuple(low)
    nw, nm, nv, nlow, npv, npm, npq, norm = update(
        place, sums, vgrad, *decayed, pieces,
    )
    return (norm.reshape(()), input_grad, nw, nm, nv, nlow, npv, npm, npq)


def solution(mesh):
    rows = P("opt", None)
    in_specs = (P("dp", None), P("dp", None), P("dp"), P("dp"), P("dp")) + (rows,) * 6
    out_specs = (P(), P("dp", None)) + (rows,) * 7
    n = mesh.shape["dp"]
    return jax.shard_map(
        functools.partial(shards, n),
        mesh=mesh,
        in_specs=in_specs,
        out_specs=out_specs,
        check_vma=False,
    )
```

```python
import functools

import jax
import jax.numpy as jnp
from jax import lax
from jax.experimental import pallas as pl
from jax.experimental.pallas import tpu as pltpu
from jax.sharding import PartitionSpec as P

D = 384
HEADS = 12
HD = 32
FF = 1536
SEQ = 1024
SEGS = 16
PAIRS = 8
STEP = 10

WIN = 576
OFF = SEQ - WIN
PAD = 640
BLOCK = 128
BANDS = tuple((q, max(0, q - 128), min(WIN, q + 256)) for q in range(0, WIN, BLOCK))
BAND_ROWS = tuple(sum(b[2] - b[1] for b in BANDS[:i]) for i in range(len(BANDS) + 1))
ROWS = 64
WIDE_ROWS = 192
LOG2E = 1.4426950408889634

LN_EPS = 1e-06
POOL_EPS = 1e-06
SCORE_SCALE = 50.0
CLIP_NORM = 0.001
BETA_ONE = 0.9
BETA_TWO = 0.98
ADAM_EPS = 1e-08
LEARN_RATE = 0.05
VECTOR_RATE = 0.3
DECAY_RATE = 0.01
NEG_BIG = -1e30
HALF = D // 2
CHUNK = HALF // 4
EXP2_SCALE = HD ** (-0.5) * 1.4426950408889634

F32 = jnp.float32
BF16 = jnp.bfloat16
VMEM = pl.BlockSpec(memory_space=pltpu.VMEM)
SMEM = pl.BlockSpec(memory_space=pltpu.SMEM)
ANY = pl.BlockSpec(memory_space=pl.ANY)


def nn(a, b):
    return jnp.dot(a, b, preferred_element_type=F32)


def nt(a, b):
    return lax.dot_general(a, b, (((1,), (1,)), ((), ())), preferred_element_type=F32)


def tn(a, b):
    return lax.dot_general(a, b, (((0,), (0,)), ((), ())), preferred_element_type=F32)


def exact(a, b, dims):
    return lax.dot_general(
        a, b, (dims, ((), ())), precision=lax.Precision.HIGHEST, preferred_element_type=F32
    )


def iota(shape, axis):
    return lax.broadcasted_iota(jnp.int32, shape, axis)


def low_pair(value):
    high = value.astype(BF16)
    return high, (value - high.astype(F32)).astype(BF16)


def aligned(start, size, unit):
    return pl.ds(pl.multiple_of(start, unit), size)


def assemble(dst, own, other, opt):
    dst[aligned(HALF * opt, HALF, 64), :] = own[0:HALF, :]
    dst[aligned(HALF * (1 - opt), HALF, 64), :] = other[0:HALF, :]


class Place:
    def __getitem__(self, i):
        if i == 0:
            return lax.axis_index("opt")
        me = lax.axis_index("dp")
        return (me & 3, me, (me >> 2) & 3)[i - 1]


def call(kernel, ins, outs, scratch=(), micros=5, name=None, vmem=12, after=()):
    if ins[0][1] is None:
        kernel = functools.partial(kernel, Place())
        ins = ins[1:]
    specs = [SMEM if s else VMEM for s, _ in ins] + [ANY] * len(after)
    count = len(ins)

    def body(*refs):
        kernel(*refs[:count], *refs[count + len(after) :])

    shapes = [jax.ShapeDtypeStruct(s, d) for s, d in outs]
    moved = sum(a.size * a.dtype.itemsize for _, a in ins)
    moved += sum(s.size * s.dtype.itemsize for s in shapes)
    return pl.pallas_call(
        body,
        out_shape=shapes,
        in_specs=specs,
        out_specs=[VMEM] * len(shapes),
        scratch_shapes=list(scratch),
        compiler_params=pltpu.CompilerParams(vmem_limit_bytes=vmem << 20),
        cost_estimate=pl.CostEstimate(
            flops=micros * 1100000000, bytes_accessed=moved, transcendentals=0
        ),
        name=name,
    )(*[a for _, a in ins], *after)


def head_stack(rows):
    lane_head = iota(rows.shape, 1) // HD
    zero = jnp.zeros_like(rows)
    return jnp.concatenate([jnp.where(lane_head == j, rows, zero) for j in range(4)], axis=0)


def attend_kernel(
    place, scalars, tokens, w_own, w_other, v_own, v_other,
    proj, att, lse, segc, segr, ownc, ownr, wanted, marks, vec, wfull, bias, vt,
):
    opt = place[0]
    assemble(wfull, w_own, w_other, opt)
    mine = v_own[...].astype(BF16).astype(F32)
    others = v_other[...].astype(BF16).astype(F32)
    first = opt == 0
    vec[0:6, :] = jnp.where(first, mine, others)
    vec[6:12, :] = jnp.where(first, others, mine)
    vec[12:16, :] = jnp.zeros((4, D), F32)

    position = iota((8, PAD), 1) + OFF * opt
    segment = jnp.zeros((8, PAD), jnp.int32)
    bound = jnp.int32(0)
    low_count = jnp.int32(0)
    for s in range(SEGS):
        bound = bound + scalars[s]
        segment = segment + (position >= bound).astype(jnp.int32)
        low_count = low_count + (bound <= WIN).astype(jnp.int32)
    mine = (segment < low_count).astype(jnp.int32) == (opt == 0).astype(jnp.int32)
    owned = jnp.where(mine, segment, -1)
    segr[...] = segment
    ownr[...] = owned
    for value, out in ((segment, segc), (owned, ownc)):
        value = value.astype(F32)
        for t in range(PAD // 128):
            rows = min(128, WIN - 128 * t)
            turned = jnp.broadcast_to(value[0:1, 128 * t : 128 * t + 128], (128, 128)).T
            out[128 * t : 128 * t + rows, :] = turned[0:rows].astype(jnp.int32)
    row, col = iota((2 * PAIRS, 128), 0), iota((2 * PAIRS, 128), 1)
    by_row = jnp.zeros((2 * PAIRS, 128), jnp.int32)
    by_col = jnp.zeros((2 * PAIRS, 128), jnp.int32)
    mark = jnp.zeros((2 * PAIRS, 128), jnp.int32)
    for j in range(PAIRS):
        mark = jnp.where(row == j, scalars[SEGS + 2 * PAIRS + j], mark)
        for at in (j, PAIRS + j):
            by_row = jnp.where(row == at, scalars[SEGS + at], by_row)
            by_col = jnp.where(col == at, scalars[SEGS + at], by_col)
    wanted[0] = by_row
    wanted[1] = by_col
    marks[...] = jnp.where(col < 64, mark >> 5, mark & 31).astype(F32).astype(BF16)
    for i, (q0, k0, k1) in enumerate(BANDS):
        bias[BAND_ROWS[i] : BAND_ROWS[i + 1], :] = jnp.where(
            segc[k0:k1, :] == segr[0:1, q0 : q0 + BLOCK], 0.0, NEG_BIG
        )

    x = tokens[aligned(OFF * opt, WIN, 64), :]
    bias_row = jnp.concatenate([vec[0:1, :], jnp.zeros((1, D), F32), vec[1:2, :]], axis=1)
    for first in range(0, 3 * D, 512):
        cols = slice(first, min(first + 512, 3 * D))
        proj[0:WIN, cols] = (nn(x, wfull[:, cols]) + bias_row[:, cols]).astype(BF16)
    proj[WIN:PAD, :] = jnp.zeros((PAD - WIN, 3 * D), BF16)

    def group(g):
        def lanes(part):
            return slice(part * D + 128 * g, part * D + 128 * g + 128)

        for t in range(PAD // 128):
            vt[:, 128 * t : 128 * t + 128] = (
                proj[128 * t : 128 * t + 128, lanes(2)].astype(F32).T.astype(BF16)
            )
        def scores(i):
            q0, k0, k1 = BANDS[i]
            return nt(proj[k0:k1, lanes(1)], head_stack(proj[q0 : q0 + BLOCK, lanes(0)]))

        coming = scores(0)
        for i, (q0, k0, k1) in enumerate(BANDS):
            st = coming
            if i + 1 < len(BANDS):
                coming = scores(i + 1)
            outs, probs, totals = [], [], []
            for j in range(4):
                t = (
                    st[:, j * BLOCK : (j + 1) * BLOCK] * EXP2_SCALE
                    + bias[BAND_ROWS[i] : BAND_ROWS[i + 1], :]
                )
                peak = jnp.max(t, axis=0, keepdims=True)
                powers = jnp.exp2(t - peak)
                total = jnp.sum(powers, axis=0, keepdims=True)
                lse[g, j : j + 1, q0 : q0 + BLOCK] = peak + jnp.log2(total)
                probs.append(powers.astype(BF16))
                totals.append(1.0 / total)
                if j % 2 == 1:
                    o = nn(vt[(j - 1) * HD : (j + 1) * HD, k0:k1], jnp.concatenate(probs[-2:], axis=1))
                    outs.append(o[0:HD, 0:BLOCK] * totals[-2])
                    outs.append(o[HD : 2 * HD, BLOCK : 2 * BLOCK] * totals[-1])
            rows = min(BLOCK, WIN - q0)
            att[q0 : q0 + rows, lanes(0)] = (
                jnp.concatenate(outs, axis=0).T[0:rows].astype(BF16)
            )

    for g in range(3):
        group(g)


def attend(place, scalars, arrays):
    return call(
        attend_kernel,
        [(1, place), (1, scalars)] + [(0, a) for a in arrays],
        [
            ((PAD, 3 * D), BF16),
            ((WIN, D), BF16),
            ((3, 4, PAD), F32),
            ((WIN, 128), jnp.int32),
            ((8, PAD), jnp.int32),
            ((WIN, 128), jnp.int32),
            ((8, PAD), jnp.int32),
            ((2, 2 * PAIRS, 128), jnp.int32),
            ((2 * PAIRS, 128), BF16),
            ((16, D), F32),
            ((D, 3 * D), BF16),
        ],
        [
            pltpu.VMEM((BAND_ROWS[-1], 128), F32),
            pltpu.VMEM((128, PAD), BF16),
        ],
        micros=8,
        name="attend",
    )


def cast_kernel(weights, wq, wo, wu, wd, buffer, sems):
    spans = [(wq, 3 * D), (wo, D), (wu, FF), (wd, FF)]
    copies = [
        pltpu.make_async_copy(
            weights.at[:, i * D : (i + 1) * D], buffer.at[:, i * D : (i + 1) * D], sems.at[i]
        )
        for i in range(12)
    ]
    for copy in copies:
        copy.start()
    at = 0
    for out, width in spans:
        for part in range(width // D):
            copies[at].wait()
            out[:, part * D : (part + 1) * D] = buffer[:, at * D : (at + 1) * D].astype(BF16)
            at += 1


def cast(weights):
    return pl.pallas_call(
        cast_kernel,
        out_shape=[jax.ShapeDtypeStruct((HALF, c), BF16) for c in (3 * D, D, FF, FF)],
        in_specs=[ANY],
        out_specs=[VMEM] * 4,
        scratch_shapes=[pltpu.VMEM(weights.shape, F32), pltpu.SemaphoreType.DMA((12,))],
        compiler_params=pltpu.CompilerParams(vmem_limit_bytes=52 << 20),
        name="cast",
    )(weights)


def bias_of(vec, c):
    first, last = 256 * c, 256 * c + 256
    parts = []
    while first < last:
        row, col = divmod(first, D)
        size = min(D - col, last - first)
        parts.append(vec[3 + row : 4 + row, col : col + size])
        first += size
    return parts[0] if len(parts) == 1 else jnp.concatenate(parts, axis=1)


def mlp_kernel(
    place, wanted, att, tokens, ownr, vec, wo_own, wo_other, wu_own, wu_other,
    wd_own, wd_other, xhat1, inv1, hlow, act, up_proj, xhat2, inv2, unit, uscale, wo, wu, wd,
    ench, encl,
):
    opt = place[0]
    assemble(wo, wo_own, wo_other, opt)
    assemble(wu, wu_own, wu_other, opt)
    assemble(wd, wd_own, wd_other, opt)

    def norm(v):
        centred = v - jnp.mean(v, axis=1, keepdims=True)
        inverse = lax.rsqrt(jnp.mean(centred * centred, axis=1, keepdims=True) + LN_EPS)
        return centred * inverse, inverse

    branch = nn(att[0:WIDE_ROWS, :], wo[...])
    for i in range(WIN // WIDE_ROWS):
        r = slice(i * WIDE_ROWS, (i + 1) * WIDE_ROWS)
        x = tokens[aligned(OFF * opt + i * WIDE_ROWS, WIDE_ROWS, 64), :].astype(F32)
        normed, inverse = norm(branch + vec[2:3, :] + x)
        if i + 1 < WIN // WIDE_ROWS:
            branch = nn(att[(i + 1) * WIDE_ROWS : (i + 2) * WIDE_ROWS, :], wo[...])
        xhat1[r, :] = normed
        inv1[r, :] = jnp.broadcast_to(inverse, (WIDE_ROWS, 128))
        h = normed * vec[8:9, :] + vec[9:10, :]
        low = h.astype(BF16)
        hlow[r, :] = low
        coming = nn(low, wu[:, 0:256])
        for c in range(6):
            cols = slice(c * 256, (c + 1) * 256)
            u = coming + bias_of(vec, c)
            if c < 5:
                coming = nn(low, wu[:, (c + 1) * 256 : (c + 2) * 256])
            up_proj[r, cols] = u
            half = lax.erf(u * 0.7071067811865476) * 0.5 + 0.5
            act[r, cols] = (u * half).astype(BF16)
        normed, inverse = norm(nt(act[r, :], wd[...]) + vec[7:8, :] + h)
        xhat2[r, :] = normed
        inv2[r, :] = jnp.broadcast_to(inverse, (WIDE_ROWS, 128))
        high, rest = low_pair(normed * vec[10:11, :] + vec[11:12, :])
        ench[r, :] = high
        encl[r, :] = rest

    onehot = jnp.where(wanted[0, :, 0:1] == ownr[0:1, 0:WIN], 1.0, 0.0)
    count = jnp.maximum(jnp.sum(onehot, axis=1, keepdims=True), 1.0)
    hot = onehot.astype(BF16)
    pooled = (nn(hot, ench[...]) + nn(hot, encl[...])) / count
    inverse_len = lax.rsqrt(jnp.sum(pooled * pooled, axis=1, keepdims=True) + POOL_EPS)
    unit[...] = pooled * inverse_len
    uscale[...] = jnp.broadcast_to(inverse_len / count, (2 * PAIRS, 128))


def slope_kernel(up_proj, out):
    def block(i, carry):
        r = aligned(i * 16, 16, 16)
        u = up_proj[r, :]
        half = lax.erf(u * 0.7071067811865476) * 0.5 + 0.5
        out[r, :] = half + u * jnp.exp2(u * u * (-0.5 * LOG2E)) * 0.3989422804014327
        return carry

    lax.fori_loop(0, WIN // 16, block, 0)


def slope_of(up_proj, after):
    return call(slope_kernel, [(0, up_proj)], [(up_proj.shape, F32)], name="slope", vmem=4, after=after)[0]


def mlp(place, wanted, att, tokens, ownr, vec, halves):
    return call(
        mlp_kernel,
        [(1, place), (0, wanted), (0, att), (0, tokens), (0, ownr), (0, vec)]
        + [(0, h) for h in halves],
        [
            ((WIN, D), F32),
            ((WIN, 128), F32),
            ((WIN, D), BF16),
            ((WIN, FF), BF16),
            ((WIN, FF), F32),
            ((WIN, D), F32),
            ((WIN, 128), F32),
            ((2 * PAIRS, D), F32),
            ((2 * PAIRS, 128), F32),
            ((D, D), BF16),
            ((D, FF), BF16),
            ((D, FF), BF16),
        ],
        [
            pltpu.VMEM((WIN, D), BF16),
            pltpu.VMEM((WIN, D), BF16),
        ],
        micros=10,
        name="mlp",
    )


def split_rows(grad, keep, send, place, *at):
    opt = place[0]
    for c in range(4):
        index = (c ^ place[1],) + at
        keep[index] = grad[aligned(HALF * opt + CHUNK * c, CHUNK, 16), :].astype(BF16)
        send[index] = grad[aligned(HALF * (1 - opt) + CHUNK * c, CHUNK, 16), :].astype(BF16)


def column_sums(value):
    return jnp.sum(value.reshape(-1, 8, D), axis=0)


def norm_backward(grad_at, normed_ref, inverse_ref, gain, out, low_out, sums, at, step=ROWS):
    def block(i, carry):
        scale_sum, shift_sum, bias_sum = carry
        r = aligned(i * step, step, 64)
        g = grad_at(r)
        normed = normed_ref[r, :]
        scaled = g * gain
        inner = (
            scaled
            - jnp.mean(scaled, axis=1, keepdims=True)
            - normed * jnp.mean(scaled * normed, axis=1, keepdims=True)
        ) * inverse_ref[r, 0:1]
        out[r, :] = inner
        low_out[r, :] = inner.astype(BF16)
        return (
            scale_sum + column_sums(g * normed),
            shift_sum + column_sums(g),
            bias_sum + column_sums(inner),
        )

    zero = jnp.zeros((8, D), F32)
    scale_sum, shift_sum, bias_sum = lax.fori_loop(0, WIN // step, block, (zero, zero, zero))
    sums[at : at + 1, :] = jnp.sum(bias_sum, axis=0, keepdims=True)
    sums[at + 1 : at + 2, :] = jnp.sum(scale_sum, axis=0, keepdims=True)
    sums[at + 2 : at + 3, :] = jnp.sum(shift_sum, axis=0, keepdims=True)


def down_kernel(
    place, count, order, wanted, units, ownc, uscale, xhat2, inv2, act, vec, *rest
):
    pieces, (dsec, dlow, keep, send, sums, queries, docs, marks, grad) = rest[:-9], rest[-9:]
    me = place[2]
    per = pieces[0].shape[0]
    for p, piece in enumerate(pieces):
        for j in range(per):
            at = order[p * per + j]
            r = slice(at * PAIRS, (at + 1) * PAIRS)
            both = piece[j].astype(F32)
            queries[r, :] = both[0:PAIRS, 0:D]
            docs[r, :] = both[PAIRS : 2 * PAIRS, 0:D]
            marks[r, :] = both[0:PAIRS, D : D + 128]
    total = count * PAIRS
    q = queries[...].astype(BF16)
    d = docs[...].astype(BF16)
    logits = SCORE_SCALE * nt(q, d)
    peak = jnp.max(logits, axis=1, keepdims=True)
    powers = jnp.exp(logits - peak)
    soft = powers / jnp.sum(powers, axis=1, keepdims=True)
    col = iota((total, total), 1)
    doc_id = ((col // PAIRS) ^ me) * PAIRS + lax.rem(col, PAIRS)
    hit = (marks[:, 0:1] * 32.0 + marks[:, 64:65]).astype(jnp.int32) == doc_id
    d_logits = (soft - jnp.where(hit, 1.0, 0.0)) * (SCORE_SCALE / total)
    high, rest_low = low_pair(d_logits[0:PAIRS, :])
    d_q = nn(high, d) + nn(rest_low, d)
    high, rest_low = low_pair(d_logits[:, 0:128].T[0:PAIRS, :])
    d_d = nn(high, q) + nn(rest_low, q)
    d_units = jnp.concatenate([d_q, d_d], axis=0)
    u = units[...]
    d_pool = uscale[:, 0:1] * (d_units - u * jnp.sum(u * d_units, axis=1, keepdims=True))
    hot = jnp.where(ownc[:, 0 : 2 * PAIRS] == wanted[1, 0:1, 0 : 2 * PAIRS], 1.0, 0.0).astype(BF16)
    high, rest_low = low_pair(d_pool)
    dsec[...] = nn(hot, high) + nn(hot, rest_low)
    norm_backward(
        lambda r: dsec[r, :], xhat2, inv2, vec[10:11, :], dsec, dlow, sums, 0, WIDE_ROWS
    )
    sums[3:8, :] = jnp.zeros((5, D), F32)
    halves = [slice(0, 2 * D), slice(2 * D, 4 * D)]
    grad[:, halves[0]] = tn(dlow[...], act[:, halves[0]])
    grad[:, halves[1]] = tn(dlow[...], act[:, halves[1]])
    for c in range(4):
        split_rows(grad.at[:, c * D : (c + 1) * D], keep, send, place, c)


def down_backward(count, order, place, wanted, units, ownc, uscale, saved, vec, pieces, after):
    total = count * PAIRS
    return call(
        lambda place, *refs: down_kernel(place, count, order, *refs),
        [(1, place), (0, wanted), (0, units), (0, ownc), (0, uscale)]
        + [(0, s) for s in saved]
        + [(0, vec)]
        + [(0, p) for p in pieces],
        [
            ((WIN, D), F32),
            ((WIN, D), BF16),
            ((4, 4, CHUNK, D), BF16),
            ((4, 4, CHUNK, D), BF16),
            ((8, D), F32),
        ],
        [
            pltpu.VMEM((total, D), F32),
            pltpu.VMEM((total, D), F32),
            pltpu.VMEM((total, 128), F32),
            pltpu.VMEM((D, FF), F32),
        ],
        micros=4,
        name="down_backward",
        after=after,
    )


def up_kernel(place, dlow, slope, hlow, wd, dup, keep, send, sums, grad):
    coming = nn(dlow[...], wd[:, 0 : 2 * D])
    for c in range(2):
        cols = slice(c * 2 * D, (c + 1) * 2 * D)
        part = (coming * slope[:, cols]).astype(BF16)
        if c == 0:
            coming = nn(dlow[...], wd[:, 2 * D : 4 * D])
        dup[:, cols] = part
        column_sum = jnp.sum(part.astype(F32), axis=0, keepdims=True)
        for j in range(2):
            sums[2 * c + j : 2 * c + j + 1, :] = column_sum[:, j * D : (j + 1) * D]
        grad[:, cols] = tn(hlow[...], dup[:, cols])
    for c in range(4):
        split_rows(grad.at[:, c * D : (c + 1) * D], keep, send, place, c)


def up_backward(place, dlow, slope, hlow, wd, after):
    return call(
        up_kernel,
        [(1, place)] + [(0, a) for a in (dlow, slope, hlow, wd)],
        [((WIN, FF), BF16), ((4, 4, CHUNK, D), BF16), ((4, 4, CHUNK, D), BF16), ((4, D), F32)],
        [pltpu.VMEM((D, FF), F32)],
        micros=3,
        name="up_backward",
        after=after,
    )


def first_kernel(
    place, dup, dsec, xhat1, inv1, att, vec, wu, wo,
    dfirst, datt, delta, okeep, osend, sums, grad, dlow,
):
    steps = [slice(i, i + WIDE_ROWS) for i in range(0, WIN, WIDE_ROWS)]
    coming = nt(dup[steps[0], :], wu[...])
    gain = vec[8:9, :]
    totals = None
    for i, r in enumerate(steps):
        g = coming + dsec[r, :]
        if i + 1 < len(steps):
            coming = nt(dup[steps[i + 1], :], wu[...])
        normed = xhat1[r, :]
        scaled = g * gain
        inner = (
            scaled
            - jnp.mean(scaled, axis=1, keepdims=True)
            - normed * jnp.mean(scaled * normed, axis=1, keepdims=True)
        ) * inv1[r, 0:1]
        dfirst[r, :] = inner
        dlow[r, :] = inner.astype(BF16)
        new = [column_sums(inner), column_sums(g * normed), column_sums(g)]
        totals = new if totals is None else [a + b for a, b in zip(totals, new)]
    for i, total in enumerate(totals):
        sums[i : i + 1, :] = jnp.sum(total, axis=0, keepdims=True)
    sums[3:8, :] = jnp.zeros((5, D), F32)
    grad[...] = tn(att[...], dlow[...])
    split_rows(grad, okeep, osend, place)
    da = nt(dlow[...], wo[...]).astype(BF16)
    datt[0:WIN, :] = da
    datt[WIN:PAD, :] = jnp.zeros((PAD - WIN, D), BF16)
    high, rest = low_pair(da.astype(F32) * att[...].astype(F32))
    heads = (iota((16, D), 1) // HD == iota((16, D), 0)).astype(F32).astype(BF16)
    delta[:, 0:WIN] = nt(heads, high) + nt(heads, rest)
    delta[:, WIN:PAD] = jnp.zeros((16, PAD - WIN), F32)


def first_backward(place, dup, dsec, xhat1, inv1, att, vec, wu, wo, after):
    return call(
        first_kernel,
        [(1, place)] + [(0, a) for a in (dup, dsec, xhat1, inv1, att, vec, wu, wo)],
        [
            ((WIN, D), F32),
            ((PAD, D), BF16),
            ((16, PAD), F32),
            ((4, CHUNK, D), BF16),
            ((4, CHUNK, D), BF16),
            ((8, D), F32),
        ],
        [
            pltpu.VMEM((D, D), F32),
            pltpu.VMEM((WIN, D), BF16),
        ],
        micros=1,
        name="first_backward",
        after=after,
    )


def heads_kernel(place, g, tokens, proj, datt, lse, delta, segc, segr, *rest):
    rest, (dproj, keep, send, sums, kt, dk, dv, grad, ktmp, stmp) = rest[:-10], rest[-10:]

    def lanes(part):
        return slice(part * D + 128 * g, part * D + 128 * g + 128)

    for t in range(PAD // 128):
        kt[:, 128 * t : 128 * t + 128] = (
            proj[128 * t : 128 * t + 128, lanes(1)].astype(F32).T.astype(BF16)
        )
    dk[...] = jnp.zeros_like(dk)
    dv[...] = jnp.zeros_like(dv)

    def products(i):
        q0, k0, k1 = BANDS[i]
        qs = head_stack(proj[q0 : q0 + BLOCK, lanes(0)])
        gs = head_stack(datt[q0 : q0 + BLOCK, lanes(0)])
        return qs, gs, nt(proj[k0:k1, lanes(1)], qs), nt(proj[k0:k1, lanes(2)], gs)

    coming = products(0)
    for i, (q0, k0, k1) in enumerate(BANDS):
        qs, gs, st, dp = coming
        if i + 1 < len(BANDS):
            coming = products(i + 1)
        same = segc[k0:k1, :] == segr[0:1, q0 : q0 + BLOCK]
        bias = jnp.where(same, 0.0, NEG_BIG)
        probs, d_scores, dq = [], [], []
        for j in range(4):
            cols = slice(j * BLOCK, (j + 1) * BLOCK)
            prob = jnp.exp2(st[:, cols] * EXP2_SCALE + bias - lse[g, j : j + 1, q0 : q0 + BLOCK])
            ds = prob * (dp[:, cols] - delta[4 * g + j : 4 * g + j + 1, q0 : q0 + BLOCK])
            ds = ds.astype(BF16)
            probs.append(prob.astype(BF16))
            d_scores.append(ds)
            if j % 2 == 1:
                part = nn(
                    kt[(j - 1) * HD : (j + 1) * HD, k0:k1], jnp.concatenate(d_scores[-2:], axis=1)
                )
                dq.append(part[0:HD, 0:BLOCK])
                dq.append(part[HD : 2 * HD, BLOCK : 2 * BLOCK])
        dv[k0:k1, :] += nn(jnp.concatenate(probs, axis=1), gs)
        dk[k0:k1, :] += nn(jnp.concatenate(d_scores, axis=1), qs)
        rows = min(BLOCK, WIN - q0)
        dqs = jnp.concatenate(dq, axis=0).T[0:rows] * HD ** (-0.5)
        dproj[q0 : q0 + rows, 0:128] = dqs.astype(BF16)
    dproj[:, 128:256] = (dk[...] * HD ** (-0.5)).astype(BF16)
    dproj[:, 256:384] = dv[...].astype(BF16)
    grad[...] = tn(tokens[aligned(OFF * place[0], WIN, 64), :], dproj[...])
    q_sum = jnp.sum(dproj[:, 0:128].astype(F32), axis=0, keepdims=True)
    v_sum = jnp.sum(dproj[:, 256:384].astype(F32), axis=0, keepdims=True)
    sums[0:1, :] = q_sum
    sums[1:2, :] = v_sum
    sums[2:8, :] = jnp.zeros((6, 128), F32)
    if g < 2:
        split_rows(grad, keep, send, place)
        return
    parts, (dsums, usums, fsums, zero, one) = rest[:6], rest[6:]
    split_rows(grad, ktmp, stmp, place)
    for dst, out_part, blocks in (
        (keep, parts[0], (parts[2], parts[4], ktmp)),
        (send, parts[1], (parts[3], parts[5], stmp)),
    ):
        dst[:, :, 3 * D : 4 * D] = out_part[...]
        for h, part in enumerate(blocks):
            for c in range(3):
                dst[:, :, D * c + 128 * h : D * c + 128 * h + 128] = part[
                    :, :, 128 * c : 128 * c + 128
                ]
    rows = jnp.concatenate(
        [
            jnp.concatenate([zero[0:1], one[0:1], q_sum], axis=1),
            jnp.concatenate([zero[1:2], one[1:2], v_sum], axis=1),
            fsums[0:1, :],
            usums[0:4, :],
            dsums[0:1, :],
            fsums[1:3, :],
            dsums[1:3, :],
            jnp.zeros((4, D), F32),
        ],
        axis=0,
    ).astype(BF16)
    for c in range(4):
        for j in range(3):
            block = rows[:, 128 * j : 128 * j + 128]
            keep[c, 16 * j : 16 * j + 16, 4 * D : 4 * D + 128] = block
            send[c, 16 * j : 16 * j + 16, 4 * D : 4 * D + 128] = block


def heads_backward(g, place, ins, more, after):
    part = ((4, CHUNK, 4 * D + 128 if g == 2 else D), BF16)
    return call(
        lambda place, *refs: heads_kernel(place, g, *refs),
        [(1, place)] + [(0, a) for a in tuple(ins) + tuple(more)],
        [((WIN, D), BF16), part, part, ((8, 128), F32)],
        [
            pltpu.VMEM((128, PAD), BF16),
            pltpu.VMEM((WIN, 128), F32),
            pltpu.VMEM((WIN, 128), F32),
            pltpu.VMEM((D, D), F32),
            pltpu.VMEM((4, CHUNK, D), BF16),
            pltpu.VMEM((4, CHUNK, D), BF16),
        ],
        micros=1,
        name="heads_backward",
        after=after,
    )


def input_kernel(dp0, dp1, dp2, dfirst, wfull, igrad, dproj):
    for g, part in enumerate((dp0, dp1, dp2)):
        for c in range(3):
            dproj[:, c * D + 128 * g : c * D + 128 * g + 128] = part[:, 128 * c : 128 * c + 128]
    igrad[...] = (nt(dproj[...], wfull[...]) + dfirst[...]).astype(BF16)


def input_backward(parts, dfirst, wqkv, after):
    return call(
        input_kernel,
        [(0, a) for a in tuple(parts) + (dfirst, wqkv)],
        [((WIN, D), BF16)],
        [pltpu.VMEM((WIN, 3 * D), BF16)],
        micros=2,
        name="input_backward",
        after=after,
    )[0]


def flips(axis, size, bits):
    return [(i, i ^ bits) for i in range(size)]


def pair(value):
    return swap(value, "opt", 2, 1)


def swap(value, axis, size, bits):
    return lax.ppermute(value, axis, flips(axis, size, bits))


def bit_groups(size):
    bits = size.bit_length() - 1
    return [(s, 1 << min(2, bits - s)) for s in range(0, bits, 2)]


def trades(values, n, shift):
    return [values[0]] + [swap(values[k], "dp", n, k << shift) for k in (1, 2, 3)]


def added(a, b):
    return (a.astype(F32) + b.astype(F32)).astype(BF16)


def core_sum_kernel(keep, other, *outs):
    for r, out in enumerate(outs):
        out[...] = added(keep[r], other[r])


def core_sum(keep, other, after):
    return call(
        core_sum_kernel,
        [(0, keep), (0, other)],
        [(keep.shape[1:], BF16)] * 4,
        name="core_sum",
        vmem=4,
        after=after,
    )


def pair_sum_kernel(bit, keep, other, stay, go):
    for i, r in enumerate((0, 3 - bit)):
        stay[i] = added(keep[r], other[r])
        go[i] = added(keep[r + bit], other[r + bit])


def pair_sum(bit, keep, other, after):
    return call(
        functools.partial(pair_sum_kernel, bit),
        [(0, keep), (0, other)],
        [((2,) + keep.shape[1:], BF16)] * 2,
        name="pair_sum",
        vmem=4,
        after=after,
    )


def wide_step_kernel(down, dother, up, uother, dkeep, dsend, ukeep, usend):
    dkeep[...] = added(down[0], dother[0])
    dsend[...] = added(down[1], dother[1])
    ukeep[...] = added(up[0], uother[0])
    usend[...] = added(up[1], uother[1])


def wide_step(parts, after):
    return call(
        wide_step_kernel,
        [(0, p) for p in parts],
        [((4, CHUNK, D), BF16)] * 4,
        name="wide_step",
        vmem=4,
        after=after,
    )


def total_of(refs, at):
    a, b, c, d = (ref[at].astype(F32) for ref in refs)
    return ((a + b) + (c + d)).astype(BF16)


def wide_plane_kernel(place, down, dother, up, uother, *outs):
    for k, out in enumerate(outs):
        at = place[3] ^ k
        out[0] = added(down[at], dother[at])
        out[1] = added(up[at], uother[at])


def wide_plane_sum(place, parts, after):
    return call(
        wide_plane_kernel,
        [(1, place)] + [(0, p) for p in parts],
        [((2, CHUNK, D), BF16)] * 4,
        name="wide_plane_sum",
        vmem=4,
        after=after,
    )


def low_plane_kernel(a, b, c, d, out):
    out[...] = total_of((a, b, c, d), slice(None))


def low_plane_sum(parts, after=()):
    return call(
        low_plane_kernel,
        [(0, p) for p in parts],
        [(parts[0].shape, BF16)],
        name="low_plane_sum",
        vmem=4,
        after=after,
    )[0]


def low_next_kernel(keep, other, out):
    out[...] = added(keep[...], other[...])


def low_next(keep, other, after=()):
    return call(
        low_next_kernel,
        [(0, keep), (0, other)],
        [(keep.shape, BF16)],
        name="low_next",
        vmem=4,
        after=after,
    )[0]


def low_last_kernel(keep, other, out, vgrad):
    out[...] = added(keep[:, 0 : 4 * D], other[:, 0 : 4 * D])
    vgrad[...] = added(keep[:, 4 * D : 4 * D + 128], other[:, 4 * D : 4 * D + 128])


def low_last(keep, other, after):
    return call(
        low_last_kernel,
        [(0, keep), (0, other)],
        [((CHUNK, 4 * D), BF16), ((CHUNK, 128), BF16)],
        name="low_last",
        vmem=4,
        after=after,
    )


def chain_kernel(*refs):
    ins, out = refs[:-1], refs[-1]
    at = 0
    for ref in ins:
        flat = ref.reshape(-1, CHUNK, D)
        out[at : at + flat.shape[0]] = flat[...]
        at += flat.shape[0]


def chain(parts, after=()):
    count = sum(p.size for p in parts) // (CHUNK * D)
    return call(
        chain_kernel,
        [(0, p) for p in parts],
        [((count, CHUNK, D), BF16)],
        name="chain",
        vmem=4,
        after=after,
    )[0]


def rest_sum(value, n):
    bit = 16
    while bit < n:
        other = swap(value, "dp", n, bit)
        value = (value.astype(F32) + other.astype(F32)).astype(BF16)
        bit *= 2
    return value


def join_kernel(*refs):
    ins, out = refs[:-1], refs[-1]
    for i, ref in enumerate(ins):
        out[i] = ref[...]


def join(parts, after=()):
    return call(
        join_kernel,
        [(0, p) for p in parts],
        [((len(parts),) + parts[0].shape, parts[0].dtype)],
        name="join",
        vmem=4,
        after=after,
    )[0]


def pack_kernel(marks, unit, other, units, packed):
    both = unit[...] + other[...]
    units[...] = both
    packed[:, 0:D] = both.astype(BF16)
    packed[:, D : D + 128] = marks[...]


def pack(marks, unit, other):
    return call(
        pack_kernel,
        [(0, marks), (0, unit), (0, other)],
        [(unit.shape, F32), ((2 * PAIRS, D + 128), BF16)],
        name="pack",
        vmem=4,
    )


def squares_of(parts):
    acc = jnp.zeros((8, D), F32)
    for part in parts:
        flat = part.reshape(-1, CHUNK, part.shape[-1])
        for k in range(flat.shape[0]):
            for c in range(0, part.shape[-1], D):
                v = flat[k, :, c : c + D].astype(F32)
                acc = acc + jnp.sum((v * v).reshape(CHUNK // 8, 8, D), axis=0)
    return acc[:, 0:128] + acc[:, 128:256] + acc[:, 256:384]


def wide_squares_kernel(*refs):
    refs[-1][...] = squares_of(refs[:-1])


def squares_kernel(place, *refs):
    parts, (vgrad, before, out) = refs[:-3], refs[-3:]
    acc = squares_of(parts) + before[...]
    row = iota((16, 128), 0)
    low_row = 6 * place[0]
    mine = (row >= low_row) & (row < low_row + 6)
    for j in range(3):
        v = jnp.where(mine, vgrad[16 * j : 16 * j + 16, :].astype(F32), 0.0)
        v = v * v
        acc = acc + (v[0:8] + v[8:16])
    out[...] = acc


def squares(place, parts, vgrad=None, before=None, after=()):
    ins = [(0, p) for p in parts]
    kernel = wide_squares_kernel
    if before is not None:
        ins = [(1, place)] + ins + [(0, vgrad), (0, before)]
        kernel = squares_kernel
    return call(kernel, ins, [((8, 128), F32)], name="squares", vmem=4, after=after)[0]


def merge_kernel(place, igrad, other, out, flag):
    flag[...] = jnp.zeros((8, 128), F32)

    @pl.when(place[0] == 0)
    def low_core():
        out[0:OFF, :] = igrad[0:OFF, :]
        out[OFF:WIN, :] = added(igrad[OFF:WIN, :], other[0 : WIN - OFF, :])
        out[WIN:SEQ, :] = other[WIN - OFF : WIN, :]

    @pl.when(place[0] != 0)
    def high_core():
        out[0:OFF, :] = other[0:OFF, :]
        out[OFF:WIN, :] = added(other[OFF:WIN, :], igrad[0 : WIN - OFF, :])
        out[WIN:SEQ, :] = igrad[WIN - OFF : WIN, :]


def merge(place, igrad, other, after):
    return call(
        merge_kernel,
        [(1, place), (0, igrad), (0, other)],
        [((SEQ, D), BF16), ((8, 128), F32)],
        name="merge",
        vmem=4,
        after=after,
    )


def adamw(parameter, first_state, second, clipped, rate):
    first_new = first_state + (1.0 - BETA_ONE) * clipped
    second_new = second + (1.0 - BETA_TWO) * clipped * clipped
    root = (1.0 - BETA_TWO**STEP) ** 0.5
    below = pl.reciprocal(second_new * lax.rsqrt(second_new) + ADAM_EPS * root)
    scale = rate * root / (1.0 - BETA_ONE**STEP)
    return parameter - scale * (first_new * below), first_new, second_new


def decay_kernel(w, m, v, pv, pm, pq, nw, nm, nv, npv, npm, npq):
    for ins, outs, rate in (
        ((w, m, v), (nw, nm, nv), LEARN_RATE),
        ((pv, pm, pq), (npv, npm, npq), VECTOR_RATE),
    ):
        for ref, out, scale in zip(ins, outs, (1.0 - rate * DECAY_RATE, BETA_ONE, BETA_TWO)):
            out[...] = ref[...] * scale


def decay(arrays, after):
    return call(
        decay_kernel,
        [(0, a) for a in arrays],
        [(a.shape, F32) for a in arrays],
        name="decay",
        vmem=4,
        after=after,
    )


def adamw_kernel(*refs):
    place = Place()
    sums, refs = refs[:2], refs[2:]
    (vgrad, w, m, v, pv, pm, pq), refs = refs[:7], refs[7:]
    wide, low, refs = refs[:4], refs[4:8], refs[8:]
    outs, (npv, npm, npq, norm), scrs, sems = refs[:4], refs[4:8], refs[8:12], refs[12]
    opt = place[0]
    total = sums[0][...] + sums[1][...]
    total = jnp.sum(jnp.sum(total, axis=1, keepdims=True), axis=0, keepdims=True)
    grad_norm = jnp.sqrt(total)
    factor = jnp.minimum(1.0, CLIP_NORM / (grad_norm + 1e-06))
    norm[...] = grad_norm
    for j in range(3):
        cols = slice(128 * j, 128 * j + 128)
        g = vgrad[16 * j : 16 * j + 16, :].astype(F32)
        g = jnp.where(opt == 0, g[0:6], g[6:12])
        a, b, c = adamw(pv[:, cols], pm[:, cols], pq[:, cols], g * factor, VECTOR_RATE)
        npv[:, cols] = a
        npm[:, cols] = b
        npq[:, cols] = c

    def block(grad, rows, cols):
        new = adamw(w[rows, cols], m[rows, cols], v[rows, cols], grad * factor, LEARN_RATE)
        for scr, value in zip(scrs, new + (new[0].astype(BF16),)):
            scr[rows, cols] = value

    def copies(r, i):
        rows = aligned(CHUNK * (place[1] ^ r) + i * 16, 16, 16)
        return [
            pltpu.make_async_copy(scr.at[rows, :], out.at[rows, :], sems.at[3 * r + i, j])
            for j, (scr, out) in enumerate(zip(scrs, outs))
        ]

    for r in range(4):

        def step(i, carry, r=r):
            rows = aligned(CHUNK * (place[1] ^ r) + i * 16, 16, 16)
            here = aligned(i * 16, 16, 16)
            for j in range(4):
                at = D * (place[3] ^ j)
                for p, start in enumerate((4 * D + FF, 4 * D)):
                    grad = wide[r][2 * j + p, here, :].astype(F32)
                    block(grad, rows, aligned(start + at, D, 128))
            for c in range(4):
                grad = low[r][here, D * c : D * c + D].astype(F32)
                block(grad, rows, slice(D * c, D * c + D))
            for copy in copies(r, i):
                copy.start()
            return carry

        lax.fori_loop(0, CHUNK // 16, step, 0)
    for r in range(4):

        def finish(i, carry, r=r):
            for copy in copies(r, i):
                copy.wait()
            return carry

        lax.fori_loop(0, CHUNK // 16, finish, 0)


def update(place, sums, vgrad, w, m, v, pv, pm, pq, parts):
    ins = tuple(sums) + (vgrad, w, m, v, pv, pm, pq) + tuple(parts)
    shapes = [(w.shape, F32)] * 3 + [(w.shape, BF16)] + [(pv.shape, F32)] * 3 + [((1, 1), F32)]
    return pl.pallas_call(
        adamw_kernel,
        out_shape=[jax.ShapeDtypeStruct(s, d) for s, d in shapes],
        in_specs=[VMEM] * len(ins),
        out_specs=[ANY] * 4 + [VMEM] * 4,
        scratch_shapes=[
            pltpu.VMEM(w.shape, F32),
            pltpu.VMEM(w.shape, F32),
            pltpu.VMEM(w.shape, F32),
            pltpu.VMEM(w.shape, BF16),
            pltpu.SemaphoreType.DMA((12, 4)),
        ],
        compiler_params=pltpu.CompilerParams(vmem_limit_bytes=16 << 20),
        cost_estimate=pl.CostEstimate(
            flops=4000000000, bytes_accessed=26 * w.size, transcendentals=0
        ),
        name="adamw",
    )(*ins)


def shards(
    n,
    tokens,
    lengths,
    query_index,
    doc_index,
    targets,
    weights,
    first_moment,
    second_moment,
    vectors,
    vec_first,
    vec_second,
):
    place = None
    scalars = jnp.concatenate([lengths.reshape(SEGS), query_index, doc_index, targets])
    groups = bit_groups(n)

    w_own, wo_own, wu_own, wd_own = cast(weights)
    w_other = pair(w_own)
    vectors_late, w_own = lax.optimization_barrier((vectors, w_own))
    v_other = pair(vectors_late)
    wo = (wo_own, pair(wo_own))
    wu = (wu_own, pair(wu_own))
    wd = (wd_own, pair(wd_own))

    proj, att, lse, segc, segr, ownc, ownr, wanted, marks, vec, wqkv = attend(
        place, scalars, (tokens, w_own, w_other, vectors, v_other)
    )
    xhat1, inv1, hlow, act, up_proj, xhat2, inv2, unit, uscale, wo, wu, wd = mlp(
        place, wanted, att, tokens, ownr, vec, wo + wu + wd
    )
    units, packed = pack(marks, unit, pair(unit))
    groups = bit_groups(n)
    order = [0]
    stack = packed
    for i, (shift, size) in enumerate(groups[1:] + groups[:1]):
        pieces = [stack] + [swap(stack, "dp", n, k << shift) for k in range(1, size)]
        order = [o | (k << shift) for k in range(size) for o in order]
        if i < len(groups) - 1:
            slope = slope_of(up_proj, [packed])
            stack = join(pieces, [slope]).reshape(-1, 2 * PAIRS, D + 128)
    decayed = decay(
        (weights, first_moment, second_moment, vectors, vec_first, vec_second), [packed]
    )
    dsec, dlow, keep, send, dsums = down_backward(
        n, order, place, wanted, units, ownc, uscale, (xhat2, inv2, act), vec, pieces,
        decayed,
    )
    other = pair(send)
    dup, ukeep, usend, usums = up_backward(place, dlow, slope, hlow, wd, [])
    down, go = pair_sum(1, keep, other, [dup])
    dother = swap(go, "dp", n, 1)
    up, go = pair_sum(2, ukeep, pair(usend), [down])
    uother = swap(go, "dp", n, 2)
    dfirst, datt, delta, okeep, osend, fsums = first_backward(
        place, dup, dsec, xhat1, inv1, att, vec, wu, wo, [up]
    )
    ins = (tokens, proj, datt, lse, delta, segc, segr)
    part0, keep0, send0, sums0 = heads_backward(0, place, ins, (), [])
    part1, keep1, send1, sums1 = heads_backward(1, place, ins, (), [part0])
    down, dsend, up, usend = wide_step((down, dother, up, uother), [part1])
    dother, uother = swap(dsend, "dp", n, 2), swap(usend, "dp", n, 1)
    part2, keep, send, _ = heads_backward(
        2, place, ins,
        (okeep, osend, keep0, send0, keep1, send1, dsums, usums, fsums, sums0, sums1),
        [down, part1],
    )
    other = pair(send)
    igrad = input_backward((part0, part1, part2), dfirst, wqkv, [part2])
    iother = pair(igrad)
    wide = wide_plane_sum(place, (down, dother, up, uother), [igrad])
    wide_got = trades(wide, n, 2)
    low = core_sum(keep, other, [wide[0]])
    low_got = trades(low, n, 0)
    wide = rest_sum(low_plane_sum(wide_got, [low[0]]), n)
    wide_got = trades([wide] * 4, n, 2)
    low = low_plane_sum(low_got, [wide])
    other = swap(low, "dp", n, 4)
    wide = chain(wide_got, [low])
    wide = trades([wide] * 4, n, 0)
    low = low_next(low, other, [wide[0]])
    other = swap(low, "dp", n, 8)
    input_grad, flag = merge(place, igrad, iother, [low])
    low, vgrad = low_last(low, other, [flag])
    low, vgrad = rest_sum(low, n), rest_sum(vgrad, n)
    low = trades([low] * 4, n, 0)
    sums = squares(place, low, vgrad, squares(place, wide, after=[low[0]]))
    sums = (sums, pair(sums))
    pieces = tuple(wide) + tuple(low)
    nw, nm, nv, nlow, npv, npm, npq, norm = update(
        place, sums, vgrad, *decayed, pieces,
    )
    return (norm.reshape(()), input_grad, nw, nm, nv, nlow, npv, npm, npq)


def solution(mesh):
    rows = P("opt", None)
    in_specs = (P("dp", None), P("dp", None), P("dp"), P("dp"), P("dp")) + (rows,) * 6
    out_specs = (P(), P("dp", None)) + (rows,) * 7
    n = mesh.shape["dp"]
    return jax.shard_map(
        functools.partial(shards, n),
        mesh=mesh,
        in_specs=in_specs,
        out_specs=out_specs,
        check_vma=False,
    )
```

```python
import functools

import jax
import jax.numpy as jnp
from jax import lax
from jax.experimental import pallas as pl
from jax.experimental.pallas import tpu as pltpu
from jax.sharding import PartitionSpec as P

D = 384
HEADS = 12
HD = 32
FF = 1536
SEQ = 1024
SEGS = 16
PAIRS = 8
STEP = 10

WIN = 576
OFF = SEQ - WIN
PAD = 640
BLOCK = 128
BANDS = tuple((q, max(0, q - 128), min(WIN, q + 256)) for q in range(0, WIN, BLOCK))
BAND_ROWS = tuple(sum(b[2] - b[1] for b in BANDS[:i]) for i in range(len(BANDS) + 1))
ROWS = 64
WIDE_ROWS = 192
LOG2E = 1.4426950408889634

LN_EPS = 1e-06
POOL_EPS = 1e-06
SCORE_SCALE = 50.0
CLIP_NORM = 0.001
BETA_ONE = 0.9
BETA_TWO = 0.98
ADAM_EPS = 1e-08
LEARN_RATE = 0.05
VECTOR_RATE = 0.3
DECAY_RATE = 0.01
NEG_BIG = -1e30
HALF = D // 2
CHUNK = HALF // 4
EXP2_SCALE = HD ** (-0.5) * 1.4426950408889634

F32 = jnp.float32
BF16 = jnp.bfloat16
VMEM = pl.BlockSpec(memory_space=pltpu.VMEM)
SMEM = pl.BlockSpec(memory_space=pltpu.SMEM)
ANY = pl.BlockSpec(memory_space=pl.ANY)


def nn(a, b):
    return jnp.dot(a, b, preferred_element_type=F32)


def nt(a, b):
    return lax.dot_general(a, b, (((1,), (1,)), ((), ())), preferred_element_type=F32)


def tn(a, b):
    return lax.dot_general(a, b, (((0,), (0,)), ((), ())), preferred_element_type=F32)


def exact(a, b, dims):
    return lax.dot_general(
        a, b, (dims, ((), ())), precision=lax.Precision.HIGHEST, preferred_element_type=F32
    )


def iota(shape, axis):
    return lax.broadcasted_iota(jnp.int32, shape, axis)


def low_pair(value):
    high = value.astype(BF16)
    return high, (value - high.astype(F32)).astype(BF16)


def aligned(start, size, unit):
    return pl.ds(pl.multiple_of(start, unit), size)


def assemble(dst, own, other, opt):
    dst[aligned(HALF * opt, HALF, 64), :] = own[0:HALF, :]
    dst[aligned(HALF * (1 - opt), HALF, 64), :] = other[0:HALF, :]


class Place:
    def __getitem__(self, i):
        if i == 0:
            return lax.axis_index("opt")
        me = lax.axis_index("dp")
        return (me & 3, me, (me >> 2) & 3)[i - 1]


def call(kernel, ins, outs, scratch=(), micros=5, name=None, vmem=12, after=()):
    if ins[0][1] is None:
        kernel = functools.partial(kernel, Place())
        ins = ins[1:]
    specs = [SMEM if s else VMEM for s, _ in ins] + [ANY] * len(after)
    count = len(ins)

    def body(*refs):
        kernel(*refs[:count], *refs[count + len(after) :])

    shapes = [jax.ShapeDtypeStruct(s, d) for s, d in outs]
    moved = sum(a.size * a.dtype.itemsize for _, a in ins)
    moved += sum(s.size * s.dtype.itemsize for s in shapes)
    return pl.pallas_call(
        body,
        out_shape=shapes,
        in_specs=specs,
        out_specs=[VMEM] * len(shapes),
        scratch_shapes=list(scratch),
        compiler_params=pltpu.CompilerParams(vmem_limit_bytes=vmem << 20),
        cost_estimate=pl.CostEstimate(
            flops=micros * 1100000000, bytes_accessed=moved, transcendentals=0
        ),
        name=name,
    )(*[a for _, a in ins], *after)


def head_stack(rows):
    lane_head = iota(rows.shape, 1) // HD
    zero = jnp.zeros_like(rows)
    return jnp.concatenate([jnp.where(lane_head == j, rows, zero) for j in range(4)], axis=0)


def attend_kernel(
    place, scalars, tokens, w_own, w_other, v_own, v_other,
    proj, att, lse, segc, segr, ownc, ownr, wanted, marks, vec, wfull, bias, vt,
):
    opt = place[0]
    assemble(wfull, w_own, w_other, opt)
    mine = v_own[...].astype(BF16).astype(F32)
    others = v_other[...].astype(BF16).astype(F32)
    first = opt == 0
    vec[0:6, :] = jnp.where(first, mine, others)
    vec[6:12, :] = jnp.where(first, others, mine)
    vec[12:16, :] = jnp.zeros((4, D), F32)

    position = iota((8, PAD), 1) + OFF * opt
    segment = jnp.zeros((8, PAD), jnp.int32)
    bound = jnp.int32(0)
    low_count = jnp.int32(0)
    for s in range(SEGS):
        bound = bound + scalars[s]
        segment = segment + (position >= bound).astype(jnp.int32)
        low_count = low_count + (bound <= WIN).astype(jnp.int32)
    mine = (segment < low_count).astype(jnp.int32) == (opt == 0).astype(jnp.int32)
    owned = jnp.where(mine, segment, -1)
    segr[...] = segment
    ownr[...] = owned
    for value, out in ((segment, segc), (owned, ownc)):
        value = value.astype(F32)
        for t in range(PAD // 128):
            rows = min(128, WIN - 128 * t)
            turned = jnp.broadcast_to(value[0:1, 128 * t : 128 * t + 128], (128, 128)).T
            out[128 * t : 128 * t + rows, :] = turned[0:rows].astype(jnp.int32)
    row, col = iota((2 * PAIRS, 128), 0), iota((2 * PAIRS, 128), 1)
    by_row = jnp.zeros((2 * PAIRS, 128), jnp.int32)
    by_col = jnp.zeros((2 * PAIRS, 128), jnp.int32)
    mark = jnp.zeros((2 * PAIRS, 128), jnp.int32)
    for j in range(PAIRS):
        mark = jnp.where(row == j, scalars[SEGS + 2 * PAIRS + j], mark)
        for at in (j, PAIRS + j):
            by_row = jnp.where(row == at, scalars[SEGS + at], by_row)
            by_col = jnp.where(col == at, scalars[SEGS + at], by_col)
    wanted[0] = by_row
    wanted[1] = by_col
    marks[...] = jnp.where(col < 64, mark >> 5, mark & 31).astype(F32).astype(BF16)
    for i, (q0, k0, k1) in enumerate(BANDS):
        bias[BAND_ROWS[i] : BAND_ROWS[i + 1], :] = jnp.where(
            segc[k0:k1, :] == segr[0:1, q0 : q0 + BLOCK], 0.0, NEG_BIG
        )

    x = tokens[aligned(OFF * opt, WIN, 64), :]
    bias_row = jnp.concatenate([vec[0:1, :], jnp.zeros((1, D), F32), vec[1:2, :]], axis=1)
    for first in range(0, 3 * D, 512):
        cols = slice(first, min(first + 512, 3 * D))
        proj[0:WIN, cols] = (nn(x, wfull[:, cols]) + bias_row[:, cols]).astype(BF16)
    proj[WIN:PAD, :] = jnp.zeros((PAD - WIN, 3 * D), BF16)

    def group(g):
        def lanes(part):
            return slice(part * D + 128 * g, part * D + 128 * g + 128)

        for t in range(PAD // 128):
            vt[:, 128 * t : 128 * t + 128] = (
                proj[128 * t : 128 * t + 128, lanes(2)].astype(F32).T.astype(BF16)
            )
        def scores(i):
            q0, k0, k1 = BANDS[i]
            return nt(proj[k0:k1, lanes(1)], head_stack(proj[q0 : q0 + BLOCK, lanes(0)]))

        coming = scores(0)
        for i, (q0, k0, k1) in enumerate(BANDS):
            st = coming
            if i + 1 < len(BANDS):
                coming = scores(i + 1)
            outs, probs, totals = [], [], []
            for j in range(4):
                t = (
                    st[:, j * BLOCK : (j + 1) * BLOCK] * EXP2_SCALE
                    + bias[BAND_ROWS[i] : BAND_ROWS[i + 1], :]
                )
                peak = jnp.max(t, axis=0, keepdims=True)
                powers = jnp.exp2(t - peak)
                total = jnp.sum(powers, axis=0, keepdims=True)
                lse[g, j : j + 1, q0 : q0 + BLOCK] = peak + jnp.log2(total)
                probs.append(powers.astype(BF16))
                totals.append(1.0 / total)
                if j % 2 == 1:
                    o = nn(vt[(j - 1) * HD : (j + 1) * HD, k0:k1], jnp.concatenate(probs[-2:], axis=1))
                    outs.append(o[0:HD, 0:BLOCK] * totals[-2])
                    outs.append(o[HD : 2 * HD, BLOCK : 2 * BLOCK] * totals[-1])
            rows = min(BLOCK, WIN - q0)
            att[q0 : q0 + rows, lanes(0)] = (
                jnp.concatenate(outs, axis=0).T[0:rows].astype(BF16)
            )

    for g in range(3):
        group(g)


def attend(place, scalars, arrays):
    return call(
        attend_kernel,
        [(1, place), (1, scalars)] + [(0, a) for a in arrays],
        [
            ((PAD, 3 * D), BF16),
            ((WIN, D), BF16),
            ((3, 4, PAD), F32),
            ((WIN, 128), jnp.int32),
            ((8, PAD), jnp.int32),
            ((WIN, 128), jnp.int32),
            ((8, PAD), jnp.int32),
            ((2, 2 * PAIRS, 128), jnp.int32),
            ((2 * PAIRS, 128), BF16),
            ((16, D), F32),
            ((D, 3 * D), BF16),
        ],
        [
            pltpu.VMEM((BAND_ROWS[-1], 128), F32),
            pltpu.VMEM((128, PAD), BF16),
        ],
        micros=8,
        name="attend",
    )


def cast_kernel(weights, wq, wo, wu, wd, buffer, sems):
    spans = [(wq, 3 * D), (wo, D), (wu, FF), (wd, FF)]
    copies = [
        pltpu.make_async_copy(
            weights.at[:, i * D : (i + 1) * D], buffer.at[:, i * D : (i + 1) * D], sems.at[i]
        )
        for i in range(12)
    ]
    for copy in copies:
        copy.start()
    at = 0
    for out, width in spans:
        for part in range(width // D):
            copies[at].wait()
            out[:, part * D : (part + 1) * D] = buffer[:, at * D : (at + 1) * D].astype(BF16)
            at += 1


def cast(weights):
    return pl.pallas_call(
        cast_kernel,
        out_shape=[jax.ShapeDtypeStruct((HALF, c), BF16) for c in (3 * D, D, FF, FF)],
        in_specs=[ANY],
        out_specs=[VMEM] * 4,
        scratch_shapes=[pltpu.VMEM(weights.shape, F32), pltpu.SemaphoreType.DMA((12,))],
        compiler_params=pltpu.CompilerParams(vmem_limit_bytes=52 << 20),
        name="cast",
    )(weights)


def bias_of(vec, c):
    first, last = 256 * c, 256 * c + 256
    parts = []
    while first < last:
        row, col = divmod(first, D)
        size = min(D - col, last - first)
        parts.append(vec[3 + row : 4 + row, col : col + size])
        first += size
    return parts[0] if len(parts) == 1 else jnp.concatenate(parts, axis=1)


def mlp_kernel(
    place, wanted, att, tokens, ownr, vec, wo_own, wo_other, wu_own, wu_other,
    wd_own, wd_other, xhat1, inv1, hlow, act, up_proj, xhat2, inv2, unit, uscale, wo, wu, wd,
    ench, encl,
):
    opt = place[0]
    assemble(wo, wo_own, wo_other, opt)
    assemble(wu, wu_own, wu_other, opt)
    assemble(wd, wd_own, wd_other, opt)

    def norm(v):
        centred = v - jnp.mean(v, axis=1, keepdims=True)
        inverse = lax.rsqrt(jnp.mean(centred * centred, axis=1, keepdims=True) + LN_EPS)
        return centred * inverse, inverse

    branch = nn(att[0:WIDE_ROWS, :], wo[...])
    for i in range(WIN // WIDE_ROWS):
        r = slice(i * WIDE_ROWS, (i + 1) * WIDE_ROWS)
        x = tokens[aligned(OFF * opt + i * WIDE_ROWS, WIDE_ROWS, 64), :].astype(F32)
        normed, inverse = norm(branch + vec[2:3, :] + x)
        if i + 1 < WIN // WIDE_ROWS:
            branch = nn(att[(i + 1) * WIDE_ROWS : (i + 2) * WIDE_ROWS, :], wo[...])
        xhat1[r, :] = normed
        inv1[r, :] = jnp.broadcast_to(inverse, (WIDE_ROWS, 128))
        h = normed * vec[8:9, :] + vec[9:10, :]
        low = h.astype(BF16)
        hlow[r, :] = low
        coming = nn(low, wu[:, 0:256])
        for c in range(6):
            cols = slice(c * 256, (c + 1) * 256)
            u = coming + bias_of(vec, c)
            if c < 5:
                coming = nn(low, wu[:, (c + 1) * 256 : (c + 2) * 256])
            up_proj[r, cols] = u
            half = lax.erf(u * 0.7071067811865476) * 0.5 + 0.5
            act[r, cols] = (u * half).astype(BF16)
        normed, inverse = norm(nt(act[r, :], wd[...]) + vec[7:8, :] + h)
        xhat2[r, :] = normed
        inv2[r, :] = jnp.broadcast_to(inverse, (WIDE_ROWS, 128))
        high, rest = low_pair(normed * vec[10:11, :] + vec[11:12, :])
        ench[r, :] = high
        encl[r, :] = rest

    onehot = jnp.where(wanted[0, :, 0:1] == ownr[0:1, 0:WIN], 1.0, 0.0)
    count = jnp.maximum(jnp.sum(onehot, axis=1, keepdims=True), 1.0)
    hot = onehot.astype(BF16)
    pooled = (nn(hot, ench[...]) + nn(hot, encl[...])) / count
    inverse_len = lax.rsqrt(jnp.sum(pooled * pooled, axis=1, keepdims=True) + POOL_EPS)
    unit[...] = pooled * inverse_len
    uscale[...] = jnp.broadcast_to(inverse_len / count, (2 * PAIRS, 128))


def slope_kernel(up_proj, out):
    def block(i, carry):
        r = aligned(i * 16, 16, 16)
        u = up_proj[r, :]
        half = lax.erf(u * 0.7071067811865476) * 0.5 + 0.5
        out[r, :] = half + u * jnp.exp2(u * u * (-0.5 * LOG2E)) * 0.3989422804014327
        return carry

    lax.fori_loop(0, WIN // 16, block, 0)


def slope_of(up_proj, after):
    return call(slope_kernel, [(0, up_proj)], [(up_proj.shape, F32)], name="slope", vmem=4, after=after)[0]


def mlp(place, wanted, att, tokens, ownr, vec, halves):
    return call(
        mlp_kernel,
        [(1, place), (0, wanted), (0, att), (0, tokens), (0, ownr), (0, vec)]
        + [(0, h) for h in halves],
        [
            ((WIN, D), F32),
            ((WIN, 128), F32),
            ((WIN, D), BF16),
            ((WIN, FF), BF16),
            ((WIN, FF), F32),
            ((WIN, D), F32),
            ((WIN, 128), F32),
            ((2 * PAIRS, D), F32),
            ((2 * PAIRS, 128), F32),
            ((D, D), BF16),
            ((D, FF), BF16),
            ((D, FF), BF16),
        ],
        [
            pltpu.VMEM((WIN, D), BF16),
            pltpu.VMEM((WIN, D), BF16),
        ],
        micros=10,
        name="mlp",
    )


def split_rows(grad, keep, send, place, *at):
    opt = place[0]
    for c in range(4):
        index = (c ^ place[1],) + at
        keep[index] = grad[aligned(HALF * opt + CHUNK * c, CHUNK, 16), :].astype(BF16)
        send[index] = grad[aligned(HALF * (1 - opt) + CHUNK * c, CHUNK, 16), :].astype(BF16)


def column_sums(value):
    return jnp.sum(value.reshape(-1, 8, D), axis=0)


def norm_backward(grad_at, normed_ref, inverse_ref, gain, out, low_out, sums, at, step=ROWS):
    def block(i, carry):
        scale_sum, shift_sum, bias_sum = carry
        r = aligned(i * step, step, 64)
        g = grad_at(r)
        normed = normed_ref[r, :]
        scaled = g * gain
        inner = (
            scaled
            - jnp.mean(scaled, axis=1, keepdims=True)
            - normed * jnp.mean(scaled * normed, axis=1, keepdims=True)
        ) * inverse_ref[r, 0:1]
        out[r, :] = inner
        low_out[r, :] = inner.astype(BF16)
        return (
            scale_sum + column_sums(g * normed),
            shift_sum + column_sums(g),
            bias_sum + column_sums(inner),
        )

    zero = jnp.zeros((8, D), F32)
    scale_sum, shift_sum, bias_sum = lax.fori_loop(0, WIN // step, block, (zero, zero, zero))
    sums[at : at + 1, :] = jnp.sum(bias_sum, axis=0, keepdims=True)
    sums[at + 1 : at + 2, :] = jnp.sum(scale_sum, axis=0, keepdims=True)
    sums[at + 2 : at + 3, :] = jnp.sum(shift_sum, axis=0, keepdims=True)


def down_kernel(
    place, count, order, wanted, units, ownc, uscale, xhat2, inv2, act, vec, *rest
):
    pieces, (dsec, dlow, keep, send, sums, queries, docs, marks, grad) = rest[:-9], rest[-9:]
    me = place[2]
    per = pieces[0].shape[0]
    for p, piece in enumerate(pieces):
        for j in range(per):
            at = order[p * per + j]
            r = slice(at * PAIRS, (at + 1) * PAIRS)
            both = piece[j].astype(F32)
            queries[r, :] = both[0:PAIRS, 0:D]
            docs[r, :] = both[PAIRS : 2 * PAIRS, 0:D]
            marks[r, :] = both[0:PAIRS, D : D + 128]
    total = count * PAIRS
    q = queries[...].astype(BF16)
    d = docs[...].astype(BF16)
    logits = SCORE_SCALE * nt(q, d)
    peak = jnp.max(logits, axis=1, keepdims=True)
    powers = jnp.exp(logits - peak)
    soft = powers / jnp.sum(powers, axis=1, keepdims=True)
    col = iota((total, total), 1)
    doc_id = ((col // PAIRS) ^ me) * PAIRS + lax.rem(col, PAIRS)
    hit = (marks[:, 0:1] * 32.0 + marks[:, 64:65]).astype(jnp.int32) == doc_id
    d_logits = (soft - jnp.where(hit, 1.0, 0.0)) * (SCORE_SCALE / total)
    high, rest_low = low_pair(d_logits[0:PAIRS, :])
    d_q = nn(high, d) + nn(rest_low, d)
    high, rest_low = low_pair(d_logits[:, 0:128].T[0:PAIRS, :])
    d_d = nn(high, q) + nn(rest_low, q)
    d_units = jnp.concatenate([d_q, d_d], axis=0)
    u = units[...]
    d_pool = uscale[:, 0:1] * (d_units - u * jnp.sum(u * d_units, axis=1, keepdims=True))
    hot = jnp.where(ownc[:, 0 : 2 * PAIRS] == wanted[1, 0:1, 0 : 2 * PAIRS], 1.0, 0.0).astype(BF16)
    high, rest_low = low_pair(d_pool)
    dsec[...] = nn(hot, high) + nn(hot, rest_low)
    norm_backward(
        lambda r: dsec[r, :], xhat2, inv2, vec[10:11, :], dsec, dlow, sums, 0, WIDE_ROWS
    )
    sums[3:8, :] = jnp.zeros((5, D), F32)
    halves = [slice(0, 2 * D), slice(2 * D, 4 * D)]
    grad[:, halves[0]] = tn(dlow[...], act[:, halves[0]])
    grad[:, halves[1]] = tn(dlow[...], act[:, halves[1]])
    for c in range(4):
        split_rows(grad.at[:, c * D : (c + 1) * D], keep, send, place, c)


def down_backward(count, order, place, wanted, units, ownc, uscale, saved, vec, pieces, after):
    total = count * PAIRS
    return call(
        lambda place, *refs: down_kernel(place, count, order, *refs),
        [(1, place), (0, wanted), (0, units), (0, ownc), (0, uscale)]
        + [(0, s) for s in saved]
        + [(0, vec)]
        + [(0, p) for p in pieces],
        [
            ((WIN, D), F32),
            ((WIN, D), BF16),
            ((4, 4, CHUNK, D), BF16),
            ((4, 4, CHUNK, D), BF16),
            ((8, D), F32),
        ],
        [
            pltpu.VMEM((total, D), F32),
            pltpu.VMEM((total, D), F32),
            pltpu.VMEM((total, 128), F32),
            pltpu.VMEM((D, FF), F32),
        ],
        micros=4,
        name="down_backward",
        after=after,
    )


def up_kernel(place, dlow, slope, hlow, wd, dup, keep, send, sums, grad):
    coming = nn(dlow[...], wd[:, 0 : 2 * D])
    for c in range(2):
        cols = slice(c * 2 * D, (c + 1) * 2 * D)
        part = (coming * slope[:, cols]).astype(BF16)
        if c == 0:
            coming = nn(dlow[...], wd[:, 2 * D : 4 * D])
        dup[:, cols] = part
        column_sum = jnp.sum(part.astype(F32), axis=0, keepdims=True)
        for j in range(2):
            sums[2 * c + j : 2 * c + j + 1, :] = column_sum[:, j * D : (j + 1) * D]
        grad[:, cols] = tn(hlow[...], dup[:, cols])
    for c in range(4):
        split_rows(grad.at[:, c * D : (c + 1) * D], keep, send, place, c)


def up_backward(place, dlow, slope, hlow, wd, after):
    return call(
        up_kernel,
        [(1, place)] + [(0, a) for a in (dlow, slope, hlow, wd)],
        [((WIN, FF), BF16), ((4, 4, CHUNK, D), BF16), ((4, 4, CHUNK, D), BF16), ((4, D), F32)],
        [pltpu.VMEM((D, FF), F32)],
        micros=3,
        name="up_backward",
        after=after,
    )


def first_kernel(dup, dsec, xhat1, inv1, vec, wu, dfirst, dlow, sums):
    steps = [slice(i, i + WIDE_ROWS) for i in range(0, WIN, WIDE_ROWS)]
    coming = nt(dup[steps[0], :], wu[...])
    gain = vec[8:9, :]
    totals = None
    for i, r in enumerate(steps):
        g = coming + dsec[r, :]
        if i + 1 < len(steps):
            coming = nt(dup[steps[i + 1], :], wu[...])
        normed = xhat1[r, :]
        scaled = g * gain
        inner = (
            scaled
            - jnp.mean(scaled, axis=1, keepdims=True)
            - normed * jnp.mean(scaled * normed, axis=1, keepdims=True)
        ) * inv1[r, 0:1]
        dfirst[r, :] = inner
        dlow[r, :] = inner.astype(BF16)
        new = [column_sums(inner), column_sums(g * normed), column_sums(g)]
        totals = new if totals is None else [a + b for a, b in zip(totals, new)]
    for i, total in enumerate(totals):
        sums[i : i + 1, :] = jnp.sum(total, axis=0, keepdims=True)
    sums[3:8, :] = jnp.zeros((5, D), F32)


def first_backward(dup, dsec, xhat1, inv1, vec, wu, after):
    return call(
        first_kernel,
        [(0, a) for a in (dup, dsec, xhat1, inv1, vec, wu)],
        [((WIN, D), F32), ((WIN, D), BF16), ((8, D), F32)],
        micros=1,
        name="first_backward",
        after=after,
    )


def branch_kernel(place, dlow, att, wo, datt, delta, okeep, osend, grad):
    grad[...] = tn(att[...], dlow[...])
    da = nt(dlow[...], wo[...]).astype(BF16)
    split_rows(grad, okeep, osend, place)
    datt[0:WIN, :] = da
    datt[WIN:PAD, :] = jnp.zeros((PAD - WIN, D), BF16)
    high, rest = low_pair(da.astype(F32) * att[...].astype(F32))
    heads = (iota((16, D), 1) // HD == iota((16, D), 0)).astype(F32).astype(BF16)
    delta[:, 0:WIN] = nt(heads, high) + nt(heads, rest)
    delta[:, WIN:PAD] = jnp.zeros((16, PAD - WIN), F32)


def branch_backward(place, dlow, att, wo, after):
    return call(
        branch_kernel,
        [(1, place), (0, dlow), (0, att), (0, wo)],
        [
            ((PAD, D), BF16),
            ((16, PAD), F32),
            ((4, CHUNK, D), BF16),
            ((4, CHUNK, D), BF16),
        ],
        [pltpu.VMEM((D, D), F32)],
        micros=1,
        name="branch_backward",
        after=after,
    )


def heads_kernel(place, g, tokens, proj, datt, lse, delta, segc, segr, *rest):
    rest, (dproj, keep, send, sums, kt, dk, dv, grad, ktmp, stmp) = rest[:-10], rest[-10:]

    def lanes(part):
        return slice(part * D + 128 * g, part * D + 128 * g + 128)

    for t in range(PAD // 128):
        kt[:, 128 * t : 128 * t + 128] = (
            proj[128 * t : 128 * t + 128, lanes(1)].astype(F32).T.astype(BF16)
        )
    dk[...] = jnp.zeros_like(dk)
    dv[...] = jnp.zeros_like(dv)

    def products(i):
        q0, k0, k1 = BANDS[i]
        qs = head_stack(proj[q0 : q0 + BLOCK, lanes(0)])
        gs = head_stack(datt[q0 : q0 + BLOCK, lanes(0)])
        return qs, gs, nt(proj[k0:k1, lanes(1)], qs), nt(proj[k0:k1, lanes(2)], gs)

    coming = products(0)
    for i, (q0, k0, k1) in enumerate(BANDS):
        qs, gs, st, dp = coming
        if i + 1 < len(BANDS):
            coming = products(i + 1)
        same = segc[k0:k1, :] == segr[0:1, q0 : q0 + BLOCK]
        bias = jnp.where(same, 0.0, NEG_BIG)
        probs, d_scores, dq = [], [], []
        for j in range(4):
            cols = slice(j * BLOCK, (j + 1) * BLOCK)
            prob = jnp.exp2(st[:, cols] * EXP2_SCALE + bias - lse[g, j : j + 1, q0 : q0 + BLOCK])
            ds = prob * (dp[:, cols] - delta[4 * g + j : 4 * g + j + 1, q0 : q0 + BLOCK])
            ds = ds.astype(BF16)
            probs.append(prob.astype(BF16))
            d_scores.append(ds)
            if j % 2 == 1:
                part = nn(
                    kt[(j - 1) * HD : (j + 1) * HD, k0:k1], jnp.concatenate(d_scores[-2:], axis=1)
                )
                dq.append(part[0:HD, 0:BLOCK])
                dq.append(part[HD : 2 * HD, BLOCK : 2 * BLOCK])
        dv[k0:k1, :] += nn(jnp.concatenate(probs, axis=1), gs)
        dk[k0:k1, :] += nn(jnp.concatenate(d_scores, axis=1), qs)
        rows = min(BLOCK, WIN - q0)
        dqs = jnp.concatenate(dq, axis=0).T[0:rows] * HD ** (-0.5)
        dproj[q0 : q0 + rows, 0:128] = dqs.astype(BF16)
    dproj[:, 128:256] = (dk[...] * HD ** (-0.5)).astype(BF16)
    dproj[:, 256:384] = dv[...].astype(BF16)
    grad[...] = tn(tokens[aligned(OFF * place[0], WIN, 64), :], dproj[...])
    q_sum = jnp.sum(dproj[:, 0:128].astype(F32), axis=0, keepdims=True)
    v_sum = jnp.sum(dproj[:, 256:384].astype(F32), axis=0, keepdims=True)
    sums[0:1, :] = q_sum
    sums[1:2, :] = v_sum
    sums[2:8, :] = jnp.zeros((6, 128), F32)
    if g < 2:
        split_rows(grad, keep, send, place)
        return
    parts, (dsums, usums, fsums, zero, one) = rest[:6], rest[6:]
    split_rows(grad, ktmp, stmp, place)
    for dst, out_part, blocks in (
        (keep, parts[0], (parts[2], parts[4], ktmp)),
        (send, parts[1], (parts[3], parts[5], stmp)),
    ):
        dst[:, :, 3 * D : 4 * D] = out_part[...]
        for h, part in enumerate(blocks):
            for c in range(3):
                dst[:, :, D * c + 128 * h : D * c + 128 * h + 128] = part[
                    :, :, 128 * c : 128 * c + 128
                ]
    rows = jnp.concatenate(
        [
            jnp.concatenate([zero[0:1], one[0:1], q_sum], axis=1),
            jnp.concatenate([zero[1:2], one[1:2], v_sum], axis=1),
            fsums[0:1, :],
            usums[0:4, :],
            dsums[0:1, :],
            fsums[1:3, :],
            dsums[1:3, :],
            jnp.zeros((4, D), F32),
        ],
        axis=0,
    ).astype(BF16)
    for c in range(4):
        for j in range(3):
            block = rows[:, 128 * j : 128 * j + 128]
            keep[c, 16 * j : 16 * j + 16, 4 * D : 4 * D + 128] = block
            send[c, 16 * j : 16 * j + 16, 4 * D : 4 * D + 128] = block


def heads_backward(g, place, ins, more, after):
    part = ((4, CHUNK, 4 * D + 128 if g == 2 else D), BF16)
    return call(
        lambda place, *refs: heads_kernel(place, g, *refs),
        [(1, place)] + [(0, a) for a in tuple(ins) + tuple(more)],
        [((WIN, D), BF16), part, part, ((8, 128), F32)],
        [
            pltpu.VMEM((128, PAD), BF16),
            pltpu.VMEM((WIN, 128), F32),
            pltpu.VMEM((WIN, 128), F32),
            pltpu.VMEM((D, D), F32),
            pltpu.VMEM((4, CHUNK, D), BF16),
            pltpu.VMEM((4, CHUNK, D), BF16),
        ],
        micros=1,
        name="heads_backward",
        after=after,
    )


def input_kernel(dp0, dp1, dp2, dfirst, wfull, igrad, dproj):
    for g, part in enumerate((dp0, dp1, dp2)):
        for c in range(3):
            dproj[:, c * D + 128 * g : c * D + 128 * g + 128] = part[:, 128 * c : 128 * c + 128]
    igrad[...] = (nt(dproj[...], wfull[...]) + dfirst[...]).astype(BF16)


def input_backward(parts, dfirst, wqkv, after):
    return call(
        input_kernel,
        [(0, a) for a in tuple(parts) + (dfirst, wqkv)],
        [((WIN, D), BF16)],
        [pltpu.VMEM((WIN, 3 * D), BF16)],
        micros=2,
        name="input_backward",
        after=after,
    )[0]


def flips(axis, size, bits):
    return [(i, i ^ bits) for i in range(size)]


def pair(value):
    return swap(value, "opt", 2, 1)


def swap(value, axis, size, bits):
    return lax.ppermute(value, axis, flips(axis, size, bits))


def bit_groups(size):
    bits = size.bit_length() - 1
    return [(s, 1 << min(2, bits - s)) for s in range(0, bits, 2)]


def trades(values, n, shift):
    return [values[0]] + [swap(values[k], "dp", n, k << shift) for k in (1, 2, 3)]


def added(a, b):
    return (a.astype(F32) + b.astype(F32)).astype(BF16)


def core_sum_kernel(keep, other, *outs):
    for r, out in enumerate(outs):
        out[...] = added(keep[r], other[r])


def core_sum(keep, other, after):
    return call(
        core_sum_kernel,
        [(0, keep), (0, other)],
        [(keep.shape[1:], BF16)] * 4,
        name="core_sum",
        vmem=4,
        after=after,
    )


def pair_sum_kernel(bit, keep, other, stay, go):
    for i, r in enumerate((0, 3 - bit)):
        stay[i] = added(keep[r], other[r])
        go[i] = added(keep[r + bit], other[r + bit])


def pair_sum(bit, keep, other, after):
    return call(
        functools.partial(pair_sum_kernel, bit),
        [(0, keep), (0, other)],
        [((2,) + keep.shape[1:], BF16)] * 2,
        name="pair_sum",
        vmem=4,
        after=after,
    )


def wide_step_kernel(down, dother, up, uother, dkeep, dsend, ukeep, usend):
    dkeep[...] = added(down[0], dother[0])
    dsend[...] = added(down[1], dother[1])
    ukeep[...] = added(up[0], uother[0])
    usend[...] = added(up[1], uother[1])


def wide_step(parts, after):
    return call(
        wide_step_kernel,
        [(0, p) for p in parts],
        [((4, CHUNK, D), BF16)] * 4,
        name="wide_step",
        vmem=4,
        after=after,
    )


def total_of(refs, at):
    a, b, c, d = (ref[at].astype(F32) for ref in refs)
    return ((a + b) + (c + d)).astype(BF16)


def wide_plane_kernel(place, down, dother, up, uother, *outs):
    for k, out in enumerate(outs):
        at = place[3] ^ k
        out[0] = added(down[at], dother[at])
        out[1] = added(up[at], uother[at])


def wide_plane_sum(place, parts, after):
    return call(
        wide_plane_kernel,
        [(1, place)] + [(0, p) for p in parts],
        [((2, CHUNK, D), BF16)] * 4,
        name="wide_plane_sum",
        vmem=4,
        after=after,
    )


def low_plane_kernel(a, b, c, d, out):
    out[...] = total_of((a, b, c, d), slice(None))


def low_plane_sum(parts, after=()):
    return call(
        low_plane_kernel,
        [(0, p) for p in parts],
        [(parts[0].shape, BF16)],
        name="low_plane_sum",
        vmem=4,
        after=after,
    )[0]


def low_next_kernel(keep, other, out):
    out[...] = added(keep[...], other[...])


def low_next(keep, other, after=()):
    return call(
        low_next_kernel,
        [(0, keep), (0, other)],
        [(keep.shape, BF16)],
        name="low_next",
        vmem=4,
        after=after,
    )[0]


def low_last_kernel(keep, other, out, vgrad):
    out[...] = added(keep[:, 0 : 4 * D], other[:, 0 : 4 * D])
    vgrad[...] = added(keep[:, 4 * D : 4 * D + 128], other[:, 4 * D : 4 * D + 128])


def low_last(keep, other, after):
    return call(
        low_last_kernel,
        [(0, keep), (0, other)],
        [((CHUNK, 4 * D), BF16), ((CHUNK, 128), BF16)],
        name="low_last",
        vmem=4,
        after=after,
    )


def chain_kernel(*refs):
    ins, out = refs[:-1], refs[-1]
    at = 0
    for ref in ins:
        flat = ref.reshape(-1, CHUNK, D)
        out[at : at + flat.shape[0]] = flat[...]
        at += flat.shape[0]


def chain(parts, after=()):
    count = sum(p.size for p in parts) // (CHUNK * D)
    return call(
        chain_kernel,
        [(0, p) for p in parts],
        [((count, CHUNK, D), BF16)],
        name="chain",
        vmem=4,
        after=after,
    )[0]


def rest_sum(value, n):
    bit = 16
    while bit < n:
        other = swap(value, "dp", n, bit)
        value = (value.astype(F32) + other.astype(F32)).astype(BF16)
        bit *= 2
    return value


def join_kernel(*refs):
    ins, out = refs[:-1], refs[-1]
    for i, ref in enumerate(ins):
        out[i] = ref[...]


def join(parts, after=()):
    return call(
        join_kernel,
        [(0, p) for p in parts],
        [((len(parts),) + parts[0].shape, parts[0].dtype)],
        name="join",
        vmem=4,
        after=after,
    )[0]


def pack_kernel(marks, unit, other, units, packed):
    both = unit[...] + other[...]
    units[...] = both
    packed[:, 0:D] = both.astype(BF16)
    packed[:, D : D + 128] = marks[...]


def pack(marks, unit, other):
    return call(
        pack_kernel,
        [(0, marks), (0, unit), (0, other)],
        [(unit.shape, F32), ((2 * PAIRS, D + 128), BF16)],
        name="pack",
        vmem=4,
    )


def squares_of(parts):
    acc = jnp.zeros((8, D), F32)
    for part in parts:
        flat = part.reshape(-1, CHUNK, part.shape[-1])
        for k in range(flat.shape[0]):
            for c in range(0, part.shape[-1], D):
                v = flat[k, :, c : c + D].astype(F32)
                acc = acc + jnp.sum((v * v).reshape(CHUNK // 8, 8, D), axis=0)
    return acc[:, 0:128] + acc[:, 128:256] + acc[:, 256:384]


def wide_squares_kernel(*refs):
    refs[-1][...] = squares_of(refs[:-1])


def squares_kernel(place, *refs):
    parts, (vgrad, before, out) = refs[:-3], refs[-3:]
    acc = squares_of(parts) + before[...]
    row = iota((16, 128), 0)
    low_row = 6 * place[0]
    mine = (row >= low_row) & (row < low_row + 6)
    for j in range(3):
        v = jnp.where(mine, vgrad[16 * j : 16 * j + 16, :].astype(F32), 0.0)
        v = v * v
        acc = acc + (v[0:8] + v[8:16])
    out[...] = acc


def squares(place, parts, vgrad=None, before=None, after=()):
    ins = [(0, p) for p in parts]
    kernel = wide_squares_kernel
    if before is not None:
        ins = [(1, place)] + ins + [(0, vgrad), (0, before)]
        kernel = squares_kernel
    return call(kernel, ins, [((8, 128), F32)], name="squares", vmem=4, after=after)[0]


def merge_kernel(place, igrad, other, out, flag):
    flag[...] = jnp.zeros((8, 128), F32)

    @pl.when(place[0] == 0)
    def low_core():
        out[0:OFF, :] = igrad[0:OFF, :]
        out[OFF:WIN, :] = added(igrad[OFF:WIN, :], other[0 : WIN - OFF, :])
        out[WIN:SEQ, :] = other[WIN - OFF : WIN, :]

    @pl.when(place[0] != 0)
    def high_core():
        out[0:OFF, :] = other[0:OFF, :]
        out[OFF:WIN, :] = added(other[OFF:WIN, :], igrad[0 : WIN - OFF, :])
        out[WIN:SEQ, :] = igrad[WIN - OFF : WIN, :]


def merge(place, igrad, other, after):
    return call(
        merge_kernel,
        [(1, place), (0, igrad), (0, other)],
        [((SEQ, D), BF16), ((8, 128), F32)],
        name="merge",
        vmem=4,
        after=after,
    )


def adamw(parameter, first_state, second, clipped, rate):
    first_new = first_state + (1.0 - BETA_ONE) * clipped
    second_new = second + (1.0 - BETA_TWO) * clipped * clipped
    root = (1.0 - BETA_TWO**STEP) ** 0.5
    below = pl.reciprocal(second_new * lax.rsqrt(second_new) + ADAM_EPS * root)
    scale = rate * root / (1.0 - BETA_ONE**STEP)
    return parameter - scale * (first_new * below), first_new, second_new


def decay_kernel(w, m, v, pv, pm, pq, nw, nm, nv, npv, npm, npq):
    for ins, outs, rate in (
        ((w, m, v), (nw, nm, nv), LEARN_RATE),
        ((pv, pm, pq), (npv, npm, npq), VECTOR_RATE),
    ):
        for ref, out, scale in zip(ins, outs, (1.0 - rate * DECAY_RATE, BETA_ONE, BETA_TWO)):
            out[...] = ref[...] * scale


def decay(arrays, after):
    return call(
        decay_kernel,
        [(0, a) for a in arrays],
        [(a.shape, F32) for a in arrays],
        name="decay",
        vmem=4,
        after=after,
    )


def adamw_kernel(*refs):
    place = Place()
    sums, refs = refs[:2], refs[2:]
    (vgrad, w, m, v, pv, pm, pq), refs = refs[:7], refs[7:]
    wide, low, refs = refs[:4], refs[4:8], refs[8:]
    outs, (npv, npm, npq, norm), scrs, sems = refs[:4], refs[4:8], refs[8:12], refs[12]
    opt = place[0]
    total = sums[0][...] + sums[1][...]
    total = jnp.sum(jnp.sum(total, axis=1, keepdims=True), axis=0, keepdims=True)
    grad_norm = jnp.sqrt(total)
    factor = jnp.minimum(1.0, CLIP_NORM / (grad_norm + 1e-06))
    norm[...] = grad_norm
    for j in range(3):
        cols = slice(128 * j, 128 * j + 128)
        g = vgrad[16 * j : 16 * j + 16, :].astype(F32)
        g = jnp.where(opt == 0, g[0:6], g[6:12])
        a, b, c = adamw(pv[:, cols], pm[:, cols], pq[:, cols], g * factor, VECTOR_RATE)
        npv[:, cols] = a
        npm[:, cols] = b
        npq[:, cols] = c

    def block(grad, rows, cols):
        new = adamw(w[rows, cols], m[rows, cols], v[rows, cols], grad * factor, LEARN_RATE)
        for scr, value in zip(scrs, new + (new[0].astype(BF16),)):
            scr[rows, cols] = value

    def copies(r, i):
        rows = aligned(CHUNK * (place[1] ^ r) + i * 16, 16, 16)
        return [
            pltpu.make_async_copy(scr.at[rows, :], out.at[rows, :], sems.at[3 * r + i, j])
            for j, (scr, out) in enumerate(zip(scrs, outs))
        ]

    for r in range(4):

        def step(i, carry, r=r):
            rows = aligned(CHUNK * (place[1] ^ r) + i * 16, 16, 16)
            here = aligned(i * 16, 16, 16)
            for j in range(4):
                at = D * (place[3] ^ j)
                for p, start in enumerate((4 * D + FF, 4 * D)):
                    grad = wide[r][2 * j + p, here, :].astype(F32)
                    block(grad, rows, aligned(start + at, D, 128))
            for c in range(4):
                grad = low[r][here, D * c : D * c + D].astype(F32)
                block(grad, rows, slice(D * c, D * c + D))
            for copy in copies(r, i):
                copy.start()
            return carry

        lax.fori_loop(0, CHUNK // 16, step, 0)
    for r in range(4):

        def finish(i, carry, r=r):
            for copy in copies(r, i):
                copy.wait()
            return carry

        lax.fori_loop(0, CHUNK // 16, finish, 0)


def update(place, sums, vgrad, w, m, v, pv, pm, pq, parts):
    ins = tuple(sums) + (vgrad, w, m, v, pv, pm, pq) + tuple(parts)
    shapes = [(w.shape, F32)] * 3 + [(w.shape, BF16)] + [(pv.shape, F32)] * 3 + [((1, 1), F32)]
    return pl.pallas_call(
        adamw_kernel,
        out_shape=[jax.ShapeDtypeStruct(s, d) for s, d in shapes],
        in_specs=[VMEM] * len(ins),
        out_specs=[ANY] * 4 + [VMEM] * 4,
        scratch_shapes=[
            pltpu.VMEM(w.shape, F32),
            pltpu.VMEM(w.shape, F32),
            pltpu.VMEM(w.shape, F32),
            pltpu.VMEM(w.shape, BF16),
            pltpu.SemaphoreType.DMA((12, 4)),
        ],
        compiler_params=pltpu.CompilerParams(vmem_limit_bytes=16 << 20),
        cost_estimate=pl.CostEstimate(
            flops=4000000000, bytes_accessed=26 * w.size, transcendentals=0
        ),
        name="adamw",
    )(*ins)


def shards(
    n,
    tokens,
    lengths,
    query_index,
    doc_index,
    targets,
    weights,
    first_moment,
    second_moment,
    vectors,
    vec_first,
    vec_second,
):
    place = None
    scalars = jnp.concatenate([lengths.reshape(SEGS), query_index, doc_index, targets])
    groups = bit_groups(n)

    w_own, wo_own, wu_own, wd_own = cast(weights)
    w_other = pair(w_own)
    vectors_late, w_own = lax.optimization_barrier((vectors, w_own))
    v_other = pair(vectors_late)
    wo = (wo_own, pair(wo_own))
    wu = (wu_own, pair(wu_own))
    wd = (wd_own, pair(wd_own))

    proj, att, lse, segc, segr, ownc, ownr, wanted, marks, vec, wqkv = attend(
        place, scalars, (tokens, w_own, w_other, vectors, v_other)
    )
    xhat1, inv1, hlow, act, up_proj, xhat2, inv2, unit, uscale, wo, wu, wd = mlp(
        place, wanted, att, tokens, ownr, vec, wo + wu + wd
    )
    units, packed = pack(marks, unit, pair(unit))
    groups = bit_groups(n)
    order = [0]
    stack = packed
    for i, (shift, size) in enumerate(groups[1:] + groups[:1]):
        pieces = [stack] + [swap(stack, "dp", n, k << shift) for k in range(1, size)]
        order = [o | (k << shift) for k in range(size) for o in order]
        if i < len(groups) - 1:
            slope = slope_of(up_proj, [packed])
            stack = join(pieces, [slope]).reshape(-1, 2 * PAIRS, D + 128)
    decayed = decay(
        (weights, first_moment, second_moment, vectors, vec_first, vec_second), [packed]
    )
    dsec, dlow, keep, send, dsums = down_backward(
        n, order, place, wanted, units, ownc, uscale, (xhat2, inv2, act), vec, pieces,
        decayed,
    )
    other = pair(send)
    dup, ukeep, usend, usums = up_backward(place, dlow, slope, hlow, wd, [])
    down, go = pair_sum(1, keep, other, [dup])
    dother = swap(go, "dp", n, 1)
    uother = pair(usend)
    dfirst, dlow, fsums = first_backward(dup, dsec, xhat1, inv1, vec, wu, [down])
    up, go = pair_sum(2, ukeep, uother, [dlow])
    uother = swap(go, "dp", n, 2)
    datt, delta, okeep, osend = branch_backward(place, dlow, att, wo, [up])
    ins = (tokens, proj, datt, lse, delta, segc, segr)
    part0, keep0, send0, sums0 = heads_backward(0, place, ins, (), [])
    part1, keep1, send1, sums1 = heads_backward(1, place, ins, (), [part0])
    part2, keep, send, _ = heads_backward(
        2, place, ins,
        (okeep, osend, keep0, send0, keep1, send1, dsums, usums, fsums, sums0, sums1), [part1],
    )
    other = pair(send)
    down, dsend, up, usend = wide_step((down, dother, up, uother), [part2])
    dother, uother = swap(dsend, "dp", n, 2), swap(usend, "dp", n, 1)
    igrad = input_backward((part0, part1, part2), dfirst, wqkv, [down])
    low = core_sum(keep, other, [igrad])
    low_got = trades(low, n, 0)
    wide = wide_plane_sum(place, (down, dother, up, uother), [low[0]])
    wide_got = trades(wide, n, 2)
    low = low_plane_sum(low_got, [wide[0]])
    other = swap(low, "dp", n, 4)
    wide = rest_sum(low_plane_sum(wide_got, [low]), n)
    wide_got = trades([wide] * 4, n, 2)
    wide = chain(wide_got)
    wide = trades([wide] * 4, n, 0)
    low = low_next(low, other, [wide[0]])
    other = swap(low, "dp", n, 8)
    igrad, low = lax.optimization_barrier((igrad, low))
    input_grad, flag = merge(place, igrad, pair(igrad), [low])
    low, vgrad = low_last(low, other, [flag])
    low, vgrad = rest_sum(low, n), rest_sum(vgrad, n)
    low = trades([low] * 4, n, 0)
    sums = squares(place, low, vgrad, squares(place, wide, after=[low[0]]))
    sums = (sums, pair(sums))
    pieces = tuple(wide) + tuple(low)
    nw, nm, nv, nlow, npv, npm, npq, norm = update(
        place, sums, vgrad, *decayed, pieces,
    )
    return (norm.reshape(()), input_grad, nw, nm, nv, nlow, npv, npm, npq)


def solution(mesh):
    rows = P("opt", None)
    in_specs = (P("dp", None), P("dp", None), P("dp"), P("dp"), P("dp")) + (rows,) * 6
    out_specs = (P(), P("dp", None)) + (rows,) * 7
    n = mesh.shape["dp"]
    return jax.shard_map(
        functools.partial(shards, n),
        mesh=mesh,
        in_specs=in_specs,
        out_specs=out_specs,
        check_vma=False,
    )
```
